32 devices in a mesh: section: 2 (over y), dp: 4 (over z), tensor: 4 (over x, core).
Axes of the slice: x: 2, y: 2, z: 4, core: 2. Of those that a mesh axis runs over, the one named last changes fastest.
Arguments:
- block_input: bfloat16 [2, 8192, 1024], P(None, ('dp', 'tensor')), may hold values from -6 to 6
- segment_ids: int32 [2, 8192], P(None, 'dp'), may hold values from 0 to 2, as said below
- cotangent: bfloat16 [2, 8192, 1024], P(None, ('dp', 'tensor')), may hold values from -6 to 6
- norm_one_gain: float32 [2, 1024], P('section'), may hold values from 0.1 to 1.9
- qkv_weight: float32 [2, 1024, 16, 192], P('section', 'dp', 'tensor'), may hold values from -0.1875 to 0.1875
- out_weight: float32 [2, 16, 64, 1024], P('section', 'tensor', None, 'dp'), may hold values from -5 to 5
- norm_two_gain: float32 [2, 1024], P('section'), may hold values from 0.1 to 1.9
- up_weight: float32 [2, 1024, 4096], P('section', 'dp', 'tensor'), may hold values from -0.1875 to 0.1875
- down_weight: float32 [2, 4096, 1024], P('section', 'tensor', 'dp'), may hold values from -0.09375 to 0.09375
Outputs:
- layer_outputs: bfloat16 [2, 2, 8192, 1024], P('section', None, ('dp', 'tensor'))
- input_grads: bfloat16 [2, 2, 8192, 1024], P('section', None, ('dp', 'tensor'))
- norm_one_grad: float32 [2, 1024], P('section')
- qkv_grad: float32 [2, 1024, 16, 192], P('section', 'dp', 'tensor')
- out_grad: float32 [2, 16, 64, 1024], P('section', 'tensor', None, 'dp')
- norm_two_grad: float32 [2, 1024], P('section')
- up_grad: float32 [2, 1024, 4096], P('section', 'dp', 'tensor')
- down_grad: float32 [2, 4096, 1024], P('section', 'tensor', 'dp')
The draws below stay inside these ranges and needn't reach their ends.
Inputs may be any that keep to these rules, and one draw needn't show every extreme that they name: `segment_ids`: within each replica's micro-batch of 2048 tokens, scene numbers run 0, 1, 2 in order, each scene nonempty; scene 1 begins within the first 512 tokens and ends within the last 512 tokens.
All inputs are finite; a program needn't handle non-finite values.
Results may differ from the reference program's by a relative error of at most 0.033.
Values may be sent and summed in bfloat16 or wider, within the bound.
A program may use at most 384 MiB of HBM per device.

```python
import jax
import jax.numpy as jnp
from jax import lax

D = 1024
HEADS = 16
HEAD_DIM = 64
FF = 4096
MB = 2
LAYERS = 2
SEQ = 2048
TOK_DEV = 512
TOKENS = 8192


def draw_segment_ids(key, part):
    seq_rows = MB * (TOKENS // SEQ)
    first_key = jax.random.fold_in(key, 11)
    second_key = jax.random.fold_in(key, 23)
    begins = jax.random.randint(first_key, (seq_rows, 1), 1, TOK_DEV)
    finish = jax.random.randint(second_key, (seq_rows, 1), SEQ - TOK_DEV + 1, SEQ)
    places = jnp.arange(SEQ, dtype=jnp.int32)[None, :]
    scenes = (places >= begins).astype(jnp.int32) + (places >= finish).astype(jnp.int32)
    return scenes.reshape(MB, TOKENS)


def block_levels(stream_key, dims, cuts, smallest, top_value):
    def one(position, blocks):
        draws = jax.random.uniform(jax.random.fold_in(jax.random.fold_in(stream_key, 6), position), (blocks,), jnp.float32, smallest / len(cuts), top_value / len(cuts))
        return jnp.repeat(jnp.exp(draws), dims[position] // blocks).reshape((-1,) + (1,) * (len(dims) - position - 1))

    loudness = one(*cuts[0])
    for cut in cuts[1:]:
        loudness = loudness * one(*cut)
    return loudness


def normal_values(own_key, shape, deviation, bound, shards=(), kind=jnp.bfloat16):
    loudness = block_levels(own_key, shape, shards, -0.22, 0.18) if shards else 1.0
    array = jax.random.normal(own_key, shape, jnp.float32) * deviation * loudness
    return jnp.minimum(jnp.maximum(array, -bound), bound).astype(kind)


def setup_inputs(seed: int = 0) -> dict:
    arg_keys = jax.random.split(jax.random.key(seed), 10)
    block_input = normal_values(arg_keys[0], (MB, TOKENS, D), 1.0, 6.0, ((1, 16),))
    segment_ids = draw_segment_ids(jax.random.fold_in(arg_keys[9], 71), 0)
    cotangent = normal_values(arg_keys[2], (MB, TOKENS, D), 1.0, 6.0, ((1, 16),))
    norm_one_gain = jnp.clip(1.0 + 0.18 * jax.random.normal(arg_keys[3], (LAYERS, D), jnp.float32), 0.1, 1.9)
    qkv_weight = normal_values(arg_keys[4], (LAYERS, D, HEADS, 3 * HEAD_DIM), D ** -0.5, 0.1875, ((0, 2), (1, 4), (2, 4)), jnp.float32)
    out_weight = normal_values(arg_keys[5], (LAYERS, HEADS, HEAD_DIM, D), ((SEQ // 3) ** 0.5 * D ** -0.5), 5.0, ((0, 2), (1, 4), (3, 4)), jnp.float32)
    norm_two_gain = jnp.clip(1.0 + 0.18 * jax.random.normal(arg_keys[6], (LAYERS, D), jnp.float32), 0.1, 1.9)
    up_weight = normal_values(arg_keys[7], (LAYERS, D, FF), D ** -0.5, 0.1875, ((0, 2), (1, 4), (2, 4)), jnp.float32)
    down_weight = normal_values(arg_keys[8], (LAYERS, FF, D), FF ** -0.5, 0.09375, ((0, 2), (1, 4), (2, 4)), jnp.float32)
    return dict(block_input=block_input, segment_ids=segment_ids, cotangent=cotangent, norm_one_gain=norm_one_gain, qkv_weight=qkv_weight, out_weight=out_weight, norm_two_gain=norm_two_gain, up_weight=up_weight, down_weight=down_weight)


PRECISE = lax.Precision.HIGHEST

@jax.custom_vjp
def low(v):
    return lax.optimization_barrier(v.astype(jnp.bfloat16)).astype(jnp.float32)

@jax.custom_vjp
def low_back(v):
    return v

def low_keep(v):
    return (low(v), None)

def low_pass(kept, grad):
    return (grad,)

def back_keep(v):
    return (v, None)

def back_low(kept, grad):
    return (low(grad),)
low.defvjp(low_keep, low_pass)
low_back.defvjp(back_keep, back_low)

def layer_norm(source, gain_vec):
    center = source - lax.optimization_barrier(jnp.mean(source, axis=-1, keepdims=True))
    spread_sq = lax.optimization_barrier(jnp.mean(center * center, axis=-1, keepdims=True))
    return center * lax.rsqrt(spread_sq + 1e-05) * gain_vec

def attend(queries, key_rows, value_rows, segments):
    head_count, length, head_dim = queries.shape
    block_rows = min(512, length)
    score_scale = head_dim ** (-0.5)

    def one_block(start):
        query_block = lax.dynamic_slice_in_dim(queries, start, block_rows, 1)
        query_segs = lax.dynamic_slice_in_dim(segments, start, block_rows, 0)
        raw_scores = low_back(jnp.einsum('hqd,hkd->hqk', query_block, key_rows, precision=PRECISE))
        same_scene = (query_segs[:, None] == segments[None, :])[None]
        scores = jnp.where(same_scene, raw_scores * score_scale, -1e+30)
        exponents = jnp.exp(scores - lax.optimization_barrier(jnp.max(scores, axis=-1, keepdims=True)))
        attn_probs = low(exponents / lax.optimization_barrier(jnp.sum(exponents, axis=-1, keepdims=True)))
        return jnp.einsum('hqk,hkd->hqd', attn_probs, value_rows, precision=PRECISE)
    starts = jnp.arange(length // block_rows, dtype=jnp.int32) * block_rows
    blocks = lax.map(jax.checkpoint(one_block), starts)
    return jnp.moveaxis(blocks, 0, 1).reshape(head_count, length, head_dim)

def layer(params, inputs, segments):
    gain_one, qkv_w, out_w, gain_two, up_w, down_w = params
    resid = low_back(inputs)
    normed_one = low(layer_norm(resid, gain_one))
    qkv_all = low(low_back(jnp.einsum('sd,dhe->hse', normed_one, low(qkv_w), precision=PRECISE)))
    head_dim = qkv_all.shape[2] // 3
    context = attend(qkv_all[..., :head_dim], qkv_all[..., head_dim:2 * head_dim], qkv_all[..., 2 * head_dim:], segments)
    context = low(low_back(context))
    attn_out = low_back(jnp.einsum('hse,hed->sd', context, low(out_w), precision=PRECISE))
    resid_mid = resid + attn_out
    normed_two = low(layer_norm(resid_mid, gain_two))
    up_proj = low_back(jnp.dot(normed_two, low(up_w), precision=PRECISE))
    hidden = low(jax.nn.gelu(up_proj, approximate=False))
    mlp_out = low_back(jnp.dot(hidden, low(down_w), precision=PRECISE))
    return low(resid_mid + mlp_out)

def reference(block_input, segment_ids, cotangent, norm_one_gain, qkv_weight, out_weight, norm_two_gain, up_weight, down_weight):
    seq_count = MB * (TOKENS // SEQ)
    inputs = block_input.astype(jnp.float32).reshape(seq_count, SEQ, D)
    cot_rows = cotangent.astype(jnp.float32).reshape(seq_count, SEQ, D)
    segments = segment_ids.reshape(seq_count, SEQ)
    weights = (norm_one_gain, qkv_weight, out_weight, norm_two_gain, up_weight, down_weight)
    params_one = tuple((weight_item[0] for weight_item in weights))
    params_two = tuple((weight_item[1] for weight_item in weights))

    def one_sequence(totals, pieces):
        seq_in, seq_cot, seq_segs = pieces

        def layer_fn(params, rows_in):
            return layer(params, rows_in, seq_segs)
        middle, back_one = jax.vjp(layer_fn, params_one, seq_in)
        final, back_two = jax.vjp(layer_fn, params_two, middle)
        grads_two, d_middle = back_two(seq_cot)
        grads_one, d_input = back_one(d_middle)
        totals = (jax.tree.map(jnp.add, totals[0], grads_one), jax.tree.map(jnp.add, totals[1], grads_two))
        return (totals, (middle, final, d_input, d_middle))
    zero_one = jax.tree.map(jnp.zeros_like, params_one)
    zero_two = jax.tree.map(jnp.zeros_like, params_two)
    totals, stacked = lax.scan(one_sequence, (zero_one, zero_two), (inputs, cot_rows, segments))
    middle, final, d_input, d_middle = stacked
    shape_out = (MB, TOKENS, D)
    layer_outputs = jnp.stack([middle.reshape(shape_out), final.reshape(shape_out)]).astype(jnp.bfloat16)
    input_grads = jnp.stack([d_input.reshape(shape_out), d_middle.reshape(shape_out)]).astype(jnp.bfloat16)
    grads = tuple((jnp.stack([grad_first, grad_second]) for grad_first, grad_second in zip(totals[0], totals[1])))
    return (layer_outputs, input_grads, grads[0], grads[1], grads[2], grads[3], grads[4], grads[5])
```

```python
import functools
import math

import jax
import jax.numpy as jnp
from jax import lax
from jax.experimental import pallas as pl
from jax.experimental.pallas import tpu as pltpu
from jax.sharding import PartitionSpec as P

F32 = jnp.float32
BF = jnp.bfloat16
NT = (((1,), (1,)), ((), ()))
NN = (((1,), (0,)), ((), ()))
MASKED = -1e30
SCENES = 3


def dg(a, b, dims):
    return lax.dot_general(a, b, dims, preferred_element_type=F32)


def query_block(length):
    return 512 if length % 512 == 0 else length


def attend_kernel(bq, kc, qkv_ref, qm_ref, km_ref, ctx_ref, lse_ref, ka, vt):
    heads, length, width = qkv_ref.shape
    e = width // 3
    c = e**-0.5 * math.log2(math.e)
    for h in range(heads):
        ka[h, :, :e] = qkv_ref[h, :, e : 2 * e]
        ka[h, :, e:] = km_ref[...]
        vt[h, :e, :] = qkv_ref[h, :, 2 * e :].T
        vt[h, e:, :] = jnp.ones((16, length), BF)

    def body(i, _):
        rows = pl.ds(pl.multiple_of(i * bq, bq), bq)
        for h in range(heads):
            q = jnp.concatenate([qkv_ref[h, rows, :e], qm_ref[rows, :]], axis=1)
            parts = []
            top = None
            for k in range(length // kc):
                s = dg(ka[h, k * kc : (k + 1) * kc, :], q, NT)
                t = jnp.max(s, axis=0, keepdims=True)
                top = t if top is None else jnp.maximum(top, t)
                parts.append(s)
            top = top * c
            acc = None
            for k in range(length // kc):
                p = jnp.exp2(parts[k] * c - top).astype(BF)
                a = dg(vt[h, :, k * kc : (k + 1) * kc], p, NN)
                acc = a if acc is None else acc + a
            total = acc[e : e + 1]
            ctx_ref[h, rows, :] = (acc[:e] * (1.0 / total)).T.astype(BF)
            lse_ref[h, 0:1, rows] = top + jnp.log2(total)
        return 0

    lax.fori_loop(0, length // bq, body, 0)


def attend(qkv, qm, km):
    heads, length, width = qkv.shape
    e = width // 3
    vm = pl.BlockSpec(memory_space=pltpu.VMEM)
    bq = query_block(length)
    return pl.pallas_call(
        functools.partial(attend_kernel, bq, bq),
        out_shape=(
            jax.ShapeDtypeStruct((heads, length, e), BF),
            jax.ShapeDtypeStruct((heads, 1, length), F32),
        ),
        in_specs=[vm] * 3,
        out_specs=(vm, vm),
        scratch_shapes=[
            pltpu.VMEM((heads, length, 2 * e), BF),
            pltpu.VMEM((heads, e + 16, length), BF),
        ],
        compiler_params=pltpu.CompilerParams(vmem_limit_bytes=56 << 20),
        cost_estimate=pl.CostEstimate(
            flops=16 * heads * length * length * e,
            bytes_accessed=8 * heads * length * e,
            transcendentals=heads * length * length,
        ),
    )(qkv, qm, km)


def attend_back_kernel(
    bq, kc, qkv_ref, qm_ref, km_ref, ctx_ref, lse_ref, dctx_ref, dqkv_ref, ka, va, kt, dk, dv
):
    heads, length, width = qkv_ref.shape
    e = width // 3
    scale = e**-0.5
    c = scale * math.log2(math.e)
    lane = lax.broadcasted_iota(jnp.int32, (length, e), 1)
    for h in range(heads):
        ka[h, :, :e] = qkv_ref[h, :, e : 2 * e]
        ka[h, :, e:] = km_ref[...]
        va[h, :, :e] = qkv_ref[h, :, 2 * e :]
        va[h, :, e:] = jnp.where(lane < 3, 1.0, 0.0).astype(BF)
        kt[h] = qkv_ref[h, :, e : 2 * e].T
    dk[...] = jnp.zeros_like(dk)
    dv[...] = jnp.zeros_like(dv)
    ql = lax.broadcasted_iota(jnp.int32, (bq, e), 1)

    def body(i, _):
        rows = pl.ds(pl.multiple_of(i * bq, bq), bq)
        for h in range(heads):
            qq = qkv_ref[h, rows, :e]
            q = jnp.concatenate([qq, qm_ref[rows, :]], axis=1)
            dc = dctx_ref[h, rows, :]
            d = -jnp.sum(dc.astype(F32) * ctx_ref[h, rows, :].astype(F32), axis=1, keepdims=True)
            d1 = d.astype(BF).astype(F32)
            d2 = (d - d1).astype(BF).astype(F32)
            d3 = d - d1 - d2
            da = jnp.where(ql == 0, d1, jnp.where(ql == 1, d2, jnp.where(ql == 2, d3, 0.0)))
            dca = jnp.concatenate([dc, da.astype(BF)], axis=1)
            lse = lse_ref[h, 0:1, rows]
            dqt = None
            for k in range(length // kc):
                ks = slice(k * kc, (k + 1) * kc)
                s = dg(ka[h, ks, :], q, NT)
                p = jnp.exp2(s * c - lse)
                ds = (p * dg(va[h, ks, :], dca, NT)).astype(BF)
                dv[h, ks, :] += dg(p.astype(BF), dc, NN)
                dk[h, ks, :] += dg(ds, qq, NN)
                a = dg(kt[h, :, ks], ds, NN)
                dqt = a if dqt is None else dqt + a
            dqkv_ref[h, rows, :e] = (dqt * scale).T.astype(BF)
        return 0

    lax.fori_loop(0, length // bq, body, 0)
    for h in range(heads):
        dqkv_ref[h, :, e : 2 * e] = (dk[h] * scale).astype(BF)
        dqkv_ref[h, :, 2 * e :] = dv[h].astype(BF)


def attend_back(qkv, qm, km, ctx, lse, dctx):
    heads, length, width = qkv.shape
    e = width // 3
    vm = pl.BlockSpec(memory_space=pltpu.VMEM)
    bq = query_block(length)
    return pl.pallas_call(
        functools.partial(attend_back_kernel, bq, bq),
        out_shape=jax.ShapeDtypeStruct((heads, length, width), BF),
        in_specs=[vm] * 6,
        out_specs=vm,
        scratch_shapes=[
            pltpu.VMEM((heads, length, 2 * e), BF),
            pltpu.VMEM((heads, length, 2 * e), BF),
            pltpu.VMEM((heads, e, length), BF),
            pltpu.VMEM((heads, length, e), F32),
            pltpu.VMEM((heads, length, e), F32),
        ],
        compiler_params=pltpu.CompilerParams(vmem_limit_bytes=60 << 20),
        cost_estimate=pl.CostEstimate(
            flops=40 * heads * length * length * e,
            bytes_accessed=20 * heads * length * e,
            transcendentals=heads * length * length,
        ),
    )(qkv, qm, km, ctx, lse, dctx)


def scene_masks(segments, e):
    same = (segments[:, None] == jnp.arange(e, dtype=jnp.int32)[None]).astype(F32)
    used = jnp.arange(e)[None] < SCENES
    return (
        jnp.where(used, same * MASKED, 0.0).astype(BF),
        jnp.where(used, 1.0 - same, 0.0).astype(BF),
    )


def norm_stats(source):
    center = source - jnp.mean(source, axis=-1, keepdims=True)
    r = lax.rsqrt(jnp.mean(center * center, axis=-1, keepdims=True) + 1e-05)
    return center * r, r


def norm_back(source, gain, grad):
    n, r = norm_stats(source)
    e = grad * gain
    dh = r * (
        e - jnp.mean(e, axis=-1, keepdims=True) - n * jnp.mean(e * n, axis=-1, keepdims=True)
    )
    return dh, jnp.sum(grad * n, axis=0)


def spread(source):
    return lax.all_gather(source, "tensor", axis=0, tiled=True)


def collect(source):
    return lax.psum_scatter(
        source.astype(BF), "tensor", scatter_dimension=0, tiled=True
    ).astype(F32)


def ein(spec, a, b):
    return jnp.einsum(spec, a, b, preferred_element_type=F32)


def swap_section(value):
    return lax.ppermute(value, "section", [(0, 1), (1, 0)])


def shards(
    block_input,
    segment_ids,
    cotangent,
    norm_one_gain,
    qkv_weight,
    out_weight,
    norm_two_gain,
    up_weight,
    down_weight,
):
    section = lax.axis_index("section")
    layers = lax.axis_size("section")

    def gather_weight(w, axis):
        got = lax.all_gather(w[0].astype(BF), ("section", "dp"), axis=0, tiled=False)
        return got.reshape((layers, -1) + got.shape[1:])

    def join(w, axis):
        return jnp.concatenate([w[i] for i in range(w.shape[0])], axis=axis)

    w_qkv = gather_weight(qkv_weight, 0)
    w_out = gather_weight(out_weight, 2)
    w_up = gather_weight(up_weight, 0)
    w_down = gather_weight(down_weight, 1)
    gains_one = lax.all_gather(norm_one_gain[0], "section", axis=0, tiled=False)
    gains_two = lax.all_gather(norm_two_gain[0], "section", axis=0, tiled=False)
    segments = lax.dynamic_index_in_dim(segment_ids, section, 0, keepdims=False)
    x = lax.dynamic_index_in_dim(block_input, section, 0, keepdims=False)
    head_dim = qkv_weight.shape[3] // 3
    qm, km = scene_masks(segments, head_dim)
    kept = []
    ys = []
    for layer in range(2):
        wq = join(w_qkv[layer], 0)
        wo = join(w_out[layer], 2)
        wu = join(w_up[layer], 0)
        wd = join(w_down[layer], 1)
        g1, g2 = gains_one[layer], gains_two[layer]
        resid = x.astype(F32)
        a1 = spread((norm_stats(resid)[0] * g1).astype(BF))
        qkv = ein("sd,dhe->hse", a1, wq).astype(BF)
        ctx, lse = attend(qkv, qm, km)
        h1 = resid + collect(ein("hse,hed->sd", ctx, wo))
        a2 = spread((norm_stats(h1)[0] * g2).astype(BF))
        up = jnp.dot(a2, wu, preferred_element_type=F32)
        half = 0.5 * (1.0 + lax.erf(up * (0.5**0.5)))
        slope = (half + up * jnp.exp(-0.5 * up * up) * ((2 * math.pi) ** -0.5)).astype(BF)
        hidden = (up * half).astype(BF)
        x = (h1 + collect(jnp.dot(hidden, wd, preferred_element_type=F32))).astype(BF)
        ys.append(x)
        kept.append((wq, wo, wu, wd, g1, g2, resid, a1, qkv, ctx, lse, h1, a2, slope, hidden))
    other_y = swap_section(jnp.where(section == 0, ys[1], ys[0]))
    grad = lax.dynamic_index_in_dim(cotangent, section, 0, keepdims=False)
    dxs = [None, None]
    gain_sums = [None, None]
    sums = [None, None]

    def reduce_rows(value, axis):
        return lax.psum_scatter(value.astype(BF), "dp", scatter_dimension=axis, tiled=True)

    for layer in (1, 0):
        wq, wo, wu, wd, g1, g2, resid, a1, qkv, ctx, lse, h1, a2, slope, hidden = kept[layer]
        grad_in = grad.astype(F32)
        g_low = spread(grad)
        d_down = ein("sf,sd->fd", hidden, g_low)
        d_up = (ein("sd,fd->sf", g_low, wd) * slope.astype(F32)).astype(BF)
        g_up = ein("sd,sf->df", a2, d_up)
        dh, gain_two = norm_back(h1, g2, collect(ein("sf,df->sd", d_up, wu)))
        d_mid = dh + grad_in
        d_attn = spread(d_mid.astype(BF))
        g_out = ein("hse,sd->hed", ctx, d_attn)
        d_ctx = ein("sd,hed->hse", d_attn, wo).astype(BF)
        d_qkv = attend_back(qkv, qm, km, ctx, lse, d_ctx)
        g_qkv = ein("sd,hse->dhe", a1, d_qkv)
        dh, gain_one = norm_back(resid, g1, collect(ein("hse,dhe->sd", d_qkv, wq)))
        grad = (dh + d_mid).astype(BF)
        dxs[layer] = grad
        gain_sums[layer] = (gain_one, gain_two)
        sums[layer] = (
            reduce_rows(g_qkv, 0),
            reduce_rows(g_out, 2),
            reduce_rows(g_up, 0),
            reduce_rows(d_down, 1),
        )
    other_dx = swap_section(jnp.where(section == 0, dxs[1], dxs[0]))

    def own_layer(mine, other):
        first = jnp.where(section == 0, mine, other)
        second = jnp.where(section == 0, other, mine)
        return jnp.stack([first, second])[None]

    layer_out = own_layer(jnp.where(section == 0, ys[0], ys[1]), other_y)
    input_out = own_layer(jnp.where(section == 0, dxs[0], dxs[1]), other_dx)

    def finish(zero, one):
        send = swap_section(jnp.where(section == 0, one, zero))
        return (jnp.where(section == 0, zero, one).astype(F32) + send.astype(F32))[None]

    qkv_grad, out_grad, up_grad, down_grad = [finish(a, b) for a, b in zip(sums[0], sums[1])]
    gains = lax.psum(
        jnp.stack([jnp.stack(gain_sums[0]), jnp.stack(gain_sums[1])]), ("section", "dp", "tensor")
    )
    gains = lax.dynamic_index_in_dim(gains, section, 0, keepdims=False)
    return (
        layer_out,
        input_out,
        gains[0][None],
        qkv_grad,
        out_grad,
        gains[1][None],
        up_grad,
        down_grad,
    )


def solution(mesh):
    return jax.shard_map(
        shards,
        mesh=mesh,
        in_specs=(
            P(None, ("dp", "tensor"), None),
            P(None, "dp"),
            P(None, ("dp", "tensor"), None),
            P("section", None),
            P("section", "dp", "tensor", None),
            P("section", "tensor", None, "dp"),
            P("section", None),
            P("section", "dp", "tensor"),
            P("section", "tensor", "dp"),
        ),
        out_specs=(
            P("section", None, ("dp", "tensor"), None),
            P("section", None, ("dp", "tensor"), None),
            P("section", None),
            P("section", "dp", "tensor", None),
            P("section", "tensor", None, "dp"),
            P("section", None),
            P("section", "dp", "tensor"),
            P("section", "tensor", "dp"),
        ),
        check_vma=False,
    )
```

```python
import functools
import math

import jax
import jax.numpy as jnp
from jax import lax
from jax.experimental import pallas as pl
from jax.experimental.pallas import tpu as pltpu
from jax.sharding import PartitionSpec as P

F32 = jnp.float32
BF = jnp.bfloat16
NT = (((1,), (1,)), ((), ()))
NN = (((1,), (0,)), ((), ()))
TN = (((0,), (0,)), ((), ()))
MASKED = -1e30
SCENES = 3
MESH = pl.DeviceIdType.MESH
VM = pl.BlockSpec(memory_space=pltpu.VMEM)
HB = pl.BlockSpec(memory_space=pl.ANY)
DMA = pltpu.SemaphoreType.DMA
LIMIT = 58 << 20


def dg(a, b, dims):
    return lax.dot_general(a, b, dims, preferred_element_type=F32)


def chunks(rows):
    return 4 if rows % 64 == 0 else 1


def shape(dims, dtype):
    return jax.ShapeDtypeStruct(dims, dtype)


class Group:
    def __init__(self, size):
        self.size = size
        self.chips = size // 2
        self.me = lax.axis_index("tensor")
        self.chip = lax.div(self.me, 2)
        self.core = lax.rem(self.me, 2)
        self.sibling = self.chip * 2 + 1 - self.core

    def ahead(self, k):
        return lax.rem(self.chip + k, self.chips)

    def behind(self, k):
        return lax.rem(self.chip + self.chips - k, self.chips)

    def greet(self):
        barrier = pltpu.get_barrier_semaphore()
        targets = [self.sibling] + [self.ahead(k) * 2 + self.core for k in range(1, self.chips)]
        for target in targets:
            pl.semaphore_signal(
                barrier, inc=1, device_id={"tensor": target}, device_id_type=MESH
            )
        pl.semaphore_wait(barrier, self.chips)


def remote(src, dst, send, recv, target):
    return pltpu.make_async_remote_copy(
        src_ref=src,
        dst_ref=dst,
        send_sem=send,
        recv_sem=recv,
        device_id={"tensor": target},
        device_id_type=MESH,
    )


def span(j, rc):
    return pl.ds(pl.multiple_of(j * rc, rc), rc)


def comm_sems(group_size, n):
    c = group_size // 2
    far, near = DMA((max(c - 1, 1), n)), DMA((c, n))
    return [far, far, near, near]


class Gather:
    def __init__(self, g, buf, rc, sems):
        self.g, self.buf, self.rc = g, buf, rc
        self.far_send, self.far_recv, self.near_send, self.near_recv = sems

    def far(self, k, j, origin, target):
        ref = self.buf.at[origin, span(j, self.rc)]
        return remote(ref, ref, self.far_send.at[k - 1, j], self.far_recv.at[k - 1, j], target)

    def near(self, k, j, origin):
        ref = self.buf.at[origin, span(j, self.rc)]
        return remote(
            ref, ref, self.near_send.at[k, j], self.near_recv.at[k, j], self.g.sibling
        )

    def start(self, j):
        g = self.g
        for k in range(1, g.chips):
            self.far(k, j, g.me, g.ahead(k) * 2 + g.core).start()
        self.near(0, j, g.me).start()

    def relay(self, j):
        g = self.g
        for k in range(1, g.chips):
            origin = g.behind(k) * 2 + g.core
            self.far(k, j, origin, g.me).wait_recv()
            self.near(k, j, origin).start()

    def ready(self, j):
        g = self.g
        self.near(0, j, g.sibling).wait_recv()
        for k in range(1, g.chips):
            self.near(k, j, g.behind(k) * 2 + 1 - g.core).wait_recv()

    def drain(self, n):
        g = self.g

        def one(j, _):
            for k in range(1, g.chips):
                self.far(k, j, g.me, g.sibling).wait_send()
            for k in range(g.chips):
                self.near(k, j, g.me).wait_send()
            return 0

        lax.fori_loop(0, n, one, 0)


def scatter_scratch(group_size, rows, width, n):
    c = group_size // 2
    far = pltpu.VMEM((max(c - 1, 1), rows, width), BF)
    near = pltpu.VMEM((c, rows, width), BF)
    return [pltpu.VMEM((group_size, rows, width), F32), near, near, far, far] + comm_sems(
        group_size, n
    )


class Scatter:
    def __init__(self, g, rc, scratch):
        self.g, self.rc = g, rc
        self.part, self.near_out, self.near_in, self.far_out, self.far_in = scratch[:5]
        self.far_send, self.far_recv, self.near_send, self.near_recv = scratch[5:]

    def near(self, k, j):
        rows = span(j, self.rc)
        return remote(
            self.near_out.at[k, rows],
            self.near_in.at[k, rows],
            self.near_send.at[k, j],
            self.near_recv.at[k, j],
            self.g.sibling,
        )

    def far(self, k, j):
        rows = span(j, self.rc)
        return remote(
            self.far_out.at[k - 1, rows],
            self.far_in.at[k - 1, rows],
            self.far_send.at[k - 1, j],
            self.far_recv.at[k - 1, j],
            self.g.ahead(k) * 2 + self.g.core,
        )

    def first(self, j):
        g, rows = self.g, span(j, self.rc)
        for k in list(range(1, g.chips)) + [0]:
            owner = g.ahead(k) * 2 + 1 - g.core
            self.near_out[k, rows, :] = self.part[owner, rows, :].astype(BF)
            self.near(k, j).start()

    def second(self, j):
        g, rows = self.g, span(j, self.rc)
        for k in range(1, g.chips):
            owner = g.ahead(k) * 2 + g.core
            self.near(k, j).wait_recv()
            both = self.part[owner, rows, :] + self.near_in[k, rows, :].astype(F32)
            self.far_out[k - 1, rows, :] = both.astype(BF)
            self.far(k, j).start()

    def third(self, j):
        g, rows = self.g, span(j, self.rc)
        self.near(0, j).wait_recv()
        total = self.part[g.me, rows, :] + self.near_in[0, rows, :].astype(F32)
        for k in range(1, g.chips):
            self.far(k, j).wait_recv()
            total = total + self.far_in[k - 1, rows, :].astype(F32)
        return total

    def drain(self, n):
        g = self.g

        def one(j, _):
            for k in range(1, g.chips):
                self.far(k, j).wait_send()
            for k in range(g.chips):
                self.near(k, j).wait_send()
            return 0

        lax.fori_loop(0, n, one, 0)


def params(key):
    return pltpu.CompilerParams(
        vmem_limit_bytes=LIMIT, collective_id=key, has_side_effects=True
    )


def cost(flops, moved, exps=0):
    return pl.CostEstimate(flops=int(flops), bytes_accessed=int(moved), transcendentals=int(exps))


def normed(source):
    center = source - jnp.mean(source, axis=-1, keepdims=True)
    r = lax.rsqrt(jnp.mean(center * center, axis=-1, keepdims=True) + 1e-05)
    return center * r, r


def normed_back(source, gain, grad):
    n, r = normed(source)
    e = grad * gain
    dh = r * (
        e - jnp.mean(e, axis=-1, keepdims=True) - n * jnp.mean(e * n, axis=-1, keepdims=True)
    )
    return dh, jnp.sum(grad * n, axis=0, keepdims=True)


def flat(value):
    return value.reshape((value.shape[0] * value.shape[1],) + value.shape[2:])


def run(n, body):
    def one(j, carry):
        body(j)
        return carry

    lax.fori_loop(0, n, one, 0)


def qkv_kernel(
    size, layer, x_ref, gain_ref, w_ref, qkv_ref, a1_out, a1, w, w_sem, out_sem, *sems
):
    rows, width = x_ref.shape
    heads = qkv_ref.shape[0]
    parts, depth = w_ref.shape[0] // 2, w_ref.shape[2]
    n = chunks(rows)
    rc = rows // n
    g = Group(size)
    copies = [
        pltpu.make_async_copy(
            w_ref.at[layer * parts + z], w.at[:, pl.ds(z * depth, depth)], w_sem.at[z]
        )
        for z in range(parts)
    ]
    for copy in copies:
        copy.start()
    g.greet()
    gather = Gather(g, a1, rc, sems)

    def send(j):
        at = span(j, rc)
        a = normed(x_ref[at, :].astype(F32))[0] * gain_ref[layer : layer + 1, :]
        a1[g.me, at, :] = a.astype(BF)
        gather.start(j)

    run(n, send)
    for copy in copies:
        copy.wait()

    def work(j):
        at = span(j, rc)
        gather.relay(j)
        gather.ready(j)
        a = flat(a1[:, at, :])
        for h in range(heads):
            r = dg(a, w[h], NN).astype(BF)
            qkv_ref[h, :, at, :] = r.reshape(size, rc, r.shape[1])

    run(n, work)
    out = pltpu.make_async_copy(a1, a1_out, out_sem.at[0])
    out.start()
    gather.drain(n)
    out.wait()


def qkv_forward(size, layer, x, gains, w):
    rows, width = x.shape
    _, heads, depth, wide = w.shape
    n = chunks(rows)
    return pl.pallas_call(
        functools.partial(qkv_kernel, size, layer),
        out_shape=(
            shape((heads, size, rows, wide), BF),
            shape((size, rows, width), BF),
        ),
        in_specs=[VM, VM, HB],
        out_specs=(VM, HB),
        scratch_shapes=[
            pltpu.VMEM((size, rows, width), BF),
            pltpu.VMEM((heads, width, wide), BF),
            DMA((w.shape[0] // 2,)),
            DMA((1,)),
        ]
        + comm_sems(size, n),
        compiler_params=params(layer),
        cost_estimate=cost(20e9, 30e6),
    )(x, gains, w)


def attend_kernel(
    size, layer, qkv_ref, qm_ref, km_ref, x_ref, w_ref,
    h1_ref, ctx_ref, lse_ref, ka, vt, w, w_sem, *scratch
):
    heads, _, rows, wide = qkv_ref.shape
    length = size * rows
    e = wide // 3
    c = e**-0.5 * math.log2(math.e)
    parts, depth = w_ref.shape[0] // 2, w_ref.shape[2]
    n = chunks(rows)
    rc = rows // n
    bq = size * rc
    kc = bq
    g = Group(size)
    copies = [
        pltpu.make_async_copy(
            w_ref.at[layer * parts + z], w.at[:, pl.ds(z * depth, depth)], w_sem.at[z]
        )
        for z in range(parts)
    ]
    for copy in copies:
        copy.start()
    g.greet()
    scatter = Scatter(g, rc, scratch)
    for h in range(heads):
        whole = flat(qkv_ref[h])
        ka[h, :, :e] = whole[:, e : 2 * e]
        ka[h, :, e:] = flat(km_ref[...])
        vt[h, :e, :] = whole[:, 2 * e :].T
        vt[h, e:, :] = jnp.ones((16, length), BF)
    for copy in copies:
        copy.wait()

    def work(j):
        at = span(j, rc)
        qm = flat(qm_ref[:, at, :])
        found = []
        for h in range(heads):
            q = jnp.concatenate([flat(qkv_ref[h, :, at, :])[:, :e], qm], axis=1)
            held = []
            top = None
            for k in range(length // kc):
                s = dg(ka[h, k * kc : (k + 1) * kc, :], q, NT)
                t = jnp.max(s, axis=0, keepdims=True)
                top = t if top is None else jnp.maximum(top, t)
                held.append(s)
            top = top * c
            acc = None
            for k in range(length // kc):
                p = jnp.exp2(held[k] * c - top).astype(BF)
                a = dg(vt[h, :, k * kc : (k + 1) * kc], p, NN)
                acc = a if acc is None else acc + a
            total = acc[e : e + 1]
            found.append((acc[:e] * (1.0 / total)).astype(BF))
            lse_ref[j, h : h + 1, :] = top + jnp.log2(total)
        ctx = (jnp.concatenate(found, axis=0) if heads > 1 else found[0]).T
        ctx_ref[:, at, :] = ctx.reshape(size, rc, heads * e)
        for z in range(parts):
            scatter.part[:, at, z * depth : (z + 1) * depth] = dg(
                ctx, w[:, z * depth : (z + 1) * depth], NN
            ).reshape(size, rc, depth)
        scatter.first(j)
        scatter.second(j)

    run(n, work)

    def last(j):
        at = span(j, rc)
        h1_ref[at, :] = x_ref[at, :].astype(F32) + scatter.third(j)

    run(n, last)
    scatter.drain(n)


def attend(size, layer, qkv, qm, km, x, w):
    heads, _, rows, wide = qkv.shape
    e = wide // 3
    width = x.shape[1]
    n = chunks(rows)
    return pl.pallas_call(
        functools.partial(attend_kernel, size, layer),
        out_shape=(
            shape((rows, width), F32),
            shape((size, rows, heads * e), BF),
            shape((n, heads, size * rows // n), F32),
        ),
        in_specs=[VM, VM, VM, VM, HB],
        out_specs=(VM, VM, VM),
        scratch_shapes=[
            pltpu.VMEM((heads, size * rows, 2 * e), BF),
            pltpu.VMEM((heads, e + 16, size * rows), BF),
            pltpu.VMEM((heads * e, width), BF),
            DMA((w.shape[0] // 2,)),
        ]
        + scatter_scratch(size, rows, width, n),
        compiler_params=params(2 + layer),
        cost_estimate=cost(60e9, 20e6),
    )(qkv, qm, km, x, w)


def mlp_kernel(
    size, layer, h1_ref, gain_ref, wu_ref, wd_ref,
    y_ref, a2_out, hid_out, slope_out, a2, hid, slope, wu, wd, w_sem, out_sem, *scratch
):
    rows, width = h1_ref.shape
    parts, depth, hidden = wu_ref.shape[0] // 2, wu_ref.shape[1], wu_ref.shape[2]
    fb = min(256, hidden)
    n = chunks(rows)
    rc = rows // n
    g = Group(size)
    copies = []
    for z in range(parts):
        at = pl.ds(z * depth, depth)
        copies.append(pltpu.make_async_copy(wu_ref.at[layer * parts + z], wu.at[at], w_sem.at[z]))
        copies.append(
            pltpu.make_async_copy(wd_ref.at[layer * parts + z], wd.at[:, at], w_sem.at[parts + z])
        )
    for copy in copies:
        copy.start()
    g.greet()
    gather = Gather(g, a2, rc, scratch[:4])
    scatter = Scatter(g, rc, scratch[4:])

    def send(j):
        at = span(j, rc)
        a = normed(h1_ref[at, :])[0] * gain_ref[layer : layer + 1, :]
        a2[g.me, at, :] = a.astype(BF)
        gather.start(j)

    run(n, send)
    for copy in copies:
        copy.wait()

    def work(j):
        at = span(j, rc)
        gather.relay(j)
        gather.ready(j)
        a = flat(a2[:, at, :])
        for f in range(hidden // fb):
            cols = slice(f * fb, (f + 1) * fb)
            u = dg(a, wu[:, cols], NN)
            half = 0.5 + 0.5 * lax.erf(u * (0.5**0.5))
            slope[:, at, cols] = (
                (half + u * jnp.exp(-0.5 * u * u) * ((2 * math.pi) ** -0.5))
                .astype(BF)
                .reshape(size, rc, fb)
            )
            hid[:, at, cols] = (u * half).astype(BF).reshape(size, rc, fb)
        held = flat(hid[:, at, :])
        for z in range(parts):
            cols = slice(z * depth, (z + 1) * depth)
            scatter.part[:, at, cols] = dg(held, wd[:, cols], NN).reshape(size, rc, depth)
        scatter.first(j)
        scatter.second(j)

    run(n, work)
    outs = [
        pltpu.make_async_copy(a2, a2_out, out_sem.at[0]),
        pltpu.make_async_copy(hid, hid_out, out_sem.at[1]),
        pltpu.make_async_copy(slope, slope_out, out_sem.at[2]),
    ]
    for out in outs:
        out.start()

    def last(j):
        at = span(j, rc)
        y_ref[at, :] = (h1_ref[at, :] + scatter.third(j)).astype(BF)

    run(n, last)
    gather.drain(n)
    scatter.drain(n)
    for out in outs:
        out.wait()


def mlp_forward(size, layer, h1, gains, wu, wd):
    rows, width = h1.shape
    hidden = wu.shape[2]
    n = chunks(rows)
    return pl.pallas_call(
        functools.partial(mlp_kernel, size, layer),
        out_shape=(
            shape((rows, width), BF),
            shape((size, rows, width), BF),
            shape((size, rows, hidden), BF),
            shape((size, rows, hidden), BF),
        ),
        in_specs=[VM, VM, HB, HB],
        out_specs=(VM, HB, HB, HB),
        scratch_shapes=[
            pltpu.VMEM((size, rows, width), BF),
            pltpu.VMEM((size, rows, hidden), BF),
            pltpu.VMEM((size, rows, hidden), BF),
            pltpu.VMEM((width, hidden), BF),
            pltpu.VMEM((hidden, width), BF),
            DMA((wu.shape[0],)),
            DMA((3,)),
        ]
        + comm_sems(size, n)
        + scatter_scratch(size, rows, width, n),
        compiler_params=params(4 + layer),
        cost_estimate=cost(50e9, 30e6),
    )(h1, gains, wu, wd)


def mlp_back_kernel(
    size, layer, g_ref, h1_ref, gain_ref, a2_ref, hid_ref, slope_ref, wu_ref, wd_ref,
    mid_ref, gain_out, gup_ref, gdown_ref,
    grad, a2, hid, dup, wu, wd, w_sem, *scratch
):
    rows, width = h1_ref.shape
    parts, depth, hidden = wu_ref.shape[0] // 2, wu_ref.shape[1], wu_ref.shape[2]
    fb = min(256, hidden)
    n = chunks(rows)
    rc = rows // n
    g = Group(size)
    copies = []
    for z in range(parts):
        at = pl.ds(z * depth, depth)
        copies.append(pltpu.make_async_copy(wd_ref.at[layer * parts + z], wd.at[:, at], w_sem.at[z]))
        copies.append(
            pltpu.make_async_copy(wu_ref.at[layer * parts + z], wu.at[at], w_sem.at[parts + z])
        )
    copies.append(pltpu.make_async_copy(slope_ref, dup, w_sem.at[2 * parts]))
    late = [
        pltpu.make_async_copy(hid_ref, hid, w_sem.at[2 * parts + 1]),
        pltpu.make_async_copy(a2_ref, a2, w_sem.at[2 * parts + 2]),
    ]
    for copy in copies + late:
        copy.start()
    g.greet()
    gather = Gather(g, grad, rc, scratch[:4])
    scatter = Scatter(g, rc, scratch[4:])

    def send(j):
        at = span(j, rc)
        grad[g.me, at, :] = g_ref[at, :]
        gather.start(j)

    run(n, send)
    for copy in copies:
        copy.wait()

    def work(j):
        at = span(j, rc)
        gather.relay(j)
        gather.ready(j)
        held = flat(grad[:, at, :])
        for f in range(hidden // fb):
            cols = slice(f * fb, (f + 1) * fb)
            d = dg(held, wd[cols, :], NT) * flat(dup[:, at, cols]).astype(F32)
            dup[:, at, cols] = d.astype(BF).reshape(size, rc, fb)
        held = flat(dup[:, at, :])
        for z in range(parts):
            cols = slice(z * depth, (z + 1) * depth)
            scatter.part[:, at, cols] = dg(held, wu[cols, :], NT).reshape(size, rc, depth)
        scatter.first(j)
        scatter.second(j)

    run(n, work)
    for copy in late:
        copy.wait()

    def up_grad(z):
        cols = pl.ds(pl.multiple_of(z * depth, depth), depth)
        gup_ref[z] = dg(flat(a2[:, :, cols]), flat(dup[...]), TN).astype(BF)

    run(parts, up_grad)

    def down_grad(f):
        cols = pl.ds(pl.multiple_of(f * fb, fb), fb)
        r = dg(flat(hid[:, :, cols]), flat(grad[...]), TN).astype(BF)
        for z in range(parts):
            gdown_ref[z, cols, :] = r[:, z * depth : (z + 1) * depth]

    run(hidden // fb, down_grad)
    gain_out[...] = jnp.zeros_like(gain_out)

    def last(j):
        at = span(j, rc)
        dh, dgain = normed_back(h1_ref[at, :], gain_ref[layer : layer + 1, :], scatter.third(j))
        mid_ref[at, :] = g_ref[at, :].astype(F32) + dh
        gain_out[...] += dgain

    run(n, last)
    gather.drain(n)
    scatter.drain(n)


def mlp_backward(size, layer, grad, h1, gains, a2, hid, slope, wu, wd):
    rows, width = h1.shape
    depth, hidden = wu.shape[1:]
    parts = wu.shape[0] // 2
    n = chunks(rows)
    return pl.pallas_call(
        functools.partial(mlp_back_kernel, size, layer),
        out_shape=(
            shape((rows, width), F32),
            shape((1, width), F32),
            shape((parts, depth, hidden), BF),
            shape((parts, hidden, depth), BF),
        ),
        in_specs=[VM, VM, VM, HB, HB, HB, HB, HB],
        out_specs=(VM, VM, VM, VM),
        scratch_shapes=[
            pltpu.VMEM((size, rows, width), BF),
            pltpu.VMEM((size, rows, width), BF),
            pltpu.VMEM((size, rows, hidden), BF),
            pltpu.VMEM((size, rows, hidden), BF),
            pltpu.VMEM((width, hidden), BF),
            pltpu.VMEM((hidden, width), BF),
            DMA((2 * parts + 3,)),
        ]
        + comm_sems(size, n)
        + scatter_scratch(size, rows, width, n),
        compiler_params=params(6 + layer),
        cost_estimate=cost(60e9, 40e6),
    )(grad, h1, gains, a2, hid, slope, wu, wd)


def attend_back_kernel(
    size, layer, mid_ref, qkv_ref, qm_ref, km_ref, ctx_ref, lse_ref, w_ref,
    dqkv_ref, gout_ref, da, ka, va, kt, dk, dv, w, w_sem, *sems
):
    heads, _, rows, wide = qkv_ref.shape
    length = size * rows
    e = wide // 3
    scale = e**-0.5
    c = scale * math.log2(math.e)
    parts, depth = w_ref.shape[0] // 2, w_ref.shape[2]
    n = chunks(rows)
    rc = rows // n
    bq = size * rc
    kc = bq
    g = Group(size)
    copies = [
        pltpu.make_async_copy(
            w_ref.at[layer * parts + z], w.at[:, pl.ds(z * depth, depth)], w_sem.at[z]
        )
        for z in range(parts)
    ]
    for copy in copies:
        copy.start()
    g.greet()
    gather = Gather(g, da, rc, sems)

    def send(j):
        at = span(j, rc)
        da[g.me, at, :] = mid_ref[at, :].astype(BF)
        gather.start(j)

    run(n, send)
    lane = lax.broadcasted_iota(jnp.int32, (length, e), 1)
    for h in range(heads):
        whole = flat(qkv_ref[h])
        ka[h, :, :e] = whole[:, e : 2 * e]
        ka[h, :, e:] = flat(km_ref[...])
        va[h, :, :e] = whole[:, 2 * e :]
        va[h, :, e:] = jnp.where(lane < 3, 1.0, 0.0).astype(BF)
        kt[h] = whole[:, e : 2 * e].T
    dk[...] = jnp.zeros_like(dk)
    dv[...] = jnp.zeros_like(dv)
    ql = lax.broadcasted_iota(jnp.int32, (bq, e), 1)
    for copy in copies:
        copy.wait()

    def work(j):
        at = span(j, rc)
        gather.relay(j)
        gather.ready(j)
        qm = flat(qm_ref[:, at, :])
        dctx = dg(flat(da[:, at, :]), w[...], NT).astype(BF)
        ctx = flat(ctx_ref[:, at, :])
        for h in range(heads):
            qq = flat(qkv_ref[h, :, at, :])[:, :e]
            q = jnp.concatenate([qq, qm], axis=1)
            dc = dctx[:, h * e : (h + 1) * e]
            prod = dc.astype(F32) * ctx[:, h * e : (h + 1) * e].astype(F32)
            d = -jnp.sum(prod, axis=1, keepdims=True)
            d1 = d.astype(BF).astype(F32)
            d2 = (d - d1).astype(BF).astype(F32)
            d3 = d - d1 - d2
            ds_col = jnp.where(ql == 0, d1, jnp.where(ql == 1, d2, jnp.where(ql == 2, d3, 0.0)))
            dca = jnp.concatenate([dc, ds_col.astype(BF)], axis=1)
            lse = lse_ref[j, h : h + 1, :]
            dqt = None
            for k in range(length // kc):
                ks = slice(k * kc, (k + 1) * kc)
                s = dg(ka[h, ks, :], q, NT)
                p = jnp.exp2(s * c - lse)
                ds = (p * dg(va[h, ks, :], dca, NT)).astype(BF)
                dv[h, ks, :] += dg(p.astype(BF), dc, NN)
                dk[h, ks, :] += dg(ds, qq, NN)
                a = dg(kt[h, :, ks], ds, NN)
                dqt = a if dqt is None else dqt + a
            dqkv_ref[h, :, at, :e] = (dqt * scale).T.astype(BF).reshape(size, rc, e)

    run(n, work)
    for h in range(heads):
        dqkv_ref[h, :, :, e : 2 * e] = (dk[h] * scale).astype(BF).reshape(size, rows, e)
        dqkv_ref[h, :, :, 2 * e :] = dv[h].astype(BF).reshape(size, rows, e)

    def out_grad(z):
        cols = pl.ds(pl.multiple_of(z * depth, depth), depth)
        gout_ref[z] = dg(flat(ctx_ref[...]), flat(da[:, :, cols]), TN).astype(BF)

    run(parts, out_grad)
    gather.drain(n)


def attend_backward(size, layer, mid, qkv, qm, km, ctx, lse, w):
    heads, _, rows, wide = qkv.shape
    e = wide // 3
    width = mid.shape[1]
    parts, depth = w.shape[0] // 2, w.shape[2]
    length = size * rows
    n = chunks(rows)
    return pl.pallas_call(
        functools.partial(attend_back_kernel, size, layer),
        out_shape=(shape(qkv.shape, BF), shape((parts, heads * e, depth), BF)),
        in_specs=[VM] * 6 + [HB],
        out_specs=(VM, VM),
        scratch_shapes=[
            pltpu.VMEM((size, rows, width), BF),
            pltpu.VMEM((heads, length, 2 * e), BF),
            pltpu.VMEM((heads, length, 2 * e), BF),
            pltpu.VMEM((heads, e, length), BF),
            pltpu.VMEM((heads, length, e), F32),
            pltpu.VMEM((heads, length, e), F32),
            pltpu.VMEM((heads * e, width), BF),
            DMA((parts,)),
        ]
        + comm_sems(size, n),
        compiler_params=params(8 + layer),
        cost_estimate=cost(90e9, 40e6),
    )(mid, qkv, qm, km, ctx, lse, w)


def qkv_back_kernel(
    size, layer, dqkv_ref, a1_ref, x_ref, mid_ref, gain_ref, w_ref,
    dx_ref, gain_out, gqkv_ref, w, w_sem, *scratch
):
    rows, width = x_ref.shape
    heads = dqkv_ref.shape[0]
    parts, depth = w_ref.shape[0] // 2, w_ref.shape[2]
    n = chunks(rows)
    rc = rows // n
    g = Group(size)
    copies = [
        pltpu.make_async_copy(
            w_ref.at[layer * parts + z], w.at[:, pl.ds(z * depth, depth)], w_sem.at[z]
        )
        for z in range(parts)
    ]
    for copy in copies:
        copy.start()
    g.greet()
    scatter = Scatter(g, rc, scratch)
    for copy in copies:
        copy.wait()

    def work(j):
        at = span(j, rc)
        for z in range(parts):
            cols = slice(z * depth, (z + 1) * depth)
            total = None
            for h in range(heads):
                r = dg(flat(dqkv_ref[h, :, at, :]), w[h, cols, :], NT)
                total = r if total is None else total + r
            scatter.part[:, at, cols] = total.reshape(size, rc, depth)
        scatter.first(j)
        scatter.second(j)

    run(n, work)

    def qkv_grad(z):
        cols = pl.ds(pl.multiple_of(z * depth, depth), depth)
        for h in range(heads):
            gqkv_ref[z, h] = dg(flat(a1_ref[:, :, cols]), flat(dqkv_ref[h]), TN).astype(BF)

    run(parts, qkv_grad)
    gain_out[...] = jnp.zeros_like(gain_out)

    def last(j):
        at = span(j, rc)
        dh, dgain = normed_back(
            x_ref[at, :].astype(F32), gain_ref[layer : layer + 1, :], scatter.third(j)
        )
        dx_ref[at, :] = (mid_ref[at, :] + dh).astype(BF)
        gain_out[...] += dgain

    run(n, last)
    scatter.drain(n)


def qkv_backward(size, layer, dqkv, a1, x, mid, gains, w):
    rows, width = x.shape
    heads, _, _, wide = dqkv.shape
    parts, depth = w.shape[0] // 2, w.shape[2]
    n = chunks(rows)
    return pl.pallas_call(
        functools.partial(qkv_back_kernel, size, layer),
        out_shape=(
            shape((rows, width), BF),
            shape((1, width), F32),
            shape((parts, heads, depth, wide), BF),
        ),
        in_specs=[VM] * 5 + [HB],
        out_specs=(VM, VM, VM),
        scratch_shapes=[
            pltpu.VMEM((heads, width, wide), BF),
            DMA((parts,)),
        ]
        + scatter_scratch(size, rows, width, n),
        compiler_params=params(10 + layer),
        cost_estimate=cost(30e9, 30e6),
    )(dqkv, a1, x, mid, gains, w)


def scene_masks(segments, e):
    same = (segments[..., None] == jnp.arange(e, dtype=jnp.int32)).astype(F32)
    used = jnp.arange(e) < SCENES
    return (
        jnp.where(used, same * MASKED, 0.0).astype(BF),
        jnp.where(used, 1.0 - same, 0.0).astype(BF),
    )


def swap_section(value):
    return lax.ppermute(value, "section", [(0, 1), (1, 0)])


def shards(
    block_input,
    segment_ids,
    cotangent,
    norm_one_gain,
    qkv_weight,
    out_weight,
    norm_two_gain,
    up_weight,
    down_weight,
):
    section = lax.axis_index("section")
    size = lax.axis_size("tensor")

    def gather_weight(w):
        return lax.all_gather(w.astype(BF), ("section", "dp"), axis=0, tiled=False)

    w_qkv = gather_weight(jnp.swapaxes(qkv_weight[0], 0, 1))
    w_out = gather_weight(out_weight[0].reshape((-1, out_weight.shape[3])))
    w_up = gather_weight(up_weight[0])
    w_down = gather_weight(down_weight[0])
    gains_one = lax.all_gather(norm_one_gain[0], "section", axis=0, tiled=False)
    gains_two = lax.all_gather(norm_two_gain[0], "section", axis=0, tiled=False)
    segments = lax.dynamic_index_in_dim(segment_ids, section, 0, keepdims=False)
    x = lax.dynamic_index_in_dim(block_input, section, 0, keepdims=False)
    head_dim = qkv_weight.shape[3] // 3
    qm, km = scene_masks(segments.reshape((size, -1)), head_dim)
    kept = []
    ys = []
    for layer in range(2):
        qkv, a1 = qkv_forward(size, layer, x, gains_one, w_qkv)
        h1, ctx, lse = attend(size, layer, qkv, qm, km, x, w_out)
        y, a2, hid, slope = mlp_forward(size, layer, h1, gains_two, w_up, w_down)
        kept.append((x, a1, qkv, ctx, lse, h1, a2, hid, slope))
        ys.append(y)
        x = y
    other_y = swap_section(jnp.where(section == 0, ys[1], ys[0]))
    grad = lax.dynamic_index_in_dim(cotangent, section, 0, keepdims=False)
    dxs = [None, None]
    gain_sums = [None, None]
    sums = [None, None]

    def reduce_rows(value):
        return lax.psum_scatter(value, "dp", scatter_dimension=0, tiled=False)

    for layer in (1, 0):
        x, a1, qkv, ctx, lse, h1, a2, hid, slope = kept[layer]
        mid, gain_two, g_up, g_down = mlp_backward(
            size, layer, grad, h1, gains_two, a2, hid, slope, w_up, w_down
        )
        d_qkv, g_out = attend_backward(size, layer, mid, qkv, qm, km, ctx, lse, w_out)
        grad, gain_one, g_qkv = qkv_backward(size, layer, d_qkv, a1, x, mid, gains_one, w_qkv)
        dxs[layer] = grad
        gain_sums[layer] = jnp.concatenate([gain_one, gain_two], axis=0)
        sums[layer] = [reduce_rows(v) for v in (g_qkv, g_out, g_up, g_down)]
    other_dx = swap_section(jnp.where(section == 0, dxs[1], dxs[0]))

    def own_layer(mine, other):
        first = jnp.where(section == 0, mine, other)
        second = jnp.where(section == 0, other, mine)
        return jnp.stack([first, second])[None]

    layer_out = own_layer(jnp.where(section == 0, ys[0], ys[1]), other_y)
    input_out = own_layer(jnp.where(section == 0, dxs[0], dxs[1]), other_dx)

    def finish(zero, one):
        send = swap_section(jnp.where(section == 0, one, zero))
        return jnp.where(section == 0, zero, one).astype(F32) + send.astype(F32)

    qkv_grad, out_grad, up_grad, down_grad = [finish(a, b) for a, b in zip(sums[0], sums[1])]
    gains = lax.psum(jnp.stack(gain_sums), ("section", "dp", "tensor"))
    gains = lax.dynamic_index_in_dim(gains, section, 0, keepdims=False)
    return (
        layer_out,
        input_out,
        gains[0][None],
        jnp.swapaxes(qkv_grad, 0, 1)[None],
        out_grad.reshape(out_weight.shape),
        gains[1][None],
        up_grad[None],
        down_grad[None],
    )


def solution(mesh):
    return jax.shard_map(
        shards,
        mesh=mesh,
        in_specs=(
            P(None, ("dp", "tensor"), None),
            P(None, "dp"),
            P(None, ("dp", "tensor"), None),
            P("section", None),
            P("section", "dp", "tensor", None),
            P("section", "tensor", None, "dp"),
            P("section", None),
            P("section", "dp", "tensor"),
            P("section", "tensor", "dp"),
        ),
        out_specs=(
            P("section", None, ("dp", "tensor"), None),
            P("section", None, ("dp", "tensor"), None),
            P("section", None),
            P("section", "dp", "tensor", None),
            P("section", "tensor", None, "dp"),
            P("section", None),
            P("section", "dp", "tensor"),
            P("section", "tensor", "dp"),
        ),
        check_vma=False,
    )
```

```python
import functools
import math

import jax
import jax.numpy as jnp
from jax import lax
from jax.experimental import pallas as pl
from jax.experimental.pallas import tpu as pltpu
from jax.sharding import PartitionSpec as P

F32 = jnp.float32
BF = jnp.bfloat16
NT = (((1,), (1,)), ((), ()))
NN = (((1,), (0,)), ((), ()))
TN = (((0,), (0,)), ((), ()))
MASKED = -1e30
SCENES = 3
MESH = pl.DeviceIdType.MESH
VM = pl.BlockSpec(memory_space=pltpu.VMEM)
HB = pl.BlockSpec(memory_space=pl.ANY)
DMA = pltpu.SemaphoreType.DMA
LIMIT = 58 << 20


def dg(a, b, dims):
    return lax.dot_general(a, b, dims, preferred_element_type=F32)


def chunks(rows):
    return 4 if rows % 64 == 0 else 1


def shape(dims, dtype):
    return jax.ShapeDtypeStruct(dims, dtype)


class Group:
    def __init__(self, size):
        self.size = size
        self.chips = size // 2
        self.me = lax.axis_index("tensor")
        self.chip = lax.div(self.me, 2)
        self.core = lax.rem(self.me, 2)
        self.sibling = self.chip * 2 + 1 - self.core

    def ahead(self, k):
        return lax.rem(self.chip + k, self.chips)

    def behind(self, k):
        return lax.rem(self.chip + self.chips - k, self.chips)

    def greet(self, replicas=0):
        barrier = pltpu.get_barrier_semaphore()
        targets = [self.sibling] + [self.ahead(k) * 2 + self.core for k in range(1, self.chips)]
        targets = [{"tensor": target} for target in targets]
        if replicas:
            d = lax.axis_index("dp")
            targets += [{"dp": lax.rem(d + k, replicas)} for k in range(1, replicas)]
            targets += [{"section": 1 - lax.axis_index("section")}]
        for target in targets:
            pl.semaphore_signal(barrier, inc=1, device_id=target, device_id_type=MESH)
        pl.semaphore_wait(barrier, len(targets))


def remote(src, dst, send, recv, target):
    return pltpu.make_async_remote_copy(
        src_ref=src,
        dst_ref=dst,
        send_sem=send,
        recv_sem=recv,
        device_id={"tensor": target},
        device_id_type=MESH,
    )


def span(j, rc):
    return pl.ds(pl.multiple_of(j * rc, rc), rc)


def comm_sems(group_size, n):
    c = group_size // 2
    far, near = DMA((max(c - 1, 1), n)), DMA((c, n))
    return [far, far, near, near]


class Gather:
    def __init__(self, g, buf, rc, sems):
        self.g, self.buf, self.rc = g, buf, rc
        self.far_send, self.far_recv, self.near_send, self.near_recv = sems

    def far(self, k, j, origin, target):
        ref = self.buf.at[origin, span(j, self.rc)]
        return remote(ref, ref, self.far_send.at[k - 1, j], self.far_recv.at[k - 1, j], target)

    def near(self, k, j, origin):
        ref = self.buf.at[origin, span(j, self.rc)]
        return remote(
            ref, ref, self.near_send.at[k, j], self.near_recv.at[k, j], self.g.sibling
        )

    def start(self, j):
        g = self.g
        for k in range(1, g.chips):
            self.far(k, j, g.me, g.ahead(k) * 2 + g.core).start()
        self.near(0, j, g.me).start()

    def relay(self, j):
        g = self.g
        for k in range(1, g.chips):
            origin = g.behind(k) * 2 + g.core
            self.far(k, j, origin, g.me).wait_recv()
            self.near(k, j, origin).start()

    def ready(self, j):
        g = self.g
        self.near(0, j, g.sibling).wait_recv()
        for k in range(1, g.chips):
            self.near(k, j, g.behind(k) * 2 + 1 - g.core).wait_recv()

    def drain(self, n):
        g = self.g

        def one(j, _):
            for k in range(1, g.chips):
                self.far(k, j, g.me, g.sibling).wait_send()
            for k in range(g.chips):
                self.near(k, j, g.me).wait_send()
            return 0

        lax.fori_loop(0, n, one, 0)


def scatter_scratch(group_size, rows, width, n):
    c = group_size // 2
    far = pltpu.VMEM((max(c - 1, 1), rows, width), BF)
    near = pltpu.VMEM((c, rows, width), BF)
    return [pltpu.VMEM((group_size, rows, width), F32), near, near, far, far] + comm_sems(
        group_size, n
    )


class Scatter:
    def __init__(self, g, rc, scratch):
        self.g, self.rc = g, rc
        self.part, self.near_out, self.near_in, self.far_out, self.far_in = scratch[:5]
        self.far_send, self.far_recv, self.near_send, self.near_recv = scratch[5:]

    def near(self, k, j):
        rows = span(j, self.rc)
        return remote(
            self.near_out.at[k, rows],
            self.near_in.at[k, rows],
            self.near_send.at[k, j],
            self.near_recv.at[k, j],
            self.g.sibling,
        )

    def far(self, k, j):
        rows = span(j, self.rc)
        return remote(
            self.far_out.at[k - 1, rows],
            self.far_in.at[k - 1, rows],
            self.far_send.at[k - 1, j],
            self.far_recv.at[k - 1, j],
            self.g.ahead(k) * 2 + self.g.core,
        )

    def first(self, j):
        g, rows = self.g, span(j, self.rc)
        for k in list(range(1, g.chips)) + [0]:
            owner = g.ahead(k) * 2 + 1 - g.core
            self.near_out[k, rows, :] = self.part[owner, rows, :].astype(BF)
            self.near(k, j).start()

    def second(self, j):
        g, rows = self.g, span(j, self.rc)
        for k in range(1, g.chips):
            owner = g.ahead(k) * 2 + g.core
            self.near(k, j).wait_recv()
            both = self.part[owner, rows, :] + self.near_in[k, rows, :].astype(F32)
            self.far_out[k - 1, rows, :] = both.astype(BF)
            self.far(k, j).start()

    def third(self, j):
        g, rows = self.g, span(j, self.rc)
        self.near(0, j).wait_recv()
        total = self.part[g.me, rows, :] + self.near_in[0, rows, :].astype(F32)
        for k in range(1, g.chips):
            self.far(k, j).wait_recv()
            total = total + self.far_in[k - 1, rows, :].astype(F32)
        return total

    def drain(self, n):
        g = self.g

        def one(j, _):
            for k in range(1, g.chips):
                self.far(k, j).wait_send()
            for k in range(g.chips):
                self.near(k, j).wait_send()
            return 0

        lax.fori_loop(0, n, one, 0)


class Spread:
    def __init__(self, src, dst, by_columns, sems):
        self.src, self.dst, self.by_columns = src, dst, by_columns
        self.own_sem, self.far_send, self.far_recv, self.side_send, self.side_recv = sems
        self.replicas = far = self.side_send.shape[0]
        self.s = lax.axis_index("section")
        self.d = lax.axis_index("dp")
        self.stages = [
            sorted({k, far - k}) for k in range(1, far // 2 + 1)
        ]

    def place(self, half, z):
        rows, cols = self.src.shape
        if self.by_columns:
            return self.dst.at[
                pl.ds(pl.multiple_of(half * rows, rows), rows),
                pl.ds(pl.multiple_of(z * cols, cols), cols),
            ]
        return self.dst.at[pl.ds(pl.multiple_of((2 * z + half) * rows, rows), rows)]

    def origin(self, k):
        return lax.rem(self.d + self.replicas - k, self.replicas)

    def own(self):
        return pltpu.make_async_copy(self.src, self.place(self.s, self.d), self.own_sem.at[0])

    def far(self, k, origin):
        return pltpu.make_async_remote_copy(
            src_ref=self.src,
            dst_ref=self.place(self.s, origin),
            send_sem=self.far_send.at[k - 1],
            recv_sem=self.far_recv.at[k - 1],
            device_id={"dp": lax.rem(self.d + k, self.replicas)},
            device_id_type=MESH,
        )

    def side(self, k, half):
        place = self.place(half, self.origin(k))
        return pltpu.make_async_remote_copy(
            src_ref=self.src if k == 0 else place,
            dst_ref=place,
            send_sem=self.side_send.at[k],
            recv_sem=self.side_recv.at[k],
            device_id={"section": 1 - self.s},
            device_id_type=MESH,
        )

    def start(self):
        for k in self.stages[0]:
            self.far(k, self.d).start()
        self.side(0, self.s).start()
        self.own().start()

    def step(self, i):
        for k in self.stages[i]:
            self.far(k, self.origin(k)).wait_recv()
            self.side(k, self.s).start()
        if i + 1 < len(self.stages):
            for k in self.stages[i + 1]:
                self.far(k, self.d).start()

    def finish(self):
        self.own().wait()
        for k in range(self.replicas):
            self.side(k, 1 - self.s).wait_recv()
        for k in range(1, self.replicas):
            self.far(k, self.d).wait_send()
        for k in range(self.replicas):
            self.side(k, self.s).wait_send()


def rider_sems(replicas):
    far, side = DMA((replicas - 1,)), DMA((replicas,))
    return [DMA((1,)), far, far, side, side]


class Riders:
    def __init__(self, srcs, dsts, columns, sems):
        self.all = [
            Spread(src, dst, by, sems[5 * i : 5 * i + 5])
            for i, (src, dst, by) in enumerate(zip(srcs, dsts, columns))
        ]
        self.replicas = self.all[0].replicas if self.all else 0

    def start(self):
        for one in self.all:
            one.start()

    def step(self, j, n):
        if not self.all:
            return
        stages = len(self.all[0].stages)
        for i in range(stages):

            @pl.when(j == n * (i + 1) // stages - 1)
            def _(i=i):
                for one in self.all:
                    one.step(i)

    def finish(self):
        for one in self.all:
            one.finish()


def riding(riders, replicas):
    halves = [half for half, _ in riders]
    columns = tuple(by for _, by in riders)
    outs = []
    for half, by in riders:
        rows, cols = half.shape
        outs.append(
            shape((2 * rows, replicas * cols) if by else (2 * replicas * rows, cols), BF)
        )
    sems = rider_sems(replicas) * len(riders)
    return halves, columns, outs, sems


def params(key):
    return pltpu.CompilerParams(
        vmem_limit_bytes=LIMIT, collective_id=key, has_side_effects=True
    )


def cost(flops, moved, exps=0):
    return pl.CostEstimate(flops=int(flops), bytes_accessed=int(moved), transcendentals=int(exps))


def normed(source):
    center = source - jnp.mean(source, axis=-1, keepdims=True)
    r = lax.rsqrt(jnp.mean(center * center, axis=-1, keepdims=True) + 1e-05)
    return center * r, r


def normed_back(source, gain, grad):
    n, r = normed(source)
    e = grad * gain
    dh = r * (
        e - jnp.mean(e, axis=-1, keepdims=True) - n * jnp.mean(e * n, axis=-1, keepdims=True)
    )
    return dh, jnp.sum(grad * n, axis=0, keepdims=True)


def flat(value):
    return value.reshape((value.shape[0] * value.shape[1],) + value.shape[2:])


def run(n, body):
    def one(j, carry):
        body(j)
        return carry

    lax.fori_loop(0, n, one, 0)


def qkv_kernel(size, layer, columns, fresh, *refs):
    m = len(columns)
    x_ref, gain_ref, w_ref = refs[:3]
    halves, refs = refs[3 : 3 + m], refs[3 + m :]
    qkv_ref, a1_out = refs[:2]
    wholes, refs = refs[2 : 2 + m], refs[2 + m :]
    if fresh:
        w_out, refs = refs[0], refs[1:]
    a1, w, w_sem, out_sem = refs[:4]
    sems, refs = refs[4:8], refs[8:]
    if fresh:
        spread_w, refs = Spread(w_ref, w, False, refs[:5]), refs[5:]
    riders = Riders(halves, wholes, columns, refs)
    rows, width = x_ref.shape
    n = chunks(rows)
    rc = rows // n
    g = Group(size)
    if not fresh:
        copy = pltpu.make_async_copy(w_ref, w, w_sem.at[0])
        copy.start()
    else:
        riders.all.insert(0, spread_w)
        riders.replicas = spread_w.replicas
    g.greet(riders.replicas)
    gather = Gather(g, a1, rc, sems)
    riders.start()

    def send(j):
        at = span(j, rc)
        a = normed(x_ref[at, :].astype(F32))[0] * gain_ref[layer : layer + 1, :]
        a1[g.me, at, :] = a.astype(BF)
        gather.start(j)

    run(n, send)

    def multiply(j):
        at = span(j, rc)
        gather.ready(j)
        r = dg(flat(a1[:, at, :]), w[...], NN).astype(BF)
        qkv_ref[:, at, :] = r.reshape(size, rc, r.shape[1])

    if fresh:

        def relay(j):
            gather.relay(j)
            riders.step(j, n)

        run(n, relay)
        riders.finish()
        outs = [
            pltpu.make_async_copy(w, w_out, w_sem.at[0]),
            pltpu.make_async_copy(a1, a1_out, out_sem.at[0]),
        ]
        outs[0].start()
        run(n, multiply)
        outs[1].start()
    else:
        copy.wait()

        def work(j):
            gather.relay(j)
            multiply(j)
            riders.step(j, n)

        run(n, work)
        outs = [pltpu.make_async_copy(a1, a1_out, out_sem.at[0])]
        outs[0].start()
        riders.finish()
    gather.drain(n)
    for out in outs:
        out.wait()


def qkv_forward(size, replicas, layer, x, gains, w, riders, fresh):
    rows, width = x.shape
    wide = w.shape[1]
    n = chunks(rows)
    halves, columns, outs, sems = riding(riders, replicas)
    extra = [shape((width, wide), BF)] if fresh else []
    return pl.pallas_call(
        functools.partial(qkv_kernel, size, layer, columns, fresh),
        out_shape=[
            shape((size, rows, wide), BF),
            shape((size, rows, width), BF),
        ]
        + outs
        + extra,
        in_specs=[VM, VM, HB] + [HB] * len(riders),
        out_specs=[VM, HB] + [HB] * (len(outs) + len(extra)),
        scratch_shapes=[
            pltpu.VMEM((size, rows, width), BF),
            pltpu.VMEM((width, wide), BF),
            DMA((1,)),
            DMA((1,)),
        ]
        + comm_sems(size, n)
        + (rider_sems(replicas) if fresh else [])
        + sems,
        compiler_params=params(layer),
        cost_estimate=cost(20e9, 30e6),
    )(x, gains, w, *halves)


def attend_kernel(size, layer, columns, *refs):
    m = len(columns)
    qkv_ref, qm_ref, km_ref, x_ref, w_ref = refs[:5]
    halves, refs = refs[5 : 5 + m], refs[5 + m :]
    h1_ref, ctx_ref, lse_ref = refs[:3]
    wholes, refs = refs[3 : 3 + m], refs[3 + m :]
    ka, vt, w, w_sem = refs[:4]
    scratch, refs = refs[4:13], refs[13:]
    riders = Riders(halves, wholes, columns, refs)
    _, rows, wide = qkv_ref.shape
    length = size * rows
    e = qm_ref.shape[2]
    heads = wide // (3 * e)
    c = e**-0.5 * math.log2(math.e)
    n = chunks(rows)
    rc = rows // n
    bq = size * rc
    kc = bq
    g = Group(size)
    copy = pltpu.make_async_copy(w_ref, w, w_sem.at[0])
    copy.start()
    g.greet(riders.replicas)
    riders.start()
    scatter = Scatter(g, rc, scratch)
    whole = flat(qkv_ref[...])
    for h in range(heads):
        o = 3 * e * h
        ka[h, :, :e] = whole[:, o + e : o + 2 * e]
        ka[h, :, e:] = flat(km_ref[...])
        vt[h, :e, :] = whole[:, o + 2 * e : o + 3 * e].T
        vt[h, e:, :] = jnp.ones((16, length), BF)
    copy.wait()

    def work(j):
        at = span(j, rc)
        qm = flat(qm_ref[:, at, :])
        found = []
        held_qkv = flat(qkv_ref[:, at, :])
        for h in range(heads):
            o = 3 * e * h
            q = jnp.concatenate([held_qkv[:, o : o + e], qm], axis=1)
            held = []
            top = None
            for k in range(length // kc):
                s = dg(ka[h, k * kc : (k + 1) * kc, :], q, NT)
                t = jnp.max(s, axis=0, keepdims=True)
                top = t if top is None else jnp.maximum(top, t)
                held.append(s)
            top = top * c
            acc = None
            for k in range(length // kc):
                p = jnp.exp2(held[k] * c - top).astype(BF)
                a = dg(vt[h, :, k * kc : (k + 1) * kc], p, NN)
                acc = a if acc is None else acc + a
            total = acc[e : e + 1]
            found.append((acc[:e] * (1.0 / total)).astype(BF))
            lse_ref[j, h : h + 1, :] = top + jnp.log2(total)
        ctx = (jnp.concatenate(found, axis=0) if heads > 1 else found[0]).T
        ctx_ref[:, at, :] = ctx.reshape(size, rc, heads * e)
        width = x_ref.shape[1]
        scatter.part[:, at, :] = dg(ctx, w[...], NN).reshape(size, rc, width)
        scatter.first(j)
        scatter.second(j)
        riders.step(j, n)

    run(n, work)

    def last(j):
        at = span(j, rc)
        h1_ref[at, :] = x_ref[at, :].astype(F32) + scatter.third(j)

    run(n, last)
    scatter.drain(n)
    riders.finish()


def attend(size, replicas, layer, qkv, qm, km, x, w, riders):
    _, rows, wide = qkv.shape
    e = qm.shape[2]
    heads = wide // (3 * e)
    width = x.shape[1]
    n = chunks(rows)
    halves, columns, outs, sems = riding(riders, replicas)
    return pl.pallas_call(
        functools.partial(attend_kernel, size, layer, columns),
        out_shape=[
            shape((rows, width), F32),
            shape((size, rows, heads * e), BF),
            shape((n, heads, size * rows // n), F32),
        ]
        + outs,
        in_specs=[VM, VM, VM, VM, HB] + [HB] * len(riders),
        out_specs=[VM, VM, VM] + [HB] * len(outs),
        scratch_shapes=[
            pltpu.VMEM((heads, size * rows, 2 * e), BF),
            pltpu.VMEM((heads, e + 16, size * rows), BF),
            pltpu.VMEM((heads * e, width), BF),
            DMA((1,)),
        ]
        + scatter_scratch(size, rows, width, n)
        + sems,
        compiler_params=params(2 + layer),
        cost_estimate=cost(60e9, 20e6),
    )(qkv, qm, km, x, w, *halves)


def mlp_kernel(size, layer, columns, *refs):
    m = len(columns)
    h1_ref, gain_ref, wu_ref, wd_ref = refs[:4]
    halves, refs = refs[4 : 4 + m], refs[4 + m :]
    y_ref, a2_out, hid_out, slope_out = refs[:4]
    wholes, refs = refs[4 : 4 + m], refs[4 + m :]
    a2, hid, slope, wu, wd, w_sem, out_sem = refs[:7]
    scratch, refs = refs[7:20], refs[20:]
    riders = Riders(halves, wholes, columns, refs)
    rows, width = h1_ref.shape
    hidden = wu_ref.shape[1]
    fb = min(256, hidden)
    n = chunks(rows)
    rc = rows // n
    g = Group(size)
    copies = [
        pltpu.make_async_copy(wu_ref, wu, w_sem.at[0]),
        pltpu.make_async_copy(wd_ref, wd, w_sem.at[1]),
    ]
    for copy in copies:
        copy.start()
    g.greet(riders.replicas)
    gather = Gather(g, a2, rc, scratch[:4])
    scatter = Scatter(g, rc, scratch[4:])

    def send(j):
        at = span(j, rc)
        a = normed(h1_ref[at, :])[0] * gain_ref[layer : layer + 1, :]
        a2[g.me, at, :] = a.astype(BF)
        gather.start(j)

    run(n, send)
    riders.start()
    for copy in copies:
        copy.wait()

    def work(j):
        at = span(j, rc)
        gather.relay(j)
        gather.ready(j)
        a = flat(a2[:, at, :])
        for f in range(hidden // fb):
            cols = slice(f * fb, (f + 1) * fb)
            u = dg(a, wu[:, cols], NN)
            half = 0.5 + 0.5 * lax.erf(u * (0.5**0.5))
            slope[:, at, cols] = (
                (half + u * jnp.exp(-0.5 * u * u) * ((2 * math.pi) ** -0.5))
                .astype(BF)
                .reshape(size, rc, fb)
            )
            hid[:, at, cols] = (u * half).astype(BF).reshape(size, rc, fb)
        held = flat(hid[:, at, :])
        for f in range(width // 256):
            cols = slice(f * 256, (f + 1) * 256)
            scatter.part[:, at, cols] = dg(held, wd[:, cols], NN).reshape(size, rc, 256)
        scatter.first(j)
        scatter.second(j)
        riders.step(j, n)

    run(n, work)
    outs = [
        pltpu.make_async_copy(a2, a2_out, out_sem.at[0]),
        pltpu.make_async_copy(hid, hid_out, out_sem.at[1]),
        pltpu.make_async_copy(slope, slope_out, out_sem.at[2]),
    ]
    for out in outs:
        out.start()

    def last(j):
        at = span(j, rc)
        y_ref[at, :] = (h1_ref[at, :] + scatter.third(j)).astype(BF)

    run(n, last)
    riders.finish()
    gather.drain(n)
    scatter.drain(n)
    for out in outs:
        out.wait()


def mlp_forward(size, replicas, layer, h1, gains, wu, wd, riders):
    rows, width = h1.shape
    hidden = wu.shape[1]
    n = chunks(rows)
    halves, columns, outs, sems = riding(riders, replicas)
    return pl.pallas_call(
        functools.partial(mlp_kernel, size, layer, columns),
        out_shape=[
            shape((rows, width), BF),
            shape((size, rows, width), BF),
            shape((size, rows, hidden), BF),
            shape((size, rows, hidden), BF),
        ]
        + outs,
        in_specs=[VM, VM, HB, HB] + [HB] * len(riders),
        out_specs=[VM, HB, HB, HB] + [HB] * len(outs),
        scratch_shapes=[
            pltpu.VMEM((size, rows, width), BF),
            pltpu.VMEM((size, rows, hidden), BF),
            pltpu.VMEM((size, rows, hidden), BF),
            pltpu.VMEM((width, hidden), BF),
            pltpu.VMEM((hidden, width), BF),
            DMA((2,)),
            DMA((3,)),
        ]
        + comm_sems(size, n)
        + scatter_scratch(size, rows, width, n)
        + sems,
        compiler_params=params(4 + layer),
        cost_estimate=cost(50e9, 30e6),
    )(h1, gains, wu, wd, *halves)


def mlp_back_kernel(
    size, layer, parts, g_ref, h1_ref, gain_ref, a2_ref, hid_ref, slope_ref, wu_ref, wd_ref,
    mid_ref, gain_out, gup_ref, gdown_ref,
    grad, a2, hid, dup, wu, wd, w_sem, *scratch
):
    rows, width = h1_ref.shape
    hidden = wu_ref.shape[1]
    depth = width // parts
    fb = min(256, hidden)
    n = chunks(rows)
    rc = rows // n
    g = Group(size)
    copies = [
        pltpu.make_async_copy(wd_ref, wd, w_sem.at[0]),
        pltpu.make_async_copy(slope_ref, dup, w_sem.at[1]),
        pltpu.make_async_copy(wu_ref, wu, w_sem.at[2]),
    ]
    late = [
        pltpu.make_async_copy(hid_ref, hid, w_sem.at[3]),
        pltpu.make_async_copy(a2_ref, a2, w_sem.at[4]),
    ]
    for copy in copies + late:
        copy.start()
    g.greet()
    gather = Gather(g, grad, rc, scratch[:4])
    scatter = Scatter(g, rc, scratch[4:])

    def send(j):
        at = span(j, rc)
        grad[g.me, at, :] = g_ref[at, :]
        gather.start(j)

    run(n, send)
    for copy in copies:
        copy.wait()

    def work(j):
        at = span(j, rc)
        gather.relay(j)
        gather.ready(j)
        held = flat(grad[:, at, :])
        for f in range(hidden // fb):
            cols = slice(f * fb, (f + 1) * fb)
            d = dg(held, wd[cols, :], NT) * flat(dup[:, at, cols]).astype(F32)
            dup[:, at, cols] = d.astype(BF).reshape(size, rc, fb)
        held = flat(dup[:, at, :])
        for z in range(parts):
            cols = slice(z * depth, (z + 1) * depth)
            scatter.part[:, at, cols] = dg(held, wu[cols, :], NT).reshape(size, rc, depth)
        scatter.first(j)
        scatter.second(j)

    run(n, work)
    for copy in late:
        copy.wait()

    def up_grad(z):
        cols = pl.ds(pl.multiple_of(z * depth, depth), depth)
        gup_ref[z] = dg(flat(a2[:, :, cols]), flat(dup[...]), TN).astype(BF)

    run(parts, up_grad)

    def down_grad(f):
        cols = pl.ds(pl.multiple_of(f * fb, fb), fb)
        r = dg(flat(hid[:, :, cols]), flat(grad[...]), TN).astype(BF)
        for z in range(parts):
            gdown_ref[z, cols, :] = r[:, z * depth : (z + 1) * depth]

    run(hidden // fb, down_grad)
    gain_out[...] = jnp.zeros_like(gain_out)

    def last(j):
        at = span(j, rc)
        dh, dgain = normed_back(h1_ref[at, :], gain_ref[layer : layer + 1, :], scatter.third(j))
        mid_ref[at, :] = g_ref[at, :].astype(F32) + dh
        gain_out[...] += dgain

    run(n, last)
    gather.drain(n)
    scatter.drain(n)


def mlp_backward(size, replicas, layer, grad, h1, gains, a2, hid, slope, wu, wd):
    rows, width = h1.shape
    hidden = wu.shape[1]
    parts, depth = replicas, width // replicas
    n = chunks(rows)
    return pl.pallas_call(
        functools.partial(mlp_back_kernel, size, layer, parts),
        out_shape=(
            shape((rows, width), F32),
            shape((1, width), F32),
            shape((parts, depth, hidden), BF),
            shape((parts, hidden, depth), BF),
        ),
        in_specs=[VM, VM, VM, HB, HB, HB, HB, HB],
        out_specs=(VM, VM, VM, VM),
        scratch_shapes=[
            pltpu.VMEM((size, rows, width), BF),
            pltpu.VMEM((size, rows, width), BF),
            pltpu.VMEM((size, rows, hidden), BF),
            pltpu.VMEM((size, rows, hidden), BF),
            pltpu.VMEM((width, hidden), BF),
            pltpu.VMEM((hidden, width), BF),
            DMA((5,)),
        ]
        + comm_sems(size, n)
        + scatter_scratch(size, rows, width, n),
        compiler_params=params(6 + layer),
        cost_estimate=cost(60e9, 40e6),
    )(grad, h1, gains, a2, hid, slope, wu, wd)


def attend_back_kernel(
    size, layer, parts, mid_ref, qkv_ref, qm_ref, km_ref, ctx_ref, lse_ref, w_ref,
    dqkv_ref, gout_ref, da, ka, va, kt, dk, dv, w, w_sem, *sems
):
    _, rows, wide = qkv_ref.shape
    length = size * rows
    e = qm_ref.shape[2]
    heads = wide // (3 * e)
    scale = e**-0.5
    c = scale * math.log2(math.e)
    depth = w_ref.shape[1] // parts
    n = chunks(rows)
    rc = rows // n
    bq = size * rc
    kc = bq
    g = Group(size)
    copies = [pltpu.make_async_copy(w_ref, w, w_sem.at[0])]
    for copy in copies:
        copy.start()
    g.greet()
    gather = Gather(g, da, rc, sems)

    def send(j):
        at = span(j, rc)
        da[g.me, at, :] = mid_ref[at, :].astype(BF)
        gather.start(j)

    run(n, send)
    lane = lax.broadcasted_iota(jnp.int32, (length, e), 1)
    whole = flat(qkv_ref[...])
    for h in range(heads):
        o = 3 * e * h
        ka[h, :, :e] = whole[:, o + e : o + 2 * e]
        ka[h, :, e:] = flat(km_ref[...])
        va[h, :, :e] = whole[:, o + 2 * e : o + 3 * e]
        va[h, :, e:] = jnp.where(lane < 3, 1.0, 0.0).astype(BF)
        kt[h] = whole[:, o + e : o + 2 * e].T
    dk[...] = jnp.zeros_like(dk)
    dv[...] = jnp.zeros_like(dv)
    ql = lax.broadcasted_iota(jnp.int32, (bq, e), 1)
    for copy in copies:
        copy.wait()

    def work(j):
        at = span(j, rc)
        gather.relay(j)
        gather.ready(j)
        qm = flat(qm_ref[:, at, :])
        dctx = dg(flat(da[:, at, :]), w[...], NT).astype(BF)
        ctx = flat(ctx_ref[:, at, :])
        held_qkv = flat(qkv_ref[:, at, :])
        for h in range(heads):
            o = 3 * e * h
            qq = held_qkv[:, o : o + e]
            q = jnp.concatenate([qq, qm], axis=1)
            dc = dctx[:, h * e : (h + 1) * e]
            prod = dc.astype(F32) * ctx[:, h * e : (h + 1) * e].astype(F32)
            d = -jnp.sum(prod, axis=1, keepdims=True)
            d1 = d.astype(BF).astype(F32)
            d2 = (d - d1).astype(BF).astype(F32)
            d3 = d - d1 - d2
            ds_col = jnp.where(ql == 0, d1, jnp.where(ql == 1, d2, jnp.where(ql == 2, d3, 0.0)))
            dca = jnp.concatenate([dc, ds_col.astype(BF)], axis=1)
            lse = lse_ref[j, h : h + 1, :]
            dqt = None
            for k in range(length // kc):
                ks = slice(k * kc, (k + 1) * kc)
                s = dg(ka[h, ks, :], q, NT)
                p = jnp.exp2(s * c - lse)
                ds = (p * dg(va[h, ks, :], dca, NT)).astype(BF)
                dv[h, ks, :] += dg(p.astype(BF), dc, NN)
                dk[h, ks, :] += dg(ds, qq, NN)
                a = dg(kt[h, :, ks], ds, NN)
                dqt = a if dqt is None else dqt + a
            dqkv_ref[:, at, o : o + e] = (dqt * scale).T.astype(BF).reshape(size, rc, e)

    run(n, work)
    for h in range(heads):
        o = 3 * e * h
        dqkv_ref[:, :, o + e : o + 2 * e] = (dk[h] * scale).astype(BF).reshape(size, rows, e)
        dqkv_ref[:, :, o + 2 * e : o + 3 * e] = dv[h].astype(BF).reshape(size, rows, e)

    def out_grad(z):
        cols = pl.ds(pl.multiple_of(z * depth, depth), depth)
        gout_ref[z] = dg(flat(ctx_ref[...]), flat(da[:, :, cols]), TN).astype(BF)

    run(parts, out_grad)
    gather.drain(n)


def attend_backward(size, replicas, layer, mid, qkv, qm, km, ctx, lse, w):
    _, rows, wide = qkv.shape
    e = qm.shape[2]
    heads = wide // (3 * e)
    width = mid.shape[1]
    parts, depth = replicas, width // replicas
    length = size * rows
    n = chunks(rows)
    return pl.pallas_call(
        functools.partial(attend_back_kernel, size, layer, parts),
        out_shape=(shape(qkv.shape, BF), shape((parts, heads * e, depth), BF)),
        in_specs=[VM] * 6 + [HB],
        out_specs=(VM, VM),
        scratch_shapes=[
            pltpu.VMEM((size, rows, width), BF),
            pltpu.VMEM((heads, length, 2 * e), BF),
            pltpu.VMEM((heads, length, 2 * e), BF),
            pltpu.VMEM((heads, e, length), BF),
            pltpu.VMEM((heads, length, e), F32),
            pltpu.VMEM((heads, length, e), F32),
            pltpu.VMEM((heads * e, width), BF),
            DMA((1,)),
        ]
        + comm_sems(size, n),
        compiler_params=params(8 + layer),
        cost_estimate=cost(90e9, 40e6),
    )(mid, qkv, qm, km, ctx, lse, w)


def qkv_back_kernel(
    size, layer, parts, dqkv_ref, a1_ref, x_ref, mid_ref, gain_ref, w_ref,
    dx_ref, gain_out, gqkv_ref, w, w_sem, *scratch
):
    rows, width = x_ref.shape
    depth = width // parts
    n = chunks(rows)
    rc = rows // n
    g = Group(size)
    copies = [pltpu.make_async_copy(w_ref, w, w_sem.at[0])]
    for copy in copies:
        copy.start()
    g.greet()
    scatter = Scatter(g, rc, scratch)
    for copy in copies:
        copy.wait()

    def work(j):
        at = span(j, rc)
        held = flat(dqkv_ref[:, at, :])
        for z in range(parts):
            cols = slice(z * depth, (z + 1) * depth)
            scatter.part[:, at, cols] = dg(held, w[cols, :], NT).reshape(size, rc, depth)
        scatter.first(j)
        scatter.second(j)

    run(n, work)

    def qkv_grad(z):
        cols = pl.ds(pl.multiple_of(z * depth, depth), depth)
        gqkv_ref[z] = dg(flat(a1_ref[:, :, cols]), flat(dqkv_ref[...]), TN).astype(BF)

    run(parts, qkv_grad)
    gain_out[...] = jnp.zeros_like(gain_out)

    def last(j):
        at = span(j, rc)
        dh, dgain = normed_back(
            x_ref[at, :].astype(F32), gain_ref[layer : layer + 1, :], scatter.third(j)
        )
        dx_ref[at, :] = (mid_ref[at, :] + dh).astype(BF)
        gain_out[...] += dgain

    run(n, last)
    scatter.drain(n)


def qkv_backward(size, replicas, layer, dqkv, a1, x, mid, gains, w):
    rows, width = x.shape
    wide = w.shape[1]
    parts, depth = replicas, width // replicas
    n = chunks(rows)
    return pl.pallas_call(
        functools.partial(qkv_back_kernel, size, layer, parts),
        out_shape=(
            shape((rows, width), BF),
            shape((1, width), F32),
            shape((parts, depth, wide), BF),
        ),
        in_specs=[VM] * 5 + [HB],
        out_specs=(VM, VM, VM),
        scratch_shapes=[
            pltpu.VMEM((width, wide), BF),
            DMA((1,)),
        ]
        + scatter_scratch(size, rows, width, n),
        compiler_params=params(11),
        cost_estimate=cost(30e9, 30e6),
    )(dqkv, a1, x, mid, gains, w)


def far_copy(src, dst, send, recv, target):
    return pltpu.make_async_remote_copy(
        src_ref=src, dst_ref=dst, send_sem=send, recv_sem=recv, device_id=target,
        device_id_type=MESH,
    )


def last_kernel(
    size, parts, dqkv_ref, a1_ref, x_ref, mid_ref, gain_ref, w_ref, two_ref, above_ref,
    dx_ref, gain_out, gqkv_ref,
    w, own, away, came, over, back, gsum, gcame, w_sem,
    z_send, z_recv, y_send, y_recv, g_send, g_recv, *scratch
):
    rows, width = x_ref.shape
    depth = width // parts
    half = depth // 2
    n = chunks(rows)
    rc = rows // n
    g = Group(size)
    section = lax.axis_index("section")
    d = lax.axis_index("dp")
    copy = pltpu.make_async_copy(w_ref, w, w_sem.at[0])
    copy.start()
    g.greet(parts)
    scatter = Scatter(g, rc, scratch)

    def block(z):
        cols = pl.ds(pl.multiple_of(z * depth, depth), depth)
        return dg(flat(a1_ref[:, :, cols]), flat(dqkv_ref[...]), TN)

    def z_copy(k, i):
        part = pl.ds(pl.multiple_of(i * half, half), half)
        return far_copy(
            away.at[k - 1, part], came.at[k - 1, part], z_send.at[k - 1, i], z_recv.at[k - 1, i],
            {"dp": lax.rem(d + k, parts)},
        )

    def y_copy(i):
        part = pl.ds(pl.multiple_of(i * half, half), half)
        return far_copy(
            over.at[part], back.at[part], y_send.at[i], y_recv.at[i], {"section": 1 - section}
        )

    def send(i):
        k = i + 1
        away[i] = block(lax.rem(d + k, parts)).astype(BF)
        z_copy(k, 0).start()
        z_copy(k, 1).start()

    run(parts - 1, send)
    copy.wait()

    def work(j):
        at = span(j, rc)
        held = flat(dqkv_ref[:, at, :])
        for z in range(parts):
            cols = slice(z * depth, (z + 1) * depth)
            scatter.part[:, at, cols] = dg(held, w[cols, :], NT).reshape(size, rc, depth)
        scatter.first(j)
        scatter.second(j)

    run(n, work)
    own[...] = block(d)
    gsum[0] = jnp.zeros_like(gsum[0])

    def last(j):
        at = span(j, rc)
        dh, dgain = normed_back(x_ref[at, :].astype(F32), gain_ref[0:1, :], scatter.third(j))
        dx_ref[at, :] = (mid_ref[at, :] + dh).astype(BF)
        gsum[0, 0:1, :] += dgain

    run(n, last)
    gsum[0, 1:2, :] = two_ref[...]
    gsum[0, 2:4, :] = above_ref[...]

    targets = [
        [{"tensor": g.sibling}],
        [{"tensor": g.ahead(k) * 2 + g.core} for k in range(1, g.chips)],
        [{"dp": lax.rem(d + k, parts)} for k in range(1, parts)],
        [{"section": 1 - section}],
    ]
    slot = 0
    sent = []

    def exchange(stage):
        nonlocal slot
        copies = []
        for target in targets[stage]:
            copies.append(
                far_copy(gsum.at[stage], gcame.at[slot], g_send.at[slot], g_recv.at[slot], target)
            )
            copies[-1].start()
            slot += 1
        total = gsum[stage]
        for i, copy in enumerate(copies):
            copy.wait_recv()
            total = total + gcame[slot - len(copies) + i]
        gsum[stage + 1] = total
        sent.extend(copies)

    exchange(0)
    exchange(1)

    def collect(i):
        part = pl.ds(pl.multiple_of(i * half, half), half)
        total = own[part, :]
        for k in range(1, parts):
            z_copy(k, i).wait_recv()
            total = total + came[k - 1, part, :].astype(F32)
        own[part, :] = total
        over[part, :] = total.astype(BF)

        @pl.when(section == 1)
        def _():
            y_copy(i).start()

    run(2, collect)
    exchange(2)
    exchange(3)
    gain_out[...] = gsum[4]

    @pl.when(section == 0)
    def _():
        y_copy(0).wait_recv()
        y_copy(1).wait_recv()

    gqkv_ref[...] = own[...] + back[...].astype(F32)

    @pl.when(section == 1)
    def _():
        y_copy(0).wait_send()
        y_copy(1).wait_send()

    for copy in sent:
        copy.wait_send()
    for k in range(1, parts):
        z_copy(k, 0).wait_send()
        z_copy(k, 1).wait_send()
    scatter.drain(n)


def last_backward(size, replicas, dqkv, a1, x, mid, gains, w, two, above):
    rows, width = x.shape
    wide = w.shape[1]
    depth = width // replicas
    n = chunks(rows)
    slots = 1 + (size // 2 - 1) + (replicas - 1) + 1
    return pl.pallas_call(
        functools.partial(last_kernel, size, replicas),
        out_shape=(
            shape((rows, width), BF),
            shape((8, width), F32),
            shape((depth, wide), F32),
        ),
        in_specs=[VM] * 5 + [HB, VM, VM],
        out_specs=(VM, VM, VM),
        scratch_shapes=[
            pltpu.VMEM((width, wide), BF),
            pltpu.VMEM((depth, wide), F32),
            pltpu.VMEM((replicas - 1, depth, wide), BF),
            pltpu.VMEM((replicas - 1, depth, wide), BF),
            pltpu.VMEM((depth, wide), BF),
            pltpu.VMEM((depth, wide), BF),
            pltpu.VMEM((5, 8, width), F32),
            pltpu.VMEM((slots, 8, width), F32),
            DMA((1,)),
            DMA((replicas - 1, 2)),
            DMA((replicas - 1, 2)),
            DMA((2,)),
            DMA((2,)),
            DMA((slots,)),
            DMA((slots,)),
        ]
        + scatter_scratch(size, rows, width, n),
        compiler_params=params(10),
        cost_estimate=cost(40e9, 30e6),
    )(dqkv, a1, x, mid, gains, w, two, above)


def scene_masks(segments, e):
    same = (segments[..., None] == jnp.arange(e, dtype=jnp.int32)).astype(F32)
    used = jnp.arange(e) < SCENES
    return (
        jnp.where(used, same * MASKED, 0.0).astype(BF),
        jnp.where(used, 1.0 - same, 0.0).astype(BF),
    )


def swap_section(value):
    return lax.ppermute(value, "section", [(0, 1), (1, 0)])


def shards(
    block_input,
    segment_ids,
    cotangent,
    norm_one_gain,
    qkv_weight,
    out_weight,
    norm_two_gain,
    up_weight,
    down_weight,
):
    section = lax.axis_index("section")
    size = lax.axis_size("tensor")
    replicas = lax.axis_size("dp")

    mine = [
        qkv_weight[0].reshape((qkv_weight.shape[1], -1)),
        out_weight[0].reshape((-1, out_weight.shape[3])),
        up_weight[0],
        down_weight[0],
    ]
    def halves(w):
        w = w.astype(BF).reshape((2, -1, w.shape[1]))
        keep = jnp.where(section == 0, w[0], w[1])
        other = swap_section(jnp.where(section == 0, w[1], w[0]))
        return [jnp.where(section == layer, keep, other) for layer in range(2)]

    h_qkv, h_out, h_up, h_down = [halves(w) for w in mine]
    gains_mine = jnp.concatenate([norm_one_gain, norm_two_gain], axis=0)
    gains_other = swap_section(gains_mine)
    gains = [jnp.where(section == layer, gains_mine, gains_other) for layer in range(2)]
    gains_one = jnp.stack([gains[0][0], gains[1][0]])
    gains_two = jnp.stack([gains[0][1], gains[1][1]])
    segments = lax.dynamic_index_in_dim(segment_ids, section, 0, keepdims=False)
    x = lax.dynamic_index_in_dim(block_input, section, 0, keepdims=False)
    head_dim = qkv_weight.shape[3] // 3
    qm, km = scene_masks(segments.reshape((size, -1)), head_dim)
    qkv, a1, w_out_0, w_qkv_0 = qkv_forward(
        size, replicas, 0, x, gains_one, h_qkv[0], [(h_out[0], True)], True
    )
    h1, ctx, lse, w_up_0, w_down_0 = attend(
        size, replicas, 0, qkv, qm, km, x, w_out_0, [(h_up[0], False), (h_down[0], True)]
    )
    y0, a2, hid, slope, w_qkv_1, w_out_1 = mlp_forward(
        size, replicas, 0, h1, gains_two, w_up_0, w_down_0, [(h_qkv[1], False), (h_out[1], True)]
    )
    kept = [(x, a1, qkv, ctx, lse, h1, a2, hid, slope)]
    qkv, a1, w_up_1 = qkv_forward(
        size, replicas, 1, y0, gains_one, w_qkv_1, [(h_up[1], False)], False
    )
    h1, ctx, lse, w_down_1 = attend(
        size, replicas, 1, qkv, qm, km, y0, w_out_1, [(h_down[1], True)]
    )
    y1, a2, hid, slope = mlp_forward(size, replicas, 1, h1, gains_two, w_up_1, w_down_1, [])
    kept.append((y0, a1, qkv, ctx, lse, h1, a2, hid, slope))
    ys = [y0, y1]
    weights = [
        (w_qkv_0, w_out_0, w_up_0, w_down_0),
        (w_qkv_1, w_out_1, w_up_1, w_down_1),
    ]
    other_y = swap_section(jnp.where(section == 0, ys[1], ys[0]))
    grad = lax.dynamic_index_in_dim(cotangent, section, 0, keepdims=False)
    dxs = [None, None]

    def reduce_rows(value):
        return lax.psum_scatter(value, "dp", scatter_dimension=0, tiled=False)

    for layer in (1, 0):
        x, a1, qkv, ctx, lse, h1, a2, hid, slope = kept[layer]
        w_qkv, w_out, w_up, w_down = weights[layer]
        mid, gain_two, g_up, g_down = mlp_backward(
            size, replicas, layer, grad, h1, gains_two, a2, hid, slope, w_up, w_down
        )
        if layer == 0:
            mid, sums = lax.optimization_barrier((mid, sums))
        d_qkv, g_out = attend_backward(size, replicas, layer, mid, qkv, qm, km, ctx, lse, w_out)
        up, down = reduce_rows(g_up), reduce_rows(g_down)
        if layer == 1:
            grad, gain_one, g_qkv = qkv_backward(
                size, replicas, layer, d_qkv, a1, x, mid, gains_one, w_qkv
            )
            gains_above = jnp.concatenate([gain_one, gain_two], axis=0)
            grad, up, down = lax.optimization_barrier((grad, up, down))
            sums = [reduce_rows(g_qkv), reduce_rows(g_out), up, down]
        else:
            d_qkv, g_out, up, down = lax.optimization_barrier((d_qkv, g_out, up, down))
            grad, gains, qkv_grad = last_backward(
                size, replicas, d_qkv, a1, x, mid, gains_one, w_qkv, gain_two, gains_above
            )
            lower = [None, reduce_rows(g_out), up, down]
        dxs[layer] = grad
    other_dx = swap_section(jnp.where(section == 0, dxs[1], dxs[0]))

    def own_layer(mine, other):
        first = jnp.where(section == 0, mine, other)
        second = jnp.where(section == 0, other, mine)
        return jnp.stack([first, second])[None]

    layer_out = own_layer(jnp.where(section == 0, ys[0], ys[1]), other_y)
    input_out = own_layer(jnp.where(section == 0, dxs[0], dxs[1]), other_dx)

    def finish(zero, one):
        send = swap_section(jnp.where(section == 0, one, zero))
        return jnp.where(section == 0, zero, one).astype(F32) + send.astype(F32)

    qkv_grad = jnp.where(
        section == 0, qkv_grad, sums[0].astype(F32) + swap_section(sums[0]).astype(F32)
    )
    out_grad, up_grad, down_grad = [finish(a, b) for a, b in zip(lower[1:], sums[1:])]
    gains = lax.dynamic_slice_in_dim(gains, 2 * section, 2, 0)
    return (
        layer_out,
        input_out,
        gains[0:1],
        qkv_grad.reshape(qkv_weight.shape),
        out_grad.reshape(out_weight.shape),
        gains[1:2],
        up_grad[None],
        down_grad[None],
    )


def solution(mesh):
    return jax.shard_map(
        shards,
        mesh=mesh,
        in_specs=(
            P(None, ("dp", "tensor"), None),
            P(None, "dp"),
            P(None, ("dp", "tensor"), None),
            P("section", None),
            P("section", "dp", "tensor", None),
            P("section", "tensor", None, "dp"),
            P("section", None),
            P("section", "dp", "tensor"),
            P("section", "tensor", "dp"),
        ),
        out_specs=(
            P("section", None, ("dp", "tensor"), None),
            P("section", None, ("dp", "tensor"), None),
            P("section", None),
            P("section", "dp", "tensor", None),
            P("section", "tensor", None, "dp"),
            P("section", None),
            P("section", "dp", "tensor"),
            P("section", "tensor", "dp"),
        ),
        check_vma=False,
    )
```

```python
import functools
import math

import jax
import jax.numpy as jnp
from jax import lax
from jax.experimental import pallas as pl
from jax.experimental.pallas import tpu as pltpu
from jax.sharding import PartitionSpec as P

F32 = jnp.float32
BF = jnp.bfloat16
NT = (((1,), (1,)), ((), ()))
NN = (((1,), (0,)), ((), ()))
TN = (((0,), (0,)), ((), ()))
MASKED = -1e30
SCENES = 3
MESH = pl.DeviceIdType.MESH
VM = pl.BlockSpec(memory_space=pltpu.VMEM)
HB = pl.BlockSpec(memory_space=pl.ANY)
DMA = pltpu.SemaphoreType.DMA
LIMIT = 58 << 20


def dg(a, b, dims):
    return lax.dot_general(a, b, dims, preferred_element_type=F32)


def chunks(rows):
    return 4 if rows % 64 == 0 else 1


def shape(dims, dtype):
    return jax.ShapeDtypeStruct(dims, dtype)


class Group:
    def __init__(self, size):
        self.size = size
        self.chips = size // 2
        self.me = lax.axis_index("tensor")
        self.chip = lax.div(self.me, 2)
        self.core = lax.rem(self.me, 2)
        self.sibling = self.chip * 2 + 1 - self.core

    def ahead(self, k):
        return lax.rem(self.chip + k, self.chips)

    def behind(self, k):
        return lax.rem(self.chip + self.chips - k, self.chips)

    def greet(self, replicas=0, side=False):
        barrier = pltpu.get_barrier_semaphore()
        targets = [self.sibling] + [self.ahead(k) * 2 + self.core for k in range(1, self.chips)]
        targets = [{"tensor": target} for target in targets]
        if replicas:
            d = lax.axis_index("dp")
            targets += [{"dp": lax.rem(d + k, replicas)} for k in range(1, replicas)]
        if replicas or side:
            targets += [{"section": 1 - lax.axis_index("section")}]
        for target in targets:
            pl.semaphore_signal(barrier, inc=1, device_id=target, device_id_type=MESH)
        pl.semaphore_wait(barrier, len(targets))


def remote(src, dst, send, recv, target):
    return pltpu.make_async_remote_copy(
        src_ref=src,
        dst_ref=dst,
        send_sem=send,
        recv_sem=recv,
        device_id={"tensor": target},
        device_id_type=MESH,
    )


def span(j, rc):
    return pl.ds(pl.multiple_of(j * rc, rc), rc)


def comm_sems(group_size, n):
    c = group_size // 2
    far, near = DMA((max(c - 1, 1), n)), DMA((c, n))
    return [far, far, near, near]


class Gather:
    def __init__(self, g, buf, rc, sems):
        self.g, self.buf, self.rc = g, buf, rc
        self.far_send, self.far_recv, self.near_send, self.near_recv = sems

    def far(self, k, j, origin, target):
        ref = self.buf.at[origin, span(j, self.rc)]
        return remote(ref, ref, self.far_send.at[k - 1, j], self.far_recv.at[k - 1, j], target)

    def near(self, k, j, origin):
        ref = self.buf.at[origin, span(j, self.rc)]
        return remote(
            ref, ref, self.near_send.at[k, j], self.near_recv.at[k, j], self.g.sibling
        )

    def start(self, j):
        g = self.g
        for k in range(1, g.chips):
            self.far(k, j, g.me, g.ahead(k) * 2 + g.core).start()
        self.near(0, j, g.me).start()

    def relay(self, j):
        g = self.g
        for k in range(1, g.chips):
            origin = g.behind(k) * 2 + g.core
            self.far(k, j, origin, g.me).wait_recv()
            self.near(k, j, origin).start()

    def ready(self, j):
        g = self.g
        self.near(0, j, g.sibling).wait_recv()
        for k in range(1, g.chips):
            self.near(k, j, g.behind(k) * 2 + 1 - g.core).wait_recv()

    def drain(self, n):
        g = self.g

        def one(j, _):
            for k in range(1, g.chips):
                self.far(k, j, g.me, g.sibling).wait_send()
            for k in range(g.chips):
                self.near(k, j, g.me).wait_send()
            return 0

        lax.fori_loop(0, n, one, 0)


def scatter_scratch(group_size, rows, width, n):
    c = group_size // 2
    far = pltpu.VMEM((max(c - 1, 1), rows, width), BF)
    near = pltpu.VMEM((c, rows, width), BF)
    return [pltpu.VMEM((group_size, rows, width), F32), near, near, far, far] + comm_sems(
        group_size, n
    )


class Scatter:
    def __init__(self, g, rc, scratch):
        self.g, self.rc = g, rc
        self.part, self.near_out, self.near_in, self.far_out, self.far_in = scratch[:5]
        self.far_send, self.far_recv, self.near_send, self.near_recv = scratch[5:]

    def near(self, k, j):
        rows = span(j, self.rc)
        return remote(
            self.near_out.at[k, rows],
            self.near_in.at[k, rows],
            self.near_send.at[k, j],
            self.near_recv.at[k, j],
            self.g.sibling,
        )

    def far(self, k, j):
        rows = span(j, self.rc)
        return remote(
            self.far_out.at[k - 1, rows],
            self.far_in.at[k - 1, rows],
            self.far_send.at[k - 1, j],
            self.far_recv.at[k - 1, j],
            self.g.ahead(k) * 2 + self.g.core,
        )

    def first(self, j):
        g, rows = self.g, span(j, self.rc)
        for k in list(range(1, g.chips)) + [0]:
            owner = g.ahead(k) * 2 + 1 - g.core
            self.near_out[k, rows, :] = self.part[owner, rows, :].astype(BF)
            self.near(k, j).start()

    def second(self, j):
        g, rows = self.g, span(j, self.rc)
        for k in range(1, g.chips):
            owner = g.ahead(k) * 2 + g.core
            self.near(k, j).wait_recv()
            both = self.part[owner, rows, :] + self.near_in[k, rows, :].astype(F32)
            self.far_out[k - 1, rows, :] = both.astype(BF)
            self.far(k, j).start()

    def third(self, j):
        g, rows = self.g, span(j, self.rc)
        self.near(0, j).wait_recv()
        total = self.part[g.me, rows, :] + self.near_in[0, rows, :].astype(F32)
        for k in range(1, g.chips):
            self.far(k, j).wait_recv()
            total = total + self.far_in[k - 1, rows, :].astype(F32)
        return total

    def drain(self, n):
        g = self.g

        def one(j, _):
            for k in range(1, g.chips):
                self.far(k, j).wait_send()
            for k in range(g.chips):
                self.near(k, j).wait_send()
            return 0

        lax.fori_loop(0, n, one, 0)


def far_copy(src, dst, send, recv, target):
    return pltpu.make_async_remote_copy(
        src_ref=src,
        dst_ref=dst,
        send_sem=send,
        recv_sem=recv,
        device_id=target,
        device_id_type=MESH,
    )


class Swap:
    def __init__(self, src, stage, sems):
        self.src, self.stage, self.sems = src, stage, sems
        self.s = lax.axis_index("section")

    def copies(self, layer):
        local = pltpu.make_async_copy(self.src.at[self.s], self.stage.at[self.s], self.sems.at[0])
        side = far_copy(
            self.src.at[1 - self.s],
            self.stage.at[layer],
            self.sems.at[1],
            self.sems.at[2],
            {"section": 1 - self.s},
        )
        return local, side

    def start(self):
        for copy in self.copies(self.s):
            copy.start()

    def arrive(self):
        local, side = self.copies(1 - self.s)
        local.wait()
        side.wait_recv()

    def finish(self):
        self.copies(self.s)[1].wait_send()


def reduce_scratch(replicas, rows, cols):
    many = pltpu.VMEM((replicas - 1, rows, cols), BF)
    one = pltpu.VMEM((rows, cols), BF)
    far, side = DMA((replicas - 1, 2)), DMA((2,))
    return [pltpu.VMEM((rows, cols), F32), many, many, one, one, far, far, side, side]


class Reduce:
    def __init__(self, layer, scratch):
        self.layer = layer
        self.own, self.away, self.came, self.over, self.back = scratch[:5]
        self.z_send, self.z_recv, self.y_send, self.y_recv = scratch[5:]
        self.replicas = self.away.shape[0] + 1
        self.half = self.own.shape[0] // 2
        self.d = lax.axis_index("dp")
        self.s = lax.axis_index("section")

    def target(self, k):
        return lax.rem(self.d + k, self.replicas)

    def part(self, i):
        return pl.ds(pl.multiple_of(i * self.half, self.half), self.half)

    def z_copy(self, k, i):
        part = self.part(i)
        return far_copy(
            self.away.at[k - 1, part],
            self.came.at[k - 1, part],
            self.z_send.at[k - 1, i],
            self.z_recv.at[k - 1, i],
            {"dp": self.target(k)},
        )

    def y_copy(self, i):
        part = self.part(i)
        return far_copy(
            self.over.at[part],
            self.back.at[part],
            self.y_send.at[i],
            self.y_recv.at[i],
            {"section": 1 - self.s},
        )

    def send(self, block):
        def one(i):
            k = i + 1
            self.away[i] = block(self.target(k)).astype(BF)
            self.z_copy(k, 0).start()
            self.z_copy(k, 1).start()

        run(self.replicas - 1, one)
        self.own[...] = block(self.d)

    def collect(self):
        def one(i):
            part = self.part(i)
            total = self.own[part, :]
            for k in range(1, self.replicas):
                self.z_copy(k, i).wait_recv()
                total = total + self.came[k - 1, part, :].astype(F32)
            self.own[part, :] = total
            self.over[part, :] = total.astype(BF)

            @pl.when(self.s != self.layer)
            def _():
                self.y_copy(i).start()

        run(2, one)

    def finish(self, out):
        @pl.when(self.s == self.layer)
        def _():
            self.y_copy(0).wait_recv()
            self.y_copy(1).wait_recv()
            out[...] = self.own[...] + self.back[...].astype(F32)

        @pl.when(self.s != self.layer)
        def _():
            self.y_copy(0).wait_send()
            self.y_copy(1).wait_send()
            out[...] = self.own[...]

        for k in range(1, self.replicas):
            self.z_copy(k, 0).wait_send()
            self.z_copy(k, 1).wait_send()


class Spread:
    def __init__(self, src, dst, by_columns, sems):
        self.src, self.dst, self.by_columns = src, dst, by_columns
        self.own_sem, self.far_send, self.far_recv, self.side_send, self.side_recv = sems
        self.replicas = far = self.side_send.shape[0]
        self.s = lax.axis_index("section")
        self.d = lax.axis_index("dp")
        self.stages = [
            sorted({k, far - k}) for k in range(1, far // 2 + 1)
        ]

    def place(self, half, z):
        rows, cols = self.src.shape
        if self.by_columns:
            return self.dst.at[
                pl.ds(pl.multiple_of(half * rows, rows), rows),
                pl.ds(pl.multiple_of(z * cols, cols), cols),
            ]
        return self.dst.at[pl.ds(pl.multiple_of((2 * z + half) * rows, rows), rows)]

    def origin(self, k):
        return lax.rem(self.d + self.replicas - k, self.replicas)

    def own(self):
        return pltpu.make_async_copy(self.src, self.place(self.s, self.d), self.own_sem.at[0])

    def far(self, k, origin):
        return pltpu.make_async_remote_copy(
            src_ref=self.src,
            dst_ref=self.place(self.s, origin),
            send_sem=self.far_send.at[k - 1],
            recv_sem=self.far_recv.at[k - 1],
            device_id={"dp": lax.rem(self.d + k, self.replicas)},
            device_id_type=MESH,
        )

    def side(self, k, half):
        place = self.place(half, self.origin(k))
        return pltpu.make_async_remote_copy(
            src_ref=self.src if k == 0 else place,
            dst_ref=place,
            send_sem=self.side_send.at[k],
            recv_sem=self.side_recv.at[k],
            device_id={"section": 1 - self.s},
            device_id_type=MESH,
        )

    def start(self):
        for k in self.stages[0]:
            self.far(k, self.d).start()
        self.side(0, self.s).start()
        self.own().start()

    def step(self, i):
        for k in self.stages[i]:
            self.far(k, self.origin(k)).wait_recv()
            self.side(k, self.s).start()
        if i + 1 < len(self.stages):
            for k in self.stages[i + 1]:
                self.far(k, self.d).start()

    def finish(self):
        self.own().wait()
        for k in range(self.replicas):
            self.side(k, 1 - self.s).wait_recv()
        for k in range(1, self.replicas):
            self.far(k, self.d).wait_send()
        for k in range(self.replicas):
            self.side(k, self.s).wait_send()


def rider_sems(replicas):
    far, side = DMA((replicas - 1,)), DMA((replicas,))
    return [DMA((1,)), far, far, side, side]


class Riders:
    def __init__(self, srcs, dsts, columns, sems):
        self.all = [
            Spread(src.at[layer], dst, by, sems[5 * i : 5 * i + 5])
            for i, (src, dst, (layer, by)) in enumerate(zip(srcs, dsts, columns))
        ]
        self.replicas = self.all[0].replicas if self.all else 0

    def start(self):
        for one in self.all:
            one.start()

    def step(self, j, n):
        if not self.all:
            return
        stages = len(self.all[0].stages)
        for i in range(stages):

            @pl.when(j == n * (i + 1) // stages - 1)
            def _(i=i):
                for one in self.all:
                    one.step(i)

    def finish(self):
        for one in self.all:
            one.finish()


def riding(riders, replicas):
    halves = [stage for stage, _, _ in riders]
    columns = tuple((layer, by) for _, layer, by in riders)
    outs = []
    for stage, _, by in riders:
        _, rows, cols = stage.shape
        outs.append(
            shape((2 * rows, replicas * cols) if by else (2 * replicas * rows, cols), BF)
        )
    sems = rider_sems(replicas) * len(riders)
    return halves, columns, outs, sems


def params(key):
    return pltpu.CompilerParams(
        vmem_limit_bytes=LIMIT, collective_id=key, has_side_effects=True
    )


def cost(flops, moved, exps=0):
    return pl.CostEstimate(flops=int(flops), bytes_accessed=int(moved), transcendentals=int(exps))


def normed(source):
    center = source - jnp.mean(source, axis=-1, keepdims=True)
    r = lax.rsqrt(jnp.mean(center * center, axis=-1, keepdims=True) + 1e-05)
    return center * r, r


def normed_back(source, gain, grad):
    n, r = normed(source)
    e = grad * gain
    dh = r * (
        e - jnp.mean(e, axis=-1, keepdims=True) - n * jnp.mean(e * n, axis=-1, keepdims=True)
    )
    return dh, jnp.sum(grad * n, axis=0, keepdims=True)


def flat(value):
    return value.reshape((value.shape[0] * value.shape[1],) + value.shape[2:])


def run(n, body):
    def one(j, carry):
        body(j)
        return carry

    lax.fori_loop(0, n, one, 0)


def first_kernel(
    size, replicas, x_ref, gain_ref, wq_ref, wo_ref, wu_ref, wd_ref,
    qkv_ref, gains_out, a1_out, wq_out, wo_out, q_stage, o_stage, u_stage, d_stage,
    a1, w, gains, own_sem, q_sem, o_sem, u_sem, d_sem, gain_sem, *sems
):
    rows, width = x_ref.shape
    n = chunks(rows)
    rc = rows // n
    g = Group(size)
    section = lax.axis_index("section")
    gather = Gather(g, a1, rc, sems[:4])
    swaps = [
        Swap(wq_ref, q_stage, q_sem),
        Swap(wo_ref, o_stage, o_sem),
        Swap(wu_ref, u_stage, u_sem),
        Swap(wd_ref, d_stage, d_sem),
    ]
    spreads = [
        Spread(q_stage.at[0], w, False, sems[4:9]),
        Spread(o_stage.at[0], wo_out, True, sems[9:14]),
    ]
    riders = Riders([], [], (), [])
    riders.all = spreads
    riders.replicas = replicas
    g.greet(replicas)

    def gain_copy(layer):
        return far_copy(
            gain_ref, gains.at[layer], gain_sem.at[0], gain_sem.at[1], {"section": 1 - section}
        )

    gain_copy(section).start()
    swaps[0].start()
    swaps[1].start()
    gains[section] = gain_ref[...]
    gain_copy(1 - section).wait_recv()
    gains_out[...] = gains[...]

    def send(j):
        at = span(j, rc)
        a = normed(x_ref[at, :].astype(F32))[0] * gains[0, 0:1, :]
        a1[g.me, at, :] = a.astype(BF)
        gather.start(j)

    run(n, send)
    swaps[0].arrive()
    swaps[1].arrive()
    riders.start()
    swaps[2].start()
    swaps[3].start()

    def relay(j):
        gather.relay(j)
        riders.step(j, n)

    run(n, relay)
    riders.finish()
    outs = [
        pltpu.make_async_copy(w, wq_out, own_sem.at[0]),
        pltpu.make_async_copy(a1, a1_out, own_sem.at[1]),
    ]
    outs[0].start()

    def multiply(j):
        at = span(j, rc)
        gather.ready(j)
        r = dg(flat(a1[:, at, :]), w[...], NN).astype(BF)
        qkv_ref[:, at, :] = r.reshape(size, rc, r.shape[1])

    run(n, multiply)
    outs[1].start()
    swaps[2].arrive()
    swaps[3].arrive()
    for swap in swaps:
        swap.finish()
    gain_copy(section).wait_send()
    gather.drain(n)
    for out in outs:
        out.wait()


def first_forward(size, replicas, x, gains, ws):
    rows, width = x.shape
    wide = ws[0].shape[2]
    deep = 2 * ws[1].shape[1]
    n = chunks(rows)
    return pl.pallas_call(
        functools.partial(first_kernel, size, replicas),
        out_shape=[
            shape((size, rows, wide), BF),
            shape((2,) + gains.shape, F32),
            shape((size, rows, width), BF),
            shape((width, wide), BF),
            shape((deep, width), BF),
        ]
        + [shape(w.shape, BF) for w in ws],
        in_specs=[VM, VM] + [HB] * 4,
        out_specs=[VM, VM] + [HB] * 7,
        scratch_shapes=[
            pltpu.VMEM((size, rows, width), BF),
            pltpu.VMEM((width, wide), BF),
            pltpu.VMEM((2,) + gains.shape, F32),
            DMA((2,)),
            DMA((3,)),
            DMA((3,)),
            DMA((3,)),
            DMA((3,)),
            DMA((2,)),
        ]
        + comm_sems(size, n)
        + rider_sems(replicas) * 2,
        compiler_params=params(0),
        cost_estimate=cost(30e9, 30e6),
    )(x, gains, *ws)


def qkv_kernel(size, layer, columns, *refs):
    m = len(columns)
    x_ref, gain_ref, w_ref = refs[:3]
    halves, refs = refs[3 : 3 + m], refs[3 + m :]
    qkv_ref, a1_out = refs[:2]
    wholes, refs = refs[2 : 2 + m], refs[2 + m :]
    a1, w, w_sem, out_sem = refs[:4]
    sems, refs = refs[4:8], refs[8:]
    riders = Riders(halves, wholes, columns, refs)
    rows, width = x_ref.shape
    n = chunks(rows)
    rc = rows // n
    g = Group(size)
    copy = pltpu.make_async_copy(w_ref, w, w_sem.at[0])
    copy.start()
    g.greet(riders.replicas)
    gather = Gather(g, a1, rc, sems)
    riders.start()

    def send(j):
        at = span(j, rc)
        a = normed(x_ref[at, :].astype(F32))[0] * gain_ref[layer, 0:1, :]
        a1[g.me, at, :] = a.astype(BF)
        gather.start(j)

    run(n, send)
    copy.wait()

    def work(j):
        at = span(j, rc)
        gather.relay(j)
        gather.ready(j)
        r = dg(flat(a1[:, at, :]), w[...], NN).astype(BF)
        qkv_ref[:, at, :] = r.reshape(size, rc, r.shape[1])
        riders.step(j, n)

    run(n, work)
    out = pltpu.make_async_copy(a1, a1_out, out_sem.at[0])
    out.start()
    riders.finish()
    gather.drain(n)
    out.wait()


def qkv_forward(size, replicas, layer, x, gains, w, riders):
    rows, width = x.shape
    wide = w.shape[1]
    n = chunks(rows)
    halves, columns, outs, sems = riding(riders, replicas)
    return pl.pallas_call(
        functools.partial(qkv_kernel, size, layer, columns),
        out_shape=[
            shape((size, rows, wide), BF),
            shape((size, rows, width), BF),
        ]
        + outs,
        in_specs=[VM, VM, HB] + [HB] * len(riders),
        out_specs=[VM, HB] + [HB] * len(outs),
        scratch_shapes=[
            pltpu.VMEM((size, rows, width), BF),
            pltpu.VMEM((width, wide), BF),
            DMA((1,)),
            DMA((1,)),
        ]
        + comm_sems(size, n)
        + sems,
        compiler_params=params(layer),
        cost_estimate=cost(20e9, 30e6),
    )(x, gains, w, *halves)


def attend_kernel(size, layer, columns, *refs):
    m = len(columns)
    qkv_ref, qm_ref, km_ref, x_ref, w_ref = refs[:5]
    halves, refs = refs[5 : 5 + m], refs[5 + m :]
    h1_ref, ctx_ref, lse_ref = refs[:3]
    wholes, refs = refs[3 : 3 + m], refs[3 + m :]
    ka, vt, w, w_sem = refs[:4]
    scratch, refs = refs[4:13], refs[13:]
    riders = Riders(halves, wholes, columns, refs)
    _, rows, wide = qkv_ref.shape
    length = size * rows
    e = qm_ref.shape[2]
    heads = wide // (3 * e)
    c = e**-0.5 * math.log2(math.e)
    n = chunks(rows)
    rc = rows // n
    bq = size * rc
    kc = bq
    g = Group(size)
    copy = pltpu.make_async_copy(w_ref, w, w_sem.at[0])
    copy.start()
    g.greet(riders.replicas)
    riders.start()
    scatter = Scatter(g, rc, scratch)
    whole = flat(qkv_ref[...])
    for h in range(heads):
        o = 3 * e * h
        ka[h, :, :e] = whole[:, o + e : o + 2 * e]
        ka[h, :, e:] = flat(km_ref[...])
        vt[h, :e, :] = whole[:, o + 2 * e : o + 3 * e].T
        vt[h, e:, :] = jnp.ones((16, length), BF)
    copy.wait()

    def work(j):
        at = span(j, rc)
        qm = flat(qm_ref[:, at, :])
        found = []
        held_qkv = flat(qkv_ref[:, at, :])
        for h in range(heads):
            o = 3 * e * h
            q = jnp.concatenate([held_qkv[:, o : o + e], qm], axis=1)
            held = []
            top = None
            for k in range(length // kc):
                s = dg(ka[h, k * kc : (k + 1) * kc, :], q, NT)
                t = jnp.max(s, axis=0, keepdims=True)
                top = t if top is None else jnp.maximum(top, t)
                held.append(s)
            top = top * c
            acc = None
            for k in range(length // kc):
                p = jnp.exp2(held[k] * c - top).astype(BF)
                a = dg(vt[h, :, k * kc : (k + 1) * kc], p, NN)
                acc = a if acc is None else acc + a
            total = acc[e : e + 1]
            found.append((acc[:e] * (1.0 / total)).astype(BF))
            lse_ref[j, h : h + 1, :] = top + jnp.log2(total)
        ctx = (jnp.concatenate(found, axis=0) if heads > 1 else found[0]).T
        ctx_ref[:, at, :] = ctx.reshape(size, rc, heads * e)
        width = x_ref.shape[1]
        scatter.part[:, at, :] = dg(ctx, w[...], NN).reshape(size, rc, width)
        scatter.first(j)
        scatter.second(j)
        riders.step(j, n)

    run(n, work)

    def last(j):
        at = span(j, rc)
        h1_ref[at, :] = x_ref[at, :].astype(F32) + scatter.third(j)

    run(n, last)
    scatter.drain(n)
    riders.finish()


def attend(size, replicas, layer, qkv, qm, km, x, w, riders):
    _, rows, wide = qkv.shape
    e = qm.shape[2]
    heads = wide // (3 * e)
    width = x.shape[1]
    n = chunks(rows)
    halves, columns, outs, sems = riding(riders, replicas)
    return pl.pallas_call(
        functools.partial(attend_kernel, size, layer, columns),
        out_shape=[
            shape((rows, width), F32),
            shape((size, rows, heads * e), BF),
            shape((n, heads, size * rows // n), F32),
        ]
        + outs,
        in_specs=[VM, VM, VM, VM, HB] + [HB] * len(riders),
        out_specs=[VM, VM, VM] + [HB] * len(outs),
        scratch_shapes=[
            pltpu.VMEM((heads, size * rows, 2 * e), BF),
            pltpu.VMEM((heads, e + 16, size * rows), BF),
            pltpu.VMEM((heads * e, width), BF),
            DMA((1,)),
        ]
        + scatter_scratch(size, rows, width, n)
        + sems,
        compiler_params=params(2 + layer),
        cost_estimate=cost(60e9, 20e6),
    )(qkv, qm, km, x, w, *halves)


def mlp_kernel(size, layer, columns, *refs):
    m = len(columns)
    h1_ref, gain_ref, wu_ref, wd_ref = refs[:4]
    halves, refs = refs[4 : 4 + m], refs[4 + m :]
    y_ref, a2_out, hid_out, slope_out = refs[:4]
    wholes, refs = refs[4 : 4 + m], refs[4 + m :]
    a2, hid, slope, wu, wd, w_sem, out_sem = refs[:7]
    scratch, refs = refs[7:20], refs[20:]
    riders = Riders(halves, wholes, columns, refs)
    rows, width = h1_ref.shape
    hidden = wu_ref.shape[1]
    fb = min(256, hidden)
    n = chunks(rows)
    rc = rows // n
    g = Group(size)
    copies = [
        pltpu.make_async_copy(wu_ref, wu, w_sem.at[0]),
        pltpu.make_async_copy(wd_ref, wd, w_sem.at[1]),
    ]
    for copy in copies:
        copy.start()
    g.greet(riders.replicas)
    gather = Gather(g, a2, rc, scratch[:4])
    scatter = Scatter(g, rc, scratch[4:])

    def send(j):
        at = span(j, rc)
        a = normed(h1_ref[at, :])[0] * gain_ref[layer, 1:2, :]
        a2[g.me, at, :] = a.astype(BF)
        gather.start(j)

    run(n, send)
    riders.start()
    for copy in copies:
        copy.wait()

    def work(j):
        at = span(j, rc)
        gather.relay(j)
        gather.ready(j)
        a = flat(a2[:, at, :])
        for f in range(hidden // fb):
            cols = slice(f * fb, (f + 1) * fb)
            u = dg(a, wu[:, cols], NN)
            half = 0.5 + 0.5 * lax.erf(u * (0.5**0.5))
            slope[:, at, cols] = (
                (half + u * jnp.exp(-0.5 * u * u) * ((2 * math.pi) ** -0.5))
                .astype(BF)
                .reshape(size, rc, fb)
            )
            hid[:, at, cols] = (u * half).astype(BF).reshape(size, rc, fb)
        held = flat(hid[:, at, :])
        for f in range(width // 256):
            cols = slice(f * 256, (f + 1) * 256)
            scatter.part[:, at, cols] = dg(held, wd[:, cols], NN).reshape(size, rc, 256)
        scatter.first(j)
        scatter.second(j)
        riders.step(j, n)

    run(n, work)
    outs = [
        pltpu.make_async_copy(a2, a2_out, out_sem.at[0]),
        pltpu.make_async_copy(hid, hid_out, out_sem.at[1]),
        pltpu.make_async_copy(slope, slope_out, out_sem.at[2]),
    ]
    for out in outs:
        out.start()

    def last(j):
        at = span(j, rc)
        y_ref[at, :] = (h1_ref[at, :] + scatter.third(j)).astype(BF)

    run(n, last)
    riders.finish()
    gather.drain(n)
    scatter.drain(n)
    for out in outs:
        out.wait()


def mlp_forward(size, replicas, layer, h1, gains, wu, wd, riders):
    rows, width = h1.shape
    hidden = wu.shape[1]
    n = chunks(rows)
    halves, columns, outs, sems = riding(riders, replicas)
    return pl.pallas_call(
        functools.partial(mlp_kernel, size, layer, columns),
        out_shape=[
            shape((rows, width), BF),
            shape((size, rows, width), BF),
            shape((size, rows, hidden), BF),
            shape((size, rows, hidden), BF),
        ]
        + outs,
        in_specs=[VM, VM, HB, HB] + [HB] * len(riders),
        out_specs=[VM, HB, HB, HB] + [HB] * len(outs),
        scratch_shapes=[
            pltpu.VMEM((size, rows, width), BF),
            pltpu.VMEM((size, rows, hidden), BF),
            pltpu.VMEM((size, rows, hidden), BF),
            pltpu.VMEM((width, hidden), BF),
            pltpu.VMEM((hidden, width), BF),
            DMA((2,)),
            DMA((3,)),
        ]
        + comm_sems(size, n)
        + scatter_scratch(size, rows, width, n)
        + sems,
        compiler_params=params(4 + layer),
        cost_estimate=cost(50e9, 30e6),
    )(h1, gains, wu, wd, *halves)


def mlp_back_kernel(size, layer, parts, *refs):
    g_ref, h1_ref, gain_ref, a2_ref, hid_ref, slope_ref, wu_ref, wd_ref = refs[:8]
    refs = refs[8:]
    if layer == 1:
        ys, refs = refs[:2], refs[2:]
    mid_ref, gain_out, gup_ref, gdown_ref = refs[:4]
    refs = refs[4:]
    if layer == 1:
        y_out, refs = refs[0], refs[1:]
    grad, a2, hid, dup, wu, wd, w_sem = refs[:7]
    scratch, refs = refs[7:20], refs[20:]
    rows, width = h1_ref.shape
    hidden = wu_ref.shape[1]
    depth = width // parts
    fb = min(256, hidden)
    n = chunks(rows)
    rc = rows // n
    g = Group(size)
    copies = [
        pltpu.make_async_copy(wd_ref, wd, w_sem.at[0]),
        pltpu.make_async_copy(slope_ref, dup, w_sem.at[1]),
        pltpu.make_async_copy(wu_ref, wu, w_sem.at[2]),
    ]
    late = [
        pltpu.make_async_copy(hid_ref, hid, w_sem.at[3]),
        pltpu.make_async_copy(a2_ref, a2, w_sem.at[4]),
    ]
    for copy in copies + late:
        copy.start()
    g.greet(side=layer == 1)
    section = lax.axis_index("section")
    if layer == 1:
        y_sem = refs[0]

        def y_copies(own, other, at):
            return (
                pltpu.make_async_copy(own, y_out.at[section], y_sem.at[0]),
                far_copy(
                    other, y_out.at[at], y_sem.at[1], y_sem.at[2], {"section": 1 - section}
                ),
            )

        for i in range(2):

            @pl.when(section == i)
            def _(i=i):
                for copy in y_copies(ys[i], ys[1 - i], section):
                    copy.start()

    gather = Gather(g, grad, rc, scratch[:4])
    scatter = Scatter(g, rc, scratch[4:])

    def send(j):
        at = span(j, rc)
        grad[g.me, at, :] = g_ref[at, :]
        gather.start(j)

    run(n, send)
    for copy in copies:
        copy.wait()

    def work(j):
        at = span(j, rc)
        gather.relay(j)
        gather.ready(j)
        held = flat(grad[:, at, :])
        for f in range(hidden // fb):
            cols = slice(f * fb, (f + 1) * fb)
            d = dg(held, wd[cols, :], NT) * flat(dup[:, at, cols]).astype(F32)
            dup[:, at, cols] = d.astype(BF).reshape(size, rc, fb)
        held = flat(dup[:, at, :])
        for z in range(parts):
            cols = slice(z * depth, (z + 1) * depth)
            scatter.part[:, at, cols] = dg(held, wu[cols, :], NT).reshape(size, rc, depth)
        scatter.first(j)
        scatter.second(j)

    run(n, work)
    for copy in late:
        copy.wait()

    def up_grad(z):
        cols = pl.ds(pl.multiple_of(z * depth, depth), depth)
        gup_ref[z] = dg(flat(a2[:, :, cols]), flat(dup[...]), TN).astype(BF)

    run(parts, up_grad)

    def down_grad(f):
        cols = pl.ds(pl.multiple_of(f * fb, fb), fb)
        r = dg(flat(hid[:, :, cols]), flat(grad[...]), TN).astype(BF)
        for z in range(parts):
            gdown_ref[z, cols, :] = r[:, z * depth : (z + 1) * depth]

    run(hidden // fb, down_grad)
    gain_out[...] = jnp.zeros_like(gain_out)

    def last(j):
        at = span(j, rc)
        dh, dgain = normed_back(h1_ref[at, :], gain_ref[layer, 1:2, :], scatter.third(j))
        mid_ref[at, :] = g_ref[at, :].astype(F32) + dh
        gain_out[...] += dgain

    run(n, last)
    if layer == 1:
        local, side = y_copies(ys[0], ys[1], 1 - section)
        local.wait()
        side.wait_recv()
        y_copies(ys[0], ys[1], section)[1].wait_send()
    gather.drain(n)
    scatter.drain(n)


def mlp_backward(size, replicas, layer, grad, h1, gains, a2, hid, slope, wu, wd, ys):
    rows, width = h1.shape
    hidden = wu.shape[1]
    parts, depth = replicas, width // replicas
    n = chunks(rows)
    return pl.pallas_call(
        functools.partial(mlp_back_kernel, size, layer, parts),
        out_shape=[
            shape((rows, width), F32),
            shape((1, width), F32),
            shape((parts, depth, hidden), BF),
            shape((parts, hidden, depth), BF),
        ]
        + [shape((2, rows, width), BF)] * (len(ys) // 2),
        in_specs=[VM, VM, VM] + [HB] * (5 + len(ys)),
        out_specs=[VM, VM, VM, VM] + [HB] * (len(ys) // 2),
        scratch_shapes=[
            pltpu.VMEM((size, rows, width), BF),
            pltpu.VMEM((size, rows, width), BF),
            pltpu.VMEM((size, rows, hidden), BF),
            pltpu.VMEM((size, rows, hidden), BF),
            pltpu.VMEM((width, hidden), BF),
            pltpu.VMEM((hidden, width), BF),
            DMA((5,)),
        ]
        + comm_sems(size, n)
        + scatter_scratch(size, rows, width, n)
        + [DMA((3,))] * (len(ys) // 2),
        compiler_params=params(6 + layer),
        cost_estimate=cost(60e9, 40e6),
    )(grad, h1, gains, a2, hid, slope, wu, wd, *ys)


def attend_back_kernel(
    size, layer, parts, mid_ref, qkv_ref, qm_ref, km_ref, ctx_ref, lse_ref, w_ref,
    dqkv_ref, gout_ref, da, ka, va, kt, dk, dv, w, w_sem, *sems
):
    reduce = Reduce(layer, sems[4:])
    sems = sems[:4]
    _, rows, wide = qkv_ref.shape
    length = size * rows
    e = qm_ref.shape[2]
    heads = wide // (3 * e)
    scale = e**-0.5
    c = scale * math.log2(math.e)
    depth = w_ref.shape[1] // parts
    n = chunks(rows)
    rc = rows // n
    bq = size * rc
    kc = bq
    g = Group(size)
    copies = [pltpu.make_async_copy(w_ref, w, w_sem.at[0])]
    for copy in copies:
        copy.start()
    g.greet(parts)
    gather = Gather(g, da, rc, sems)

    def send(j):
        at = span(j, rc)
        da[g.me, at, :] = mid_ref[at, :].astype(BF)
        gather.start(j)

    run(n, send)
    lane = lax.broadcasted_iota(jnp.int32, (length, e), 1)
    whole = flat(qkv_ref[...])
    for h in range(heads):
        o = 3 * e * h
        ka[h, :, :e] = whole[:, o + e : o + 2 * e]
        ka[h, :, e:] = flat(km_ref[...])
        va[h, :, :e] = whole[:, o + 2 * e : o + 3 * e]
        va[h, :, e:] = jnp.where(lane < 3, 1.0, 0.0).astype(BF)
        kt[h] = whole[:, o + e : o + 2 * e].T
    dk[...] = jnp.zeros_like(dk)
    dv[...] = jnp.zeros_like(dv)
    ql = lax.broadcasted_iota(jnp.int32, (bq, e), 1)
    for copy in copies:
        copy.wait()

    def out_grad(z):
        cols = pl.ds(pl.multiple_of(z * depth, depth), depth)
        return dg(flat(ctx_ref[...]), flat(da[:, :, cols]), TN)

    def work(j):
        at = span(j, rc)

        @pl.when(j == 0)
        def _():
            gather.relay(0)
            gather.ready(0)

        @pl.when(j == min(1, n - 1))
        def _():
            for i in range(1, n):
                gather.relay(i)
            for i in range(1, n):
                gather.ready(i)
            reduce.send(out_grad)

        qm = flat(qm_ref[:, at, :])
        dctx = dg(flat(da[:, at, :]), w[...], NT).astype(BF)
        ctx = flat(ctx_ref[:, at, :])
        held_qkv = flat(qkv_ref[:, at, :])
        for h in range(heads):
            o = 3 * e * h
            qq = held_qkv[:, o : o + e]
            q = jnp.concatenate([qq, qm], axis=1)
            dc = dctx[:, h * e : (h + 1) * e]
            prod = dc.astype(F32) * ctx[:, h * e : (h + 1) * e].astype(F32)
            d = -jnp.sum(prod, axis=1, keepdims=True)
            d1 = d.astype(BF).astype(F32)
            d2 = (d - d1).astype(BF).astype(F32)
            d3 = d - d1 - d2
            ds_col = jnp.where(ql == 0, d1, jnp.where(ql == 1, d2, jnp.where(ql == 2, d3, 0.0)))
            dca = jnp.concatenate([dc, ds_col.astype(BF)], axis=1)
            lse = lse_ref[j, h : h + 1, :]
            dqt = None
            for k in range(length // kc):
                ks = slice(k * kc, (k + 1) * kc)
                s = dg(ka[h, ks, :], q, NT)
                p = jnp.exp2(s * c - lse)
                ds = (p * dg(va[h, ks, :], dca, NT)).astype(BF)
                dv[h, ks, :] += dg(p.astype(BF), dc, NN)
                dk[h, ks, :] += dg(ds, qq, NN)
                a = dg(kt[h, :, ks], ds, NN)
                dqt = a if dqt is None else dqt + a
            dqkv_ref[:, at, o : o + e] = (dqt * scale).T.astype(BF).reshape(size, rc, e)

    run(n, work)
    for h in range(heads):
        o = 3 * e * h
        dqkv_ref[:, :, o + e : o + 2 * e] = (dk[h] * scale).astype(BF).reshape(size, rows, e)
        dqkv_ref[:, :, o + 2 * e : o + 3 * e] = dv[h].astype(BF).reshape(size, rows, e)

    reduce.collect()
    reduce.finish(gout_ref)
    gather.drain(n)


def attend_backward(size, replicas, layer, mid, qkv, qm, km, ctx, lse, w):
    _, rows, wide = qkv.shape
    e = qm.shape[2]
    heads = wide // (3 * e)
    width = mid.shape[1]
    parts, depth = replicas, width // replicas
    length = size * rows
    n = chunks(rows)
    return pl.pallas_call(
        functools.partial(attend_back_kernel, size, layer, parts),
        out_shape=(shape(qkv.shape, BF), shape((heads * e, depth), F32)),
        in_specs=[VM] * 6 + [HB],
        out_specs=(VM, VM),
        scratch_shapes=[
            pltpu.VMEM((size, rows, width), BF),
            pltpu.VMEM((heads, length, 2 * e), BF),
            pltpu.VMEM((heads, length, 2 * e), BF),
            pltpu.VMEM((heads, e, length), BF),
            pltpu.VMEM((heads, length, e), F32),
            pltpu.VMEM((heads, length, e), F32),
            pltpu.VMEM((heads * e, width), BF),
            DMA((1,)),
        ]
        + comm_sems(size, n)
        + reduce_scratch(parts, heads * e, depth),
        compiler_params=params(8 + layer),
        cost_estimate=cost(90e9, 40e6),
    )(mid, qkv, qm, km, ctx, lse, w)


def qkv_back_kernel(
    size, layer, parts, dqkv_ref, a1_ref, x_ref, mid_ref, gain_ref, w_ref,
    dx_ref, gain_out, gqkv_ref, w, w_sem, *scratch
):
    rows, width = x_ref.shape
    depth = width // parts
    n = chunks(rows)
    rc = rows // n
    g = Group(size)
    copies = [pltpu.make_async_copy(w_ref, w, w_sem.at[0])]
    for copy in copies:
        copy.start()
    g.greet()
    scatter = Scatter(g, rc, scratch)
    for copy in copies:
        copy.wait()

    def work(j):
        at = span(j, rc)
        held = flat(dqkv_ref[:, at, :])
        for z in range(parts):
            cols = slice(z * depth, (z + 1) * depth)
            scatter.part[:, at, cols] = dg(held, w[cols, :], NT).reshape(size, rc, depth)
        scatter.first(j)
        scatter.second(j)

    run(n, work)

    def qkv_grad(z):
        cols = pl.ds(pl.multiple_of(z * depth, depth), depth)
        gqkv_ref[z] = dg(flat(a1_ref[:, :, cols]), flat(dqkv_ref[...]), TN).astype(BF)

    run(parts, qkv_grad)
    gain_out[...] = jnp.zeros_like(gain_out)

    def last(j):
        at = span(j, rc)
        dh, dgain = normed_back(
            x_ref[at, :].astype(F32), gain_ref[layer, 0:1, :], scatter.third(j)
        )
        dx_ref[at, :] = (mid_ref[at, :] + dh).astype(BF)
        gain_out[...] += dgain

    run(n, last)
    scatter.drain(n)


def qkv_backward(size, replicas, layer, dqkv, a1, x, mid, gains, w):
    rows, width = x.shape
    wide = w.shape[1]
    parts, depth = replicas, width // replicas
    n = chunks(rows)
    return pl.pallas_call(
        functools.partial(qkv_back_kernel, size, layer, parts),
        out_shape=(
            shape((rows, width), BF),
            shape((1, width), F32),
            shape((parts, depth, wide), BF),
        ),
        in_specs=[VM] * 5 + [HB],
        out_specs=(VM, VM, VM),
        scratch_shapes=[
            pltpu.VMEM((width, wide), BF),
            DMA((1,)),
        ]
        + scatter_scratch(size, rows, width, n),
        compiler_params=params(11),
        cost_estimate=cost(30e9, 30e6),
    )(dqkv, a1, x, mid, gains, w)


def last_kernel(
    size, parts, dqkv_ref, a1_ref, x_ref, mid_ref, gain_ref, w_ref, two_ref, above_ref, dx1_ref,
    gain_out, gqkv_ref, dx_out,
    w, dx, gsum, gcame, w_sem, x_sem, x_send, x_recv, g_send, g_recv, *scratch
):
    rows, width = x_ref.shape
    depth = width // parts
    n = chunks(rows)
    rc = rows // n
    g = Group(size)
    section = lax.axis_index("section")
    d = lax.axis_index("dp")
    copy = pltpu.make_async_copy(w_ref, w, w_sem.at[0])
    copy.start()
    reduce = Reduce(0, scratch[:9])
    scatter = Scatter(g, rc, scratch[9:])
    g.greet(parts)

    def upper():
        return far_copy(
            dx1_ref, dx_out.at[0], x_send.at[n], x_recv.at[n], {"section": 1 - section}
        )

    def keep_upper():
        return pltpu.make_async_copy(dx1_ref, dx_out.at[1], x_sem.at[0])

    def lower(j):
        at = span(j, rc)
        return far_copy(
            dx.at[at], dx_out.at[1, at], x_send.at[j], x_recv.at[j], {"section": 1 - section}
        )

    def keep_lower(j):
        at = span(j, rc)
        return pltpu.make_async_copy(dx.at[at], dx_out.at[0, at], x_sem.at[j])

    @pl.when(section == 0)
    def _():
        upper().start()

    @pl.when(section == 1)
    def _():
        keep_upper().start()

    def block(z):
        cols = pl.ds(pl.multiple_of(z * depth, depth), depth)
        return dg(flat(a1_ref[:, :, cols]), flat(dqkv_ref[...]), TN)

    reduce.send(block)
    copy.wait()

    def work(j):
        at = span(j, rc)
        held = flat(dqkv_ref[:, at, :])
        for z in range(parts):
            cols = slice(z * depth, (z + 1) * depth)
            scatter.part[:, at, cols] = dg(held, w[cols, :], NT).reshape(size, rc, depth)
        scatter.first(j)
        scatter.second(j)

    run(n, work)
    gsum[0] = jnp.zeros_like(gsum[0])

    def last(j):
        at = span(j, rc)
        dh, dgain = normed_back(x_ref[at, :].astype(F32), gain_ref[0, 0:1, :], scatter.third(j))
        dx[at, :] = (mid_ref[at, :] + dh).astype(BF)

        @pl.when(section == 0)
        def _():
            keep_lower(j).start()

        @pl.when(section == 1)
        def _():
            lower(j).start()

        gsum[0, 0:1, :] += dgain

    run(n, last)
    gsum[0, 1:2, :] = two_ref[...]
    gsum[0, 2:4, :] = above_ref[...]

    targets = [
        [{"tensor": g.sibling}],
        [{"tensor": g.ahead(k) * 2 + g.core} for k in range(1, g.chips)],
        [{"dp": lax.rem(d + k, parts)} for k in range(1, parts)],
        [{"section": 1 - section}],
    ]
    slot = 0
    sent = []

    def exchange(stage):
        nonlocal slot
        copies = []
        for target in targets[stage]:
            copies.append(
                far_copy(gsum.at[stage], gcame.at[slot], g_send.at[slot], g_recv.at[slot], target)
            )
            copies[-1].start()
            slot += 1
        total = gsum[stage]
        for i, copy in enumerate(copies):
            copy.wait_recv()
            total = total + gcame[slot - len(copies) + i]
        gsum[stage + 1] = total
        sent.extend(copies)

    for stage in range(4):
        exchange(stage)
    gain_out[...] = gsum[4]
    reduce.collect()

    @pl.when(section == 0)
    def _():
        for j in range(n):
            lower(j).wait_recv()
            keep_lower(j).wait()
        upper().wait_send()

    @pl.when(section == 1)
    def _():
        keep_upper().wait()
        upper().wait_recv()
        for j in range(n):
            lower(j).wait_send()

    reduce.finish(gqkv_ref)
    for copy in sent:
        copy.wait_send()
    scatter.drain(n)


def last_backward(size, replicas, dqkv, a1, x, mid, gains, w, two, above, dx1):
    rows, width = x.shape
    wide = w.shape[1]
    depth = width // replicas
    n = chunks(rows)
    slots = 1 + (size // 2 - 1) + (replicas - 1) + 1
    return pl.pallas_call(
        functools.partial(last_kernel, size, replicas),
        out_shape=(
            shape((8, width), F32),
            shape((depth, wide), F32),
            shape((2, rows, width), BF),
        ),
        in_specs=[VM] * 5 + [HB, VM, VM, HB],
        out_specs=(VM, VM, HB),
        scratch_shapes=[
            pltpu.VMEM((width, wide), BF),
            pltpu.VMEM((rows, width), BF),
            pltpu.VMEM((5, 8, width), F32),
            pltpu.VMEM((slots, 8, width), F32),
            DMA((1,)),
            DMA((n,)),
            DMA((n + 1,)),
            DMA((n + 1,)),
            DMA((slots,)),
            DMA((slots,)),
        ]
        + reduce_scratch(replicas, depth, wide)
        + scatter_scratch(size, rows, width, n),
        compiler_params=params(10),
        cost_estimate=cost(40e9, 30e6),
    )(dqkv, a1, x, mid, gains, w, two, above, dx1)


def scene_masks(segments, e):
    same = (segments[..., None] == jnp.arange(e, dtype=jnp.int32)).astype(F32)
    used = jnp.arange(e) < SCENES
    return (
        jnp.where(used, same * MASKED, 0.0).astype(BF),
        jnp.where(used, 1.0 - same, 0.0).astype(BF),
    )


def swap_section(value):
    return lax.ppermute(value, "section", [(0, 1), (1, 0)])


def shards(
    block_input,
    segment_ids,
    cotangent,
    norm_one_gain,
    qkv_weight,
    out_weight,
    norm_two_gain,
    up_weight,
    down_weight,
):
    section = lax.axis_index("section")
    size = lax.axis_size("tensor")
    replicas = lax.axis_size("dp")

    mine = [
        qkv_weight[0].reshape((qkv_weight.shape[1], -1)),
        out_weight[0].reshape((-1, out_weight.shape[3])),
        up_weight[0],
        down_weight[0],
    ]
    mine = [w.astype(BF).reshape((2, -1, w.shape[1])) for w in mine]
    gains = jnp.concatenate(
        [norm_one_gain, norm_two_gain, jnp.zeros((6, norm_one_gain.shape[1]), F32)], axis=0
    )
    segments = lax.dynamic_index_in_dim(segment_ids, section, 0, keepdims=False)
    x = lax.dynamic_index_in_dim(block_input, section, 0, keepdims=False)
    head_dim = qkv_weight.shape[3] // 3
    qm, km = scene_masks(segments.reshape((size, -1)), head_dim)
    qkv, gains, a1, w_qkv_0, w_out_0, h_qkv, h_out, h_up, h_down = first_forward(
        size, replicas, x, gains, mine
    )
    h1, ctx, lse, w_up_0, w_down_0 = attend(
        size, replicas, 0, qkv, qm, km, x, w_out_0, [(h_up, 0, False), (h_down, 0, True)]
    )
    y0, a2, hid, slope, w_qkv_1, w_out_1 = mlp_forward(
        size, replicas, 0, h1, gains, w_up_0, w_down_0, [(h_qkv, 1, False), (h_out, 1, True)]
    )
    kept = [(x, a1, qkv, ctx, lse, h1, a2, hid, slope)]
    qkv, a1, w_up_1 = qkv_forward(
        size, replicas, 1, y0, gains, w_qkv_1, [(h_up, 1, False)]
    )
    h1, ctx, lse, w_down_1 = attend(
        size, replicas, 1, qkv, qm, km, y0, w_out_1, [(h_down, 1, True)]
    )
    y1, a2, hid, slope = mlp_forward(size, replicas, 1, h1, gains, w_up_1, w_down_1, [])
    kept.append((y0, a1, qkv, ctx, lse, h1, a2, hid, slope))
    weights = [
        (w_qkv_0, w_out_0, w_up_0, w_down_0),
        (w_qkv_1, w_out_1, w_up_1, w_down_1),
    ]
    grad = lax.dynamic_index_in_dim(cotangent, section, 0, keepdims=False)

    def reduce_rows(value):
        return lax.psum_scatter(value, "dp", scatter_dimension=0, tiled=False)

    x, a1, qkv, ctx, lse, h1, a2, hid, slope = kept[1]
    w_qkv, w_out, w_up, w_down = weights[1]
    mid, gain_two, g_up, g_down, layer_out = mlp_backward(
        size, replicas, 1, grad, h1, gains, a2, hid, slope, w_up, w_down, [y0, y1]
    )
    d_qkv, out_1 = attend_backward(size, replicas, 1, mid, qkv, qm, km, ctx, lse, w_out)
    up_1, down_1 = reduce_rows(g_up), reduce_rows(g_down)
    dx1, gain_one, g_qkv = qkv_backward(size, replicas, 1, d_qkv, a1, x, mid, gains, w_qkv)
    gains_above = jnp.concatenate([gain_one, gain_two], axis=0)
    dx1, up_1, down_1 = lax.optimization_barrier((dx1, up_1, down_1))
    qkv_1 = reduce_rows(g_qkv)

    x, a1, qkv, ctx, lse, h1, a2, hid, slope = kept[0]
    w_qkv, w_out, w_up, w_down = weights[0]
    mid, gain_two, g_up, g_down = mlp_backward(
        size, replicas, 0, dx1, h1, gains, a2, hid, slope, w_up, w_down, []
    )
    mid, qkv_1 = lax.optimization_barrier((mid, qkv_1))
    d_qkv, out_0 = attend_backward(size, replicas, 0, mid, qkv, qm, km, ctx, lse, w_out)
    up_0, down_0 = reduce_rows(g_up), reduce_rows(g_down)
    d_qkv, up_0, down_0 = lax.optimization_barrier((d_qkv, up_0, down_0))
    gains, qkv_0, input_out = last_backward(
        size, replicas, d_qkv, a1, x, mid, gains, w_qkv, gain_two, gains_above, dx1
    )

    def finish(zero, one):
        send = swap_section(jnp.where(section == 0, one, zero))
        return jnp.where(section == 0, zero, one).astype(F32) + send.astype(F32)

    other_qkv_1 = swap_section(qkv_1)
    qkv_grad = jnp.where(section == 0, qkv_0, qkv_1.astype(F32) + other_qkv_1.astype(F32))
    out_grad = jnp.where(section == 0, out_0, out_1)
    up_grad, down_grad = finish(up_0, up_1), finish(down_0, down_1)
    gains = lax.dynamic_slice_in_dim(gains, 2 * section, 2, 0)
    return (
        layer_out[None],
        input_out[None],
        gains[0:1],
        qkv_grad.reshape(qkv_weight.shape),
        out_grad.reshape(out_weight.shape),
        gains[1:2],
        up_grad[None],
        down_grad[None],
    )


def solution(mesh):
    return jax.shard_map(
        shards,
        mesh=mesh,
        in_specs=(
            P(None, ("dp", "tensor"), None),
            P(None, "dp"),
            P(None, ("dp", "tensor"), None),
            P("section", None),
            P("section", "dp", "tensor", None),
            P("section", "tensor", None, "dp"),
            P("section", None),
            P("section", "dp", "tensor"),
            P("section", "tensor", "dp"),
        ),
        out_specs=(
            P("section", None, ("dp", "tensor"), None),
            P("section", None, ("dp", "tensor"), None),
            P("section", None),
            P("section", "dp", "tensor", None),
            P("section", "tensor", None, "dp"),
            P("section", None),
            P("section", "dp", "tensor"),
            P("section", "tensor", "dp"),
        ),
        check_vma=False,
    )
```

```python
import functools
import math

import jax
import jax.numpy as jnp
from jax import lax
from jax.experimental import pallas as pl
from jax.experimental.pallas import tpu as pltpu
from jax.sharding import PartitionSpec as P

F32 = jnp.float32
BF = jnp.bfloat16
NT = (((1,), (1,)), ((), ()))
NN = (((1,), (0,)), ((), ()))
TN = (((0,), (0,)), ((), ()))
MASKED = -1e30
SCENES = 3
MESH = pl.DeviceIdType.MESH
VM = pl.BlockSpec(memory_space=pltpu.VMEM)
HB = pl.BlockSpec(memory_space=pl.ANY)
DMA = pltpu.SemaphoreType.DMA
LIMIT = 58 << 20


def dg(a, b, dims):
    return lax.dot_general(a, b, dims, preferred_element_type=F32)


def chunks(rows):
    return 4 if rows % 64 == 0 else 1


def shape(dims, dtype):
    return jax.ShapeDtypeStruct(dims, dtype)


class Group:
    def __init__(self, size):
        self.size = size
        self.chips = size // 2
        self.me = lax.axis_index("tensor")
        self.chip = lax.div(self.me, 2)
        self.core = lax.rem(self.me, 2)
        self.sibling = self.chip * 2 + 1 - self.core

    def ahead(self, k):
        return lax.rem(self.chip + k, self.chips)

    def behind(self, k):
        return lax.rem(self.chip + self.chips - k, self.chips)

    def greet(self, replicas=0, side=False):
        barrier = pltpu.get_barrier_semaphore()
        targets = [self.sibling] + [self.ahead(k) * 2 + self.core for k in range(1, self.chips)]
        targets = [{"tensor": target} for target in targets]
        if replicas:
            d = lax.axis_index("dp")
            targets += [{"dp": lax.rem(d + k, replicas)} for k in range(1, replicas)]
        if replicas or side:
            targets += [{"section": 1 - lax.axis_index("section")}]
        for target in targets:
            pl.semaphore_signal(barrier, inc=1, device_id=target, device_id_type=MESH)
        pl.semaphore_wait(barrier, len(targets))


def remote(src, dst, send, recv, target):
    return pltpu.make_async_remote_copy(
        src_ref=src,
        dst_ref=dst,
        send_sem=send,
        recv_sem=recv,
        device_id={"tensor": target},
        device_id_type=MESH,
    )


def span(j, rc):
    return pl.ds(pl.multiple_of(j * rc, rc), rc)


def comm_sems(group_size, n):
    c = group_size // 2
    far, near = DMA((max(c - 1, 1), n)), DMA((c, n))
    return [far, far, near, near]


class Gather:
    def __init__(self, g, buf, rc, sems):
        self.g, self.buf, self.rc = g, buf, rc
        self.far_send, self.far_recv, self.near_send, self.near_recv = sems

    def far(self, k, j, origin, target):
        ref = self.buf.at[origin, span(j, self.rc)]
        return remote(ref, ref, self.far_send.at[k - 1, j], self.far_recv.at[k - 1, j], target)

    def near(self, k, j, origin):
        ref = self.buf.at[origin, span(j, self.rc)]
        return remote(
            ref, ref, self.near_send.at[k, j], self.near_recv.at[k, j], self.g.sibling
        )

    def start(self, j):
        g = self.g
        for k in range(1, g.chips):
            self.far(k, j, g.me, g.ahead(k) * 2 + g.core).start()
        self.near(0, j, g.me).start()

    def relay(self, j):
        g = self.g
        for k in range(1, g.chips):
            origin = g.behind(k) * 2 + g.core
            self.far(k, j, origin, g.me).wait_recv()
            self.near(k, j, origin).start()

    def ready(self, j):
        g = self.g
        self.near(0, j, g.sibling).wait_recv()
        for k in range(1, g.chips):
            self.near(k, j, g.behind(k) * 2 + 1 - g.core).wait_recv()

    def drain(self, n):
        g = self.g

        def one(j, _):
            for k in range(1, g.chips):
                self.far(k, j, g.me, g.sibling).wait_send()
            for k in range(g.chips):
                self.near(k, j, g.me).wait_send()
            return 0

        lax.fori_loop(0, n, one, 0)


def scatter_scratch(group_size, rows, width, n):
    c = group_size // 2
    far = pltpu.VMEM((max(c - 1, 1), rows, width), BF)
    near = pltpu.VMEM((c, rows, width), BF)
    return [pltpu.VMEM((group_size, rows, width), F32), near, near, far, far] + comm_sems(
        group_size, n
    )


class Scatter:
    def __init__(self, g, rc, scratch):
        self.g, self.rc = g, rc
        self.part, self.near_out, self.near_in, self.far_out, self.far_in = scratch[:5]
        self.far_send, self.far_recv, self.near_send, self.near_recv = scratch[5:]

    def near(self, k, j):
        rows = span(j, self.rc)
        return remote(
            self.near_out.at[k, rows],
            self.near_in.at[k, rows],
            self.near_send.at[k, j],
            self.near_recv.at[k, j],
            self.g.sibling,
        )

    def far(self, k, j):
        rows = span(j, self.rc)
        return remote(
            self.far_out.at[k - 1, rows],
            self.far_in.at[k - 1, rows],
            self.far_send.at[k - 1, j],
            self.far_recv.at[k - 1, j],
            self.g.ahead(k) * 2 + self.g.core,
        )

    def first(self, j):
        g, rows = self.g, span(j, self.rc)
        for k in list(range(1, g.chips)) + [0]:
            owner = g.ahead(k) * 2 + 1 - g.core
            self.near_out[k, rows, :] = self.part[owner, rows, :].astype(BF)
            self.near(k, j).start()

    def second(self, j):
        g, rows = self.g, span(j, self.rc)
        for k in range(1, g.chips):
            owner = g.ahead(k) * 2 + g.core
            self.near(k, j).wait_recv()
            both = self.part[owner, rows, :] + self.near_in[k, rows, :].astype(F32)
            self.far_out[k - 1, rows, :] = both.astype(BF)
            self.far(k, j).start()

    def third(self, j):
        g, rows = self.g, span(j, self.rc)
        self.near(0, j).wait_recv()
        total = self.part[g.me, rows, :] + self.near_in[0, rows, :].astype(F32)
        for k in range(1, g.chips):
            self.far(k, j).wait_recv()
            total = total + self.far_in[k - 1, rows, :].astype(F32)
        return total

    def drain(self, n):
        g = self.g

        def one(j, _):
            for k in range(1, g.chips):
                self.far(k, j).wait_send()
            for k in range(g.chips):
                self.near(k, j).wait_send()
            return 0

        lax.fori_loop(0, n, one, 0)


def far_copy(src, dst, send, recv, target):
    return pltpu.make_async_remote_copy(
        src_ref=src,
        dst_ref=dst,
        send_sem=send,
        recv_sem=recv,
        device_id=target,
        device_id_type=MESH,
    )


class Swap:
    def __init__(self, src, stage, sems):
        self.src, self.stage, self.sems = src, stage, sems
        self.s = lax.axis_index("section")

    def copies(self, layer):
        local = pltpu.make_async_copy(self.src.at[self.s], self.stage.at[self.s], self.sems.at[0])
        side = far_copy(
            self.src.at[1 - self.s],
            self.stage.at[layer],
            self.sems.at[1],
            self.sems.at[2],
            {"section": 1 - self.s},
        )
        return local, side

    def start(self):
        for copy in self.copies(self.s):
            copy.start()

    def arrive(self):
        local, side = self.copies(1 - self.s)
        local.wait()
        side.wait_recv()

    def finish(self):
        self.copies(self.s)[1].wait_send()


def reduce_scratch(replicas, rows, cols):
    many = pltpu.VMEM((replicas - 1, rows, cols), BF)
    one = pltpu.VMEM((rows, cols), BF)
    far, side = DMA((replicas - 1, 2)), DMA((2,))
    return [pltpu.VMEM((rows, cols), F32), many, many, one, one, far, far, side, side]


class Reduce:
    def __init__(self, layer, scratch):
        self.layer = layer
        self.own, self.away, self.came, self.over, self.back = scratch[:5]
        self.z_send, self.z_recv, self.y_send, self.y_recv = scratch[5:]
        self.replicas = self.away.shape[0] + 1
        self.half = self.own.shape[0] // 2
        self.d = lax.axis_index("dp")
        self.s = lax.axis_index("section")

    def target(self, k):
        return lax.rem(self.d + k, self.replicas)

    def part(self, i):
        return pl.ds(pl.multiple_of(i * self.half, self.half), self.half)

    def z_copy(self, k, i):
        part = self.part(i)
        return far_copy(
            self.away.at[k - 1, part],
            self.came.at[k - 1, part],
            self.z_send.at[k - 1, i],
            self.z_recv.at[k - 1, i],
            {"dp": self.target(k)},
        )

    def y_copy(self, i):
        part = self.part(i)
        return far_copy(
            self.over.at[part],
            self.back.at[part],
            self.y_send.at[i],
            self.y_recv.at[i],
            {"section": 1 - self.s},
        )

    def send(self, block):
        def one(i):
            k = i + 1
            self.away[i] = block(self.target(k)).astype(BF)
            self.z_copy(k, 0).start()
            self.z_copy(k, 1).start()

        run(self.replicas - 1, one)
        self.own[...] = block(self.d)

    def collect(self):
        def one(i):
            part = self.part(i)
            total = self.own[part, :]
            for k in range(1, self.replicas):
                self.z_copy(k, i).wait_recv()
                total = total + self.came[k - 1, part, :].astype(F32)
            self.own[part, :] = total
            self.over[part, :] = total.astype(BF)

            @pl.when(self.s != self.layer)
            def _():
                self.y_copy(i).start()

        run(2, one)

    def finish(self, out):
        @pl.when(self.s == self.layer)
        def _():
            self.y_copy(0).wait_recv()
            self.y_copy(1).wait_recv()
            out[...] = self.own[...] + self.back[...].astype(F32)

        @pl.when(self.s != self.layer)
        def _():
            self.y_copy(0).wait_send()
            self.y_copy(1).wait_send()
            out[...] = self.own[...]

        for k in range(1, self.replicas):
            self.z_copy(k, 0).wait_send()
            self.z_copy(k, 1).wait_send()


class HalfSwap:
    def __init__(self, src, came, sems):
        self.src, self.came, self.sems = src, came, sems
        self.s = lax.axis_index("section")
        self.rows = came.shape[1]

    def copy(self):
        at = pl.ds(pl.multiple_of((1 - self.s) * self.rows, self.rows), self.rows)
        return far_copy(
            self.src.at[:, at],
            self.came,
            self.sems.at[0],
            self.sems.at[1],
            {"section": 1 - self.s},
        )


def half_scratch(replicas, rows, cols):
    rows = rows // 2
    all_, far = pltpu.VMEM((replicas, rows, cols), BF), pltpu.VMEM((replicas - 1, rows, cols), BF)
    one = pltpu.VMEM((rows, cols), BF)
    z = DMA((replicas - 1,))
    return [all_, all_, far, far, pltpu.VMEM((rows, cols), F32), one, one, DMA((3,)), z, z, DMA((2,))]


HALF = 11


class HalfReduce:
    def __init__(self, layer, scratch):
        self.layer = layer
        self.mine, self.other, self.away, self.came, self.own, self.over, self.back = scratch[:7]
        self.in_sem, self.z_send, self.z_recv, self.y_sem = scratch[7:]
        self.replicas, self.rows = self.mine.shape[:2]
        self.s = lax.axis_index("section")
        self.d = lax.axis_index("dp")

    def half(self, s):
        return pl.ds(pl.multiple_of(s * self.rows, self.rows), self.rows)

    def loads(self, src, other):
        loads = [pltpu.make_async_copy(src.at[:, self.half(self.s)], self.mine, self.in_sem.at[0])]
        if other is not None:
            loads.append(pltpu.make_async_copy(other, self.other, self.in_sem.at[1]))
        return loads

    def z_copy(self, k):
        return far_copy(
            self.away.at[k - 1],
            self.came.at[k - 1],
            self.z_send.at[k - 1],
            self.z_recv.at[k - 1],
            {"dp": lax.rem(self.d + k, self.replicas)},
        )

    def y_copy(self):
        return far_copy(
            self.over, self.back, self.y_sem.at[0], self.y_sem.at[1], {"section": 1 - self.s}
        )

    def middle(self):
        def both(z):
            return self.mine[z].astype(F32) + self.other[z].astype(F32)

        for k in range(1, self.replicas):
            self.away[k - 1] = both(lax.rem(self.d + k, self.replicas)).astype(BF)
            self.z_copy(k).start()
        self.own[...] = both(self.d)

    def late(self):
        total = self.own[...]
        for k in range(1, self.replicas):
            self.z_copy(k).wait_recv()
            total = total + self.came[k - 1].astype(F32)
        self.own[...] = total
        self.over[...] = total.astype(BF)

        @pl.when(self.s != self.layer)
        def _():
            self.y_copy().start()

    def finish(self, out, above=None):
        @pl.when(self.s == self.layer)
        def _():
            self.y_copy().wait_recv()
            out[self.half(self.s), :] = self.own[...]
            out[self.half(1 - self.s), :] = self.back[...].astype(F32)

        @pl.when(self.s != self.layer)
        def _():
            if above is None:
                out[...] = jnp.zeros_like(out)
            else:
                copy = pltpu.make_async_copy(above, out, self.in_sem.at[2])
                copy.start()
                copy.wait()
            self.y_copy().wait_send()

        for k in range(1, self.replicas):
            self.z_copy(k).wait_send()


class Spread:
    def __init__(self, src, dst, by_columns, sems):
        self.src, self.dst, self.by_columns = src, dst, by_columns
        self.own_sem, self.far_send, self.far_recv, self.side_send, self.side_recv = sems
        self.replicas = far = self.side_send.shape[0]
        self.s = lax.axis_index("section")
        self.d = lax.axis_index("dp")
        self.stages = [
            sorted({k, far - k}) for k in range(1, far // 2 + 1)
        ]

    def place(self, half, z):
        rows, cols = self.src.shape
        if self.by_columns:
            return self.dst.at[
                pl.ds(pl.multiple_of(half * rows, rows), rows),
                pl.ds(pl.multiple_of(z * cols, cols), cols),
            ]
        return self.dst.at[pl.ds(pl.multiple_of((2 * z + half) * rows, rows), rows)]

    def origin(self, k):
        return lax.rem(self.d + self.replicas - k, self.replicas)

    def own(self):
        return pltpu.make_async_copy(self.src, self.place(self.s, self.d), self.own_sem.at[0])

    def far(self, k, origin):
        return pltpu.make_async_remote_copy(
            src_ref=self.src,
            dst_ref=self.place(self.s, origin),
            send_sem=self.far_send.at[k - 1],
            recv_sem=self.far_recv.at[k - 1],
            device_id={"dp": lax.rem(self.d + k, self.replicas)},
            device_id_type=MESH,
        )

    def side(self, k, half):
        place = self.place(half, self.origin(k))
        return pltpu.make_async_remote_copy(
            src_ref=self.src if k == 0 else place,
            dst_ref=place,
            send_sem=self.side_send.at[k],
            recv_sem=self.side_recv.at[k],
            device_id={"section": 1 - self.s},
            device_id_type=MESH,
        )

    def start(self):
        for k in self.stages[0]:
            self.far(k, self.d).start()
        self.side(0, self.s).start()
        self.own().start()

    def step(self, i):
        for k in self.stages[i]:
            self.far(k, self.origin(k)).wait_recv()
            self.side(k, self.s).start()
        if i + 1 < len(self.stages):
            for k in self.stages[i + 1]:
                self.far(k, self.d).start()

    def finish(self):
        self.own().wait()
        for k in range(self.replicas):
            self.side(k, 1 - self.s).wait_recv()
        for k in range(1, self.replicas):
            self.far(k, self.d).wait_send()
        for k in range(self.replicas):
            self.side(k, self.s).wait_send()


def rider_sems(replicas):
    far, side = DMA((replicas - 1,)), DMA((replicas,))
    return [DMA((1,)), far, far, side, side]


class Riders:
    def __init__(self, srcs, dsts, columns, sems):
        self.all = [
            Spread(src.at[layer], dst, by, sems[5 * i : 5 * i + 5])
            for i, (src, dst, (layer, by)) in enumerate(zip(srcs, dsts, columns))
        ]
        self.replicas = self.all[0].replicas if self.all else 0

    def start(self):
        for one in self.all:
            one.start()

    def step(self, j, n):
        if not self.all:
            return
        stages = len(self.all[0].stages)
        for i in range(stages):

            @pl.when(j == n * (i + 1) // stages - 1)
            def _(i=i):
                for one in self.all:
                    one.step(i)

    def finish(self):
        for one in self.all:
            one.finish()


def riding(riders, replicas):
    halves = [stage for stage, _, _ in riders]
    columns = tuple((layer, by) for _, layer, by in riders)
    outs = []
    for stage, _, by in riders:
        _, rows, cols = stage.shape
        outs.append(
            shape((2 * rows, replicas * cols) if by else (2 * replicas * rows, cols), BF)
        )
    sems = rider_sems(replicas) * len(riders)
    return halves, columns, outs, sems


def params(key):
    return pltpu.CompilerParams(
        vmem_limit_bytes=LIMIT, collective_id=key, has_side_effects=True
    )


def cost(flops, moved, exps=0):
    return pl.CostEstimate(flops=int(flops), bytes_accessed=int(moved), transcendentals=int(exps))


def normed(source):
    center = source - jnp.mean(source, axis=-1, keepdims=True)
    r = lax.rsqrt(jnp.mean(center * center, axis=-1, keepdims=True) + 1e-05)
    return center * r, r


def normed_back(source, gain, grad):
    n, r = normed(source)
    e = grad * gain
    dh = r * (
        e - jnp.mean(e, axis=-1, keepdims=True) - n * jnp.mean(e * n, axis=-1, keepdims=True)
    )
    return dh, jnp.sum(grad * n, axis=0, keepdims=True)


def flat(value):
    return value.reshape((value.shape[0] * value.shape[1],) + value.shape[2:])


def run(n, body):
    def one(j, carry):
        body(j)
        return carry

    lax.fori_loop(0, n, one, 0)


def first_kernel(
    size, replicas, x_ref, gain_ref, wq_ref, wo_ref, wu_ref, wd_ref,
    qkv_ref, gains_out, a1_out, wq_out, wo_out, q_stage, o_stage, u_stage, d_stage,
    a1, w, gains, own_sem, q_sem, o_sem, u_sem, d_sem, gain_sem, *sems
):
    rows, width = x_ref.shape
    n = chunks(rows)
    rc = rows // n
    g = Group(size)
    section = lax.axis_index("section")
    gather = Gather(g, a1, rc, sems[:4])
    swaps = [
        Swap(wq_ref, q_stage, q_sem),
        Swap(wo_ref, o_stage, o_sem),
        Swap(wu_ref, u_stage, u_sem),
        Swap(wd_ref, d_stage, d_sem),
    ]
    spreads = [
        Spread(q_stage.at[0], w, False, sems[4:9]),
        Spread(o_stage.at[0], wo_out, True, sems[9:14]),
    ]
    riders = Riders([], [], (), [])
    riders.all = spreads
    riders.replicas = replicas
    g.greet(replicas)

    def gain_copy(layer):
        return far_copy(
            gain_ref, gains.at[layer], gain_sem.at[0], gain_sem.at[1], {"section": 1 - section}
        )

    gain_copy(section).start()
    swaps[0].start()
    swaps[1].start()
    gains[section] = gain_ref[...]
    gain_copy(1 - section).wait_recv()
    gains_out[...] = gains[...]

    def send(j):
        at = span(j, rc)
        a = normed(x_ref[at, :].astype(F32))[0] * gains[0, 0:1, :]
        a1[g.me, at, :] = a.astype(BF)
        gather.start(j)

    run(n, send)
    swaps[0].arrive()
    swaps[1].arrive()
    riders.start()
    swaps[2].start()
    swaps[3].start()

    def relay(j):
        gather.relay(j)
        riders.step(j, n)

    run(n, relay)
    riders.finish()
    outs = [
        pltpu.make_async_copy(w, wq_out, own_sem.at[0]),
        pltpu.make_async_copy(a1, a1_out, own_sem.at[1]),
    ]
    outs[0].start()

    def multiply(j):
        at = span(j, rc)
        gather.ready(j)
        r = dg(flat(a1[:, at, :]), w[...], NN).astype(BF)
        qkv_ref[:, at, :] = r.reshape(size, rc, r.shape[1])

    run(n, multiply)
    outs[1].start()
    swaps[2].arrive()
    swaps[3].arrive()
    for swap in swaps:
        swap.finish()
    gain_copy(section).wait_send()
    gather.drain(n)
    for out in outs:
        out.wait()


def first_forward(size, replicas, x, gains, ws):
    rows, width = x.shape
    wide = ws[0].shape[2]
    deep = 2 * ws[1].shape[1]
    n = chunks(rows)
    return pl.pallas_call(
        functools.partial(first_kernel, size, replicas),
        out_shape=[
            shape((size, rows, wide), BF),
            shape((2,) + gains.shape, F32),
            shape((size, rows, width), BF),
            shape((width, wide), BF),
            shape((deep, width), BF),
        ]
        + [shape(w.shape, BF) for w in ws],
        in_specs=[VM, VM] + [HB] * 4,
        out_specs=[VM, VM] + [HB] * 7,
        scratch_shapes=[
            pltpu.VMEM((size, rows, width), BF),
            pltpu.VMEM((width, wide), BF),
            pltpu.VMEM((2,) + gains.shape, F32),
            DMA((2,)),
            DMA((3,)),
            DMA((3,)),
            DMA((3,)),
            DMA((3,)),
            DMA((2,)),
        ]
        + comm_sems(size, n)
        + rider_sems(replicas) * 2,
        compiler_params=params(0),
        cost_estimate=cost(30e9, 30e6),
    )(x, gains, *ws)


def qkv_kernel(size, layer, columns, *refs):
    m = len(columns)
    x_ref, gain_ref, w_ref = refs[:3]
    halves, refs = refs[3 : 3 + m], refs[3 + m :]
    qkv_ref, a1_out = refs[:2]
    wholes, refs = refs[2 : 2 + m], refs[2 + m :]
    a1, w, w_sem, out_sem = refs[:4]
    sems, refs = refs[4:8], refs[8:]
    riders = Riders(halves, wholes, columns, refs)
    rows, width = x_ref.shape
    n = chunks(rows)
    rc = rows // n
    g = Group(size)
    copy = pltpu.make_async_copy(w_ref, w, w_sem.at[0])
    copy.start()
    g.greet(riders.replicas)
    gather = Gather(g, a1, rc, sems)
    riders.start()

    def send(j):
        at = span(j, rc)
        a = normed(x_ref[at, :].astype(F32))[0] * gain_ref[layer, 0:1, :]
        a1[g.me, at, :] = a.astype(BF)
        gather.start(j)

    run(n, send)
    copy.wait()

    def work(j):
        at = span(j, rc)
        gather.relay(j)
        gather.ready(j)
        r = dg(flat(a1[:, at, :]), w[...], NN).astype(BF)
        qkv_ref[:, at, :] = r.reshape(size, rc, r.shape[1])
        riders.step(j, n)

    run(n, work)
    out = pltpu.make_async_copy(a1, a1_out, out_sem.at[0])
    out.start()
    riders.finish()
    gather.drain(n)
    out.wait()


def qkv_forward(size, replicas, layer, x, gains, w, riders):
    rows, width = x.shape
    wide = w.shape[1]
    n = chunks(rows)
    halves, columns, outs, sems = riding(riders, replicas)
    return pl.pallas_call(
        functools.partial(qkv_kernel, size, layer, columns),
        out_shape=[
            shape((size, rows, wide), BF),
            shape((size, rows, width), BF),
        ]
        + outs,
        in_specs=[VM, VM, HB] + [HB] * len(riders),
        out_specs=[VM, HB] + [HB] * len(outs),
        scratch_shapes=[
            pltpu.VMEM((size, rows, width), BF),
            pltpu.VMEM((width, wide), BF),
            DMA((1,)),
            DMA((1,)),
        ]
        + comm_sems(size, n)
        + sems,
        compiler_params=params(layer),
        cost_estimate=cost(20e9, 30e6),
    )(x, gains, w, *halves)


def attend_kernel(size, layer, columns, *refs):
    m = len(columns)
    qkv_ref, qm_ref, km_ref, x_ref, w_ref = refs[:5]
    halves, refs = refs[5 : 5 + m], refs[5 + m :]
    h1_ref, ctx_ref, lse_ref = refs[:3]
    wholes, refs = refs[3 : 3 + m], refs[3 + m :]
    ka, vt, w, w_sem = refs[:4]
    scratch, refs = refs[4:13], refs[13:]
    riders = Riders(halves, wholes, columns, refs)
    _, rows, wide = qkv_ref.shape
    length = size * rows
    e = qm_ref.shape[2]
    heads = wide // (3 * e)
    c = e**-0.5 * math.log2(math.e)
    n = chunks(rows)
    rc = rows // n
    bq = size * rc
    kc = bq
    g = Group(size)
    copy = pltpu.make_async_copy(w_ref, w, w_sem.at[0])
    copy.start()
    g.greet(riders.replicas)
    riders.start()
    scatter = Scatter(g, rc, scratch)
    whole = flat(qkv_ref[...])
    for h in range(heads):
        o = 3 * e * h
        ka[h, :, :e] = whole[:, o + e : o + 2 * e]
        ka[h, :, e:] = flat(km_ref[...])
        vt[h, :e, :] = whole[:, o + 2 * e : o + 3 * e].T
        vt[h, e:, :] = jnp.ones((16, length), BF)
    copy.wait()

    def work(j):
        at = span(j, rc)
        qm = flat(qm_ref[:, at, :])
        found = []
        held_qkv = flat(qkv_ref[:, at, :])
        for h in range(heads):
            o = 3 * e * h
            q = jnp.concatenate([held_qkv[:, o : o + e], qm], axis=1)
            held = []
            top = None
            for k in range(length // kc):
                s = dg(ka[h, k * kc : (k + 1) * kc, :], q, NT)
                t = jnp.max(s, axis=0, keepdims=True)
                top = t if top is None else jnp.maximum(top, t)
                held.append(s)
            top = top * c
            acc = None
            for k in range(length // kc):
                p = jnp.exp2(held[k] * c - top).astype(BF)
                a = dg(vt[h, :, k * kc : (k + 1) * kc], p, NN)
                acc = a if acc is None else acc + a
            total = acc[e : e + 1]
            found.append((acc[:e] * (1.0 / total)).astype(BF))
            lse_ref[j, h : h + 1, :] = top + jnp.log2(total)
        ctx = (jnp.concatenate(found, axis=0) if heads > 1 else found[0]).T
        ctx_ref[:, at, :] = ctx.reshape(size, rc, heads * e)
        width = x_ref.shape[1]
        scatter.part[:, at, :] = dg(ctx, w[...], NN).reshape(size, rc, width)
        scatter.first(j)
        scatter.second(j)
        riders.step(j, n)

    run(n, work)

    def last(j):
        at = span(j, rc)
        h1_ref[at, :] = x_ref[at, :].astype(F32) + scatter.third(j)

    run(n, last)
    scatter.drain(n)
    riders.finish()


def attend(size, replicas, layer, qkv, qm, km, x, w, riders):
    _, rows, wide = qkv.shape
    e = qm.shape[2]
    heads = wide // (3 * e)
    width = x.shape[1]
    n = chunks(rows)
    halves, columns, outs, sems = riding(riders, replicas)
    return pl.pallas_call(
        functools.partial(attend_kernel, size, layer, columns),
        out_shape=[
            shape((rows, width), F32),
            shape((size, rows, heads * e), BF),
            shape((n, heads, size * rows // n), F32),
        ]
        + outs,
        in_specs=[VM, VM, VM, VM, HB] + [HB] * len(riders),
        out_specs=[VM, VM, VM] + [HB] * len(outs),
        scratch_shapes=[
            pltpu.VMEM((heads, size * rows, 2 * e), BF),
            pltpu.VMEM((heads, e + 16, size * rows), BF),
            pltpu.VMEM((heads * e, width), BF),
            DMA((1,)),
        ]
        + scatter_scratch(size, rows, width, n)
        + sems,
        compiler_params=params(2 + layer),
        cost_estimate=cost(60e9, 20e6),
    )(qkv, qm, km, x, w, *halves)


def mlp_kernel(size, layer, columns, *refs):
    m = len(columns)
    h1_ref, gain_ref, wu_ref, wd_ref = refs[:4]
    halves, refs = refs[4 : 4 + m], refs[4 + m :]
    y_ref, a2_out, hid_out, slope_out = refs[:4]
    wholes, refs = refs[4 : 4 + m], refs[4 + m :]
    a2, hid, slope, wu, wd, w_sem, out_sem = refs[:7]
    scratch, refs = refs[7:20], refs[20:]
    riders = Riders(halves, wholes, columns, refs)
    rows, width = h1_ref.shape
    hidden = wu_ref.shape[1]
    fb = min(256, hidden)
    n = chunks(rows)
    rc = rows // n
    g = Group(size)
    copies = [
        pltpu.make_async_copy(wu_ref, wu, w_sem.at[0]),
        pltpu.make_async_copy(wd_ref, wd, w_sem.at[1]),
    ]
    for copy in copies:
        copy.start()
    g.greet(riders.replicas)
    gather = Gather(g, a2, rc, scratch[:4])
    scatter = Scatter(g, rc, scratch[4:])

    def send(j):
        at = span(j, rc)
        a = normed(h1_ref[at, :])[0] * gain_ref[layer, 1:2, :]
        a2[g.me, at, :] = a.astype(BF)
        gather.start(j)

    run(n, send)
    riders.start()
    for copy in copies:
        copy.wait()

    def work(j):
        at = span(j, rc)
        gather.relay(j)
        gather.ready(j)
        a = flat(a2[:, at, :])
        for f in range(hidden // fb):
            cols = slice(f * fb, (f + 1) * fb)
            u = dg(a, wu[:, cols], NN)
            half = 0.5 + 0.5 * lax.erf(u * (0.5**0.5))
            slope[:, at, cols] = (
                (half + u * jnp.exp(-0.5 * u * u) * ((2 * math.pi) ** -0.5))
                .astype(BF)
                .reshape(size, rc, fb)
            )
            hid[:, at, cols] = (u * half).astype(BF).reshape(size, rc, fb)
        held = flat(hid[:, at, :])
        for f in range(width // 256):
            cols = slice(f * 256, (f + 1) * 256)
            scatter.part[:, at, cols] = dg(held, wd[:, cols], NN).reshape(size, rc, 256)
        scatter.first(j)
        scatter.second(j)
        riders.step(j, n)

    run(n, work)
    outs = [
        pltpu.make_async_copy(a2, a2_out, out_sem.at[0]),
        pltpu.make_async_copy(hid, hid_out, out_sem.at[1]),
        pltpu.make_async_copy(slope, slope_out, out_sem.at[2]),
    ]
    for out in outs:
        out.start()

    def last(j):
        at = span(j, rc)
        y_ref[at, :] = (h1_ref[at, :] + scatter.third(j)).astype(BF)

    run(n, last)
    riders.finish()
    gather.drain(n)
    scatter.drain(n)
    for out in outs:
        out.wait()


def mlp_forward(size, replicas, layer, h1, gains, wu, wd, riders):
    rows, width = h1.shape
    hidden = wu.shape[1]
    n = chunks(rows)
    halves, columns, outs, sems = riding(riders, replicas)
    return pl.pallas_call(
        functools.partial(mlp_kernel, size, layer, columns),
        out_shape=[
            shape((rows, width), BF),
            shape((size, rows, width), BF),
            shape((size, rows, hidden), BF),
            shape((size, rows, hidden), BF),
        ]
        + outs,
        in_specs=[VM, VM, HB, HB] + [HB] * len(riders),
        out_specs=[VM, HB, HB, HB] + [HB] * len(outs),
        scratch_shapes=[
            pltpu.VMEM((size, rows, width), BF),
            pltpu.VMEM((size, rows, hidden), BF),
            pltpu.VMEM((size, rows, hidden), BF),
            pltpu.VMEM((width, hidden), BF),
            pltpu.VMEM((hidden, width), BF),
            DMA((2,)),
            DMA((3,)),
        ]
        + comm_sems(size, n)
        + scatter_scratch(size, rows, width, n)
        + sems,
        compiler_params=params(4 + layer),
        cost_estimate=cost(50e9, 30e6),
    )(h1, gains, wu, wd, *halves)


def mlp_back_kernel(size, layer, parts, *refs):
    g_ref, h1_ref, gain_ref, a2_ref, hid_ref, slope_ref, wu_ref, wd_ref = refs[:8]
    refs = refs[8:]
    extra, refs = refs[:2], refs[2:]
    mid_ref, gain_out, gup_ref, gdown_out, down_came, extra_out = refs[:6]
    gdown_ref, refs = refs[6], refs[7:]
    grad, a2, hid, dup, wu, wd, w_sem = refs[:7]
    scratch, refs = refs[7:20], refs[20:]
    down_sem, out_sem, refs = refs[0], refs[1], refs[2:]
    rows, width = h1_ref.shape
    hidden = wu_ref.shape[1]
    depth = width // parts
    fb = min(256, hidden)
    n = chunks(rows)
    rc = rows // n
    g = Group(size)
    copies = [
        pltpu.make_async_copy(wd_ref, wd, w_sem.at[0]),
        pltpu.make_async_copy(slope_ref, dup, w_sem.at[1]),
        pltpu.make_async_copy(wu_ref, wu, w_sem.at[2]),
    ]
    late = [
        pltpu.make_async_copy(hid_ref, hid, w_sem.at[3]),
        pltpu.make_async_copy(a2_ref, a2, w_sem.at[4]),
    ]
    for copy in copies + late:
        copy.start()
    g.greet(parts if layer == 0 else 0, side=True)
    down_swap = HalfSwap(gdown_ref, down_came, down_sem)
    section = lax.axis_index("section")
    if layer == 1:
        y_sem = refs[0]
        ys, y_out = extra, extra_out

        def y_copies(own, other, at):
            return (
                pltpu.make_async_copy(own, y_out.at[section], y_sem.at[0]),
                far_copy(
                    other, y_out.at[at], y_sem.at[1], y_sem.at[2], {"section": 1 - section}
                ),
            )

        for i in range(2):

            @pl.when(section == i)
            def _(i=i):
                for copy in y_copies(ys[i], ys[1 - i], section):
                    copy.start()

    else:
        above = HalfReduce(1, refs)
        loads = above.loads(*extra)
        for load in loads:
            load.start()

    gather = Gather(g, grad, rc, scratch[:4])
    scatter = Scatter(g, rc, scratch[4:])

    def send(j):
        at = span(j, rc)
        grad[g.me, at, :] = g_ref[at, :]
        gather.start(j)

    run(n, send)
    for copy in copies:
        copy.wait()
    if layer == 0:
        for load in loads:
            load.wait()
        above.middle()

    def work(j):
        at = span(j, rc)
        gather.relay(j)
        gather.ready(j)
        held = flat(grad[:, at, :])
        for f in range(hidden // fb):
            cols = slice(f * fb, (f + 1) * fb)
            d = dg(held, wd[cols, :], NT) * flat(dup[:, at, cols]).astype(F32)
            dup[:, at, cols] = d.astype(BF).reshape(size, rc, fb)
        held = flat(dup[:, at, :])
        for z in range(parts):
            cols = slice(z * depth, (z + 1) * depth)
            scatter.part[:, at, cols] = dg(held, wu[cols, :], NT).reshape(size, rc, depth)
        scatter.first(j)
        scatter.second(j)

    run(n, work)
    for copy in late:
        copy.wait()

    def up_grad(z):
        cols = pl.ds(pl.multiple_of(z * depth, depth), depth)
        gup_ref[z] = dg(flat(a2[:, :, cols]), flat(dup[...]), TN).astype(BF)

    def down_grad(f):
        cols = pl.ds(pl.multiple_of(f * fb, fb), fb)
        r = dg(flat(hid[:, :, cols]), flat(grad[...]), TN).astype(BF)
        for z in range(parts):
            gdown_ref[z, cols, :] = r[:, z * depth : (z + 1) * depth]

    run(hidden // fb, down_grad)
    down_swap.copy().start()
    down_out = pltpu.make_async_copy(gdown_ref, gdown_out, out_sem.at[0])
    down_out.start()
    run(parts, up_grad)
    if layer == 0:
        above.late()
    gain_out[...] = jnp.zeros_like(gain_out)

    def last(j):
        at = span(j, rc)
        dh, dgain = normed_back(h1_ref[at, :], gain_ref[layer, 1:2, :], scatter.third(j))
        mid_ref[at, :] = g_ref[at, :].astype(F32) + dh
        gain_out[...] += dgain

    run(n, last)
    if layer == 1:
        local, side = y_copies(ys[0], ys[1], 1 - section)
        local.wait()
        side.wait_recv()
        y_copies(ys[0], ys[1], section)[1].wait_send()
    else:
        above.finish(extra_out)
    down_swap.copy().wait_recv()
    down_swap.copy().wait_send()
    down_out.wait()
    gather.drain(n)
    scatter.drain(n)


def mlp_backward(size, replicas, layer, grad, h1, gains, a2, hid, slope, wu, wd, extra):
    rows, width = h1.shape
    hidden = wu.shape[1]
    parts, depth = replicas, width // replicas
    n = chunks(rows)
    return pl.pallas_call(
        functools.partial(mlp_back_kernel, size, layer, parts),
        out_shape=[
            shape((rows, width), F32),
            shape((1, width), F32),
            shape((parts, depth, hidden), BF),
            shape((parts, hidden, depth), BF),
            shape((parts, hidden // 2, depth), BF),
            (
                shape((2, rows, width), BF)
                if layer == 1
                else shape((extra[0].shape[1], extra[0].shape[2]), F32)
            ),
        ],
        in_specs=[VM, VM, VM] + [HB] * 7,
        out_specs=[VM, VM, VM, HB, HB, HB if layer == 1 else VM],
        scratch_shapes=[
            pltpu.VMEM((parts, hidden, depth), BF),
            pltpu.VMEM((size, rows, width), BF),
            pltpu.VMEM((size, rows, width), BF),
            pltpu.VMEM((size, rows, hidden), BF),
            pltpu.VMEM((size, rows, hidden), BF),
            pltpu.VMEM((width, hidden), BF),
            pltpu.VMEM((hidden, width), BF),
            DMA((5,)),
        ]
        + comm_sems(size, n)
        + scatter_scratch(size, rows, width, n)
        + [DMA((2,)), DMA((1,))]
        + ([DMA((3,))] if layer == 1 else half_scratch(parts, *extra[0].shape[1:])),
        compiler_params=params(6 + layer),
        cost_estimate=cost(60e9, 40e6),
    )(grad, h1, gains, a2, hid, slope, wu, wd, *extra)


def attend_back_kernel(size, layer, parts, *refs):
    mid_ref, qkv_ref, qm_ref, km_ref, ctx_ref, lse_ref, w_ref, gdown_ref, down_came, gup_ref = refs[:10]
    refs = refs[10:]
    if layer == 0:
        aboves, refs = refs[:2], refs[2:]
    else:
        aboves = (None, None)
    dqkv_ref, gout_ref, down_out, up_out = refs[:4]
    da, ka, va, kt, dk, dv, w, w_sem = refs[4:12]
    sems, refs = refs[12:16], refs[16:]
    reduce = Reduce(layer, refs[:9])
    down = HalfReduce(layer, refs[9 : 9 + HALF])
    up = HalfReduce(layer, refs[9 + HALF : 9 + 2 * HALF])
    up_swap = HalfSwap(gup_ref, up.other, refs[9 + 2 * HALF])
    _, rows, wide = qkv_ref.shape
    length = size * rows
    e = qm_ref.shape[2]
    heads = wide // (3 * e)
    scale = e**-0.5
    c = scale * math.log2(math.e)
    depth = w_ref.shape[1] // parts
    n = chunks(rows)
    rc = rows // n
    bq = size * rc
    kc = bq
    g = Group(size)
    copies = [pltpu.make_async_copy(w_ref, w, w_sem.at[0])]
    for copy in copies:
        copy.start()
    g.greet(parts)
    gather = Gather(g, da, rc, sems)
    up_swap.copy().start()
    loads = down.loads(gdown_ref, down_came) + up.loads(gup_ref, None)
    for load in loads:
        load.start()

    def send(j):
        at = span(j, rc)
        da[g.me, at, :] = mid_ref[at, :].astype(BF)
        gather.start(j)

    run(n, send)
    lane = lax.broadcasted_iota(jnp.int32, (length, e), 1)
    whole = flat(qkv_ref[...])
    for h in range(heads):
        o = 3 * e * h
        ka[h, :, :e] = whole[:, o + e : o + 2 * e]
        ka[h, :, e:] = flat(km_ref[...])
        va[h, :, :e] = whole[:, o + 2 * e : o + 3 * e]
        va[h, :, e:] = jnp.where(lane < 3, 1.0, 0.0).astype(BF)
        kt[h] = whole[:, o + e : o + 2 * e].T
    dk[...] = jnp.zeros_like(dk)
    dv[...] = jnp.zeros_like(dv)
    ql = lax.broadcasted_iota(jnp.int32, (bq, e), 1)
    for copy in copies + loads:
        copy.wait()
    down.middle()

    def out_grad(z):
        cols = pl.ds(pl.multiple_of(z * depth, depth), depth)
        return dg(flat(ctx_ref[...]), flat(da[:, :, cols]), TN)

    def work(j):
        at = span(j, rc)

        @pl.when(j == 0)
        def _():
            gather.relay(0)
            gather.ready(0)

        @pl.when(j == min(1, n - 1))
        def _():
            for i in range(1, n):
                gather.relay(i)
            for i in range(1, n):
                gather.ready(i)
            reduce.send(out_grad)

        @pl.when(j == n // 2)
        def _():
            up_swap.copy().wait_recv()
            up.middle()

        @pl.when(j == n - 1)
        def _():
            down.late()

        qm = flat(qm_ref[:, at, :])
        dctx = dg(flat(da[:, at, :]), w[...], NT).astype(BF)
        ctx = flat(ctx_ref[:, at, :])
        held_qkv = flat(qkv_ref[:, at, :])
        for h in range(heads):
            o = 3 * e * h
            qq = held_qkv[:, o : o + e]
            q = jnp.concatenate([qq, qm], axis=1)
            dc = dctx[:, h * e : (h + 1) * e]
            prod = dc.astype(F32) * ctx[:, h * e : (h + 1) * e].astype(F32)
            d = -jnp.sum(prod, axis=1, keepdims=True)
            d1 = d.astype(BF).astype(F32)
            d2 = (d - d1).astype(BF).astype(F32)
            d3 = d - d1 - d2
            ds_col = jnp.where(ql == 0, d1, jnp.where(ql == 1, d2, jnp.where(ql == 2, d3, 0.0)))
            dca = jnp.concatenate([dc, ds_col.astype(BF)], axis=1)
            lse = lse_ref[j, h : h + 1, :]
            dqt = None
            for k in range(length // kc):
                ks = slice(k * kc, (k + 1) * kc)
                s = dg(ka[h, ks, :], q, NT)
                p = jnp.exp2(s * c - lse)
                ds = (p * dg(va[h, ks, :], dca, NT)).astype(BF)
                dv[h, ks, :] += dg(p.astype(BF), dc, NN)
                dk[h, ks, :] += dg(ds, qq, NN)
                a = dg(kt[h, :, ks], ds, NN)
                dqt = a if dqt is None else dqt + a
            dqkv_ref[:, at, o : o + e] = (dqt * scale).T.astype(BF).reshape(size, rc, e)

    run(n, work)
    for h in range(heads):
        o = 3 * e * h
        dqkv_ref[:, :, o + e : o + 2 * e] = (dk[h] * scale).astype(BF).reshape(size, rows, e)
        dqkv_ref[:, :, o + 2 * e : o + 3 * e] = dv[h].astype(BF).reshape(size, rows, e)

    reduce.collect()
    up.late()
    down.finish(down_out, aboves[0])
    reduce.finish(gout_ref)
    up.finish(up_out, aboves[1])
    up_swap.copy().wait_send()
    gather.drain(n)


def attend_backward(size, replicas, layer, mid, qkv, qm, km, ctx, lse, w, grads, aboves):
    _, rows, wide = qkv.shape
    e = qm.shape[2]
    heads = wide // (3 * e)
    width = mid.shape[1]
    parts, depth = replicas, width // replicas
    length = size * rows
    n = chunks(rows)
    return pl.pallas_call(
        functools.partial(attend_back_kernel, size, layer, parts),
        out_shape=(
            shape(qkv.shape, BF),
            shape((heads * e, depth), F32),
            shape(grads[0].shape[1:], F32),
            shape(grads[2].shape[1:], F32),
        ),
        in_specs=[VM] * 6 + [HB] * (4 + len(aboves)),
        out_specs=(VM, VM, VM, VM),
        scratch_shapes=[
            pltpu.VMEM((size, rows, width), BF),
            pltpu.VMEM((heads, length, 2 * e), BF),
            pltpu.VMEM((heads, length, 2 * e), BF),
            pltpu.VMEM((heads, e, length), BF),
            pltpu.VMEM((heads, length, e), F32),
            pltpu.VMEM((heads, length, e), F32),
            pltpu.VMEM((heads * e, width), BF),
            DMA((1,)),
        ]
        + comm_sems(size, n)
        + reduce_scratch(parts, heads * e, depth)
        + half_scratch(parts, *grads[0].shape[1:])
        + half_scratch(parts, *grads[2].shape[1:])
        + [DMA((2,))],
        compiler_params=params(8 + layer),
        cost_estimate=cost(90e9, 40e6),
    )(mid, qkv, qm, km, ctx, lse, w, *grads, *aboves)


def qkv_back_kernel(
    size, layer, parts, dqkv_ref, a1_ref, x_ref, mid_ref, gain_ref, w_ref,
    dx_ref, gain_out, gqkv_out, came, gqkv_ref, w, w_sem, swap_sem, *scratch
):
    rows, width = x_ref.shape
    depth = width // parts
    n = chunks(rows)
    rc = rows // n
    g = Group(size)
    copies = [pltpu.make_async_copy(w_ref, w, w_sem.at[0])]
    for copy in copies:
        copy.start()
    g.greet(side=True)
    swap = HalfSwap(gqkv_ref, came, swap_sem)
    scatter = Scatter(g, rc, scratch)
    def qkv_grad(z):
        cols = pl.ds(pl.multiple_of(z * depth, depth), depth)
        gqkv_ref[z] = dg(flat(a1_ref[:, :, cols]), flat(dqkv_ref[...]), TN).astype(BF)

    run(parts, qkv_grad)
    swap.copy().start()
    out = pltpu.make_async_copy(gqkv_ref, gqkv_out, w_sem.at[1])
    out.start()
    for copy in copies:
        copy.wait()

    def work(j):
        at = span(j, rc)
        held = flat(dqkv_ref[:, at, :])
        for z in range(parts):
            cols = slice(z * depth, (z + 1) * depth)
            scatter.part[:, at, cols] = dg(held, w[cols, :], NT).reshape(size, rc, depth)
        scatter.first(j)
        scatter.second(j)

    run(n, work)
    gain_out[...] = jnp.zeros_like(gain_out)

    def last(j):
        at = span(j, rc)
        dh, dgain = normed_back(
            x_ref[at, :].astype(F32), gain_ref[layer, 0:1, :], scatter.third(j)
        )
        dx_ref[at, :] = (mid_ref[at, :] + dh).astype(BF)
        gain_out[...] += dgain

    run(n, last)
    swap.copy().wait_recv()
    swap.copy().wait_send()
    out.wait()
    scatter.drain(n)


def qkv_backward(size, replicas, layer, dqkv, a1, x, mid, gains, w):
    rows, width = x.shape
    wide = w.shape[1]
    parts, depth = replicas, width // replicas
    n = chunks(rows)
    return pl.pallas_call(
        functools.partial(qkv_back_kernel, size, layer, parts),
        out_shape=(
            shape((rows, width), BF),
            shape((1, width), F32),
            shape((parts, depth, wide), BF),
            shape((parts, depth // 2, wide), BF),
        ),
        in_specs=[VM] * 5 + [HB],
        out_specs=(VM, VM, HB, HB),
        scratch_shapes=[
            pltpu.VMEM((parts, depth, wide), BF),
            pltpu.VMEM((width, wide), BF),
            DMA((2,)),
            DMA((2,)),
        ]
        + scatter_scratch(size, rows, width, n),
        compiler_params=params(11),
        cost_estimate=cost(30e9, 30e6),
    )(dqkv, a1, x, mid, gains, w)


def last_kernel(
    size, parts, dqkv_ref, a1_ref, x_ref, mid_ref, gain_ref, w_ref, two_ref, above_ref, dx1_ref,
    qkv_above, gain_out, gqkv_out, dx_out,
    gqkv, swap_sem, w, dx, gsum, gcame, w_sem, x_sem, x_send, x_recv, g_send, g_recv, *scratch
):
    rows, width = x_ref.shape
    depth = width // parts
    n = chunks(rows)
    rc = rows // n
    g = Group(size)
    section = lax.axis_index("section")
    d = lax.axis_index("dp")
    copy = pltpu.make_async_copy(w_ref, w, w_sem.at[0])
    copy.start()
    reduce = HalfReduce(0, scratch[:HALF])
    swap = HalfSwap(gqkv, reduce.other, swap_sem)
    scatter = Scatter(g, rc, scratch[HALF:])
    g.greet(parts)

    def upper():
        return far_copy(
            dx1_ref, dx_out.at[0], x_send.at[n], x_recv.at[n], {"section": 1 - section}
        )

    def keep_upper():
        return pltpu.make_async_copy(dx1_ref, dx_out.at[1], x_sem.at[0])

    def lower(j):
        at = span(j, rc)
        return far_copy(
            dx.at[at], dx_out.at[1, at], x_send.at[j], x_recv.at[j], {"section": 1 - section}
        )

    def keep_lower(j):
        at = span(j, rc)
        return pltpu.make_async_copy(dx.at[at], dx_out.at[0, at], x_sem.at[j])

    def qkv_grad(z):
        cols = pl.ds(pl.multiple_of(z * depth, depth), depth)
        gqkv[z] = dg(flat(a1_ref[:, :, cols]), flat(dqkv_ref[...]), TN).astype(BF)

    run(parts, qkv_grad)
    swap.copy().start()
    load = reduce.loads(gqkv, None)[0]
    load.start()

    @pl.when(section == 1)
    def _():
        keep_upper().start()

    copy.wait()

    def work(j):
        at = span(j, rc)
        held = flat(dqkv_ref[:, at, :])
        for z in range(parts):
            cols = slice(z * depth, (z + 1) * depth)
            scatter.part[:, at, cols] = dg(held, w[cols, :], NT).reshape(size, rc, depth)
        scatter.first(j)
        scatter.second(j)

    run(n, work)
    load.wait()
    swap.copy().wait_recv()
    reduce.middle()

    @pl.when(section == 0)
    def _():
        upper().start()

    gsum[0] = jnp.zeros_like(gsum[0])

    def last(j):
        at = span(j, rc)
        dh, dgain = normed_back(x_ref[at, :].astype(F32), gain_ref[0, 0:1, :], scatter.third(j))
        dx[at, :] = (mid_ref[at, :] + dh).astype(BF)

        @pl.when(section == 0)
        def _():
            keep_lower(j).start()

        @pl.when(section == 1)
        def _():
            lower(j).start()

        gsum[0, 0:1, :] += dgain

    run(n, last)
    gsum[0, 1:2, :] = two_ref[...]
    gsum[0, 2:4, :] = above_ref[...]

    targets = [
        [{"tensor": g.sibling}],
        [{"tensor": g.ahead(k) * 2 + g.core} for k in range(1, g.chips)],
        [{"dp": lax.rem(d + k, parts)} for k in range(1, parts)],
        [{"section": 1 - section}],
    ]
    slot = 0
    sent = []

    def exchange(stage):
        nonlocal slot
        copies = []
        for target in targets[stage]:
            copies.append(
                far_copy(gsum.at[stage], gcame.at[slot], g_send.at[slot], g_recv.at[slot], target)
            )
            copies[-1].start()
            slot += 1
        total = gsum[stage]
        for i, copy in enumerate(copies):
            copy.wait_recv()
            total = total + gcame[slot - len(copies) + i]
        gsum[stage + 1] = total
        sent.extend(copies)

    for stage in range(4):
        exchange(stage)
    gain_out[...] = gsum[4]
    reduce.late()

    @pl.when(section == 0)
    def _():
        for j in range(n):
            lower(j).wait_recv()
            keep_lower(j).wait()
        upper().wait_send()

    @pl.when(section == 1)
    def _():
        keep_upper().wait()
        upper().wait_recv()
        for j in range(n):
            lower(j).wait_send()

    reduce.finish(gqkv_out, qkv_above)
    swap.copy().wait_send()
    for copy in sent:
        copy.wait_send()
    scatter.drain(n)


def last_backward(size, replicas, dqkv, a1, x, mid, gains, w, two, above, dx1, qkv_above):
    rows, width = x.shape
    wide = w.shape[1]
    depth = width // replicas
    n = chunks(rows)
    slots = 1 + (size // 2 - 1) + (replicas - 1) + 1
    return pl.pallas_call(
        functools.partial(last_kernel, size, replicas),
        out_shape=(
            shape((8, width), F32),
            shape((depth, wide), F32),
            shape((2, rows, width), BF),
        ),
        in_specs=[VM] * 5 + [HB, VM, VM, HB, HB],
        out_specs=(VM, VM, HB),
        scratch_shapes=[
            pltpu.VMEM((replicas, depth, wide), BF),
            DMA((2,)),
            pltpu.VMEM((width, wide), BF),
            pltpu.VMEM((rows, width), BF),
            pltpu.VMEM((5, 8, width), F32),
            pltpu.VMEM((slots, 8, width), F32),
            DMA((1,)),
            DMA((n,)),
            DMA((n + 1,)),
            DMA((n + 1,)),
            DMA((slots,)),
            DMA((slots,)),
        ]
        + half_scratch(replicas, depth, wide)
        + scatter_scratch(size, rows, width, n),
        compiler_params=params(10),
        cost_estimate=cost(40e9, 30e6),
    )(dqkv, a1, x, mid, gains, w, two, above, dx1, qkv_above)


def scene_masks(segments, e):
    same = (segments[..., None] == jnp.arange(e, dtype=jnp.int32)).astype(F32)
    used = jnp.arange(e) < SCENES
    return (
        jnp.where(used, same * MASKED, 0.0).astype(BF),
        jnp.where(used, 1.0 - same, 0.0).astype(BF),
    )


def shards(
    block_input,
    segment_ids,
    cotangent,
    norm_one_gain,
    qkv_weight,
    out_weight,
    norm_two_gain,
    up_weight,
    down_weight,
):
    section = lax.axis_index("section")
    size = lax.axis_size("tensor")
    replicas = lax.axis_size("dp")

    mine = [
        qkv_weight[0].reshape((qkv_weight.shape[1], -1)),
        out_weight[0].reshape((-1, out_weight.shape[3])),
        up_weight[0],
        down_weight[0],
    ]
    mine = [w.astype(BF).reshape((2, -1, w.shape[1])) for w in mine]
    gains = jnp.concatenate(
        [norm_one_gain, norm_two_gain, jnp.zeros((6, norm_one_gain.shape[1]), F32)], axis=0
    )
    segments = lax.dynamic_index_in_dim(segment_ids, section, 0, keepdims=False)
    x = lax.dynamic_index_in_dim(block_input, section, 0, keepdims=False)
    head_dim = qkv_weight.shape[3] // 3
    qm, km = scene_masks(segments.reshape((size, -1)), head_dim)
    qkv, gains, a1, w_qkv_0, w_out_0, h_qkv, h_out, h_up, h_down = first_forward(
        size, replicas, x, gains, mine
    )
    h1, ctx, lse, w_up_0, w_down_0 = attend(
        size, replicas, 0, qkv, qm, km, x, w_out_0, [(h_up, 0, False), (h_down, 0, True)]
    )
    y0, a2, hid, slope, w_qkv_1, w_out_1, w_up_1 = mlp_forward(
        size, replicas, 0, h1, gains, w_up_0, w_down_0,
        [(h_qkv, 1, False), (h_out, 1, True), (h_up, 1, False)],
    )
    kept = [(x, a1, qkv, ctx, lse, h1, a2, hid, slope)]
    qkv, a1 = qkv_forward(size, replicas, 1, y0, gains, w_qkv_1, [])
    h1, ctx, lse, w_down_1 = attend(
        size, replicas, 1, qkv, qm, km, y0, w_out_1, [(h_down, 1, True)]
    )
    y1, a2, hid, slope = mlp_forward(size, replicas, 1, h1, gains, w_up_1, w_down_1, [])
    kept.append((y0, a1, qkv, ctx, lse, h1, a2, hid, slope))
    weights = [
        (w_qkv_0, w_out_0, w_up_0, w_down_0),
        (w_qkv_1, w_out_1, w_up_1, w_down_1),
    ]
    grad = lax.dynamic_index_in_dim(cotangent, section, 0, keepdims=False)

    x, a1, qkv, ctx, lse, h1, a2, hid, slope = kept[1]
    w_qkv, w_out, w_up, w_down = weights[1]
    mid, gain_two, g_up, g_down, came, layer_out = mlp_backward(
        size, replicas, 1, grad, h1, gains, a2, hid, slope, w_up, w_down, [y0, y1]
    )
    d_qkv, out_1, down_1, up_1 = attend_backward(
        size, replicas, 1, mid, qkv, qm, km, ctx, lse, w_out, [g_down, came, g_up], []
    )
    dx1, gain_one, g_qkv, came = qkv_backward(
        size, replicas, 1, d_qkv, a1, x, mid, gains, w_qkv
    )
    gains_above = jnp.concatenate([gain_one, gain_two], axis=0)

    x, a1, qkv, ctx, lse, h1, a2, hid, slope = kept[0]
    w_qkv, w_out, w_up, w_down = weights[0]
    mid, gain_two, g_up, g_down, came, qkv_1 = mlp_backward(
        size, replicas, 0, dx1, h1, gains, a2, hid, slope, w_up, w_down, [g_qkv, came]
    )
    d_qkv, out_0, down_grad, up_grad = attend_backward(
        size, replicas, 0, mid, qkv, qm, km, ctx, lse, w_out,
        [g_down, came, g_up], [down_1, up_1],
    )
    gains, qkv_grad, input_out = last_backward(
        size, replicas, d_qkv, a1, x, mid, gains, w_qkv, gain_two, gains_above, dx1, qkv_1
    )
    out_grad = jnp.where(section == 0, out_0, out_1)
    gains = lax.dynamic_slice_in_dim(gains, 2 * section, 2, 0)
    return (
        layer_out[None],
        input_out[None],
        gains[0:1],
        qkv_grad.reshape(qkv_weight.shape),
        out_grad.reshape(out_weight.shape),
        gains[1:2],
        up_grad[None],
        down_grad[None],
    )


def solution(mesh):
    return jax.shard_map(
        shards,
        mesh=mesh,
        in_specs=(
            P(None, ("dp", "tensor"), None),
            P(None, "dp"),
            P(None, ("dp", "tensor"), None),
            P("section", None),
            P("section", "dp", "tensor", None),
            P("section", "tensor", None, "dp"),
            P("section", None),
            P("section", "dp", "tensor"),
            P("section", "tensor", "dp"),
        ),
        out_specs=(
            P("section", None, ("dp", "tensor"), None),
            P("section", None, ("dp", "tensor"), None),
            P("section", None),
            P("section", "dp", "tensor", None),
            P("section", "tensor", None, "dp"),
            P("section", None),
            P("section", "dp", "tensor"),
            P("section", "tensor", "dp"),
        ),
        check_vma=False,
    )
```

```python
import functools
import math

import jax
import jax.numpy as jnp
from jax import lax
from jax.experimental import pallas as pl
from jax.experimental.pallas import tpu as pltpu
from jax.sharding import PartitionSpec as P

F32 = jnp.float32
BF = jnp.bfloat16
NT = (((1,), (1,)), ((), ()))
NN = (((1,), (0,)), ((), ()))
TN = (((0,), (0,)), ((), ()))
MASKED = -1e30
SCENES = 3
MESH = pl.DeviceIdType.MESH
VM = pl.BlockSpec(memory_space=pltpu.VMEM)
HB = pl.BlockSpec(memory_space=pl.ANY)
DMA = pltpu.SemaphoreType.DMA
LIMIT = 58 << 20


def dg(a, b, dims):
    return lax.dot_general(a, b, dims, preferred_element_type=F32)


def chunks(rows):
    return 4 if rows % 64 == 0 else 1


def shape(dims, dtype):
    return jax.ShapeDtypeStruct(dims, dtype)


class Group:
    def __init__(self, size):
        self.size = size
        self.chips = size // 2
        self.me = lax.axis_index("tensor")
        self.chip = lax.div(self.me, 2)
        self.core = lax.rem(self.me, 2)
        self.sibling = self.chip * 2 + 1 - self.core

    def ahead(self, k):
        return lax.rem(self.chip + k, self.chips)

    def behind(self, k):
        return lax.rem(self.chip + self.chips - k, self.chips)

    def greet(self, replicas=0, side=False):
        barrier = pltpu.get_barrier_semaphore()
        targets = [self.sibling] + [self.ahead(k) * 2 + self.core for k in range(1, self.chips)]
        targets = [{"tensor": target} for target in targets]
        if replicas:
            d = lax.axis_index("dp")
            targets += [{"dp": lax.rem(d + k, replicas)} for k in range(1, replicas)]
        if replicas or side:
            targets += [{"section": 1 - lax.axis_index("section")}]
        for target in targets:
            pl.semaphore_signal(barrier, inc=1, device_id=target, device_id_type=MESH)
        pl.semaphore_wait(barrier, len(targets))


def remote(src, dst, send, recv, target):
    return pltpu.make_async_remote_copy(
        src_ref=src,
        dst_ref=dst,
        send_sem=send,
        recv_sem=recv,
        device_id={"tensor": target},
        device_id_type=MESH,
    )


def span(j, rc):
    return pl.ds(pl.multiple_of(j * rc, rc), rc)


def comm_sems(group_size, n):
    c = group_size // 2
    far, near = DMA((max(c - 1, 1), n)), DMA((c, n))
    return [far, far, near, near]


class Gather:
    def __init__(self, g, buf, rc, sems):
        self.g, self.buf, self.rc = g, buf, rc
        self.far_send, self.far_recv, self.near_send, self.near_recv = sems

    def far(self, k, j, origin, target):
        ref = self.buf.at[origin, span(j, self.rc)]
        return remote(ref, ref, self.far_send.at[k - 1, j], self.far_recv.at[k - 1, j], target)

    def near(self, k, j, origin):
        ref = self.buf.at[origin, span(j, self.rc)]
        return remote(
            ref, ref, self.near_send.at[k, j], self.near_recv.at[k, j], self.g.sibling
        )

    def start(self, j):
        g = self.g
        for k in range(1, g.chips):
            self.far(k, j, g.me, g.ahead(k) * 2 + g.core).start()
        self.near(0, j, g.me).start()

    def relay(self, j):
        g = self.g
        for k in range(1, g.chips):
            origin = g.behind(k) * 2 + g.core
            self.far(k, j, origin, g.me).wait_recv()
            self.near(k, j, origin).start()

    def ready(self, j):
        g = self.g
        self.near(0, j, g.sibling).wait_recv()
        for k in range(1, g.chips):
            self.near(k, j, g.behind(k) * 2 + 1 - g.core).wait_recv()

    def drain(self, n):
        g = self.g

        def one(j, _):
            for k in range(1, g.chips):
                self.far(k, j, g.me, g.sibling).wait_send()
            for k in range(g.chips):
                self.near(k, j, g.me).wait_send()
            return 0

        lax.fori_loop(0, n, one, 0)


def scatter_scratch(group_size, rows, width, n):
    c = group_size // 2
    far = pltpu.VMEM((max(c - 1, 1), rows, width), BF)
    near = pltpu.VMEM((c, rows, width), BF)
    return [pltpu.VMEM((group_size, rows, width), F32), near, near, far, far] + comm_sems(
        group_size, n
    )


class Scatter:
    def __init__(self, g, rc, scratch):
        self.g, self.rc = g, rc
        self.part, self.near_out, self.near_in, self.far_out, self.far_in = scratch[:5]
        self.far_send, self.far_recv, self.near_send, self.near_recv = scratch[5:]

    def near(self, k, j):
        rows = span(j, self.rc)
        return remote(
            self.near_out.at[k, rows],
            self.near_in.at[k, rows],
            self.near_send.at[k, j],
            self.near_recv.at[k, j],
            self.g.sibling,
        )

    def far(self, k, j):
        rows = span(j, self.rc)
        return remote(
            self.far_out.at[k - 1, rows],
            self.far_in.at[k - 1, rows],
            self.far_send.at[k - 1, j],
            self.far_recv.at[k - 1, j],
            self.g.ahead(k) * 2 + self.g.core,
        )

    def first(self, j):
        g, rows = self.g, span(j, self.rc)
        for k in list(range(1, g.chips)) + [0]:
            owner = g.ahead(k) * 2 + 1 - g.core
            self.near_out[k, rows, :] = self.part[owner, rows, :].astype(BF)
            self.near(k, j).start()

    def second(self, j):
        g, rows = self.g, span(j, self.rc)
        for k in range(1, g.chips):
            owner = g.ahead(k) * 2 + g.core
            self.near(k, j).wait_recv()
            both = self.part[owner, rows, :] + self.near_in[k, rows, :].astype(F32)
            self.far_out[k - 1, rows, :] = both.astype(BF)
            self.far(k, j).start()

    def third(self, j):
        g, rows = self.g, span(j, self.rc)
        self.near(0, j).wait_recv()
        total = self.part[g.me, rows, :] + self.near_in[0, rows, :].astype(F32)
        for k in range(1, g.chips):
            self.far(k, j).wait_recv()
            total = total + self.far_in[k - 1, rows, :].astype(F32)
        return total

    def drain(self, n):
        g = self.g

        def one(j, _):
            for k in range(1, g.chips):
                self.far(k, j).wait_send()
            for k in range(g.chips):
                self.near(k, j).wait_send()
            return 0

        lax.fori_loop(0, n, one, 0)


def far_copy(src, dst, send, recv, target):
    return pltpu.make_async_remote_copy(
        src_ref=src,
        dst_ref=dst,
        send_sem=send,
        recv_sem=recv,
        device_id=target,
        device_id_type=MESH,
    )


class Swap:
    def __init__(self, src, stage, sems):
        self.src, self.stage, self.sems = src, stage, sems
        self.s = lax.axis_index("section")

    def copies(self, layer):
        local = pltpu.make_async_copy(self.src.at[self.s], self.stage.at[self.s], self.sems.at[0])
        side = far_copy(
            self.src.at[1 - self.s],
            self.stage.at[layer],
            self.sems.at[1],
            self.sems.at[2],
            {"section": 1 - self.s},
        )
        return local, side

    def start(self):
        for copy in self.copies(self.s):
            copy.start()

    def arrive(self):
        local, side = self.copies(1 - self.s)
        local.wait()
        side.wait_recv()

    def finish(self):
        self.copies(self.s)[1].wait_send()


def reduce_scratch(replicas, rows, cols):
    many = pltpu.VMEM((replicas - 1, rows, cols), BF)
    one = pltpu.VMEM((rows, cols), BF)
    far, side = DMA((replicas - 1, 2)), DMA((2,))
    return [pltpu.VMEM((rows, cols), F32), many, many, one, one, far, far, side, side]


class Reduce:
    def __init__(self, layer, scratch):
        self.layer = layer
        self.own, self.away, self.came, self.over, self.back = scratch[:5]
        self.z_send, self.z_recv, self.y_send, self.y_recv = scratch[5:]
        self.replicas = self.away.shape[0] + 1
        self.half = self.own.shape[0] // 2
        self.d = lax.axis_index("dp")
        self.s = lax.axis_index("section")

    def target(self, k):
        return lax.rem(self.d + k, self.replicas)

    def part(self, i):
        return pl.ds(pl.multiple_of(i * self.half, self.half), self.half)

    def z_copy(self, k, i):
        part = self.part(i)
        return far_copy(
            self.away.at[k - 1, part],
            self.came.at[k - 1, part],
            self.z_send.at[k - 1, i],
            self.z_recv.at[k - 1, i],
            {"dp": self.target(k)},
        )

    def y_copy(self, i):
        part = self.part(i)
        return far_copy(
            self.over.at[part],
            self.back.at[part],
            self.y_send.at[i],
            self.y_recv.at[i],
            {"section": 1 - self.s},
        )

    def send(self, block):
        def one(i):
            k = i + 1
            self.away[i] = block(self.target(k)).astype(BF)
            self.z_copy(k, 0).start()
            self.z_copy(k, 1).start()

        run(self.replicas - 1, one)
        self.own[...] = block(self.d)

    def collect(self):
        def one(i):
            part = self.part(i)
            total = self.own[part, :]
            for k in range(1, self.replicas):
                self.z_copy(k, i).wait_recv()
                total = total + self.came[k - 1, part, :].astype(F32)
            self.own[part, :] = total
            self.over[part, :] = total.astype(BF)

            @pl.when(self.s != self.layer)
            def _():
                self.y_copy(i).start()

        run(2, one)

    def finish(self, out):
        @pl.when(self.s == self.layer)
        def _():
            self.y_copy(0).wait_recv()
            self.y_copy(1).wait_recv()
            out[...] = self.own[...] + self.back[...].astype(F32)

        @pl.when(self.s != self.layer)
        def _():
            self.y_copy(0).wait_send()
            self.y_copy(1).wait_send()
            out[...] = self.own[...]

        for k in range(1, self.replicas):
            self.z_copy(k, 0).wait_send()
            self.z_copy(k, 1).wait_send()


class HalfSwap:
    def __init__(self, src, came, sems):
        self.src, self.came, self.sems = src, came, sems
        self.s = lax.axis_index("section")
        self.rows = came.shape[1]

    def copy(self):
        at = pl.ds(pl.multiple_of((1 - self.s) * self.rows, self.rows), self.rows)
        return far_copy(
            self.src.at[:, at],
            self.came,
            self.sems.at[0],
            self.sems.at[1],
            {"section": 1 - self.s},
        )


def half_scratch(replicas, rows, cols):
    rows = rows // 2
    all_, far = pltpu.VMEM((replicas, rows, cols), BF), pltpu.VMEM((replicas - 1, rows, cols), BF)
    one = pltpu.VMEM((rows, cols), BF)
    z = DMA((replicas - 1,))
    return [all_, all_, far, far, pltpu.VMEM((rows, cols), F32), one, one, DMA((3,)), z, z, DMA((2,))]


HALF = 11


class HalfReduce:
    def __init__(self, layer, scratch):
        self.layer = layer
        self.mine, self.other, self.away, self.came, self.own, self.over, self.back = scratch[:7]
        self.in_sem, self.z_send, self.z_recv, self.y_sem = scratch[7:]
        self.replicas, self.rows = self.mine.shape[:2]
        self.s = lax.axis_index("section")
        self.d = lax.axis_index("dp")

    def half(self, s):
        return pl.ds(pl.multiple_of(s * self.rows, self.rows), self.rows)

    def loads(self, src, other):
        loads = [pltpu.make_async_copy(src.at[:, self.half(self.s)], self.mine, self.in_sem.at[0])]
        if other is not None:
            loads.append(pltpu.make_async_copy(other, self.other, self.in_sem.at[1]))
        return loads

    def z_copy(self, k):
        return far_copy(
            self.away.at[k - 1],
            self.came.at[k - 1],
            self.z_send.at[k - 1],
            self.z_recv.at[k - 1],
            {"dp": lax.rem(self.d + k, self.replicas)},
        )

    def y_copy(self):
        return far_copy(
            self.over, self.back, self.y_sem.at[0], self.y_sem.at[1], {"section": 1 - self.s}
        )

    def middle(self):
        def both(z):
            return self.mine[z].astype(F32) + self.other[z].astype(F32)

        for k in range(1, self.replicas):
            self.away[k - 1] = both(lax.rem(self.d + k, self.replicas)).astype(BF)
            self.z_copy(k).start()
        self.own[...] = both(self.d)

    def late(self):
        total = self.own[...]
        for k in range(1, self.replicas):
            self.z_copy(k).wait_recv()
            total = total + self.came[k - 1].astype(F32)
        self.own[...] = total
        self.over[...] = total.astype(BF)

        @pl.when(self.s != self.layer)
        def _():
            self.y_copy().start()

    def finish(self, out, above=None):
        @pl.when(self.s == self.layer)
        def _():
            self.y_copy().wait_recv()
            out[self.half(self.s), :] = self.own[...]
            out[self.half(1 - self.s), :] = self.back[...].astype(F32)

        @pl.when(self.s != self.layer)
        def _():
            if above is None:
                out[...] = jnp.zeros_like(out)
            else:
                copy = pltpu.make_async_copy(above, out, self.in_sem.at[2])
                copy.start()
                copy.wait()
            self.y_copy().wait_send()

        for k in range(1, self.replicas):
            self.z_copy(k).wait_send()


class Spread:
    def __init__(self, src, dst, by_columns, sems):
        self.src, self.dst, self.by_columns = src, dst, by_columns
        self.own_sem, self.far_send, self.far_recv, self.side_send, self.side_recv = sems
        self.replicas = far = self.side_send.shape[0]
        self.s = lax.axis_index("section")
        self.d = lax.axis_index("dp")
        self.stages = [
            sorted({k, far - k}) for k in range(1, far // 2 + 1)
        ]

    def place(self, half, z):
        rows, cols = self.src.shape
        if self.by_columns:
            return self.dst.at[
                pl.ds(pl.multiple_of(half * rows, rows), rows),
                pl.ds(pl.multiple_of(z * cols, cols), cols),
            ]
        return self.dst.at[pl.ds(pl.multiple_of((2 * z + half) * rows, rows), rows)]

    def origin(self, k):
        return lax.rem(self.d + self.replicas - k, self.replicas)

    def own(self):
        return pltpu.make_async_copy(self.src, self.place(self.s, self.d), self.own_sem.at[0])

    def far(self, k, origin):
        return pltpu.make_async_remote_copy(
            src_ref=self.src,
            dst_ref=self.place(self.s, origin),
            send_sem=self.far_send.at[k - 1],
            recv_sem=self.far_recv.at[k - 1],
            device_id={"dp": lax.rem(self.d + k, self.replicas)},
            device_id_type=MESH,
        )

    def side(self, k, half):
        place = self.place(half, self.origin(k))
        return pltpu.make_async_remote_copy(
            src_ref=self.src if k == 0 else place,
            dst_ref=place,
            send_sem=self.side_send.at[k],
            recv_sem=self.side_recv.at[k],
            device_id={"section": 1 - self.s},
            device_id_type=MESH,
        )

    def start(self):
        for k in self.stages[0]:
            self.far(k, self.d).start()
        self.side(0, self.s).start()
        self.own().start()

    def step(self, i):
        for k in self.stages[i]:
            self.far(k, self.origin(k)).wait_recv()
            self.side(k, self.s).start()
        if i + 1 < len(self.stages):
            for k in self.stages[i + 1]:
                self.far(k, self.d).start()

    def finish(self):
        self.own().wait()
        for k in range(self.replicas):
            self.side(k, 1 - self.s).wait_recv()
        for k in range(1, self.replicas):
            self.far(k, self.d).wait_send()
        for k in range(self.replicas):
            self.side(k, self.s).wait_send()


class ZGather:
    def __init__(self, src, got, sems):
        self.src, self.got = src, got
        self.own_sem, self.send, self.recv = sems
        self.replicas = got.shape[0]
        self.d = lax.axis_index("dp")

    def own(self):
        return pltpu.make_async_copy(self.src, self.got.at[self.d], self.own_sem.at[0])

    def far(self, k, origin):
        return far_copy(
            self.src,
            self.got.at[origin],
            self.send.at[k - 1],
            self.recv.at[k - 1],
            {"dp": lax.rem(self.d + k, self.replicas)},
        )

    def start(self):
        for k in range(1, self.replicas):
            self.far(k, self.d).start()
        self.own().start()

    def step(self, i):
        pass

    def finish(self):
        self.own().wait()
        for k in range(1, self.replicas):
            self.far(k, lax.rem(self.d + self.replicas - k, self.replicas)).wait_recv()
        for k in range(1, self.replicas):
            self.far(k, self.d).wait_send()


class YJoin:
    def __init__(self, got, dst, by_columns, sems):
        self.got, self.dst, self.by_columns = got, dst, by_columns
        self.own_sem, self.send, self.recv = sems
        self.replicas, self.rows, self.cols = got.shape
        self.s = lax.axis_index("section")

    def place(self, half, z):
        rows, cols = self.rows, self.cols
        if self.by_columns:
            return self.dst.at[
                pl.ds(pl.multiple_of(half * rows, rows), rows), pl.ds(z * cols, cols)
            ]
        return self.dst.at[pl.ds(pl.multiple_of((2 * z + half) * rows, rows), rows)]

    def own(self, z):
        return pltpu.make_async_copy(self.got.at[z], self.place(self.s, z), self.own_sem.at[z])

    def side(self, z, half):
        return far_copy(
            self.got.at[z],
            self.place(half, z),
            self.send.at[z],
            self.recv.at[z],
            {"section": 1 - self.s},
        )

    def start(self):
        for z in range(self.replicas):
            self.side(z, self.s).start()
            self.own(z).start()

    def step(self, i):
        pass

    def finish(self):
        for z in range(self.replicas):
            self.own(z).wait()
            self.side(z, 1 - self.s).wait_recv()
        for z in range(self.replicas):
            self.side(z, self.s).wait_send()


def rider_sems(replicas):
    far, side = DMA((replicas - 1,)), DMA((replicas,))
    return [DMA((1,)), far, far, side, side]


class Riders:
    def __init__(self, srcs, dsts, columns, sems):
        self.all = []
        for src, dst, (kind, layer, by) in zip(srcs, dsts, columns):
            count = 5 if kind == "spread" else 3
            own, sems = sems[:count], sems[count:]
            if kind == "spread":
                self.all.append(Spread(src.at[layer], dst, by, own))
            elif kind == "z":
                self.all.append(ZGather(src.at[layer], dst, own))
            else:
                self.all.append(YJoin(src, dst, by, own))
        self.replicas = self.all[0].replicas if self.all else 0

    def start(self):
        for one in self.all:
            one.start()

    def step(self, j, n):
        if not self.all:
            return
        stages = self.replicas // 2
        for i in range(stages):

            @pl.when(j == n * (i + 1) // stages - 1)
            def _(i=i):
                for one in self.all:
                    one.step(i)

    def finish(self):
        for one in self.all:
            one.finish()


def riding(riders, replicas):
    arrays = [array for array, _, _, _ in riders]
    columns = tuple(rider[1:] for rider in riders)
    outs, sems = [], []
    for array, kind, _, by in riders:
        rows, cols = array.shape[1:]
        if kind == "z":
            outs.append(shape((replicas, rows, cols), BF))
        else:
            outs.append(
                shape((2 * rows, replicas * cols) if by else (2 * replicas * rows, cols), BF)
            )
        far, side = DMA((replicas - 1,)), DMA((replicas,))
        sems += {
            "spread": rider_sems(replicas),
            "z": [DMA((1,)), far, far],
            "y": [side, side, side],
        }[kind]
    return arrays, columns, outs, sems


def params(key):
    return pltpu.CompilerParams(
        vmem_limit_bytes=LIMIT, collective_id=key, has_side_effects=True
    )


def cost(flops, moved, exps=0):
    return pl.CostEstimate(flops=int(flops), bytes_accessed=int(moved), transcendentals=int(exps))


def normed(source):
    center = source - jnp.mean(source, axis=-1, keepdims=True)
    r = lax.rsqrt(jnp.mean(center * center, axis=-1, keepdims=True) + 1e-05)
    return center * r, r


def normed_back(source, gain, grad):
    n, r = normed(source)
    e = grad * gain
    dh = r * (
        e - jnp.mean(e, axis=-1, keepdims=True) - n * jnp.mean(e * n, axis=-1, keepdims=True)
    )
    return dh, jnp.sum(grad * n, axis=0, keepdims=True)


def flat(value):
    return value.reshape((value.shape[0] * value.shape[1],) + value.shape[2:])


def run(n, body):
    def one(j, carry):
        body(j)
        return carry

    lax.fori_loop(0, n, one, 0)


def first_kernel(
    size, replicas, x_ref, gain_ref, wq_ref, wo_ref, wu_ref, wd_ref,
    qkv_ref, gains_out, a1_out, wq_out, wo_out, q_stage, o_stage, u_stage, d_stage, u_got,
    a1, w, gains, own_sem, q_sem, o_sem, u_sem, d_sem, gain_sem, *sems
):
    rows, width = x_ref.shape
    n = chunks(rows)
    rc = rows // n
    g = Group(size)
    section = lax.axis_index("section")
    gather = Gather(g, a1, rc, sems[:4])
    swaps = [
        Swap(wq_ref, q_stage, q_sem),
        Swap(wo_ref, o_stage, o_sem),
        Swap(wu_ref, u_stage, u_sem),
        Swap(wd_ref, d_stage, d_sem),
    ]
    spreads = [
        Spread(q_stage.at[0], w, False, sems[4:9]),
        Spread(o_stage.at[0], wo_out, True, sems[9:14]),
    ]
    riders = Riders([], [], (), [])
    riders.all = spreads
    riders.replicas = replicas
    g.greet(replicas)

    def gain_copy(layer):
        return far_copy(
            gain_ref, gains.at[layer], gain_sem.at[0], gain_sem.at[1], {"section": 1 - section}
        )

    gain_copy(section).start()
    swaps[0].start()
    swaps[1].start()
    gains[section] = gain_ref[...]
    gain_copy(1 - section).wait_recv()
    gains_out[...] = gains[...]

    def send(j):
        at = span(j, rc)
        a = normed(x_ref[at, :].astype(F32))[0] * gains[0, 0:1, :]
        a1[g.me, at, :] = a.astype(BF)
        gather.start(j)

    run(n, send)
    swaps[0].arrive()
    swaps[1].arrive()
    riders.start()
    swaps[2].start()
    swaps[3].start()

    u_gather = ZGather(u_stage.at[0], u_got, sems[14:17])

    def relay(j):
        gather.relay(j)

        @pl.when(j == n - 1)
        def _():
            swaps[2].arrive()
            u_gather.start()

        riders.step(j, n)

    run(n, relay)
    riders.finish()
    outs = [
        pltpu.make_async_copy(w, wq_out, own_sem.at[0]),
        pltpu.make_async_copy(a1, a1_out, own_sem.at[1]),
    ]
    outs[0].start()

    def multiply(j):
        at = span(j, rc)
        gather.ready(j)
        r = dg(flat(a1[:, at, :]), w[...], NN).astype(BF)
        qkv_ref[:, at, :] = r.reshape(size, rc, r.shape[1])

    run(n, multiply)
    outs[1].start()
    swaps[3].arrive()
    u_gather.finish()
    for swap in swaps:
        swap.finish()
    gain_copy(section).wait_send()
    gather.drain(n)
    for out in outs:
        out.wait()


def first_forward(size, replicas, x, gains, ws):
    rows, width = x.shape
    wide = ws[0].shape[2]
    deep = 2 * ws[1].shape[1]
    n = chunks(rows)
    return pl.pallas_call(
        functools.partial(first_kernel, size, replicas),
        out_shape=[
            shape((size, rows, wide), BF),
            shape((2,) + gains.shape, F32),
            shape((size, rows, width), BF),
            shape((width, wide), BF),
            shape((deep, width), BF),
        ]
        + [shape(w.shape, BF) for w in ws]
        + [shape((replicas,) + ws[2].shape[1:], BF)],
        in_specs=[VM, VM] + [HB] * 4,
        out_specs=[VM, VM] + [HB] * 8,
        scratch_shapes=[
            pltpu.VMEM((size, rows, width), BF),
            pltpu.VMEM((width, wide), BF),
            pltpu.VMEM((2,) + gains.shape, F32),
            DMA((2,)),
            DMA((3,)),
            DMA((3,)),
            DMA((3,)),
            DMA((3,)),
            DMA((2,)),
        ]
        + comm_sems(size, n)
        + rider_sems(replicas) * 2
        + [DMA((1,)), DMA((replicas - 1,)), DMA((replicas - 1,))],
        compiler_params=params(0),
        cost_estimate=cost(30e9, 30e6),
    )(x, gains, *ws)


def qkv_kernel(size, layer, columns, *refs):
    m = len(columns)
    x_ref, gain_ref, w_ref = refs[:3]
    halves, refs = refs[3 : 3 + m], refs[3 + m :]
    qkv_ref, a1_out = refs[:2]
    wholes, refs = refs[2 : 2 + m], refs[2 + m :]
    a1, w, w_sem, out_sem = refs[:4]
    sems, refs = refs[4:8], refs[8:]
    riders = Riders(halves, wholes, columns, refs)
    rows, width = x_ref.shape
    n = chunks(rows)
    rc = rows // n
    g = Group(size)
    copy = pltpu.make_async_copy(w_ref, w, w_sem.at[0])
    copy.start()
    g.greet(riders.replicas)
    gather = Gather(g, a1, rc, sems)
    riders.start()

    def send(j):
        at = span(j, rc)
        a = normed(x_ref[at, :].astype(F32))[0] * gain_ref[layer, 0:1, :]
        a1[g.me, at, :] = a.astype(BF)
        gather.start(j)

    run(n, send)
    copy.wait()

    def work(j):
        at = span(j, rc)
        gather.relay(j)
        gather.ready(j)
        r = dg(flat(a1[:, at, :]), w[...], NN).astype(BF)
        qkv_ref[:, at, :] = r.reshape(size, rc, r.shape[1])
        riders.step(j, n)

    run(n, work)
    out = pltpu.make_async_copy(a1, a1_out, out_sem.at[0])
    out.start()
    riders.finish()
    gather.drain(n)
    out.wait()


def qkv_forward(size, replicas, layer, x, gains, w, riders):
    rows, width = x.shape
    wide = w.shape[1]
    n = chunks(rows)
    halves, columns, outs, sems = riding(riders, replicas)
    return pl.pallas_call(
        functools.partial(qkv_kernel, size, layer, columns),
        out_shape=[
            shape((size, rows, wide), BF),
            shape((size, rows, width), BF),
        ]
        + outs,
        in_specs=[VM, VM, HB] + [HB] * len(riders),
        out_specs=[VM, HB] + [HB] * len(outs),
        scratch_shapes=[
            pltpu.VMEM((size, rows, width), BF),
            pltpu.VMEM((width, wide), BF),
            DMA((1,)),
            DMA((1,)),
        ]
        + comm_sems(size, n)
        + sems,
        compiler_params=params(layer),
        cost_estimate=cost(20e9, 30e6),
    )(x, gains, w, *halves)


def attend_kernel(size, layer, columns, *refs):
    m = len(columns)
    qkv_ref, qm_ref, km_ref, x_ref, w_ref = refs[:5]
    halves, refs = refs[5 : 5 + m], refs[5 + m :]
    h1_ref, ctx_ref, lse_ref = refs[:3]
    wholes, refs = refs[3 : 3 + m], refs[3 + m :]
    ka, vt, w, w_sem = refs[:4]
    scratch, refs = refs[4:13], refs[13:]
    riders = Riders(halves, wholes, columns, refs)
    _, rows, wide = qkv_ref.shape
    length = size * rows
    e = qm_ref.shape[2]
    heads = wide // (3 * e)
    c = e**-0.5 * math.log2(math.e)
    n = chunks(rows)
    rc = rows // n
    bq = size * rc
    kc = bq
    g = Group(size)
    copy = pltpu.make_async_copy(w_ref, w, w_sem.at[0])
    copy.start()
    g.greet(riders.replicas)
    riders.start()
    scatter = Scatter(g, rc, scratch)
    whole = flat(qkv_ref[...])
    for h in range(heads):
        o = 3 * e * h
        ka[h, :, :e] = whole[:, o + e : o + 2 * e]
        ka[h, :, e:] = flat(km_ref[...])
        vt[h, :e, :] = whole[:, o + 2 * e : o + 3 * e].T
        vt[h, e:, :] = jnp.ones((16, length), BF)
    copy.wait()

    def work(j):
        at = span(j, rc)
        qm = flat(qm_ref[:, at, :])
        found = []
        held_qkv = flat(qkv_ref[:, at, :])
        for h in range(heads):
            o = 3 * e * h
            q = jnp.concatenate([held_qkv[:, o : o + e], qm], axis=1)
            held = []
            top = None
            for k in range(length // kc):
                s = dg(ka[h, k * kc : (k + 1) * kc, :], q, NT)
                t = jnp.max(s, axis=0, keepdims=True)
                top = t if top is None else jnp.maximum(top, t)
                held.append(s)
            top = top * c
            acc = None
            for k in range(length // kc):
                p = jnp.exp2(held[k] * c - top).astype(BF)
                a = dg(vt[h, :, k * kc : (k + 1) * kc], p, NN)
                acc = a if acc is None else acc + a
            total = acc[e : e + 1]
            found.append((acc[:e] * (1.0 / total)).astype(BF))
            lse_ref[j, h : h + 1, :] = top + jnp.log2(total)
        ctx = (jnp.concatenate(found, axis=0) if heads > 1 else found[0]).T
        ctx_ref[:, at, :] = ctx.reshape(size, rc, heads * e)
        width = x_ref.shape[1]
        scatter.part[:, at, :] = dg(ctx, w[...], NN).reshape(size, rc, width)
        scatter.first(j)
        scatter.second(j)
        riders.step(j, n)

    run(n, work)

    def last(j):
        at = span(j, rc)
        h1_ref[at, :] = x_ref[at, :].astype(F32) + scatter.third(j)

    run(n, last)
    scatter.drain(n)
    riders.finish()


def attend(size, replicas, layer, qkv, qm, km, x, w, riders):
    _, rows, wide = qkv.shape
    e = qm.shape[2]
    heads = wide // (3 * e)
    width = x.shape[1]
    n = chunks(rows)
    halves, columns, outs, sems = riding(riders, replicas)
    return pl.pallas_call(
        functools.partial(attend_kernel, size, layer, columns),
        out_shape=[
            shape((rows, width), F32),
            shape((size, rows, heads * e), BF),
            shape((n, heads, size * rows // n), F32),
        ]
        + outs,
        in_specs=[VM, VM, VM, VM, HB] + [HB] * len(riders),
        out_specs=[VM, VM, VM] + [HB] * len(outs),
        scratch_shapes=[
            pltpu.VMEM((heads, size * rows, 2 * e), BF),
            pltpu.VMEM((heads, e + 16, size * rows), BF),
            pltpu.VMEM((heads * e, width), BF),
            DMA((1,)),
        ]
        + scatter_scratch(size, rows, width, n)
        + sems,
        compiler_params=params(2 + layer),
        cost_estimate=cost(60e9, 20e6),
    )(qkv, qm, km, x, w, *halves)


def mlp_kernel(size, layer, columns, *refs):
    m = len(columns)
    h1_ref, gain_ref, wu_ref, wd_ref = refs[:4]
    halves, refs = refs[4 : 4 + m], refs[4 + m :]
    y_ref, a2_out, hid_out, slope_out = refs[:4]
    wholes, refs = refs[4 : 4 + m], refs[4 + m :]
    a2, hid, slope, wu, wd, w_sem, out_sem = refs[:7]
    scratch, refs = refs[7:20], refs[20:]
    riders = Riders(halves, wholes, columns, refs)
    rows, width = h1_ref.shape
    hidden = wu_ref.shape[1]
    fb = min(256, hidden)
    n = chunks(rows)
    rc = rows // n
    g = Group(size)
    copies = [
        pltpu.make_async_copy(wu_ref, wu, w_sem.at[0]),
        pltpu.make_async_copy(wd_ref, wd, w_sem.at[1]),
    ]
    for copy in copies:
        copy.start()
    g.greet(riders.replicas)
    gather = Gather(g, a2, rc, scratch[:4])
    scatter = Scatter(g, rc, scratch[4:])

    def send(j):
        at = span(j, rc)
        a = normed(h1_ref[at, :])[0] * gain_ref[layer, 1:2, :]
        a2[g.me, at, :] = a.astype(BF)
        gather.start(j)

    run(n, send)
    riders.start()
    for copy in copies:
        copy.wait()

    def work(j):
        at = span(j, rc)
        gather.relay(j)
        gather.ready(j)
        a = flat(a2[:, at, :])
        for f in range(hidden // fb):
            cols = slice(f * fb, (f + 1) * fb)
            u = dg(a, wu[:, cols], NN)
            half = 0.5 + 0.5 * lax.erf(u * (0.5**0.5))
            slope[:, at, cols] = (
                (half + u * jnp.exp(-0.5 * u * u) * ((2 * math.pi) ** -0.5))
                .astype(BF)
                .reshape(size, rc, fb)
            )
            hid[:, at, cols] = (u * half).astype(BF).reshape(size, rc, fb)
        held = flat(hid[:, at, :])
        for f in range(width // 256):
            cols = slice(f * 256, (f + 1) * 256)
            scatter.part[:, at, cols] = dg(held, wd[:, cols], NN).reshape(size, rc, 256)
        scatter.first(j)
        scatter.second(j)
        riders.step(j, n)

    run(n, work)
    outs = [
        pltpu.make_async_copy(a2, a2_out, out_sem.at[0]),
        pltpu.make_async_copy(hid, hid_out, out_sem.at[1]),
        pltpu.make_async_copy(slope, slope_out, out_sem.at[2]),
    ]
    for out in outs:
        out.start()

    def last(j):
        at = span(j, rc)
        y_ref[at, :] = (h1_ref[at, :] + scatter.third(j)).astype(BF)

    run(n, last)
    riders.finish()
    gather.drain(n)
    scatter.drain(n)
    for out in outs:
        out.wait()


def mlp_forward(size, replicas, layer, h1, gains, wu, wd, riders):
    rows, width = h1.shape
    hidden = wu.shape[1]
    n = chunks(rows)
    halves, columns, outs, sems = riding(riders, replicas)
    return pl.pallas_call(
        functools.partial(mlp_kernel, size, layer, columns),
        out_shape=[
            shape((rows, width), BF),
            shape((size, rows, width), BF),
            shape((size, rows, hidden), BF),
            shape((size, rows, hidden), BF),
        ]
        + outs,
        in_specs=[VM, VM, HB, HB] + [HB] * len(riders),
        out_specs=[VM, HB, HB, HB] + [HB] * len(outs),
        scratch_shapes=[
            pltpu.VMEM((size, rows, width), BF),
            pltpu.VMEM((size, rows, hidden), BF),
            pltpu.VMEM((size, rows, hidden), BF),
            pltpu.VMEM((width, hidden), BF),
            pltpu.VMEM((hidden, width), BF),
            DMA((2,)),
            DMA((3,)),
        ]
        + comm_sems(size, n)
        + scatter_scratch(size, rows, width, n)
        + sems,
        compiler_params=params(4 + layer),
        cost_estimate=cost(50e9, 30e6),
    )(h1, gains, wu, wd, *halves)


def mlp_back_kernel(size, layer, parts, *refs):
    g_ref, h1_ref, gain_ref, a2_ref, hid_ref, slope_ref, wu_ref, wd_ref = refs[:8]
    refs = refs[8:]
    extra, refs = refs[:2], refs[2:]
    mid_ref, gain_out, gup_ref, gdown_out, down_came, extra_out = refs[:6]
    gdown_ref, refs = refs[6], refs[7:]
    grad, a2, hid, dup, wu, wd, w_sem = refs[:7]
    scratch, refs = refs[7:20], refs[20:]
    down_sem, out_sem, refs = refs[0], refs[1], refs[2:]
    rows, width = h1_ref.shape
    hidden = wu_ref.shape[1]
    depth = width // parts
    fb = min(256, hidden)
    n = chunks(rows)
    rc = rows // n
    g = Group(size)
    copies = [
        pltpu.make_async_copy(wd_ref, wd, w_sem.at[0]),
        pltpu.make_async_copy(slope_ref, dup, w_sem.at[1]),
        pltpu.make_async_copy(wu_ref, wu, w_sem.at[2]),
    ]
    late = [
        pltpu.make_async_copy(hid_ref, hid, w_sem.at[3]),
        pltpu.make_async_copy(a2_ref, a2, w_sem.at[4]),
    ]
    for copy in copies + late:
        copy.start()
    g.greet(parts if layer == 0 else 0, side=True)
    down_swap = HalfSwap(gdown_ref, down_came, down_sem)
    section = lax.axis_index("section")
    if layer == 1:
        y_sem = refs[0]
        ys, y_out = extra, extra_out

        def y_copies(own, other, at):
            return (
                pltpu.make_async_copy(own, y_out.at[section], y_sem.at[0]),
                far_copy(
                    other, y_out.at[at], y_sem.at[1], y_sem.at[2], {"section": 1 - section}
                ),
            )

        for i in range(2):

            @pl.when(section == i)
            def _(i=i):
                for copy in y_copies(ys[i], ys[1 - i], section):
                    copy.start()

    else:
        above = HalfReduce(1, refs)
        loads = above.loads(*extra)
        for load in loads:
            load.start()

    gather = Gather(g, grad, rc, scratch[:4])
    scatter = Scatter(g, rc, scratch[4:])

    def send(j):
        at = span(j, rc)
        grad[g.me, at, :] = g_ref[at, :]
        gather.start(j)

    run(n, send)
    for copy in copies:
        copy.wait()
    if layer == 0:
        for load in loads:
            load.wait()
        above.middle()

    for copy in late:
        copy.wait()

    def down_grad(f):
        cols = pl.ds(pl.multiple_of(f * fb, fb), fb)
        r = dg(flat(hid[:, :, cols]), flat(grad[...]), TN).astype(BF)
        for z in range(parts):
            gdown_ref[z, cols, :] = r[:, z * depth : (z + 1) * depth]

    down_out = pltpu.make_async_copy(gdown_ref, gdown_out, out_sem.at[0])

    def work(j):
        at = span(j, rc)
        gather.relay(j)
        gather.ready(j)

        @pl.when(j == n - 1)
        def _():
            run(hidden // fb, down_grad)
            down_swap.copy().start()
            down_out.start()

        held = flat(grad[:, at, :])
        for f in range(hidden // fb):
            cols = slice(f * fb, (f + 1) * fb)
            d = dg(held, wd[cols, :], NT) * flat(dup[:, at, cols]).astype(F32)
            dup[:, at, cols] = d.astype(BF).reshape(size, rc, fb)
        held = flat(dup[:, at, :])
        for z in range(parts):
            cols = slice(z * depth, (z + 1) * depth)
            scatter.part[:, at, cols] = dg(held, wu[cols, :], NT).reshape(size, rc, depth)
        scatter.first(j)
        scatter.second(j)

    run(n, work)

    def up_grad(z):
        cols = pl.ds(pl.multiple_of(z * depth, depth), depth)
        gup_ref[z] = dg(flat(a2[:, :, cols]), flat(dup[...]), TN).astype(BF)

    run(parts, up_grad)
    if layer == 0:
        above.late()
    gain_out[...] = jnp.zeros_like(gain_out)

    def last(j):
        at = span(j, rc)
        dh, dgain = normed_back(h1_ref[at, :], gain_ref[layer, 1:2, :], scatter.third(j))
        mid_ref[at, :] = g_ref[at, :].astype(F32) + dh
        gain_out[...] += dgain

    run(n, last)
    if layer == 1:
        local, side = y_copies(ys[0], ys[1], 1 - section)
        local.wait()
        side.wait_recv()
        y_copies(ys[0], ys[1], section)[1].wait_send()
    else:
        above.finish(extra_out)
    down_swap.copy().wait_recv()
    down_swap.copy().wait_send()
    down_out.wait()
    gather.drain(n)
    scatter.drain(n)


def mlp_backward(size, replicas, layer, grad, h1, gains, a2, hid, slope, wu, wd, extra):
    rows, width = h1.shape
    hidden = wu.shape[1]
    parts, depth = replicas, width // replicas
    n = chunks(rows)
    return pl.pallas_call(
        functools.partial(mlp_back_kernel, size, layer, parts),
        out_shape=[
            shape((rows, width), F32),
            shape((1, width), F32),
            shape((parts, depth, hidden), BF),
            shape((parts, hidden, depth), BF),
            shape((parts, hidden // 2, depth), BF),
            (
                shape((2, rows, width), BF)
                if layer == 1
                else shape((extra[0].shape[1], extra[0].shape[2]), F32)
            ),
        ],
        in_specs=[VM, VM, VM] + [HB] * 7,
        out_specs=[VM, VM, VM, HB, HB, HB if layer == 1 else VM],
        scratch_shapes=[
            pltpu.VMEM((parts, hidden, depth), BF),
            pltpu.VMEM((size, rows, width), BF),
            pltpu.VMEM((size, rows, width), BF),
            pltpu.VMEM((size, rows, hidden), BF),
            pltpu.VMEM((size, rows, hidden), BF),
            pltpu.VMEM((width, hidden), BF),
            pltpu.VMEM((hidden, width), BF),
            DMA((5,)),
        ]
        + comm_sems(size, n)
        + scatter_scratch(size, rows, width, n)
        + [DMA((2,)), DMA((1,))]
        + ([DMA((3,))] if layer == 1 else half_scratch(parts, *extra[0].shape[1:])),
        compiler_params=params(6 + layer),
        cost_estimate=cost(60e9, 40e6),
    )(grad, h1, gains, a2, hid, slope, wu, wd, *extra)


def attend_back_kernel(size, layer, parts, *refs):
    mid_ref, qkv_ref, qm_ref, km_ref, ctx_ref, lse_ref, w_ref, gdown_ref, down_came, gup_ref = refs[:10]
    refs = refs[10:]
    if layer == 0:
        aboves, refs = refs[:2], refs[2:]
    else:
        aboves = (None, None)
    dqkv_ref, gout_ref, down_out, up_out = refs[:4]
    da, ka, va, kt, dk, dv, w, w_sem = refs[4:12]
    sems, refs = refs[12:16], refs[16:]
    reduce = Reduce(layer, refs[:9])
    down = HalfReduce(layer, refs[9 : 9 + HALF])
    up = HalfReduce(layer, refs[9 + HALF : 9 + 2 * HALF])
    up_swap = HalfSwap(gup_ref, up.other, refs[9 + 2 * HALF])
    _, rows, wide = qkv_ref.shape
    length = size * rows
    e = qm_ref.shape[2]
    heads = wide // (3 * e)
    scale = e**-0.5
    c = scale * math.log2(math.e)
    depth = w_ref.shape[1] // parts
    n = chunks(rows)
    rc = rows // n
    bq = size * rc
    kc = bq
    g = Group(size)
    copies = [pltpu.make_async_copy(w_ref, w, w_sem.at[0])]
    for copy in copies:
        copy.start()
    g.greet(parts)
    gather = Gather(g, da, rc, sems)
    up_swap.copy().start()
    loads = down.loads(gdown_ref, down_came) + up.loads(gup_ref, None)
    for load in loads:
        load.start()

    def send(j):
        at = span(j, rc)
        da[g.me, at, :] = mid_ref[at, :].astype(BF)
        gather.start(j)

    run(n, send)
    lane = lax.broadcasted_iota(jnp.int32, (length, e), 1)
    whole = flat(qkv_ref[...])
    for h in range(heads):
        o = 3 * e * h
        ka[h, :, :e] = whole[:, o + e : o + 2 * e]
        ka[h, :, e:] = flat(km_ref[...])
        va[h, :, :e] = whole[:, o + 2 * e : o + 3 * e]
        va[h, :, e:] = jnp.where(lane < 3, 1.0, 0.0).astype(BF)
        kt[h] = whole[:, o + e : o + 2 * e].T
    dk[...] = jnp.zeros_like(dk)
    dv[...] = jnp.zeros_like(dv)
    ql = lax.broadcasted_iota(jnp.int32, (bq, e), 1)
    for copy in copies + loads:
        copy.wait()
    down.middle()

    def out_grad(z):
        cols = pl.ds(pl.multiple_of(z * depth, depth), depth)
        return dg(flat(ctx_ref[...]), flat(da[:, :, cols]), TN)

    def work(j):
        at = span(j, rc)

        @pl.when(j == 0)
        def _():
            gather.relay(0)
            gather.ready(0)

        @pl.when(j == min(1, n - 1))
        def _():
            for i in range(1, n):
                gather.relay(i)
            for i in range(1, n):
                gather.ready(i)
            reduce.send(out_grad)

        qm = flat(qm_ref[:, at, :])
        dctx = dg(flat(da[:, at, :]), w[...], NT).astype(BF)
        ctx = flat(ctx_ref[:, at, :])
        held_qkv = flat(qkv_ref[:, at, :])
        for h in range(heads):
            o = 3 * e * h
            qq = held_qkv[:, o : o + e]
            q = jnp.concatenate([qq, qm], axis=1)
            dc = dctx[:, h * e : (h + 1) * e]
            prod = dc.astype(F32) * ctx[:, h * e : (h + 1) * e].astype(F32)
            d = -jnp.sum(prod, axis=1, keepdims=True)
            d1 = d.astype(BF).astype(F32)
            d2 = (d - d1).astype(BF).astype(F32)
            d3 = d - d1 - d2
            ds_col = jnp.where(ql == 0, d1, jnp.where(ql == 1, d2, jnp.where(ql == 2, d3, 0.0)))
            dca = jnp.concatenate([dc, ds_col.astype(BF)], axis=1)
            lse = lse_ref[j, h : h + 1, :]
            dqt = None
            for k in range(length // kc):
                ks = slice(k * kc, (k + 1) * kc)
                s = dg(ka[h, ks, :], q, NT)
                p = jnp.exp2(s * c - lse)
                ds = (p * dg(va[h, ks, :], dca, NT)).astype(BF)
                dv[h, ks, :] += dg(p.astype(BF), dc, NN)
                dk[h, ks, :] += dg(ds, qq, NN)
                a = dg(kt[h, :, ks], ds, NN)
                dqt = a if dqt is None else dqt + a
            if h == heads // 2:

                @pl.when(j == min(1, n - 1))
                def _():
                    up_swap.copy().wait_recv()
                    up.middle()

            if h == heads - 1:

                @pl.when(j == n // 2)
                def _():
                    down.late()

            dqkv_ref[:, at, o : o + e] = (dqt * scale).T.astype(BF).reshape(size, rc, e)

    run(n, work)
    reduce.collect()
    up.late()
    for h in range(heads):
        o = 3 * e * h
        dqkv_ref[:, :, o + e : o + 2 * e] = (dk[h] * scale).astype(BF).reshape(size, rows, e)
        dqkv_ref[:, :, o + 2 * e : o + 3 * e] = dv[h].astype(BF).reshape(size, rows, e)

    down.finish(down_out, aboves[0])
    reduce.finish(gout_ref)
    up.finish(up_out, aboves[1])
    up_swap.copy().wait_send()
    gather.drain(n)


def attend_backward(size, replicas, layer, mid, qkv, qm, km, ctx, lse, w, grads, aboves):
    _, rows, wide = qkv.shape
    e = qm.shape[2]
    heads = wide // (3 * e)
    width = mid.shape[1]
    parts, depth = replicas, width // replicas
    length = size * rows
    n = chunks(rows)
    return pl.pallas_call(
        functools.partial(attend_back_kernel, size, layer, parts),
        out_shape=(
            shape(qkv.shape, BF),
            shape((heads * e, depth), F32),
            shape(grads[0].shape[1:], F32),
            shape(grads[2].shape[1:], F32),
        ),
        in_specs=[VM] * 6 + [HB] * (4 + len(aboves)),
        out_specs=(VM, VM, VM, VM),
        scratch_shapes=[
            pltpu.VMEM((size, rows, width), BF),
            pltpu.VMEM((heads, length, 2 * e), BF),
            pltpu.VMEM((heads, length, 2 * e), BF),
            pltpu.VMEM((heads, e, length), BF),
            pltpu.VMEM((heads, length, e), F32),
            pltpu.VMEM((heads, length, e), F32),
            pltpu.VMEM((heads * e, width), BF),
            DMA((1,)),
        ]
        + comm_sems(size, n)
        + reduce_scratch(parts, heads * e, depth)
        + half_scratch(parts, *grads[0].shape[1:])
        + half_scratch(parts, *grads[2].shape[1:])
        + [DMA((2,))],
        compiler_params=params(8 + layer),
        cost_estimate=cost(90e9, 40e6),
    )(mid, qkv, qm, km, ctx, lse, w, *grads, *aboves)


def qkv_back_kernel(
    size, layer, parts, dqkv_ref, a1_ref, x_ref, mid_ref, gain_ref, w_ref,
    dx_ref, gain_out, gqkv_out, came, gqkv_ref, w, w_sem, swap_sem, *scratch
):
    rows, width = x_ref.shape
    depth = width // parts
    n = chunks(rows)
    rc = rows // n
    g = Group(size)
    copies = [pltpu.make_async_copy(w_ref, w, w_sem.at[0])]
    for copy in copies:
        copy.start()
    g.greet(side=True)
    swap = HalfSwap(gqkv_ref, came, swap_sem)
    scatter = Scatter(g, rc, scratch)
    def qkv_grad(z):
        cols = pl.ds(pl.multiple_of(z * depth, depth), depth)
        gqkv_ref[z] = dg(flat(a1_ref[:, :, cols]), flat(dqkv_ref[...]), TN).astype(BF)

    for copy in copies:
        copy.wait()

    def work(j):
        at = span(j, rc)
        held = flat(dqkv_ref[:, at, :])
        for z in range(parts):
            cols = slice(z * depth, (z + 1) * depth)
            scatter.part[:, at, cols] = dg(held, w[cols, :], NT).reshape(size, rc, depth)
        scatter.first(j)
        scatter.second(j)

    run(n, work)
    run(parts, qkv_grad)
    swap.copy().start()
    out = pltpu.make_async_copy(gqkv_ref, gqkv_out, w_sem.at[1])
    out.start()
    gain_out[...] = jnp.zeros_like(gain_out)

    def last(j):
        at = span(j, rc)
        dh, dgain = normed_back(
            x_ref[at, :].astype(F32), gain_ref[layer, 0:1, :], scatter.third(j)
        )
        dx_ref[at, :] = (mid_ref[at, :] + dh).astype(BF)
        gain_out[...] += dgain

    run(n, last)
    swap.copy().wait_recv()
    swap.copy().wait_send()
    out.wait()
    scatter.drain(n)


def qkv_backward(size, replicas, layer, dqkv, a1, x, mid, gains, w):
    rows, width = x.shape
    wide = w.shape[1]
    parts, depth = replicas, width // replicas
    n = chunks(rows)
    return pl.pallas_call(
        functools.partial(qkv_back_kernel, size, layer, parts),
        out_shape=(
            shape((rows, width), BF),
            shape((1, width), F32),
            shape((parts, depth, wide), BF),
            shape((parts, depth // 2, wide), BF),
        ),
        in_specs=[VM] * 5 + [HB],
        out_specs=(VM, VM, HB, HB),
        scratch_shapes=[
            pltpu.VMEM((parts, depth, wide), BF),
            pltpu.VMEM((width, wide), BF),
            DMA((2,)),
            DMA((2,)),
        ]
        + scatter_scratch(size, rows, width, n),
        compiler_params=params(11),
        cost_estimate=cost(30e9, 30e6),
    )(dqkv, a1, x, mid, gains, w)


def last_kernel(
    size, parts, dqkv_ref, a1_ref, x_ref, mid_ref, gain_ref, w_ref, two_ref, above_ref, dx1_ref,
    qkv_above, gain_out, gqkv_out, dx_out,
    gqkv, swap_sem, w, dx, gsum, gcame, w_sem, x_sem, x_send, x_recv, g_send, g_recv, *scratch
):
    rows, width = x_ref.shape
    depth = width // parts
    n = chunks(rows)
    rc = rows // n
    g = Group(size)
    section = lax.axis_index("section")
    d = lax.axis_index("dp")
    copy = pltpu.make_async_copy(w_ref, w, w_sem.at[0])
    copy.start()
    reduce = HalfReduce(0, scratch[:HALF])
    swap = HalfSwap(gqkv, reduce.other, swap_sem)
    scatter = Scatter(g, rc, scratch[HALF:])
    g.greet(parts)

    def upper():
        return far_copy(
            dx1_ref, dx_out.at[0], x_send.at[n], x_recv.at[n], {"section": 1 - section}
        )

    def keep_upper():
        return pltpu.make_async_copy(dx1_ref, dx_out.at[1], x_sem.at[0])

    def lower(j):
        at = span(j, rc)
        return far_copy(
            dx.at[at], dx_out.at[1, at], x_send.at[j], x_recv.at[j], {"section": 1 - section}
        )

    def keep_lower(j):
        at = span(j, rc)
        return pltpu.make_async_copy(dx.at[at], dx_out.at[0, at], x_sem.at[j])

    def qkv_grad(z):
        cols = pl.ds(pl.multiple_of(z * depth, depth), depth)
        gqkv[z] = dg(flat(a1_ref[:, :, cols]), flat(dqkv_ref[...]), TN).astype(BF)

    run(parts, qkv_grad)
    swap.copy().start()
    load = reduce.loads(gqkv, None)[0]
    load.start()

    @pl.when(section == 1)
    def _():
        keep_upper().start()

    copy.wait()

    def work(j):
        at = span(j, rc)
        held = flat(dqkv_ref[:, at, :])
        for z in range(parts):
            cols = slice(z * depth, (z + 1) * depth)
            scatter.part[:, at, cols] = dg(held, w[cols, :], NT).reshape(size, rc, depth)
        scatter.first(j)
        scatter.second(j)

    run(n, work)
    gsum[0] = jnp.zeros_like(gsum[0])

    def last(j):
        at = span(j, rc)
        dh, dgain = normed_back(x_ref[at, :].astype(F32), gain_ref[0, 0:1, :], scatter.third(j))
        dx[at, :] = (mid_ref[at, :] + dh).astype(BF)

        @pl.when(section == 0)
        def _():
            keep_lower(j).start()

        @pl.when(section == 1)
        def _():
            lower(j).start()

        gsum[0, 0:1, :] += dgain

    def rest(j):
        @pl.when(j == n // 2)
        def _():
            load.wait()
            swap.copy().wait_recv()
            reduce.middle()

            @pl.when(section == 0)
            def _():
                upper().start()

        last(j)

    run(n, rest)
    gsum[0, 1:2, :] = two_ref[...]
    gsum[0, 2:4, :] = above_ref[...]

    targets = [
        [{"tensor": g.sibling}],
        [{"tensor": g.ahead(k) * 2 + g.core} for k in range(1, g.chips)],
        [{"dp": lax.rem(d + k, parts)} for k in range(1, parts)],
        [{"section": 1 - section}],
    ]
    slot = 0
    sent = []

    def exchange(stage):
        nonlocal slot
        copies = []
        for target in targets[stage]:
            copies.append(
                far_copy(gsum.at[stage], gcame.at[slot], g_send.at[slot], g_recv.at[slot], target)
            )
            copies[-1].start()
            slot += 1
        total = gsum[stage]
        for i, copy in enumerate(copies):
            copy.wait_recv()
            total = total + gcame[slot - len(copies) + i]
        gsum[stage + 1] = total
        sent.extend(copies)

    for stage in range(4):
        exchange(stage)
    gain_out[...] = gsum[4]
    reduce.late()

    @pl.when(section == 0)
    def _():
        for j in range(n):
            lower(j).wait_recv()
            keep_lower(j).wait()
        upper().wait_send()

    @pl.when(section == 1)
    def _():
        keep_upper().wait()
        upper().wait_recv()
        for j in range(n):
            lower(j).wait_send()

    reduce.finish(gqkv_out, qkv_above)
    swap.copy().wait_send()
    for copy in sent:
        copy.wait_send()
    scatter.drain(n)


def last_backward(size, replicas, dqkv, a1, x, mid, gains, w, two, above, dx1, qkv_above):
    rows, width = x.shape
    wide = w.shape[1]
    depth = width // replicas
    n = chunks(rows)
    slots = 1 + (size // 2 - 1) + (replicas - 1) + 1
    return pl.pallas_call(
        functools.partial(last_kernel, size, replicas),
        out_shape=(
            shape((8, width), F32),
            shape((depth, wide), F32),
            shape((2, rows, width), BF),
        ),
        in_specs=[VM] * 5 + [HB, VM, VM, HB, HB],
        out_specs=(VM, VM, HB),
        scratch_shapes=[
            pltpu.VMEM((replicas, depth, wide), BF),
            DMA((2,)),
            pltpu.VMEM((width, wide), BF),
            pltpu.VMEM((rows, width), BF),
            pltpu.VMEM((5, 8, width), F32),
            pltpu.VMEM((slots, 8, width), F32),
            DMA((1,)),
            DMA((n,)),
            DMA((n + 1,)),
            DMA((n + 1,)),
            DMA((slots,)),
            DMA((slots,)),
        ]
        + half_scratch(replicas, depth, wide)
        + scatter_scratch(size, rows, width, n),
        compiler_params=params(10),
        cost_estimate=cost(40e9, 30e6),
    )(dqkv, a1, x, mid, gains, w, two, above, dx1, qkv_above)


def scene_masks(segments, e):
    same = (segments[..., None] == jnp.arange(e, dtype=jnp.int32)).astype(F32)
    used = jnp.arange(e) < SCENES
    return (
        jnp.where(used, same * MASKED, 0.0).astype(BF),
        jnp.where(used, 1.0 - same, 0.0).astype(BF),
    )


def shards(
    block_input,
    segment_ids,
    cotangent,
    norm_one_gain,
    qkv_weight,
    out_weight,
    norm_two_gain,
    up_weight,
    down_weight,
):
    section = lax.axis_index("section")
    size = lax.axis_size("tensor")
    replicas = lax.axis_size("dp")

    mine = [
        qkv_weight[0].reshape((qkv_weight.shape[1], -1)),
        out_weight[0].reshape((-1, out_weight.shape[3])),
        up_weight[0],
        down_weight[0],
    ]
    mine = [w.astype(BF).reshape((2, -1, w.shape[1])) for w in mine]
    gains = jnp.concatenate(
        [norm_one_gain, norm_two_gain, jnp.zeros((6, norm_one_gain.shape[1]), F32)], axis=0
    )
    segments = lax.dynamic_index_in_dim(segment_ids, section, 0, keepdims=False)
    x = lax.dynamic_index_in_dim(block_input, section, 0, keepdims=False)
    head_dim = qkv_weight.shape[3] // 3
    qm, km = scene_masks(segments.reshape((size, -1)), head_dim)
    qkv, gains, a1, w_qkv_0, w_out_0, h_qkv, h_out, h_up, h_down, got_up = first_forward(
        size, replicas, x, gains, mine
    )
    h1, ctx, lse, w_up_0, w_down_0, got_qkv, got_out = attend(
        size, replicas, 0, qkv, qm, km, x, w_out_0,
        [
            (got_up, "y", 0, False),
            (h_down, "spread", 0, True),
            (h_qkv, "z", 1, False),
            (h_out, "z", 1, True),
        ],
    )
    y0, a2, hid, slope, w_qkv_1, w_out_1, got_up, got_down = mlp_forward(
        size, replicas, 0, h1, gains, w_up_0, w_down_0,
        [
            (got_qkv, "y", 1, False),
            (got_out, "y", 1, True),
            (h_up, "z", 1, False),
            (h_down, "z", 1, True),
        ],
    )
    kept = [(x, a1, qkv, ctx, lse, h1, a2, hid, slope)]
    qkv, a1, w_up_1 = qkv_forward(
        size, replicas, 1, y0, gains, w_qkv_1, [(got_up, "y", 1, False)]
    )
    h1, ctx, lse, w_down_1 = attend(
        size, replicas, 1, qkv, qm, km, y0, w_out_1, [(got_down, "y", 1, True)]
    )
    y1, a2, hid, slope = mlp_forward(size, replicas, 1, h1, gains, w_up_1, w_down_1, [])
    kept.append((y0, a1, qkv, ctx, lse, h1, a2, hid, slope))
    weights = [
        (w_qkv_0, w_out_0, w_up_0, w_down_0),
        (w_qkv_1, w_out_1, w_up_1, w_down_1),
    ]
    grad = lax.dynamic_index_in_dim(cotangent, section, 0, keepdims=False)

    x, a1, qkv, ctx, lse, h1, a2, hid, slope = kept[1]
    w_qkv, w_out, w_up, w_down = weights[1]
    mid, gain_two, g_up, g_down, came, layer_out = mlp_backward(
        size, replicas, 1, grad, h1, gains, a2, hid, slope, w_up, w_down, [y0, y1]
    )
    d_qkv, out_1, down_1, up_1 = attend_backward(
        size, replicas, 1, mid, qkv, qm, km, ctx, lse, w_out, [g_down, came, g_up], []
    )
    dx1, gain_one, g_qkv, came = qkv_backward(
        size, replicas, 1, d_qkv, a1, x, mid, gains, w_qkv
    )
    gains_above = jnp.concatenate([gain_one, gain_two], axis=0)

    x, a1, qkv, ctx, lse, h1, a2, hid, slope = kept[0]
    w_qkv, w_out, w_up, w_down = weights[0]
    mid, gain_two, g_up, g_down, came, qkv_1 = mlp_backward(
        size, replicas, 0, dx1, h1, gains, a2, hid, slope, w_up, w_down, [g_qkv, came]
    )
    d_qkv, out_0, down_grad, up_grad = attend_backward(
        size, replicas, 0, mid, qkv, qm, km, ctx, lse, w_out,
        [g_down, came, g_up], [down_1, up_1],
    )
    gains, qkv_grad, input_out = last_backward(
        size, replicas, d_qkv, a1, x, mid, gains, w_qkv, gain_two, gains_above, dx1, qkv_1
    )
    out_grad = jnp.where(section == 0, out_0, out_1)
    gains = lax.dynamic_slice_in_dim(gains, 2 * section, 2, 0)
    return (
        layer_out[None],
        input_out[None],
        gains[0:1],
        qkv_grad.reshape(qkv_weight.shape),
        out_grad.reshape(out_weight.shape),
        gains[1:2],
        up_grad[None],
        down_grad[None],
    )


def solution(mesh):
    return jax.shard_map(
        shards,
        mesh=mesh,
        in_specs=(
            P(None, ("dp", "tensor"), None),
            P(None, "dp"),
            P(None, ("dp", "tensor"), None),
            P("section", None),
            P("section", "dp", "tensor", None),
            P("section", "tensor", None, "dp"),
            P("section", None),
            P("section", "dp", "tensor"),
            P("section", "tensor", "dp"),
        ),
        out_specs=(
            P("section", None, ("dp", "tensor"), None),
            P("section", None, ("dp", "tensor"), None),
            P("section", None),
            P("section", "dp", "tensor", None),
            P("section", "tensor", None, "dp"),
            P("section", None),
            P("section", "dp", "tensor"),
            P("section", "tensor", "dp"),
        ),
        check_vma=False,
    )
```

```python
import functools
import math

import jax
import jax.numpy as jnp
from jax import lax
from jax.experimental import pallas as pl
from jax.experimental.pallas import tpu as pltpu
from jax.sharding import PartitionSpec as P

F32 = jnp.float32
BF = jnp.bfloat16
NT = (((1,), (1,)), ((), ()))
NN = (((1,), (0,)), ((), ()))
TN = (((0,), (0,)), ((), ()))
MASKED = -1e30
SCENES = 3
MESH = pl.DeviceIdType.MESH
VM = pl.BlockSpec(memory_space=pltpu.VMEM)
HB = pl.BlockSpec(memory_space=pl.ANY)
DMA = pltpu.SemaphoreType.DMA
LIMIT = 58 << 20


def dg(a, b, dims):
    return lax.dot_general(a, b, dims, preferred_element_type=F32)


def chunks(rows):
    return 4 if rows % 64 == 0 else 1


def shape(dims, dtype):
    return jax.ShapeDtypeStruct(dims, dtype)


class Group:
    def __init__(self, size):
        self.size = size
        self.chips = size // 2
        self.me = lax.axis_index("tensor")
        self.chip = lax.div(self.me, 2)
        self.core = lax.rem(self.me, 2)
        self.sibling = self.chip * 2 + 1 - self.core

    def ahead(self, k):
        return lax.rem(self.chip + k, self.chips)

    def behind(self, k):
        return lax.rem(self.chip + self.chips - k, self.chips)

    def greet(self, replicas=0, side=False):
        barrier = pltpu.get_barrier_semaphore()
        targets = [self.sibling] + [self.ahead(k) * 2 + self.core for k in range(1, self.chips)]
        targets = [{"tensor": target} for target in targets]
        if replicas:
            d = lax.axis_index("dp")
            targets += [{"dp": lax.rem(d + k, replicas)} for k in range(1, replicas)]
        if replicas or side:
            targets += [{"section": 1 - lax.axis_index("section")}]
        for target in targets:
            pl.semaphore_signal(barrier, inc=1, device_id=target, device_id_type=MESH)
        pl.semaphore_wait(barrier, len(targets))


def remote(src, dst, send, recv, target):
    return pltpu.make_async_remote_copy(
        src_ref=src,
        dst_ref=dst,
        send_sem=send,
        recv_sem=recv,
        device_id={"tensor": target},
        device_id_type=MESH,
    )


def span(j, rc):
    return pl.ds(pl.multiple_of(j * rc, rc), rc)


def comm_sems(group_size, n):
    c = group_size // 2
    far, near = DMA((max(c - 1, 1), n)), DMA((c, n))
    return [far, far, near, near]


class Gather:
    def __init__(self, g, buf, rc, sems):
        self.g, self.buf, self.rc = g, buf, rc
        self.far_send, self.far_recv, self.near_send, self.near_recv = sems

    def far(self, k, j, origin, target):
        ref = self.buf.at[origin, span(j, self.rc)]
        return remote(ref, ref, self.far_send.at[k - 1, j], self.far_recv.at[k - 1, j], target)

    def near(self, k, j, origin):
        ref = self.buf.at[origin, span(j, self.rc)]
        return remote(
            ref, ref, self.near_send.at[k, j], self.near_recv.at[k, j], self.g.sibling
        )

    def start(self, j):
        g = self.g
        for k in range(1, g.chips):
            self.far(k, j, g.me, g.ahead(k) * 2 + g.core).start()
        self.near(0, j, g.me).start()

    def relay(self, j):
        g = self.g
        for k in range(1, g.chips):
            origin = g.behind(k) * 2 + g.core
            self.far(k, j, origin, g.me).wait_recv()
            self.near(k, j, origin).start()

    def ready(self, j):
        g = self.g
        self.near(0, j, g.sibling).wait_recv()
        for k in range(1, g.chips):
            self.near(k, j, g.behind(k) * 2 + 1 - g.core).wait_recv()

    def drain(self, n):
        g = self.g

        def one(j, _):
            for k in range(1, g.chips):
                self.far(k, j, g.me, g.sibling).wait_send()
            for k in range(g.chips):
                self.near(k, j, g.me).wait_send()
            return 0

        lax.fori_loop(0, n, one, 0)


def scatter_scratch(group_size, rows, width, n):
    c = group_size // 2
    far = pltpu.VMEM((max(c - 1, 1), rows, width), BF)
    near = pltpu.VMEM((c, rows, width), BF)
    return [pltpu.VMEM((group_size, rows, width), F32), near, near, far, far] + comm_sems(
        group_size, n
    )


class Scatter:
    def __init__(self, g, rc, scratch):
        self.g, self.rc = g, rc
        self.part, self.near_out, self.near_in, self.far_out, self.far_in = scratch[:5]
        self.far_send, self.far_recv, self.near_send, self.near_recv = scratch[5:]

    def near(self, k, j):
        rows = span(j, self.rc)
        return remote(
            self.near_out.at[k, rows],
            self.near_in.at[k, rows],
            self.near_send.at[k, j],
            self.near_recv.at[k, j],
            self.g.sibling,
        )

    def far(self, k, j):
        rows = span(j, self.rc)
        return remote(
            self.far_out.at[k - 1, rows],
            self.far_in.at[k - 1, rows],
            self.far_send.at[k - 1, j],
            self.far_recv.at[k - 1, j],
            self.g.ahead(k) * 2 + self.g.core,
        )

    def first(self, j):
        g, rows = self.g, span(j, self.rc)
        for k in list(range(1, g.chips)) + [0]:
            owner = g.ahead(k) * 2 + 1 - g.core
            self.near_out[k, rows, :] = self.part[owner, rows, :].astype(BF)
            self.near(k, j).start()

    def second(self, j):
        g, rows = self.g, span(j, self.rc)
        for k in range(1, g.chips):
            owner = g.ahead(k) * 2 + g.core
            self.near(k, j).wait_recv()
            both = self.part[owner, rows, :] + self.near_in[k, rows, :].astype(F32)
            self.far_out[k - 1, rows, :] = both.astype(BF)
            self.far(k, j).start()

    def third(self, j):
        g, rows = self.g, span(j, self.rc)
        self.near(0, j).wait_recv()
        total = self.part[g.me, rows, :] + self.near_in[0, rows, :].astype(F32)
        for k in range(1, g.chips):
            self.far(k, j).wait_recv()
            total = total + self.far_in[k - 1, rows, :].astype(F32)
        return total

    def drain(self, n):
        g = self.g

        def one(j, _):
            for k in range(1, g.chips):
                self.far(k, j).wait_send()
            for k in range(g.chips):
                self.near(k, j).wait_send()
            return 0

        lax.fori_loop(0, n, one, 0)


def far_copy(src, dst, send, recv, target):
    return pltpu.make_async_remote_copy(
        src_ref=src,
        dst_ref=dst,
        send_sem=send,
        recv_sem=recv,
        device_id=target,
        device_id_type=MESH,
    )


class Swap:
    def __init__(self, src, stage, sems):
        self.src, self.stage, self.sems = src, stage, sems
        self.s = lax.axis_index("section")

    def copies(self, layer):
        local = pltpu.make_async_copy(self.src.at[self.s], self.stage.at[self.s], self.sems.at[0])
        side = far_copy(
            self.src.at[1 - self.s],
            self.stage.at[layer],
            self.sems.at[1],
            self.sems.at[2],
            {"section": 1 - self.s},
        )
        return local, side

    def start(self):
        for copy in self.copies(self.s):
            copy.start()

    def arrive(self):
        local, side = self.copies(1 - self.s)
        local.wait()
        side.wait_recv()

    def finish(self):
        self.copies(self.s)[1].wait_send()


def reduce_scratch(replicas, rows, cols):
    many = pltpu.VMEM((replicas - 1, rows, cols), BF)
    one = pltpu.VMEM((rows, cols), BF)
    far, side = DMA((replicas - 1, 2)), DMA((2,))
    return [pltpu.VMEM((rows, cols), F32), many, many, one, one, far, far, side, side]


class Reduce:
    def __init__(self, layer, scratch):
        self.layer = layer
        self.own, self.away, self.came, self.over, self.back = scratch[:5]
        self.z_send, self.z_recv, self.y_send, self.y_recv = scratch[5:]
        self.replicas = self.away.shape[0] + 1
        self.half = self.own.shape[0] // 2
        self.d = lax.axis_index("dp")
        self.s = lax.axis_index("section")

    def target(self, k):
        return lax.rem(self.d + k, self.replicas)

    def part(self, i):
        return pl.ds(pl.multiple_of(i * self.half, self.half), self.half)

    def z_copy(self, k, i):
        part = self.part(i)
        return far_copy(
            self.away.at[k - 1, part],
            self.came.at[k - 1, part],
            self.z_send.at[k - 1, i],
            self.z_recv.at[k - 1, i],
            {"dp": self.target(k)},
        )

    def y_copy(self, i):
        part = self.part(i)
        return far_copy(
            self.over.at[part],
            self.back.at[part],
            self.y_send.at[i],
            self.y_recv.at[i],
            {"section": 1 - self.s},
        )

    def send(self, block):
        def one(i):
            k = i + 1
            self.away[i] = block(self.target(k)).astype(BF)
            self.z_copy(k, 0).start()
            self.z_copy(k, 1).start()

        run(self.replicas - 1, one)
        self.own[...] = block(self.d)

    def collect(self):
        def one(i):
            part = self.part(i)
            total = self.own[part, :]
            for k in range(1, self.replicas):
                self.z_copy(k, i).wait_recv()
                total = total + self.came[k - 1, part, :].astype(F32)
            self.own[part, :] = total
            self.over[part, :] = total.astype(BF)

            @pl.when(self.s != self.layer)
            def _():
                self.y_copy(i).start()

        run(2, one)

    def finish(self, out):
        @pl.when(self.s == self.layer)
        def _():
            self.y_copy(0).wait_recv()
            self.y_copy(1).wait_recv()
            out[...] = self.own[...] + self.back[...].astype(F32)

        @pl.when(self.s != self.layer)
        def _():
            self.y_copy(0).wait_send()
            self.y_copy(1).wait_send()
            out[...] = self.own[...]

        for k in range(1, self.replicas):
            self.z_copy(k, 0).wait_send()
            self.z_copy(k, 1).wait_send()


class HalfSwap:
    def __init__(self, src, came, sems):
        self.src, self.came, self.sems = src, came, sems
        self.s = lax.axis_index("section")
        self.rows = came.shape[1]

    def copy(self):
        at = pl.ds(pl.multiple_of((1 - self.s) * self.rows, self.rows), self.rows)
        return far_copy(
            self.src.at[:, at],
            self.came,
            self.sems.at[0],
            self.sems.at[1],
            {"section": 1 - self.s},
        )


def half_scratch(replicas, rows, cols):
    rows = rows // 2
    all_, far = pltpu.VMEM((replicas, rows, cols), BF), pltpu.VMEM((replicas - 1, rows, cols), BF)
    one = pltpu.VMEM((rows, cols), BF)
    z = DMA((replicas - 1,))
    return [all_, all_, far, far, pltpu.VMEM((rows, cols), F32), one, one, DMA((3,)), z, z, DMA((2,))]


HALF = 11


class HalfReduce:
    def __init__(self, layer, scratch):
        self.layer = layer
        self.mine, self.other, self.away, self.came, self.own, self.over, self.back = scratch[:7]
        self.in_sem, self.z_send, self.z_recv, self.y_sem = scratch[7:]
        self.replicas, self.rows = self.mine.shape[:2]
        self.s = lax.axis_index("section")
        self.d = lax.axis_index("dp")

    def half(self, s):
        return pl.ds(pl.multiple_of(s * self.rows, self.rows), self.rows)

    def loads(self, src, other):
        loads = [pltpu.make_async_copy(src.at[:, self.half(self.s)], self.mine, self.in_sem.at[0])]
        if other is not None:
            loads.append(pltpu.make_async_copy(other, self.other, self.in_sem.at[1]))
        return loads

    def z_copy(self, k):
        return far_copy(
            self.away.at[k - 1],
            self.came.at[k - 1],
            self.z_send.at[k - 1],
            self.z_recv.at[k - 1],
            {"dp": lax.rem(self.d + k, self.replicas)},
        )

    def y_copy(self):
        return far_copy(
            self.over, self.back, self.y_sem.at[0], self.y_sem.at[1], {"section": 1 - self.s}
        )

    def middle(self):
        def both(z):
            return self.mine[z].astype(F32) + self.other[z].astype(F32)

        for k in range(1, self.replicas):
            self.away[k - 1] = both(lax.rem(self.d + k, self.replicas)).astype(BF)
            self.z_copy(k).start()
        self.own[...] = both(self.d)

    def late(self):
        total = self.own[...]
        for k in range(1, self.replicas):
            self.z_copy(k).wait_recv()
            total = total + self.came[k - 1].astype(F32)
        self.own[...] = total
        self.over[...] = total.astype(BF)

        @pl.when(self.s != self.layer)
        def _():
            self.y_copy().start()

    def finish(self, out, above=None):
        @pl.when(self.s == self.layer)
        def _():
            self.y_copy().wait_recv()
            out[self.half(self.s), :] = self.own[...]
            out[self.half(1 - self.s), :] = self.back[...].astype(F32)

        @pl.when(self.s != self.layer)
        def _():
            if above is None:
                out[...] = jnp.zeros_like(out)
            else:
                copy = pltpu.make_async_copy(above, out, self.in_sem.at[2])
                copy.start()
                copy.wait()
            self.y_copy().wait_send()

        for k in range(1, self.replicas):
            self.z_copy(k).wait_send()


class Spread:
    def __init__(self, src, dst, by_columns, sems):
        self.src, self.dst, self.by_columns = src, dst, by_columns
        self.own_sem, self.far_send, self.far_recv, self.side_send, self.side_recv = sems
        self.replicas = far = self.side_send.shape[0]
        self.s = lax.axis_index("section")
        self.d = lax.axis_index("dp")
        self.stages = [
            sorted({k, far - k}) for k in range(1, far // 2 + 1)
        ]

    def place(self, half, z):
        rows, cols = self.src.shape
        if self.by_columns:
            return self.dst.at[
                pl.ds(pl.multiple_of(half * rows, rows), rows),
                pl.ds(pl.multiple_of(z * cols, cols), cols),
            ]
        return self.dst.at[pl.ds(pl.multiple_of((2 * z + half) * rows, rows), rows)]

    def origin(self, k):
        return lax.rem(self.d + self.replicas - k, self.replicas)

    def own(self):
        return pltpu.make_async_copy(self.src, self.place(self.s, self.d), self.own_sem.at[0])

    def far(self, k, origin):
        return pltpu.make_async_remote_copy(
            src_ref=self.src,
            dst_ref=self.place(self.s, origin),
            send_sem=self.far_send.at[k - 1],
            recv_sem=self.far_recv.at[k - 1],
            device_id={"dp": lax.rem(self.d + k, self.replicas)},
            device_id_type=MESH,
        )

    def side(self, k, half):
        place = self.place(half, self.origin(k))
        return pltpu.make_async_remote_copy(
            src_ref=self.src if k == 0 else place,
            dst_ref=place,
            send_sem=self.side_send.at[k],
            recv_sem=self.side_recv.at[k],
            device_id={"section": 1 - self.s},
            device_id_type=MESH,
        )

    def start(self):
        for k in self.stages[0]:
            self.far(k, self.d).start()
        self.side(0, self.s).start()
        self.own().start()

    def step(self, i):
        for k in self.stages[i]:
            self.far(k, self.origin(k)).wait_recv()
            self.side(k, self.s).start()
        if i + 1 < len(self.stages):
            for k in self.stages[i + 1]:
                self.far(k, self.d).start()

    def finish(self):
        self.own().wait()
        for k in range(self.replicas):
            self.side(k, 1 - self.s).wait_recv()
        for k in range(1, self.replicas):
            self.far(k, self.d).wait_send()
        for k in range(self.replicas):
            self.side(k, self.s).wait_send()


class ZGather:
    def __init__(self, src, got, sems):
        self.src, self.got = src, got
        self.own_sem, self.send, self.recv = sems
        self.replicas = got.shape[0]
        self.d = lax.axis_index("dp")

    def own(self):
        return pltpu.make_async_copy(self.src, self.got.at[self.d], self.own_sem.at[0])

    def far(self, k, origin):
        return far_copy(
            self.src,
            self.got.at[origin],
            self.send.at[k - 1],
            self.recv.at[k - 1],
            {"dp": lax.rem(self.d + k, self.replicas)},
        )

    def start(self):
        for k in range(1, self.replicas):
            self.far(k, self.d).start()
        self.own().start()

    def step(self, i):
        pass

    def finish(self):
        self.own().wait()
        for k in range(1, self.replicas):
            self.far(k, lax.rem(self.d + self.replicas - k, self.replicas)).wait_recv()
        for k in range(1, self.replicas):
            self.far(k, self.d).wait_send()


class YJoin:
    def __init__(self, got, dst, by_columns, sems):
        self.got, self.dst, self.by_columns = got, dst, by_columns
        self.own_sem, self.send, self.recv = sems
        self.replicas, self.rows, self.cols = got.shape
        self.s = lax.axis_index("section")

    def place(self, half, z):
        rows, cols = self.rows, self.cols
        if self.by_columns:
            return self.dst.at[
                pl.ds(pl.multiple_of(half * rows, rows), rows), pl.ds(z * cols, cols)
            ]
        return self.dst.at[pl.ds(pl.multiple_of((2 * z + half) * rows, rows), rows)]

    def own(self, z):
        return pltpu.make_async_copy(self.got.at[z], self.place(self.s, z), self.own_sem.at[z])

    def side(self, z, half):
        return far_copy(
            self.got.at[z],
            self.place(half, z),
            self.send.at[z],
            self.recv.at[z],
            {"section": 1 - self.s},
        )

    def start(self):
        for z in range(self.replicas):
            self.side(z, self.s).start()
            self.own(z).start()

    def step(self, i):
        pass

    def finish(self):
        for z in range(self.replicas):
            self.own(z).wait()
            self.side(z, 1 - self.s).wait_recv()
        for z in range(self.replicas):
            self.side(z, self.s).wait_send()


def rider_sems(replicas):
    far, side = DMA((replicas - 1,)), DMA((replicas,))
    return [DMA((1,)), far, far, side, side]


class Riders:
    def __init__(self, srcs, dsts, columns, sems):
        self.all = []
        for src, dst, (kind, layer, by) in zip(srcs, dsts, columns):
            count = 5 if kind == "spread" else 3
            own, sems = sems[:count], sems[count:]
            if kind == "spread":
                self.all.append(Spread(src.at[layer], dst, by, own))
            elif kind == "z":
                self.all.append(ZGather(src.at[layer], dst, own))
            else:
                self.all.append(YJoin(src, dst, by, own))
        self.replicas = self.all[0].replicas if self.all else 0

    def start(self):
        for one in self.all:
            one.start()

    def step(self, j, n):
        if not self.all:
            return
        stages = self.replicas // 2
        for i in range(stages):

            @pl.when(j == n * (i + 1) // stages - 1)
            def _(i=i):
                for one in self.all:
                    one.step(i)

    def finish(self):
        for one in self.all:
            one.finish()


def riding(riders, replicas):
    arrays = [array for array, _, _, _ in riders]
    columns = tuple(rider[1:] for rider in riders)
    outs, sems = [], []
    for array, kind, _, by in riders:
        rows, cols = array.shape[1:]
        if kind == "z":
            outs.append(shape((replicas, rows, cols), BF))
        else:
            outs.append(
                shape((2 * rows, replicas * cols) if by else (2 * replicas * rows, cols), BF)
            )
        far, side = DMA((replicas - 1,)), DMA((replicas,))
        sems += {
            "spread": rider_sems(replicas),
            "z": [DMA((1,)), far, far],
            "y": [side, side, side],
        }[kind]
    return arrays, columns, outs, sems


def params(key):
    return pltpu.CompilerParams(
        vmem_limit_bytes=LIMIT, collective_id=key, has_side_effects=True
    )


def cost(flops, moved, exps=0):
    return pl.CostEstimate(flops=int(flops), bytes_accessed=int(moved), transcendentals=int(exps))


def normed(source):
    center = source - jnp.mean(source, axis=-1, keepdims=True)
    r = lax.rsqrt(jnp.mean(center * center, axis=-1, keepdims=True) + 1e-05)
    return center * r, r


def normed_back(source, gain, grad):
    n, r = normed(source)
    e = grad * gain
    dh = r * (
        e - jnp.mean(e, axis=-1, keepdims=True) - n * jnp.mean(e * n, axis=-1, keepdims=True)
    )
    return dh, jnp.sum(grad * n, axis=0, keepdims=True)


def flat(value):
    return value.reshape((value.shape[0] * value.shape[1],) + value.shape[2:])


def run(n, body):
    def one(j, carry):
        body(j)
        return carry

    lax.fori_loop(0, n, one, 0)


def first_kernel(
    size, replicas, x_ref, gain_ref, wq_ref, wo_ref, wu_ref, wd_ref,
    qkv_ref, gains_out, a1_out, wq_out, wo_out, q_stage, o_stage, u_stage, d_stage,
    a1, w, gains, own_sem, q_sem, o_sem, u_sem, d_sem, gain_sem, *sems
):
    rows, width = x_ref.shape
    n = chunks(rows)
    rc = rows // n
    g = Group(size)
    section = lax.axis_index("section")
    gather = Gather(g, a1, rc, sems[:4])
    swaps = [
        Swap(wq_ref, q_stage, q_sem),
        Swap(wo_ref, o_stage, o_sem),
        Swap(wu_ref, u_stage, u_sem),
        Swap(wd_ref, d_stage, d_sem),
    ]
    spreads = [
        Spread(q_stage.at[0], w, False, sems[4:9]),
        Spread(o_stage.at[0], wo_out, True, sems[9:14]),
    ]
    riders = Riders([], [], (), [])
    riders.all = spreads
    riders.replicas = replicas
    g.greet(replicas)

    def gain_copy(layer):
        return far_copy(
            gain_ref, gains.at[layer], gain_sem.at[0], gain_sem.at[1], {"section": 1 - section}
        )

    gain_copy(section).start()
    swaps[0].start()
    swaps[1].start()
    gains[section] = gain_ref[...]
    gain_copy(1 - section).wait_recv()
    gains_out[...] = gains[...]

    def send(j):
        at = span(j, rc)
        a = normed(x_ref[at, :].astype(F32))[0] * gains[0, 0:1, :]
        a1[g.me, at, :] = a.astype(BF)
        gather.start(j)

    run(n, send)
    swaps[0].arrive()
    swaps[1].arrive()
    riders.start()
    swaps[2].start()
    swaps[3].start()

    def relay(j):
        gather.relay(j)
        riders.step(j, n)

    run(n, relay)
    riders.finish()
    outs = [
        pltpu.make_async_copy(w, wq_out, own_sem.at[0]),
        pltpu.make_async_copy(a1, a1_out, own_sem.at[1]),
    ]
    outs[0].start()

    def multiply(j):
        at = span(j, rc)
        gather.ready(j)
        r = dg(flat(a1[:, at, :]), w[...], NN).astype(BF)
        qkv_ref[:, at, :] = r.reshape(size, rc, r.shape[1])

    run(n, multiply)
    outs[1].start()
    swaps[2].arrive()
    swaps[3].arrive()
    for swap in swaps:
        swap.finish()
    gain_copy(section).wait_send()
    gather.drain(n)
    for out in outs:
        out.wait()


def first_forward(size, replicas, x, gains, ws):
    rows, width = x.shape
    wide = ws[0].shape[2]
    deep = 2 * ws[1].shape[1]
    n = chunks(rows)
    return pl.pallas_call(
        functools.partial(first_kernel, size, replicas),
        out_shape=[
            shape((size, rows, wide), BF),
            shape((2,) + gains.shape, F32),
            shape((size, rows, width), BF),
            shape((width, wide), BF),
            shape((deep, width), BF),
        ]
        + [shape(w.shape, BF) for w in ws],
        in_specs=[VM, VM] + [HB] * 4,
        out_specs=[VM, VM] + [HB] * 7,
        scratch_shapes=[
            pltpu.VMEM((size, rows, width), BF),
            pltpu.VMEM((width, wide), BF),
            pltpu.VMEM((2,) + gains.shape, F32),
            DMA((2,)),
            DMA((3,)),
            DMA((3,)),
            DMA((3,)),
            DMA((3,)),
            DMA((2,)),
        ]
        + comm_sems(size, n)
        + rider_sems(replicas) * 2,
        compiler_params=params(0),
        cost_estimate=cost(30e9, 30e6),
    )(x, gains, *ws)


def qkv_kernel(size, layer, columns, *refs):
    m = len(columns)
    x_ref, gain_ref, w_ref = refs[:3]
    halves, refs = refs[3 : 3 + m], refs[3 + m :]
    qkv_ref, a1_out = refs[:2]
    wholes, refs = refs[2 : 2 + m], refs[2 + m :]
    a1, w, w_sem, out_sem = refs[:4]
    sems, refs = refs[4:8], refs[8:]
    riders = Riders(halves, wholes, columns, refs)
    rows, width = x_ref.shape
    n = chunks(rows)
    rc = rows // n
    g = Group(size)
    copy = pltpu.make_async_copy(w_ref, w, w_sem.at[0])
    copy.start()
    g.greet(riders.replicas)
    gather = Gather(g, a1, rc, sems)
    riders.start()

    def send(j):
        at = span(j, rc)
        a = normed(x_ref[at, :].astype(F32))[0] * gain_ref[layer, 0:1, :]
        a1[g.me, at, :] = a.astype(BF)
        gather.start(j)

    run(n, send)
    copy.wait()

    def work(j):
        at = span(j, rc)
        gather.relay(j)
        gather.ready(j)
        r = dg(flat(a1[:, at, :]), w[...], NN).astype(BF)
        qkv_ref[:, at, :] = r.reshape(size, rc, r.shape[1])
        riders.step(j, n)

    run(n, work)
    out = pltpu.make_async_copy(a1, a1_out, out_sem.at[0])
    out.start()
    riders.finish()
    gather.drain(n)
    out.wait()


def qkv_forward(size, replicas, layer, x, gains, w, riders):
    rows, width = x.shape
    wide = w.shape[1]
    n = chunks(rows)
    halves, columns, outs, sems = riding(riders, replicas)
    return pl.pallas_call(
        functools.partial(qkv_kernel, size, layer, columns),
        out_shape=[
            shape((size, rows, wide), BF),
            shape((size, rows, width), BF),
        ]
        + outs,
        in_specs=[VM, VM, HB] + [HB] * len(riders),
        out_specs=[VM, HB] + [HB] * len(outs),
        scratch_shapes=[
            pltpu.VMEM((size, rows, width), BF),
            pltpu.VMEM((width, wide), BF),
            DMA((1,)),
            DMA((1,)),
        ]
        + comm_sems(size, n)
        + sems,
        compiler_params=params(layer),
        cost_estimate=cost(20e9, 30e6),
    )(x, gains, w, *halves)


def attend_kernel(size, layer, columns, *refs):
    m = len(columns)
    qkv_ref, qm_ref, km_ref, x_ref, w_ref = refs[:5]
    refs = refs[5:]
    if layer == 1:
        cot_ref, refs = refs[0], refs[1:]
    halves, refs = refs[:m], refs[m:]
    h1_ref, ctx_ref, lse_ref = refs[:3]
    refs = refs[3:]
    if layer == 1:
        cot_out, refs = refs[0], refs[1:]
    wholes, refs = refs[:m], refs[m:]
    ka, vt, w, w_sem = refs[:4]
    scratch, refs = refs[4:13], refs[13:]
    if layer == 1:
        cot_sems, cot_sem, refs = refs[:4], refs[4], refs[5:]
    riders = Riders(halves, wholes, columns, refs)
    _, rows, wide = qkv_ref.shape
    length = size * rows
    e = qm_ref.shape[2]
    heads = wide // (3 * e)
    c = e**-0.5 * math.log2(math.e)
    n = chunks(rows)
    rc = rows // n
    bq = size * rc
    kc = bq
    g = Group(size)
    copy = pltpu.make_async_copy(w_ref, w, w_sem.at[0])
    copy.start()
    g.greet(riders.replicas)
    riders.start()
    if layer == 1:
        cot = Gather(g, cot_out, rows, cot_sems)
        own = pltpu.make_async_copy(cot_ref, cot_out.at[g.me], cot_sem.at[0])
        own.start()
        own.wait()
        cot.start(0)
    scatter = Scatter(g, rc, scratch)
    whole = flat(qkv_ref[...])
    for h in range(heads):
        o = 3 * e * h
        ka[h, :, :e] = whole[:, o + e : o + 2 * e]
        ka[h, :, e:] = flat(km_ref[...])
        vt[h, :e, :] = whole[:, o + 2 * e : o + 3 * e].T
        vt[h, e:, :] = jnp.ones((16, length), BF)
    copy.wait()

    def work(j):
        at = span(j, rc)
        qm = flat(qm_ref[:, at, :])
        found = []
        held_qkv = flat(qkv_ref[:, at, :])
        for h in range(heads):
            o = 3 * e * h
            q = jnp.concatenate([held_qkv[:, o : o + e], qm], axis=1)
            held = []
            top = None
            for k in range(length // kc):
                s = dg(ka[h, k * kc : (k + 1) * kc, :], q, NT)
                t = jnp.max(s, axis=0, keepdims=True)
                top = t if top is None else jnp.maximum(top, t)
                held.append(s)
            top = top * c
            acc = None
            for k in range(length // kc):
                p = jnp.exp2(held[k] * c - top).astype(BF)
                a = dg(vt[h, :, k * kc : (k + 1) * kc], p, NN)
                acc = a if acc is None else acc + a
            total = acc[e : e + 1]
            found.append((acc[:e] * (1.0 / total)).astype(BF))
            lse_ref[j, h : h + 1, :] = top + jnp.log2(total)
        ctx = (jnp.concatenate(found, axis=0) if heads > 1 else found[0]).T
        ctx_ref[:, at, :] = ctx.reshape(size, rc, heads * e)
        width = x_ref.shape[1]
        scatter.part[:, at, :] = dg(ctx, w[...], NN).reshape(size, rc, width)
        scatter.first(j)
        scatter.second(j)
        riders.step(j, n)
        if layer == 1:

            @pl.when(j == n - 1)
            def _():
                cot.relay(0)

    run(n, work)

    def last(j):
        at = span(j, rc)
        h1_ref[at, :] = x_ref[at, :].astype(F32) + scatter.third(j)

    run(n, last)
    scatter.drain(n)
    if layer == 1:
        cot.ready(0)
        cot.drain(1)
    riders.finish()


def attend(size, replicas, layer, qkv, qm, km, x, w, riders, cot=()):
    _, rows, wide = qkv.shape
    e = qm.shape[2]
    heads = wide // (3 * e)
    width = x.shape[1]
    n = chunks(rows)
    halves, columns, outs, sems = riding(riders, replicas)
    return pl.pallas_call(
        functools.partial(attend_kernel, size, layer, columns),
        out_shape=[
            shape((rows, width), F32),
            shape((size, rows, heads * e), BF),
            shape((n, heads, size * rows // n), F32),
        ]
        + [shape((size, rows, width), BF) for _ in cot]
        + outs,
        in_specs=[VM, VM, VM, VM, HB] + [HB] * (len(cot) + len(riders)),
        out_specs=[VM, VM, VM] + [HB] * (len(cot) + len(outs)),
        scratch_shapes=[
            pltpu.VMEM((heads, size * rows, 2 * e), BF),
            pltpu.VMEM((heads, e + 16, size * rows), BF),
            pltpu.VMEM((heads * e, width), BF),
            DMA((1,)),
        ]
        + scatter_scratch(size, rows, width, n)
        + (comm_sems(size, 1) + [DMA((1,))]) * len(cot)
        + sems,
        compiler_params=params(2 + layer),
        cost_estimate=cost(60e9, 20e6),
    )(qkv, qm, km, x, w, *cot, *halves)


def mlp_kernel(size, layer, columns, *refs):
    m = len(columns)
    h1_ref, gain_ref, wu_ref, wd_ref = refs[:4]
    halves, refs = refs[4 : 4 + m], refs[4 + m :]
    y_ref, a2_out, hid_out, slope_out = refs[:4]
    wholes, refs = refs[4 : 4 + m], refs[4 + m :]
    a2, hid, slope, wu, wd, w_sem, out_sem = refs[:7]
    scratch, refs = refs[7:20], refs[20:]
    riders = Riders(halves, wholes, columns, refs)
    rows, width = h1_ref.shape
    hidden = wu_ref.shape[1]
    fb = min(256, hidden)
    n = chunks(rows)
    rc = rows // n
    g = Group(size)
    copies = [
        pltpu.make_async_copy(wu_ref, wu, w_sem.at[0]),
        pltpu.make_async_copy(wd_ref, wd, w_sem.at[1]),
    ]
    for copy in copies:
        copy.start()
    g.greet(riders.replicas)
    gather = Gather(g, a2, rc, scratch[:4])
    scatter = Scatter(g, rc, scratch[4:])

    def send(j):
        at = span(j, rc)
        a = normed(h1_ref[at, :])[0] * gain_ref[layer, 1:2, :]
        a2[g.me, at, :] = a.astype(BF)
        gather.start(j)

    run(n, send)
    riders.start()
    for copy in copies:
        copy.wait()

    def work(j):
        at = span(j, rc)
        gather.relay(j)
        gather.ready(j)
        a = flat(a2[:, at, :])
        for f in range(hidden // fb):
            cols = slice(f * fb, (f + 1) * fb)
            u = dg(a, wu[:, cols], NN)
            half = 0.5 + 0.5 * lax.erf(u * (0.5**0.5))
            slope[:, at, cols] = (
                (half + u * jnp.exp(-0.5 * u * u) * ((2 * math.pi) ** -0.5))
                .astype(BF)
                .reshape(size, rc, fb)
            )
            hid[:, at, cols] = (u * half).astype(BF).reshape(size, rc, fb)
        held = flat(hid[:, at, :])
        for f in range(width // 256):
            cols = slice(f * 256, (f + 1) * 256)
            scatter.part[:, at, cols] = dg(held, wd[:, cols], NN).reshape(size, rc, 256)
        scatter.first(j)
        scatter.second(j)
        riders.step(j, n)

    run(n, work)
    outs = [
        pltpu.make_async_copy(a2, a2_out, out_sem.at[0]),
        pltpu.make_async_copy(hid, hid_out, out_sem.at[1]),
        pltpu.make_async_copy(slope, slope_out, out_sem.at[2]),
    ]
    for out in outs:
        out.start()

    def last(j):
        at = span(j, rc)
        y_ref[at, :] = (h1_ref[at, :] + scatter.third(j)).astype(BF)

    run(n, last)
    riders.finish()
    gather.drain(n)
    scatter.drain(n)
    for out in outs:
        out.wait()


def mlp_forward(size, replicas, layer, h1, gains, wu, wd, riders):
    rows, width = h1.shape
    hidden = wu.shape[1]
    n = chunks(rows)
    halves, columns, outs, sems = riding(riders, replicas)
    return pl.pallas_call(
        functools.partial(mlp_kernel, size, layer, columns),
        out_shape=[
            shape((rows, width), BF),
            shape((size, rows, width), BF),
            shape((size, rows, hidden), BF),
            shape((size, rows, hidden), BF),
        ]
        + outs,
        in_specs=[VM, VM, HB, HB] + [HB] * len(riders),
        out_specs=[VM, HB, HB, HB] + [HB] * len(outs),
        scratch_shapes=[
            pltpu.VMEM((size, rows, width), BF),
            pltpu.VMEM((size, rows, hidden), BF),
            pltpu.VMEM((size, rows, hidden), BF),
            pltpu.VMEM((width, hidden), BF),
            pltpu.VMEM((hidden, width), BF),
            DMA((2,)),
            DMA((3,)),
        ]
        + comm_sems(size, n)
        + scatter_scratch(size, rows, width, n)
        + sems,
        compiler_params=params(4 + layer),
        cost_estimate=cost(50e9, 30e6),
    )(h1, gains, wu, wd, *halves)


def mlp_back_kernel(size, layer, parts, *refs):
    g_ref, h1_ref, gain_ref, a2_ref, hid_ref, slope_ref, wu_ref, wd_ref = refs[:8]
    refs = refs[8:]
    if layer == 1:
        ys, whole_ref, refs = refs[:2], refs[2], refs[3:]
    mid_ref, gain_out, gup_ref, gdown_ref = refs[:4]
    refs = refs[4:]
    if layer == 1:
        y_out, refs = refs[0], refs[1:]
    grad, a2, hid, dup, wu, wd, w_sem = refs[:7]
    scratch, refs = refs[7:20], refs[20:]
    rows, width = h1_ref.shape
    hidden = wu_ref.shape[1]
    depth = width // parts
    fb = min(256, hidden)
    n = chunks(rows)
    rc = rows // n
    g = Group(size)
    copies = [
        pltpu.make_async_copy(wd_ref, wd, w_sem.at[0]),
        pltpu.make_async_copy(slope_ref, dup, w_sem.at[1]),
        pltpu.make_async_copy(wu_ref, wu, w_sem.at[2]),
    ]
    late = [
        pltpu.make_async_copy(hid_ref, hid, w_sem.at[3]),
        pltpu.make_async_copy(a2_ref, a2, w_sem.at[4]),
    ]
    for copy in copies + late:
        copy.start()
    g.greet(side=layer == 1)
    section = lax.axis_index("section")
    if layer == 1:
        y_sem = refs[0]

        def y_copies(own, other, at):
            return (
                pltpu.make_async_copy(own, y_out.at[section], y_sem.at[0]),
                far_copy(
                    other, y_out.at[at], y_sem.at[1], y_sem.at[2], {"section": 1 - section}
                ),
            )

        for i in range(2):

            @pl.when(section == i)
            def _(i=i):
                for copy in y_copies(ys[i], ys[1 - i], section):
                    copy.start()

    gather = Gather(g, grad, rc, scratch[:4])
    scatter = Scatter(g, rc, scratch[4:])

    def send(j):
        at = span(j, rc)
        grad[g.me, at, :] = g_ref[at, :]
        gather.start(j)

    if layer == 1:
        whole = pltpu.make_async_copy(whole_ref, grad, w_sem.at[5])
        whole.start()
        copies.append(whole)
    else:
        run(n, send)
    for copy in copies:
        copy.wait()

    def work(j):
        at = span(j, rc)
        if layer == 0:
            gather.relay(j)
            gather.ready(j)
        held = flat(grad[:, at, :])
        for f in range(hidden // fb):
            cols = slice(f * fb, (f + 1) * fb)
            d = dg(held, wd[cols, :], NT) * flat(dup[:, at, cols]).astype(F32)
            dup[:, at, cols] = d.astype(BF).reshape(size, rc, fb)
        held = flat(dup[:, at, :])
        for z in range(parts):
            cols = slice(z * depth, (z + 1) * depth)
            scatter.part[:, at, cols] = dg(held, wu[cols, :], NT).reshape(size, rc, depth)
        scatter.first(j)
        scatter.second(j)

    run(n, work)
    for copy in late:
        copy.wait()

    def up_grad(z):
        cols = pl.ds(pl.multiple_of(z * depth, depth), depth)
        gup_ref[z] = dg(flat(a2[:, :, cols]), flat(dup[...]), TN).astype(BF)

    run(parts, up_grad)

    def down_grad(f):
        cols = pl.ds(pl.multiple_of(f * fb, fb), fb)
        r = dg(flat(hid[:, :, cols]), flat(grad[...]), TN).astype(BF)
        for z in range(parts):
            gdown_ref[z, cols, :] = r[:, z * depth : (z + 1) * depth]

    run(hidden // fb, down_grad)
    gain_out[...] = jnp.zeros_like(gain_out)

    def last(j):
        at = span(j, rc)
        dh, dgain = normed_back(h1_ref[at, :], gain_ref[layer, 1:2, :], scatter.third(j))
        mid_ref[at, :] = g_ref[at, :].astype(F32) + dh
        gain_out[...] += dgain

    run(n, last)
    if layer == 1:
        local, side = y_copies(ys[0], ys[1], 1 - section)
        local.wait()
        side.wait_recv()
        y_copies(ys[0], ys[1], section)[1].wait_send()
    if layer == 0:
        gather.drain(n)
    scatter.drain(n)


def mlp_backward(size, replicas, layer, grad, h1, gains, a2, hid, slope, wu, wd, extra):
    rows, width = h1.shape
    hidden = wu.shape[1]
    parts, depth = replicas, width // replicas
    n = chunks(rows)
    return pl.pallas_call(
        functools.partial(mlp_back_kernel, size, layer, parts),
        out_shape=[
            shape((rows, width), F32),
            shape((1, width), F32),
            shape((parts, depth, hidden), BF),
            shape((parts, hidden, depth), BF),
        ]
        + [shape((2, rows, width), BF)] * (len(extra) // 3),
        in_specs=[VM, VM, VM] + [HB] * (5 + len(extra)),
        out_specs=[VM, VM, VM, VM] + [HB] * (len(extra) // 3),
        scratch_shapes=[
            pltpu.VMEM((size, rows, width), BF),
            pltpu.VMEM((size, rows, width), BF),
            pltpu.VMEM((size, rows, hidden), BF),
            pltpu.VMEM((size, rows, hidden), BF),
            pltpu.VMEM((width, hidden), BF),
            pltpu.VMEM((hidden, width), BF),
            DMA((6,)),
        ]
        + comm_sems(size, n)
        + scatter_scratch(size, rows, width, n)
        + [DMA((3,))] * (len(extra) // 3),
        compiler_params=params(6 + layer),
        cost_estimate=cost(60e9, 40e6),
    )(grad, h1, gains, a2, hid, slope, wu, wd, *extra)


def attend_back_kernel(size, layer, parts, *refs):
    mid_ref, qkv_ref, qm_ref, km_ref, ctx_ref, lse_ref, w_ref = refs[:7]
    refs = refs[7:]
    if layer == 0:
        gdown_ref, refs = refs[0], refs[1:]
    dqkv_ref, gout_ref, refs = refs[0], refs[1], refs[2:]
    if layer == 0:
        down_out, refs = refs[0], refs[1:]
    da, ka, va, kt, dk, dv, w, w_sem = refs[:8]
    sems, refs = refs[8:12], refs[12:]
    reduce = Reduce(layer, refs[:9])
    if layer == 0:
        down = HalfReduce(layer, refs[9 : 9 + HALF])
        down_swap = HalfSwap(gdown_ref, down.other, refs[9 + HALF])
    _, rows, wide = qkv_ref.shape
    length = size * rows
    e = qm_ref.shape[2]
    heads = wide // (3 * e)
    scale = e**-0.5
    c = scale * math.log2(math.e)
    depth = w_ref.shape[1] // parts
    n = chunks(rows)
    rc = rows // n
    bq = size * rc
    kc = bq
    g = Group(size)
    copies = [pltpu.make_async_copy(w_ref, w, w_sem.at[0])]
    for copy in copies:
        copy.start()
    g.greet(parts)
    gather = Gather(g, da, rc, sems)
    loads = []
    if layer == 0:
        down_swap.copy().start()
        loads = down.loads(gdown_ref, None)
        for load in loads:
            load.start()

    def send(j):
        at = span(j, rc)
        da[g.me, at, :] = mid_ref[at, :].astype(BF)
        gather.start(j)

    run(n, send)
    lane = lax.broadcasted_iota(jnp.int32, (length, e), 1)
    whole = flat(qkv_ref[...])
    for h in range(heads):
        o = 3 * e * h
        ka[h, :, :e] = whole[:, o + e : o + 2 * e]
        ka[h, :, e:] = flat(km_ref[...])
        va[h, :, :e] = whole[:, o + 2 * e : o + 3 * e]
        va[h, :, e:] = jnp.where(lane < 3, 1.0, 0.0).astype(BF)
        kt[h] = whole[:, o + e : o + 2 * e].T
    dk[...] = jnp.zeros_like(dk)
    dv[...] = jnp.zeros_like(dv)
    ql = lax.broadcasted_iota(jnp.int32, (bq, e), 1)
    for copy in copies + loads:
        copy.wait()

    def out_grad(z):
        cols = pl.ds(pl.multiple_of(z * depth, depth), depth)
        return dg(flat(ctx_ref[...]), flat(da[:, :, cols]), TN)

    def work(j):
        at = span(j, rc)

        @pl.when(j == 0)
        def _():
            gather.relay(0)
            gather.ready(0)

        @pl.when(j == min(1, n - 1))
        def _():
            for i in range(1, n):
                gather.relay(i)
            for i in range(1, n):
                gather.ready(i)
            reduce.send(out_grad)

        qm = flat(qm_ref[:, at, :])
        dctx = dg(flat(da[:, at, :]), w[...], NT).astype(BF)
        ctx = flat(ctx_ref[:, at, :])
        held_qkv = flat(qkv_ref[:, at, :])
        for h in range(heads):
            o = 3 * e * h
            qq = held_qkv[:, o : o + e]
            q = jnp.concatenate([qq, qm], axis=1)
            dc = dctx[:, h * e : (h + 1) * e]
            prod = dc.astype(F32) * ctx[:, h * e : (h + 1) * e].astype(F32)
            d = -jnp.sum(prod, axis=1, keepdims=True)
            d1 = d.astype(BF).astype(F32)
            d2 = (d - d1).astype(BF).astype(F32)
            d3 = d - d1 - d2
            ds_col = jnp.where(ql == 0, d1, jnp.where(ql == 1, d2, jnp.where(ql == 2, d3, 0.0)))
            dca = jnp.concatenate([dc, ds_col.astype(BF)], axis=1)
            lse = lse_ref[j, h : h + 1, :]
            dqt = None
            for k in range(length // kc):
                ks = slice(k * kc, (k + 1) * kc)
                s = dg(ka[h, ks, :], q, NT)
                p = jnp.exp2(s * c - lse)
                ds = (p * dg(va[h, ks, :], dca, NT)).astype(BF)
                dv[h, ks, :] += dg(p.astype(BF), dc, NN)
                dk[h, ks, :] += dg(ds, qq, NN)
                a = dg(kt[h, :, ks], ds, NN)
                dqt = a if dqt is None else dqt + a
            if layer == 0 and h == heads // 2:

                @pl.when(j == min(1, n - 1))
                def _():
                    down_swap.copy().wait_recv()
                    down.middle()

            if layer == 0 and h == heads - 1:

                @pl.when(j == n - 1)
                def _():
                    down.late()

            dqkv_ref[:, at, o : o + e] = (dqt * scale).T.astype(BF).reshape(size, rc, e)

    run(n, work)
    for h in range(heads):
        o = 3 * e * h
        dqkv_ref[:, :, o + e : o + 2 * e] = (dk[h] * scale).astype(BF).reshape(size, rows, e)
        dqkv_ref[:, :, o + 2 * e : o + 3 * e] = dv[h].astype(BF).reshape(size, rows, e)

    reduce.collect()
    reduce.finish(gout_ref)
    if layer == 0:
        down.finish(down_out)
        down_swap.copy().wait_send()
    gather.drain(n)


def attend_backward(size, replicas, layer, mid, qkv, qm, km, ctx, lse, w, grads):
    _, rows, wide = qkv.shape
    e = qm.shape[2]
    heads = wide // (3 * e)
    width = mid.shape[1]
    parts, depth = replicas, width // replicas
    length = size * rows
    n = chunks(rows)
    return pl.pallas_call(
        functools.partial(attend_back_kernel, size, layer, parts),
        out_shape=[shape(qkv.shape, BF), shape((heads * e, depth), F32)]
        + [shape(grad.shape[1:], F32) for grad in grads],
        in_specs=[VM] * 6 + [HB] * (1 + len(grads)),
        out_specs=[VM, VM] + [VM] * len(grads),
        scratch_shapes=[
            pltpu.VMEM((size, rows, width), BF),
            pltpu.VMEM((heads, length, 2 * e), BF),
            pltpu.VMEM((heads, length, 2 * e), BF),
            pltpu.VMEM((heads, e, length), BF),
            pltpu.VMEM((heads, length, e), F32),
            pltpu.VMEM((heads, length, e), F32),
            pltpu.VMEM((heads * e, width), BF),
            DMA((1,)),
        ]
        + comm_sems(size, n)
        + reduce_scratch(parts, heads * e, depth)
        + sum([half_scratch(parts, *grad.shape[1:]) + [DMA((2,))] for grad in grads], []),
        compiler_params=params(8 + layer),
        cost_estimate=cost(90e9, 40e6),
    )(mid, qkv, qm, km, ctx, lse, w, *grads)


def qkv_back_kernel(
    size, layer, parts, dqkv_ref, a1_ref, x_ref, mid_ref, gain_ref, w_ref,
    dx_ref, gain_out, gqkv_ref, w, w_sem, *scratch
):
    rows, width = x_ref.shape
    depth = width // parts
    n = chunks(rows)
    rc = rows // n
    g = Group(size)
    copies = [pltpu.make_async_copy(w_ref, w, w_sem.at[0])]
    for copy in copies:
        copy.start()
    g.greet()
    scatter = Scatter(g, rc, scratch)
    for copy in copies:
        copy.wait()

    def work(j):
        at = span(j, rc)
        held = flat(dqkv_ref[:, at, :])
        for z in range(parts):
            cols = slice(z * depth, (z + 1) * depth)
            scatter.part[:, at, cols] = dg(held, w[cols, :], NT).reshape(size, rc, depth)
        scatter.first(j)
        scatter.second(j)

    run(n, work)

    def qkv_grad(z):
        cols = pl.ds(pl.multiple_of(z * depth, depth), depth)
        gqkv_ref[z] = dg(flat(a1_ref[:, :, cols]), flat(dqkv_ref[...]), TN).astype(BF)

    run(parts, qkv_grad)
    gain_out[...] = jnp.zeros_like(gain_out)

    def last(j):
        at = span(j, rc)
        dh, dgain = normed_back(
            x_ref[at, :].astype(F32), gain_ref[layer, 0:1, :], scatter.third(j)
        )
        dx_ref[at, :] = (mid_ref[at, :] + dh).astype(BF)
        gain_out[...] += dgain

    run(n, last)
    scatter.drain(n)


def qkv_backward(size, replicas, layer, dqkv, a1, x, mid, gains, w):
    rows, width = x.shape
    wide = w.shape[1]
    parts, depth = replicas, width // replicas
    n = chunks(rows)
    return pl.pallas_call(
        functools.partial(qkv_back_kernel, size, layer, parts),
        out_shape=(
            shape((rows, width), BF),
            shape((1, width), F32),
            shape((parts, depth, wide), BF),
        ),
        in_specs=[VM] * 5 + [HB],
        out_specs=(VM, VM, VM),
        scratch_shapes=[
            pltpu.VMEM((width, wide), BF),
            DMA((1,)),
        ]
        + scatter_scratch(size, rows, width, n),
        compiler_params=params(11),
        cost_estimate=cost(30e9, 30e6),
    )(dqkv, a1, x, mid, gains, w)


def last_kernel(
    size, parts, dqkv_ref, a1_ref, x_ref, mid_ref, gain_ref, w_ref, two_ref, above_ref, dx1_ref,
    gain_out, gqkv_out, dx_out,
    gqkv, swap_sem, w, dx, gsum, gcame, w_sem, x_sem, x_send, x_recv, g_send, g_recv, *scratch
):
    rows, width = x_ref.shape
    depth = width // parts
    n = chunks(rows)
    rc = rows // n
    g = Group(size)
    section = lax.axis_index("section")
    d = lax.axis_index("dp")
    copy = pltpu.make_async_copy(w_ref, w, w_sem.at[0])
    copy.start()
    reduce = HalfReduce(0, scratch[:HALF])
    swap = HalfSwap(gqkv, reduce.other, swap_sem)
    scatter = Scatter(g, rc, scratch[HALF:])
    g.greet(parts)

    def upper():
        return far_copy(
            dx1_ref, dx_out.at[0], x_send.at[n], x_recv.at[n], {"section": 1 - section}
        )

    def keep_upper():
        return pltpu.make_async_copy(dx1_ref, dx_out.at[1], x_sem.at[0])

    def lower(j):
        at = span(j, rc)
        return far_copy(
            dx.at[at], dx_out.at[1, at], x_send.at[j], x_recv.at[j], {"section": 1 - section}
        )

    def keep_lower(j):
        at = span(j, rc)
        return pltpu.make_async_copy(dx.at[at], dx_out.at[0, at], x_sem.at[j])

    def qkv_grad(z):
        cols = pl.ds(pl.multiple_of(z * depth, depth), depth)
        gqkv[z] = dg(flat(a1_ref[:, :, cols]), flat(dqkv_ref[...]), TN).astype(BF)

    run(parts, qkv_grad)
    swap.copy().start()
    load = reduce.loads(gqkv, None)[0]
    load.start()

    @pl.when(section == 1)
    def _():
        keep_upper().start()

    copy.wait()

    def work(j):
        at = span(j, rc)
        held = flat(dqkv_ref[:, at, :])
        for z in range(parts):
            cols = slice(z * depth, (z + 1) * depth)
            scatter.part[:, at, cols] = dg(held, w[cols, :], NT).reshape(size, rc, depth)
        scatter.first(j)
        scatter.second(j)

    run(n, work)
    gsum[0] = jnp.zeros_like(gsum[0])

    def last(j):
        at = span(j, rc)
        dh, dgain = normed_back(x_ref[at, :].astype(F32), gain_ref[0, 0:1, :], scatter.third(j))
        dx[at, :] = (mid_ref[at, :] + dh).astype(BF)

        @pl.when(section == 0)
        def _():
            keep_lower(j).start()

        @pl.when(section == 1)
        def _():
            lower(j).start()

        gsum[0, 0:1, :] += dgain

    def rest(j):
        @pl.when(j == n // 2)
        def _():
            load.wait()
            swap.copy().wait_recv()
            reduce.middle()

            @pl.when(section == 0)
            def _():
                upper().start()

        last(j)

    run(n, rest)
    gsum[0, 1:2, :] = two_ref[...]
    gsum[0, 2:4, :] = above_ref[...]

    targets = [
        [{"tensor": g.sibling}],
        [{"tensor": g.ahead(k) * 2 + g.core} for k in range(1, g.chips)],
        [{"dp": lax.rem(d + k, parts)} for k in range(1, parts)],
        [{"section": 1 - section}],
    ]
    slot = 0
    sent = []

    def exchange(stage):
        nonlocal slot
        copies = []
        for target in targets[stage]:
            copies.append(
                far_copy(gsum.at[stage], gcame.at[slot], g_send.at[slot], g_recv.at[slot], target)
            )
            copies[-1].start()
            slot += 1
        total = gsum[stage]
        for i, copy in enumerate(copies):
            copy.wait_recv()
            total = total + gcame[slot - len(copies) + i]
        gsum[stage + 1] = total
        sent.extend(copies)

    exchange(0)
    exchange(1)
    reduce.late()
    exchange(2)
    exchange(3)
    gain_out[...] = gsum[4]

    @pl.when(section == 0)
    def _():
        for j in range(n):
            lower(j).wait_recv()
            keep_lower(j).wait()
        upper().wait_send()

    @pl.when(section == 1)
    def _():
        keep_upper().wait()
        upper().wait_recv()
        for j in range(n):
            lower(j).wait_send()

    reduce.finish(gqkv_out)
    swap.copy().wait_send()
    for copy in sent:
        copy.wait_send()
    scatter.drain(n)


def last_backward(size, replicas, dqkv, a1, x, mid, gains, w, two, above, dx1):
    rows, width = x.shape
    wide = w.shape[1]
    depth = width // replicas
    n = chunks(rows)
    slots = 1 + (size // 2 - 1) + (replicas - 1) + 1
    return pl.pallas_call(
        functools.partial(last_kernel, size, replicas),
        out_shape=(
            shape((8, width), F32),
            shape((depth, wide), F32),
            shape((2, rows, width), BF),
        ),
        in_specs=[VM] * 5 + [HB, VM, VM, HB],
        out_specs=(VM, VM, HB),
        scratch_shapes=[
            pltpu.VMEM((replicas, depth, wide), BF),
            DMA((2,)),
            pltpu.VMEM((width, wide), BF),
            pltpu.VMEM((rows, width), BF),
            pltpu.VMEM((5, 8, width), F32),
            pltpu.VMEM((slots, 8, width), F32),
            DMA((1,)),
            DMA((n,)),
            DMA((n + 1,)),
            DMA((n + 1,)),
            DMA((slots,)),
            DMA((slots,)),
        ]
        + half_scratch(replicas, depth, wide)
        + scatter_scratch(size, rows, width, n),
        compiler_params=params(10),
        cost_estimate=cost(40e9, 30e6),
    )(dqkv, a1, x, mid, gains, w, two, above, dx1)


def scene_masks(segments, e):
    same = (segments[..., None] == jnp.arange(e, dtype=jnp.int32)).astype(F32)
    used = jnp.arange(e) < SCENES
    return (
        jnp.where(used, same * MASKED, 0.0).astype(BF),
        jnp.where(used, 1.0 - same, 0.0).astype(BF),
    )


def swap_section(value):
    return lax.ppermute(value, "section", [(0, 1), (1, 0)])


def shards(
    block_input,
    segment_ids,
    cotangent,
    norm_one_gain,
    qkv_weight,
    out_weight,
    norm_two_gain,
    up_weight,
    down_weight,
):
    section = lax.axis_index("section")
    size = lax.axis_size("tensor")
    replicas = lax.axis_size("dp")

    mine = [
        qkv_weight[0].reshape((qkv_weight.shape[1], -1)),
        out_weight[0].reshape((-1, out_weight.shape[3])),
        up_weight[0],
        down_weight[0],
    ]
    mine = [w.astype(BF).reshape((2, -1, w.shape[1])) for w in mine]
    gains = jnp.concatenate(
        [norm_one_gain, norm_two_gain, jnp.zeros((6, norm_one_gain.shape[1]), F32)], axis=0
    )
    segments = lax.dynamic_index_in_dim(segment_ids, section, 0, keepdims=False)
    x = lax.dynamic_index_in_dim(block_input, section, 0, keepdims=False)
    head_dim = qkv_weight.shape[3] // 3
    qm, km = scene_masks(segments.reshape((size, -1)), head_dim)
    qkv, gains, a1, w_qkv_0, w_out_0, h_qkv, h_out, h_up, h_down = first_forward(
        size, replicas, x, gains, mine
    )
    h1, ctx, lse, w_up_0, w_down_0 = attend(
        size, replicas, 0, qkv, qm, km, x, w_out_0,
        [(h_up, "spread", 0, False), (h_down, "spread", 0, True)],
    )
    y0, a2, hid, slope, w_qkv_1, w_out_1, got_up = mlp_forward(
        size, replicas, 0, h1, gains, w_up_0, w_down_0,
        [(h_qkv, "spread", 1, False), (h_out, "spread", 1, True), (h_up, "z", 1, False)],
    )
    kept = [(x, a1, qkv, ctx, lse, h1, a2, hid, slope)]
    qkv, a1, got_down = qkv_forward(
        size, replicas, 1, y0, gains, w_qkv_1, [(h_down, "z", 1, True)]
    )
    grad = lax.dynamic_index_in_dim(cotangent, section, 0, keepdims=False)
    h1, ctx, lse, grad_all, w_up_1, w_down_1 = attend(
        size, replicas, 1, qkv, qm, km, y0, w_out_1,
        [(got_up, "y", 1, False), (got_down, "y", 1, True)], [grad],
    )
    y1, a2, hid, slope = mlp_forward(size, replicas, 1, h1, gains, w_up_1, w_down_1, [])
    kept.append((y0, a1, qkv, ctx, lse, h1, a2, hid, slope))
    weights = [
        (w_qkv_0, w_out_0, w_up_0, w_down_0),
        (w_qkv_1, w_out_1, w_up_1, w_down_1),
    ]
    def reduce_rows(value):
        return lax.psum_scatter(value, "dp", scatter_dimension=0, tiled=False)

    x, a1, qkv, ctx, lse, h1, a2, hid, slope = kept[1]
    w_qkv, w_out, w_up, w_down = weights[1]
    mid, gain_two, g_up, g_down, layer_out = mlp_backward(
        size, replicas, 1, grad, h1, gains, a2, hid, slope, w_up, w_down, [y0, y1, grad_all]
    )
    d_qkv, out_1 = attend_backward(size, replicas, 1, mid, qkv, qm, km, ctx, lse, w_out, [])
    up_1, down_1 = reduce_rows(g_up), reduce_rows(g_down)
    dx1, gain_one, g_qkv = qkv_backward(size, replicas, 1, d_qkv, a1, x, mid, gains, w_qkv)
    gains_above = jnp.concatenate([gain_one, gain_two], axis=0)
    dx1, up_1, down_1 = lax.optimization_barrier((dx1, up_1, down_1))
    qkv_1 = reduce_rows(g_qkv)

    x, a1, qkv, ctx, lse, h1, a2, hid, slope = kept[0]
    w_qkv, w_out, w_up, w_down = weights[0]
    mid, gain_two, g_up, g_down = mlp_backward(
        size, replicas, 0, dx1, h1, gains, a2, hid, slope, w_up, w_down, []
    )
    mid, qkv_1 = lax.optimization_barrier((mid, qkv_1))
    d_qkv, out_0, down_0 = attend_backward(
        size, replicas, 0, mid, qkv, qm, km, ctx, lse, w_out, [g_down]
    )
    up_0 = reduce_rows(g_up)
    d_qkv, up_0 = lax.optimization_barrier((d_qkv, up_0))
    gains, qkv_0, input_out = last_backward(
        size, replicas, d_qkv, a1, x, mid, gains, w_qkv, gain_two, gains_above, dx1
    )

    def finish(zero, one):
        send = swap_section(jnp.where(section == 0, one, zero))
        return jnp.where(section == 0, zero, one).astype(F32) + send.astype(F32)

    other_qkv_1 = swap_section(qkv_1)
    qkv_grad = jnp.where(section == 0, qkv_0, qkv_1.astype(F32) + other_qkv_1.astype(F32))
    out_grad = jnp.where(section == 0, out_0, out_1)
    up_grad = finish(up_0, up_1)
    other_down_1 = swap_section(down_1)
    down_grad = jnp.where(section == 0, down_0, down_1.astype(F32) + other_down_1.astype(F32))
    gains = lax.dynamic_slice_in_dim(gains, 2 * section, 2, 0)
    return (
        layer_out[None],
        input_out[None],
        gains[0:1],
        qkv_grad.reshape(qkv_weight.shape),
        out_grad.reshape(out_weight.shape),
        gains[1:2],
        up_grad[None],
        down_grad[None],
    )


def solution(mesh):
    return jax.shard_map(
        shards,
        mesh=mesh,
        in_specs=(
            P(None, ("dp", "tensor"), None),
            P(None, "dp"),
            P(None, ("dp", "tensor"), None),
            P("section", None),
            P("section", "dp", "tensor", None),
            P("section", "tensor", None, "dp"),
            P("section", None),
            P("section", "dp", "tensor"),
            P("section", "tensor", "dp"),
        ),
        out_specs=(
            P("section", None, ("dp", "tensor"), None),
            P("section", None, ("dp", "tensor"), None),
            P("section", None),
            P("section", "dp", "tensor", None),
            P("section", "tensor", None, "dp"),
            P("section", None),
            P("section", "dp", "tensor"),
            P("section", "tensor", "dp"),
        ),
        check_vma=False,
    )
```

```python
import functools
import math

import jax
import jax.numpy as jnp
from jax import lax
from jax.experimental import pallas as pl
from jax.experimental.pallas import tpu as pltpu
from jax.sharding import PartitionSpec as P

F32 = jnp.float32
BF = jnp.bfloat16
NT = (((1,), (1,)), ((), ()))
NN = (((1,), (0,)), ((), ()))
TN = (((0,), (0,)), ((), ()))
MASKED = -1e30
SCENES = 3
MESH = pl.DeviceIdType.MESH
VM = pl.BlockSpec(memory_space=pltpu.VMEM)
HB = pl.BlockSpec(memory_space=pl.ANY)
DMA = pltpu.SemaphoreType.DMA
LIMIT = 58 << 20


def dg(a, b, dims):
    return lax.dot_general(a, b, dims, preferred_element_type=F32)


def chunks(rows):
    return 4 if rows % 64 == 0 else 1


def shape(dims, dtype):
    return jax.ShapeDtypeStruct(dims, dtype)


class Group:
    def __init__(self, size):
        self.size = size
        self.chips = size // 2
        self.me = lax.axis_index("tensor")
        self.chip = lax.div(self.me, 2)
        self.core = lax.rem(self.me, 2)
        self.sibling = self.chip * 2 + 1 - self.core

    def ahead(self, k):
        return lax.rem(self.chip + k, self.chips)

    def behind(self, k):
        return lax.rem(self.chip + self.chips - k, self.chips)

    def greet(self, replicas=0, side=False):
        barrier = pltpu.get_barrier_semaphore()
        targets = [self.sibling] + [self.ahead(k) * 2 + self.core for k in range(1, self.chips)]
        targets = [{"tensor": target} for target in targets]
        if replicas:
            d = lax.axis_index("dp")
            targets += [{"dp": lax.rem(d + k, replicas)} for k in range(1, replicas)]
        if replicas or side:
            targets += [{"section": 1 - lax.axis_index("section")}]
        for target in targets:
            pl.semaphore_signal(barrier, inc=1, device_id=target, device_id_type=MESH)
        pl.semaphore_wait(barrier, len(targets))


def remote(src, dst, send, recv, target):
    return pltpu.make_async_remote_copy(
        src_ref=src,
        dst_ref=dst,
        send_sem=send,
        recv_sem=recv,
        device_id={"tensor": target},
        device_id_type=MESH,
    )


def span(j, rc):
    return pl.ds(pl.multiple_of(j * rc, rc), rc)


def comm_sems(group_size, n):
    c = group_size // 2
    far, near = DMA((max(c - 1, 1), n)), DMA((c, n))
    return [far, far, near, near]


class Gather:
    def __init__(self, g, buf, rc, sems):
        self.g, self.buf, self.rc = g, buf, rc
        self.far_send, self.far_recv, self.near_send, self.near_recv = sems

    def far(self, k, j, origin, target, src=None):
        ref = self.buf.at[origin, span(j, self.rc)]
        src = ref if src is None else src
        return remote(src, ref, self.far_send.at[k - 1, j], self.far_recv.at[k - 1, j], target)

    def near(self, k, j, origin, src=None):
        ref = self.buf.at[origin, span(j, self.rc)]
        src = ref if src is None else src
        return remote(
            src, ref, self.near_send.at[k, j], self.near_recv.at[k, j], self.g.sibling
        )

    def start(self, j, src=None):
        g = self.g
        for k in range(1, g.chips):
            self.far(k, j, g.me, g.ahead(k) * 2 + g.core, src).start()
        self.near(0, j, g.me, src).start()

    def relay(self, j):
        g = self.g
        for k in range(1, g.chips):
            origin = g.behind(k) * 2 + g.core
            self.far(k, j, origin, g.me).wait_recv()
            self.near(k, j, origin).start()

    def ready(self, j):
        g = self.g
        self.near(0, j, g.sibling).wait_recv()
        for k in range(1, g.chips):
            self.near(k, j, g.behind(k) * 2 + 1 - g.core).wait_recv()

    def drain(self, n):
        g = self.g

        def one(j, _):
            for k in range(1, g.chips):
                self.far(k, j, g.me, g.sibling).wait_send()
            for k in range(g.chips):
                self.near(k, j, g.me).wait_send()
            return 0

        lax.fori_loop(0, n, one, 0)


def scatter_scratch(group_size, rows, width, n):
    c = group_size // 2
    far = pltpu.VMEM((max(c - 1, 1), rows, width), BF)
    near = pltpu.VMEM((c, rows, width), BF)
    return [pltpu.VMEM((group_size, rows, width), F32), near, near, far, far] + comm_sems(
        group_size, n
    )


class Scatter:
    def __init__(self, g, rc, scratch):
        self.g, self.rc = g, rc
        self.part, self.near_out, self.near_in, self.far_out, self.far_in = scratch[:5]
        self.far_send, self.far_recv, self.near_send, self.near_recv = scratch[5:]

    def near(self, k, j):
        rows = span(j, self.rc)
        return remote(
            self.near_out.at[k, rows],
            self.near_in.at[k, rows],
            self.near_send.at[k, j],
            self.near_recv.at[k, j],
            self.g.sibling,
        )

    def far(self, k, j):
        rows = span(j, self.rc)
        return remote(
            self.far_out.at[k - 1, rows],
            self.far_in.at[k - 1, rows],
            self.far_send.at[k - 1, j],
            self.far_recv.at[k - 1, j],
            self.g.ahead(k) * 2 + self.g.core,
        )

    def first(self, j):
        g, rows = self.g, span(j, self.rc)
        for k in list(range(1, g.chips)) + [0]:
            owner = g.ahead(k) * 2 + 1 - g.core
            self.near_out[k, rows, :] = self.part[owner, rows, :].astype(BF)
            self.near(k, j).start()

    def second(self, j):
        g, rows = self.g, span(j, self.rc)
        for k in range(1, g.chips):
            owner = g.ahead(k) * 2 + g.core
            self.near(k, j).wait_recv()
            both = self.part[owner, rows, :] + self.near_in[k, rows, :].astype(F32)
            self.far_out[k - 1, rows, :] = both.astype(BF)
            self.far(k, j).start()

    def third(self, j):
        g, rows = self.g, span(j, self.rc)
        self.near(0, j).wait_recv()
        total = self.part[g.me, rows, :] + self.near_in[0, rows, :].astype(F32)
        for k in range(1, g.chips):
            self.far(k, j).wait_recv()
            total = total + self.far_in[k - 1, rows, :].astype(F32)
        return total

    def drain(self, n):
        g = self.g

        def one(j, _):
            for k in range(1, g.chips):
                self.far(k, j).wait_send()
            for k in range(g.chips):
                self.near(k, j).wait_send()
            return 0

        lax.fori_loop(0, n, one, 0)


def far_copy(src, dst, send, recv, target):
    return pltpu.make_async_remote_copy(
        src_ref=src,
        dst_ref=dst,
        send_sem=send,
        recv_sem=recv,
        device_id=target,
        device_id_type=MESH,
    )


class Swap:
    def __init__(self, src, stage, sems):
        self.src, self.stage, self.sems = src, stage, sems
        self.s = lax.axis_index("section")

    def copies(self, layer):
        local = pltpu.make_async_copy(self.src.at[self.s], self.stage.at[self.s], self.sems.at[0])
        side = far_copy(
            self.src.at[1 - self.s],
            self.stage.at[layer],
            self.sems.at[1],
            self.sems.at[2],
            {"section": 1 - self.s},
        )
        return local, side

    def start(self):
        for copy in self.copies(self.s):
            copy.start()

    def arrive(self):
        local, side = self.copies(1 - self.s)
        local.wait()
        side.wait_recv()

    def finish(self):
        self.copies(self.s)[1].wait_send()


def reduce_scratch(replicas, rows, cols):
    many = pltpu.VMEM((replicas - 1, rows, cols), BF)
    one = pltpu.VMEM((rows, cols), BF)
    far, side = DMA((replicas - 1, 2)), DMA((2,))
    return [pltpu.VMEM((rows, cols), F32), many, many, one, one, far, far, side, side]


class Reduce:
    def __init__(self, layer, scratch):
        self.layer = layer
        self.own, self.away, self.came, self.over, self.back = scratch[:5]
        self.z_send, self.z_recv, self.y_send, self.y_recv = scratch[5:]
        self.replicas = self.away.shape[0] + 1
        self.half = self.own.shape[0] // 2
        self.d = lax.axis_index("dp")
        self.s = lax.axis_index("section")

    def target(self, k):
        return lax.rem(self.d + k, self.replicas)

    def part(self, i):
        return pl.ds(pl.multiple_of(i * self.half, self.half), self.half)

    def z_copy(self, k, i):
        part = self.part(i)
        return far_copy(
            self.away.at[k - 1, part],
            self.came.at[k - 1, part],
            self.z_send.at[k - 1, i],
            self.z_recv.at[k - 1, i],
            {"dp": self.target(k)},
        )

    def y_copy(self, i):
        part = self.part(i)
        return far_copy(
            self.over.at[part],
            self.back.at[part],
            self.y_send.at[i],
            self.y_recv.at[i],
            {"section": 1 - self.s},
        )

    def send(self, block):
        def one(i):
            k = i + 1
            self.away[i] = block(self.target(k)).astype(BF)
            self.z_copy(k, 0).start()
            self.z_copy(k, 1).start()

        run(self.replicas - 1, one)
        self.own[...] = block(self.d)

    def collect(self):
        def one(i):
            part = self.part(i)
            total = self.own[part, :]
            for k in range(1, self.replicas):
                self.z_copy(k, i).wait_recv()
                total = total + self.came[k - 1, part, :].astype(F32)
            self.own[part, :] = total
            self.over[part, :] = total.astype(BF)

            @pl.when(self.s != self.layer)
            def _():
                self.y_copy(i).start()

        run(2, one)

    def finish(self, out):
        @pl.when(self.s == self.layer)
        def _():
            self.y_copy(0).wait_recv()
            self.y_copy(1).wait_recv()
            out[...] = self.own[...] + self.back[...].astype(F32)

        @pl.when(self.s != self.layer)
        def _():
            self.y_copy(0).wait_send()
            self.y_copy(1).wait_send()
            out[...] = self.own[...]

        for k in range(1, self.replicas):
            self.z_copy(k, 0).wait_send()
            self.z_copy(k, 1).wait_send()


class HalfSwap:
    def __init__(self, src, came, sems):
        self.src, self.came, self.sems = src, came, sems
        self.s = lax.axis_index("section")
        self.rows = came.shape[1]

    def copy(self):
        at = pl.ds(pl.multiple_of((1 - self.s) * self.rows, self.rows), self.rows)
        return far_copy(
            self.src.at[:, at],
            self.came,
            self.sems.at[0],
            self.sems.at[1],
            {"section": 1 - self.s},
        )


def half_scratch(replicas, rows, cols):
    rows = rows // 2
    all_, far = pltpu.VMEM((replicas, rows, cols), BF), pltpu.VMEM((replicas - 1, rows, cols), BF)
    one = pltpu.VMEM((rows, cols), BF)
    z = DMA((replicas - 1,))
    return [all_, all_, far, far, pltpu.VMEM((rows, cols), F32), one, one, DMA((3,)), z, z, DMA((2,))]


HALF = 11


class HalfReduce:
    def __init__(self, layer, scratch):
        self.layer = layer
        self.mine, self.other, self.away, self.came, self.own, self.over, self.back = scratch[:7]
        self.in_sem, self.z_send, self.z_recv, self.y_sem = scratch[7:]
        self.replicas, self.rows = self.mine.shape[:2]
        self.s = lax.axis_index("section")
        self.d = lax.axis_index("dp")

    def half(self, s):
        return pl.ds(pl.multiple_of(s * self.rows, self.rows), self.rows)

    def loads(self, src, other):
        loads = [pltpu.make_async_copy(src.at[:, self.half(self.s)], self.mine, self.in_sem.at[0])]
        if other is not None:
            loads.append(pltpu.make_async_copy(other, self.other, self.in_sem.at[1]))
        return loads

    def z_copy(self, k):
        return far_copy(
            self.away.at[k - 1],
            self.came.at[k - 1],
            self.z_send.at[k - 1],
            self.z_recv.at[k - 1],
            {"dp": lax.rem(self.d + k, self.replicas)},
        )

    def y_copy(self):
        return far_copy(
            self.over, self.back, self.y_sem.at[0], self.y_sem.at[1], {"section": 1 - self.s}
        )

    def middle(self):
        def both(z):
            return self.mine[z].astype(F32) + self.other[z].astype(F32)

        for k in range(1, self.replicas):
            self.away[k - 1] = both(lax.rem(self.d + k, self.replicas)).astype(BF)
            self.z_copy(k).start()
        self.own[...] = both(self.d)

    def late(self):
        total = self.own[...]
        for k in range(1, self.replicas):
            self.z_copy(k).wait_recv()
            total = total + self.came[k - 1].astype(F32)
        self.own[...] = total
        self.over[...] = total.astype(BF)

        @pl.when(self.s != self.layer)
        def _():
            self.y_copy().start()

    def finish(self, out, above=None):
        @pl.when(self.s == self.layer)
        def _():
            self.y_copy().wait_recv()
            out[self.half(self.s), :] = self.own[...]
            out[self.half(1 - self.s), :] = self.back[...].astype(F32)

        @pl.when(self.s != self.layer)
        def _():
            if above is None:
                out[...] = jnp.zeros_like(out)
            else:
                copy = pltpu.make_async_copy(above, out, self.in_sem.at[2])
                copy.start()
                copy.wait()
            self.y_copy().wait_send()

        for k in range(1, self.replicas):
            self.z_copy(k).wait_send()


class Spread:
    def __init__(self, src, dst, by_columns, sems):
        self.src, self.dst, self.by_columns = src, dst, by_columns
        self.own_sem, self.far_send, self.far_recv, self.side_send, self.side_recv = sems
        self.replicas = far = self.side_send.shape[0]
        self.s = lax.axis_index("section")
        self.d = lax.axis_index("dp")
        self.stages = [
            sorted({k, far - k}) for k in range(1, far // 2 + 1)
        ]

    def place(self, half, z):
        rows, cols = self.src.shape
        if self.by_columns:
            return self.dst.at[
                pl.ds(pl.multiple_of(half * rows, rows), rows),
                pl.ds(pl.multiple_of(z * cols, cols), cols),
            ]
        return self.dst.at[pl.ds(pl.multiple_of((2 * z + half) * rows, rows), rows)]

    def origin(self, k):
        return lax.rem(self.d + self.replicas - k, self.replicas)

    def own(self):
        return pltpu.make_async_copy(self.src, self.place(self.s, self.d), self.own_sem.at[0])

    def far(self, k, origin):
        return pltpu.make_async_remote_copy(
            src_ref=self.src,
            dst_ref=self.place(self.s, origin),
            send_sem=self.far_send.at[k - 1],
            recv_sem=self.far_recv.at[k - 1],
            device_id={"dp": lax.rem(self.d + k, self.replicas)},
            device_id_type=MESH,
        )

    def side(self, k, half):
        place = self.place(half, self.origin(k))
        return pltpu.make_async_remote_copy(
            src_ref=self.src if k == 0 else place,
            dst_ref=place,
            send_sem=self.side_send.at[k],
            recv_sem=self.side_recv.at[k],
            device_id={"section": 1 - self.s},
            device_id_type=MESH,
        )

    def start(self):
        for k in self.stages[0]:
            self.far(k, self.d).start()
        self.side(0, self.s).start()
        self.own().start()

    def step(self, i):
        for k in self.stages[i]:
            self.far(k, self.origin(k)).wait_recv()
            self.side(k, self.s).start()
        if i + 1 < len(self.stages):
            for k in self.stages[i + 1]:
                self.far(k, self.d).start()

    def finish(self):
        self.own().wait()
        for k in range(self.replicas):
            self.side(k, 1 - self.s).wait_recv()
        for k in range(1, self.replicas):
            self.far(k, self.d).wait_send()
        for k in range(self.replicas):
            self.side(k, self.s).wait_send()


class ZGather:
    def __init__(self, src, got, sems):
        self.src, self.got = src, got
        self.own_sem, self.send, self.recv = sems
        self.replicas = got.shape[0]
        self.d = lax.axis_index("dp")

    def own(self):
        return pltpu.make_async_copy(self.src, self.got.at[self.d], self.own_sem.at[0])

    def far(self, k, origin):
        return far_copy(
            self.src,
            self.got.at[origin],
            self.send.at[k - 1],
            self.recv.at[k - 1],
            {"dp": lax.rem(self.d + k, self.replicas)},
        )

    def start(self):
        for k in range(1, self.replicas):
            self.far(k, self.d).start()
        self.own().start()

    def step(self, i):
        pass

    def finish(self):
        self.own().wait()
        for k in range(1, self.replicas):
            self.far(k, lax.rem(self.d + self.replicas - k, self.replicas)).wait_recv()
        for k in range(1, self.replicas):
            self.far(k, self.d).wait_send()


class YJoin:
    def __init__(self, got, dst, by_columns, sems):
        self.src, self.dst, self.by_columns = got, dst, by_columns
        self.own_sem, self.send, self.recv, self.got, self.in_sem = sems
        self.replicas, self.rows, self.cols = got.shape
        self.s = lax.axis_index("section")

    def place(self, half, z):
        rows, cols = self.rows, self.cols
        if self.by_columns:
            return self.dst.at[
                pl.ds(pl.multiple_of(half * rows, rows), rows), pl.ds(z * cols, cols)
            ]
        return self.dst.at[pl.ds(pl.multiple_of((2 * z + half) * rows, rows), rows)]

    def own(self, z):
        return pltpu.make_async_copy(self.got.at[z], self.place(self.s, z), self.own_sem.at[z])

    def side(self, z, half):
        return far_copy(
            self.got.at[z],
            self.place(half, z),
            self.send.at[z],
            self.recv.at[z],
            {"section": 1 - self.s},
        )

    def start(self):
        load = pltpu.make_async_copy(self.src, self.got, self.in_sem.at[0])
        load.start()
        load.wait()
        for z in range(self.replicas):
            self.side(z, self.s).start()
            self.own(z).start()

    def step(self, i):
        pass

    def finish(self):
        for z in range(self.replicas):
            self.own(z).wait()
            self.side(z, 1 - self.s).wait_recv()
        for z in range(self.replicas):
            self.side(z, self.s).wait_send()


def rider_sems(replicas):
    far, side = DMA((replicas - 1,)), DMA((replicas,))
    return [DMA((1,)), far, far, side, side]


class Riders:
    def __init__(self, srcs, dsts, columns, sems):
        self.all = []
        for src, dst, (kind, layer, by) in zip(srcs, dsts, columns):
            count = 3 if kind == "z" else 5
            own, sems = sems[:count], sems[count:]
            if kind == "spread":
                self.all.append(Spread(src.at[layer], dst, by, own))
            elif kind == "z":
                self.all.append(ZGather(src.at[layer], dst, own))
            else:
                self.all.append(YJoin(src, dst, by, own))
        self.replicas = self.all[0].replicas if self.all else 0

    def start(self):
        for one in self.all:
            one.start()

    def step(self, j, n):
        if not self.all:
            return
        stages = self.replicas // 2
        for i in range(stages):

            @pl.when(j == n * (i + 1) // stages - 1)
            def _(i=i):
                for one in self.all:
                    one.step(i)

    def finish(self):
        for one in self.all:
            one.finish()


def riding(riders, replicas):
    arrays = [array for array, _, _, _ in riders]
    columns = tuple(rider[1:] for rider in riders)
    outs, sems = [], []
    for array, kind, _, by in riders:
        rows, cols = array.shape[1:]
        if kind == "z":
            outs.append(shape((replicas, rows, cols), BF))
        else:
            outs.append(
                shape((2 * rows, replicas * cols) if by else (2 * replicas * rows, cols), BF)
            )
        far, side = DMA((replicas - 1,)), DMA((replicas,))
        sems += {
            "spread": rider_sems(replicas),
            "z": [DMA((1,)), far, far],
            "y": [side, side, side, pltpu.VMEM(array.shape, BF), DMA((1,))],
        }[kind]
    return arrays, columns, outs, sems


def params(key):
    return pltpu.CompilerParams(
        vmem_limit_bytes=LIMIT, collective_id=key, has_side_effects=True
    )


def cost(flops, moved, exps=0):
    return pl.CostEstimate(flops=int(flops), bytes_accessed=int(moved), transcendentals=int(exps))


def normed(source):
    center = source - jnp.mean(source, axis=-1, keepdims=True)
    r = lax.rsqrt(jnp.mean(center * center, axis=-1, keepdims=True) + 1e-05)
    return center * r, r


def normed_back(source, gain, grad):
    n, r = normed(source)
    e = grad * gain
    dh = r * (
        e - jnp.mean(e, axis=-1, keepdims=True) - n * jnp.mean(e * n, axis=-1, keepdims=True)
    )
    return dh, jnp.sum(grad * n, axis=0, keepdims=True)


def flat(value):
    return value.reshape((value.shape[0] * value.shape[1],) + value.shape[2:])


def run(n, body):
    def one(j, carry):
        body(j)
        return carry

    lax.fori_loop(0, n, one, 0)


def first_kernel(
    size, replicas, x_ref, gain_ref, wq_ref, wo_ref, wu_ref, wd_ref,
    qkv_ref, gains_out, a1_out, wq_out, wo_out, q_stage, o_stage, u_stage, d_stage,
    a1, w, gains, own_sem, q_sem, o_sem, u_sem, d_sem, gain_sem, *sems
):
    rows, width = x_ref.shape
    n = chunks(rows)
    rc = rows // n
    g = Group(size)
    section = lax.axis_index("section")
    gather = Gather(g, a1, rc, sems[:4])
    swaps = [
        Swap(wq_ref, q_stage, q_sem),
        Swap(wo_ref, o_stage, o_sem),
        Swap(wu_ref, u_stage, u_sem),
        Swap(wd_ref, d_stage, d_sem),
    ]
    spreads = [
        Spread(q_stage.at[0], w, False, sems[4:9]),
        Spread(o_stage.at[0], wo_out, True, sems[9:14]),
    ]
    riders = Riders([], [], (), [])
    riders.all = spreads
    riders.replicas = replicas
    g.greet(replicas)

    def gain_copy(layer):
        return far_copy(
            gain_ref, gains.at[layer], gain_sem.at[0], gain_sem.at[1], {"section": 1 - section}
        )

    gain_copy(section).start()
    swaps[0].start()
    swaps[1].start()
    gains[section] = gain_ref[...]
    gain_copy(1 - section).wait_recv()
    gains_out[...] = gains[...]

    def send(j):
        at = span(j, rc)
        a = normed(x_ref[at, :].astype(F32))[0] * gains[0, 0:1, :]
        a1[g.me, at, :] = a.astype(BF)
        gather.start(j)

    run(n, send)
    swaps[0].arrive()
    swaps[1].arrive()
    riders.start()
    swaps[2].start()
    swaps[3].start()

    def relay(j):
        gather.relay(j)
        riders.step(j, n)

    run(n, relay)
    riders.finish()
    outs = [
        pltpu.make_async_copy(w, wq_out, own_sem.at[0]),
        pltpu.make_async_copy(a1, a1_out, own_sem.at[1]),
    ]
    outs[0].start()

    def multiply(j):
        at = span(j, rc)
        gather.ready(j)
        r = dg(flat(a1[:, at, :]), w[...], NN).astype(BF)
        qkv_ref[:, at, :] = r.reshape(size, rc, r.shape[1])

    run(n, multiply)
    outs[1].start()
    swaps[2].arrive()
    swaps[3].arrive()
    for swap in swaps:
        swap.finish()
    gain_copy(section).wait_send()
    gather.drain(n)
    for out in outs:
        out.wait()


def first_forward(size, replicas, x, gains, ws):
    rows, width = x.shape
    wide = ws[0].shape[2]
    deep = 2 * ws[1].shape[1]
    n = chunks(rows)
    return pl.pallas_call(
        functools.partial(first_kernel, size, replicas),
        out_shape=[
            shape((size, rows, wide), BF),
            shape((2,) + gains.shape, F32),
            shape((size, rows, width), BF),
            shape((width, wide), BF),
            shape((deep, width), BF),
        ]
        + [shape(w.shape, BF) for w in ws],
        in_specs=[VM] * 6,
        out_specs=[VM, VM] + [HB] * 7,
        scratch_shapes=[
            pltpu.VMEM((size, rows, width), BF),
            pltpu.VMEM((width, wide), BF),
            pltpu.VMEM((2,) + gains.shape, F32),
            DMA((2,)),
            DMA((3,)),
            DMA((3,)),
            DMA((3,)),
            DMA((3,)),
            DMA((2,)),
        ]
        + comm_sems(size, n)
        + rider_sems(replicas) * 2,
        compiler_params=params(0),
        cost_estimate=cost(30e9, 30e6),
    )(x, gains, *ws)


def qkv_kernel(size, layer, columns, *refs):
    m = len(columns)
    x_ref, gain_ref, w_ref = refs[:3]
    halves, refs = refs[3 : 3 + m], refs[3 + m :]
    qkv_ref, a1_out = refs[:2]
    wholes, refs = refs[2 : 2 + m], refs[2 + m :]
    a1, w, w_sem, out_sem = refs[:4]
    sems, refs = refs[4:8], refs[8:]
    riders = Riders(halves, wholes, columns, refs)
    rows, width = x_ref.shape
    n = chunks(rows)
    rc = rows // n
    g = Group(size)
    copy = pltpu.make_async_copy(w_ref, w, w_sem.at[0])
    copy.start()
    g.greet(riders.replicas)
    gather = Gather(g, a1, rc, sems)
    riders.start()

    def send(j):
        at = span(j, rc)
        a = normed(x_ref[at, :].astype(F32))[0] * gain_ref[layer, 0:1, :]
        a1[g.me, at, :] = a.astype(BF)
        gather.start(j)

    run(n, send)
    copy.wait()

    def work(j):
        at = span(j, rc)
        gather.relay(j)
        gather.ready(j)
        r = dg(flat(a1[:, at, :]), w[...], NN).astype(BF)
        qkv_ref[:, at, :] = r.reshape(size, rc, r.shape[1])
        riders.step(j, n)

    run(n, work)
    out = pltpu.make_async_copy(a1, a1_out, out_sem.at[0])
    out.start()
    riders.finish()
    gather.drain(n)
    out.wait()


def qkv_forward(size, replicas, layer, x, gains, w, riders):
    rows, width = x.shape
    wide = w.shape[1]
    n = chunks(rows)
    halves, columns, outs, sems = riding(riders, replicas)
    return pl.pallas_call(
        functools.partial(qkv_kernel, size, layer, columns),
        out_shape=[
            shape((size, rows, wide), BF),
            shape((size, rows, width), BF),
        ]
        + outs,
        in_specs=[VM, VM, HB] + [HB] * len(riders),
        out_specs=[VM, HB] + [HB] * len(outs),
        scratch_shapes=[
            pltpu.VMEM((size, rows, width), BF),
            pltpu.VMEM((width, wide), BF),
            DMA((1,)),
            DMA((1,)),
        ]
        + comm_sems(size, n)
        + sems,
        compiler_params=params(layer),
        cost_estimate=cost(20e9, 30e6),
    )(x, gains, w, *halves)


def attend_kernel(size, layer, columns, *refs):
    m = len(columns)
    qkv_ref, qm_ref, km_ref, x_ref, w_ref = refs[:5]
    refs = refs[5:]
    if layer == 1:
        cot_ref, refs = refs[0], refs[1:]
    halves, refs = refs[:m], refs[m:]
    h1_ref, ctx_ref, lse_ref = refs[:3]
    refs = refs[3:]
    if layer == 1:
        cot_out, refs = refs[0], refs[1:]
    wholes, refs = refs[:m], refs[m:]
    ka, vt, w, w_sem = refs[:4]
    scratch, refs = refs[4:13], refs[13:]
    if layer == 1:
        cot_sems, cot_sem, refs = refs[:4], refs[4], refs[5:]
    riders = Riders(halves, wholes, columns, refs)
    _, rows, wide = qkv_ref.shape
    length = size * rows
    e = qm_ref.shape[2]
    heads = wide // (3 * e)
    c = e**-0.5 * math.log2(math.e)
    n = chunks(rows)
    rc = rows // n
    bq = size * rc
    kc = bq
    g = Group(size)
    copy = pltpu.make_async_copy(w_ref, w, w_sem.at[0])
    copy.start()
    g.greet(riders.replicas)
    riders.start()
    if layer == 1:
        cot = Gather(g, cot_out, rows, cot_sems)
        own = pltpu.make_async_copy(cot_ref, cot_out.at[g.me], cot_sem.at[0])
        own.start()
        cot.start(0, cot_ref)
    scatter = Scatter(g, rc, scratch)
    whole = flat(qkv_ref[...])
    for h in range(heads):
        o = 3 * e * h
        ka[h, :, :e] = whole[:, o + e : o + 2 * e]
        ka[h, :, e:] = flat(km_ref[...])
        vt[h, :e, :] = whole[:, o + 2 * e : o + 3 * e].T
        vt[h, e:, :] = jnp.ones((16, length), BF)
    copy.wait()

    def work(j):
        at = span(j, rc)
        qm = flat(qm_ref[:, at, :])
        found = []
        held_qkv = flat(qkv_ref[:, at, :])
        for h in range(heads):
            o = 3 * e * h
            q = jnp.concatenate([held_qkv[:, o : o + e], qm], axis=1)
            held = []
            top = None
            for k in range(length // kc):
                s = dg(ka[h, k * kc : (k + 1) * kc, :], q, NT)
                t = jnp.max(s, axis=0, keepdims=True)
                top = t if top is None else jnp.maximum(top, t)
                held.append(s)
            top = top * c
            acc = None
            for k in range(length // kc):
                p = jnp.exp2(held[k] * c - top).astype(BF)
                a = dg(vt[h, :, k * kc : (k + 1) * kc], p, NN)
                acc = a if acc is None else acc + a
            total = acc[e : e + 1]
            found.append((acc[:e] * (1.0 / total)).astype(BF))
            lse_ref[j, h : h + 1, :] = top + jnp.log2(total)
        ctx = (jnp.concatenate(found, axis=0) if heads > 1 else found[0]).T
        ctx_ref[:, at, :] = ctx.reshape(size, rc, heads * e)
        width = x_ref.shape[1]
        scatter.part[:, at, :] = dg(ctx, w[...], NN).reshape(size, rc, width)
        scatter.first(j)
        scatter.second(j)
        riders.step(j, n)
        if layer == 1:

            @pl.when(j == n - 1)
            def _():
                cot.relay(0)

    run(n, work)

    def last(j):
        at = span(j, rc)
        h1_ref[at, :] = x_ref[at, :].astype(F32) + scatter.third(j)

    run(n, last)
    scatter.drain(n)
    if layer == 1:
        cot.ready(0)
        cot.drain(1)
        own.wait()
    riders.finish()


def attend(size, replicas, layer, qkv, qm, km, x, w, riders, cot=()):
    _, rows, wide = qkv.shape
    e = qm.shape[2]
    heads = wide // (3 * e)
    width = x.shape[1]
    n = chunks(rows)
    halves, columns, outs, sems = riding(riders, replicas)
    return pl.pallas_call(
        functools.partial(attend_kernel, size, layer, columns),
        out_shape=[
            shape((rows, width), F32),
            shape((size, rows, heads * e), BF),
            shape((n, heads, size * rows // n), F32),
        ]
        + [shape((size, rows, width), BF) for _ in cot]
        + outs,
        in_specs=[VM, VM, VM, VM, HB] + [VM] * len(cot) + [HB] * len(riders),
        out_specs=[VM, VM, VM] + [HB] * (len(cot) + len(outs)),
        scratch_shapes=[
            pltpu.VMEM((heads, size * rows, 2 * e), BF),
            pltpu.VMEM((heads, e + 16, size * rows), BF),
            pltpu.VMEM((heads * e, width), BF),
            DMA((1,)),
        ]
        + scatter_scratch(size, rows, width, n)
        + (comm_sems(size, 1) + [DMA((1,))]) * len(cot)
        + sems,
        compiler_params=params(2 + layer),
        cost_estimate=cost(60e9, 20e6),
    )(qkv, qm, km, x, w, *cot, *halves)


def mlp_kernel(size, layer, columns, *refs):
    m = len(columns)
    h1_ref, gain_ref, wu_ref, wd_ref = refs[:4]
    halves, refs = refs[4 : 4 + m], refs[4 + m :]
    y_ref, a2_out, hid_out, slope_out = refs[:4]
    wholes, refs = refs[4 : 4 + m], refs[4 + m :]
    a2, hid, slope, wu, wd, w_sem, out_sem = refs[:7]
    scratch, refs = refs[7:20], refs[20:]
    riders = Riders(halves, wholes, columns, refs)
    rows, width = h1_ref.shape
    hidden = wu_ref.shape[1]
    fb = min(256, hidden)
    n = chunks(rows)
    rc = rows // n
    g = Group(size)
    copies = [
        pltpu.make_async_copy(wu_ref, wu, w_sem.at[0]),
        pltpu.make_async_copy(wd_ref, wd, w_sem.at[1]),
    ]
    for copy in copies:
        copy.start()
    g.greet(riders.replicas)
    gather = Gather(g, a2, rc, scratch[:4])
    scatter = Scatter(g, rc, scratch[4:])

    def send(j):
        at = span(j, rc)
        a = normed(h1_ref[at, :])[0] * gain_ref[layer, 1:2, :]
        a2[g.me, at, :] = a.astype(BF)
        gather.start(j)

    run(n, send)
    riders.start()
    for copy in copies:
        copy.wait()

    def work(j):
        at = span(j, rc)
        gather.relay(j)
        gather.ready(j)
        a = flat(a2[:, at, :])
        for f in range(hidden // fb):
            cols = slice(f * fb, (f + 1) * fb)
            u = dg(a, wu[:, cols], NN)
            half = 0.5 + 0.5 * lax.erf(u * (0.5**0.5))
            slope[:, at, cols] = (
                (half + u * jnp.exp(-0.5 * u * u) * ((2 * math.pi) ** -0.5))
                .astype(BF)
                .reshape(size, rc, fb)
            )
            hid[:, at, cols] = (u * half).astype(BF).reshape(size, rc, fb)
        held = flat(hid[:, at, :])
        for f in range(width // 256):
            cols = slice(f * 256, (f + 1) * 256)
            scatter.part[:, at, cols] = dg(held, wd[:, cols], NN).reshape(size, rc, 256)
        scatter.first(j)
        scatter.second(j)
        riders.step(j, n)

    run(n, work)
    outs = [
        pltpu.make_async_copy(a2, a2_out, out_sem.at[0]),
        pltpu.make_async_copy(hid, hid_out, out_sem.at[1]),
        pltpu.make_async_copy(slope, slope_out, out_sem.at[2]),
    ]
    for out in outs:
        out.start()

    def last(j):
        at = span(j, rc)
        y_ref[at, :] = (h1_ref[at, :] + scatter.third(j)).astype(BF)

    run(n, last)
    riders.finish()
    gather.drain(n)
    scatter.drain(n)
    for out in outs:
        out.wait()


def mlp_forward(size, replicas, layer, h1, gains, wu, wd, riders):
    rows, width = h1.shape
    hidden = wu.shape[1]
    n = chunks(rows)
    halves, columns, outs, sems = riding(riders, replicas)
    return pl.pallas_call(
        functools.partial(mlp_kernel, size, layer, columns),
        out_shape=[
            shape((rows, width), BF),
            shape((size, rows, width), BF),
            shape((size, rows, hidden), BF),
            shape((size, rows, hidden), BF),
        ]
        + outs,
        in_specs=[VM, VM, HB, HB] + [HB] * len(riders),
        out_specs=[VM, HB, HB, HB] + [HB] * len(outs),
        scratch_shapes=[
            pltpu.VMEM((size, rows, width), BF),
            pltpu.VMEM((size, rows, hidden), BF),
            pltpu.VMEM((size, rows, hidden), BF),
            pltpu.VMEM((width, hidden), BF),
            pltpu.VMEM((hidden, width), BF),
            DMA((2,)),
            DMA((3,)),
        ]
        + comm_sems(size, n)
        + scatter_scratch(size, rows, width, n)
        + sems,
        compiler_params=params(4 + layer),
        cost_estimate=cost(50e9, 30e6),
    )(h1, gains, wu, wd, *halves)


def mlp_back_kernel(size, layer, parts, *refs):
    g_ref, h1_ref, gain_ref, a2_ref, hid_ref, slope_ref, wu_ref, wd_ref = refs[:8]
    refs = refs[8:]
    if layer == 1:
        ys, whole_ref, refs = refs[:2], refs[2], refs[3:]
    mid_ref, gain_out, gup_ref, gdown_ref = refs[:4]
    refs = refs[4:]
    if layer == 1:
        y_out, refs = refs[0], refs[1:]
    grad, a2, hid, dup, wu, wd, w_sem = refs[:7]
    scratch, refs = refs[7:20], refs[20:]
    rows, width = h1_ref.shape
    hidden = wu_ref.shape[1]
    depth = width // parts
    fb = min(256, hidden)
    n = chunks(rows)
    rc = rows // n
    g = Group(size)
    copies = [
        pltpu.make_async_copy(wd_ref, wd, w_sem.at[0]),
        pltpu.make_async_copy(slope_ref, dup, w_sem.at[1]),
        pltpu.make_async_copy(wu_ref, wu, w_sem.at[2]),
    ]
    late = [
        pltpu.make_async_copy(hid_ref, hid, w_sem.at[3]),
        pltpu.make_async_copy(a2_ref, a2, w_sem.at[4]),
    ]
    for copy in copies + late:
        copy.start()
    g.greet(side=layer == 1)
    section = lax.axis_index("section")
    if layer == 1:
        y_sem, y_own = refs

        def y_load(own):
            return pltpu.make_async_copy(own, y_own, y_sem.at[3])

        def y_copies(own, other, at):
            return (
                pltpu.make_async_copy(y_own, y_out.at[section], y_sem.at[0]),
                far_copy(
                    other, y_out.at[at], y_sem.at[1], y_sem.at[2], {"section": 1 - section}
                ),
            )

        for i in range(2):

            @pl.when(section == i)
            def _(i=i):
                y_load(ys[i]).start()
                y_copies(ys[i], ys[1 - i], section)[1].start()

    gather = Gather(g, grad, rc, scratch[:4])
    scatter = Scatter(g, rc, scratch[4:])

    def send(j):
        at = span(j, rc)
        grad[g.me, at, :] = g_ref[at, :]
        gather.start(j)

    if layer == 1:
        whole = pltpu.make_async_copy(whole_ref, grad, w_sem.at[5])
        whole.start()
        copies.append(whole)
    else:
        run(n, send)
    for copy in copies:
        copy.wait()
    if layer == 1:
        y_load(ys[0]).wait()
        y_copies(ys[0], ys[1], section)[0].start()

    def work(j):
        at = span(j, rc)
        if layer == 0:
            gather.relay(j)
            gather.ready(j)
        held = flat(grad[:, at, :])
        for f in range(hidden // fb):
            cols = slice(f * fb, (f + 1) * fb)
            d = dg(held, wd[cols, :], NT) * flat(dup[:, at, cols]).astype(F32)
            dup[:, at, cols] = d.astype(BF).reshape(size, rc, fb)
        held = flat(dup[:, at, :])
        for z in range(parts):
            cols = slice(z * depth, (z + 1) * depth)
            scatter.part[:, at, cols] = dg(held, wu[cols, :], NT).reshape(size, rc, depth)
        scatter.first(j)
        scatter.second(j)

    run(n, work)
    for copy in late:
        copy.wait()

    def up_grad(z):
        cols = pl.ds(pl.multiple_of(z * depth, depth), depth)
        gup_ref[z] = dg(flat(a2[:, :, cols]), flat(dup[...]), TN).astype(BF)

    run(parts, up_grad)

    def down_grad(f):
        cols = pl.ds(pl.multiple_of(f * fb, fb), fb)
        r = dg(flat(hid[:, :, cols]), flat(grad[...]), TN).astype(BF)
        for z in range(parts):
            gdown_ref[z, cols, :] = r[:, z * depth : (z + 1) * depth]

    run(hidden // fb, down_grad)
    gain_out[...] = jnp.zeros_like(gain_out)

    def last(j):
        at = span(j, rc)
        dh, dgain = normed_back(h1_ref[at, :], gain_ref[layer, 1:2, :], scatter.third(j))
        mid_ref[at, :] = g_ref[at, :].astype(F32) + dh
        gain_out[...] += dgain

    run(n, last)
    if layer == 1:
        local, side = y_copies(ys[0], ys[1], 1 - section)
        local.wait()
        side.wait_recv()
        y_copies(ys[0], ys[1], section)[1].wait_send()
    if layer == 0:
        gather.drain(n)
    scatter.drain(n)


def mlp_backward(size, replicas, layer, grad, h1, gains, a2, hid, slope, wu, wd, extra):
    rows, width = h1.shape
    hidden = wu.shape[1]
    parts, depth = replicas, width // replicas
    n = chunks(rows)
    return pl.pallas_call(
        functools.partial(mlp_back_kernel, size, layer, parts),
        out_shape=[
            shape((rows, width), F32),
            shape((1, width), F32),
            shape((parts, depth, hidden), BF),
            shape((parts, hidden, depth), BF),
        ]
        + [shape((2, rows, width), BF)] * (len(extra) // 3),
        in_specs=[VM, VM, VM] + [HB] * (5 + len(extra)),
        out_specs=[VM, VM, VM, VM] + [HB] * (len(extra) // 3),
        scratch_shapes=[
            pltpu.VMEM((size, rows, width), BF),
            pltpu.VMEM((size, rows, width), BF),
            pltpu.VMEM((size, rows, hidden), BF),
            pltpu.VMEM((size, rows, hidden), BF),
            pltpu.VMEM((width, hidden), BF),
            pltpu.VMEM((hidden, width), BF),
            DMA((6,)),
        ]
        + comm_sems(size, n)
        + scatter_scratch(size, rows, width, n)
        + [DMA((4,)), pltpu.VMEM((rows, width), BF)] * (len(extra) // 3),
        compiler_params=params(6 + layer),
        cost_estimate=cost(60e9, 40e6),
    )(grad, h1, gains, a2, hid, slope, wu, wd, *extra)


def attend_back_kernel(size, layer, parts, *refs):
    mid_ref, qkv_ref, qm_ref, km_ref, ctx_ref, lse_ref, w_ref = refs[:7]
    refs = refs[7:]
    if layer == 0:
        gdown_ref, refs = refs[0], refs[1:]
    dqkv_ref, gout_ref, refs = refs[0], refs[1], refs[2:]
    if layer == 0:
        down_out, refs = refs[0], refs[1:]
    da, ka, va, kt, dk, dv, w, w_sem = refs[:8]
    sems, refs = refs[8:12], refs[12:]
    reduce = Reduce(layer, refs[:9])
    if layer == 0:
        down = HalfReduce(layer, refs[9 : 9 + HALF])
        down_swap = HalfSwap(gdown_ref, down.other, refs[9 + HALF])
    _, rows, wide = qkv_ref.shape
    length = size * rows
    e = qm_ref.shape[2]
    heads = wide // (3 * e)
    scale = e**-0.5
    c = scale * math.log2(math.e)
    depth = w_ref.shape[1] // parts
    n = chunks(rows)
    rc = rows // n
    bq = size * rc
    kc = bq
    g = Group(size)
    copies = [pltpu.make_async_copy(w_ref, w, w_sem.at[0])]
    for copy in copies:
        copy.start()
    g.greet(parts)
    gather = Gather(g, da, rc, sems)
    loads = []
    if layer == 0:
        down_swap.copy().start()
        loads = down.loads(gdown_ref, None)
        for load in loads:
            load.start()

    def send(j):
        at = span(j, rc)
        da[g.me, at, :] = mid_ref[at, :].astype(BF)
        gather.start(j)

    run(n, send)
    lane = lax.broadcasted_iota(jnp.int32, (length, e), 1)
    whole = flat(qkv_ref[...])
    for h in range(heads):
        o = 3 * e * h
        ka[h, :, :e] = whole[:, o + e : o + 2 * e]
        ka[h, :, e:] = flat(km_ref[...])
        va[h, :, :e] = whole[:, o + 2 * e : o + 3 * e]
        va[h, :, e:] = jnp.where(lane < 3, 1.0, 0.0).astype(BF)
        kt[h] = whole[:, o + e : o + 2 * e].T
    dk[...] = jnp.zeros_like(dk)
    dv[...] = jnp.zeros_like(dv)
    ql = lax.broadcasted_iota(jnp.int32, (bq, e), 1)
    for copy in copies + loads:
        copy.wait()

    def out_grad(z):
        cols = pl.ds(pl.multiple_of(z * depth, depth), depth)
        return dg(flat(ctx_ref[...]), flat(da[:, :, cols]), TN)

    def work(j):
        at = span(j, rc)

        @pl.when(j == 0)
        def _():
            gather.relay(0)
            gather.ready(0)

        @pl.when(j == min(1, n - 1))
        def _():
            for i in range(1, n):
                gather.relay(i)
            for i in range(1, n):
                gather.ready(i)
            reduce.send(out_grad)

        qm = flat(qm_ref[:, at, :])
        dctx = dg(flat(da[:, at, :]), w[...], NT).astype(BF)
        ctx = flat(ctx_ref[:, at, :])
        held_qkv = flat(qkv_ref[:, at, :])
        for h in range(heads):
            o = 3 * e * h
            qq = held_qkv[:, o : o + e]
            q = jnp.concatenate([qq, qm], axis=1)
            dc = dctx[:, h * e : (h + 1) * e]
            prod = dc.astype(F32) * ctx[:, h * e : (h + 1) * e].astype(F32)
            d = -jnp.sum(prod, axis=1, keepdims=True)
            d1 = d.astype(BF).astype(F32)
            d2 = (d - d1).astype(BF).astype(F32)
            d3 = d - d1 - d2
            ds_col = jnp.where(ql == 0, d1, jnp.where(ql == 1, d2, jnp.where(ql == 2, d3, 0.0)))
            dca = jnp.concatenate([dc, ds_col.astype(BF)], axis=1)
            lse = lse_ref[j, h : h + 1, :]
            dqt = None
            for k in range(length // kc):
                ks = slice(k * kc, (k + 1) * kc)
                s = dg(ka[h, ks, :], q, NT)
                p = jnp.exp2(s * c - lse)
                ds = (p * dg(va[h, ks, :], dca, NT)).astype(BF)
                dv[h, ks, :] += dg(p.astype(BF), dc, NN)
                dk[h, ks, :] += dg(ds, qq, NN)
                a = dg(kt[h, :, ks], ds, NN)
                dqt = a if dqt is None else dqt + a
            if layer == 0 and h == heads // 2:

                @pl.when(j == min(1, n - 1))
                def _():
                    down_swap.copy().wait_recv()
                    down.middle()

            if layer == 0 and h == heads - 1:

                @pl.when(j == n - 1)
                def _():
                    down.late()

            dqkv_ref[:, at, o : o + e] = (dqt * scale).T.astype(BF).reshape(size, rc, e)

    run(n, work)
    for h in range(heads):
        o = 3 * e * h
        dqkv_ref[:, :, o + e : o + 2 * e] = (dk[h] * scale).astype(BF).reshape(size, rows, e)
        dqkv_ref[:, :, o + 2 * e : o + 3 * e] = dv[h].astype(BF).reshape(size, rows, e)

    reduce.collect()
    reduce.finish(gout_ref)
    if layer == 0:
        down.finish(down_out)
        down_swap.copy().wait_send()
    gather.drain(n)


def attend_backward(size, replicas, layer, mid, qkv, qm, km, ctx, lse, w, grads):
    _, rows, wide = qkv.shape
    e = qm.shape[2]
    heads = wide // (3 * e)
    width = mid.shape[1]
    parts, depth = replicas, width // replicas
    length = size * rows
    n = chunks(rows)
    return pl.pallas_call(
        functools.partial(attend_back_kernel, size, layer, parts),
        out_shape=[shape(qkv.shape, BF), shape((heads * e, depth), F32)]
        + [shape(grad.shape[1:], F32) for grad in grads],
        in_specs=[VM] * 6 + [HB] * (1 + len(grads)),
        out_specs=[VM, VM] + [VM] * len(grads),
        scratch_shapes=[
            pltpu.VMEM((size, rows, width), BF),
            pltpu.VMEM((heads, length, 2 * e), BF),
            pltpu.VMEM((heads, length, 2 * e), BF),
            pltpu.VMEM((heads, e, length), BF),
            pltpu.VMEM((heads, length, e), F32),
            pltpu.VMEM((heads, length, e), F32),
            pltpu.VMEM((heads * e, width), BF),
            DMA((1,)),
        ]
        + comm_sems(size, n)
        + reduce_scratch(parts, heads * e, depth)
        + sum([half_scratch(parts, *grad.shape[1:]) + [DMA((2,))] for grad in grads], []),
        compiler_params=params(8 + layer),
        cost_estimate=cost(90e9, 40e6),
    )(mid, qkv, qm, km, ctx, lse, w, *grads)


def qkv_back_kernel(
    size, layer, parts, dqkv_ref, a1_ref, x_ref, mid_ref, gain_ref, w_ref,
    dx_ref, gain_out, gqkv_ref, w, w_sem, *scratch
):
    rows, width = x_ref.shape
    depth = width // parts
    n = chunks(rows)
    rc = rows // n
    g = Group(size)
    copies = [pltpu.make_async_copy(w_ref, w, w_sem.at[0])]
    for copy in copies:
        copy.start()
    g.greet()
    scatter = Scatter(g, rc, scratch)
    for copy in copies:
        copy.wait()

    def work(j):
        at = span(j, rc)
        held = flat(dqkv_ref[:, at, :])
        for z in range(parts):
            cols = slice(z * depth, (z + 1) * depth)
            scatter.part[:, at, cols] = dg(held, w[cols, :], NT).reshape(size, rc, depth)
        scatter.first(j)
        scatter.second(j)

    run(n, work)

    def qkv_grad(z):
        cols = pl.ds(pl.multiple_of(z * depth, depth), depth)
        gqkv_ref[z] = dg(flat(a1_ref[:, :, cols]), flat(dqkv_ref[...]), TN).astype(BF)

    run(parts, qkv_grad)
    gain_out[...] = jnp.zeros_like(gain_out)

    def last(j):
        at = span(j, rc)
        dh, dgain = normed_back(
            x_ref[at, :].astype(F32), gain_ref[layer, 0:1, :], scatter.third(j)
        )
        dx_ref[at, :] = (mid_ref[at, :] + dh).astype(BF)
        gain_out[...] += dgain

    run(n, last)
    scatter.drain(n)


def qkv_backward(size, replicas, layer, dqkv, a1, x, mid, gains, w):
    rows, width = x.shape
    wide = w.shape[1]
    parts, depth = replicas, width // replicas
    n = chunks(rows)
    return pl.pallas_call(
        functools.partial(qkv_back_kernel, size, layer, parts),
        out_shape=(
            shape((rows, width), BF),
            shape((1, width), F32),
            shape((parts, depth, wide), BF),
        ),
        in_specs=[VM] * 5 + [HB],
        out_specs=(VM, VM, VM),
        scratch_shapes=[
            pltpu.VMEM((width, wide), BF),
            DMA((1,)),
        ]
        + scatter_scratch(size, rows, width, n),
        compiler_params=params(11),
        cost_estimate=cost(30e9, 30e6),
    )(dqkv, a1, x, mid, gains, w)


def last_kernel(
    size, parts, dqkv_ref, a1_ref, x_ref, mid_ref, gain_ref, w_ref, two_ref, above_ref, dx1_ref,
    gain_out, gqkv_out, dx_out,
    gqkv, swap_sem, w, dx, gsum, gcame, w_sem, x_sem, x_send, x_recv, g_send, g_recv, *scratch
):
    rows, width = x_ref.shape
    depth = width // parts
    n = chunks(rows)
    rc = rows // n
    g = Group(size)
    section = lax.axis_index("section")
    d = lax.axis_index("dp")
    copy = pltpu.make_async_copy(w_ref, w, w_sem.at[0])
    copy.start()
    reduce = HalfReduce(0, scratch[:HALF])
    swap = HalfSwap(gqkv, reduce.other, swap_sem)
    scatter = Scatter(g, rc, scratch[HALF:])
    g.greet(parts)

    def upper():
        return far_copy(
            dx1_ref, dx_out.at[0], x_send.at[n], x_recv.at[n], {"section": 1 - section}
        )

    def keep_upper():
        return pltpu.make_async_copy(dx1_ref, dx_out.at[1], x_sem.at[0])

    def lower(j):
        at = span(j, rc)
        return far_copy(
            dx.at[at], dx_out.at[1, at], x_send.at[j], x_recv.at[j], {"section": 1 - section}
        )

    def keep_lower(j):
        at = span(j, rc)
        return pltpu.make_async_copy(dx.at[at], dx_out.at[0, at], x_sem.at[j])

    def qkv_grad(z):
        cols = pl.ds(pl.multiple_of(z * depth, depth), depth)
        gqkv[z] = dg(flat(a1_ref[:, :, cols]), flat(dqkv_ref[...]), TN).astype(BF)

    run(parts, qkv_grad)
    swap.copy().start()
    load = reduce.loads(gqkv, None)[0]
    load.start()

    @pl.when(section == 1)
    def _():
        keep_upper().start()

    copy.wait()

    def work(j):
        at = span(j, rc)
        held = flat(dqkv_ref[:, at, :])
        for z in range(parts):
            cols = slice(z * depth, (z + 1) * depth)
            scatter.part[:, at, cols] = dg(held, w[cols, :], NT).reshape(size, rc, depth)
        scatter.first(j)
        scatter.second(j)

    run(n, work)
    gsum[0] = jnp.zeros_like(gsum[0])

    def last(j):
        at = span(j, rc)
        dh, dgain = normed_back(x_ref[at, :].astype(F32), gain_ref[0, 0:1, :], scatter.third(j))
        dx[at, :] = (mid_ref[at, :] + dh).astype(BF)

        @pl.when(section == 0)
        def _():
            keep_lower(j).start()

        @pl.when(section == 1)
        def _():
            lower(j).start()

        gsum[0, 0:1, :] += dgain

    def rest(j):
        @pl.when(j == n // 2)
        def _():
            load.wait()
            swap.copy().wait_recv()
            reduce.middle()

            @pl.when(section == 0)
            def _():
                upper().start()

        last(j)

    run(n, rest)
    gsum[0, 1:2, :] = two_ref[...]
    gsum[0, 2:4, :] = above_ref[...]

    targets = [
        [{"tensor": g.sibling}],
        [{"tensor": g.ahead(k) * 2 + g.core} for k in range(1, g.chips)],
        [{"dp": lax.rem(d + k, parts)} for k in range(1, parts)],
        [{"section": 1 - section}],
    ]
    slot = 0
    sent = []

    def exchange(stage):
        nonlocal slot
        copies = []
        for target in targets[stage]:
            copies.append(
                far_copy(gsum.at[stage], gcame.at[slot], g_send.at[slot], g_recv.at[slot], target)
            )
            copies[-1].start()
            slot += 1
        total = gsum[stage]
        for i, copy in enumerate(copies):
            copy.wait_recv()
            total = total + gcame[slot - len(copies) + i]
        gsum[stage + 1] = total
        sent.extend(copies)

    exchange(0)
    exchange(1)
    reduce.late()
    exchange(2)
    exchange(3)
    gain_out[...] = gsum[4]

    @pl.when(section == 0)
    def _():
        for j in range(n):
            lower(j).wait_recv()
            keep_lower(j).wait()
        upper().wait_send()

    @pl.when(section == 1)
    def _():
        keep_upper().wait()
        upper().wait_recv()
        for j in range(n):
            lower(j).wait_send()

    reduce.finish(gqkv_out)
    swap.copy().wait_send()
    for copy in sent:
        copy.wait_send()
    scatter.drain(n)


def last_backward(size, replicas, dqkv, a1, x, mid, gains, w, two, above, dx1):
    rows, width = x.shape
    wide = w.shape[1]
    depth = width // replicas
    n = chunks(rows)
    slots = 1 + (size // 2 - 1) + (replicas - 1) + 1
    return pl.pallas_call(
        functools.partial(last_kernel, size, replicas),
        out_shape=(
            shape((8, width), F32),
            shape((depth, wide), F32),
            shape((2, rows, width), BF),
        ),
        in_specs=[VM] * 5 + [HB, VM, VM, VM],
        out_specs=(VM, VM, HB),
        scratch_shapes=[
            pltpu.VMEM((replicas, depth, wide), BF),
            DMA((2,)),
            pltpu.VMEM((width, wide), BF),
            pltpu.VMEM((rows, width), BF),
            pltpu.VMEM((5, 8, width), F32),
            pltpu.VMEM((slots, 8, width), F32),
            DMA((1,)),
            DMA((n,)),
            DMA((n + 1,)),
            DMA((n + 1,)),
            DMA((slots,)),
            DMA((slots,)),
        ]
        + half_scratch(replicas, depth, wide)
        + scatter_scratch(size, rows, width, n),
        compiler_params=params(10),
        cost_estimate=cost(40e9, 30e6),
    )(dqkv, a1, x, mid, gains, w, two, above, dx1)


def scene_masks(segments, e):
    same = (segments[..., None] == jnp.arange(e, dtype=jnp.int32)).astype(F32)
    used = jnp.arange(e) < SCENES
    return (
        jnp.where(used, same * MASKED, 0.0).astype(BF),
        jnp.where(used, 1.0 - same, 0.0).astype(BF),
    )


def swap_section(value):
    return lax.ppermute(value, "section", [(0, 1), (1, 0)])


def shards(
    block_input,
    segment_ids,
    cotangent,
    norm_one_gain,
    qkv_weight,
    out_weight,
    norm_two_gain,
    up_weight,
    down_weight,
):
    section = lax.axis_index("section")
    size = lax.axis_size("tensor")
    replicas = lax.axis_size("dp")

    mine = [
        qkv_weight[0].reshape((qkv_weight.shape[1], -1)),
        out_weight[0].reshape((-1, out_weight.shape[3])),
        up_weight[0],
        down_weight[0],
    ]
    mine = [w.astype(BF).reshape((2, -1, w.shape[1])) for w in mine]
    gains = jnp.concatenate(
        [norm_one_gain, norm_two_gain, jnp.zeros((6, norm_one_gain.shape[1]), F32)], axis=0
    )
    segments = lax.dynamic_index_in_dim(segment_ids, section, 0, keepdims=False)
    x = lax.dynamic_index_in_dim(block_input, section, 0, keepdims=False)
    head_dim = qkv_weight.shape[3] // 3
    qm, km = scene_masks(segments.reshape((size, -1)), head_dim)
    qkv, gains, a1, w_qkv_0, w_out_0, h_qkv, h_out, h_up, h_down = first_forward(
        size, replicas, x, gains, mine
    )
    h1, ctx, lse, w_up_0, w_down_0 = attend(
        size, replicas, 0, qkv, qm, km, x, w_out_0,
        [(h_up, "spread", 0, False), (h_down, "spread", 0, True)],
    )
    y0, a2, hid, slope, w_qkv_1, w_out_1, got_up = mlp_forward(
        size, replicas, 0, h1, gains, w_up_0, w_down_0,
        [(h_qkv, "spread", 1, False), (h_out, "spread", 1, True), (h_up, "z", 1, False)],
    )
    kept = [(x, a1, qkv, ctx, lse, h1, a2, hid, slope)]
    qkv, a1, got_down = qkv_forward(
        size, replicas, 1, y0, gains, w_qkv_1, [(h_down, "z", 1, True)]
    )
    grad = lax.dynamic_index_in_dim(cotangent, section, 0, keepdims=False)
    h1, ctx, lse, grad_all, w_up_1, w_down_1 = attend(
        size, replicas, 1, qkv, qm, km, y0, w_out_1,
        [(got_up, "y", 1, False), (got_down, "y", 1, True)], [grad],
    )
    y1, a2, hid, slope = mlp_forward(size, replicas, 1, h1, gains, w_up_1, w_down_1, [])
    kept.append((y0, a1, qkv, ctx, lse, h1, a2, hid, slope))
    weights = [
        (w_qkv_0, w_out_0, w_up_0, w_down_0),
        (w_qkv_1, w_out_1, w_up_1, w_down_1),
    ]
    def reduce_rows(value):
        return lax.psum_scatter(value, "dp", scatter_dimension=0, tiled=False)

    x, a1, qkv, ctx, lse, h1, a2, hid, slope = kept[1]
    w_qkv, w_out, w_up, w_down = weights[1]
    mid, gain_two, g_up, g_down, layer_out = mlp_backward(
        size, replicas, 1, grad, h1, gains, a2, hid, slope, w_up, w_down, [y0, y1, grad_all]
    )
    d_qkv, out_1 = attend_backward(size, replicas, 1, mid, qkv, qm, km, ctx, lse, w_out, [])
    up_1, down_1 = reduce_rows(g_up), reduce_rows(g_down)
    dx1, gain_one, g_qkv = qkv_backward(size, replicas, 1, d_qkv, a1, x, mid, gains, w_qkv)
    gains_above = jnp.concatenate([gain_one, gain_two], axis=0)
    dx1, up_1, down_1 = lax.optimization_barrier((dx1, up_1, down_1))
    qkv_1 = reduce_rows(g_qkv)

    x, a1, qkv, ctx, lse, h1, a2, hid, slope = kept[0]
    w_qkv, w_out, w_up, w_down = weights[0]
    mid, gain_two, g_up, g_down = mlp_backward(
        size, replicas, 0, dx1, h1, gains, a2, hid, slope, w_up, w_down, []
    )
    mid, qkv_1 = lax.optimization_barrier((mid, qkv_1))
    d_qkv, out_0, down_0 = attend_backward(
        size, replicas, 0, mid, qkv, qm, km, ctx, lse, w_out, [g_down]
    )
    up_0 = reduce_rows(g_up)
    d_qkv, up_0 = lax.optimization_barrier((d_qkv, up_0))
    gains, qkv_0, input_out = last_backward(
        size, replicas, d_qkv, a1, x, mid, gains, w_qkv, gain_two, gains_above, dx1
    )

    def finish(zero, one):
        send = swap_section(jnp.where(section == 0, one, zero))
        return jnp.where(section == 0, zero, one).astype(F32) + send.astype(F32)

    other_qkv_1 = swap_section(qkv_1)
    qkv_grad = jnp.where(section == 0, qkv_0, qkv_1.astype(F32) + other_qkv_1.astype(F32))
    out_grad = jnp.where(section == 0, out_0, out_1)
    up_grad = finish(up_0, up_1)
    other_down_1 = swap_section(down_1)
    down_grad = jnp.where(section == 0, down_0, down_1.astype(F32) + other_down_1.astype(F32))
    gains = lax.dynamic_slice_in_dim(gains, 2 * section, 2, 0)
    return (
        layer_out[None],
        input_out[None],
        gains[0:1],
        qkv_grad.reshape(qkv_weight.shape),
        out_grad.reshape(out_weight.shape),
        gains[1:2],
        up_grad[None],
        down_grad[None],
    )


def solution(mesh):
    return jax.shard_map(
        shards,
        mesh=mesh,
        in_specs=(
            P(None, ("dp", "tensor"), None),
            P(None, "dp"),
            P(None, ("dp", "tensor"), None),
            P("section", None),
            P("section", "dp", "tensor", None),
            P("section", "tensor", None, "dp"),
            P("section", None),
            P("section", "dp", "tensor"),
            P("section", "tensor", "dp"),
        ),
        out_specs=(
            P("section", None, ("dp", "tensor"), None),
            P("section", None, ("dp", "tensor"), None),
            P("section", None),
            P("section", "dp", "tensor", None),
            P("section", "tensor", None, "dp"),
            P("section", None),
            P("section", "dp", "tensor"),
            P("section", "tensor", "dp"),
        ),
        check_vma=False,
    )
```

```python
import functools
import math

import jax
import jax.numpy as jnp
from jax import lax
from jax.experimental import pallas as pl
from jax.experimental.pallas import tpu as pltpu
from jax.sharding import PartitionSpec as P

F32 = jnp.float32
BF = jnp.bfloat16
NT = (((1,), (1,)), ((), ()))
NN = (((1,), (0,)), ((), ()))
TN = (((0,), (0,)), ((), ()))
MASKED = -1e30
SCENES = 3
MESH = pl.DeviceIdType.MESH
VM = pl.BlockSpec(memory_space=pltpu.VMEM)
HB = pl.BlockSpec(memory_space=pl.ANY)
DMA = pltpu.SemaphoreType.DMA
LIMIT = 58 << 20


def dg(a, b, dims):
    return lax.dot_general(a, b, dims, preferred_element_type=F32)


def chunks(rows):
    return 4 if rows % 64 == 0 else 1


def thin_chunks(rows):
    return 8 if rows % 128 == 0 else chunks(rows)


def shape(dims, dtype):
    return jax.ShapeDtypeStruct(dims, dtype)


class Group:
    def __init__(self, size):
        self.size = size
        self.chips = size // 2
        self.me = lax.axis_index("tensor")
        self.chip = lax.div(self.me, 2)
        self.core = lax.rem(self.me, 2)
        self.sibling = self.chip * 2 + 1 - self.core

    def ahead(self, k):
        return lax.rem(self.chip + k, self.chips)

    def behind(self, k):
        return lax.rem(self.chip + self.chips - k, self.chips)

    def greet(self, replicas=0, side=False):
        barrier = pltpu.get_barrier_semaphore()
        targets = [self.sibling] + [self.ahead(k) * 2 + self.core for k in range(1, self.chips)]
        targets = [{"tensor": target} for target in targets]
        if replicas:
            d = lax.axis_index("dp")
            targets += [{"dp": lax.rem(d + k, replicas)} for k in range(1, replicas)]
        if replicas or side:
            targets += [{"section": 1 - lax.axis_index("section")}]
        for target in targets:
            pl.semaphore_signal(barrier, inc=1, device_id=target, device_id_type=MESH)
        pl.semaphore_wait(barrier, len(targets))


def remote(src, dst, send, recv, target):
    return pltpu.make_async_remote_copy(
        src_ref=src,
        dst_ref=dst,
        send_sem=send,
        recv_sem=recv,
        device_id={"tensor": target},
        device_id_type=MESH,
    )


def span(j, rc):
    return pl.ds(pl.multiple_of(j * rc, rc), rc)


def comm_sems(group_size, n):
    c = group_size // 2
    far, near = DMA((max(c - 1, 1), n)), DMA((c, n))
    return [far, far, near, near]


class Gather:
    def __init__(self, g, buf, rc, sems):
        self.g, self.buf, self.rc = g, buf, rc
        self.far_send, self.far_recv, self.near_send, self.near_recv = sems

    def far(self, k, j, origin, target, src=None):
        ref = self.buf.at[origin, span(j, self.rc)]
        src = ref if src is None else src
        return remote(src, ref, self.far_send.at[k - 1, j], self.far_recv.at[k - 1, j], target)

    def near(self, k, j, origin, src=None):
        ref = self.buf.at[origin, span(j, self.rc)]
        src = ref if src is None else src
        return remote(
            src, ref, self.near_send.at[k, j], self.near_recv.at[k, j], self.g.sibling
        )

    def start(self, j, src=None):
        g = self.g
        for k in range(1, g.chips):
            self.far(k, j, g.me, g.ahead(k) * 2 + g.core, src).start()
        self.near(0, j, g.me, src).start()

    def relay(self, j):
        g = self.g
        for k in range(1, g.chips):
            origin = g.behind(k) * 2 + g.core
            self.far(k, j, origin, g.me).wait_recv()
            self.near(k, j, origin).start()

    def ready(self, j):
        g = self.g
        self.near(0, j, g.sibling).wait_recv()
        for k in range(1, g.chips):
            self.near(k, j, g.behind(k) * 2 + 1 - g.core).wait_recv()

    def drain(self, n):
        g = self.g

        def one(j, _):
            for k in range(1, g.chips):
                self.far(k, j, g.me, g.sibling).wait_send()
            for k in range(g.chips):
                self.near(k, j, g.me).wait_send()
            return 0

        lax.fori_loop(0, n, one, 0)


def scatter_scratch(group_size, rows, width, n):
    c = group_size // 2
    far = pltpu.VMEM((max(c - 1, 1), rows, width), BF)
    near = pltpu.VMEM((c, rows, width), BF)
    return [pltpu.VMEM((group_size, rows, width), F32), near, near, far, far] + comm_sems(
        group_size, n
    )


class Scatter:
    def __init__(self, g, rc, scratch):
        self.g, self.rc = g, rc
        self.part, self.near_out, self.near_in, self.far_out, self.far_in = scratch[:5]
        self.far_send, self.far_recv, self.near_send, self.near_recv = scratch[5:]

    def near(self, k, j):
        rows = span(j, self.rc)
        return remote(
            self.near_out.at[k, rows],
            self.near_in.at[k, rows],
            self.near_send.at[k, j],
            self.near_recv.at[k, j],
            self.g.sibling,
        )

    def far(self, k, j):
        rows = span(j, self.rc)
        return remote(
            self.far_out.at[k - 1, rows],
            self.far_in.at[k - 1, rows],
            self.far_send.at[k - 1, j],
            self.far_recv.at[k - 1, j],
            self.g.ahead(k) * 2 + self.g.core,
        )

    def first(self, j):
        g, rows = self.g, span(j, self.rc)
        for k in list(range(1, g.chips)) + [0]:
            owner = g.ahead(k) * 2 + 1 - g.core
            self.near_out[k, rows, :] = self.part[owner, rows, :].astype(BF)
            self.near(k, j).start()

    def second(self, j):
        g, rows = self.g, span(j, self.rc)
        for k in range(1, g.chips):
            owner = g.ahead(k) * 2 + g.core
            self.near(k, j).wait_recv()
            both = self.part[owner, rows, :] + self.near_in[k, rows, :].astype(F32)
            self.far_out[k - 1, rows, :] = both.astype(BF)
            self.far(k, j).start()

    def third(self, j):
        g, rows = self.g, span(j, self.rc)
        self.near(0, j).wait_recv()
        total = self.part[g.me, rows, :] + self.near_in[0, rows, :].astype(F32)
        for k in range(1, g.chips):
            self.far(k, j).wait_recv()
            total = total + self.far_in[k - 1, rows, :].astype(F32)
        return total

    def drain(self, n):
        g = self.g

        def one(j, _):
            for k in range(1, g.chips):
                self.far(k, j).wait_send()
            for k in range(g.chips):
                self.near(k, j).wait_send()
            return 0

        lax.fori_loop(0, n, one, 0)


def far_copy(src, dst, send, recv, target):
    return pltpu.make_async_remote_copy(
        src_ref=src,
        dst_ref=dst,
        send_sem=send,
        recv_sem=recv,
        device_id=target,
        device_id_type=MESH,
    )


class Swap:
    def __init__(self, src, stage, sems):
        self.src, self.stage, self.sems = src, stage, sems
        self.s = lax.axis_index("section")

    def copies(self, layer):
        local = pltpu.make_async_copy(self.src.at[self.s], self.stage.at[self.s], self.sems.at[0])
        side = far_copy(
            self.src.at[1 - self.s],
            self.stage.at[layer],
            self.sems.at[1],
            self.sems.at[2],
            {"section": 1 - self.s},
        )
        return local, side

    def start(self):
        for copy in self.copies(self.s):
            copy.start()

    def arrive(self):
        local, side = self.copies(1 - self.s)
        local.wait()
        side.wait_recv()

    def finish(self):
        self.copies(self.s)[1].wait_send()


def reduce_scratch(replicas, rows, cols):
    many = pltpu.VMEM((replicas - 1, rows, cols), BF)
    one = pltpu.VMEM((rows, cols), BF)
    far, side = DMA((replicas - 1, 2)), DMA((2,))
    return [pltpu.VMEM((rows, cols), F32), many, many, one, one, far, far, side, side]


class Reduce:
    def __init__(self, layer, scratch):
        self.layer = layer
        self.own, self.away, self.came, self.over, self.back = scratch[:5]
        self.z_send, self.z_recv, self.y_send, self.y_recv = scratch[5:]
        self.replicas = self.away.shape[0] + 1
        self.half = self.own.shape[0] // 2
        self.d = lax.axis_index("dp")
        self.s = lax.axis_index("section")

    def target(self, k):
        return lax.rem(self.d + k, self.replicas)

    def part(self, i):
        return pl.ds(pl.multiple_of(i * self.half, self.half), self.half)

    def z_copy(self, k, i):
        part = self.part(i)
        return far_copy(
            self.away.at[k - 1, part],
            self.came.at[k - 1, part],
            self.z_send.at[k - 1, i],
            self.z_recv.at[k - 1, i],
            {"dp": self.target(k)},
        )

    def y_copy(self, i):
        part = self.part(i)
        return far_copy(
            self.over.at[part],
            self.back.at[part],
            self.y_send.at[i],
            self.y_recv.at[i],
            {"section": 1 - self.s},
        )

    def send(self, block):
        def one(i):
            k = i + 1
            self.away[i] = block(self.target(k)).astype(BF)
            self.z_copy(k, 0).start()
            self.z_copy(k, 1).start()

        run(self.replicas - 1, one)
        self.own[...] = block(self.d)

    def collect(self):
        def one(i):
            part = self.part(i)
            total = self.own[part, :]
            for k in range(1, self.replicas):
                self.z_copy(k, i).wait_recv()
                total = total + self.came[k - 1, part, :].astype(F32)
            self.own[part, :] = total
            self.over[part, :] = total.astype(BF)

            @pl.when(self.s != self.layer)
            def _():
                self.y_copy(i).start()

        run(2, one)

    def finish(self, out):
        @pl.when(self.s == self.layer)
        def _():
            self.y_copy(0).wait_recv()
            self.y_copy(1).wait_recv()
            out[...] = self.own[...] + self.back[...].astype(F32)

        @pl.when(self.s != self.layer)
        def _():
            self.y_copy(0).wait_send()
            self.y_copy(1).wait_send()
            out[...] = self.own[...]

        for k in range(1, self.replicas):
            self.z_copy(k, 0).wait_send()
            self.z_copy(k, 1).wait_send()


class HalfSwap:
    def __init__(self, src, came, sems):
        self.src, self.came, self.sems = src, came, sems
        self.s = lax.axis_index("section")
        self.rows = came.shape[1]

    def copy(self):
        at = pl.ds(pl.multiple_of((1 - self.s) * self.rows, self.rows), self.rows)
        return far_copy(
            self.src.at[:, at],
            self.came,
            self.sems.at[0],
            self.sems.at[1],
            {"section": 1 - self.s},
        )


def half_scratch(replicas, rows, cols):
    rows = rows // 2
    all_, far = pltpu.VMEM((replicas, rows, cols), BF), pltpu.VMEM((replicas - 1, rows, cols), BF)
    one = pltpu.VMEM((rows, cols), BF)
    z = DMA((replicas - 1,))
    return [all_, all_, far, far, pltpu.VMEM((rows, cols), F32), one, one, DMA((3,)), z, z, DMA((2,))]


HALF = 11


class HalfReduce:
    def __init__(self, layer, scratch):
        self.layer = layer
        self.mine, self.other, self.away, self.came, self.own, self.over, self.back = scratch[:7]
        self.in_sem, self.z_send, self.z_recv, self.y_sem = scratch[7:]
        self.replicas, self.rows = self.mine.shape[:2]
        self.s = lax.axis_index("section")
        self.d = lax.axis_index("dp")

    def half(self, s):
        return pl.ds(pl.multiple_of(s * self.rows, self.rows), self.rows)

    def loads(self, src, other):
        loads = [pltpu.make_async_copy(src.at[:, self.half(self.s)], self.mine, self.in_sem.at[0])]
        if other is not None:
            loads.append(pltpu.make_async_copy(other, self.other, self.in_sem.at[1]))
        return loads

    def z_copy(self, k):
        return far_copy(
            self.away.at[k - 1],
            self.came.at[k - 1],
            self.z_send.at[k - 1],
            self.z_recv.at[k - 1],
            {"dp": lax.rem(self.d + k, self.replicas)},
        )

    def y_copy(self):
        return far_copy(
            self.over, self.back, self.y_sem.at[0], self.y_sem.at[1], {"section": 1 - self.s}
        )

    def middle(self):
        def both(z):
            return self.mine[z].astype(F32) + self.other[z].astype(F32)

        for k in range(1, self.replicas):
            self.away[k - 1] = both(lax.rem(self.d + k, self.replicas)).astype(BF)
            self.z_copy(k).start()
        self.own[...] = both(self.d)

    def late(self):
        total = self.own[...]
        for k in range(1, self.replicas):
            self.z_copy(k).wait_recv()
            total = total + self.came[k - 1].astype(F32)
        self.own[...] = total
        self.over[...] = total.astype(BF)

        @pl.when(self.s != self.layer)
        def _():
            self.y_copy().start()

    def finish(self, out, above=None):
        @pl.when(self.s == self.layer)
        def _():
            self.y_copy().wait_recv()
            out[self.half(self.s), :] = self.own[...]
            out[self.half(1 - self.s), :] = self.back[...].astype(F32)

        @pl.when(self.s != self.layer)
        def _():
            if above is None:
                out[...] = jnp.zeros_like(out)
            else:
                copy = pltpu.make_async_copy(above, out, self.in_sem.at[2])
                copy.start()
                copy.wait()
            self.y_copy().wait_send()

        for k in range(1, self.replicas):
            self.z_copy(k).wait_send()


class Spread:
    def __init__(self, src, dst, by_columns, sems):
        self.src, self.dst, self.by_columns = src, dst, by_columns
        self.own_sem, self.far_send, self.far_recv, self.side_send, self.side_recv = sems
        self.replicas = far = self.side_send.shape[0]
        self.s = lax.axis_index("section")
        self.d = lax.axis_index("dp")
        self.stages = [
            sorted({k, far - k}) for k in range(1, far // 2 + 1)
        ]

    def place(self, half, z):
        rows, cols = self.src.shape
        if self.by_columns:
            return self.dst.at[
                pl.ds(pl.multiple_of(half * rows, rows), rows),
                pl.ds(pl.multiple_of(z * cols, cols), cols),
            ]
        return self.dst.at[pl.ds(pl.multiple_of((2 * z + half) * rows, rows), rows)]

    def origin(self, k):
        return lax.rem(self.d + self.replicas - k, self.replicas)

    def own(self):
        return pltpu.make_async_copy(self.src, self.place(self.s, self.d), self.own_sem.at[0])

    def far(self, k, origin):
        return pltpu.make_async_remote_copy(
            src_ref=self.src,
            dst_ref=self.place(self.s, origin),
            send_sem=self.far_send.at[k - 1],
            recv_sem=self.far_recv.at[k - 1],
            device_id={"dp": lax.rem(self.d + k, self.replicas)},
            device_id_type=MESH,
        )

    def side(self, k, half):
        place = self.place(half, self.origin(k))
        return pltpu.make_async_remote_copy(
            src_ref=self.src if k == 0 else place,
            dst_ref=place,
            send_sem=self.side_send.at[k],
            recv_sem=self.side_recv.at[k],
            device_id={"section": 1 - self.s},
            device_id_type=MESH,
        )

    def start(self):
        for k in self.stages[0]:
            self.far(k, self.d).start()
        self.side(0, self.s).start()
        self.own().start()

    def step(self, i):
        for k in self.stages[i]:
            self.far(k, self.origin(k)).wait_recv()
            self.side(k, self.s).start()
        if i + 1 < len(self.stages):
            for k in self.stages[i + 1]:
                self.far(k, self.d).start()

    def finish(self):
        self.own().wait()
        for k in range(self.replicas):
            self.side(k, 1 - self.s).wait_recv()
        for k in range(1, self.replicas):
            self.far(k, self.d).wait_send()
        for k in range(self.replicas):
            self.side(k, self.s).wait_send()


class ZGather:
    def __init__(self, src, got, sems):
        self.src, self.got = src, got
        self.own_sem, self.send, self.recv = sems
        self.replicas = got.shape[0]
        self.d = lax.axis_index("dp")

    def own(self):
        return pltpu.make_async_copy(self.src, self.got.at[self.d], self.own_sem.at[0])

    def far(self, k, origin):
        return far_copy(
            self.src,
            self.got.at[origin],
            self.send.at[k - 1],
            self.recv.at[k - 1],
            {"dp": lax.rem(self.d + k, self.replicas)},
        )

    def start(self):
        for k in range(1, self.replicas):
            self.far(k, self.d).start()
        self.own().start()

    def step(self, i):
        pass

    def finish(self):
        self.own().wait()
        for k in range(1, self.replicas):
            self.far(k, lax.rem(self.d + self.replicas - k, self.replicas)).wait_recv()
        for k in range(1, self.replicas):
            self.far(k, self.d).wait_send()


class YJoin:
    def __init__(self, got, dst, by_columns, sems):
        self.src, self.dst, self.by_columns = got, dst, by_columns
        self.own_sem, self.send, self.recv, self.got, self.in_sem = sems
        self.replicas, self.rows, self.cols = got.shape
        self.s = lax.axis_index("section")

    def place(self, half, z):
        rows, cols = self.rows, self.cols
        if self.by_columns:
            return self.dst.at[
                pl.ds(pl.multiple_of(half * rows, rows), rows), pl.ds(z * cols, cols)
            ]
        return self.dst.at[pl.ds(pl.multiple_of((2 * z + half) * rows, rows), rows)]

    def own(self, z):
        return pltpu.make_async_copy(self.got.at[z], self.place(self.s, z), self.own_sem.at[z])

    def side(self, z, half):
        return far_copy(
            self.got.at[z],
            self.place(half, z),
            self.send.at[z],
            self.recv.at[z],
            {"section": 1 - self.s},
        )

    def start(self):
        load = pltpu.make_async_copy(self.src, self.got, self.in_sem.at[0])
        load.start()
        load.wait()
        for z in range(self.replicas):
            self.side(z, self.s).start()
            self.own(z).start()

    def step(self, i):
        pass

    def finish(self):
        for z in range(self.replicas):
            self.own(z).wait()
            self.side(z, 1 - self.s).wait_recv()
        for z in range(self.replicas):
            self.side(z, self.s).wait_send()


def rider_sems(replicas):
    far, side = DMA((replicas - 1,)), DMA((replicas,))
    return [DMA((1,)), far, far, side, side]


class Riders:
    def __init__(self, srcs, dsts, columns, sems):
        self.all = []
        for src, dst, (kind, layer, by) in zip(srcs, dsts, columns):
            count = 3 if kind == "z" else 5
            own, sems = sems[:count], sems[count:]
            if kind == "spread":
                self.all.append(Spread(src.at[layer], dst, by, own))
            elif kind == "z":
                self.all.append(ZGather(src.at[layer], dst, own))
            else:
                self.all.append(YJoin(src, dst, by, own))
        self.replicas = self.all[0].replicas if self.all else 0

    def start(self):
        for one in self.all:
            one.start()

    def step(self, j, n):
        if not self.all:
            return
        stages = self.replicas // 2
        for i in range(stages):

            @pl.when(j == n * (i + 1) // stages - 1)
            def _(i=i):
                for one in self.all:
                    one.step(i)

    def finish(self):
        for one in self.all:
            one.finish()


def riding(riders, replicas):
    arrays = [array for array, _, _, _ in riders]
    columns = tuple(rider[1:] for rider in riders)
    outs, sems = [], []
    for array, kind, _, by in riders:
        rows, cols = array.shape[1:]
        if kind == "z":
            outs.append(shape((replicas, rows, cols), BF))
        else:
            outs.append(
                shape((2 * rows, replicas * cols) if by else (2 * replicas * rows, cols), BF)
            )
        far, side = DMA((replicas - 1,)), DMA((replicas,))
        sems += {
            "spread": rider_sems(replicas),
            "z": [DMA((1,)), far, far],
            "y": [side, side, side, pltpu.VMEM(array.shape, BF), DMA((1,))],
        }[kind]
    return arrays, columns, outs, sems


def params(key):
    return pltpu.CompilerParams(
        vmem_limit_bytes=LIMIT, collective_id=key, has_side_effects=True
    )


def cost(flops, moved, exps=0):
    return pl.CostEstimate(flops=int(flops), bytes_accessed=int(moved), transcendentals=int(exps))


def normed(source):
    center = source - jnp.mean(source, axis=-1, keepdims=True)
    r = lax.rsqrt(jnp.mean(center * center, axis=-1, keepdims=True) + 1e-05)
    return center * r, r


def normed_back(source, gain, grad):
    n, r = normed(source)
    e = grad * gain
    dh = r * (
        e - jnp.mean(e, axis=-1, keepdims=True) - n * jnp.mean(e * n, axis=-1, keepdims=True)
    )
    return dh, jnp.sum(grad * n, axis=0, keepdims=True)


def flat(value):
    return value.reshape((value.shape[0] * value.shape[1],) + value.shape[2:])


def run(n, body):
    def one(j, carry):
        body(j)
        return carry

    lax.fori_loop(0, n, one, 0)


def first_kernel(
    size, replicas, x_ref, gain_ref, wq_ref, wo_ref, wu_ref, wd_ref,
    qkv_ref, gains_out, a1_out, wq_out, wo_out, q_stage, o_stage, u_stage, d_stage,
    a1, w, gains, own_sem, q_sem, o_sem, u_sem, d_sem, gain_sem, *sems
):
    rows, width = x_ref.shape
    n = thin_chunks(rows)
    rc = rows // n
    g = Group(size)
    section = lax.axis_index("section")
    gather = Gather(g, a1, rc, sems[:4])
    swaps = [
        Swap(wq_ref, q_stage, q_sem),
        Swap(wo_ref, o_stage, o_sem),
        Swap(wu_ref, u_stage, u_sem),
        Swap(wd_ref, d_stage, d_sem),
    ]
    spreads = [
        Spread(q_stage.at[0], w, False, sems[4:9]),
        Spread(o_stage.at[0], wo_out, True, sems[9:14]),
    ]
    riders = Riders([], [], (), [])
    riders.all = spreads
    riders.replicas = replicas
    g.greet(replicas)

    def gain_copy(layer):
        return far_copy(
            gain_ref, gains.at[layer], gain_sem.at[0], gain_sem.at[1], {"section": 1 - section}
        )

    gain_copy(section).start()
    swaps[0].start()
    swaps[1].start()
    gains[section] = gain_ref[...]
    gain_copy(1 - section).wait_recv()
    gains_out[...] = gains[...]

    def send(j):
        at = span(j, rc)
        a = normed(x_ref[at, :].astype(F32))[0] * gains[0, 0:1, :]
        a1[g.me, at, :] = a.astype(BF)
        gather.start(j)

    run(n, send)
    swaps[0].arrive()
    swaps[1].arrive()
    riders.start()
    swaps[2].start()
    swaps[3].start()

    def relay(j):
        gather.relay(j)
        riders.step(j, n)

    run(n, relay)
    riders.finish()
    outs = [
        pltpu.make_async_copy(w, wq_out, own_sem.at[0]),
        pltpu.make_async_copy(a1, a1_out, own_sem.at[1]),
    ]
    outs[0].start()

    def multiply(j):
        at = span(j, rc)
        gather.ready(j)
        r = dg(flat(a1[:, at, :]), w[...], NN).astype(BF)
        qkv_ref[:, at, :] = r.reshape(size, rc, r.shape[1])

    run(n, multiply)
    outs[1].start()
    swaps[2].arrive()
    swaps[3].arrive()
    for swap in swaps:
        swap.finish()
    gain_copy(section).wait_send()
    gather.drain(n)
    for out in outs:
        out.wait()


def first_forward(size, replicas, x, gains, ws):
    rows, width = x.shape
    wide = ws[0].shape[2]
    deep = 2 * ws[1].shape[1]
    n = thin_chunks(rows)
    return pl.pallas_call(
        functools.partial(first_kernel, size, replicas),
        out_shape=[
            shape((size, rows, wide), BF),
            shape((2,) + gains.shape, F32),
            shape((size, rows, width), BF),
            shape((width, wide), BF),
            shape((deep, width), BF),
        ]
        + [shape(w.shape, BF) for w in ws],
        in_specs=[VM] * 6,
        out_specs=[VM, VM] + [HB] * 7,
        scratch_shapes=[
            pltpu.VMEM((size, rows, width), BF),
            pltpu.VMEM((width, wide), BF),
            pltpu.VMEM((2,) + gains.shape, F32),
            DMA((2,)),
            DMA((3,)),
            DMA((3,)),
            DMA((3,)),
            DMA((3,)),
            DMA((2,)),
        ]
        + comm_sems(size, n)
        + rider_sems(replicas) * 2,
        compiler_params=params(0),
        cost_estimate=cost(30e9, 30e6),
    )(x, gains, *ws)


def attend_kernel(size, layer, columns, *refs):
    m = len(columns)
    qkv_ref, qm_ref, km_ref, x_ref, w_ref = refs[:5]
    refs = refs[5:]
    if layer == 1:
        cot_ref, refs = refs[0], refs[1:]
    halves, refs = refs[:m], refs[m:]
    h1_ref, ctx_ref, lse_ref = refs[:3]
    refs = refs[3:]
    if layer == 1:
        cot_out, refs = refs[0], refs[1:]
    wholes, refs = refs[:m], refs[m:]
    ka, vt, w, w_sem = refs[:4]
    scratch, refs = refs[4:13], refs[13:]
    if layer == 1:
        cot_sems, cot_sem, refs = refs[:4], refs[4], refs[5:]
    riders = Riders(halves, wholes, columns, refs)
    _, rows, wide = qkv_ref.shape
    length = size * rows
    e = qm_ref.shape[2]
    heads = wide // (3 * e)
    c = e**-0.5 * math.log2(math.e)
    n = chunks(rows)
    rc = rows // n
    bq = size * rc
    kc = bq
    g = Group(size)
    copy = pltpu.make_async_copy(w_ref, w, w_sem.at[0])
    copy.start()
    g.greet(riders.replicas)
    riders.start()
    if layer == 1:
        cot = Gather(g, cot_out, rows, cot_sems)
        own = pltpu.make_async_copy(cot_ref, cot_out.at[g.me], cot_sem.at[0])
        own.start()
        cot.start(0, cot_ref)
    scatter = Scatter(g, rc, scratch)
    whole = flat(qkv_ref[...])
    for h in range(heads):
        o = 3 * e * h
        ka[h, :, :e] = whole[:, o + e : o + 2 * e]
        ka[h, :, e:] = flat(km_ref[...])
        vt[h, :e, :] = whole[:, o + 2 * e : o + 3 * e].T
        vt[h, e:, :] = jnp.ones((16, length), BF)
    copy.wait()

    def work(j):
        at = span(j, rc)
        qm = flat(qm_ref[:, at, :])
        found = []
        held_qkv = flat(qkv_ref[:, at, :])
        for h in range(heads):
            o = 3 * e * h
            q = jnp.concatenate([held_qkv[:, o : o + e], qm], axis=1)
            held = []
            top = None
            for k in range(length // kc):
                s = dg(ka[h, k * kc : (k + 1) * kc, :], q, NT)
                t = jnp.max(s, axis=0, keepdims=True)
                top = t if top is None else jnp.maximum(top, t)
                held.append(s)
            top = top * c
            acc = None
            for k in range(length // kc):
                p = jnp.exp2(held[k] * c - top).astype(BF)
                a = dg(vt[h, :, k * kc : (k + 1) * kc], p, NN)
                acc = a if acc is None else acc + a
            total = acc[e : e + 1]
            found.append((acc[:e] * (1.0 / total)).astype(BF))
            lse_ref[j, h : h + 1, :] = top + jnp.log2(total)
        ctx = (jnp.concatenate(found, axis=0) if heads > 1 else found[0]).T
        ctx_ref[:, at, :] = ctx.reshape(size, rc, heads * e)
        width = x_ref.shape[1]
        scatter.part[:, at, :] = dg(ctx, w[...], NN).reshape(size, rc, width)
        scatter.first(j)
        scatter.second(j)
        riders.step(j, n)
        if layer == 1:

            @pl.when(j == n - 1)
            def _():
                cot.relay(0)

    run(n, work)

    def last(j):
        at = span(j, rc)
        h1_ref[at, :] = x_ref[at, :].astype(F32) + scatter.third(j)

    run(n, last)
    scatter.drain(n)
    if layer == 1:
        cot.ready(0)
        cot.drain(1)
        own.wait()
    riders.finish()


def attend(size, replicas, layer, qkv, qm, km, x, w, riders, cot=()):
    _, rows, wide = qkv.shape
    e = qm.shape[2]
    heads = wide // (3 * e)
    width = x.shape[1]
    n = chunks(rows)
    halves, columns, outs, sems = riding(riders, replicas)
    return pl.pallas_call(
        functools.partial(attend_kernel, size, layer, columns),
        out_shape=[
            shape((rows, width), F32),
            shape((size, rows, heads * e), BF),
            shape((n, heads, size * rows // n), F32),
        ]
        + [shape((size, rows, width), BF) for _ in cot]
        + outs,
        in_specs=[VM, VM, VM, VM, HB] + [VM] * len(cot) + [HB] * len(riders),
        out_specs=[VM, VM, VM] + [HB] * (len(cot) + len(outs)),
        scratch_shapes=[
            pltpu.VMEM((heads, size * rows, 2 * e), BF),
            pltpu.VMEM((heads, e + 16, size * rows), BF),
            pltpu.VMEM((heads * e, width), BF),
            DMA((1,)),
        ]
        + scatter_scratch(size, rows, width, n)
        + (comm_sems(size, 1) + [DMA((1,))]) * len(cot)
        + sems,
        compiler_params=params(2 + layer),
        cost_estimate=cost(60e9, 20e6),
    )(qkv, qm, km, x, w, *cot, *halves)


def mlp_kernel(size, layer, columns, *refs):
    m = len(columns)
    h1_ref, gain_ref, wu_ref, wd_ref = refs[:4]
    halves, refs = refs[4 : 4 + m], refs[4 + m :]
    y_ref, a2_out, hid_out, slope_out = refs[:4]
    wholes, refs = refs[4 : 4 + m], refs[4 + m :]
    a2, hid, slope, wu, wd, w_sem, out_sem = refs[:7]
    scratch, refs = refs[7:20], refs[20:]
    riders = Riders(halves, wholes, columns, refs)
    rows, width = h1_ref.shape
    hidden = wu_ref.shape[1]
    fb = min(256, hidden)
    n = thin_chunks(rows)
    rc = rows // n
    g = Group(size)
    copies = [
        pltpu.make_async_copy(wu_ref, wu, w_sem.at[0]),
        pltpu.make_async_copy(wd_ref, wd, w_sem.at[1]),
    ]
    for copy in copies:
        copy.start()
    g.greet(riders.replicas)
    gather = Gather(g, a2, rc, scratch[:4])
    scatter = Scatter(g, rc, scratch[4:])

    def send(j):
        at = span(j, rc)
        a = normed(h1_ref[at, :])[0] * gain_ref[layer, 1:2, :]
        a2[g.me, at, :] = a.astype(BF)
        gather.start(j)

    run(n, send)
    riders.start()
    for copy in copies:
        copy.wait()

    def work(j):
        at = span(j, rc)
        gather.relay(j)
        gather.ready(j)
        a = flat(a2[:, at, :])
        for f in range(hidden // fb):
            cols = slice(f * fb, (f + 1) * fb)
            u = dg(a, wu[:, cols], NN)
            half = 0.5 + 0.5 * lax.erf(u * (0.5**0.5))
            slope[:, at, cols] = (
                (half + u * jnp.exp(-0.5 * u * u) * ((2 * math.pi) ** -0.5))
                .astype(BF)
                .reshape(size, rc, fb)
            )
            hid[:, at, cols] = (u * half).astype(BF).reshape(size, rc, fb)
        held = flat(hid[:, at, :])
        for f in range(width // 256):
            cols = slice(f * 256, (f + 1) * 256)
            scatter.part[:, at, cols] = dg(held, wd[:, cols], NN).reshape(size, rc, 256)
        scatter.first(j)
        scatter.second(j)
        riders.step(j, n)

    run(n, work)
    outs = [
        pltpu.make_async_copy(a2, a2_out, out_sem.at[0]),
        pltpu.make_async_copy(hid, hid_out, out_sem.at[1]),
        pltpu.make_async_copy(slope, slope_out, out_sem.at[2]),
    ]
    for out in outs:
        out.start()

    def last(j):
        at = span(j, rc)
        y_ref[at, :] = (h1_ref[at, :] + scatter.third(j)).astype(BF)

    run(n, last)
    riders.finish()
    gather.drain(n)
    scatter.drain(n)
    for out in outs:
        out.wait()


def mlp_forward(size, replicas, layer, h1, gains, wu, wd, riders):
    rows, width = h1.shape
    hidden = wu.shape[1]
    n = thin_chunks(rows)
    halves, columns, outs, sems = riding(riders, replicas)
    return pl.pallas_call(
        functools.partial(mlp_kernel, size, layer, columns),
        out_shape=[
            shape((rows, width), BF),
            shape((size, rows, width), BF),
            shape((size, rows, hidden), BF),
            shape((size, rows, hidden), BF),
        ]
        + outs,
        in_specs=[VM, VM, HB, HB] + [HB] * len(riders),
        out_specs=[VM, HB, HB, HB] + [HB] * len(outs),
        scratch_shapes=[
            pltpu.VMEM((size, rows, width), BF),
            pltpu.VMEM((size, rows, hidden), BF),
            pltpu.VMEM((size, rows, hidden), BF),
            pltpu.VMEM((width, hidden), BF),
            pltpu.VMEM((hidden, width), BF),
            DMA((2,)),
            DMA((3,)),
        ]
        + comm_sems(size, n)
        + scatter_scratch(size, rows, width, n)
        + sems,
        compiler_params=params(4 + layer),
        cost_estimate=cost(50e9, 30e6),
    )(h1, gains, wu, wd, *halves)


def turn_kernel(size, columns, *refs):
    m = len(columns)
    h1_ref, gain_ref, wu_ref, wd_ref, q_stage = refs[:5]
    halves, refs = refs[5 : 5 + m], refs[5 + m :]
    y_ref, qkv_ref, a2_out, hid_out, slope_out, a1_out, wq_out = refs[:7]
    wholes, refs = refs[7 : 7 + m], refs[7 + m :]
    a2, hid, slope, wu, wd, a1, wq, w_sem, out_sem = refs[:9]
    gather_sems, next_sems, refs = refs[9:13], refs[13:17], refs[17:]
    scratch, refs = refs[:9], refs[9:]
    spread = Spread(q_stage.at[1], wq, False, refs[:5])
    riders = Riders(halves, wholes, columns, refs[5:])
    riders.all.insert(0, spread)
    riders.replicas = spread.replicas
    rows, width = h1_ref.shape
    hidden = wu_ref.shape[1]
    fb = min(256, hidden)
    n = thin_chunks(rows)
    rc = rows // n
    g = Group(size)
    copies = [
        pltpu.make_async_copy(wu_ref, wu, w_sem.at[0]),
        pltpu.make_async_copy(wd_ref, wd, w_sem.at[1]),
    ]
    for copy in copies:
        copy.start()
    g.greet(riders.replicas)
    gather = Gather(g, a2, rc, gather_sems)
    onward = Gather(g, a1, rc, next_sems)
    scatter = Scatter(g, rc, scratch)

    def send(j):
        at = span(j, rc)
        a = normed(h1_ref[at, :])[0] * gain_ref[0, 1:2, :]
        a2[g.me, at, :] = a.astype(BF)
        gather.start(j)

    run(n, send)
    riders.start()
    for copy in copies:
        copy.wait()

    def pass_on(j):
        at = span(j, rc)
        y = (h1_ref[at, :] + scatter.third(j)).astype(BF)
        y_ref[at, :] = y
        a = normed(y.astype(F32))[0] * gain_ref[1, 0:1, :]
        a1[g.me, at, :] = a.astype(BF)
        onward.start(j)

    lag = min(2, n)

    def work(j):
        at = span(j, rc)
        gather.relay(j)
        gather.ready(j)
        a = flat(a2[:, at, :])
        for f in range(hidden // fb):
            cols = slice(f * fb, (f + 1) * fb)
            u = dg(a, wu[:, cols], NN)
            half = 0.5 + 0.5 * lax.erf(u * (0.5**0.5))
            slope[:, at, cols] = (
                (half + u * jnp.exp(-0.5 * u * u) * ((2 * math.pi) ** -0.5))
                .astype(BF)
                .reshape(size, rc, fb)
            )
            hid[:, at, cols] = (u * half).astype(BF).reshape(size, rc, fb)
        held = flat(hid[:, at, :])
        for f in range(width // 256):
            cols = slice(f * 256, (f + 1) * 256)
            scatter.part[:, at, cols] = dg(held, wd[:, cols], NN).reshape(size, rc, 256)
        scatter.first(j)
        scatter.second(j)

        @pl.when(j >= lag)
        def _():
            pass_on(j - lag)

        riders.step(j, n)

    run(n, work)
    outs = [
        pltpu.make_async_copy(a2, a2_out, out_sem.at[0]),
        pltpu.make_async_copy(hid, hid_out, out_sem.at[1]),
        pltpu.make_async_copy(slope, slope_out, out_sem.at[2]),
    ]
    for out in outs:
        out.start()
    for j in range(n - lag, n):
        pass_on(j)
    spread.finish()
    riders.all.pop(0)
    outs.append(pltpu.make_async_copy(wq, wq_out, out_sem.at[3]))
    outs[3].start()

    def multiply(j):
        at = span(j, rc)
        onward.relay(j)
        onward.ready(j)
        r = dg(flat(a1[:, at, :]), wq[...], NN).astype(BF)
        qkv_ref[:, at, :] = r.reshape(size, rc, r.shape[1])

    run(n, multiply)
    outs.append(pltpu.make_async_copy(a1, a1_out, out_sem.at[4]))
    outs[4].start()
    riders.finish()
    gather.drain(n)
    onward.drain(n)
    scatter.drain(n)
    for out in outs:
        out.wait()


def turn_forward(size, replicas, h1, gains, wu, wd, stage, riders):
    rows, width = h1.shape
    hidden = wu.shape[1]
    wide = stage.shape[2]
    n = thin_chunks(rows)
    halves, columns, outs, sems = riding(riders, replicas)
    return pl.pallas_call(
        functools.partial(turn_kernel, size, columns),
        out_shape=[
            shape((rows, width), BF),
            shape((size, rows, wide), BF),
            shape((size, rows, width), BF),
            shape((size, rows, hidden), BF),
            shape((size, rows, hidden), BF),
            shape((size, rows, width), BF),
            shape((width, wide), BF),
        ]
        + outs,
        in_specs=[VM, VM] + [HB] * (3 + len(riders)),
        out_specs=[VM, VM] + [HB] * (5 + len(outs)),
        scratch_shapes=[
            pltpu.VMEM((size, rows, width), BF),
            pltpu.VMEM((size, rows, hidden), BF),
            pltpu.VMEM((size, rows, hidden), BF),
            pltpu.VMEM((width, hidden), BF),
            pltpu.VMEM((hidden, width), BF),
            pltpu.VMEM((size, rows, width), BF),
            pltpu.VMEM((width, wide), BF),
            DMA((2,)),
            DMA((5,)),
        ]
        + comm_sems(size, n) * 2
        + scatter_scratch(size, rows, width, n)
        + rider_sems(replicas)
        + sems,
        compiler_params=params(4),
        cost_estimate=cost(50e9, 30e6),
    )(h1, gains, wu, wd, stage, *halves)


def mlp_back_kernel(size, layer, parts, *refs):
    g_ref, h1_ref, gain_ref, a2_ref, hid_ref, slope_ref, wu_ref, wd_ref = refs[:8]
    refs = refs[8:]
    if layer == 1:
        ys, whole_ref, refs = refs[:2], refs[2], refs[3:]
    mid_ref, gain_out, gup_ref, gdown_ref = refs[:4]
    refs = refs[4:]
    if layer == 1:
        y_out, refs = refs[0], refs[1:]
    grad, a2, hid, dup, wu, wd, w_sem = refs[:7]
    scratch, refs = refs[7:20], refs[20:]
    rows, width = h1_ref.shape
    hidden = wu_ref.shape[1]
    depth = width // parts
    fb = min(256, hidden)
    n = thin_chunks(rows)
    rc = rows // n
    g = Group(size)
    copies = [
        pltpu.make_async_copy(wd_ref, wd, w_sem.at[0]),
        pltpu.make_async_copy(slope_ref, dup, w_sem.at[1]),
        pltpu.make_async_copy(wu_ref, wu, w_sem.at[2]),
    ]
    late = [
        pltpu.make_async_copy(hid_ref, hid, w_sem.at[3]),
        pltpu.make_async_copy(a2_ref, a2, w_sem.at[4]),
    ]
    for copy in copies + late:
        copy.start()
    g.greet(side=layer == 1)
    section = lax.axis_index("section")
    if layer == 1:
        y_sem, y_own = refs

        def y_load(own):
            return pltpu.make_async_copy(own, y_own, y_sem.at[3])

        def y_copies(own, other, at):
            return (
                pltpu.make_async_copy(y_own, y_out.at[section], y_sem.at[0]),
                far_copy(
                    other, y_out.at[at], y_sem.at[1], y_sem.at[2], {"section": 1 - section}
                ),
            )

        for i in range(2):

            @pl.when(section == i)
            def _(i=i):
                y_load(ys[i]).start()
                y_copies(ys[i], ys[1 - i], section)[1].start()

    gather = Gather(g, grad, rc, scratch[:4])
    scatter = Scatter(g, rc, scratch[4:])

    def send(j):
        at = span(j, rc)
        grad[g.me, at, :] = g_ref[at, :]
        gather.start(j)

    if layer == 1:
        whole = pltpu.make_async_copy(whole_ref, grad, w_sem.at[5])
        whole.start()
        copies.append(whole)
    else:
        run(n, send)
    for copy in copies:
        copy.wait()
    if layer == 1:
        y_load(ys[0]).wait()
        y_copies(ys[0], ys[1], section)[0].start()

    def work(j):
        at = span(j, rc)
        if layer == 0:
            gather.relay(j)
            gather.ready(j)
        held = flat(grad[:, at, :])
        for f in range(hidden // fb):
            cols = slice(f * fb, (f + 1) * fb)
            d = dg(held, wd[cols, :], NT) * flat(dup[:, at, cols]).astype(F32)
            dup[:, at, cols] = d.astype(BF).reshape(size, rc, fb)
        held = flat(dup[:, at, :])
        for z in range(parts):
            cols = slice(z * depth, (z + 1) * depth)
            scatter.part[:, at, cols] = dg(held, wu[cols, :], NT).reshape(size, rc, depth)
        scatter.first(j)
        scatter.second(j)

    run(n, work)
    for copy in late:
        copy.wait()

    def up_grad(z):
        cols = pl.ds(pl.multiple_of(z * depth, depth), depth)
        gup_ref[z] = dg(flat(a2[:, :, cols]), flat(dup[...]), TN).astype(BF)

    run(parts, up_grad)

    def down_grad(f):
        cols = pl.ds(pl.multiple_of(f * fb, fb), fb)
        r = dg(flat(hid[:, :, cols]), flat(grad[...]), TN).astype(BF)
        for z in range(parts):
            gdown_ref[z, cols, :] = r[:, z * depth : (z + 1) * depth]

    run(hidden // fb, down_grad)
    gain_out[...] = jnp.zeros_like(gain_out)

    def last(j):
        at = span(j, rc)
        dh, dgain = normed_back(h1_ref[at, :], gain_ref[layer, 1:2, :], scatter.third(j))
        mid_ref[at, :] = g_ref[at, :].astype(F32) + dh
        gain_out[...] += dgain

    run(n, last)
    if layer == 1:
        local, side = y_copies(ys[0], ys[1], 1 - section)
        local.wait()
        side.wait_recv()
        y_copies(ys[0], ys[1], section)[1].wait_send()
    if layer == 0:
        gather.drain(n)
    scatter.drain(n)


def mlp_backward(size, replicas, layer, grad, h1, gains, a2, hid, slope, wu, wd, extra):
    rows, width = h1.shape
    hidden = wu.shape[1]
    parts, depth = replicas, width // replicas
    n = thin_chunks(rows)
    return pl.pallas_call(
        functools.partial(mlp_back_kernel, size, layer, parts),
        out_shape=[
            shape((rows, width), F32),
            shape((1, width), F32),
            shape((parts, depth, hidden), BF),
            shape((parts, hidden, depth), BF),
        ]
        + [shape((2, rows, width), BF)] * (len(extra) // 3),
        in_specs=[VM, VM, VM] + [HB] * (5 + len(extra)),
        out_specs=[VM, VM, VM, VM] + [HB] * (len(extra) // 3),
        scratch_shapes=[
            pltpu.VMEM((size, rows, width), BF),
            pltpu.VMEM((size, rows, width), BF),
            pltpu.VMEM((size, rows, hidden), BF),
            pltpu.VMEM((size, rows, hidden), BF),
            pltpu.VMEM((width, hidden), BF),
            pltpu.VMEM((hidden, width), BF),
            DMA((6,)),
        ]
        + comm_sems(size, n)
        + scatter_scratch(size, rows, width, n)
        + [DMA((4,)), pltpu.VMEM((rows, width), BF)] * (len(extra) // 3),
        compiler_params=params(6 + layer),
        cost_estimate=cost(60e9, 40e6),
    )(grad, h1, gains, a2, hid, slope, wu, wd, *extra)


def attend_back_kernel(size, layer, parts, *refs):
    mid_ref, qkv_ref, qm_ref, km_ref, ctx_ref, lse_ref, w_ref = refs[:7]
    refs = refs[7:]
    if layer == 0:
        gdown_ref, refs = refs[0], refs[1:]
    dqkv_ref, gout_ref, refs = refs[0], refs[1], refs[2:]
    if layer == 0:
        down_out, refs = refs[0], refs[1:]
    da, ka, va, kt, dk, dv, w, w_sem = refs[:8]
    sems, refs = refs[8:12], refs[12:]
    reduce = Reduce(layer, refs[:9])
    if layer == 0:
        down = HalfReduce(layer, refs[9 : 9 + HALF])
        down_swap = HalfSwap(gdown_ref, down.other, refs[9 + HALF])
    _, rows, wide = qkv_ref.shape
    length = size * rows
    e = qm_ref.shape[2]
    heads = wide // (3 * e)
    scale = e**-0.5
    c = scale * math.log2(math.e)
    depth = w_ref.shape[1] // parts
    n = chunks(rows)
    rc = rows // n
    bq = size * rc
    kc = bq
    g = Group(size)
    copies = [pltpu.make_async_copy(w_ref, w, w_sem.at[0])]
    for copy in copies:
        copy.start()
    g.greet(parts)
    gather = Gather(g, da, rc, sems)
    loads = []
    if layer == 0:
        down_swap.copy().start()
        loads = down.loads(gdown_ref, None)
        for load in loads:
            load.start()

    def send(j):
        at = span(j, rc)
        da[g.me, at, :] = mid_ref[at, :].astype(BF)
        gather.start(j)

    run(n, send)
    lane = lax.broadcasted_iota(jnp.int32, (length, e), 1)
    whole = flat(qkv_ref[...])
    for h in range(heads):
        o = 3 * e * h
        ka[h, :, :e] = whole[:, o + e : o + 2 * e]
        ka[h, :, e:] = flat(km_ref[...])
        va[h, :, :e] = whole[:, o + 2 * e : o + 3 * e]
        va[h, :, e:] = jnp.where(lane < 3, 1.0, 0.0).astype(BF)
        kt[h] = whole[:, o + e : o + 2 * e].T
    dk[...] = jnp.zeros_like(dk)
    dv[...] = jnp.zeros_like(dv)
    ql = lax.broadcasted_iota(jnp.int32, (bq, e), 1)
    for copy in copies + loads:
        copy.wait()

    def out_grad(z):
        cols = pl.ds(pl.multiple_of(z * depth, depth), depth)
        return dg(flat(ctx_ref[...]), flat(da[:, :, cols]), TN)

    def work(j):
        at = span(j, rc)

        @pl.when(j == 0)
        def _():
            gather.relay(0)
            gather.ready(0)

        @pl.when(j == min(1, n - 1))
        def _():
            for i in range(1, n):
                gather.relay(i)
            for i in range(1, n):
                gather.ready(i)
            reduce.send(out_grad)

        qm = flat(qm_ref[:, at, :])
        dctx = dg(flat(da[:, at, :]), w[...], NT).astype(BF)
        ctx = flat(ctx_ref[:, at, :])
        held_qkv = flat(qkv_ref[:, at, :])
        for h in range(heads):
            o = 3 * e * h
            qq = held_qkv[:, o : o + e]
            q = jnp.concatenate([qq, qm], axis=1)
            dc = dctx[:, h * e : (h + 1) * e]
            prod = dc.astype(F32) * ctx[:, h * e : (h + 1) * e].astype(F32)
            d = -jnp.sum(prod, axis=1, keepdims=True)
            d1 = d.astype(BF).astype(F32)
            d2 = (d - d1).astype(BF).astype(F32)
            d3 = d - d1 - d2
            ds_col = jnp.where(ql == 0, d1, jnp.where(ql == 1, d2, jnp.where(ql == 2, d3, 0.0)))
            dca = jnp.concatenate([dc, ds_col.astype(BF)], axis=1)
            lse = lse_ref[j, h : h + 1, :]
            dqt = None
            for k in range(length // kc):
                ks = slice(k * kc, (k + 1) * kc)
                s = dg(ka[h, ks, :], q, NT)
                p = jnp.exp2(s * c - lse)
                ds = (p * dg(va[h, ks, :], dca, NT)).astype(BF)
                dv[h, ks, :] += dg(p.astype(BF), dc, NN)
                dk[h, ks, :] += dg(ds, qq, NN)
                a = dg(kt[h, :, ks], ds, NN)
                dqt = a if dqt is None else dqt + a
            if layer == 0 and h == heads // 2:

                @pl.when(j == min(1, n - 1))
                def _():
                    down_swap.copy().wait_recv()
                    down.middle()

            if layer == 0 and h == heads - 1:

                @pl.when(j == n - 1)
                def _():
                    down.late()

            dqkv_ref[:, at, o : o + e] = (dqt * scale).T.astype(BF).reshape(size, rc, e)

    run(n, work)
    for h in range(heads):
        o = 3 * e * h
        dqkv_ref[:, :, o + e : o + 2 * e] = (dk[h] * scale).astype(BF).reshape(size, rows, e)
        dqkv_ref[:, :, o + 2 * e : o + 3 * e] = dv[h].astype(BF).reshape(size, rows, e)

    reduce.collect()
    reduce.finish(gout_ref)
    if layer == 0:
        down.finish(down_out)
        down_swap.copy().wait_send()
    gather.drain(n)


def attend_backward(size, replicas, layer, mid, qkv, qm, km, ctx, lse, w, grads):
    _, rows, wide = qkv.shape
    e = qm.shape[2]
    heads = wide // (3 * e)
    width = mid.shape[1]
    parts, depth = replicas, width // replicas
    length = size * rows
    n = chunks(rows)
    return pl.pallas_call(
        functools.partial(attend_back_kernel, size, layer, parts),
        out_shape=[shape(qkv.shape, BF), shape((heads * e, depth), F32)]
        + [shape(grad.shape[1:], F32) for grad in grads],
        in_specs=[VM] * 6 + [HB] * (1 + len(grads)),
        out_specs=[VM, VM] + [VM] * len(grads),
        scratch_shapes=[
            pltpu.VMEM((size, rows, width), BF),
            pltpu.VMEM((heads, length, 2 * e), BF),
            pltpu.VMEM((heads, length, 2 * e), BF),
            pltpu.VMEM((heads, e, length), BF),
            pltpu.VMEM((heads, length, e), F32),
            pltpu.VMEM((heads, length, e), F32),
            pltpu.VMEM((heads * e, width), BF),
            DMA((1,)),
        ]
        + comm_sems(size, n)
        + reduce_scratch(parts, heads * e, depth)
        + sum([half_scratch(parts, *grad.shape[1:]) + [DMA((2,))] for grad in grads], []),
        compiler_params=params(8 + layer),
        cost_estimate=cost(90e9, 40e6),
    )(mid, qkv, qm, km, ctx, lse, w, *grads)


def qkv_back_kernel(
    size, layer, parts, dqkv_ref, gain_ref, a1_in, x_in, mid_in, w_ref,
    dx_ref, gain_out, gqkv_ref, a1_ref, x_ref, mid_ref, w, w_sem, *scratch
):
    rows, width = x_ref.shape
    late = [
        pltpu.make_async_copy(a1_in, a1_ref, w_sem.at[1]),
        pltpu.make_async_copy(x_in, x_ref, w_sem.at[2]),
        pltpu.make_async_copy(mid_in, mid_ref, w_sem.at[3]),
    ]
    depth = width // parts
    n = thin_chunks(rows)
    rc = rows // n
    g = Group(size)
    copies = [pltpu.make_async_copy(w_ref, w, w_sem.at[0])]
    for copy in copies + late:
        copy.start()
    g.greet()
    scatter = Scatter(g, rc, scratch)
    for copy in copies:
        copy.wait()

    def work(j):
        at = span(j, rc)
        held = flat(dqkv_ref[:, at, :])
        for z in range(parts):
            cols = slice(z * depth, (z + 1) * depth)
            scatter.part[:, at, cols] = dg(held, w[cols, :], NT).reshape(size, rc, depth)
        scatter.first(j)
        scatter.second(j)

    run(n, work)
    for copy in late:
        copy.wait()

    def qkv_grad(z):
        cols = pl.ds(pl.multiple_of(z * depth, depth), depth)
        gqkv_ref[z] = dg(flat(a1_ref[:, :, cols]), flat(dqkv_ref[...]), TN).astype(BF)

    run(parts, qkv_grad)
    gain_out[...] = jnp.zeros_like(gain_out)

    def last(j):
        at = span(j, rc)
        dh, dgain = normed_back(
            x_ref[at, :].astype(F32), gain_ref[layer, 0:1, :], scatter.third(j)
        )
        dx_ref[at, :] = (mid_ref[at, :] + dh).astype(BF)
        gain_out[...] += dgain

    run(n, last)
    scatter.drain(n)


def qkv_backward(size, replicas, layer, dqkv, a1, x, mid, gains, w):
    rows, width = x.shape
    wide = w.shape[1]
    parts, depth = replicas, width // replicas
    n = thin_chunks(rows)
    return pl.pallas_call(
        functools.partial(qkv_back_kernel, size, layer, parts),
        out_shape=(
            shape((rows, width), BF),
            shape((1, width), F32),
            shape((parts, depth, wide), BF),
        ),
        in_specs=[VM, VM] + [HB] * 4,
        out_specs=(VM, VM, VM),
        scratch_shapes=[
            pltpu.VMEM((size, rows, width), BF),
            pltpu.VMEM((rows, width), BF),
            pltpu.VMEM((rows, width), F32),
            pltpu.VMEM((width, wide), BF),
            DMA((4,)),
        ]
        + scatter_scratch(size, rows, width, n),
        compiler_params=params(11),
        cost_estimate=cost(30e9, 30e6),
    )(dqkv, gains, a1, x, mid, w)


def last_kernel(
    size, parts, dqkv_ref, a1_ref, x_ref, mid_ref, gain_ref, w_ref, two_ref, above_ref, dx1_ref,
    gain_out, gqkv_out, dx_out,
    gqkv, swap_sem, w, dx, gsum, gcame, w_sem, x_sem, x_send, x_recv, g_send, g_recv, *scratch
):
    rows, width = x_ref.shape
    depth = width // parts
    n = thin_chunks(rows)
    rc = rows // n
    g = Group(size)
    section = lax.axis_index("section")
    d = lax.axis_index("dp")
    copy = pltpu.make_async_copy(w_ref, w, w_sem.at[0])
    copy.start()
    reduce = HalfReduce(0, scratch[:HALF])
    swap = HalfSwap(gqkv, reduce.other, swap_sem)
    scatter = Scatter(g, rc, scratch[HALF:])
    g.greet(parts)

    def upper():
        return far_copy(
            dx1_ref, dx_out.at[0], x_send.at[n], x_recv.at[n], {"section": 1 - section}
        )

    def keep_upper():
        return pltpu.make_async_copy(dx1_ref, dx_out.at[1], x_sem.at[0])

    def lower(j):
        at = span(j, rc)
        return far_copy(
            dx.at[at], dx_out.at[1, at], x_send.at[j], x_recv.at[j], {"section": 1 - section}
        )

    def keep_lower(j):
        at = span(j, rc)
        return pltpu.make_async_copy(dx.at[at], dx_out.at[0, at], x_sem.at[j])

    def qkv_grad(z):
        cols = pl.ds(pl.multiple_of(z * depth, depth), depth)
        gqkv[z] = dg(flat(a1_ref[:, :, cols]), flat(dqkv_ref[...]), TN).astype(BF)

    run(parts, qkv_grad)
    swap.copy().start()
    load = reduce.loads(gqkv, None)[0]
    load.start()

    @pl.when(section == 1)
    def _():
        keep_upper().start()

    copy.wait()

    def work(j):
        at = span(j, rc)
        held = flat(dqkv_ref[:, at, :])
        for z in range(parts):
            cols = slice(z * depth, (z + 1) * depth)
            scatter.part[:, at, cols] = dg(held, w[cols, :], NT).reshape(size, rc, depth)
        scatter.first(j)
        scatter.second(j)

    run(n, work)
    gsum[0] = jnp.zeros_like(gsum[0])

    def last(j):
        at = span(j, rc)
        dh, dgain = normed_back(x_ref[at, :].astype(F32), gain_ref[0, 0:1, :], scatter.third(j))
        dx[at, :] = (mid_ref[at, :] + dh).astype(BF)

        @pl.when(section == 0)
        def _():
            keep_lower(j).start()

        @pl.when(section == 1)
        def _():
            lower(j).start()

        gsum[0, 0:1, :] += dgain

    def rest(j):
        @pl.when(j == n // 2)
        def _():
            load.wait()
            swap.copy().wait_recv()
            reduce.middle()

            @pl.when(section == 0)
            def _():
                upper().start()

        last(j)

    run(n, rest)
    gsum[0, 1:2, :] = two_ref[...]
    gsum[0, 2:4, :] = above_ref[...]

    targets = [
        [{"tensor": g.sibling}],
        [{"tensor": g.ahead(k) * 2 + g.core} for k in range(1, g.chips)],
        [{"dp": lax.rem(d + k, parts)} for k in range(1, parts)],
        [{"section": 1 - section}],
    ]
    slot = 0
    sent = []

    def exchange(stage):
        nonlocal slot
        copies = []
        for target in targets[stage]:
            copies.append(
                far_copy(gsum.at[stage], gcame.at[slot], g_send.at[slot], g_recv.at[slot], target)
            )
            copies[-1].start()
            slot += 1
        total = gsum[stage]
        for i, copy in enumerate(copies):
            copy.wait_recv()
            total = total + gcame[slot - len(copies) + i]
        gsum[stage + 1] = total
        sent.extend(copies)

    exchange(0)
    exchange(1)
    reduce.late()
    exchange(2)
    exchange(3)
    gain_out[...] = gsum[4]

    @pl.when(section == 0)
    def _():
        for j in range(n):
            lower(j).wait_recv()
            keep_lower(j).wait()
        upper().wait_send()

    @pl.when(section == 1)
    def _():
        keep_upper().wait()
        upper().wait_recv()
        for j in range(n):
            lower(j).wait_send()

    reduce.finish(gqkv_out)
    swap.copy().wait_send()
    for copy in sent:
        copy.wait_send()
    scatter.drain(n)


def last_backward(size, replicas, dqkv, a1, x, mid, gains, w, two, above, dx1):
    rows, width = x.shape
    wide = w.shape[1]
    depth = width // replicas
    n = thin_chunks(rows)
    slots = 1 + (size // 2 - 1) + (replicas - 1) + 1
    return pl.pallas_call(
        functools.partial(last_kernel, size, replicas),
        out_shape=(
            shape((8, width), F32),
            shape((depth, wide), F32),
            shape((2, rows, width), BF),
        ),
        in_specs=[VM] * 5 + [HB, VM, VM, VM],
        out_specs=(VM, VM, HB),
        scratch_shapes=[
            pltpu.VMEM((replicas, depth, wide), BF),
            DMA((2,)),
            pltpu.VMEM((width, wide), BF),
            pltpu.VMEM((rows, width), BF),
            pltpu.VMEM((5, 8, width), F32),
            pltpu.VMEM((slots, 8, width), F32),
            DMA((1,)),
            DMA((n,)),
            DMA((n + 1,)),
            DMA((n + 1,)),
            DMA((slots,)),
            DMA((slots,)),
        ]
        + half_scratch(replicas, depth, wide)
        + scatter_scratch(size, rows, width, n),
        compiler_params=params(10),
        cost_estimate=cost(40e9, 30e6),
    )(dqkv, a1, x, mid, gains, w, two, above, dx1)


def scene_masks(segments, e):
    same = (segments[..., None] == jnp.arange(e, dtype=jnp.int32)).astype(F32)
    used = jnp.arange(e) < SCENES
    return (
        jnp.where(used, same * MASKED, 0.0).astype(BF),
        jnp.where(used, 1.0 - same, 0.0).astype(BF),
    )


def swap_section(value):
    return lax.ppermute(value, "section", [(0, 1), (1, 0)])


def shards(
    block_input,
    segment_ids,
    cotangent,
    norm_one_gain,
    qkv_weight,
    out_weight,
    norm_two_gain,
    up_weight,
    down_weight,
):
    section = lax.axis_index("section")
    size = lax.axis_size("tensor")
    replicas = lax.axis_size("dp")

    mine = [
        qkv_weight[0].reshape((qkv_weight.shape[1], -1)),
        out_weight[0].reshape((-1, out_weight.shape[3])),
        up_weight[0],
        down_weight[0],
    ]
    mine = [w.astype(BF).reshape((2, -1, w.shape[1])) for w in mine]
    gains = jnp.concatenate(
        [norm_one_gain, norm_two_gain, jnp.zeros((6, norm_one_gain.shape[1]), F32)], axis=0
    )
    segments = lax.dynamic_index_in_dim(segment_ids, section, 0, keepdims=False)
    x = lax.dynamic_index_in_dim(block_input, section, 0, keepdims=False)
    head_dim = qkv_weight.shape[3] // 3
    qm, km = scene_masks(segments.reshape((size, -1)), head_dim)
    qkv, gains, a1, w_qkv_0, w_out_0, h_qkv, h_out, h_up, h_down = first_forward(
        size, replicas, x, gains, mine
    )
    h1, ctx, lse, w_up_0, w_down_0 = attend(
        size, replicas, 0, qkv, qm, km, x, w_out_0,
        [(h_up, "spread", 0, False), (h_down, "spread", 0, True)],
    )
    below = (x, a1, qkv, ctx, lse, h1)
    y0, qkv, a2, hid, slope, a1, w_qkv_1, w_out_1, w_up_1, got_down = turn_forward(
        size, replicas, h1, gains, w_up_0, w_down_0, h_qkv,
        [(h_out, "spread", 1, True), (h_up, "spread", 1, False), (h_down, "z", 1, True)],
    )
    kept = [below + (a2, hid, slope)]
    grad = lax.dynamic_index_in_dim(cotangent, section, 0, keepdims=False)
    h1, ctx, lse, grad_all, w_down_1 = attend(
        size, replicas, 1, qkv, qm, km, y0, w_out_1, [(got_down, "y", 1, True)], [grad]
    )
    y1, a2, hid, slope = mlp_forward(size, replicas, 1, h1, gains, w_up_1, w_down_1, [])
    kept.append((y0, a1, qkv, ctx, lse, h1, a2, hid, slope))
    weights = [
        (w_qkv_0, w_out_0, w_up_0, w_down_0),
        (w_qkv_1, w_out_1, w_up_1, w_down_1),
    ]
    def reduce_rows(value):
        return lax.psum_scatter(value, "dp", scatter_dimension=0, tiled=False)

    x, a1, qkv, ctx, lse, h1, a2, hid, slope = kept[1]
    w_qkv, w_out, w_up, w_down = weights[1]
    mid, gain_two, g_up, g_down, layer_out = mlp_backward(
        size, replicas, 1, grad, h1, gains, a2, hid, slope, w_up, w_down, [y0, y1, grad_all]
    )
    d_qkv, out_1 = attend_backward(size, replicas, 1, mid, qkv, qm, km, ctx, lse, w_out, [])
    up_1, down_1 = reduce_rows(g_up), reduce_rows(g_down)
    dx1, gain_one, g_qkv = qkv_backward(size, replicas, 1, d_qkv, a1, x, mid, gains, w_qkv)
    gains_above = jnp.concatenate([gain_one, gain_two], axis=0)
    dx1, up_1, down_1 = lax.optimization_barrier((dx1, up_1, down_1))
    qkv_1 = reduce_rows(g_qkv)

    x, a1, qkv, ctx, lse, h1, a2, hid, slope = kept[0]
    w_qkv, w_out, w_up, w_down = weights[0]
    mid, gain_two, g_up, g_down = mlp_backward(
        size, replicas, 0, dx1, h1, gains, a2, hid, slope, w_up, w_down, []
    )
    mid, qkv_1 = lax.optimization_barrier((mid, qkv_1))
    d_qkv, out_0, down_0 = attend_backward(
        size, replicas, 0, mid, qkv, qm, km, ctx, lse, w_out, [g_down]
    )
    up_0 = reduce_rows(g_up)
    d_qkv, up_0 = lax.optimization_barrier((d_qkv, up_0))
    gains, qkv_0, input_out = last_backward(
        size, replicas, d_qkv, a1, x, mid, gains, w_qkv, gain_two, gains_above, dx1
    )

    def finish(zero, one):
        send = swap_section(jnp.where(section == 0, one, zero))
        return jnp.where(section == 0, zero, one).astype(F32) + send.astype(F32)

    other_qkv_1 = swap_section(qkv_1)
    qkv_grad = jnp.where(section == 0, qkv_0, qkv_1.astype(F32) + other_qkv_1.astype(F32))
    out_grad = jnp.where(section == 0, out_0, out_1)
    up_grad = finish(up_0, up_1)
    other_down_1 = swap_section(down_1)
    down_grad = jnp.where(section == 0, down_0, down_1.astype(F32) + other_down_1.astype(F32))
    gains = lax.dynamic_slice_in_dim(gains, 2 * section, 2, 0)
    return (
        layer_out[None],
        input_out[None],
        gains[0:1],
        qkv_grad.reshape(qkv_weight.shape),
        out_grad.reshape(out_weight.shape),
        gains[1:2],
        up_grad[None],
        down_grad[None],
    )


def solution(mesh):
    return jax.shard_map(
        shards,
        mesh=mesh,
        in_specs=(
            P(None, ("dp", "tensor"), None),
            P(None, "dp"),
            P(None, ("dp", "tensor"), None),
            P("section", None),
            P("section", "dp", "tensor", None),
            P("section", "tensor", None, "dp"),
            P("section", None),
            P("section", "dp", "tensor"),
            P("section", "tensor", "dp"),
        ),
        out_specs=(
            P("section", None, ("dp", "tensor"), None),
            P("section", None, ("dp", "tensor"), None),
            P("section", None),
            P("section", "dp", "tensor", None),
            P("section", "tensor", None, "dp"),
            P("section", None),
            P("section", "dp", "tensor"),
            P("section", "tensor", "dp"),
        ),
        check_vma=False,
    )
```

```python
import functools
import math

import jax
import jax.numpy as jnp
from jax import lax
from jax.experimental import pallas as pl
from jax.experimental.pallas import tpu as pltpu
from jax.sharding import PartitionSpec as P

F32 = jnp.float32
BF = jnp.bfloat16
NT = (((1,), (1,)), ((), ()))
NN = (((1,), (0,)), ((), ()))
TN = (((0,), (0,)), ((), ()))
MASKED = -1e30
SCENES = 3
MESH = pl.DeviceIdType.MESH
VM = pl.BlockSpec(memory_space=pltpu.VMEM)
HB = pl.BlockSpec(memory_space=pl.ANY)
DMA = pltpu.SemaphoreType.DMA
LIMIT = 58 << 20


def dg(a, b, dims):
    return lax.dot_general(a, b, dims, preferred_element_type=F32)


def chunks(rows):
    return 4 if rows % 64 == 0 else 1


def thin_chunks(rows):
    return 8 if rows % 128 == 0 else chunks(rows)


def shape(dims, dtype):
    return jax.ShapeDtypeStruct(dims, dtype)


class Group:
    def __init__(self, size):
        self.size = size
        self.chips = size // 2
        self.me = lax.axis_index("tensor")
        self.chip = lax.div(self.me, 2)
        self.core = lax.rem(self.me, 2)
        self.sibling = self.chip * 2 + 1 - self.core

    def ahead(self, k):
        return lax.rem(self.chip + k, self.chips)

    def behind(self, k):
        return lax.rem(self.chip + self.chips - k, self.chips)

    def greet(self, replicas=0, side=False):
        barrier = pltpu.get_barrier_semaphore()
        targets = [self.sibling] + [self.ahead(k) * 2 + self.core for k in range(1, self.chips)]
        targets = [{"tensor": target} for target in targets]
        if replicas:
            d = lax.axis_index("dp")
            targets += [{"dp": lax.rem(d + k, replicas)} for k in range(1, replicas)]
        if replicas or side:
            targets += [{"section": 1 - lax.axis_index("section")}]
        for target in targets:
            pl.semaphore_signal(barrier, inc=1, device_id=target, device_id_type=MESH)
        pl.semaphore_wait(barrier, len(targets))


def remote(src, dst, send, recv, target):
    return pltpu.make_async_remote_copy(
        src_ref=src,
        dst_ref=dst,
        send_sem=send,
        recv_sem=recv,
        device_id={"tensor": target},
        device_id_type=MESH,
    )


def span(j, rc):
    return pl.ds(pl.multiple_of(j * rc, rc), rc)


def comm_sems(group_size, n):
    c = group_size // 2
    far, near = DMA((max(c - 1, 1), n)), DMA((c, n))
    return [far, far, near, near]


class Gather:
    def __init__(self, g, buf, rc, sems):
        self.g, self.buf, self.rc = g, buf, rc
        self.far_send, self.far_recv, self.near_send, self.near_recv = sems

    def far(self, k, j, origin, target, src=None):
        ref = self.buf.at[origin, span(j, self.rc)]
        src = ref if src is None else src
        return remote(src, ref, self.far_send.at[k - 1, j], self.far_recv.at[k - 1, j], target)

    def near(self, k, j, origin, src=None):
        ref = self.buf.at[origin, span(j, self.rc)]
        src = ref if src is None else src
        return remote(
            src, ref, self.near_send.at[k, j], self.near_recv.at[k, j], self.g.sibling
        )

    def start(self, j, src=None):
        g = self.g
        for k in range(1, g.chips):
            self.far(k, j, g.me, g.ahead(k) * 2 + g.core, src).start()
        self.near(0, j, g.me, src).start()

    def relay(self, j):
        g = self.g
        for k in range(1, g.chips):
            origin = g.behind(k) * 2 + g.core
            self.far(k, j, origin, g.me).wait_recv()
            self.near(k, j, origin).start()

    def ready(self, j):
        g = self.g
        self.near(0, j, g.sibling).wait_recv()
        for k in range(1, g.chips):
            self.near(k, j, g.behind(k) * 2 + 1 - g.core).wait_recv()

    def drain(self, n):
        g = self.g

        def one(j, _):
            for k in range(1, g.chips):
                self.far(k, j, g.me, g.sibling).wait_send()
            for k in range(g.chips):
                self.near(k, j, g.me).wait_send()
            return 0

        lax.fori_loop(0, n, one, 0)


def scatter_scratch(group_size, rows, width, n):
    c = group_size // 2
    far = pltpu.VMEM((max(c - 1, 1), rows, width), BF)
    near = pltpu.VMEM((c, rows, width), BF)
    return [pltpu.VMEM((group_size, rows, width), F32), near, near, far, far] + comm_sems(
        group_size, n
    )


class Scatter:
    def __init__(self, g, rc, scratch):
        self.g, self.rc = g, rc
        self.part, self.near_out, self.near_in, self.far_out, self.far_in = scratch[:5]
        self.far_send, self.far_recv, self.near_send, self.near_recv = scratch[5:]

    def near(self, k, j):
        rows = span(j, self.rc)
        return remote(
            self.near_out.at[k, rows],
            self.near_in.at[k, rows],
            self.near_send.at[k, j],
            self.near_recv.at[k, j],
            self.g.sibling,
        )

    def far(self, k, j):
        rows = span(j, self.rc)
        return remote(
            self.far_out.at[k - 1, rows],
            self.far_in.at[k - 1, rows],
            self.far_send.at[k - 1, j],
            self.far_recv.at[k - 1, j],
            self.g.ahead(k) * 2 + self.g.core,
        )

    def first(self, j):
        g, rows = self.g, span(j, self.rc)
        for k in list(range(1, g.chips)) + [0]:
            owner = g.ahead(k) * 2 + 1 - g.core
            self.near_out[k, rows, :] = self.part[owner, rows, :].astype(BF)
            self.near(k, j).start()

    def second(self, j):
        g, rows = self.g, span(j, self.rc)
        for k in range(1, g.chips):
            owner = g.ahead(k) * 2 + g.core
            self.near(k, j).wait_recv()
            both = self.part[owner, rows, :] + self.near_in[k, rows, :].astype(F32)
            self.far_out[k - 1, rows, :] = both.astype(BF)
            self.far(k, j).start()

    def third(self, j):
        g, rows = self.g, span(j, self.rc)
        self.near(0, j).wait_recv()
        total = self.part[g.me, rows, :] + self.near_in[0, rows, :].astype(F32)
        for k in range(1, g.chips):
            self.far(k, j).wait_recv()
            total = total + self.far_in[k - 1, rows, :].astype(F32)
        return total

    def drain(self, n):
        g = self.g

        def one(j, _):
            for k in range(1, g.chips):
                self.far(k, j).wait_send()
            for k in range(g.chips):
                self.near(k, j).wait_send()
            return 0

        lax.fori_loop(0, n, one, 0)


def far_copy(src, dst, send, recv, target):
    return pltpu.make_async_remote_copy(
        src_ref=src,
        dst_ref=dst,
        send_sem=send,
        recv_sem=recv,
        device_id=target,
        device_id_type=MESH,
    )


class Swap:
    def __init__(self, src, stage, sems):
        self.src, self.stage, self.sems = src, stage, sems
        self.s = lax.axis_index("section")

    def copies(self, layer):
        local = pltpu.make_async_copy(self.src.at[self.s], self.stage.at[self.s], self.sems.at[0])
        side = far_copy(
            self.src.at[1 - self.s],
            self.stage.at[layer],
            self.sems.at[1],
            self.sems.at[2],
            {"section": 1 - self.s},
        )
        return local, side

    def start(self):
        for copy in self.copies(self.s):
            copy.start()

    def arrive(self):
        local, side = self.copies(1 - self.s)
        local.wait()
        side.wait_recv()

    def finish(self):
        self.copies(self.s)[1].wait_send()


def reduce_scratch(replicas, rows, cols):
    many = pltpu.VMEM((replicas - 1, rows, cols), BF)
    one = pltpu.VMEM((rows, cols), BF)
    far, side = DMA((replicas - 1, 2)), DMA((2,))
    return [pltpu.VMEM((rows, cols), F32), many, many, one, one, far, far, side, side]


class Reduce:
    def __init__(self, layer, scratch):
        self.layer = layer
        self.own, self.away, self.came, self.over, self.back = scratch[:5]
        self.z_send, self.z_recv, self.y_send, self.y_recv = scratch[5:]
        self.replicas = self.away.shape[0] + 1
        self.half = self.own.shape[0] // 2
        self.d = lax.axis_index("dp")
        self.s = lax.axis_index("section")

    def target(self, k):
        return lax.rem(self.d + k, self.replicas)

    def part(self, i):
        return pl.ds(pl.multiple_of(i * self.half, self.half), self.half)

    def z_copy(self, k, i):
        part = self.part(i)
        return far_copy(
            self.away.at[k - 1, part],
            self.came.at[k - 1, part],
            self.z_send.at[k - 1, i],
            self.z_recv.at[k - 1, i],
            {"dp": self.target(k)},
        )

    def y_copy(self, i):
        part = self.part(i)
        return far_copy(
            self.over.at[part],
            self.back.at[part],
            self.y_send.at[i],
            self.y_recv.at[i],
            {"section": 1 - self.s},
        )

    def send(self, block):
        def one(i):
            k = i + 1
            self.away[i] = block(self.target(k)).astype(BF)
            self.z_copy(k, 0).start()
            self.z_copy(k, 1).start()

        run(self.replicas - 1, one)
        self.own[...] = block(self.d)

    def collect(self):
        def one(i):
            part = self.part(i)
            total = self.own[part, :]
            for k in range(1, self.replicas):
                self.z_copy(k, i).wait_recv()
                total = total + self.came[k - 1, part, :].astype(F32)
            self.own[part, :] = total
            self.over[part, :] = total.astype(BF)

            @pl.when(self.s != self.layer)
            def _():
                self.y_copy(i).start()

        run(2, one)

    def finish(self, out):
        @pl.when(self.s == self.layer)
        def _():
            self.y_copy(0).wait_recv()
            self.y_copy(1).wait_recv()
            out[...] = self.own[...] + self.back[...].astype(F32)

        @pl.when(self.s != self.layer)
        def _():
            self.y_copy(0).wait_send()
            self.y_copy(1).wait_send()
            out[...] = self.own[...]

        for k in range(1, self.replicas):
            self.z_copy(k, 0).wait_send()
            self.z_copy(k, 1).wait_send()


class HalfSwap:
    def __init__(self, src, came, sems):
        self.src, self.came, self.sems = src, came, sems
        self.s = lax.axis_index("section")
        self.rows = came.shape[1]

    def copy(self):
        at = pl.ds(pl.multiple_of((1 - self.s) * self.rows, self.rows), self.rows)
        return far_copy(
            self.src.at[:, at],
            self.came,
            self.sems.at[0],
            self.sems.at[1],
            {"section": 1 - self.s},
        )


def half_scratch(replicas, rows, cols):
    rows = rows // 2
    all_, far = pltpu.VMEM((replicas, rows, cols), BF), pltpu.VMEM((replicas - 1, rows, cols), BF)
    one = pltpu.VMEM((rows, cols), BF)
    z = DMA((replicas - 1,))
    return [all_, all_, far, far, pltpu.VMEM((rows, cols), F32), one, one, DMA((3,)), z, z, DMA((2,))]


HALF = 11


class HalfReduce:
    def __init__(self, layer, scratch):
        self.layer = layer
        self.mine, self.other, self.away, self.came, self.own, self.over, self.back = scratch[:7]
        self.in_sem, self.z_send, self.z_recv, self.y_sem = scratch[7:]
        self.replicas, self.rows = self.mine.shape[:2]
        self.s = lax.axis_index("section")
        self.d = lax.axis_index("dp")

    def half(self, s):
        return pl.ds(pl.multiple_of(s * self.rows, self.rows), self.rows)

    def loads(self, src, other):
        loads = [pltpu.make_async_copy(src.at[:, self.half(self.s)], self.mine, self.in_sem.at[0])]
        if other is not None:
            loads.append(pltpu.make_async_copy(other, self.other, self.in_sem.at[1]))
        return loads

    def z_copy(self, k):
        return far_copy(
            self.away.at[k - 1],
            self.came.at[k - 1],
            self.z_send.at[k - 1],
            self.z_recv.at[k - 1],
            {"dp": lax.rem(self.d + k, self.replicas)},
        )

    def y_copy(self):
        return far_copy(
            self.over, self.back, self.y_sem.at[0], self.y_sem.at[1], {"section": 1 - self.s}
        )

    def middle(self):
        def both(z):
            return self.mine[z].astype(F32) + self.other[z].astype(F32)

        for k in range(1, self.replicas):
            self.away[k - 1] = both(lax.rem(self.d + k, self.replicas)).astype(BF)
            self.z_copy(k).start()
        self.own[...] = both(self.d)

    def late(self):
        total = self.own[...]
        for k in range(1, self.replicas):
            self.z_copy(k).wait_recv()
            total = total + self.came[k - 1].astype(F32)
        self.own[...] = total
        self.over[...] = total.astype(BF)

        @pl.when(self.s != self.layer)
        def _():
            self.y_copy().start()

    def finish(self, out, above=None):
        @pl.when(self.s == self.layer)
        def _():
            self.y_copy().wait_recv()
            out[self.half(self.s), :] = self.own[...]
            out[self.half(1 - self.s), :] = self.back[...].astype(F32)

        @pl.when(self.s != self.layer)
        def _():
            if above is None:
                out[...] = jnp.zeros_like(out)
            else:
                copy = pltpu.make_async_copy(above, out, self.in_sem.at[2])
                copy.start()
                copy.wait()
            self.y_copy().wait_send()

        for k in range(1, self.replicas):
            self.z_copy(k).wait_send()


class Spread:
    def __init__(self, src, dst, by_columns, sems):
        self.src, self.dst, self.by_columns = src, dst, by_columns
        self.own_sem, self.far_send, self.far_recv, self.side_send, self.side_recv = sems
        self.replicas = far = self.side_send.shape[0]
        self.s = lax.axis_index("section")
        self.d = lax.axis_index("dp")
        self.stages = [
            sorted({k, far - k}) for k in range(1, far // 2 + 1)
        ]

    def place(self, half, z):
        rows, cols = self.src.shape
        if self.by_columns:
            return self.dst.at[
                pl.ds(pl.multiple_of(half * rows, rows), rows),
                pl.ds(pl.multiple_of(z * cols, cols), cols),
            ]
        return self.dst.at[pl.ds(pl.multiple_of((2 * z + half) * rows, rows), rows)]

    def origin(self, k):
        return lax.rem(self.d + self.replicas - k, self.replicas)

    def own(self):
        return pltpu.make_async_copy(self.src, self.place(self.s, self.d), self.own_sem.at[0])

    def far(self, k, origin):
        return pltpu.make_async_remote_copy(
            src_ref=self.src,
            dst_ref=self.place(self.s, origin),
            send_sem=self.far_send.at[k - 1],
            recv_sem=self.far_recv.at[k - 1],
            device_id={"dp": lax.rem(self.d + k, self.replicas)},
            device_id_type=MESH,
        )

    def side(self, k, half):
        place = self.place(half, self.origin(k))
        return pltpu.make_async_remote_copy(
            src_ref=self.src if k == 0 else place,
            dst_ref=place,
            send_sem=self.side_send.at[k],
            recv_sem=self.side_recv.at[k],
            device_id={"section": 1 - self.s},
            device_id_type=MESH,
        )

    def start(self):
        for k in self.stages[0]:
            self.far(k, self.d).start()
        self.side(0, self.s).start()
        self.own().start()

    def step(self, i):
        for k in self.stages[i]:
            self.far(k, self.origin(k)).wait_recv()
            self.side(k, self.s).start()
        if i + 1 < len(self.stages):
            for k in self.stages[i + 1]:
                self.far(k, self.d).start()

    def finish(self):
        self.own().wait()
        for k in range(self.replicas):
            self.side(k, 1 - self.s).wait_recv()
        for k in range(1, self.replicas):
            self.far(k, self.d).wait_send()
        for k in range(self.replicas):
            self.side(k, self.s).wait_send()


class ZGather:
    def __init__(self, src, got, sems):
        self.src, self.got = src, got
        self.own_sem, self.send, self.recv = sems
        self.replicas = got.shape[0]
        self.d = lax.axis_index("dp")

    def own(self):
        return pltpu.make_async_copy(self.src, self.got.at[self.d], self.own_sem.at[0])

    def far(self, k, origin):
        return far_copy(
            self.src,
            self.got.at[origin],
            self.send.at[k - 1],
            self.recv.at[k - 1],
            {"dp": lax.rem(self.d + k, self.replicas)},
        )

    def start(self):
        for k in range(1, self.replicas):
            self.far(k, self.d).start()
        self.own().start()

    def step(self, i):
        pass

    def finish(self):
        self.own().wait()
        for k in range(1, self.replicas):
            self.far(k, lax.rem(self.d + self.replicas - k, self.replicas)).wait_recv()
        for k in range(1, self.replicas):
            self.far(k, self.d).wait_send()


class YJoin:
    def __init__(self, got, dst, by_columns, sems):
        self.src, self.dst, self.by_columns = got, dst, by_columns
        self.own_sem, self.send, self.recv, self.got, self.in_sem = sems
        self.replicas, self.rows, self.cols = got.shape
        self.s = lax.axis_index("section")

    def place(self, half, z):
        rows, cols = self.rows, self.cols
        if self.by_columns:
            return self.dst.at[
                pl.ds(pl.multiple_of(half * rows, rows), rows), pl.ds(z * cols, cols)
            ]
        return self.dst.at[pl.ds(pl.multiple_of((2 * z + half) * rows, rows), rows)]

    def own(self, z):
        return pltpu.make_async_copy(self.got.at[z], self.place(self.s, z), self.own_sem.at[z])

    def side(self, z, half):
        return far_copy(
            self.got.at[z],
            self.place(half, z),
            self.send.at[z],
            self.recv.at[z],
            {"section": 1 - self.s},
        )

    def start(self):
        load = pltpu.make_async_copy(self.src, self.got, self.in_sem.at[0])
        load.start()
        load.wait()
        for z in range(self.replicas):
            self.side(z, self.s).start()
            self.own(z).start()

    def step(self, i):
        pass

    def finish(self):
        for z in range(self.replicas):
            self.own(z).wait()
            self.side(z, 1 - self.s).wait_recv()
        for z in range(self.replicas):
            self.side(z, self.s).wait_send()


def rider_sems(replicas):
    far, side = DMA((replicas - 1,)), DMA((replicas,))
    return [DMA((1,)), far, far, side, side]


class Riders:
    def __init__(self, srcs, dsts, columns, sems):
        self.all = []
        for src, dst, (kind, layer, by) in zip(srcs, dsts, columns):
            count = 3 if kind == "z" else 5
            own, sems = sems[:count], sems[count:]
            if kind == "spread":
                self.all.append(Spread(src.at[layer], dst, by, own))
            elif kind == "z":
                self.all.append(ZGather(src.at[layer], dst, own))
            else:
                self.all.append(YJoin(src, dst, by, own))
        self.replicas = self.all[0].replicas if self.all else 0

    def start(self):
        for one in self.all:
            one.start()

    def step(self, j, n):
        if not self.all:
            return
        stages = self.replicas // 2
        for i in range(stages):

            @pl.when(j == n * (i + 1) // stages - 1)
            def _(i=i):
                for one in self.all:
                    one.step(i)

    def finish(self):
        for one in self.all:
            one.finish()


def riding(riders, replicas):
    arrays = [array for array, _, _, _ in riders]
    columns = tuple(rider[1:] for rider in riders)
    outs, sems = [], []
    for array, kind, _, by in riders:
        rows, cols = array.shape[1:]
        if kind == "z":
            outs.append(shape((replicas, rows, cols), BF))
        else:
            outs.append(
                shape((2 * rows, replicas * cols) if by else (2 * replicas * rows, cols), BF)
            )
        far, side = DMA((replicas - 1,)), DMA((replicas,))
        sems += {
            "spread": rider_sems(replicas),
            "z": [DMA((1,)), far, far],
            "y": [side, side, side, pltpu.VMEM(array.shape, BF), DMA((1,))],
        }[kind]
    return arrays, columns, outs, sems


def params(key):
    return pltpu.CompilerParams(
        vmem_limit_bytes=LIMIT, collective_id=key, has_side_effects=True
    )


def cost(flops, moved, exps=0):
    return pl.CostEstimate(flops=int(flops), bytes_accessed=int(moved), transcendentals=int(exps))


def normed(source):
    center = source - jnp.mean(source, axis=-1, keepdims=True)
    r = lax.rsqrt(jnp.mean(center * center, axis=-1, keepdims=True) + 1e-05)
    return center * r, r


def normed_back(source, gain, grad):
    n, r = normed(source)
    e = grad * gain
    dh = r * (
        e - jnp.mean(e, axis=-1, keepdims=True) - n * jnp.mean(e * n, axis=-1, keepdims=True)
    )
    return dh, jnp.sum(grad * n, axis=0, keepdims=True)


def flat(value):
    return value.reshape((value.shape[0] * value.shape[1],) + value.shape[2:])


def run(n, body):
    def one(j, carry):
        body(j)
        return carry

    lax.fori_loop(0, n, one, 0)


def first_kernel(
    size, replicas, x_ref, gain_ref, wq_ref, wo_ref, wu_ref, wd_ref,
    qkv_ref, gains_out, a1_out, wq_out, wo_out, q_stage, o_stage, u_stage, d_stage,
    a1, w, gains, own_sem, q_sem, o_sem, u_sem, d_sem, gain_sem, *sems
):
    rows, width = x_ref.shape
    n = thin_chunks(rows)
    rc = rows // n
    g = Group(size)
    section = lax.axis_index("section")
    gather = Gather(g, a1, rc, sems[:4])
    swaps = [
        Swap(wq_ref, q_stage, q_sem),
        Swap(wo_ref, o_stage, o_sem),
        Swap(wu_ref, u_stage, u_sem),
        Swap(wd_ref, d_stage, d_sem),
    ]
    spreads = [
        Spread(q_stage.at[0], w, False, sems[4:9]),
        Spread(o_stage.at[0], wo_out, True, sems[9:14]),
    ]
    riders = Riders([], [], (), [])
    riders.all = spreads
    riders.replicas = replicas
    g.greet(replicas)

    def gain_copy(layer):
        return far_copy(
            gain_ref, gains.at[layer], gain_sem.at[0], gain_sem.at[1], {"section": 1 - section}
        )

    gain_copy(section).start()
    swaps[0].start()
    swaps[1].start()
    gains[section] = gain_ref[...]
    gain_copy(1 - section).wait_recv()
    gains_out[...] = gains[...]

    def send(j):
        at = span(j, rc)
        a = normed(x_ref[at, :].astype(F32))[0] * gains[0, 0:1, :]
        a1[g.me, at, :] = a.astype(BF)
        gather.start(j)

    run(n, send)
    swaps[0].arrive()
    swaps[1].arrive()
    riders.start()
    swaps[2].start()
    swaps[3].start()

    def relay(j):
        gather.relay(j)
        riders.step(j, n)

    run(n, relay)
    riders.finish()
    outs = [
        pltpu.make_async_copy(w, wq_out, own_sem.at[0]),
        pltpu.make_async_copy(a1, a1_out, own_sem.at[1]),
    ]
    outs[0].start()

    def multiply(j):
        at = span(j, rc)
        gather.ready(j)
        r = dg(flat(a1[:, at, :]), w[...], NN).astype(BF)
        qkv_ref[:, at, :] = r.reshape(size, rc, r.shape[1])

    run(n, multiply)
    outs[1].start()
    swaps[2].arrive()
    swaps[3].arrive()
    for swap in swaps:
        swap.finish()
    gain_copy(section).wait_send()
    gather.drain(n)
    for out in outs:
        out.wait()


def first_forward(size, replicas, x, gains, ws):
    rows, width = x.shape
    wide = ws[0].shape[2]
    deep = 2 * ws[1].shape[1]
    n = thin_chunks(rows)
    return pl.pallas_call(
        functools.partial(first_kernel, size, replicas),
        out_shape=[
            shape((size, rows, wide), BF),
            shape((2,) + gains.shape, F32),
            shape((size, rows, width), BF),
            shape((width, wide), BF),
            shape((deep, width), BF),
        ]
        + [shape(w.shape, BF) for w in ws],
        in_specs=[VM] * 6,
        out_specs=[VM, VM] + [HB] * 7,
        scratch_shapes=[
            pltpu.VMEM((size, rows, width), BF),
            pltpu.VMEM((width, wide), BF),
            pltpu.VMEM((2,) + gains.shape, F32),
            DMA((2,)),
            DMA((3,)),
            DMA((3,)),
            DMA((3,)),
            DMA((3,)),
            DMA((2,)),
        ]
        + comm_sems(size, n)
        + rider_sems(replicas) * 2,
        compiler_params=params(0),
        cost_estimate=cost(30e9, 30e6),
    )(x, gains, *ws)


def attend_kernel(size, layer, columns, *refs):
    m = len(columns)
    qkv_ref, qm_ref, km_ref, x_ref, w_ref = refs[:5]
    refs = refs[5:]
    if layer == 1:
        cot_ref, refs = refs[0], refs[1:]
    halves, refs = refs[:m], refs[m:]
    h1_ref, ctx_ref, lse_ref = refs[:3]
    refs = refs[3:]
    if layer == 1:
        cot_out, refs = refs[0], refs[1:]
    wholes, refs = refs[:m], refs[m:]
    ka, vt, w, w_sem = refs[:4]
    scratch, refs = refs[4:13], refs[13:]
    if layer == 1:
        cot_sems, cot_sem, refs = refs[:4], refs[4], refs[5:]
    riders = Riders(halves, wholes, columns, refs)
    _, rows, wide = qkv_ref.shape
    length = size * rows
    e = qm_ref.shape[2]
    heads = wide // (3 * e)
    c = e**-0.5 * math.log2(math.e)
    n = chunks(rows)
    rc = rows // n
    bq = size * rc
    kc = bq
    g = Group(size)
    copy = pltpu.make_async_copy(w_ref, w, w_sem.at[0])
    copy.start()
    g.greet(riders.replicas)
    riders.start()
    if layer == 1:
        cot = Gather(g, cot_out, rows, cot_sems)
        own = pltpu.make_async_copy(cot_ref, cot_out.at[g.me], cot_sem.at[0])
        own.start()
        cot.start(0, cot_ref)
    scatter = Scatter(g, rc, scratch)
    whole = flat(qkv_ref[...])
    for h in range(heads):
        o = 3 * e * h
        ka[h, :, :e] = whole[:, o + e : o + 2 * e]
        ka[h, :, e:] = flat(km_ref[...])
        vt[h, :e, :] = whole[:, o + 2 * e : o + 3 * e].T
        vt[h, e:, :] = jnp.ones((16, length), BF)
    copy.wait()

    def work(j):
        at = span(j, rc)
        qm = flat(qm_ref[:, at, :])
        found = []
        held_qkv = flat(qkv_ref[:, at, :])
        for h in range(heads):
            o = 3 * e * h
            q = jnp.concatenate([held_qkv[:, o : o + e], qm], axis=1)
            held = []
            top = None
            for k in range(length // kc):
                s = dg(ka[h, k * kc : (k + 1) * kc, :], q, NT)
                t = jnp.max(s, axis=0, keepdims=True)
                top = t if top is None else jnp.maximum(top, t)
                held.append(s)
            top = top * c
            acc = None
            for k in range(length // kc):
                p = jnp.exp2(held[k] * c - top).astype(BF)
                a = dg(vt[h, :, k * kc : (k + 1) * kc], p, NN)
                acc = a if acc is None else acc + a
            total = acc[e : e + 1]
            found.append((acc[:e] * (1.0 / total)).astype(BF))
            lse_ref[j, h : h + 1, :] = top + jnp.log2(total)
        ctx = (jnp.concatenate(found, axis=0) if heads > 1 else found[0]).T
        ctx_ref[:, at, :] = ctx.reshape(size, rc, heads * e)
        width = x_ref.shape[1]
        scatter.part[:, at, :] = dg(ctx, w[...], NN).reshape(size, rc, width)
        scatter.first(j)
        scatter.second(j)
        riders.step(j, n)
        if layer == 1:

            @pl.when(j == n - 1)
            def _():
                cot.relay(0)

    run(n, work)

    def last(j):
        at = span(j, rc)
        h1_ref[at, :] = x_ref[at, :].astype(F32) + scatter.third(j)

    run(n, last)
    scatter.drain(n)
    if layer == 1:
        cot.ready(0)
        cot.drain(1)
        own.wait()
    riders.finish()


def attend(size, replicas, layer, qkv, qm, km, x, w, riders, cot=()):
    _, rows, wide = qkv.shape
    e = qm.shape[2]
    heads = wide // (3 * e)
    width = x.shape[1]
    n = chunks(rows)
    halves, columns, outs, sems = riding(riders, replicas)
    return pl.pallas_call(
        functools.partial(attend_kernel, size, layer, columns),
        out_shape=[
            shape((rows, width), F32),
            shape((size, rows, heads * e), BF),
            shape((n, heads, size * rows // n), F32),
        ]
        + [shape((size, rows, width), BF) for _ in cot]
        + outs,
        in_specs=[VM, VM, VM, VM, HB] + [VM] * len(cot) + [HB] * len(riders),
        out_specs=[VM, VM, VM] + [HB] * (len(cot) + len(outs)),
        scratch_shapes=[
            pltpu.VMEM((heads, size * rows, 2 * e), BF),
            pltpu.VMEM((heads, e + 16, size * rows), BF),
            pltpu.VMEM((heads * e, width), BF),
            DMA((1,)),
        ]
        + scatter_scratch(size, rows, width, n)
        + (comm_sems(size, 1) + [DMA((1,))]) * len(cot)
        + sems,
        compiler_params=params(2 + layer),
        cost_estimate=cost(60e9, 20e6),
    )(qkv, qm, km, x, w, *cot, *halves)


def mlp_kernel(size, layer, columns, *refs):
    m = len(columns)
    h1_ref, gain_ref, wu_ref, wd_ref = refs[:4]
    halves, refs = refs[4 : 4 + m], refs[4 + m :]
    y_ref, a2_out, hid_out, slope_out = refs[:4]
    wholes, refs = refs[4 : 4 + m], refs[4 + m :]
    a2, hid, slope, wu, wd, w_sem, out_sem = refs[:7]
    scratch, refs = refs[7:20], refs[20:]
    riders = Riders(halves, wholes, columns, refs)
    rows, width = h1_ref.shape
    hidden = wu_ref.shape[1]
    fb = min(256, hidden)
    n = chunks(rows)
    rc = rows // n
    g = Group(size)
    copies = [
        pltpu.make_async_copy(wu_ref, wu, w_sem.at[0]),
        pltpu.make_async_copy(wd_ref, wd, w_sem.at[1]),
    ]
    for copy in copies:
        copy.start()
    g.greet(riders.replicas)
    gather = Gather(g, a2, rc, scratch[:4])
    scatter = Scatter(g, rc, scratch[4:])

    def send(j):
        at = span(j, rc)
        a = normed(h1_ref[at, :])[0] * gain_ref[layer, 1:2, :]
        a2[g.me, at, :] = a.astype(BF)
        gather.start(j)

    run(n, send)
    riders.start()
    for copy in copies:
        copy.wait()

    def work(j):
        at = span(j, rc)
        gather.relay(j)
        gather.ready(j)
        a = flat(a2[:, at, :])
        for f in range(hidden // fb):
            cols = slice(f * fb, (f + 1) * fb)
            u = dg(a, wu[:, cols], NN)
            half = 0.5 + 0.5 * lax.erf(u * (0.5**0.5))
            slope[:, at, cols] = (
                (half + u * jnp.exp(-0.5 * u * u) * ((2 * math.pi) ** -0.5))
                .astype(BF)
                .reshape(size, rc, fb)
            )
            hid[:, at, cols] = (u * half).astype(BF).reshape(size, rc, fb)
        held = flat(hid[:, at, :])
        for f in range(width // 256):
            cols = slice(f * 256, (f + 1) * 256)
            scatter.part[:, at, cols] = dg(held, wd[:, cols], NN).reshape(size, rc, 256)
        scatter.first(j)
        scatter.second(j)
        riders.step(j, n)

    run(n, work)
    outs = [
        pltpu.make_async_copy(a2, a2_out, out_sem.at[0]),
        pltpu.make_async_copy(hid, hid_out, out_sem.at[1]),
        pltpu.make_async_copy(slope, slope_out, out_sem.at[2]),
    ]
    for out in outs:
        out.start()

    def last(j):
        at = span(j, rc)
        y_ref[at, :] = (h1_ref[at, :] + scatter.third(j)).astype(BF)

    run(n, last)
    riders.finish()
    gather.drain(n)
    scatter.drain(n)
    for out in outs:
        out.wait()


def mlp_forward(size, replicas, layer, h1, gains, wu, wd, riders):
    rows, width = h1.shape
    hidden = wu.shape[1]
    n = chunks(rows)
    halves, columns, outs, sems = riding(riders, replicas)
    return pl.pallas_call(
        functools.partial(mlp_kernel, size, layer, columns),
        out_shape=[
            shape((rows, width), BF),
            shape((size, rows, width), BF),
            shape((size, rows, hidden), BF),
            shape((size, rows, hidden), BF),
        ]
        + outs,
        in_specs=[VM, VM, HB, HB] + [HB] * len(riders),
        out_specs=[VM, HB, HB, HB] + [HB] * len(outs),
        scratch_shapes=[
            pltpu.VMEM((size, rows, width), BF),
            pltpu.VMEM((size, rows, hidden), BF),
            pltpu.VMEM((size, rows, hidden), BF),
            pltpu.VMEM((width, hidden), BF),
            pltpu.VMEM((hidden, width), BF),
            DMA((2,)),
            DMA((3,)),
        ]
        + comm_sems(size, n)
        + scatter_scratch(size, rows, width, n)
        + sems,
        compiler_params=params(4 + layer),
        cost_estimate=cost(50e9, 30e6),
    )(h1, gains, wu, wd, *halves)


def turn_kernel(size, columns, *refs):
    m = len(columns)
    h1_ref, gain_ref, wu_ref, wd_ref, q_stage = refs[:5]
    halves, refs = refs[5 : 5 + m], refs[5 + m :]
    y_ref, qkv_ref, a2_out, hid_out, slope_out, a1_out, wq_out = refs[:7]
    wholes, refs = refs[7 : 7 + m], refs[7 + m :]
    a2, hid, slope, wu, wd, a1, wq, w_sem, out_sem = refs[:9]
    gather_sems, next_sems, refs = refs[9:13], refs[13:17], refs[17:]
    scratch, refs = refs[:9], refs[9:]
    spread = Spread(q_stage.at[1], wq, False, refs[:5])
    riders = Riders(halves, wholes, columns, refs[5:])
    out_rider, up_rider, down_rider = riders.all
    stages = len(spread.stages)
    rows, width = h1_ref.shape
    hidden = wu_ref.shape[1]
    fb = min(256, hidden)
    n = thin_chunks(rows)
    rc = rows // n
    g = Group(size)
    copies = [
        pltpu.make_async_copy(wu_ref, wu, w_sem.at[0]),
        pltpu.make_async_copy(wd_ref, wd, w_sem.at[1]),
    ]
    for copy in copies:
        copy.start()
    g.greet(spread.replicas)
    gather = Gather(g, a2, rc, gather_sems)
    onward = Gather(g, a1, rc, next_sems)
    scatter = Scatter(g, rc, scratch)

    def send(j):
        at = span(j, rc)
        a = normed(h1_ref[at, :])[0] * gain_ref[0, 1:2, :]
        a2[g.me, at, :] = a.astype(BF)
        gather.start(j)

    run(n, send)
    spread.start()
    out_rider.start()
    for copy in copies:
        copy.wait()

    def pass_on(j):
        at = span(j, rc)
        y = (h1_ref[at, :] + scatter.third(j)).astype(BF)
        y_ref[at, :] = y
        a = normed(y.astype(F32))[0] * gain_ref[1, 0:1, :]
        a1[g.me, at, :] = a.astype(BF)
        onward.start(j)

    lag = min(2, n)

    def work(j):
        at = span(j, rc)
        gather.relay(j)
        gather.ready(j)
        a = flat(a2[:, at, :])
        for f in range(hidden // fb):
            cols = slice(f * fb, (f + 1) * fb)
            u = dg(a, wu[:, cols], NN)
            half = 0.5 + 0.5 * lax.erf(u * (0.5**0.5))
            slope[:, at, cols] = (
                (half + u * jnp.exp(-0.5 * u * u) * ((2 * math.pi) ** -0.5))
                .astype(BF)
                .reshape(size, rc, fb)
            )
            hid[:, at, cols] = (u * half).astype(BF).reshape(size, rc, fb)
        held = flat(hid[:, at, :])
        for f in range(width // 256):
            cols = slice(f * 256, (f + 1) * 256)
            scatter.part[:, at, cols] = dg(held, wd[:, cols], NN).reshape(size, rc, 256)
        scatter.first(j)
        scatter.second(j)

        @pl.when(j >= lag)
        def _():
            pass_on(j - lag)

        @pl.when(j == 3 * n // 8)
        def _():
            spread.step(0)
            out_rider.step(0)
            up_rider.start()

        @pl.when(j == n - 1)
        def _():
            for i in range(1, stages):
                spread.step(i)
                out_rider.step(i)
            up_rider.step(0)
            down_rider.start()

    run(n, work)
    outs = [
        pltpu.make_async_copy(a2, a2_out, out_sem.at[0]),
        pltpu.make_async_copy(hid, hid_out, out_sem.at[1]),
        pltpu.make_async_copy(slope, slope_out, out_sem.at[2]),
    ]
    for out in outs:
        out.start()
    for j in range(n - lag, n):
        pass_on(j)
    spread.finish()
    outs.append(pltpu.make_async_copy(wq, wq_out, out_sem.at[3]))
    outs[3].start()

    def multiply(j):
        at = span(j, rc)
        onward.relay(j)
        onward.ready(j)
        r = dg(flat(a1[:, at, :]), wq[...], NN).astype(BF)
        qkv_ref[:, at, :] = r.reshape(size, rc, r.shape[1])

    run(n, multiply)
    outs.append(pltpu.make_async_copy(a1, a1_out, out_sem.at[4]))
    outs[4].start()
    for i in range(1, stages):
        up_rider.step(i)
    riders.finish()
    gather.drain(n)
    onward.drain(n)
    scatter.drain(n)
    for out in outs:
        out.wait()


def turn_forward(size, replicas, h1, gains, wu, wd, stage, riders):
    rows, width = h1.shape
    hidden = wu.shape[1]
    wide = stage.shape[2]
    n = thin_chunks(rows)
    halves, columns, outs, sems = riding(riders, replicas)
    return pl.pallas_call(
        functools.partial(turn_kernel, size, columns),
        out_shape=[
            shape((rows, width), BF),
            shape((size, rows, wide), BF),
            shape((size, rows, width), BF),
            shape((size, rows, hidden), BF),
            shape((size, rows, hidden), BF),
            shape((size, rows, width), BF),
            shape((width, wide), BF),
        ]
        + outs,
        in_specs=[VM, VM] + [HB] * (3 + len(riders)),
        out_specs=[VM, VM] + [HB] * (5 + len(outs)),
        scratch_shapes=[
            pltpu.VMEM((size, rows, width), BF),
            pltpu.VMEM((size, rows, hidden), BF),
            pltpu.VMEM((size, rows, hidden), BF),
            pltpu.VMEM((width, hidden), BF),
            pltpu.VMEM((hidden, width), BF),
            pltpu.VMEM((size, rows, width), BF),
            pltpu.VMEM((width, wide), BF),
            DMA((2,)),
            DMA((5,)),
        ]
        + comm_sems(size, n) * 2
        + scatter_scratch(size, rows, width, n)
        + rider_sems(replicas)
        + sems,
        compiler_params=params(4),
        cost_estimate=cost(50e9, 30e6),
    )(h1, gains, wu, wd, stage, *halves)


def mlp_back_kernel(size, layer, parts, *refs):
    g_ref, h1_ref, gain_ref, a2_ref, hid_ref, slope_ref, wu_ref, wd_ref = refs[:8]
    refs = refs[8:]
    if layer == 1:
        ys, whole_ref, refs = refs[:2], refs[2], refs[3:]
    mid_ref, gain_out, gup_ref, gdown_ref = refs[:4]
    refs = refs[4:]
    if layer == 1:
        y_out, refs = refs[0], refs[1:]
    grad, a2, hid, dup, wu, wd, w_sem = refs[:7]
    scratch, refs = refs[7:20], refs[20:]
    rows, width = h1_ref.shape
    hidden = wu_ref.shape[1]
    depth = width // parts
    fb = min(256, hidden)
    n = chunks(rows)
    rc = rows // n
    g = Group(size)
    copies = [
        pltpu.make_async_copy(wd_ref, wd, w_sem.at[0]),
        pltpu.make_async_copy(slope_ref, dup, w_sem.at[1]),
        pltpu.make_async_copy(wu_ref, wu, w_sem.at[2]),
    ]
    late = [
        pltpu.make_async_copy(hid_ref, hid, w_sem.at[3]),
        pltpu.make_async_copy(a2_ref, a2, w_sem.at[4]),
    ]
    for copy in copies:
        copy.start()
    g.greet(side=layer == 1)
    section = lax.axis_index("section")
    if layer == 1:
        y_sem, y_own = refs

        def y_load(own):
            return pltpu.make_async_copy(own, y_own, y_sem.at[3])

        def y_copies(own, other, at):
            return (
                pltpu.make_async_copy(y_own, y_out.at[section], y_sem.at[0]),
                far_copy(
                    other, y_out.at[at], y_sem.at[1], y_sem.at[2], {"section": 1 - section}
                ),
            )

        for i in range(2):

            @pl.when(section == i)
            def _(i=i):
                y_load(ys[i]).start()
                y_copies(ys[i], ys[1 - i], section)[1].start()

    gather = Gather(g, grad, rc, scratch[:4])
    scatter = Scatter(g, rc, scratch[4:])

    def send(j):
        at = span(j, rc)
        grad[g.me, at, :] = g_ref[at, :]
        gather.start(j)

    if layer == 1:
        whole = pltpu.make_async_copy(whole_ref, grad, w_sem.at[5])
        whole.start()
        copies.append(whole)
    else:
        run(n, send)
    for copy in copies:
        copy.wait()
    for copy in late:
        copy.start()
    if layer == 1:
        y_load(ys[0]).wait()
        y_copies(ys[0], ys[1], section)[0].start()

    def work(j):
        at = span(j, rc)
        if layer == 0:
            gather.relay(j)
            gather.ready(j)
        held = flat(grad[:, at, :])
        for f in range(hidden // fb):
            cols = slice(f * fb, (f + 1) * fb)
            d = dg(held, wd[cols, :], NT) * flat(dup[:, at, cols]).astype(F32)
            dup[:, at, cols] = d.astype(BF).reshape(size, rc, fb)
        held = flat(dup[:, at, :])
        for z in range(parts):
            cols = slice(z * depth, (z + 1) * depth)
            scatter.part[:, at, cols] = dg(held, wu[cols, :], NT).reshape(size, rc, depth)
        scatter.first(j)
        scatter.second(j)

    run(n, work)
    for copy in late:
        copy.wait()

    def up_grad(z):
        cols = pl.ds(pl.multiple_of(z * depth, depth), depth)
        gup_ref[z] = dg(flat(a2[:, :, cols]), flat(dup[...]), TN).astype(BF)

    run(parts, up_grad)

    def down_grad(f):
        cols = pl.ds(pl.multiple_of(f * fb, fb), fb)
        r = dg(flat(hid[:, :, cols]), flat(grad[...]), TN).astype(BF)
        for z in range(parts):
            gdown_ref[z, cols, :] = r[:, z * depth : (z + 1) * depth]

    run(hidden // fb, down_grad)
    gain_out[...] = jnp.zeros_like(gain_out)

    def last(j):
        at = span(j, rc)
        dh, dgain = normed_back(h1_ref[at, :], gain_ref[layer, 1:2, :], scatter.third(j))
        mid_ref[at, :] = g_ref[at, :].astype(F32) + dh
        gain_out[...] += dgain

    run(n, last)
    if layer == 1:
        local, side = y_copies(ys[0], ys[1], 1 - section)
        local.wait()
        side.wait_recv()
        y_copies(ys[0], ys[1], section)[1].wait_send()
    if layer == 0:
        gather.drain(n)
    scatter.drain(n)


def mlp_backward(size, replicas, layer, grad, h1, gains, a2, hid, slope, wu, wd, extra):
    rows, width = h1.shape
    hidden = wu.shape[1]
    parts, depth = replicas, width // replicas
    n = chunks(rows)
    return pl.pallas_call(
        functools.partial(mlp_back_kernel, size, layer, parts),
        out_shape=[
            shape((rows, width), F32),
            shape((1, width), F32),
            shape((parts, depth, hidden), BF),
            shape((parts, hidden, depth), BF),
        ]
        + [shape((2, rows, width), BF)] * (len(extra) // 3),
        in_specs=[VM, VM, VM] + [HB] * (5 + len(extra)),
        out_specs=[VM, VM, VM, VM] + [HB] * (len(extra) // 3),
        scratch_shapes=[
            pltpu.VMEM((size, rows, width), BF),
            pltpu.VMEM((size, rows, width), BF),
            pltpu.VMEM((size, rows, hidden), BF),
            pltpu.VMEM((size, rows, hidden), BF),
            pltpu.VMEM((width, hidden), BF),
            pltpu.VMEM((hidden, width), BF),
            DMA((6,)),
        ]
        + comm_sems(size, n)
        + scatter_scratch(size, rows, width, n)
        + [DMA((4,)), pltpu.VMEM((rows, width), BF)] * (len(extra) // 3),
        compiler_params=params(6 + layer),
        cost_estimate=cost(60e9, 40e6),
    )(grad, h1, gains, a2, hid, slope, wu, wd, *extra)


def attend_back_kernel(size, layer, parts, *refs):
    mid_ref, qkv_ref, qm_ref, km_ref, ctx_ref, lse_ref, w_ref = refs[:7]
    refs = refs[7:]
    if layer == 0:
        gdown_ref, refs = refs[0], refs[1:]
    dqkv_ref, gout_ref, refs = refs[0], refs[1], refs[2:]
    if layer == 0:
        down_out, refs = refs[0], refs[1:]
    da, ka, va, kt, dk, dv, w, w_sem = refs[:8]
    sems, refs = refs[8:12], refs[12:]
    reduce = Reduce(layer, refs[:9])
    if layer == 0:
        down = HalfReduce(layer, refs[9 : 9 + HALF])
        down_swap = HalfSwap(gdown_ref, down.other, refs[9 + HALF])
    _, rows, wide = qkv_ref.shape
    length = size * rows
    e = qm_ref.shape[2]
    heads = wide // (3 * e)
    scale = e**-0.5
    c = scale * math.log2(math.e)
    depth = w_ref.shape[1] // parts
    n = chunks(rows)
    rc = rows // n
    bq = size * rc
    kc = bq
    g = Group(size)
    copies = [pltpu.make_async_copy(w_ref, w, w_sem.at[0])]
    for copy in copies:
        copy.start()
    g.greet(parts)
    gather = Gather(g, da, rc, sems)
    loads = []
    if layer == 0:
        down_swap.copy().start()
        loads = down.loads(gdown_ref, None)
        for load in loads:
            load.start()

    def send(j):
        at = span(j, rc)
        da[g.me, at, :] = mid_ref[at, :].astype(BF)
        gather.start(j)

    run(n, send)
    lane = lax.broadcasted_iota(jnp.int32, (length, e), 1)
    whole = flat(qkv_ref[...])
    for h in range(heads):
        o = 3 * e * h
        ka[h, :, :e] = whole[:, o + e : o + 2 * e]
        ka[h, :, e:] = flat(km_ref[...])
        va[h, :, :e] = whole[:, o + 2 * e : o + 3 * e]
        va[h, :, e:] = jnp.where(lane < 3, 1.0, 0.0).astype(BF)
        kt[h] = whole[:, o + e : o + 2 * e].T
    dk[...] = jnp.zeros_like(dk)
    dv[...] = jnp.zeros_like(dv)
    ql = lax.broadcasted_iota(jnp.int32, (bq, e), 1)
    for copy in copies + loads:
        copy.wait()

    def out_grad(z):
        cols = pl.ds(pl.multiple_of(z * depth, depth), depth)
        return dg(flat(ctx_ref[...]), flat(da[:, :, cols]), TN)

    def work(j):
        at = span(j, rc)

        @pl.when(j == 0)
        def _():
            gather.relay(0)
            gather.ready(0)

        @pl.when(j == min(1, n - 1))
        def _():
            for i in range(1, n):
                gather.relay(i)
            for i in range(1, n):
                gather.ready(i)
            reduce.send(out_grad)

        qm = flat(qm_ref[:, at, :])
        dctx = dg(flat(da[:, at, :]), w[...], NT).astype(BF)
        ctx = flat(ctx_ref[:, at, :])
        held_qkv = flat(qkv_ref[:, at, :])
        for h in range(heads):
            o = 3 * e * h
            qq = held_qkv[:, o : o + e]
            q = jnp.concatenate([qq, qm], axis=1)
            dc = dctx[:, h * e : (h + 1) * e]
            prod = dc.astype(F32) * ctx[:, h * e : (h + 1) * e].astype(F32)
            d = -jnp.sum(prod, axis=1, keepdims=True)
            d1 = d.astype(BF).astype(F32)
            d2 = (d - d1).astype(BF).astype(F32)
            d3 = d - d1 - d2
            ds_col = jnp.where(ql == 0, d1, jnp.where(ql == 1, d2, jnp.where(ql == 2, d3, 0.0)))
            dca = jnp.concatenate([dc, ds_col.astype(BF)], axis=1)
            lse = lse_ref[j, h : h + 1, :]
            dqt = None
            for k in range(length // kc):
                ks = slice(k * kc, (k + 1) * kc)
                s = dg(ka[h, ks, :], q, NT)
                p = jnp.exp2(s * c - lse)
                ds = (p * dg(va[h, ks, :], dca, NT)).astype(BF)
                dv[h, ks, :] += dg(p.astype(BF), dc, NN)
                dk[h, ks, :] += dg(ds, qq, NN)
                a = dg(kt[h, :, ks], ds, NN)
                dqt = a if dqt is None else dqt + a
            if layer == 0 and h == heads // 2:

                @pl.when(j == min(1, n - 1))
                def _():
                    down_swap.copy().wait_recv()
                    down.middle()

            if layer == 0 and h == heads - 1:

                @pl.when(j == n - 1)
                def _():
                    down.late()

            dqkv_ref[:, at, o : o + e] = (dqt * scale).T.astype(BF).reshape(size, rc, e)

    run(n, work)
    for h in range(heads):
        o = 3 * e * h
        dqkv_ref[:, :, o + e : o + 2 * e] = (dk[h] * scale).astype(BF).reshape(size, rows, e)
        dqkv_ref[:, :, o + 2 * e : o + 3 * e] = dv[h].astype(BF).reshape(size, rows, e)

    reduce.collect()
    reduce.finish(gout_ref)
    if layer == 0:
        down.finish(down_out)
        down_swap.copy().wait_send()
    gather.drain(n)


def attend_backward(size, replicas, layer, mid, qkv, qm, km, ctx, lse, w, grads):
    _, rows, wide = qkv.shape
    e = qm.shape[2]
    heads = wide // (3 * e)
    width = mid.shape[1]
    parts, depth = replicas, width // replicas
    length = size * rows
    n = chunks(rows)
    return pl.pallas_call(
        functools.partial(attend_back_kernel, size, layer, parts),
        out_shape=[shape(qkv.shape, BF), shape((heads * e, depth), F32)]
        + [shape(grad.shape[1:], F32) for grad in grads],
        in_specs=[VM] * 6 + [HB] * (1 + len(grads)),
        out_specs=[VM, VM] + [VM] * len(grads),
        scratch_shapes=[
            pltpu.VMEM((size, rows, width), BF),
            pltpu.VMEM((heads, length, 2 * e), BF),
            pltpu.VMEM((heads, length, 2 * e), BF),
            pltpu.VMEM((heads, e, length), BF),
            pltpu.VMEM((heads, length, e), F32),
            pltpu.VMEM((heads, length, e), F32),
            pltpu.VMEM((heads * e, width), BF),
            DMA((1,)),
        ]
        + comm_sems(size, n)
        + reduce_scratch(parts, heads * e, depth)
        + sum([half_scratch(parts, *grad.shape[1:]) + [DMA((2,))] for grad in grads], []),
        compiler_params=params(8 + layer),
        cost_estimate=cost(90e9, 40e6),
    )(mid, qkv, qm, km, ctx, lse, w, *grads)


def qkv_back_kernel(
    size, layer, parts, dqkv_ref, gain_ref, a1_in, x_in, mid_in, w_ref,
    dx_ref, gain_out, gqkv_ref, a1_ref, x_ref, mid_ref, w, w_sem, *scratch
):
    rows, width = x_ref.shape
    late = [
        pltpu.make_async_copy(a1_in, a1_ref, w_sem.at[1]),
        pltpu.make_async_copy(x_in, x_ref, w_sem.at[2]),
        pltpu.make_async_copy(mid_in, mid_ref, w_sem.at[3]),
    ]
    depth = width // parts
    n = thin_chunks(rows)
    rc = rows // n
    g = Group(size)
    copies = [pltpu.make_async_copy(w_ref, w, w_sem.at[0])]
    for copy in copies + late:
        copy.start()
    g.greet()
    scatter = Scatter(g, rc, scratch)
    for copy in copies:
        copy.wait()

    def work(j):
        at = span(j, rc)
        held = flat(dqkv_ref[:, at, :])
        for z in range(parts):
            cols = slice(z * depth, (z + 1) * depth)
            scatter.part[:, at, cols] = dg(held, w[cols, :], NT).reshape(size, rc, depth)
        scatter.first(j)
        scatter.second(j)

    run(n, work)
    for copy in late:
        copy.wait()

    def qkv_grad(z):
        cols = pl.ds(pl.multiple_of(z * depth, depth), depth)
        gqkv_ref[z] = dg(flat(a1_ref[:, :, cols]), flat(dqkv_ref[...]), TN).astype(BF)

    run(parts, qkv_grad)
    gain_out[...] = jnp.zeros_like(gain_out)

    def last(j):
        at = span(j, rc)
        dh, dgain = normed_back(
            x_ref[at, :].astype(F32), gain_ref[layer, 0:1, :], scatter.third(j)
        )
        dx_ref[at, :] = (mid_ref[at, :] + dh).astype(BF)
        gain_out[...] += dgain

    run(n, last)
    scatter.drain(n)


def qkv_backward(size, replicas, layer, dqkv, a1, x, mid, gains, w):
    rows, width = x.shape
    wide = w.shape[1]
    parts, depth = replicas, width // replicas
    n = thin_chunks(rows)
    return pl.pallas_call(
        functools.partial(qkv_back_kernel, size, layer, parts),
        out_shape=(
            shape((rows, width), BF),
            shape((1, width), F32),
            shape((parts, depth, wide), BF),
        ),
        in_specs=[VM, VM] + [HB] * 4,
        out_specs=(VM, VM, VM),
        scratch_shapes=[
            pltpu.VMEM((size, rows, width), BF),
            pltpu.VMEM((rows, width), BF),
            pltpu.VMEM((rows, width), F32),
            pltpu.VMEM((width, wide), BF),
            DMA((4,)),
        ]
        + scatter_scratch(size, rows, width, n),
        compiler_params=params(11),
        cost_estimate=cost(30e9, 30e6),
    )(dqkv, gains, a1, x, mid, w)


def last_kernel(
    size, parts, dqkv_ref, a1_in, x_in, mid_in, gain_ref, w_ref, two_ref, above_ref, dx1_in,
    gain_out, gqkv_out, dx_out,
    a1_ref, x_ref, mid_ref, dx1_ref, in_sem, gqkv, swap_sem, w, dx, gsum, gcame, w_sem, x_sem, x_send, x_recv, g_send, g_recv, *scratch
):
    rows, width = x_ref.shape
    depth = width // parts
    n = thin_chunks(rows)
    rc = rows // n
    g = Group(size)
    section = lax.axis_index("section")
    d = lax.axis_index("dp")
    copy = pltpu.make_async_copy(w_ref, w, w_sem.at[0])
    copy.start()
    late = [
        pltpu.make_async_copy(a1_in, a1_ref, in_sem.at[0]),
        pltpu.make_async_copy(mid_in, mid_ref, in_sem.at[1]),
        pltpu.make_async_copy(x_in, x_ref, in_sem.at[2]),
        pltpu.make_async_copy(dx1_in, dx1_ref, in_sem.at[3]),
    ]
    for one in late:
        one.start()
    reduce = HalfReduce(0, scratch[:HALF])
    swap = HalfSwap(gqkv, reduce.other, swap_sem)
    scatter = Scatter(g, rc, scratch[HALF:])
    g.greet(parts)

    def upper():
        return far_copy(
            dx1_ref, dx_out.at[0], x_send.at[n], x_recv.at[n], {"section": 1 - section}
        )

    def keep_upper():
        return pltpu.make_async_copy(dx1_ref, dx_out.at[1], x_sem.at[0])

    def lower(j):
        at = span(j, rc)
        return far_copy(
            dx.at[at], dx_out.at[1, at], x_send.at[j], x_recv.at[j], {"section": 1 - section}
        )

    def keep_lower(j):
        at = span(j, rc)
        return pltpu.make_async_copy(dx.at[at], dx_out.at[0, at], x_sem.at[j])

    def qkv_grad(z):
        cols = pl.ds(pl.multiple_of(z * depth, depth), depth)
        gqkv[z] = dg(flat(a1_ref[:, :, cols]), flat(dqkv_ref[...]), TN).astype(BF)

    copy.wait()

    def work(j):
        at = span(j, rc)
        held = flat(dqkv_ref[:, at, :])
        for z in range(parts):
            cols = slice(z * depth, (z + 1) * depth)
            scatter.part[:, at, cols] = dg(held, w[cols, :], NT).reshape(size, rc, depth)
        scatter.first(j)
        scatter.second(j)

    run(n, work)
    for one in late:
        one.wait()
    run(parts, qkv_grad)
    swap.copy().start()
    load = reduce.loads(gqkv, None)[0]
    load.start()

    @pl.when(section == 1)
    def _():
        keep_upper().start()

    gsum[0] = jnp.zeros_like(gsum[0])

    def last(j):
        at = span(j, rc)
        dh, dgain = normed_back(x_ref[at, :].astype(F32), gain_ref[0, 0:1, :], scatter.third(j))
        dx[at, :] = (mid_ref[at, :] + dh).astype(BF)

        @pl.when(section == 0)
        def _():
            keep_lower(j).start()

        @pl.when(section == 1)
        def _():
            lower(j).start()

        gsum[0, 0:1, :] += dgain

    def rest(j):
        @pl.when(j == n // 2)
        def _():
            load.wait()
            swap.copy().wait_recv()
            reduce.middle()

            @pl.when(section == 0)
            def _():
                upper().start()

        last(j)

    run(n, rest)
    gsum[0, 1:2, :] = two_ref[...]
    gsum[0, 2:4, :] = above_ref[...]

    targets = [
        [{"tensor": g.sibling}],
        [{"tensor": g.ahead(k) * 2 + g.core} for k in range(1, g.chips)],
        [{"dp": lax.rem(d + k, parts)} for k in range(1, parts)],
        [{"section": 1 - section}],
    ]
    slot = 0
    sent = []

    def exchange(stage):
        nonlocal slot
        copies = []
        for target in targets[stage]:
            copies.append(
                far_copy(gsum.at[stage], gcame.at[slot], g_send.at[slot], g_recv.at[slot], target)
            )
            copies[-1].start()
            slot += 1
        total = gsum[stage]
        for i, copy in enumerate(copies):
            copy.wait_recv()
            total = total + gcame[slot - len(copies) + i]
        gsum[stage + 1] = total
        sent.extend(copies)

    exchange(0)
    exchange(1)
    reduce.late()
    exchange(2)
    exchange(3)
    gain_out[...] = gsum[4]

    @pl.when(section == 0)
    def _():
        for j in range(n):
            lower(j).wait_recv()
            keep_lower(j).wait()
        upper().wait_send()

    @pl.when(section == 1)
    def _():
        keep_upper().wait()
        upper().wait_recv()
        for j in range(n):
            lower(j).wait_send()

    reduce.finish(gqkv_out)
    swap.copy().wait_send()
    for copy in sent:
        copy.wait_send()
    scatter.drain(n)


def last_backward(size, replicas, dqkv, a1, x, mid, gains, w, two, above, dx1):
    rows, width = x.shape
    wide = w.shape[1]
    depth = width // replicas
    n = thin_chunks(rows)
    slots = 1 + (size // 2 - 1) + (replicas - 1) + 1
    return pl.pallas_call(
        functools.partial(last_kernel, size, replicas),
        out_shape=(
            shape((8, width), F32),
            shape((depth, wide), F32),
            shape((2, rows, width), BF),
        ),
        in_specs=[VM, HB, HB, HB, VM, HB, VM, VM, HB],
        out_specs=(VM, VM, HB),
        scratch_shapes=[
            pltpu.VMEM((size, rows, width), BF),
            pltpu.VMEM((rows, width), BF),
            pltpu.VMEM((rows, width), F32),
            pltpu.VMEM((rows, width), BF),
            DMA((4,)),
            pltpu.VMEM((replicas, depth, wide), BF),
            DMA((2,)),
            pltpu.VMEM((width, wide), BF),
            pltpu.VMEM((rows, width), BF),
            pltpu.VMEM((5, 8, width), F32),
            pltpu.VMEM((slots, 8, width), F32),
            DMA((1,)),
            DMA((n,)),
            DMA((n + 1,)),
            DMA((n + 1,)),
            DMA((slots,)),
            DMA((slots,)),
        ]
        + half_scratch(replicas, depth, wide)
        + scatter_scratch(size, rows, width, n),
        compiler_params=params(10),
        cost_estimate=cost(40e9, 30e6),
    )(dqkv, a1, x, mid, gains, w, two, above, dx1)


def scene_masks(segments, e):
    same = (segments[..., None] == jnp.arange(e, dtype=jnp.int32)).astype(F32)
    used = jnp.arange(e) < SCENES
    return (
        jnp.where(used, same * MASKED, 0.0).astype(BF),
        jnp.where(used, 1.0 - same, 0.0).astype(BF),
    )


def swap_section(value):
    return lax.ppermute(value, "section", [(0, 1), (1, 0)])


def shards(
    block_input,
    segment_ids,
    cotangent,
    norm_one_gain,
    qkv_weight,
    out_weight,
    norm_two_gain,
    up_weight,
    down_weight,
):
    section = lax.axis_index("section")
    size = lax.axis_size("tensor")
    replicas = lax.axis_size("dp")

    mine = [
        qkv_weight[0].reshape((qkv_weight.shape[1], -1)),
        out_weight[0].reshape((-1, out_weight.shape[3])),
        up_weight[0],
        down_weight[0],
    ]
    mine = [w.astype(BF).reshape((2, -1, w.shape[1])) for w in mine]
    gains = jnp.concatenate(
        [norm_one_gain, norm_two_gain, jnp.zeros((6, norm_one_gain.shape[1]), F32)], axis=0
    )
    segments = lax.dynamic_index_in_dim(segment_ids, section, 0, keepdims=False)
    x = lax.dynamic_index_in_dim(block_input, section, 0, keepdims=False)
    head_dim = qkv_weight.shape[3] // 3
    qm, km = scene_masks(segments.reshape((size, -1)), head_dim)
    qkv, gains, a1, w_qkv_0, w_out_0, h_qkv, h_out, h_up, h_down = first_forward(
        size, replicas, x, gains, mine
    )
    h1, ctx, lse, w_up_0, w_down_0 = attend(
        size, replicas, 0, qkv, qm, km, x, w_out_0,
        [(h_up, "spread", 0, False), (h_down, "spread", 0, True)],
    )
    below = (x, a1, qkv, ctx, lse, h1)
    y0, qkv, a2, hid, slope, a1, w_qkv_1, w_out_1, w_up_1, got_down = turn_forward(
        size, replicas, h1, gains, w_up_0, w_down_0, h_qkv,
        [(h_out, "spread", 1, True), (h_up, "spread", 1, False), (h_down, "z", 1, True)],
    )
    kept = [below + (a2, hid, slope)]
    grad = lax.dynamic_index_in_dim(cotangent, section, 0, keepdims=False)
    h1, ctx, lse, grad_all, w_down_1 = attend(
        size, replicas, 1, qkv, qm, km, y0, w_out_1, [(got_down, "y", 1, True)], [grad]
    )
    y1, a2, hid, slope = mlp_forward(size, replicas, 1, h1, gains, w_up_1, w_down_1, [])
    kept.append((y0, a1, qkv, ctx, lse, h1, a2, hid, slope))
    weights = [
        (w_qkv_0, w_out_0, w_up_0, w_down_0),
        (w_qkv_1, w_out_1, w_up_1, w_down_1),
    ]
    def reduce_rows(value):
        return lax.psum_scatter(value, "dp", scatter_dimension=0, tiled=False)

    x, a1, qkv, ctx, lse, h1, a2, hid, slope = kept[1]
    w_qkv, w_out, w_up, w_down = weights[1]
    mid, gain_two, g_up, g_down, layer_out = mlp_backward(
        size, replicas, 1, grad, h1, gains, a2, hid, slope, w_up, w_down, [y0, y1, grad_all]
    )
    d_qkv, out_1 = attend_backward(size, replicas, 1, mid, qkv, qm, km, ctx, lse, w_out, [])
    up_1, down_1 = reduce_rows(g_up), reduce_rows(g_down)
    dx1, gain_one, g_qkv = qkv_backward(size, replicas, 1, d_qkv, a1, x, mid, gains, w_qkv)
    gains_above = jnp.concatenate([gain_one, gain_two], axis=0)
    dx1, up_1, down_1 = lax.optimization_barrier((dx1, up_1, down_1))
    qkv_1 = reduce_rows(g_qkv)

    x, a1, qkv, ctx, lse, h1, a2, hid, slope = kept[0]
    w_qkv, w_out, w_up, w_down = weights[0]
    mid, gain_two, g_up, g_down = mlp_backward(
        size, replicas, 0, dx1, h1, gains, a2, hid, slope, w_up, w_down, []
    )
    mid, qkv_1 = lax.optimization_barrier((mid, qkv_1))
    d_qkv, out_0, down_0 = attend_backward(
        size, replicas, 0, mid, qkv, qm, km, ctx, lse, w_out, [g_down]
    )
    up_0 = reduce_rows(g_up)
    d_qkv, up_0 = lax.optimization_barrier((d_qkv, up_0))
    gains, qkv_0, input_out = last_backward(
        size, replicas, d_qkv, a1, x, mid, gains, w_qkv, gain_two, gains_above, dx1
    )

    def finish(zero, one):
        send = swap_section(jnp.where(section == 0, one, zero))
        return jnp.where(section == 0, zero, one).astype(F32) + send.astype(F32)

    other_qkv_1 = swap_section(qkv_1)
    qkv_grad = jnp.where(section == 0, qkv_0, qkv_1.astype(F32) + other_qkv_1.astype(F32))
    out_grad = jnp.where(section == 0, out_0, out_1)
    up_grad = finish(up_0, up_1)
    other_down_1 = swap_section(down_1)
    down_grad = jnp.where(section == 0, down_0, down_1.astype(F32) + other_down_1.astype(F32))
    gains = lax.dynamic_slice_in_dim(gains, 2 * section, 2, 0)
    return (
        layer_out[None],
        input_out[None],
        gains[0:1],
        qkv_grad.reshape(qkv_weight.shape),
        out_grad.reshape(out_weight.shape),
        gains[1:2],
        up_grad[None],
        down_grad[None],
    )


def solution(mesh):
    return jax.shard_map(
        shards,
        mesh=mesh,
        in_specs=(
            P(None, ("dp", "tensor"), None),
            P(None, "dp"),
            P(None, ("dp", "tensor"), None),
            P("section", None),
            P("section", "dp", "tensor", None),
            P("section", "tensor", None, "dp"),
            P("section", None),
            P("section", "dp", "tensor"),
            P("section", "tensor", "dp"),
        ),
        out_specs=(
            P("section", None, ("dp", "tensor"), None),
            P("section", None, ("dp", "tensor"), None),
            P("section", None),
            P("section", "dp", "tensor", None),
            P("section", "tensor", None, "dp"),
            P("section", None),
            P("section", "dp", "tensor"),
            P("section", "tensor", "dp"),
        ),
        check_vma=False,
    )
```

```python
import functools
import math

import jax
import jax.numpy as jnp
from jax import lax
from jax.experimental import pallas as pl
from jax.experimental.pallas import tpu as pltpu
from jax.sharding import PartitionSpec as P

F32 = jnp.float32
BF = jnp.bfloat16
NT = (((1,), (1,)), ((), ()))
NN = (((1,), (0,)), ((), ()))
TN = (((0,), (0,)), ((), ()))
MASKED = -1e30
SCENES = 3
MESH = pl.DeviceIdType.MESH
VM = pl.BlockSpec(memory_space=pltpu.VMEM)
HB = pl.BlockSpec(memory_space=pl.ANY)
DMA = pltpu.SemaphoreType.DMA
LIMIT = 58 << 20


def dg(a, b, dims):
    return lax.dot_general(a, b, dims, preferred_element_type=F32)


def chunks(rows):
    return 4 if rows % 64 == 0 else 1


def thin_chunks(rows):
    return 8 if rows % 128 == 0 else chunks(rows)


def shape(dims, dtype):
    return jax.ShapeDtypeStruct(dims, dtype)


class Group:
    def __init__(self, size):
        self.size = size
        self.chips = size // 2
        self.me = lax.axis_index("tensor")
        self.chip = lax.div(self.me, 2)
        self.core = lax.rem(self.me, 2)
        self.sibling = self.chip * 2 + 1 - self.core

    def ahead(self, k):
        return lax.rem(self.chip + k, self.chips)

    def behind(self, k):
        return lax.rem(self.chip + self.chips - k, self.chips)

    def greet(self, replicas=0, side=False):
        barrier = pltpu.get_barrier_semaphore()
        targets = [self.sibling] + [self.ahead(k) * 2 + self.core for k in range(1, self.chips)]
        targets = [{"tensor": target} for target in targets]
        if replicas:
            d = lax.axis_index("dp")
            targets += [{"dp": lax.rem(d + k, replicas)} for k in range(1, replicas)]
        if replicas or side:
            targets += [{"section": 1 - lax.axis_index("section")}]
        for target in targets:
            pl.semaphore_signal(barrier, inc=1, device_id=target, device_id_type=MESH)
        pl.semaphore_wait(barrier, len(targets))


def remote(src, dst, send, recv, target):
    return pltpu.make_async_remote_copy(
        src_ref=src,
        dst_ref=dst,
        send_sem=send,
        recv_sem=recv,
        device_id={"tensor": target},
        device_id_type=MESH,
    )


def span(j, rc):
    return pl.ds(pl.multiple_of(j * rc, rc), rc)


def comm_sems(group_size, n):
    c = group_size // 2
    far, near = DMA((max(c - 1, 1), n)), DMA((c, n))
    return [far, far, near, near]


class Gather:
    def __init__(self, g, buf, rc, sems):
        self.g, self.buf, self.rc = g, buf, rc
        self.far_send, self.far_recv, self.near_send, self.near_recv = sems

    def far(self, k, j, origin, target, src=None):
        ref = self.buf.at[origin, span(j, self.rc)]
        src = ref if src is None else src
        return remote(src, ref, self.far_send.at[k - 1, j], self.far_recv.at[k - 1, j], target)

    def near(self, k, j, origin, src=None):
        ref = self.buf.at[origin, span(j, self.rc)]
        src = ref if src is None else src
        return remote(
            src, ref, self.near_send.at[k, j], self.near_recv.at[k, j], self.g.sibling
        )

    def start(self, j, src=None):
        g = self.g
        for k in range(1, g.chips):
            self.far(k, j, g.me, g.ahead(k) * 2 + g.core, src).start()
        self.near(0, j, g.me, src).start()

    def relay(self, j):
        g = self.g
        for k in range(1, g.chips):
            origin = g.behind(k) * 2 + g.core
            self.far(k, j, origin, g.me).wait_recv()
            self.near(k, j, origin).start()

    def ready(self, j):
        g = self.g
        self.near(0, j, g.sibling).wait_recv()
        for k in range(1, g.chips):
            self.near(k, j, g.behind(k) * 2 + 1 - g.core).wait_recv()

    def drain(self, n):
        g = self.g

        def one(j, _):
            for k in range(1, g.chips):
                self.far(k, j, g.me, g.sibling).wait_send()
            for k in range(g.chips):
                self.near(k, j, g.me).wait_send()
            return 0

        lax.fori_loop(0, n, one, 0)


def scatter_scratch(group_size, rows, width, n):
    c = group_size // 2
    far = pltpu.VMEM((max(c - 1, 1), rows, width), BF)
    near = pltpu.VMEM((c, rows, width), BF)
    return [pltpu.VMEM((group_size, rows, width), F32), near, near, far, far] + comm_sems(
        group_size, n
    )


class Scatter:
    def __init__(self, g, rc, scratch):
        self.g, self.rc = g, rc
        self.part, self.near_out, self.near_in, self.far_out, self.far_in = scratch[:5]
        self.far_send, self.far_recv, self.near_send, self.near_recv = scratch[5:]

    def near(self, k, j):
        rows = span(j, self.rc)
        return remote(
            self.near_out.at[k, rows],
            self.near_in.at[k, rows],
            self.near_send.at[k, j],
            self.near_recv.at[k, j],
            self.g.sibling,
        )

    def far(self, k, j):
        rows = span(j, self.rc)
        return remote(
            self.far_out.at[k - 1, rows],
            self.far_in.at[k - 1, rows],
            self.far_send.at[k - 1, j],
            self.far_recv.at[k - 1, j],
            self.g.ahead(k) * 2 + self.g.core,
        )

    def first(self, j):
        g, rows = self.g, span(j, self.rc)
        for k in list(range(1, g.chips)) + [0]:
            owner = g.ahead(k) * 2 + 1 - g.core
            self.near_out[k, rows, :] = self.part[owner, rows, :].astype(BF)
            self.near(k, j).start()

    def second(self, j):
        g, rows = self.g, span(j, self.rc)
        for k in range(1, g.chips):
            owner = g.ahead(k) * 2 + g.core
            self.near(k, j).wait_recv()
            both = self.part[owner, rows, :] + self.near_in[k, rows, :].astype(F32)
            self.far_out[k - 1, rows, :] = both.astype(BF)
            self.far(k, j).start()

    def third(self, j):
        g, rows = self.g, span(j, self.rc)
        self.near(0, j).wait_recv()
        total = self.part[g.me, rows, :] + self.near_in[0, rows, :].astype(F32)
        for k in range(1, g.chips):
            self.far(k, j).wait_recv()
            total = total + self.far_in[k - 1, rows, :].astype(F32)
        return total

    def drain(self, n):
        g = self.g

        def one(j, _):
            for k in range(1, g.chips):
                self.far(k, j).wait_send()
            for k in range(g.chips):
                self.near(k, j).wait_send()
            return 0

        lax.fori_loop(0, n, one, 0)


def far_copy(src, dst, send, recv, target):
    return pltpu.make_async_remote_copy(
        src_ref=src,
        dst_ref=dst,
        send_sem=send,
        recv_sem=recv,
        device_id=target,
        device_id_type=MESH,
    )


class Swap:
    def __init__(self, src, stage, sems):
        self.src, self.stage, self.sems = src, stage, sems
        self.s = lax.axis_index("section")

    def copies(self, layer):
        local = pltpu.make_async_copy(self.src.at[self.s], self.stage.at[self.s], self.sems.at[0])
        side = far_copy(
            self.src.at[1 - self.s],
            self.stage.at[layer],
            self.sems.at[1],
            self.sems.at[2],
            {"section": 1 - self.s},
        )
        return local, side

    def start(self):
        for copy in self.copies(self.s):
            copy.start()

    def arrive(self):
        local, side = self.copies(1 - self.s)
        local.wait()
        side.wait_recv()

    def finish(self):
        self.copies(self.s)[1].wait_send()


def reduce_scratch(replicas, rows, cols):
    many = pltpu.VMEM((replicas - 1, rows, cols), BF)
    one = pltpu.VMEM((rows, cols), BF)
    far, side = DMA((replicas - 1, 2)), DMA((2,))
    return [pltpu.VMEM((rows, cols), F32), many, many, one, one, far, far, side, side]


class Reduce:
    def __init__(self, layer, scratch):
        self.layer = layer
        self.own, self.away, self.came, self.over, self.back = scratch[:5]
        self.z_send, self.z_recv, self.y_send, self.y_recv = scratch[5:]
        self.replicas = self.away.shape[0] + 1
        self.half = self.own.shape[0] // 2
        self.d = lax.axis_index("dp")
        self.s = lax.axis_index("section")

    def target(self, k):
        return lax.rem(self.d + k, self.replicas)

    def part(self, i):
        return pl.ds(pl.multiple_of(i * self.half, self.half), self.half)

    def z_copy(self, k, i):
        part = self.part(i)
        return far_copy(
            self.away.at[k - 1, part],
            self.came.at[k - 1, part],
            self.z_send.at[k - 1, i],
            self.z_recv.at[k - 1, i],
            {"dp": self.target(k)},
        )

    def y_copy(self, i):
        part = self.part(i)
        return far_copy(
            self.over.at[part],
            self.back.at[part],
            self.y_send.at[i],
            self.y_recv.at[i],
            {"section": 1 - self.s},
        )

    def send(self, block):
        def one(i):
            k = i + 1
            self.away[i] = block(self.target(k)).astype(BF)
            self.z_copy(k, 0).start()
            self.z_copy(k, 1).start()

        run(self.replicas - 1, one)
        self.own[...] = block(self.d)

    def collect(self):
        def one(i):
            part = self.part(i)
            total = self.own[part, :]
            for k in range(1, self.replicas):
                self.z_copy(k, i).wait_recv()
                total = total + self.came[k - 1, part, :].astype(F32)
            self.own[part, :] = total
            self.over[part, :] = total.astype(BF)

            @pl.when(self.s != self.layer)
            def _():
                self.y_copy(i).start()

        run(2, one)

    def finish(self, out):
        @pl.when(self.s == self.layer)
        def _():
            self.y_copy(0).wait_recv()
            self.y_copy(1).wait_recv()
            out[...] = self.own[...] + self.back[...].astype(F32)

        @pl.when(self.s != self.layer)
        def _():
            self.y_copy(0).wait_send()
            self.y_copy(1).wait_send()
            out[...] = self.own[...]

        for k in range(1, self.replicas):
            self.z_copy(k, 0).wait_send()
            self.z_copy(k, 1).wait_send()


class HalfSwap:
    def __init__(self, src, came, sems):
        self.src, self.came, self.sems = src, came, sems
        self.s = lax.axis_index("section")
        self.rows = came.shape[1]

    def copy(self):
        at = pl.ds(pl.multiple_of((1 - self.s) * self.rows, self.rows), self.rows)
        return far_copy(
            self.src.at[:, at],
            self.came,
            self.sems.at[0],
            self.sems.at[1],
            {"section": 1 - self.s},
        )


def half_scratch(replicas, rows, cols):
    rows = rows // 2
    all_, far = pltpu.VMEM((replicas, rows, cols), BF), pltpu.VMEM((replicas - 1, rows, cols), BF)
    one = pltpu.VMEM((rows, cols), BF)
    z = DMA((replicas - 1,))
    return [all_, all_, far, far, pltpu.VMEM((rows, cols), F32), one, one, DMA((3,)), z, z, DMA((2,))]


HALF = 11


class HalfReduce:
    def __init__(self, layer, scratch):
        self.layer = layer
        self.mine, self.other, self.away, self.came, self.own, self.over, self.back = scratch[:7]
        self.in_sem, self.z_send, self.z_recv, self.y_sem = scratch[7:]
        self.replicas, self.rows = self.mine.shape[:2]
        self.s = lax.axis_index("section")
        self.d = lax.axis_index("dp")

    def half(self, s):
        return pl.ds(pl.multiple_of(s * self.rows, self.rows), self.rows)

    def loads(self, src, other):
        loads = [pltpu.make_async_copy(src.at[:, self.half(self.s)], self.mine, self.in_sem.at[0])]
        if other is not None:
            loads.append(pltpu.make_async_copy(other, self.other, self.in_sem.at[1]))
        return loads

    def z_copy(self, k):
        return far_copy(
            self.away.at[k - 1],
            self.came.at[k - 1],
            self.z_send.at[k - 1],
            self.z_recv.at[k - 1],
            {"dp": lax.rem(self.d + k, self.replicas)},
        )

    def y_copy(self):
        return far_copy(
            self.over, self.back, self.y_sem.at[0], self.y_sem.at[1], {"section": 1 - self.s}
        )

    def middle(self):
        def both(z):
            return self.mine[z].astype(F32) + self.other[z].astype(F32)

        for k in range(1, self.replicas):
            self.away[k - 1] = both(lax.rem(self.d + k, self.replicas)).astype(BF)
            self.z_copy(k).start()
        self.own[...] = both(self.d)

    def late(self):
        total = self.own[...]
        for k in range(1, self.replicas):
            self.z_copy(k).wait_recv()
            total = total + self.came[k - 1].astype(F32)
        self.own[...] = total
        self.over[...] = total.astype(BF)

        @pl.when(self.s != self.layer)
        def _():
            self.y_copy().start()

    def finish(self, out, above=None):
        @pl.when(self.s == self.layer)
        def _():
            self.y_copy().wait_recv()
            out[self.half(self.s), :] = self.own[...]
            out[self.half(1 - self.s), :] = self.back[...].astype(F32)

        @pl.when(self.s != self.layer)
        def _():
            if above is None:
                out[...] = jnp.zeros_like(out)
            else:
                copy = pltpu.make_async_copy(above, out, self.in_sem.at[2])
                copy.start()
                copy.wait()
            self.y_copy().wait_send()

        for k in range(1, self.replicas):
            self.z_copy(k).wait_send()


class Spread:
    def __init__(self, src, dst, by_columns, sems):
        self.src, self.dst, self.by_columns = src, dst, by_columns
        self.own_sem, self.far_send, self.far_recv, self.side_send, self.side_recv = sems
        self.replicas = far = self.side_send.shape[0]
        self.s = lax.axis_index("section")
        self.d = lax.axis_index("dp")
        self.stages = [
            sorted({k, far - k}) for k in range(1, far // 2 + 1)
        ]

    def place(self, half, z):
        rows, cols = self.src.shape
        if self.by_columns:
            return self.dst.at[
                pl.ds(pl.multiple_of(half * rows, rows), rows),
                pl.ds(pl.multiple_of(z * cols, cols), cols),
            ]
        return self.dst.at[pl.ds(pl.multiple_of((2 * z + half) * rows, rows), rows)]

    def origin(self, k):
        return lax.rem(self.d + self.replicas - k, self.replicas)

    def own(self):
        return pltpu.make_async_copy(self.src, self.place(self.s, self.d), self.own_sem.at[0])

    def far(self, k, origin):
        return pltpu.make_async_remote_copy(
            src_ref=self.src,
            dst_ref=self.place(self.s, origin),
            send_sem=self.far_send.at[k - 1],
            recv_sem=self.far_recv.at[k - 1],
            device_id={"dp": lax.rem(self.d + k, self.replicas)},
            device_id_type=MESH,
        )

    def side(self, k, half):
        place = self.place(half, self.origin(k))
        return pltpu.make_async_remote_copy(
            src_ref=self.src if k == 0 else place,
            dst_ref=place,
            send_sem=self.side_send.at[k],
            recv_sem=self.side_recv.at[k],
            device_id={"section": 1 - self.s},
            device_id_type=MESH,
        )

    def start(self):
        for k in self.stages[0]:
            self.far(k, self.d).start()
        self.side(0, self.s).start()
        self.own().start()

    def step(self, i):
        for k in self.stages[i]:
            self.far(k, self.origin(k)).wait_recv()
            self.side(k, self.s).start()
        if i + 1 < len(self.stages):
            for k in self.stages[i + 1]:
                self.far(k, self.d).start()

    def finish(self):
        self.own().wait()
        for k in range(self.replicas):
            self.side(k, 1 - self.s).wait_recv()
        for k in range(1, self.replicas):
            self.far(k, self.d).wait_send()
        for k in range(self.replicas):
            self.side(k, self.s).wait_send()


class ZGather:
    def __init__(self, src, got, sems):
        self.src, self.got = src, got
        self.own_sem, self.send, self.recv = sems
        self.replicas = got.shape[0]
        self.d = lax.axis_index("dp")

    def own(self):
        return pltpu.make_async_copy(self.src, self.got.at[self.d], self.own_sem.at[0])

    def far(self, k, origin):
        return far_copy(
            self.src,
            self.got.at[origin],
            self.send.at[k - 1],
            self.recv.at[k - 1],
            {"dp": lax.rem(self.d + k, self.replicas)},
        )

    def start(self):
        for k in range(1, self.replicas):
            self.far(k, self.d).start()
        self.own().start()

    def step(self, i):
        pass

    def finish(self):
        self.own().wait()
        for k in range(1, self.replicas):
            self.far(k, lax.rem(self.d + self.replicas - k, self.replicas)).wait_recv()
        for k in range(1, self.replicas):
            self.far(k, self.d).wait_send()


class YJoin:
    def __init__(self, got, dst, by_columns, sems):
        self.src, self.dst, self.by_columns = got, dst, by_columns
        self.own_sem, self.send, self.recv, self.got, self.in_sem = sems
        self.replicas, self.rows, self.cols = got.shape
        self.s = lax.axis_index("section")

    def place(self, half, z):
        rows, cols = self.rows, self.cols
        if self.by_columns:
            return self.dst.at[
                pl.ds(pl.multiple_of(half * rows, rows), rows), pl.ds(z * cols, cols)
            ]
        return self.dst.at[pl.ds(pl.multiple_of((2 * z + half) * rows, rows), rows)]

    def own(self, z):
        return pltpu.make_async_copy(self.got.at[z], self.place(self.s, z), self.own_sem.at[z])

    def side(self, z, half):
        return far_copy(
            self.got.at[z],
            self.place(half, z),
            self.send.at[z],
            self.recv.at[z],
            {"section": 1 - self.s},
        )

    def start(self):
        load = pltpu.make_async_copy(self.src, self.got, self.in_sem.at[0])
        load.start()
        load.wait()
        for z in range(self.replicas):
            self.side(z, self.s).start()
            self.own(z).start()

    def step(self, i):
        pass

    def finish(self):
        for z in range(self.replicas):
            self.own(z).wait()
            self.side(z, 1 - self.s).wait_recv()
        for z in range(self.replicas):
            self.side(z, self.s).wait_send()


def rider_sems(replicas):
    far, side = DMA((replicas - 1,)), DMA((replicas,))
    return [DMA((1,)), far, far, side, side]


class Riders:
    def __init__(self, srcs, dsts, columns, sems):
        self.all = []
        for src, dst, (kind, layer, by) in zip(srcs, dsts, columns):
            count = 3 if kind == "z" else 5
            own, sems = sems[:count], sems[count:]
            if kind == "spread":
                self.all.append(Spread(src.at[layer], dst, by, own))
            elif kind == "z":
                self.all.append(ZGather(src.at[layer], dst, own))
            else:
                self.all.append(YJoin(src, dst, by, own))
        self.replicas = self.all[0].replicas if self.all else 0

    def start(self):
        for one in self.all:
            one.start()

    def step(self, j, n):
        if not self.all:
            return
        stages = self.replicas // 2
        for i in range(stages):

            @pl.when(j == n * (i + 1) // stages - 1)
            def _(i=i):
                for one in self.all:
                    one.step(i)

    def finish(self):
        for one in self.all:
            one.finish()


def riding(riders, replicas):
    arrays = [array for array, _, _, _ in riders]
    columns = tuple(rider[1:] for rider in riders)
    outs, sems = [], []
    for array, kind, _, by in riders:
        rows, cols = array.shape[1:]
        if kind == "z":
            outs.append(shape((replicas, rows, cols), BF))
        else:
            outs.append(
                shape((2 * rows, replicas * cols) if by else (2 * replicas * rows, cols), BF)
            )
        far, side = DMA((replicas - 1,)), DMA((replicas,))
        sems += {
            "spread": rider_sems(replicas),
            "z": [DMA((1,)), far, far],
            "y": [side, side, side, pltpu.VMEM(array.shape, BF), DMA((1,))],
        }[kind]
    return arrays, columns, outs, sems


def params(key):
    return pltpu.CompilerParams(
        vmem_limit_bytes=LIMIT, collective_id=key, has_side_effects=True
    )


def cost(flops, moved, exps=0):
    return pl.CostEstimate(flops=int(flops), bytes_accessed=int(moved), transcendentals=int(exps))


def normed(source):
    center = source - jnp.mean(source, axis=-1, keepdims=True)
    r = lax.rsqrt(jnp.mean(center * center, axis=-1, keepdims=True) + 1e-05)
    return center * r, r


def normed_back(source, gain, grad):
    n, r = normed(source)
    e = grad * gain
    dh = r * (
        e - jnp.mean(e, axis=-1, keepdims=True) - n * jnp.mean(e * n, axis=-1, keepdims=True)
    )
    return dh, jnp.sum(grad * n, axis=0, keepdims=True)


def flat(value):
    return value.reshape((value.shape[0] * value.shape[1],) + value.shape[2:])


def run(n, body):
    def one(j, carry):
        body(j)
        return carry

    lax.fori_loop(0, n, one, 0)


def first_kernel(
    size, replicas, x_ref, gain_ref, wq_ref, wo_ref, wu_ref, wd_ref,
    qkv_ref, gains_out, a1_out, wq_out, wo_out, q_stage, o_stage, u_stage, d_stage,
    a1, w, gains, own_sem, q_sem, o_sem, u_sem, d_sem, gain_sem, *sems
):
    rows, width = x_ref.shape
    n = thin_chunks(rows)
    rc = rows // n
    g = Group(size)
    section = lax.axis_index("section")
    gather = Gather(g, a1, rc, sems[:4])
    swaps = [
        Swap(wq_ref, q_stage, q_sem),
        Swap(wo_ref, o_stage, o_sem),
        Swap(wu_ref, u_stage, u_sem),
        Swap(wd_ref, d_stage, d_sem),
    ]
    spreads = [
        Spread(q_stage.at[0], w, False, sems[4:9]),
        Spread(o_stage.at[0], wo_out, True, sems[9:14]),
    ]
    riders = Riders([], [], (), [])
    riders.all = spreads
    riders.replicas = replicas
    g.greet(replicas)

    def gain_copy(layer):
        return far_copy(
            gain_ref, gains.at[layer], gain_sem.at[0], gain_sem.at[1], {"section": 1 - section}
        )

    gain_copy(section).start()
    swaps[0].start()
    swaps[1].start()
    gains[section] = gain_ref[...]
    gain_copy(1 - section).wait_recv()
    gains_out[...] = gains[...]

    def send(j):
        at = span(j, rc)
        a = normed(x_ref[at, :].astype(F32))[0] * gains[0, 0:1, :]
        a1[g.me, at, :] = a.astype(BF)
        gather.start(j)

    run(n, send)
    swaps[0].arrive()
    swaps[1].arrive()
    riders.start()
    swaps[2].start()
    swaps[3].start()

    def relay(j):
        gather.relay(j)
        riders.step(j, n)

    run(n, relay)
    riders.finish()
    outs = [
        pltpu.make_async_copy(w, wq_out, own_sem.at[0]),
        pltpu.make_async_copy(a1, a1_out, own_sem.at[1]),
    ]
    outs[0].start()

    def multiply(j):
        at = span(j, rc)
        gather.ready(j)
        r = dg(flat(a1[:, at, :]), w[...], NN).astype(BF)
        qkv_ref[:, at, :] = r.reshape(size, rc, r.shape[1])

    run(n, multiply)
    outs[1].start()
    swaps[2].arrive()
    swaps[3].arrive()
    for swap in swaps:
        swap.finish()
    gain_copy(section).wait_send()
    gather.drain(n)
    for out in outs:
        out.wait()


def first_forward(size, replicas, x, gains, ws):
    rows, width = x.shape
    wide = ws[0].shape[2]
    deep = 2 * ws[1].shape[1]
    n = thin_chunks(rows)
    return pl.pallas_call(
        functools.partial(first_kernel, size, replicas),
        out_shape=[
            shape((size, rows, wide), BF),
            shape((2,) + gains.shape, F32),
            shape((size, rows, width), BF),
            shape((width, wide), BF),
            shape((deep, width), BF),
        ]
        + [shape(w.shape, BF) for w in ws],
        in_specs=[VM] * 6,
        out_specs=[VM, VM] + [HB] * 7,
        scratch_shapes=[
            pltpu.VMEM((size, rows, width), BF),
            pltpu.VMEM((width, wide), BF),
            pltpu.VMEM((2,) + gains.shape, F32),
            DMA((2,)),
            DMA((3,)),
            DMA((3,)),
            DMA((3,)),
            DMA((3,)),
            DMA((2,)),
        ]
        + comm_sems(size, n)
        + rider_sems(replicas) * 2,
        compiler_params=params(0),
        cost_estimate=cost(30e9, 30e6),
    )(x, gains, *ws)


def attend_kernel(size, layer, columns, *refs):
    m = len(columns)
    qkv_ref, qm_ref, km_ref, x_ref, w_ref = refs[:5]
    refs = refs[5:]
    if layer == 1:
        cot_ref, refs = refs[0], refs[1:]
    halves, refs = refs[:m], refs[m:]
    h1_ref, ctx_ref, lse_ref = refs[:3]
    refs = refs[3:]
    if layer == 1:
        cot_out, refs = refs[0], refs[1:]
    wholes, refs = refs[:m], refs[m:]
    ka, vt, w, w_sem = refs[:4]
    scratch, refs = refs[4:13], refs[13:]
    if layer == 1:
        cot_sems, cot_sem, refs = refs[:4], refs[4], refs[5:]
    riders = Riders(halves, wholes, columns, refs)
    _, rows, wide = qkv_ref.shape
    length = size * rows
    e = qm_ref.shape[2]
    heads = wide // (3 * e)
    c = e**-0.5 * math.log2(math.e)
    n = chunks(rows)
    rc = rows // n
    bq = size * rc
    kc = bq
    g = Group(size)
    copy = pltpu.make_async_copy(w_ref, w, w_sem.at[0])
    copy.start()
    g.greet(riders.replicas)
    riders.start()
    if layer == 1:
        cot = Gather(g, cot_out, rows, cot_sems)
        own = pltpu.make_async_copy(cot_ref, cot_out.at[g.me], cot_sem.at[0])
        own.start()
        cot.start(0, cot_ref)
    scatter = Scatter(g, rc, scratch)
    whole = flat(qkv_ref[...])
    for h in range(heads):
        o = 3 * e * h
        ka[h, :, :e] = whole[:, o + e : o + 2 * e]
        ka[h, :, e:] = flat(km_ref[...])
        vt[h, :e, :] = whole[:, o + 2 * e : o + 3 * e].T
        vt[h, e:, :] = jnp.ones((16, length), BF)
    copy.wait()

    def work(j):
        at = span(j, rc)
        qm = flat(qm_ref[:, at, :])
        found = []
        held_qkv = flat(qkv_ref[:, at, :])
        for h in range(heads):
            o = 3 * e * h
            q = jnp.concatenate([held_qkv[:, o : o + e], qm], axis=1)
            held = []
            top = None
            for k in range(length // kc):
                s = dg(ka[h, k * kc : (k + 1) * kc, :], q, NT)
                t = jnp.max(s, axis=0, keepdims=True)
                top = t if top is None else jnp.maximum(top, t)
                held.append(s)
            top = top * c
            acc = None
            for k in range(length // kc):
                p = jnp.exp2(held[k] * c - top).astype(BF)
                a = dg(vt[h, :, k * kc : (k + 1) * kc], p, NN)
                acc = a if acc is None else acc + a
            total = acc[e : e + 1]
            found.append((acc[:e] * (1.0 / total)).astype(BF))
            lse_ref[j, h : h + 1, :] = top + jnp.log2(total)
            if h == heads // 2:

                @pl.when(j > 0)
                def _():
                    scatter.second(j - 1)

        ctx = (jnp.concatenate(found, axis=0) if heads > 1 else found[0]).T
        ctx_ref[:, at, :] = ctx.reshape(size, rc, heads * e)
        width = x_ref.shape[1]
        scatter.part[:, at, :] = dg(ctx, w[...], NN).reshape(size, rc, width)
        scatter.first(j)
        riders.step(j, n)
        if layer == 1:

            @pl.when(j == n - 1)
            def _():
                cot.relay(0)

    run(n, work)
    scatter.second(n - 1)

    def last(j):
        at = span(j, rc)
        h1_ref[at, :] = x_ref[at, :].astype(F32) + scatter.third(j)

    run(n, last)
    scatter.drain(n)
    if layer == 1:
        cot.ready(0)
        cot.drain(1)
        own.wait()
    riders.finish()


def attend(size, replicas, layer, qkv, qm, km, x, w, riders, cot=()):
    _, rows, wide = qkv.shape
    e = qm.shape[2]
    heads = wide // (3 * e)
    width = x.shape[1]
    n = chunks(rows)
    halves, columns, outs, sems = riding(riders, replicas)
    return pl.pallas_call(
        functools.partial(attend_kernel, size, layer, columns),
        out_shape=[
            shape((rows, width), F32),
            shape((size, rows, heads * e), BF),
            shape((n, heads, size * rows // n), F32),
        ]
        + [shape((size, rows, width), BF) for _ in cot]
        + outs,
        in_specs=[VM, VM, VM, VM, HB] + [VM] * len(cot) + [HB] * len(riders),
        out_specs=[VM, VM, VM] + [HB] * (len(cot) + len(outs)),
        scratch_shapes=[
            pltpu.VMEM((heads, size * rows, 2 * e), BF),
            pltpu.VMEM((heads, e + 16, size * rows), BF),
            pltpu.VMEM((heads * e, width), BF),
            DMA((1,)),
        ]
        + scatter_scratch(size, rows, width, n)
        + (comm_sems(size, 1) + [DMA((1,))]) * len(cot)
        + sems,
        compiler_params=params(2 + layer),
        cost_estimate=cost(60e9, 20e6),
    )(qkv, qm, km, x, w, *cot, *halves)


def mlp_kernel(size, layer, columns, *refs):
    m = len(columns)
    h1_ref, gain_ref, wu_ref, wd_ref = refs[:4]
    halves, refs = refs[4 : 4 + m], refs[4 + m :]
    y_ref, a2_out, hid_out, slope_out = refs[:4]
    wholes, refs = refs[4 : 4 + m], refs[4 + m :]
    a2, hid, slope, wu, wd, w_sem, out_sem = refs[:7]
    scratch, refs = refs[7:20], refs[20:]
    riders = Riders(halves, wholes, columns, refs)
    rows, width = h1_ref.shape
    hidden = wu_ref.shape[1]
    fb = min(256, hidden)
    n = chunks(rows)
    rc = rows // n
    g = Group(size)
    copies = [
        pltpu.make_async_copy(wu_ref, wu, w_sem.at[0]),
        pltpu.make_async_copy(wd_ref, wd, w_sem.at[1]),
    ]
    for copy in copies:
        copy.start()
    g.greet(riders.replicas)
    gather = Gather(g, a2, rc, scratch[:4])
    scatter = Scatter(g, rc, scratch[4:])

    def send(j):
        at = span(j, rc)
        a = normed(h1_ref[at, :])[0] * gain_ref[layer, 1:2, :]
        a2[g.me, at, :] = a.astype(BF)
        gather.start(j)

    run(n, send)
    riders.start()
    for copy in copies:
        copy.wait()

    gather.relay(0)

    def work(j):
        at = span(j, rc)
        gather.ready(j)
        a = flat(a2[:, at, :])
        for f in range(hidden // fb):
            cols = slice(f * fb, (f + 1) * fb)
            u = dg(a, wu[:, cols], NN)
            half = 0.5 + 0.5 * lax.erf(u * (0.5**0.5))
            slope[:, at, cols] = (
                (half + u * jnp.exp(-0.5 * u * u) * ((2 * math.pi) ** -0.5))
                .astype(BF)
                .reshape(size, rc, fb)
            )
            hid[:, at, cols] = (u * half).astype(BF).reshape(size, rc, fb)

        @pl.when(j + 1 < n)
        def _():
            gather.relay(j + 1)

        @pl.when(j > 0)
        def _():
            scatter.second(j - 1)

        held = flat(hid[:, at, :])
        for f in range(width // 256):
            cols = slice(f * 256, (f + 1) * 256)
            scatter.part[:, at, cols] = dg(held, wd[:, cols], NN).reshape(size, rc, 256)
        scatter.first(j)
        riders.step(j, n)

    run(n, work)
    scatter.second(n - 1)
    outs = [
        pltpu.make_async_copy(a2, a2_out, out_sem.at[0]),
        pltpu.make_async_copy(hid, hid_out, out_sem.at[1]),
        pltpu.make_async_copy(slope, slope_out, out_sem.at[2]),
    ]
    for out in outs:
        out.start()

    def last(j):
        at = span(j, rc)
        y_ref[at, :] = (h1_ref[at, :] + scatter.third(j)).astype(BF)

    run(n, last)
    riders.finish()
    gather.drain(n)
    scatter.drain(n)
    for out in outs:
        out.wait()


def mlp_forward(size, replicas, layer, h1, gains, wu, wd, riders):
    rows, width = h1.shape
    hidden = wu.shape[1]
    n = chunks(rows)
    halves, columns, outs, sems = riding(riders, replicas)
    return pl.pallas_call(
        functools.partial(mlp_kernel, size, layer, columns),
        out_shape=[
            shape((rows, width), BF),
            shape((size, rows, width), BF),
            shape((size, rows, hidden), BF),
            shape((size, rows, hidden), BF),
        ]
        + outs,
        in_specs=[VM, VM, HB, HB] + [HB] * len(riders),
        out_specs=[VM, HB, HB, HB] + [HB] * len(outs),
        scratch_shapes=[
            pltpu.VMEM((size, rows, width), BF),
            pltpu.VMEM((size, rows, hidden), BF),
            pltpu.VMEM((size, rows, hidden), BF),
            pltpu.VMEM((width, hidden), BF),
            pltpu.VMEM((hidden, width), BF),
            DMA((2,)),
            DMA((3,)),
        ]
        + comm_sems(size, n)
        + scatter_scratch(size, rows, width, n)
        + sems,
        compiler_params=params(4 + layer),
        cost_estimate=cost(50e9, 30e6),
    )(h1, gains, wu, wd, *halves)


def turn_kernel(size, columns, *refs):
    m = len(columns)
    h1_ref, gain_ref, wu_ref, wd_ref, q_stage = refs[:5]
    halves, refs = refs[5 : 5 + m], refs[5 + m :]
    y_ref, qkv_ref, a2_out, hid_out, slope_out, a1_out, wq_out = refs[:7]
    wholes, refs = refs[7 : 7 + m], refs[7 + m :]
    a2, hid, slope, wu, wd, a1, wq, w_sem, out_sem = refs[:9]
    gather_sems, next_sems, refs = refs[9:13], refs[13:17], refs[17:]
    scratch, refs = refs[:9], refs[9:]
    spread = Spread(q_stage.at[1], wq, False, refs[:5])
    riders = Riders(halves, wholes, columns, refs[5:])
    out_rider, up_rider, down_rider = riders.all
    stages = len(spread.stages)
    rows, width = h1_ref.shape
    hidden = wu_ref.shape[1]
    fb = min(256, hidden)
    n = chunks(rows)
    rc = rows // n
    g = Group(size)
    copies = [
        pltpu.make_async_copy(wu_ref, wu, w_sem.at[0]),
        pltpu.make_async_copy(wd_ref, wd, w_sem.at[1]),
    ]
    for copy in copies:
        copy.start()
    g.greet(spread.replicas)
    gather = Gather(g, a2, rc, gather_sems)
    onward = Gather(g, a1, rc, next_sems)
    scatter = Scatter(g, rc, scratch)

    def send(j):
        at = span(j, rc)
        a = normed(h1_ref[at, :])[0] * gain_ref[0, 1:2, :]
        a2[g.me, at, :] = a.astype(BF)
        gather.start(j)

    run(n, send)
    spread.start()
    out_rider.start()
    for copy in copies:
        copy.wait()

    def pass_on(j):
        at = span(j, rc)
        y = (h1_ref[at, :] + scatter.third(j)).astype(BF)
        y_ref[at, :] = y
        a = normed(y.astype(F32))[0] * gain_ref[1, 0:1, :]
        a1[g.me, at, :] = a.astype(BF)
        onward.start(j)

    lag = min(2, n)
    gather.relay(0)

    def work(j):
        at = span(j, rc)
        gather.ready(j)
        a = flat(a2[:, at, :])
        for f in range(hidden // fb):
            cols = slice(f * fb, (f + 1) * fb)
            u = dg(a, wu[:, cols], NN)
            half = 0.5 + 0.5 * lax.erf(u * (0.5**0.5))
            slope[:, at, cols] = (
                (half + u * jnp.exp(-0.5 * u * u) * ((2 * math.pi) ** -0.5))
                .astype(BF)
                .reshape(size, rc, fb)
            )
            hid[:, at, cols] = (u * half).astype(BF).reshape(size, rc, fb)

        @pl.when(j + 1 < n)
        def _():
            gather.relay(j + 1)

        @pl.when(j > 0)
        def _():
            scatter.second(j - 1)

        held = flat(hid[:, at, :])
        for f in range(width // 256):
            cols = slice(f * 256, (f + 1) * 256)
            scatter.part[:, at, cols] = dg(held, wd[:, cols], NN).reshape(size, rc, 256)
        scatter.first(j)

        @pl.when(j >= lag)
        def _():
            pass_on(j - lag)

        @pl.when(j == n // 2)
        def _():
            spread.step(0)
            out_rider.step(0)
            up_rider.start()

        @pl.when(j == n - 1)
        def _():
            for i in range(1, stages):
                spread.step(i)
                out_rider.step(i)

    run(n, work)
    scatter.second(n - 1)
    outs = [
        pltpu.make_async_copy(a2, a2_out, out_sem.at[0]),
        pltpu.make_async_copy(hid, hid_out, out_sem.at[1]),
        pltpu.make_async_copy(slope, slope_out, out_sem.at[2]),
    ]
    for out in outs:
        out.start()
    for j in range(n - lag, n):
        pass_on(j)
    up_rider.step(0)
    down_rider.start()
    spread.finish()
    outs.append(pltpu.make_async_copy(wq, wq_out, out_sem.at[3]))
    outs[3].start()

    onward.relay(0)

    def multiply(j):
        at = span(j, rc)

        @pl.when(j + 1 < n)
        def _():
            onward.relay(j + 1)

        onward.ready(j)
        r = dg(flat(a1[:, at, :]), wq[...], NN).astype(BF)
        qkv_ref[:, at, :] = r.reshape(size, rc, r.shape[1])

    run(n, multiply)
    outs.append(pltpu.make_async_copy(a1, a1_out, out_sem.at[4]))
    outs[4].start()
    for i in range(1, stages):
        up_rider.step(i)
    riders.finish()
    gather.drain(n)
    onward.drain(n)
    scatter.drain(n)
    for out in outs:
        out.wait()


def turn_forward(size, replicas, h1, gains, wu, wd, stage, riders):
    rows, width = h1.shape
    hidden = wu.shape[1]
    wide = stage.shape[2]
    n = chunks(rows)
    halves, columns, outs, sems = riding(riders, replicas)
    return pl.pallas_call(
        functools.partial(turn_kernel, size, columns),
        out_shape=[
            shape((rows, width), BF),
            shape((size, rows, wide), BF),
            shape((size, rows, width), BF),
            shape((size, rows, hidden), BF),
            shape((size, rows, hidden), BF),
            shape((size, rows, width), BF),
            shape((width, wide), BF),
        ]
        + outs,
        in_specs=[VM, VM] + [HB] * (3 + len(riders)),
        out_specs=[VM, VM] + [HB] * (5 + len(outs)),
        scratch_shapes=[
            pltpu.VMEM((size, rows, width), BF),
            pltpu.VMEM((size, rows, hidden), BF),
            pltpu.VMEM((size, rows, hidden), BF),
            pltpu.VMEM((width, hidden), BF),
            pltpu.VMEM((hidden, width), BF),
            pltpu.VMEM((size, rows, width), BF),
            pltpu.VMEM((width, wide), BF),
            DMA((2,)),
            DMA((5,)),
        ]
        + comm_sems(size, n) * 2
        + scatter_scratch(size, rows, width, n)
        + rider_sems(replicas)
        + sems,
        compiler_params=params(4),
        cost_estimate=cost(50e9, 30e6),
    )(h1, gains, wu, wd, stage, *halves)


def mlp_back_kernel(size, layer, parts, *refs):
    g_ref, h1_ref, gain_ref, a2_ref, hid_ref, slope_ref, wu_ref, wd_ref = refs[:8]
    refs = refs[8:]
    if layer == 1:
        ys, whole_ref, refs = refs[:2], refs[2], refs[3:]
    mid_ref, gain_out, gup_ref, gdown_ref = refs[:4]
    refs = refs[4:]
    if layer == 1:
        y_out, refs = refs[0], refs[1:]
    grad, a2, hid, dup, wu, wd, w_sem = refs[:7]
    scratch, refs = refs[7:20], refs[20:]
    rows, width = h1_ref.shape
    hidden = wu_ref.shape[1]
    depth = width // parts
    fb = min(256, hidden)
    n = chunks(rows)
    rc = rows // n
    g = Group(size)
    copies = [
        pltpu.make_async_copy(wd_ref, wd, w_sem.at[0]),
        pltpu.make_async_copy(slope_ref, dup, w_sem.at[1]),
        pltpu.make_async_copy(wu_ref, wu, w_sem.at[2]),
    ]
    late = [
        pltpu.make_async_copy(hid_ref, hid, w_sem.at[3]),
        pltpu.make_async_copy(a2_ref, a2, w_sem.at[4]),
    ]
    for copy in copies:
        copy.start()
    g.greet(side=layer == 1)
    section = lax.axis_index("section")
    if layer == 1:
        y_sem, y_own = refs

        def y_load(own):
            return pltpu.make_async_copy(own, y_own, y_sem.at[3])

        def y_copies(own, other, at):
            return (
                pltpu.make_async_copy(y_own, y_out.at[section], y_sem.at[0]),
                far_copy(
                    other, y_out.at[at], y_sem.at[1], y_sem.at[2], {"section": 1 - section}
                ),
            )

        for i in range(2):

            @pl.when(section == i)
            def _(i=i):
                y_load(ys[i]).start()
                y_copies(ys[i], ys[1 - i], section)[1].start()

    gather = Gather(g, grad, rc, scratch[:4])
    scatter = Scatter(g, rc, scratch[4:])

    def send(j):
        at = span(j, rc)
        grad[g.me, at, :] = g_ref[at, :]
        gather.start(j)

    if layer == 1:
        whole = pltpu.make_async_copy(whole_ref, grad, w_sem.at[5])
        whole.start()
        copies.append(whole)
    else:
        run(n, send)
    for copy in copies:
        copy.wait()
    for copy in late:
        copy.start()
    if layer == 1:
        y_load(ys[0]).wait()
        y_copies(ys[0], ys[1], section)[0].start()

    if layer == 0:
        gather.relay(0)

    def work(j):
        at = span(j, rc)
        if layer == 0:
            gather.ready(j)
        held = flat(grad[:, at, :])
        for f in range(hidden // fb):
            cols = slice(f * fb, (f + 1) * fb)
            d = dg(held, wd[cols, :], NT) * flat(dup[:, at, cols]).astype(F32)
            dup[:, at, cols] = d.astype(BF).reshape(size, rc, fb)

        if layer == 0:

            @pl.when(j + 1 < n)
            def _():
                gather.relay(j + 1)

        @pl.when(j > 0)
        def _():
            scatter.second(j - 1)

        held = flat(dup[:, at, :])
        for z in range(parts):
            cols = slice(z * depth, (z + 1) * depth)
            scatter.part[:, at, cols] = dg(held, wu[cols, :], NT).reshape(size, rc, depth)
        scatter.first(j)

    run(n, work)
    scatter.second(n - 1)
    for copy in late:
        copy.wait()

    def up_grad(z):
        cols = pl.ds(pl.multiple_of(z * depth, depth), depth)
        gup_ref[z] = dg(flat(a2[:, :, cols]), flat(dup[...]), TN).astype(BF)

    run(parts, up_grad)

    def down_grad(f):
        cols = pl.ds(pl.multiple_of(f * fb, fb), fb)
        r = dg(flat(hid[:, :, cols]), flat(grad[...]), TN).astype(BF)
        for z in range(parts):
            gdown_ref[z, cols, :] = r[:, z * depth : (z + 1) * depth]

    run(hidden // fb, down_grad)
    gain_out[...] = jnp.zeros_like(gain_out)

    def last(j):
        at = span(j, rc)
        dh, dgain = normed_back(h1_ref[at, :], gain_ref[layer, 1:2, :], scatter.third(j))
        mid_ref[at, :] = g_ref[at, :].astype(F32) + dh
        gain_out[...] += dgain

    run(n, last)
    if layer == 1:
        local, side = y_copies(ys[0], ys[1], 1 - section)
        local.wait()
        side.wait_recv()
        y_copies(ys[0], ys[1], section)[1].wait_send()
    if layer == 0:
        gather.drain(n)
    scatter.drain(n)


def mlp_backward(size, replicas, layer, grad, h1, gains, a2, hid, slope, wu, wd, extra):
    rows, width = h1.shape
    hidden = wu.shape[1]
    parts, depth = replicas, width // replicas
    n = chunks(rows)
    return pl.pallas_call(
        functools.partial(mlp_back_kernel, size, layer, parts),
        out_shape=[
            shape((rows, width), F32),
            shape((1, width), F32),
            shape((parts, depth, hidden), BF),
            shape((parts, hidden, depth), BF),
        ]
        + [shape((2, rows, width), BF)] * (len(extra) // 3),
        in_specs=[VM, VM, VM] + [HB] * (5 + len(extra)),
        out_specs=[VM, VM, VM, VM] + [HB] * (len(extra) // 3),
        scratch_shapes=[
            pltpu.VMEM((size, rows, width), BF),
            pltpu.VMEM((size, rows, width), BF),
            pltpu.VMEM((size, rows, hidden), BF),
            pltpu.VMEM((size, rows, hidden), BF),
            pltpu.VMEM((width, hidden), BF),
            pltpu.VMEM((hidden, width), BF),
            DMA((6,)),
        ]
        + comm_sems(size, n)
        + scatter_scratch(size, rows, width, n)
        + [DMA((4,)), pltpu.VMEM((rows, width), BF)] * (len(extra) // 3),
        compiler_params=params(6 + layer),
        cost_estimate=cost(60e9, 40e6),
    )(grad, h1, gains, a2, hid, slope, wu, wd, *extra)


def attend_back_kernel(size, layer, parts, *refs):
    mid_ref, qkv_ref, qm_ref, km_ref, ctx_ref, lse_ref, w_ref = refs[:7]
    refs = refs[7:]
    if layer == 0:
        gdown_ref, refs = refs[0], refs[1:]
    dqkv_ref, gout_ref, refs = refs[0], refs[1], refs[2:]
    if layer == 0:
        down_out, refs = refs[0], refs[1:]
    da, ka, va, kt, dk, dv, w, w_sem = refs[:8]
    sems, refs = refs[8:12], refs[12:]
    reduce = Reduce(layer, refs[:9])
    if layer == 0:
        down = HalfReduce(layer, refs[9 : 9 + HALF])
        down_swap = HalfSwap(gdown_ref, down.other, refs[9 + HALF])
    _, rows, wide = qkv_ref.shape
    length = size * rows
    e = qm_ref.shape[2]
    heads = wide // (3 * e)
    scale = e**-0.5
    c = scale * math.log2(math.e)
    depth = w_ref.shape[1] // parts
    n = chunks(rows)
    rc = rows // n
    bq = size * rc
    kc = bq
    g = Group(size)
    copies = [pltpu.make_async_copy(w_ref, w, w_sem.at[0])]
    for copy in copies:
        copy.start()
    g.greet(parts)
    gather = Gather(g, da, rc, sems)
    loads = []
    if layer == 0:
        down_swap.copy().start()
        loads = down.loads(gdown_ref, None)
        for load in loads:
            load.start()

    def send(j):
        at = span(j, rc)
        da[g.me, at, :] = mid_ref[at, :].astype(BF)
        gather.start(j)

    run(n, send)
    lane = lax.broadcasted_iota(jnp.int32, (length, e), 1)
    whole = flat(qkv_ref[...])
    for h in range(heads):
        o = 3 * e * h
        ka[h, :, :e] = whole[:, o + e : o + 2 * e]
        ka[h, :, e:] = flat(km_ref[...])
        va[h, :, :e] = whole[:, o + 2 * e : o + 3 * e]
        va[h, :, e:] = jnp.where(lane < 3, 1.0, 0.0).astype(BF)
        kt[h] = whole[:, o + e : o + 2 * e].T
    dk[...] = jnp.zeros_like(dk)
    dv[...] = jnp.zeros_like(dv)
    ql = lax.broadcasted_iota(jnp.int32, (bq, e), 1)
    for copy in copies + loads:
        copy.wait()

    def out_grad(z):
        cols = pl.ds(pl.multiple_of(z * depth, depth), depth)
        return dg(flat(ctx_ref[...]), flat(da[:, :, cols]), TN)

    def work(j):
        at = span(j, rc)

        @pl.when(j == 0)
        def _():
            gather.relay(0)
            gather.ready(0)

        @pl.when(j == min(1, n - 1))
        def _():
            for i in range(1, n):
                gather.relay(i)
            for i in range(1, n):
                gather.ready(i)
            reduce.send(out_grad)

        qm = flat(qm_ref[:, at, :])
        dctx = dg(flat(da[:, at, :]), w[...], NT).astype(BF)
        ctx = flat(ctx_ref[:, at, :])
        held_qkv = flat(qkv_ref[:, at, :])
        for h in range(heads):
            o = 3 * e * h
            qq = held_qkv[:, o : o + e]
            q = jnp.concatenate([qq, qm], axis=1)
            dc = dctx[:, h * e : (h + 1) * e]
            prod = dc.astype(F32) * ctx[:, h * e : (h + 1) * e].astype(F32)
            d = -jnp.sum(prod, axis=1, keepdims=True)
            d1 = d.astype(BF).astype(F32)
            d2 = (d - d1).astype(BF).astype(F32)
            d3 = d - d1 - d2
            ds_col = jnp.where(ql == 0, d1, jnp.where(ql == 1, d2, jnp.where(ql == 2, d3, 0.0)))
            dca = jnp.concatenate([dc, ds_col.astype(BF)], axis=1)
            lse = lse_ref[j, h : h + 1, :]
            dqt = None
            for k in range(length // kc):
                ks = slice(k * kc, (k + 1) * kc)
                s = dg(ka[h, ks, :], q, NT)
                p = jnp.exp2(s * c - lse)
                ds = (p * dg(va[h, ks, :], dca, NT)).astype(BF)
                dv[h, ks, :] += dg(p.astype(BF), dc, NN)
                dk[h, ks, :] += dg(ds, qq, NN)
                a = dg(kt[h, :, ks], ds, NN)
                dqt = a if dqt is None else dqt + a
            if layer == 0 and h == heads // 2:

                @pl.when(j == min(1, n - 1))
                def _():
                    down_swap.copy().wait_recv()
                    down.middle()

            if layer == 0 and h == heads - 1:

                @pl.when(j == n - 1)
                def _():
                    down.late()

            dqkv_ref[:, at, o : o + e] = (dqt * scale).T.astype(BF).reshape(size, rc, e)

    run(n, work)
    for h in range(heads):
        o = 3 * e * h
        dqkv_ref[:, :, o + e : o + 2 * e] = (dk[h] * scale).astype(BF).reshape(size, rows, e)
        dqkv_ref[:, :, o + 2 * e : o + 3 * e] = dv[h].astype(BF).reshape(size, rows, e)

    reduce.collect()
    reduce.finish(gout_ref)
    if layer == 0:
        down.finish(down_out)
        down_swap.copy().wait_send()
    gather.drain(n)


def attend_backward(size, replicas, layer, mid, qkv, qm, km, ctx, lse, w, grads):
    _, rows, wide = qkv.shape
    e = qm.shape[2]
    heads = wide // (3 * e)
    width = mid.shape[1]
    parts, depth = replicas, width // replicas
    length = size * rows
    n = chunks(rows)
    return pl.pallas_call(
        functools.partial(attend_back_kernel, size, layer, parts),
        out_shape=[shape(qkv.shape, BF), shape((heads * e, depth), F32)]
        + [shape(grad.shape[1:], F32) for grad in grads],
        in_specs=[VM] * 6 + [HB] * (1 + len(grads)),
        out_specs=[VM, VM] + [VM] * len(grads),
        scratch_shapes=[
            pltpu.VMEM((size, rows, width), BF),
            pltpu.VMEM((heads, length, 2 * e), BF),
            pltpu.VMEM((heads, length, 2 * e), BF),
            pltpu.VMEM((heads, e, length), BF),
            pltpu.VMEM((heads, length, e), F32),
            pltpu.VMEM((heads, length, e), F32),
            pltpu.VMEM((heads * e, width), BF),
            DMA((1,)),
        ]
        + comm_sems(size, n)
        + reduce_scratch(parts, heads * e, depth)
        + sum([half_scratch(parts, *grad.shape[1:]) + [DMA((2,))] for grad in grads], []),
        compiler_params=params(8 + layer),
        cost_estimate=cost(90e9, 40e6),
    )(mid, qkv, qm, km, ctx, lse, w, *grads)


def qkv_back_kernel(
    size, layer, parts, dqkv_ref, gain_ref, a1_in, x_in, mid_in, w_ref,
    dx_ref, gain_out, gqkv_ref, a1_ref, x_ref, mid_ref, w, w_sem, *scratch
):
    rows, width = x_ref.shape
    late = [
        pltpu.make_async_copy(a1_in, a1_ref, w_sem.at[1]),
        pltpu.make_async_copy(x_in, x_ref, w_sem.at[2]),
        pltpu.make_async_copy(mid_in, mid_ref, w_sem.at[3]),
    ]
    depth = width // parts
    n = thin_chunks(rows)
    rc = rows // n
    g = Group(size)
    copies = [pltpu.make_async_copy(w_ref, w, w_sem.at[0])]
    for copy in copies + late:
        copy.start()
    g.greet()
    scatter = Scatter(g, rc, scratch)
    for copy in copies:
        copy.wait()

    lag = min(2, n)

    def work(j):
        at = span(j, rc)
        held = flat(dqkv_ref[:, at, :])
        for z in range(parts):
            cols = slice(z * depth, (z + 1) * depth)
            scatter.part[:, at, cols] = dg(held, w[cols, :], NT).reshape(size, rc, depth)
        scatter.first(j)

        @pl.when(j >= lag)
        def _():
            scatter.second(j - lag)


    run(n, work)
    for j in range(n - lag, n):
        scatter.second(j)
    for copy in late:
        copy.wait()

    def qkv_grad(z):
        cols = pl.ds(pl.multiple_of(z * depth, depth), depth)
        gqkv_ref[z] = dg(flat(a1_ref[:, :, cols]), flat(dqkv_ref[...]), TN).astype(BF)

    run(parts, qkv_grad)
    gain_out[...] = jnp.zeros_like(gain_out)

    def last(j):
        at = span(j, rc)
        dh, dgain = normed_back(
            x_ref[at, :].astype(F32), gain_ref[layer, 0:1, :], scatter.third(j)
        )
        dx_ref[at, :] = (mid_ref[at, :] + dh).astype(BF)
        gain_out[...] += dgain

    run(n, last)
    scatter.drain(n)


def qkv_backward(size, replicas, layer, dqkv, a1, x, mid, gains, w):
    rows, width = x.shape
    wide = w.shape[1]
    parts, depth = replicas, width // replicas
    n = thin_chunks(rows)
    return pl.pallas_call(
        functools.partial(qkv_back_kernel, size, layer, parts),
        out_shape=(
            shape((rows, width), BF),
            shape((1, width), F32),
            shape((parts, depth, wide), BF),
        ),
        in_specs=[VM, VM] + [HB] * 4,
        out_specs=(VM, VM, VM),
        scratch_shapes=[
            pltpu.VMEM((size, rows, width), BF),
            pltpu.VMEM((rows, width), BF),
            pltpu.VMEM((rows, width), F32),
            pltpu.VMEM((width, wide), BF),
            DMA((4,)),
        ]
        + scatter_scratch(size, rows, width, n),
        compiler_params=params(11),
        cost_estimate=cost(30e9, 30e6),
    )(dqkv, gains, a1, x, mid, w)


def last_kernel(
    size, parts, dqkv_ref, a1_ref, x_ref, mid_ref, gain_ref, w_ref, two_ref, above_ref, dx1_ref,
    gain_out, gqkv_out, dx_out,
    gqkv, swap_sem, w, dx, gsum, gcame, w_sem, x_sem, x_send, x_recv, g_send, g_recv, *scratch
):
    rows, width = x_ref.shape
    depth = width // parts
    n = thin_chunks(rows)
    rc = rows // n
    g = Group(size)
    section = lax.axis_index("section")
    d = lax.axis_index("dp")
    copy = pltpu.make_async_copy(w_ref, w, w_sem.at[0])
    copy.start()
    reduce = HalfReduce(0, scratch[:HALF])
    swap = HalfSwap(gqkv, reduce.other, swap_sem)
    scatter = Scatter(g, rc, scratch[HALF:])
    g.greet(parts)

    def upper():
        return far_copy(
            dx1_ref, dx_out.at[0], x_send.at[n], x_recv.at[n], {"section": 1 - section}
        )

    def keep_upper():
        return pltpu.make_async_copy(dx1_ref, dx_out.at[1], x_sem.at[0])

    def lower(j):
        at = span(j, rc)
        return far_copy(
            dx.at[at], dx_out.at[1, at], x_send.at[j], x_recv.at[j], {"section": 1 - section}
        )

    def keep_lower(j):
        at = span(j, rc)
        return pltpu.make_async_copy(dx.at[at], dx_out.at[0, at], x_sem.at[j])

    def qkv_grad(z):
        cols = pl.ds(pl.multiple_of(z * depth, depth), depth)
        gqkv[z] = dg(flat(a1_ref[:, :, cols]), flat(dqkv_ref[...]), TN).astype(BF)

    run(parts, qkv_grad)
    swap.copy().start()
    load = reduce.loads(gqkv, None)[0]
    load.start()

    @pl.when(section == 1)
    def _():
        keep_upper().start()

    copy.wait()

    lag = min(2, n)

    def work(j):
        at = span(j, rc)
        held = flat(dqkv_ref[:, at, :])
        for z in range(parts):
            cols = slice(z * depth, (z + 1) * depth)
            scatter.part[:, at, cols] = dg(held, w[cols, :], NT).reshape(size, rc, depth)
        scatter.first(j)

        @pl.when(j >= lag)
        def _():
            scatter.second(j - lag)


    run(n, work)
    for j in range(n - lag, n):
        scatter.second(j)
    gsum[0] = jnp.zeros_like(gsum[0])

    def last(j):
        at = span(j, rc)
        dh, dgain = normed_back(x_ref[at, :].astype(F32), gain_ref[0, 0:1, :], scatter.third(j))
        dx[at, :] = (mid_ref[at, :] + dh).astype(BF)

        @pl.when(section == 0)
        def _():
            keep_lower(j).start()

        @pl.when(section == 1)
        def _():
            lower(j).start()

        gsum[0, 0:1, :] += dgain

    def rest(j):
        @pl.when(j == n // 2)
        def _():
            load.wait()
            swap.copy().wait_recv()
            reduce.middle()

            @pl.when(section == 0)
            def _():
                upper().start()

        last(j)

    run(n, rest)
    gsum[0, 1:2, :] = two_ref[...]
    gsum[0, 2:4, :] = above_ref[...]

    targets = [
        [{"tensor": g.sibling}],
        [{"tensor": g.ahead(k) * 2 + g.core} for k in range(1, g.chips)],
        [{"dp": lax.rem(d + k, parts)} for k in range(1, parts)],
        [{"section": 1 - section}],
    ]
    slot = 0
    sent = []

    def exchange(stage):
        nonlocal slot
        copies = []
        for target in targets[stage]:
            copies.append(
                far_copy(gsum.at[stage], gcame.at[slot], g_send.at[slot], g_recv.at[slot], target)
            )
            copies[-1].start()
            slot += 1
        total = gsum[stage]
        for i, copy in enumerate(copies):
            copy.wait_recv()
            total = total + gcame[slot - len(copies) + i]
        gsum[stage + 1] = total
        sent.extend(copies)

    exchange(0)
    exchange(1)
    reduce.late()
    exchange(2)
    exchange(3)
    gain_out[...] = gsum[4]

    @pl.when(section == 0)
    def _():
        for j in range(n):
            lower(j).wait_recv()
            keep_lower(j).wait()
        upper().wait_send()

    @pl.when(section == 1)
    def _():
        keep_upper().wait()
        upper().wait_recv()
        for j in range(n):
            lower(j).wait_send()

    reduce.finish(gqkv_out)
    swap.copy().wait_send()
    for copy in sent:
        copy.wait_send()
    scatter.drain(n)


def last_backward(size, replicas, dqkv, a1, x, mid, gains, w, two, above, dx1):
    rows, width = x.shape
    wide = w.shape[1]
    depth = width // replicas
    n = thin_chunks(rows)
    slots = 1 + (size // 2 - 1) + (replicas - 1) + 1
    return pl.pallas_call(
        functools.partial(last_kernel, size, replicas),
        out_shape=(
            shape((8, width), F32),
            shape((depth, wide), F32),
            shape((2, rows, width), BF),
        ),
        in_specs=[VM] * 5 + [HB, VM, VM, VM],
        out_specs=(VM, VM, HB),
        scratch_shapes=[
            pltpu.VMEM((replicas, depth, wide), BF),
            DMA((2,)),
            pltpu.VMEM((width, wide), BF),
            pltpu.VMEM((rows, width), BF),
            pltpu.VMEM((5, 8, width), F32),
            pltpu.VMEM((slots, 8, width), F32),
            DMA((1,)),
            DMA((n,)),
            DMA((n + 1,)),
            DMA((n + 1,)),
            DMA((slots,)),
            DMA((slots,)),
        ]
        + half_scratch(replicas, depth, wide)
        + scatter_scratch(size, rows, width, n),
        compiler_params=params(10),
        cost_estimate=cost(40e9, 30e6),
    )(dqkv, a1, x, mid, gains, w, two, above, dx1)


def scene_masks(segments, e):
    same = (segments[..., None] == jnp.arange(e, dtype=jnp.int32)).astype(F32)
    used = jnp.arange(e) < SCENES
    return (
        jnp.where(used, same * MASKED, 0.0).astype(BF),
        jnp.where(used, 1.0 - same, 0.0).astype(BF),
    )


def swap_section(value):
    return lax.ppermute(value, "section", [(0, 1), (1, 0)])


def shards(
    block_input,
    segment_ids,
    cotangent,
    norm_one_gain,
    qkv_weight,
    out_weight,
    norm_two_gain,
    up_weight,
    down_weight,
):
    section = lax.axis_index("section")
    size = lax.axis_size("tensor")
    replicas = lax.axis_size("dp")

    mine = [
        qkv_weight[0].reshape((qkv_weight.shape[1], -1)),
        out_weight[0].reshape((-1, out_weight.shape[3])),
        up_weight[0],
        down_weight[0],
    ]
    mine = [w.astype(BF).reshape((2, -1, w.shape[1])) for w in mine]
    gains = jnp.concatenate(
        [norm_one_gain, norm_two_gain, jnp.zeros((6, norm_one_gain.shape[1]), F32)], axis=0
    )
    segments = lax.dynamic_index_in_dim(segment_ids, section, 0, keepdims=False)
    x = lax.dynamic_index_in_dim(block_input, section, 0, keepdims=False)
    head_dim = qkv_weight.shape[3] // 3
    qm, km = scene_masks(segments.reshape((size, -1)), head_dim)
    qkv, gains, a1, w_qkv_0, w_out_0, h_qkv, h_out, h_up, h_down = first_forward(
        size, replicas, x, gains, mine
    )
    h1, ctx, lse, w_up_0, w_down_0 = attend(
        size, replicas, 0, qkv, qm, km, x, w_out_0,
        [(h_up, "spread", 0, False), (h_down, "spread", 0, True)],
    )
    below = (x, a1, qkv, ctx, lse, h1)
    y0, qkv, a2, hid, slope, a1, w_qkv_1, w_out_1, w_up_1, got_down = turn_forward(
        size, replicas, h1, gains, w_up_0, w_down_0, h_qkv,
        [(h_out, "spread", 1, True), (h_up, "spread", 1, False), (h_down, "z", 1, True)],
    )
    kept = [below + (a2, hid, slope)]
    grad = lax.dynamic_index_in_dim(cotangent, section, 0, keepdims=False)
    h1, ctx, lse, grad_all, w_down_1 = attend(
        size, replicas, 1, qkv, qm, km, y0, w_out_1, [(got_down, "y", 1, True)], [grad]
    )
    y1, a2, hid, slope = mlp_forward(size, replicas, 1, h1, gains, w_up_1, w_down_1, [])
    kept.append((y0, a1, qkv, ctx, lse, h1, a2, hid, slope))
    weights = [
        (w_qkv_0, w_out_0, w_up_0, w_down_0),
        (w_qkv_1, w_out_1, w_up_1, w_down_1),
    ]
    def reduce_rows(value):
        return lax.psum_scatter(value, "dp", scatter_dimension=0, tiled=False)

    x, a1, qkv, ctx, lse, h1, a2, hid, slope = kept[1]
    w_qkv, w_out, w_up, w_down = weights[1]
    mid, gain_two, g_up, g_down, layer_out = mlp_backward(
        size, replicas, 1, grad, h1, gains, a2, hid, slope, w_up, w_down, [y0, y1, grad_all]
    )
    d_qkv, out_1 = attend_backward(size, replicas, 1, mid, qkv, qm, km, ctx, lse, w_out, [])
    up_1, down_1 = reduce_rows(g_up), reduce_rows(g_down)
    dx1, gain_one, g_qkv = qkv_backward(size, replicas, 1, d_qkv, a1, x, mid, gains, w_qkv)
    gains_above = jnp.concatenate([gain_one, gain_two], axis=0)
    dx1, up_1, down_1 = lax.optimization_barrier((dx1, up_1, down_1))
    qkv_1 = reduce_rows(g_qkv)

    x, a1, qkv, ctx, lse, h1, a2, hid, slope = kept[0]
    w_qkv, w_out, w_up, w_down = weights[0]
    mid, gain_two, g_up, g_down = mlp_backward(
        size, replicas, 0, dx1, h1, gains, a2, hid, slope, w_up, w_down, []
    )
    mid, qkv_1 = lax.optimization_barrier((mid, qkv_1))
    d_qkv, out_0, down_0 = attend_backward(
        size, replicas, 0, mid, qkv, qm, km, ctx, lse, w_out, [g_down]
    )
    up_0 = reduce_rows(g_up)
    d_qkv, up_0 = lax.optimization_barrier((d_qkv, up_0))
    gains, qkv_0, input_out = last_backward(
        size, replicas, d_qkv, a1, x, mid, gains, w_qkv, gain_two, gains_above, dx1
    )

    def finish(zero, one):
        send = swap_section(jnp.where(section == 0, one, zero))
        return jnp.where(section == 0, zero, one).astype(F32) + send.astype(F32)

    other_qkv_1 = swap_section(qkv_1)
    qkv_grad = jnp.where(section == 0, qkv_0, qkv_1.astype(F32) + other_qkv_1.astype(F32))
    out_grad = jnp.where(section == 0, out_0, out_1)
    up_grad = finish(up_0, up_1)
    other_down_1 = swap_section(down_1)
    down_grad = jnp.where(section == 0, down_0, down_1.astype(F32) + other_down_1.astype(F32))
    gains = lax.dynamic_slice_in_dim(gains, 2 * section, 2, 0)
    return (
        layer_out[None],
        input_out[None],
        gains[0:1],
        qkv_grad.reshape(qkv_weight.shape),
        out_grad.reshape(out_weight.shape),
        gains[1:2],
        up_grad[None],
        down_grad[None],
    )


def solution(mesh):
    return jax.shard_map(
        shards,
        mesh=mesh,
        in_specs=(
            P(None, ("dp", "tensor"), None),
            P(None, "dp"),
            P(None, ("dp", "tensor"), None),
            P("section", None),
            P("section", "dp", "tensor", None),
            P("section", "tensor", None, "dp"),
            P("section", None),
            P("section", "dp", "tensor"),
            P("section", "tensor", "dp"),
        ),
        out_specs=(
            P("section", None, ("dp", "tensor"), None),
            P("section", None, ("dp", "tensor"), None),
            P("section", None),
            P("section", "dp", "tensor", None),
            P("section", "tensor", None, "dp"),
            P("section", None),
            P("section", "dp", "tensor"),
            P("section", "tensor", "dp"),
        ),
        check_vma=False,
    )
```

```python
import functools
import math

import jax
import jax.numpy as jnp
from jax import lax
from jax.experimental import pallas as pl
from jax.experimental.pallas import tpu as pltpu
from jax.sharding import PartitionSpec as P

F32 = jnp.float32
BF = jnp.bfloat16
NT = (((1,), (1,)), ((), ()))
NN = (((1,), (0,)), ((), ()))
TN = (((0,), (0,)), ((), ()))
MASKED = -1e30
SCENES = 3
MESH = pl.DeviceIdType.MESH
VM = pl.BlockSpec(memory_space=pltpu.VMEM)
HB = pl.BlockSpec(memory_space=pl.ANY)
DMA = pltpu.SemaphoreType.DMA
LIMIT = 58 << 20


def dg(a, b, dims):
    return lax.dot_general(a, b, dims, preferred_element_type=F32)


def chunks(rows):
    return 4 if rows % 64 == 0 else 1


def thin_chunks(rows):
    return 8 if rows % 128 == 0 else chunks(rows)


def shape(dims, dtype):
    return jax.ShapeDtypeStruct(dims, dtype)


class Group:
    def __init__(self, size):
        self.size = size
        self.chips = size // 2
        self.me = lax.axis_index("tensor")
        self.chip = lax.div(self.me, 2)
        self.core = lax.rem(self.me, 2)
        self.sibling = self.chip * 2 + 1 - self.core

    def ahead(self, k):
        return lax.rem(self.chip + k, self.chips)

    def behind(self, k):
        return lax.rem(self.chip + self.chips - k, self.chips)

    def greet(self, replicas=0, side=False):
        barrier = pltpu.get_barrier_semaphore()
        targets = [self.sibling] + [self.ahead(k) * 2 + self.core for k in range(1, self.chips)]
        targets = [{"tensor": target} for target in targets]
        if replicas:
            d = lax.axis_index("dp")
            targets += [{"dp": lax.rem(d + k, replicas)} for k in range(1, replicas)]
        if replicas or side:
            targets += [{"section": 1 - lax.axis_index("section")}]
        for target in targets:
            pl.semaphore_signal(barrier, inc=1, device_id=target, device_id_type=MESH)
        pl.semaphore_wait(barrier, len(targets))


def remote(src, dst, send, recv, target):
    return pltpu.make_async_remote_copy(
        src_ref=src,
        dst_ref=dst,
        send_sem=send,
        recv_sem=recv,
        device_id={"tensor": target},
        device_id_type=MESH,
    )


def span(j, rc):
    return pl.ds(pl.multiple_of(j * rc, rc), rc)


def comm_sems(group_size, n):
    c = group_size // 2
    far, near = DMA((max(c - 1, 1), n)), DMA((c, n))
    return [far, far, near, near]


class Gather:
    def __init__(self, g, buf, rc, sems):
        self.g, self.buf, self.rc = g, buf, rc
        self.far_send, self.far_recv, self.near_send, self.near_recv = sems

    def far(self, k, j, origin, target, src=None):
        ref = self.buf.at[origin, span(j, self.rc)]
        src = ref if src is None else src
        return remote(src, ref, self.far_send.at[k - 1, j], self.far_recv.at[k - 1, j], target)

    def near(self, k, j, origin, src=None):
        ref = self.buf.at[origin, span(j, self.rc)]
        src = ref if src is None else src
        return remote(
            src, ref, self.near_send.at[k, j], self.near_recv.at[k, j], self.g.sibling
        )

    def start(self, j, src=None):
        g = self.g
        for k in range(1, g.chips):
            self.far(k, j, g.me, g.ahead(k) * 2 + g.core, src).start()
        self.near(0, j, g.me, src).start()

    def relay(self, j):
        g = self.g
        for k in range(1, g.chips):
            origin = g.behind(k) * 2 + g.core
            self.far(k, j, origin, g.me).wait_recv()
            self.near(k, j, origin).start()

    def ready(self, j):
        g = self.g
        self.near(0, j, g.sibling).wait_recv()
        for k in range(1, g.chips):
            self.near(k, j, g.behind(k) * 2 + 1 - g.core).wait_recv()

    def drain(self, n):
        g = self.g

        def one(j, _):
            for k in range(1, g.chips):
                self.far(k, j, g.me, g.sibling).wait_send()
            for k in range(g.chips):
                self.near(k, j, g.me).wait_send()
            return 0

        lax.fori_loop(0, n, one, 0)


def scatter_scratch(group_size, rows, width, n):
    c = group_size // 2
    far = pltpu.VMEM((max(c - 1, 1), rows, width), BF)
    near = pltpu.VMEM((c, rows, width), BF)
    return [pltpu.VMEM((group_size, rows, width), F32), near, near, far, far] + comm_sems(
        group_size, n
    )


class Scatter:
    def __init__(self, g, rc, scratch):
        self.g, self.rc = g, rc
        self.part, self.near_out, self.near_in, self.far_out, self.far_in = scratch[:5]
        self.far_send, self.far_recv, self.near_send, self.near_recv = scratch[5:]

    def near(self, k, j):
        rows = span(j, self.rc)
        return remote(
            self.near_out.at[k, rows],
            self.near_in.at[k, rows],
            self.near_send.at[k, j],
            self.near_recv.at[k, j],
            self.g.sibling,
        )

    def far(self, k, j):
        rows = span(j, self.rc)
        return remote(
            self.far_out.at[k - 1, rows],
            self.far_in.at[k - 1, rows],
            self.far_send.at[k - 1, j],
            self.far_recv.at[k - 1, j],
            self.g.ahead(k) * 2 + self.g.core,
        )

    def first(self, j):
        g, rows = self.g, span(j, self.rc)
        for k in list(range(1, g.chips)) + [0]:
            owner = g.ahead(k) * 2 + 1 - g.core
            self.near_out[k, rows, :] = self.part[owner, rows, :].astype(BF)
            self.near(k, j).start()

    def second(self, j):
        g, rows = self.g, span(j, self.rc)
        for k in range(1, g.chips):
            owner = g.ahead(k) * 2 + g.core
            self.near(k, j).wait_recv()
            both = self.part[owner, rows, :] + self.near_in[k, rows, :].astype(F32)
            self.far_out[k - 1, rows, :] = both.astype(BF)
            self.far(k, j).start()

    def third(self, j):
        g, rows = self.g, span(j, self.rc)
        self.near(0, j).wait_recv()
        total = self.part[g.me, rows, :] + self.near_in[0, rows, :].astype(F32)
        for k in range(1, g.chips):
            self.far(k, j).wait_recv()
            total = total + self.far_in[k - 1, rows, :].astype(F32)
        return total

    def drain(self, n):
        g = self.g

        def one(j, _):
            for k in range(1, g.chips):
                self.far(k, j).wait_send()
            for k in range(g.chips):
                self.near(k, j).wait_send()
            return 0

        lax.fori_loop(0, n, one, 0)


def far_copy(src, dst, send, recv, target):
    return pltpu.make_async_remote_copy(
        src_ref=src,
        dst_ref=dst,
        send_sem=send,
        recv_sem=recv,
        device_id=target,
        device_id_type=MESH,
    )


class Swap:
    def __init__(self, src, stage, sems):
        self.src, self.stage, self.sems = src, stage, sems
        self.s = lax.axis_index("section")

    def copies(self, layer):
        local = pltpu.make_async_copy(self.src.at[self.s], self.stage.at[self.s], self.sems.at[0])
        side = far_copy(
            self.src.at[1 - self.s],
            self.stage.at[layer],
            self.sems.at[1],
            self.sems.at[2],
            {"section": 1 - self.s},
        )
        return local, side

    def start(self):
        for copy in self.copies(self.s):
            copy.start()

    def arrive(self):
        local, side = self.copies(1 - self.s)
        local.wait()
        side.wait_recv()

    def finish(self):
        self.copies(self.s)[1].wait_send()


def reduce_scratch(replicas, rows, cols):
    many = pltpu.VMEM((replicas - 1, rows, cols), BF)
    one = pltpu.VMEM((rows, cols), BF)
    far, side = DMA((replicas - 1, 2)), DMA((2,))
    return [pltpu.VMEM((rows, cols), F32), many, many, one, one, far, far, side, side]


class Reduce:
    def __init__(self, layer, scratch):
        self.layer = layer
        self.own, self.away, self.came, self.over, self.back = scratch[:5]
        self.z_send, self.z_recv, self.y_send, self.y_recv = scratch[5:]
        self.replicas = self.away.shape[0] + 1
        self.half = self.own.shape[0] // 2
        self.d = lax.axis_index("dp")
        self.s = lax.axis_index("section")

    def target(self, k):
        return lax.rem(self.d + k, self.replicas)

    def part(self, i):
        return pl.ds(pl.multiple_of(i * self.half, self.half), self.half)

    def z_copy(self, k, i):
        part = self.part(i)
        return far_copy(
            self.away.at[k - 1, part],
            self.came.at[k - 1, part],
            self.z_send.at[k - 1, i],
            self.z_recv.at[k - 1, i],
            {"dp": self.target(k)},
        )

    def y_copy(self, i):
        part = self.part(i)
        return far_copy(
            self.over.at[part],
            self.back.at[part],
            self.y_send.at[i],
            self.y_recv.at[i],
            {"section": 1 - self.s},
        )

    def send(self, block):
        def one(i):
            k = i + 1
            self.away[i] = block(self.target(k)).astype(BF)
            self.z_copy(k, 0).start()
            self.z_copy(k, 1).start()

        run(self.replicas - 1, one)
        self.own[...] = block(self.d)

    def collect(self):
        def one(i):
            part = self.part(i)
            total = self.own[part, :]
            for k in range(1, self.replicas):
                self.z_copy(k, i).wait_recv()
                total = total + self.came[k - 1, part, :].astype(F32)
            self.own[part, :] = total
            self.over[part, :] = total.astype(BF)

            @pl.when(self.s != self.layer)
            def _():
                self.y_copy(i).start()

        run(2, one)

    def finish(self, out):
        @pl.when(self.s == self.layer)
        def _():
            self.y_copy(0).wait_recv()
            self.y_copy(1).wait_recv()
            out[...] = self.own[...] + self.back[...].astype(F32)

        @pl.when(self.s != self.layer)
        def _():
            self.y_copy(0).wait_send()
            self.y_copy(1).wait_send()
            out[...] = self.own[...]

        for k in range(1, self.replicas):
            self.z_copy(k, 0).wait_send()
            self.z_copy(k, 1).wait_send()


class HalfSwap:
    def __init__(self, src, came, sems):
        self.src, self.came, self.sems = src, came, sems
        self.s = lax.axis_index("section")
        self.rows = came.shape[1]

    def copy(self):
        at = pl.ds(pl.multiple_of((1 - self.s) * self.rows, self.rows), self.rows)
        return far_copy(
            self.src.at[:, at],
            self.came,
            self.sems.at[0],
            self.sems.at[1],
            {"section": 1 - self.s},
        )


def half_scratch(replicas, rows, cols):
    rows = rows // 2
    all_, far = pltpu.VMEM((replicas, rows, cols), BF), pltpu.VMEM((replicas - 1, rows, cols), BF)
    one = pltpu.VMEM((rows, cols), BF)
    z = DMA((replicas - 1,))
    return [all_, all_, far, far, pltpu.VMEM((rows, cols), F32), one, one, DMA((3,)), z, z, DMA((2,))]


HALF = 11


class HalfReduce:
    def __init__(self, layer, scratch):
        self.layer = layer
        self.mine, self.other, self.away, self.came, self.own, self.over, self.back = scratch[:7]
        self.in_sem, self.z_send, self.z_recv, self.y_sem = scratch[7:]
        self.replicas, self.rows = self.mine.shape[:2]
        self.s = lax.axis_index("section")
        self.d = lax.axis_index("dp")

    def half(self, s):
        return pl.ds(pl.multiple_of(s * self.rows, self.rows), self.rows)

    def loads(self, src, other):
        loads = [pltpu.make_async_copy(src.at[:, self.half(self.s)], self.mine, self.in_sem.at[0])]
        if other is not None:
            loads.append(pltpu.make_async_copy(other, self.other, self.in_sem.at[1]))
        return loads

    def z_copy(self, k):
        return far_copy(
            self.away.at[k - 1],
            self.came.at[k - 1],
            self.z_send.at[k - 1],
            self.z_recv.at[k - 1],
            {"dp": lax.rem(self.d + k, self.replicas)},
        )

    def y_copy(self):
        return far_copy(
            self.over, self.back, self.y_sem.at[0], self.y_sem.at[1], {"section": 1 - self.s}
        )

    def middle(self):
        def both(z):
            return self.mine[z].astype(F32) + self.other[z].astype(F32)

        for k in range(1, self.replicas):
            self.away[k - 1] = both(lax.rem(self.d + k, self.replicas)).astype(BF)
            self.z_copy(k).start()
        self.own[...] = both(self.d)

    def late(self):
        total = self.own[...]
        for k in range(1, self.replicas):
            self.z_copy(k).wait_recv()
            total = total + self.came[k - 1].astype(F32)
        self.own[...] = total
        self.over[...] = total.astype(BF)

        @pl.when(self.s != self.layer)
        def _():
            self.y_copy().start()

    def finish(self, out, above=None):
        @pl.when(self.s == self.layer)
        def _():
            self.y_copy().wait_recv()
            out[self.half(self.s), :] = self.own[...]
            out[self.half(1 - self.s), :] = self.back[...].astype(F32)

        @pl.when(self.s != self.layer)
        def _():
            if above is None:
                out[...] = jnp.zeros_like(out)
            else:
                copy = pltpu.make_async_copy(above, out, self.in_sem.at[2])
                copy.start()
                copy.wait()
            self.y_copy().wait_send()

        for k in range(1, self.replicas):
            self.z_copy(k).wait_send()


class Spread:
    def __init__(self, src, dst, by_columns, sems):
        self.src, self.dst, self.by_columns = src, dst, by_columns
        self.own_sem, self.far_send, self.far_recv, self.side_send, self.side_recv = sems
        self.replicas = far = self.side_send.shape[0]
        self.s = lax.axis_index("section")
        self.d = lax.axis_index("dp")
        self.stages = [
            sorted({k, far - k}) for k in range(1, far // 2 + 1)
        ]

    def place(self, half, z):
        rows, cols = self.src.shape
        if self.by_columns:
            return self.dst.at[
                pl.ds(pl.multiple_of(half * rows, rows), rows),
                pl.ds(pl.multiple_of(z * cols, cols), cols),
            ]
        return self.dst.at[pl.ds(pl.multiple_of((2 * z + half) * rows, rows), rows)]

    def origin(self, k):
        return lax.rem(self.d + self.replicas - k, self.replicas)

    def own(self):
        return pltpu.make_async_copy(self.src, self.place(self.s, self.d), self.own_sem.at[0])

    def far(self, k, origin):
        return pltpu.make_async_remote_copy(
            src_ref=self.src,
            dst_ref=self.place(self.s, origin),
            send_sem=self.far_send.at[k - 1],
            recv_sem=self.far_recv.at[k - 1],
            device_id={"dp": lax.rem(self.d + k, self.replicas)},
            device_id_type=MESH,
        )

    def side(self, k, half):
        place = self.place(half, self.origin(k))
        return pltpu.make_async_remote_copy(
            src_ref=self.src if k == 0 else place,
            dst_ref=place,
            send_sem=self.side_send.at[k],
            recv_sem=self.side_recv.at[k],
            device_id={"section": 1 - self.s},
            device_id_type=MESH,
        )

    def start(self):
        for k in self.stages[0]:
            self.far(k, self.d).start()
        self.side(0, self.s).start()
        self.own().start()

    def step(self, i):
        for k in self.stages[i]:
            self.far(k, self.origin(k)).wait_recv()
            self.side(k, self.s).start()
        if i + 1 < len(self.stages):
            for k in self.stages[i + 1]:
                self.far(k, self.d).start()

    def finish(self):
        self.own().wait()
        for k in range(self.replicas):
            self.side(k, 1 - self.s).wait_recv()
        for k in range(1, self.replicas):
            self.far(k, self.d).wait_send()
        for k in range(self.replicas):
            self.side(k, self.s).wait_send()


class ZGather:
    def __init__(self, src, got, sems):
        self.src, self.got = src, got
        self.own_sem, self.send, self.recv = sems
        self.replicas = got.shape[0]
        self.d = lax.axis_index("dp")

    def own(self):
        return pltpu.make_async_copy(self.src, self.got.at[self.d], self.own_sem.at[0])

    def far(self, k, origin):
        return far_copy(
            self.src,
            self.got.at[origin],
            self.send.at[k - 1],
            self.recv.at[k - 1],
            {"dp": lax.rem(self.d + k, self.replicas)},
        )

    def start(self):
        for k in range(1, self.replicas):
            self.far(k, self.d).start()
        self.own().start()

    def step(self, i):
        pass

    def finish(self):
        self.own().wait()
        for k in range(1, self.replicas):
            self.far(k, lax.rem(self.d + self.replicas - k, self.replicas)).wait_recv()
        for k in range(1, self.replicas):
            self.far(k, self.d).wait_send()


class YJoin:
    def __init__(self, got, dst, by_columns, sems):
        self.src, self.dst, self.by_columns = got, dst, by_columns
        self.own_sem, self.send, self.recv, self.got, self.in_sem = sems
        self.replicas, self.rows, self.cols = got.shape
        self.s = lax.axis_index("section")

    def place(self, half, z):
        rows, cols = self.rows, self.cols
        if self.by_columns:
            return self.dst.at[
                pl.ds(pl.multiple_of(half * rows, rows), rows), pl.ds(z * cols, cols)
            ]
        return self.dst.at[pl.ds(pl.multiple_of((2 * z + half) * rows, rows), rows)]

    def own(self, z):
        return pltpu.make_async_copy(self.got.at[z], self.place(self.s, z), self.own_sem.at[z])

    def side(self, z, half):
        return far_copy(
            self.got.at[z],
            self.place(half, z),
            self.send.at[z],
            self.recv.at[z],
            {"section": 1 - self.s},
        )

    def start(self):
        load = pltpu.make_async_copy(self.src, self.got, self.in_sem.at[0])
        load.start()
        load.wait()
        for z in range(self.replicas):
            self.side(z, self.s).start()
            self.own(z).start()

    def step(self, i):
        pass

    def finish(self):
        for z in range(self.replicas):
            self.own(z).wait()
            self.side(z, 1 - self.s).wait_recv()
        for z in range(self.replicas):
            self.side(z, self.s).wait_send()


def rider_sems(replicas):
    far, side = DMA((replicas - 1,)), DMA((replicas,))
    return [DMA((1,)), far, far, side, side]


class Riders:
    def __init__(self, srcs, dsts, columns, sems):
        self.all = []
        for src, dst, (kind, layer, by) in zip(srcs, dsts, columns):
            count = 3 if kind == "z" else 5
            own, sems = sems[:count], sems[count:]
            if kind == "spread":
                self.all.append(Spread(src.at[layer], dst, by, own))
            elif kind == "z":
                self.all.append(ZGather(src.at[layer], dst, own))
            else:
                self.all.append(YJoin(src, dst, by, own))
        self.replicas = self.all[0].replicas if self.all else 0

    def start(self):
        for one in self.all:
            one.start()

    def step(self, j, n):
        if not self.all:
            return
        stages = self.replicas // 2
        for i in range(stages):

            @pl.when(j == n * (i + 1) // stages - 1)
            def _(i=i):
                for one in self.all:
                    one.step(i)

    def finish(self):
        for one in self.all:
            one.finish()


def riding(riders, replicas):
    arrays = [array for array, _, _, _ in riders]
    columns = tuple(rider[1:] for rider in riders)
    outs, sems = [], []
    for array, kind, _, by in riders:
        rows, cols = array.shape[1:]
        if kind == "z":
            outs.append(shape((replicas, rows, cols), BF))
        else:
            outs.append(
                shape((2 * rows, replicas * cols) if by else (2 * replicas * rows, cols), BF)
            )
        far, side = DMA((replicas - 1,)), DMA((replicas,))
        sems += {
            "spread": rider_sems(replicas),
            "z": [DMA((1,)), far, far],
            "y": [side, side, side, pltpu.VMEM(array.shape, BF), DMA((1,))],
        }[kind]
    return arrays, columns, outs, sems


def params(key):
    return pltpu.CompilerParams(
        vmem_limit_bytes=LIMIT, collective_id=key, has_side_effects=True
    )


def cost(flops, moved, exps=0):
    return pl.CostEstimate(flops=int(flops), bytes_accessed=int(moved), transcendentals=int(exps))


def normed(source):
    center = source - jnp.mean(source, axis=-1, keepdims=True)
    r = lax.rsqrt(jnp.mean(center * center, axis=-1, keepdims=True) + 1e-05)
    return center * r, r


def normed_back(source, gain, grad):
    n, r = normed(source)
    e = grad * gain
    dh = r * (
        e - jnp.mean(e, axis=-1, keepdims=True) - n * jnp.mean(e * n, axis=-1, keepdims=True)
    )
    return dh, jnp.sum(grad * n, axis=0, keepdims=True)


def flat(value):
    return value.reshape((value.shape[0] * value.shape[1],) + value.shape[2:])


def run(n, body):
    def one(j, carry):
        body(j)
        return carry

    lax.fori_loop(0, n, one, 0)


def first_kernel(
    size, replicas, x_ref, gain_ref, wq_ref, wo_ref, wu_ref, wd_ref,
    qkv_ref, gains_out, a1_out, wq_out, wo_out, q_stage, o_stage, u_stage, d_stage,
    a1, w, gains, own_sem, q_sem, o_sem, u_sem, d_sem, gain_sem, *sems
):
    rows, width = x_ref.shape
    n = thin_chunks(rows)
    rc = rows // n
    g = Group(size)
    section = lax.axis_index("section")
    gather = Gather(g, a1, rc, sems[:4])
    swaps = [
        Swap(wq_ref, q_stage, q_sem),
        Swap(wo_ref, o_stage, o_sem),
        Swap(wu_ref, u_stage, u_sem),
        Swap(wd_ref, d_stage, d_sem),
    ]
    spreads = [
        Spread(q_stage.at[0], w, False, sems[4:9]),
        Spread(o_stage.at[0], wo_out, True, sems[9:14]),
    ]
    riders = Riders([], [], (), [])
    riders.all = spreads
    riders.replicas = replicas
    g.greet(replicas)

    def gain_copy(layer):
        return far_copy(
            gain_ref, gains.at[layer], gain_sem.at[0], gain_sem.at[1], {"section": 1 - section}
        )

    gain_copy(section).start()
    swaps[0].start()
    swaps[1].start()
    gains[section] = gain_ref[...]
    gain_copy(1 - section).wait_recv()
    gains_out[...] = gains[...]

    def send(j):
        at = span(j, rc)
        a = normed(x_ref[at, :].astype(F32))[0] * gains[0, 0:1, :]
        a1[g.me, at, :] = a.astype(BF)
        gather.start(j)

    run(n, send)
    swaps[0].arrive()
    swaps[1].arrive()
    riders.start()

    def relay(j):
        gather.relay(j)
        riders.step(j, n)

    run(n, relay)
    swaps[2].start()
    swaps[3].start()
    riders.finish()
    outs = [
        pltpu.make_async_copy(w, wq_out, own_sem.at[0]),
        pltpu.make_async_copy(a1, a1_out, own_sem.at[1]),
    ]
    outs[0].start()

    def multiply(j):
        at = span(j, rc)
        gather.ready(j)
        r = dg(flat(a1[:, at, :]), w[...], NN).astype(BF)
        qkv_ref[:, at, :] = r.reshape(size, rc, r.shape[1])

    run(n, multiply)
    outs[1].start()
    swaps[2].arrive()
    swaps[3].arrive()
    for swap in swaps:
        swap.finish()
    gain_copy(section).wait_send()
    gather.drain(n)
    for out in outs:
        out.wait()


def first_forward(size, replicas, x, gains, ws):
    rows, width = x.shape
    wide = ws[0].shape[2]
    deep = 2 * ws[1].shape[1]
    n = thin_chunks(rows)
    return pl.pallas_call(
        functools.partial(first_kernel, size, replicas),
        out_shape=[
            shape((size, rows, wide), BF),
            shape((2,) + gains.shape, F32),
            shape((size, rows, width), BF),
            shape((width, wide), BF),
            shape((deep, width), BF),
        ]
        + [shape(w.shape, BF) for w in ws],
        in_specs=[VM] * 6,
        out_specs=[VM, VM] + [HB] * 7,
        scratch_shapes=[
            pltpu.VMEM((size, rows, width), BF),
            pltpu.VMEM((width, wide), BF),
            pltpu.VMEM((2,) + gains.shape, F32),
            DMA((2,)),
            DMA((3,)),
            DMA((3,)),
            DMA((3,)),
            DMA((3,)),
            DMA((2,)),
        ]
        + comm_sems(size, n)
        + rider_sems(replicas) * 2,
        compiler_params=params(0),
        cost_estimate=cost(30e9, 30e6),
    )(x, gains, *ws)


def attend_kernel(size, layer, columns, *refs):
    m = len(columns)
    qkv_ref, qm_ref, km_ref, x_ref, w_ref = refs[:5]
    refs = refs[5:]
    if layer == 1:
        cot_ref, refs = refs[0], refs[1:]
    halves, refs = refs[:m], refs[m:]
    h1_ref, ctx_ref, lse_ref = refs[:3]
    refs = refs[3:]
    if layer == 1:
        cot_out, refs = refs[0], refs[1:]
    wholes, refs = refs[:m], refs[m:]
    ka, vt, w, w_sem = refs[:4]
    scratch, refs = refs[4:13], refs[13:]
    if layer == 1:
        cot_sems, cot_sem, refs = refs[:4], refs[4], refs[5:]
    riders = Riders(halves, wholes, columns, refs)
    _, rows, wide = qkv_ref.shape
    length = size * rows
    e = qm_ref.shape[2]
    heads = wide // (3 * e)
    c = e**-0.5 * math.log2(math.e)
    n = chunks(rows)
    rc = rows // n
    bq = size * rc
    kc = bq
    g = Group(size)
    copy = pltpu.make_async_copy(w_ref, w, w_sem.at[0])
    copy.start()
    g.greet(riders.replicas)
    riders.start()
    if layer == 1:
        cot = Gather(g, cot_out, rows, cot_sems)
        own = pltpu.make_async_copy(cot_ref, cot_out.at[g.me], cot_sem.at[0])
        own.start()
        cot.start(0, cot_ref)
    scatter = Scatter(g, rc, scratch)
    whole = flat(qkv_ref[...])
    for h in range(heads):
        o = 3 * e * h
        ka[h, :, :e] = whole[:, o + e : o + 2 * e]
        ka[h, :, e:] = flat(km_ref[...])
        vt[h, :e, :] = whole[:, o + 2 * e : o + 3 * e].T
        vt[h, e:, :] = jnp.ones((16, length), BF)
    copy.wait()

    def work(j):
        at = span(j, rc)
        qm = flat(qm_ref[:, at, :])
        found = []
        held_qkv = flat(qkv_ref[:, at, :])
        for h in range(heads):
            o = 3 * e * h
            q = jnp.concatenate([held_qkv[:, o : o + e], qm], axis=1)
            held = []
            top = None
            for k in range(length // kc):
                s = dg(ka[h, k * kc : (k + 1) * kc, :], q, NT)
                t = jnp.max(s, axis=0, keepdims=True)
                top = t if top is None else jnp.maximum(top, t)
                held.append(s)
            top = top * c
            acc = None
            for k in range(length // kc):
                p = jnp.exp2(held[k] * c - top).astype(BF)
                a = dg(vt[h, :, k * kc : (k + 1) * kc], p, NN)
                acc = a if acc is None else acc + a
            total = acc[e : e + 1]
            found.append((acc[:e] * (1.0 / total)).astype(BF))
            lse_ref[j, h : h + 1, :] = top + jnp.log2(total)
            if h == heads // 2:

                @pl.when(j > 0)
                def _():
                    scatter.second(j - 1)

        ctx = (jnp.concatenate(found, axis=0) if heads > 1 else found[0]).T
        ctx_ref[:, at, :] = ctx.reshape(size, rc, heads * e)
        width = x_ref.shape[1]
        scatter.part[:, at, :] = dg(ctx, w[...], NN).reshape(size, rc, width)
        scatter.first(j)
        riders.step(j, n)
        if layer == 1:

            @pl.when(j == n - 1)
            def _():
                cot.relay(0)

    run(n, work)
    scatter.second(n - 1)

    def last(j):
        at = span(j, rc)
        h1_ref[at, :] = x_ref[at, :].astype(F32) + scatter.third(j)

    run(n, last)
    scatter.drain(n)
    if layer == 1:
        cot.ready(0)
        cot.drain(1)
        own.wait()
    riders.finish()


def attend(size, replicas, layer, qkv, qm, km, x, w, riders, cot=()):
    _, rows, wide = qkv.shape
    e = qm.shape[2]
    heads = wide // (3 * e)
    width = x.shape[1]
    n = chunks(rows)
    halves, columns, outs, sems = riding(riders, replicas)
    return pl.pallas_call(
        functools.partial(attend_kernel, size, layer, columns),
        out_shape=[
            shape((rows, width), F32),
            shape((size, rows, heads * e), BF),
            shape((n, heads, size * rows // n), F32),
        ]
        + [shape((size, rows, width), BF) for _ in cot]
        + outs,
        in_specs=[VM, VM, VM, VM, HB] + [VM] * len(cot) + [HB] * len(riders),
        out_specs=[VM, VM, VM] + [HB] * (len(cot) + len(outs)),
        scratch_shapes=[
            pltpu.VMEM((heads, size * rows, 2 * e), BF),
            pltpu.VMEM((heads, e + 16, size * rows), BF),
            pltpu.VMEM((heads * e, width), BF),
            DMA((1,)),
        ]
        + scatter_scratch(size, rows, width, n)
        + (comm_sems(size, 1) + [DMA((1,))]) * len(cot)
        + sems,
        compiler_params=params(2 + layer),
        cost_estimate=cost(60e9, 20e6),
    )(qkv, qm, km, x, w, *cot, *halves)


def mlp_kernel(size, layer, columns, *refs):
    m = len(columns)
    h1_ref, gain_ref, wu_ref, wd_ref = refs[:4]
    halves, refs = refs[4 : 4 + m], refs[4 + m :]
    y_ref, a2_out, hid_out, slope_out = refs[:4]
    wholes, refs = refs[4 : 4 + m], refs[4 + m :]
    a2, hid, slope, wu, wd, w_sem, out_sem = refs[:7]
    scratch, refs = refs[7:20], refs[20:]
    riders = Riders(halves, wholes, columns, refs)
    rows, width = h1_ref.shape
    hidden = wu_ref.shape[1]
    fb = min(256, hidden)
    n = chunks(rows)
    rc = rows // n
    g = Group(size)
    copies = [
        pltpu.make_async_copy(wu_ref, wu, w_sem.at[0]),
        pltpu.make_async_copy(wd_ref, wd, w_sem.at[1]),
    ]
    for copy in copies:
        copy.start()
    g.greet(riders.replicas)
    gather = Gather(g, a2, rc, scratch[:4])
    scatter = Scatter(g, rc, scratch[4:])

    def send(j):
        at = span(j, rc)
        a = normed(h1_ref[at, :])[0] * gain_ref[layer, 1:2, :]
        a2[g.me, at, :] = a.astype(BF)
        gather.start(j)

    run(n, send)
    riders.start()
    for copy in copies:
        copy.wait()

    gather.relay(0)

    def work(j):
        at = span(j, rc)
        gather.ready(j)
        a = flat(a2[:, at, :])
        for f in range(hidden // fb):
            cols = slice(f * fb, (f + 1) * fb)
            u = dg(a, wu[:, cols], NN)
            half = 0.5 + 0.5 * lax.erf(u * (0.5**0.5))
            slope[:, at, cols] = (
                (half + u * jnp.exp(-0.5 * u * u) * ((2 * math.pi) ** -0.5))
                .astype(BF)
                .reshape(size, rc, fb)
            )
            hid[:, at, cols] = (u * half).astype(BF).reshape(size, rc, fb)

        @pl.when(j + 1 < n)
        def _():
            gather.relay(j + 1)

        @pl.when(j > 0)
        def _():
            scatter.second(j - 1)

        held = flat(hid[:, at, :])
        for f in range(width // 256):
            cols = slice(f * 256, (f + 1) * 256)
            scatter.part[:, at, cols] = dg(held, wd[:, cols], NN).reshape(size, rc, 256)
        scatter.first(j)
        riders.step(j, n)

    run(n, work)
    scatter.second(n - 1)
    outs = [
        pltpu.make_async_copy(a2, a2_out, out_sem.at[0]),
        pltpu.make_async_copy(hid, hid_out, out_sem.at[1]),
        pltpu.make_async_copy(slope, slope_out, out_sem.at[2]),
    ]
    for out in outs:
        out.start()

    def last(j):
        at = span(j, rc)
        y_ref[at, :] = (h1_ref[at, :] + scatter.third(j)).astype(BF)

    run(n, last)
    riders.finish()
    gather.drain(n)
    scatter.drain(n)
    for out in outs:
        out.wait()


def mlp_forward(size, replicas, layer, h1, gains, wu, wd, riders):
    rows, width = h1.shape
    hidden = wu.shape[1]
    n = chunks(rows)
    halves, columns, outs, sems = riding(riders, replicas)
    return pl.pallas_call(
        functools.partial(mlp_kernel, size, layer, columns),
        out_shape=[
            shape((rows, width), BF),
            shape((size, rows, width), BF),
            shape((size, rows, hidden), BF),
            shape((size, rows, hidden), BF),
        ]
        + outs,
        in_specs=[VM, VM, HB, HB] + [HB] * len(riders),
        out_specs=[VM, HB, HB, HB] + [HB] * len(outs),
        scratch_shapes=[
            pltpu.VMEM((size, rows, width), BF),
            pltpu.VMEM((size, rows, hidden), BF),
            pltpu.VMEM((size, rows, hidden), BF),
            pltpu.VMEM((width, hidden), BF),
            pltpu.VMEM((hidden, width), BF),
            DMA((2,)),
            DMA((3,)),
        ]
        + comm_sems(size, n)
        + scatter_scratch(size, rows, width, n)
        + sems,
        compiler_params=params(4 + layer),
        cost_estimate=cost(50e9, 30e6),
    )(h1, gains, wu, wd, *halves)


def turn_kernel(size, columns, *refs):
    m = len(columns)
    h1_ref, gain_ref, wu_ref, wd_ref, q_stage = refs[:5]
    halves, refs = refs[5 : 5 + m], refs[5 + m :]
    y_ref, qkv_ref, a2_out, hid_out, slope_out, a1_out, wq_out = refs[:7]
    wholes, refs = refs[7 : 7 + m], refs[7 + m :]
    a2, hid, slope, wu, wd, a1, wq, w_sem, out_sem = refs[:9]
    gather_sems, next_sems, refs = refs[9:13], refs[13:17], refs[17:]
    scratch, refs = refs[:9], refs[9:]
    spread = Spread(q_stage.at[1], wq, False, refs[:5])
    riders = Riders(halves, wholes, columns, refs[5:])
    out_rider, up_rider = riders.all
    stages = len(spread.stages)
    rows, width = h1_ref.shape
    hidden = wu_ref.shape[1]
    fb = min(256, hidden)
    n = chunks(rows)
    rc = rows // n
    g = Group(size)
    copies = [
        pltpu.make_async_copy(wu_ref, wu, w_sem.at[0]),
        pltpu.make_async_copy(wd_ref, wd, w_sem.at[1]),
    ]
    for copy in copies:
        copy.start()
    g.greet(spread.replicas)
    gather = Gather(g, a2, rc, gather_sems)
    onward = Gather(g, a1, rc, next_sems)
    scatter = Scatter(g, rc, scratch)

    def send(j):
        at = span(j, rc)
        a = normed(h1_ref[at, :])[0] * gain_ref[0, 1:2, :]
        a2[g.me, at, :] = a.astype(BF)
        gather.start(j)

    run(n, send)
    spread.start()
    out_rider.start()
    for copy in copies:
        copy.wait()

    def pass_on(j):
        at = span(j, rc)
        y = (h1_ref[at, :] + scatter.third(j)).astype(BF)
        y_ref[at, :] = y
        a = normed(y.astype(F32))[0] * gain_ref[1, 0:1, :]
        a1[g.me, at, :] = a.astype(BF)
        onward.start(j)

    lag = min(2, n)
    gather.relay(0)

    def work(j):
        at = span(j, rc)
        gather.ready(j)
        a = flat(a2[:, at, :])
        for f in range(hidden // fb):
            cols = slice(f * fb, (f + 1) * fb)
            u = dg(a, wu[:, cols], NN)
            half = 0.5 + 0.5 * lax.erf(u * (0.5**0.5))
            slope[:, at, cols] = (
                (half + u * jnp.exp(-0.5 * u * u) * ((2 * math.pi) ** -0.5))
                .astype(BF)
                .reshape(size, rc, fb)
            )
            hid[:, at, cols] = (u * half).astype(BF).reshape(size, rc, fb)

        @pl.when(j + 1 < n)
        def _():
            gather.relay(j + 1)

        @pl.when(j > 0)
        def _():
            scatter.second(j - 1)

        held = flat(hid[:, at, :])
        for f in range(width // 256):
            cols = slice(f * 256, (f + 1) * 256)
            scatter.part[:, at, cols] = dg(held, wd[:, cols], NN).reshape(size, rc, 256)
        scatter.first(j)

        @pl.when(j >= lag)
        def _():
            pass_on(j - lag)

        @pl.when(j == n // 2)
        def _():
            spread.step(0)
            out_rider.step(0)
            up_rider.start()

        @pl.when(j == n - 1)
        def _():
            for i in range(1, stages):
                spread.step(i)
                out_rider.step(i)

    run(n, work)
    scatter.second(n - 1)
    outs = [
        pltpu.make_async_copy(a2, a2_out, out_sem.at[0]),
        pltpu.make_async_copy(hid, hid_out, out_sem.at[1]),
        pltpu.make_async_copy(slope, slope_out, out_sem.at[2]),
    ]
    for out in outs:
        out.start()
    for j in range(n - lag, n):
        pass_on(j)
    up_rider.step(0)
    spread.finish()
    outs.append(pltpu.make_async_copy(wq, wq_out, out_sem.at[3]))
    outs[3].start()

    onward.relay(0)

    def multiply(j):
        at = span(j, rc)

        @pl.when(j + 1 < n)
        def _():
            onward.relay(j + 1)

        onward.ready(j)
        r = dg(flat(a1[:, at, :]), wq[...], NN).astype(BF)
        qkv_ref[:, at, :] = r.reshape(size, rc, r.shape[1])

    run(n, multiply)
    outs.append(pltpu.make_async_copy(a1, a1_out, out_sem.at[4]))
    outs[4].start()
    for i in range(1, stages):
        up_rider.step(i)
    riders.finish()
    gather.drain(n)
    onward.drain(n)
    scatter.drain(n)
    for out in outs:
        out.wait()


def turn_forward(size, replicas, h1, gains, wu, wd, stage, riders):
    rows, width = h1.shape
    hidden = wu.shape[1]
    wide = stage.shape[2]
    n = chunks(rows)
    halves, columns, outs, sems = riding(riders, replicas)
    return pl.pallas_call(
        functools.partial(turn_kernel, size, columns),
        out_shape=[
            shape((rows, width), BF),
            shape((size, rows, wide), BF),
            shape((size, rows, width), BF),
            shape((size, rows, hidden), BF),
            shape((size, rows, hidden), BF),
            shape((size, rows, width), BF),
            shape((width, wide), BF),
        ]
        + outs,
        in_specs=[VM, VM] + [HB] * (3 + len(riders)),
        out_specs=[VM, VM] + [HB] * (5 + len(outs)),
        scratch_shapes=[
            pltpu.VMEM((size, rows, width), BF),
            pltpu.VMEM((size, rows, hidden), BF),
            pltpu.VMEM((size, rows, hidden), BF),
            pltpu.VMEM((width, hidden), BF),
            pltpu.VMEM((hidden, width), BF),
            pltpu.VMEM((size, rows, width), BF),
            pltpu.VMEM((width, wide), BF),
            DMA((2,)),
            DMA((5,)),
        ]
        + comm_sems(size, n) * 2
        + scatter_scratch(size, rows, width, n)
        + rider_sems(replicas)
        + sems,
        compiler_params=params(4),
        cost_estimate=cost(50e9, 30e6),
    )(h1, gains, wu, wd, stage, *halves)


def mlp_back_kernel(size, layer, parts, *refs):
    g_ref, h1_ref, gain_ref, a2_ref, hid_ref, slope_ref, wu_ref, wd_ref = refs[:8]
    refs = refs[8:]
    if layer == 1:
        ys, whole_ref, refs = refs[:2], refs[2], refs[3:]
    mid_ref, gain_out, gup_ref, gdown_ref = refs[:4]
    refs = refs[4:]
    if layer == 1:
        y_out, refs = refs[0], refs[1:]
    grad, a2, hid, dup, wu, wd, w_sem = refs[:7]
    scratch, refs = refs[7:20], refs[20:]
    rows, width = h1_ref.shape
    hidden = wu_ref.shape[1]
    depth = width // parts
    fb = min(256, hidden)
    n = chunks(rows)
    rc = rows // n
    g = Group(size)
    copies = [
        pltpu.make_async_copy(wd_ref, wd, w_sem.at[0]),
        pltpu.make_async_copy(slope_ref, dup, w_sem.at[1]),
        pltpu.make_async_copy(wu_ref, wu, w_sem.at[2]),
    ]
    late = [
        pltpu.make_async_copy(hid_ref, hid, w_sem.at[3]),
        pltpu.make_async_copy(a2_ref, a2, w_sem.at[4]),
    ]
    for copy in copies:
        copy.start()
    g.greet(side=layer == 1)
    section = lax.axis_index("section")
    if layer == 1:
        y_sem, y_own = refs

        def y_load(own):
            return pltpu.make_async_copy(own, y_own, y_sem.at[3])

        def y_copies(own, other, at):
            return (
                pltpu.make_async_copy(y_own, y_out.at[section], y_sem.at[0]),
                far_copy(
                    other, y_out.at[at], y_sem.at[1], y_sem.at[2], {"section": 1 - section}
                ),
            )

        for i in range(2):

            @pl.when(section == i)
            def _(i=i):
                y_load(ys[i]).start()
                y_copies(ys[i], ys[1 - i], section)[1].start()

    gather = Gather(g, grad, rc, scratch[:4])
    scatter = Scatter(g, rc, scratch[4:])

    def send(j):
        at = span(j, rc)
        grad[g.me, at, :] = g_ref[at, :]
        gather.start(j)

    if layer == 1:
        whole = pltpu.make_async_copy(whole_ref, grad, w_sem.at[5])
        whole.start()
        copies.append(whole)
    else:
        run(n, send)
    for copy in copies:
        copy.wait()
    for copy in late:
        copy.start()
    if layer == 1:
        y_load(ys[0]).wait()
        y_copies(ys[0], ys[1], section)[0].start()

    if layer == 0:
        gather.relay(0)

    def work(j):
        at = span(j, rc)
        if layer == 0:
            gather.ready(j)
        held = flat(grad[:, at, :])
        for f in range(hidden // fb):
            cols = slice(f * fb, (f + 1) * fb)
            d = dg(held, wd[cols, :], NT) * flat(dup[:, at, cols]).astype(F32)
            dup[:, at, cols] = d.astype(BF).reshape(size, rc, fb)

        if layer == 0:

            @pl.when(j + 1 < n)
            def _():
                gather.relay(j + 1)

        @pl.when(j > 0)
        def _():
            scatter.second(j - 1)

        held = flat(dup[:, at, :])
        for z in range(parts):
            cols = slice(z * depth, (z + 1) * depth)
            scatter.part[:, at, cols] = dg(held, wu[cols, :], NT).reshape(size, rc, depth)
        scatter.first(j)

    run(n, work)
    scatter.second(n - 1)
    for copy in late:
        copy.wait()

    def up_grad(z):
        cols = pl.ds(pl.multiple_of(z * depth, depth), depth)
        gup_ref[z] = dg(flat(a2[:, :, cols]), flat(dup[...]), TN).astype(BF)

    run(parts, up_grad)

    def down_grad(f):
        cols = pl.ds(pl.multiple_of(f * fb, fb), fb)
        r = dg(flat(hid[:, :, cols]), flat(grad[...]), TN).astype(BF)
        for z in range(parts):
            gdown_ref[z, cols, :] = r[:, z * depth : (z + 1) * depth]

    run(hidden // fb, down_grad)
    gain_out[...] = jnp.zeros_like(gain_out)

    def last(j):
        at = span(j, rc)
        dh, dgain = normed_back(h1_ref[at, :], gain_ref[layer, 1:2, :], scatter.third(j))
        mid_ref[at, :] = g_ref[at, :].astype(F32) + dh
        gain_out[...] += dgain

    run(n, last)
    if layer == 1:
        local, side = y_copies(ys[0], ys[1], 1 - section)
        local.wait()
        side.wait_recv()
        y_copies(ys[0], ys[1], section)[1].wait_send()
    if layer == 0:
        gather.drain(n)
    scatter.drain(n)


def mlp_backward(size, replicas, layer, grad, h1, gains, a2, hid, slope, wu, wd, extra):
    rows, width = h1.shape
    hidden = wu.shape[1]
    parts, depth = replicas, width // replicas
    n = chunks(rows)
    return pl.pallas_call(
        functools.partial(mlp_back_kernel, size, layer, parts),
        out_shape=[
            shape((rows, width), F32),
            shape((1, width), F32),
            shape((parts, depth, hidden), BF),
            shape((parts, hidden, depth), BF),
        ]
        + [shape((2, rows, width), BF)] * (len(extra) // 3),
        in_specs=[VM, VM, VM] + [HB] * (5 + len(extra)),
        out_specs=[VM, VM, VM, VM] + [HB] * (len(extra) // 3),
        scratch_shapes=[
            pltpu.VMEM((size, rows, width), BF),
            pltpu.VMEM((size, rows, width), BF),
            pltpu.VMEM((size, rows, hidden), BF),
            pltpu.VMEM((size, rows, hidden), BF),
            pltpu.VMEM((width, hidden), BF),
            pltpu.VMEM((hidden, width), BF),
            DMA((6,)),
        ]
        + comm_sems(size, n)
        + scatter_scratch(size, rows, width, n)
        + [DMA((4,)), pltpu.VMEM((rows, width), BF)] * (len(extra) // 3),
        compiler_params=params(6 + layer),
        cost_estimate=cost(60e9, 40e6),
    )(grad, h1, gains, a2, hid, slope, wu, wd, *extra)


def attend_back_kernel(size, layer, parts, *refs):
    mid_ref, qkv_ref, qm_ref, km_ref, ctx_ref, lse_ref, w_ref = refs[:7]
    refs = refs[7:]
    if layer == 0:
        gdown_ref, refs = refs[0], refs[1:]
    dqkv_ref, gout_ref, refs = refs[0], refs[1], refs[2:]
    if layer == 0:
        down_out, refs = refs[0], refs[1:]
    da, ka, va, kt, dk, dv, w, w_sem = refs[:8]
    sems, refs = refs[8:12], refs[12:]
    reduce = Reduce(layer, refs[:9])
    if layer == 0:
        down = HalfReduce(layer, refs[9 : 9 + HALF])
        down_swap = HalfSwap(gdown_ref, down.other, refs[9 + HALF])
    _, rows, wide = qkv_ref.shape
    length = size * rows
    e = qm_ref.shape[2]
    heads = wide // (3 * e)
    scale = e**-0.5
    c = scale * math.log2(math.e)
    depth = w_ref.shape[1] // parts
    n = chunks(rows)
    rc = rows // n
    bq = size * rc
    kc = bq
    g = Group(size)
    copies = [pltpu.make_async_copy(w_ref, w, w_sem.at[0])]
    for copy in copies:
        copy.start()
    g.greet(parts)
    gather = Gather(g, da, rc, sems)
    loads = []
    if layer == 0:
        down_swap.copy().start()
        loads = down.loads(gdown_ref, None)
        for load in loads:
            load.start()

    def send(j):
        at = span(j, rc)
        da[g.me, at, :] = mid_ref[at, :].astype(BF)
        gather.start(j)

    run(n, send)
    lane = lax.broadcasted_iota(jnp.int32, (length, e), 1)
    whole = flat(qkv_ref[...])
    for h in range(heads):
        o = 3 * e * h
        ka[h, :, :e] = whole[:, o + e : o + 2 * e]
        ka[h, :, e:] = flat(km_ref[...])
        va[h, :, :e] = whole[:, o + 2 * e : o + 3 * e]
        va[h, :, e:] = jnp.where(lane < 3, 1.0, 0.0).astype(BF)
        kt[h] = whole[:, o + e : o + 2 * e].T
    dk[...] = jnp.zeros_like(dk)
    dv[...] = jnp.zeros_like(dv)
    ql = lax.broadcasted_iota(jnp.int32, (bq, e), 1)
    for copy in copies + loads:
        copy.wait()

    def out_grad(z):
        cols = pl.ds(pl.multiple_of(z * depth, depth), depth)
        return dg(flat(ctx_ref[...]), flat(da[:, :, cols]), TN)

    def work(j):
        at = span(j, rc)

        @pl.when(j == 0)
        def _():
            gather.relay(0)
            gather.ready(0)

        @pl.when(j == min(1, n - 1))
        def _():
            for i in range(1, n):
                gather.relay(i)
            for i in range(1, n):
                gather.ready(i)
            reduce.send(out_grad)

        qm = flat(qm_ref[:, at, :])
        dctx = dg(flat(da[:, at, :]), w[...], NT).astype(BF)
        ctx = flat(ctx_ref[:, at, :])
        held_qkv = flat(qkv_ref[:, at, :])
        for h in range(heads):
            o = 3 * e * h
            qq = held_qkv[:, o : o + e]
            q = jnp.concatenate([qq, qm], axis=1)
            dc = dctx[:, h * e : (h + 1) * e]
            prod = dc.astype(F32) * ctx[:, h * e : (h + 1) * e].astype(F32)
            d = -jnp.sum(prod, axis=1, keepdims=True)
            d1 = d.astype(BF).astype(F32)
            d2 = (d - d1).astype(BF).astype(F32)
            d3 = d - d1 - d2
            ds_col = jnp.where(ql == 0, d1, jnp.where(ql == 1, d2, jnp.where(ql == 2, d3, 0.0)))
            dca = jnp.concatenate([dc, ds_col.astype(BF)], axis=1)
            lse = lse_ref[j, h : h + 1, :]
            dqt = None
            for k in range(length // kc):
                ks = slice(k * kc, (k + 1) * kc)
                s = dg(ka[h, ks, :], q, NT)
                p = jnp.exp2(s * c - lse)
                ds = (p * dg(va[h, ks, :], dca, NT)).astype(BF)
                dv[h, ks, :] += dg(p.astype(BF), dc, NN)
                dk[h, ks, :] += dg(ds, qq, NN)
                a = dg(kt[h, :, ks], ds, NN)
                dqt = a if dqt is None else dqt + a
            if layer == 0 and h == heads // 2:

                @pl.when(j == min(1, n - 1))
                def _():
                    down_swap.copy().wait_recv()
                    down.middle()

            if layer == 0 and h == heads - 1:

                @pl.when(j == n - 1)
                def _():
                    down.late()

            dqkv_ref[:, at, o : o + e] = (dqt * scale).T.astype(BF).reshape(size, rc, e)

    run(n, work)
    for h in range(heads):
        o = 3 * e * h
        dqkv_ref[:, :, o + e : o + 2 * e] = (dk[h] * scale).astype(BF).reshape(size, rows, e)
        dqkv_ref[:, :, o + 2 * e : o + 3 * e] = dv[h].astype(BF).reshape(size, rows, e)

    reduce.collect()
    reduce.finish(gout_ref)
    if layer == 0:
        down.finish(down_out)
        down_swap.copy().wait_send()
    gather.drain(n)


def attend_backward(size, replicas, layer, mid, qkv, qm, km, ctx, lse, w, grads):
    _, rows, wide = qkv.shape
    e = qm.shape[2]
    heads = wide // (3 * e)
    width = mid.shape[1]
    parts, depth = replicas, width // replicas
    length = size * rows
    n = chunks(rows)
    return pl.pallas_call(
        functools.partial(attend_back_kernel, size, layer, parts),
        out_shape=[shape(qkv.shape, BF), shape((heads * e, depth), F32)]
        + [shape(grad.shape[1:], F32) for grad in grads],
        in_specs=[VM] * 6 + [HB] * (1 + len(grads)),
        out_specs=[VM, VM] + [VM] * len(grads),
        scratch_shapes=[
            pltpu.VMEM((size, rows, width), BF),
            pltpu.VMEM((heads, length, 2 * e), BF),
            pltpu.VMEM((heads, length, 2 * e), BF),
            pltpu.VMEM((heads, e, length), BF),
            pltpu.VMEM((heads, length, e), F32),
            pltpu.VMEM((heads, length, e), F32),
            pltpu.VMEM((heads * e, width), BF),
            DMA((1,)),
        ]
        + comm_sems(size, n)
        + reduce_scratch(parts, heads * e, depth)
        + sum([half_scratch(parts, *grad.shape[1:]) + [DMA((2,))] for grad in grads], []),
        compiler_params=params(8 + layer),
        cost_estimate=cost(90e9, 40e6),
    )(mid, qkv, qm, km, ctx, lse, w, *grads)


def qkv_back_kernel(
    size, layer, parts, dqkv_ref, gain_ref, a1_in, x_in, mid_in, w_ref,
    dx_ref, gain_out, gqkv_ref, a1_ref, x_ref, mid_ref, w, w_sem, *scratch
):
    rows, width = x_ref.shape
    late = [
        pltpu.make_async_copy(a1_in, a1_ref, w_sem.at[1]),
        pltpu.make_async_copy(x_in, x_ref, w_sem.at[2]),
        pltpu.make_async_copy(mid_in, mid_ref, w_sem.at[3]),
    ]
    depth = width // parts
    n = thin_chunks(rows)
    rc = rows // n
    g = Group(size)
    copies = [pltpu.make_async_copy(w_ref, w, w_sem.at[0])]
    for copy in copies + late:
        copy.start()
    g.greet()
    scatter = Scatter(g, rc, scratch)
    for copy in copies:
        copy.wait()

    lag = min(2, n)

    def work(j):
        at = span(j, rc)
        held = flat(dqkv_ref[:, at, :])
        for z in range(parts):
            cols = slice(z * depth, (z + 1) * depth)
            scatter.part[:, at, cols] = dg(held, w[cols, :], NT).reshape(size, rc, depth)
        scatter.first(j)

        @pl.when(j >= lag)
        def _():
            scatter.second(j - lag)


    run(n, work)
    for j in range(n - lag, n):
        scatter.second(j)
    for copy in late:
        copy.wait()

    def qkv_grad(z):
        cols = pl.ds(pl.multiple_of(z * depth, depth), depth)
        gqkv_ref[z] = dg(flat(a1_ref[:, :, cols]), flat(dqkv_ref[...]), TN).astype(BF)

    run(parts, qkv_grad)
    gain_out[...] = jnp.zeros_like(gain_out)

    def last(j):
        at = span(j, rc)
        dh, dgain = normed_back(
            x_ref[at, :].astype(F32), gain_ref[layer, 0:1, :], scatter.third(j)
        )
        dx_ref[at, :] = (mid_ref[at, :] + dh).astype(BF)
        gain_out[...] += dgain

    run(n, last)
    scatter.drain(n)


def qkv_backward(size, replicas, layer, dqkv, a1, x, mid, gains, w):
    rows, width = x.shape
    wide = w.shape[1]
    parts, depth = replicas, width // replicas
    n = thin_chunks(rows)
    return pl.pallas_call(
        functools.partial(qkv_back_kernel, size, layer, parts),
        out_shape=(
            shape((rows, width), BF),
            shape((1, width), F32),
            shape((parts, depth, wide), BF),
        ),
        in_specs=[VM, VM] + [HB] * 4,
        out_specs=(VM, VM, VM),
        scratch_shapes=[
            pltpu.VMEM((size, rows, width), BF),
            pltpu.VMEM((rows, width), BF),
            pltpu.VMEM((rows, width), F32),
            pltpu.VMEM((width, wide), BF),
            DMA((4,)),
        ]
        + scatter_scratch(size, rows, width, n),
        compiler_params=params(11),
        cost_estimate=cost(30e9, 30e6),
    )(dqkv, gains, a1, x, mid, w)


def last_kernel(
    size, parts, dqkv_ref, a1_ref, x_ref, mid_ref, gain_ref, w_ref, two_ref, above_ref, dx1_ref,
    gain_out, gqkv_out, dx_out,
    gqkv, swap_sem, w, dx, gsum, gcame, w_sem, x_sem, x_send, x_recv, g_send, g_recv, *scratch
):
    rows, width = x_ref.shape
    depth = width // parts
    n = thin_chunks(rows)
    rc = rows // n
    g = Group(size)
    section = lax.axis_index("section")
    d = lax.axis_index("dp")
    copy = pltpu.make_async_copy(w_ref, w, w_sem.at[0])
    copy.start()
    reduce = HalfReduce(0, scratch[:HALF])
    swap = HalfSwap(gqkv, reduce.other, swap_sem)
    scatter = Scatter(g, rc, scratch[HALF:])
    g.greet(parts)

    def upper():
        return far_copy(
            dx1_ref, dx_out.at[0], x_send.at[n], x_recv.at[n], {"section": 1 - section}
        )

    def keep_upper():
        return pltpu.make_async_copy(dx1_ref, dx_out.at[1], x_sem.at[0])

    def lower(j):
        at = span(j, rc)
        return far_copy(
            dx.at[at], dx_out.at[1, at], x_send.at[j], x_recv.at[j], {"section": 1 - section}
        )

    def keep_lower(j):
        at = span(j, rc)
        return pltpu.make_async_copy(dx.at[at], dx_out.at[0, at], x_sem.at[j])

    def qkv_grad(z):
        cols = pl.ds(pl.multiple_of(z * depth, depth), depth)
        gqkv[z] = dg(flat(a1_ref[:, :, cols]), flat(dqkv_ref[...]), TN).astype(BF)

    run(parts, qkv_grad)
    swap.copy().start()
    load = reduce.loads(gqkv, None)[0]
    load.start()

    @pl.when(section == 1)
    def _():
        keep_upper().start()

    copy.wait()

    lag = min(2, n)

    def work(j):
        at = span(j, rc)
        held = flat(dqkv_ref[:, at, :])
        for z in range(parts):
            cols = slice(z * depth, (z + 1) * depth)
            scatter.part[:, at, cols] = dg(held, w[cols, :], NT).reshape(size, rc, depth)
        scatter.first(j)

        @pl.when(j >= lag)
        def _():
            scatter.second(j - lag)


    run(n, work)
    for j in range(n - lag, n):
        scatter.second(j)
    gsum[0] = jnp.zeros_like(gsum[0])

    def last(j):
        at = span(j, rc)
        dh, dgain = normed_back(x_ref[at, :].astype(F32), gain_ref[0, 0:1, :], scatter.third(j))
        dx[at, :] = (mid_ref[at, :] + dh).astype(BF)

        @pl.when(section == 0)
        def _():
            keep_lower(j).start()

        @pl.when(section == 1)
        def _():
            lower(j).start()

        gsum[0, 0:1, :] += dgain

    def rest(j):
        @pl.when(j == n // 2)
        def _():
            load.wait()
            swap.copy().wait_recv()
            reduce.middle()

            @pl.when(section == 0)
            def _():
                upper().start()

        last(j)

    run(n, rest)
    gsum[0, 1:2, :] = two_ref[...]
    gsum[0, 2:4, :] = above_ref[...]

    targets = [
        [{"tensor": g.sibling}],
        [{"tensor": g.ahead(k) * 2 + g.core} for k in range(1, g.chips)],
        [{"dp": lax.rem(d + k, parts)} for k in range(1, parts)],
        [{"section": 1 - section}],
    ]
    slot = 0
    sent = []

    def exchange(stage):
        nonlocal slot
        copies = []
        for target in targets[stage]:
            copies.append(
                far_copy(gsum.at[stage], gcame.at[slot], g_send.at[slot], g_recv.at[slot], target)
            )
            copies[-1].start()
            slot += 1
        total = gsum[stage]
        for i, copy in enumerate(copies):
            copy.wait_recv()
            total = total + gcame[slot - len(copies) + i]
        gsum[stage + 1] = total
        sent.extend(copies)

    exchange(0)
    exchange(1)
    reduce.late()
    exchange(2)
    exchange(3)
    gain_out[...] = gsum[4]

    @pl.when(section == 0)
    def _():
        for j in range(n):
            lower(j).wait_recv()
            keep_lower(j).wait()
        upper().wait_send()

    @pl.when(section == 1)
    def _():
        keep_upper().wait()
        upper().wait_recv()
        for j in range(n):
            lower(j).wait_send()

    reduce.finish(gqkv_out)
    swap.copy().wait_send()
    for copy in sent:
        copy.wait_send()
    scatter.drain(n)


def last_backward(size, replicas, dqkv, a1, x, mid, gains, w, two, above, dx1):
    rows, width = x.shape
    wide = w.shape[1]
    depth = width // replicas
    n = thin_chunks(rows)
    slots = 1 + (size // 2 - 1) + (replicas - 1) + 1
    return pl.pallas_call(
        functools.partial(last_kernel, size, replicas),
        out_shape=(
            shape((8, width), F32),
            shape((depth, wide), F32),
            shape((2, rows, width), BF),
        ),
        in_specs=[VM] * 5 + [HB, VM, VM, VM],
        out_specs=(VM, VM, HB),
        scratch_shapes=[
            pltpu.VMEM((replicas, depth, wide), BF),
            DMA((2,)),
            pltpu.VMEM((width, wide), BF),
            pltpu.VMEM((rows, width), BF),
            pltpu.VMEM((5, 8, width), F32),
            pltpu.VMEM((slots, 8, width), F32),
            DMA((1,)),
            DMA((n,)),
            DMA((n + 1,)),
            DMA((n + 1,)),
            DMA((slots,)),
            DMA((slots,)),
        ]
        + half_scratch(replicas, depth, wide)
        + scatter_scratch(size, rows, width, n),
        compiler_params=params(10),
        cost_estimate=cost(40e9, 30e6),
    )(dqkv, a1, x, mid, gains, w, two, above, dx1)


def scene_masks(segments, e):
    same = (segments[..., None] == jnp.arange(e, dtype=jnp.int32)).astype(F32)
    used = jnp.arange(e) < SCENES
    return (
        jnp.where(used, same * MASKED, 0.0).astype(BF),
        jnp.where(used, 1.0 - same, 0.0).astype(BF),
    )


def swap_section(value):
    return lax.ppermute(value, "section", [(0, 1), (1, 0)])


def shards(
    block_input,
    segment_ids,
    cotangent,
    norm_one_gain,
    qkv_weight,
    out_weight,
    norm_two_gain,
    up_weight,
    down_weight,
):
    section = lax.axis_index("section")
    size = lax.axis_size("tensor")
    replicas = lax.axis_size("dp")

    mine = [
        qkv_weight[0].reshape((qkv_weight.shape[1], -1)),
        out_weight[0].reshape((-1, out_weight.shape[3])),
        up_weight[0],
        down_weight[0],
    ]
    mine = [w.astype(BF).reshape((2, -1, w.shape[1])) for w in mine]
    gains = jnp.concatenate(
        [norm_one_gain, norm_two_gain, jnp.zeros((6, norm_one_gain.shape[1]), F32)], axis=0
    )
    segments = lax.dynamic_index_in_dim(segment_ids, section, 0, keepdims=False)
    x = lax.dynamic_index_in_dim(block_input, section, 0, keepdims=False)
    head_dim = qkv_weight.shape[3] // 3
    qm, km = scene_masks(segments.reshape((size, -1)), head_dim)
    qkv, gains, a1, w_qkv_0, w_out_0, h_qkv, h_out, h_up, h_down = first_forward(
        size, replicas, x, gains, mine
    )
    h1, ctx, lse, w_up_0, w_down_0 = attend(
        size, replicas, 0, qkv, qm, km, x, w_out_0,
        [(h_up, "spread", 0, False), (h_down, "spread", 0, True)],
    )
    below = (x, a1, qkv, ctx, lse, h1)
    y0, qkv, a2, hid, slope, a1, w_qkv_1, w_out_1, w_up_1 = turn_forward(
        size, replicas, h1, gains, w_up_0, w_down_0, h_qkv,
        [(h_out, "spread", 1, True), (h_up, "spread", 1, False)],
    )
    kept = [below + (a2, hid, slope)]
    grad = lax.dynamic_index_in_dim(cotangent, section, 0, keepdims=False)
    h1, ctx, lse, grad_all, w_down_1 = attend(
        size, replicas, 1, qkv, qm, km, y0, w_out_1, [(h_down, "spread", 1, True)], [grad]
    )
    y1, a2, hid, slope = mlp_forward(size, replicas, 1, h1, gains, w_up_1, w_down_1, [])
    kept.append((y0, a1, qkv, ctx, lse, h1, a2, hid, slope))
    weights = [
        (w_qkv_0, w_out_0, w_up_0, w_down_0),
        (w_qkv_1, w_out_1, w_up_1, w_down_1),
    ]
    def reduce_rows(value):
        return lax.psum_scatter(value, "dp", scatter_dimension=0, tiled=False)

    x, a1, qkv, ctx, lse, h1, a2, hid, slope = kept[1]
    w_qkv, w_out, w_up, w_down = weights[1]
    mid, gain_two, g_up, g_down, layer_out = mlp_backward(
        size, replicas, 1, grad, h1, gains, a2, hid, slope, w_up, w_down, [y0, y1, grad_all]
    )
    d_qkv, out_1 = attend_backward(size, replicas, 1, mid, qkv, qm, km, ctx, lse, w_out, [])
    up_1, down_1 = reduce_rows(g_up), reduce_rows(g_down)
    dx1, gain_one, g_qkv = qkv_backward(size, replicas, 1, d_qkv, a1, x, mid, gains, w_qkv)
    gains_above = jnp.concatenate([gain_one, gain_two], axis=0)
    dx1, up_1, down_1 = lax.optimization_barrier((dx1, up_1, down_1))
    qkv_1 = reduce_rows(g_qkv)

    x, a1, qkv, ctx, lse, h1, a2, hid, slope = kept[0]
    w_qkv, w_out, w_up, w_down = weights[0]
    mid, gain_two, g_up, g_down = mlp_backward(
        size, replicas, 0, dx1, h1, gains, a2, hid, slope, w_up, w_down, []
    )
    mid, qkv_1 = lax.optimization_barrier((mid, qkv_1))
    d_qkv, out_0, down_0 = attend_backward(
        size, replicas, 0, mid, qkv, qm, km, ctx, lse, w_out, [g_down]
    )
    up_0 = reduce_rows(g_up)
    d_qkv, up_0 = lax.optimization_barrier((d_qkv, up_0))
    gains, qkv_0, input_out = last_backward(
        size, replicas, d_qkv, a1, x, mid, gains, w_qkv, gain_two, gains_above, dx1
    )

    def finish(zero, one):
        send = swap_section(jnp.where(section == 0, one, zero))
        return jnp.where(section == 0, zero, one).astype(F32) + send.astype(F32)

    other_qkv_1 = swap_section(qkv_1)
    qkv_grad = jnp.where(section == 0, qkv_0, qkv_1.astype(F32) + other_qkv_1.astype(F32))
    out_grad = jnp.where(section == 0, out_0, out_1)
    up_grad = finish(up_0, up_1)
    other_down_1 = swap_section(down_1)
    down_grad = jnp.where(section == 0, down_0, down_1.astype(F32) + other_down_1.astype(F32))
    gains = lax.dynamic_slice_in_dim(gains, 2 * section, 2, 0)
    return (
        layer_out[None],
        input_out[None],
        gains[0:1],
        qkv_grad.reshape(qkv_weight.shape),
        out_grad.reshape(out_weight.shape),
        gains[1:2],
        up_grad[None],
        down_grad[None],
    )


def solution(mesh):
    return jax.shard_map(
        shards,
        mesh=mesh,
        in_specs=(
            P(None, ("dp", "tensor"), None),
            P(None, "dp"),
            P(None, ("dp", "tensor"), None),
            P("section", None),
            P("section", "dp", "tensor", None),
            P("section", "tensor", None, "dp"),
            P("section", None),
            P("section", "dp", "tensor"),
            P("section", "tensor", "dp"),
        ),
        out_specs=(
            P("section", None, ("dp", "tensor"), None),
            P("section", None, ("dp", "tensor"), None),
            P("section", None),
            P("section", "dp", "tensor", None),
            P("section", "tensor", None, "dp"),
            P("section", None),
            P("section", "dp", "tensor"),
            P("section", "tensor", "dp"),
        ),
        check_vma=False,
    )
```

```python
import functools
import math

import jax
import jax.numpy as jnp
from jax import lax
from jax.experimental import pallas as pl
from jax.experimental.pallas import tpu as pltpu
from jax.sharding import PartitionSpec as P

F32 = jnp.float32
BF = jnp.bfloat16
NT = (((1,), (1,)), ((), ()))
NN = (((1,), (0,)), ((), ()))
TN = (((0,), (0,)), ((), ()))
MASKED = -1e30
SCENES = 3
MESH = pl.DeviceIdType.MESH
VM = pl.BlockSpec(memory_space=pltpu.VMEM)
HB = pl.BlockSpec(memory_space=pl.ANY)
DMA = pltpu.SemaphoreType.DMA
LIMIT = 58 << 20


def dg(a, b, dims):
    return lax.dot_general(a, b, dims, preferred_element_type=F32)


def chunks(rows):
    return 4 if rows % 64 == 0 else 1


def thin_chunks(rows):
    return 8 if rows % 128 == 0 else chunks(rows)


def shape(dims, dtype):
    return jax.ShapeDtypeStruct(dims, dtype)


class Group:
    def __init__(self, size):
        self.size = size
        self.chips = size // 2
        self.me = lax.axis_index("tensor")
        self.chip = lax.div(self.me, 2)
        self.core = lax.rem(self.me, 2)
        self.sibling = self.chip * 2 + 1 - self.core

    def ahead(self, k):
        return lax.rem(self.chip + k, self.chips)

    def behind(self, k):
        return lax.rem(self.chip + self.chips - k, self.chips)

    def greet(self, replicas=0, side=False):
        barrier = pltpu.get_barrier_semaphore()
        targets = [self.sibling] + [self.ahead(k) * 2 + self.core for k in range(1, self.chips)]
        targets = [{"tensor": target} for target in targets]
        if replicas:
            d = lax.axis_index("dp")
            targets += [{"dp": lax.rem(d + k, replicas)} for k in range(1, replicas)]
        if replicas or side:
            targets += [{"section": 1 - lax.axis_index("section")}]
        for target in targets:
            pl.semaphore_signal(barrier, inc=1, device_id=target, device_id_type=MESH)
        pl.semaphore_wait(barrier, len(targets))


def remote(src, dst, send, recv, target):
    return pltpu.make_async_remote_copy(
        src_ref=src,
        dst_ref=dst,
        send_sem=send,
        recv_sem=recv,
        device_id={"tensor": target},
        device_id_type=MESH,
    )


def span(j, rc):
    return pl.ds(pl.multiple_of(j * rc, rc), rc)


def comm_sems(group_size, n):
    c = group_size // 2
    far, near = DMA((max(c - 1, 1), n)), DMA((c, n))
    return [far, far, near, near]


class Gather:
    def __init__(self, g, buf, rc, sems):
        self.g, self.buf, self.rc = g, buf, rc
        self.far_send, self.far_recv, self.near_send, self.near_recv = sems

    def far(self, k, j, origin, target, src=None):
        ref = self.buf.at[origin, span(j, self.rc)]
        src = ref if src is None else src
        return remote(src, ref, self.far_send.at[k - 1, j], self.far_recv.at[k - 1, j], target)

    def near(self, k, j, origin, src=None):
        ref = self.buf.at[origin, span(j, self.rc)]
        src = ref if src is None else src
        return remote(
            src, ref, self.near_send.at[k, j], self.near_recv.at[k, j], self.g.sibling
        )

    def start(self, j, src=None):
        g = self.g
        for k in range(1, g.chips):
            self.far(k, j, g.me, g.ahead(k) * 2 + g.core, src).start()
        self.near(0, j, g.me, src).start()

    def relay(self, j):
        g = self.g
        for k in range(1, g.chips):
            origin = g.behind(k) * 2 + g.core
            self.far(k, j, origin, g.me).wait_recv()
            self.near(k, j, origin).start()

    def ready(self, j):
        g = self.g
        self.near(0, j, g.sibling).wait_recv()
        for k in range(1, g.chips):
            self.near(k, j, g.behind(k) * 2 + 1 - g.core).wait_recv()

    def drain(self, n):
        g = self.g

        def one(j, _):
            for k in range(1, g.chips):
                self.far(k, j, g.me, g.sibling).wait_send()
            for k in range(g.chips):
                self.near(k, j, g.me).wait_send()
            return 0

        lax.fori_loop(0, n, one, 0)


def scatter_scratch(group_size, rows, width, n):
    c = group_size // 2
    far = pltpu.VMEM((max(c - 1, 1), rows, width), BF)
    near = pltpu.VMEM((c, rows, width), BF)
    return [pltpu.VMEM((group_size, rows, width), F32), near, near, far, far] + comm_sems(
        group_size, n
    )


class Scatter:
    def __init__(self, g, rc, scratch):
        self.g, self.rc = g, rc
        self.part, self.near_out, self.near_in, self.far_out, self.far_in = scratch[:5]
        self.far_send, self.far_recv, self.near_send, self.near_recv = scratch[5:]

    def near(self, k, j):
        rows = span(j, self.rc)
        return remote(
            self.near_out.at[k, rows],
            self.near_in.at[k, rows],
            self.near_send.at[k, j],
            self.near_recv.at[k, j],
            self.g.sibling,
        )

    def far(self, k, j):
        rows = span(j, self.rc)
        return remote(
            self.far_out.at[k - 1, rows],
            self.far_in.at[k - 1, rows],
            self.far_send.at[k - 1, j],
            self.far_recv.at[k - 1, j],
            self.g.ahead(k) * 2 + self.g.core,
        )

    def first(self, j):
        g, rows = self.g, span(j, self.rc)
        for k in list(range(1, g.chips)) + [0]:
            owner = g.ahead(k) * 2 + 1 - g.core
            self.near_out[k, rows, :] = self.part[owner, rows, :].astype(BF)
            self.near(k, j).start()

    def second(self, j):
        g, rows = self.g, span(j, self.rc)
        for k in range(1, g.chips):
            owner = g.ahead(k) * 2 + g.core
            self.near(k, j).wait_recv()
            both = self.part[owner, rows, :] + self.near_in[k, rows, :].astype(F32)
            self.far_out[k - 1, rows, :] = both.astype(BF)
            self.far(k, j).start()

    def third(self, j):
        g, rows = self.g, span(j, self.rc)
        self.near(0, j).wait_recv()
        total = self.part[g.me, rows, :] + self.near_in[0, rows, :].astype(F32)
        for k in range(1, g.chips):
            self.far(k, j).wait_recv()
            total = total + self.far_in[k - 1, rows, :].astype(F32)
        return total

    def drain(self, n):
        g = self.g

        def one(j, _):
            for k in range(1, g.chips):
                self.far(k, j).wait_send()
            for k in range(g.chips):
                self.near(k, j).wait_send()
            return 0

        lax.fori_loop(0, n, one, 0)


def far_copy(src, dst, send, recv, target):
    return pltpu.make_async_remote_copy(
        src_ref=src,
        dst_ref=dst,
        send_sem=send,
        recv_sem=recv,
        device_id=target,
        device_id_type=MESH,
    )


class Swap:
    def __init__(self, src, stage, sems):
        self.src, self.stage, self.sems = src, stage, sems
        self.s = lax.axis_index("section")

    def copies(self, layer):
        local = pltpu.make_async_copy(self.src.at[self.s], self.stage.at[self.s], self.sems.at[0])
        side = far_copy(
            self.src.at[1 - self.s],
            self.stage.at[layer],
            self.sems.at[1],
            self.sems.at[2],
            {"section": 1 - self.s},
        )
        return local, side

    def start(self):
        for copy in self.copies(self.s):
            copy.start()

    def arrive(self):
        local, side = self.copies(1 - self.s)
        local.wait()
        side.wait_recv()

    def finish(self):
        self.copies(self.s)[1].wait_send()


def reduce_scratch(replicas, rows, cols):
    many = pltpu.VMEM((replicas - 1, rows, cols), BF)
    one = pltpu.VMEM((rows, cols), BF)
    far, side = DMA((replicas - 1, 2)), DMA((2,))
    return [pltpu.VMEM((rows, cols), F32), many, many, one, one, far, far, side, side]


class Reduce:
    def __init__(self, layer, scratch):
        self.layer = layer
        self.own, self.away, self.came, self.over, self.back = scratch[:5]
        self.z_send, self.z_recv, self.y_send, self.y_recv = scratch[5:]
        self.replicas = self.away.shape[0] + 1
        self.half = self.own.shape[0] // 2
        self.d = lax.axis_index("dp")
        self.s = lax.axis_index("section")

    def target(self, k):
        return lax.rem(self.d + k, self.replicas)

    def part(self, i):
        return pl.ds(pl.multiple_of(i * self.half, self.half), self.half)

    def z_copy(self, k, i):
        part = self.part(i)
        return far_copy(
            self.away.at[k - 1, part],
            self.came.at[k - 1, part],
            self.z_send.at[k - 1, i],
            self.z_recv.at[k - 1, i],
            {"dp": self.target(k)},
        )

    def y_copy(self, i):
        part = self.part(i)
        return far_copy(
            self.over.at[part],
            self.back.at[part],
            self.y_send.at[i],
            self.y_recv.at[i],
            {"section": 1 - self.s},
        )

    def send(self, block):
        def one(i):
            k = i + 1
            self.away[i] = block(self.target(k)).astype(BF)
            self.z_copy(k, 0).start()
            self.z_copy(k, 1).start()

        run(self.replicas - 1, one)
        self.own[...] = block(self.d)

    def collect(self):
        def one(i):
            part = self.part(i)
            total = self.own[part, :]
            for k in range(1, self.replicas):
                self.z_copy(k, i).wait_recv()
                total = total + self.came[k - 1, part, :].astype(F32)
            self.own[part, :] = total
            self.over[part, :] = total.astype(BF)

            @pl.when(self.s != self.layer)
            def _():
                self.y_copy(i).start()

        run(2, one)

    def finish(self, out):
        @pl.when(self.s == self.layer)
        def _():
            self.y_copy(0).wait_recv()
            self.y_copy(1).wait_recv()
            out[...] = self.own[...] + self.back[...].astype(F32)

        @pl.when(self.s != self.layer)
        def _():
            self.y_copy(0).wait_send()
            self.y_copy(1).wait_send()
            out[...] = self.own[...]

        for k in range(1, self.replicas):
            self.z_copy(k, 0).wait_send()
            self.z_copy(k, 1).wait_send()


class HalfSwap:
    def __init__(self, src, came, sems):
        self.src, self.came, self.sems = src, came, sems
        self.s = lax.axis_index("section")
        self.rows = came.shape[1]

    def copy(self):
        at = pl.ds(pl.multiple_of((1 - self.s) * self.rows, self.rows), self.rows)
        return far_copy(
            self.src.at[:, at],
            self.came,
            self.sems.at[0],
            self.sems.at[1],
            {"section": 1 - self.s},
        )


def half_scratch(replicas, rows, cols):
    rows = rows // 2
    all_, far = pltpu.VMEM((replicas, rows, cols), BF), pltpu.VMEM((replicas - 1, rows, cols), BF)
    one = pltpu.VMEM((rows, cols), BF)
    z = DMA((replicas - 1,))
    return [all_, all_, far, far, pltpu.VMEM((rows, cols), F32), one, one, DMA((3,)), z, z, DMA((2,))]


HALF = 11


class HalfReduce:
    def __init__(self, layer, scratch):
        self.layer = layer
        self.mine, self.other, self.away, self.came, self.own, self.over, self.back = scratch[:7]
        self.in_sem, self.z_send, self.z_recv, self.y_sem = scratch[7:]
        self.replicas, self.rows = self.mine.shape[:2]
        self.s = lax.axis_index("section")
        self.d = lax.axis_index("dp")

    def half(self, s):
        return pl.ds(pl.multiple_of(s * self.rows, self.rows), self.rows)

    def loads(self, src, other):
        loads = [pltpu.make_async_copy(src.at[:, self.half(self.s)], self.mine, self.in_sem.at[0])]
        if other is not None:
            loads.append(pltpu.make_async_copy(other, self.other, self.in_sem.at[1]))
        return loads

    def z_copy(self, k):
        return far_copy(
            self.away.at[k - 1],
            self.came.at[k - 1],
            self.z_send.at[k - 1],
            self.z_recv.at[k - 1],
            {"dp": lax.rem(self.d + k, self.replicas)},
        )

    def y_copy(self):
        return far_copy(
            self.over, self.back, self.y_sem.at[0], self.y_sem.at[1], {"section": 1 - self.s}
        )

    def middle(self):
        def both(z):
            return self.mine[z].astype(F32) + self.other[z].astype(F32)

        for k in range(1, self.replicas):
            self.away[k - 1] = both(lax.rem(self.d + k, self.replicas)).astype(BF)
            self.z_copy(k).start()
        self.own[...] = both(self.d)

    def late(self):
        total = self.own[...]
        for k in range(1, self.replicas):
            self.z_copy(k).wait_recv()
            total = total + self.came[k - 1].astype(F32)
        self.own[...] = total
        self.over[...] = total.astype(BF)

        @pl.when(self.s != self.layer)
        def _():
            self.y_copy().start()

    def finish(self, out, above=None):
        @pl.when(self.s == self.layer)
        def _():
            self.y_copy().wait_recv()
            out[self.half(self.s), :] = self.own[...]
            out[self.half(1 - self.s), :] = self.back[...].astype(F32)

        @pl.when(self.s != self.layer)
        def _():
            if above is None:
                out[...] = jnp.zeros_like(out)
            else:
                copy = pltpu.make_async_copy(above, out, self.in_sem.at[2])
                copy.start()
                copy.wait()
            self.y_copy().wait_send()

        for k in range(1, self.replicas):
            self.z_copy(k).wait_send()


class Spread:
    def __init__(self, src, dst, by_columns, sems):
        self.src, self.dst, self.by_columns = src, dst, by_columns
        self.own_sem, self.far_send, self.far_recv, self.side_send, self.side_recv = sems
        self.replicas = far = self.side_send.shape[0]
        self.s = lax.axis_index("section")
        self.d = lax.axis_index("dp")
        self.stages = [
            sorted({k, far - k}) for k in range(1, far // 2 + 1)
        ]

    def place(self, half, z):
        rows, cols = self.src.shape
        if self.by_columns:
            return self.dst.at[
                pl.ds(pl.multiple_of(half * rows, rows), rows),
                pl.ds(pl.multiple_of(z * cols, cols), cols),
            ]
        return self.dst.at[pl.ds(pl.multiple_of((2 * z + half) * rows, rows), rows)]

    def origin(self, k):
        return lax.rem(self.d + self.replicas - k, self.replicas)

    def own(self):
        return pltpu.make_async_copy(self.src, self.place(self.s, self.d), self.own_sem.at[0])

    def far(self, k, origin):
        return pltpu.make_async_remote_copy(
            src_ref=self.src,
            dst_ref=self.place(self.s, origin),
            send_sem=self.far_send.at[k - 1],
            recv_sem=self.far_recv.at[k - 1],
            device_id={"dp": lax.rem(self.d + k, self.replicas)},
            device_id_type=MESH,
        )

    def side(self, k, half):
        place = self.place(half, self.origin(k))
        return pltpu.make_async_remote_copy(
            src_ref=self.src if k == 0 else place,
            dst_ref=place,
            send_sem=self.side_send.at[k],
            recv_sem=self.side_recv.at[k],
            device_id={"section": 1 - self.s},
            device_id_type=MESH,
        )

    def start(self):
        for k in self.stages[0]:
            self.far(k, self.d).start()
        self.side(0, self.s).start()
        self.own().start()

    def step(self, i):
        for k in self.stages[i]:
            self.far(k, self.origin(k)).wait_recv()
            self.side(k, self.s).start()
        if i + 1 < len(self.stages):
            for k in self.stages[i + 1]:
                self.far(k, self.d).start()

    def finish(self):
        self.own().wait()
        for k in range(self.replicas):
            self.side(k, 1 - self.s).wait_recv()
        for k in range(1, self.replicas):
            self.far(k, self.d).wait_send()
        for k in range(self.replicas):
            self.side(k, self.s).wait_send()


class ZGather:
    def __init__(self, src, got, sems):
        self.src, self.got = src, got
        self.own_sem, self.send, self.recv = sems
        self.replicas = got.shape[0]
        self.d = lax.axis_index("dp")

    def own(self):
        return pltpu.make_async_copy(self.src, self.got.at[self.d], self.own_sem.at[0])

    def far(self, k, origin):
        return far_copy(
            self.src,
            self.got.at[origin],
            self.send.at[k - 1],
            self.recv.at[k - 1],
            {"dp": lax.rem(self.d + k, self.replicas)},
        )

    def start(self):
        for k in range(1, self.replicas):
            self.far(k, self.d).start()
        self.own().start()

    def step(self, i):
        pass

    def finish(self):
        self.own().wait()
        for k in range(1, self.replicas):
            self.far(k, lax.rem(self.d + self.replicas - k, self.replicas)).wait_recv()
        for k in range(1, self.replicas):
            self.far(k, self.d).wait_send()


class YJoin:
    def __init__(self, got, dst, by_columns, sems):
        self.src, self.dst, self.by_columns = got, dst, by_columns
        self.own_sem, self.send, self.recv, self.got, self.in_sem = sems
        self.replicas, self.rows, self.cols = got.shape
        self.s = lax.axis_index("section")

    def place(self, half, z):
        rows, cols = self.rows, self.cols
        if self.by_columns:
            return self.dst.at[
                pl.ds(pl.multiple_of(half * rows, rows), rows), pl.ds(z * cols, cols)
            ]
        return self.dst.at[pl.ds(pl.multiple_of((2 * z + half) * rows, rows), rows)]

    def own(self, z):
        return pltpu.make_async_copy(self.got.at[z], self.place(self.s, z), self.own_sem.at[z])

    def side(self, z, half):
        return far_copy(
            self.got.at[z],
            self.place(half, z),
            self.send.at[z],
            self.recv.at[z],
            {"section": 1 - self.s},
        )

    def start(self):
        load = pltpu.make_async_copy(self.src, self.got, self.in_sem.at[0])
        load.start()
        load.wait()
        for z in range(self.replicas):
            self.side(z, self.s).start()
            self.own(z).start()

    def step(self, i):
        pass

    def finish(self):
        for z in range(self.replicas):
            self.own(z).wait()
            self.side(z, 1 - self.s).wait_recv()
        for z in range(self.replicas):
            self.side(z, self.s).wait_send()


def rider_sems(replicas):
    far, side = DMA((replicas - 1,)), DMA((replicas,))
    return [DMA((1,)), far, far, side, side]


class Riders:
    def __init__(self, srcs, dsts, columns, sems):
        self.all = []
        for src, dst, (kind, layer, by) in zip(srcs, dsts, columns):
            count = 3 if kind == "z" else 5
            own, sems = sems[:count], sems[count:]
            if kind == "spread":
                self.all.append(Spread(src.at[layer], dst, by, own))
            elif kind == "z":
                self.all.append(ZGather(src.at[layer], dst, own))
            else:
                self.all.append(YJoin(src, dst, by, own))
        self.replicas = self.all[0].replicas if self.all else 0

    def start(self):
        for one in self.all:
            one.start()

    def step(self, j, n):
        if not self.all:
            return
        stages = self.replicas // 2
        for i in range(stages):

            @pl.when(j == n * (i + 1) // stages - 1)
            def _(i=i):
                for one in self.all:
                    one.step(i)

    def finish(self):
        for one in self.all:
            one.finish()


def riding(riders, replicas):
    arrays = [array for array, _, _, _ in riders]
    columns = tuple(rider[1:] for rider in riders)
    outs, sems = [], []
    for array, kind, _, by in riders:
        rows, cols = array.shape[1:]
        if kind == "z":
            outs.append(shape((replicas, rows, cols), BF))
        else:
            outs.append(
                shape((2 * rows, replicas * cols) if by else (2 * replicas * rows, cols), BF)
            )
        far, side = DMA((replicas - 1,)), DMA((replicas,))
        sems += {
            "spread": rider_sems(replicas),
            "z": [DMA((1,)), far, far],
            "y": [side, side, side, pltpu.VMEM(array.shape, BF), DMA((1,))],
        }[kind]
    return arrays, columns, outs, sems


def params(key):
    return pltpu.CompilerParams(
        vmem_limit_bytes=LIMIT, collective_id=key, has_side_effects=True
    )


def cost(flops, moved, exps=0):
    return pl.CostEstimate(flops=int(flops), bytes_accessed=int(moved), transcendentals=int(exps))


def normed(source):
    center = source - jnp.mean(source, axis=-1, keepdims=True)
    r = lax.rsqrt(jnp.mean(center * center, axis=-1, keepdims=True) + 1e-05)
    return center * r, r


def normed_back(source, gain, grad):
    n, r = normed(source)
    e = grad * gain
    dh = r * (
        e - jnp.mean(e, axis=-1, keepdims=True) - n * jnp.mean(e * n, axis=-1, keepdims=True)
    )
    return dh, jnp.sum(grad * n, axis=0, keepdims=True)


def flat(value):
    return value.reshape((value.shape[0] * value.shape[1],) + value.shape[2:])


def run(n, body):
    def one(j, carry):
        body(j)
        return carry

    lax.fori_loop(0, n, one, 0)


def first_kernel(
    size, replicas, x_ref, gain_ref, wq_ref, wo_ref, wu_ref, wd_ref,
    qkv_ref, gains_out, a1_out, wq_out, wo_out, q_stage, o_stage, u_stage, d_stage,
    a1, w, gains, own_sem, q_sem, o_sem, u_sem, d_sem, gain_sem, *sems
):
    rows, width = x_ref.shape
    n = thin_chunks(rows)
    rc = rows // n
    g = Group(size)
    section = lax.axis_index("section")
    gather = Gather(g, a1, rc, sems[:4])
    swaps = [
        Swap(wq_ref, q_stage, q_sem),
        Swap(wo_ref, o_stage, o_sem),
        Swap(wu_ref, u_stage, u_sem),
        Swap(wd_ref, d_stage, d_sem),
    ]
    spreads = [
        Spread(q_stage.at[0], w, False, sems[4:9]),
        Spread(o_stage.at[0], wo_out, True, sems[9:14]),
    ]
    riders = Riders([], [], (), [])
    riders.all = spreads
    riders.replicas = replicas
    g.greet(replicas)

    def gain_copy(layer):
        return far_copy(
            gain_ref, gains.at[layer], gain_sem.at[0], gain_sem.at[1], {"section": 1 - section}
        )

    gain_copy(section).start()
    swaps[0].start()
    swaps[1].start()
    gains[section] = gain_ref[...]
    gain_copy(1 - section).wait_recv()
    gains_out[...] = gains[...]

    def send(j):
        at = span(j, rc)
        a = normed(x_ref[at, :].astype(F32))[0] * gains[0, 0:1, :]
        a1[g.me, at, :] = a.astype(BF)
        gather.start(j)

    run(n, send)
    swaps[0].arrive()
    swaps[1].arrive()
    riders.start()

    def relay(j):
        gather.relay(j)
        riders.step(j, n)

    run(n, relay)
    swaps[2].start()
    swaps[3].start()
    riders.finish()
    outs = [
        pltpu.make_async_copy(w, wq_out, own_sem.at[0]),
        pltpu.make_async_copy(a1, a1_out, own_sem.at[1]),
    ]
    outs[0].start()

    def multiply(j):
        at = span(j, rc)
        gather.ready(j)
        r = dg(flat(a1[:, at, :]), w[...], NN).astype(BF)
        qkv_ref[:, at, :] = r.reshape(size, rc, r.shape[1])

    run(n, multiply)
    outs[1].start()
    swaps[2].arrive()
    swaps[3].arrive()
    for swap in swaps:
        swap.finish()
    gain_copy(section).wait_send()
    gather.drain(n)
    for out in outs:
        out.wait()


def first_forward(size, replicas, x, gains, ws):
    rows, width = x.shape
    wide = ws[0].shape[2]
    deep = 2 * ws[1].shape[1]
    n = thin_chunks(rows)
    return pl.pallas_call(
        functools.partial(first_kernel, size, replicas),
        out_shape=[
            shape((size, rows, wide), BF),
            shape((2,) + gains.shape, F32),
            shape((size, rows, width), BF),
            shape((width, wide), BF),
            shape((deep, width), BF),
        ]
        + [shape(w.shape, BF) for w in ws],
        in_specs=[VM] * 6,
        out_specs=[VM, VM] + [HB] * 7,
        scratch_shapes=[
            pltpu.VMEM((size, rows, width), BF),
            pltpu.VMEM((width, wide), BF),
            pltpu.VMEM((2,) + gains.shape, F32),
            DMA((2,)),
            DMA((3,)),
            DMA((3,)),
            DMA((3,)),
            DMA((3,)),
            DMA((2,)),
        ]
        + comm_sems(size, n)
        + rider_sems(replicas) * 2,
        compiler_params=params(0),
        cost_estimate=cost(30e9, 30e6),
    )(x, gains, *ws)


def attend_kernel(size, layer, columns, *refs):
    m = len(columns)
    qkv_ref, qm_ref, km_ref, x_ref, w_ref = refs[:5]
    refs = refs[5:]
    if layer == 1:
        cot_ref, refs = refs[0], refs[1:]
    halves, refs = refs[:m], refs[m:]
    h1_ref, ctx_ref, lse_ref = refs[:3]
    refs = refs[3:]
    if layer == 1:
        cot_out, refs = refs[0], refs[1:]
    wholes, refs = refs[:m], refs[m:]
    ka, vt, w, w_sem = refs[:4]
    scratch, refs = refs[4:13], refs[13:]
    if layer == 1:
        cot_sems, cot_sem, refs = refs[:4], refs[4], refs[5:]
    riders = Riders(halves, wholes, columns, refs)
    _, rows, wide = qkv_ref.shape
    length = size * rows
    e = qm_ref.shape[2]
    heads = wide // (3 * e)
    c = e**-0.5 * math.log2(math.e)
    n = chunks(rows)
    rc = rows // n
    bq = size * rc
    kc = bq
    g = Group(size)
    copy = pltpu.make_async_copy(w_ref, w, w_sem.at[0])
    copy.start()
    g.greet(riders.replicas)
    riders.start()
    if layer == 1:
        cot = Gather(g, cot_out, rows, cot_sems)
        own = pltpu.make_async_copy(cot_ref, cot_out.at[g.me], cot_sem.at[0])
        own.start()
        cot.start(0, cot_ref)
    scatter = Scatter(g, rc, scratch)
    whole = flat(qkv_ref[...])
    for h in range(heads):
        o = 3 * e * h
        ka[h, :, :e] = whole[:, o + e : o + 2 * e]
        ka[h, :, e:] = flat(km_ref[...])
        vt[h, :e, :] = whole[:, o + 2 * e : o + 3 * e].T
        vt[h, e:, :] = jnp.ones((16, length), BF)
    copy.wait()

    def work(j):
        at = span(j, rc)
        qm = flat(qm_ref[:, at, :])
        found = []
        held_qkv = flat(qkv_ref[:, at, :])
        for h in range(heads):
            o = 3 * e * h
            q = jnp.concatenate([held_qkv[:, o : o + e], qm], axis=1)
            held = []
            top = None
            for k in range(length // kc):
                s = dg(ka[h, k * kc : (k + 1) * kc, :], q, NT)
                t = jnp.max(s, axis=0, keepdims=True)
                top = t if top is None else jnp.maximum(top, t)
                held.append(s)
            top = top * c
            acc = None
            for k in range(length // kc):
                p = jnp.exp2(held[k] * c - top).astype(BF)
                a = dg(vt[h, :, k * kc : (k + 1) * kc], p, NN)
                acc = a if acc is None else acc + a
            total = acc[e : e + 1]
            found.append((acc[:e] * (1.0 / total)).astype(BF))
            lse_ref[j, h : h + 1, :] = top + jnp.log2(total)
            if h == heads // 2:

                @pl.when(j > 0)
                def _():
                    scatter.second(j - 1)

        ctx = (jnp.concatenate(found, axis=0) if heads > 1 else found[0]).T
        ctx_ref[:, at, :] = ctx.reshape(size, rc, heads * e)
        width = x_ref.shape[1]
        scatter.part[:, at, :] = dg(ctx, w[...], NN).reshape(size, rc, width)
        scatter.first(j)
        riders.step(j, n)
        if layer == 1:

            @pl.when(j == n - 1)
            def _():
                cot.relay(0)

    run(n, work)
    scatter.second(n - 1)

    def last(j):
        at = span(j, rc)
        h1_ref[at, :] = x_ref[at, :].astype(F32) + scatter.third(j)

    run(n, last)
    scatter.drain(n)
    if layer == 1:
        cot.ready(0)
        cot.drain(1)
        own.wait()
    riders.finish()


def attend(size, replicas, layer, qkv, qm, km, x, w, riders, cot=()):
    _, rows, wide = qkv.shape
    e = qm.shape[2]
    heads = wide // (3 * e)
    width = x.shape[1]
    n = chunks(rows)
    halves, columns, outs, sems = riding(riders, replicas)
    return pl.pallas_call(
        functools.partial(attend_kernel, size, layer, columns),
        out_shape=[
            shape((rows, width), F32),
            shape((size, rows, heads * e), BF),
            shape((n, heads, size * rows // n), F32),
        ]
        + [shape((size, rows, width), BF) for _ in cot]
        + outs,
        in_specs=[VM, VM, VM, VM, HB] + [VM] * len(cot) + [HB] * len(riders),
        out_specs=[VM, VM, VM] + [HB] * (len(cot) + len(outs)),
        scratch_shapes=[
            pltpu.VMEM((heads, size * rows, 2 * e), BF),
            pltpu.VMEM((heads, e + 16, size * rows), BF),
            pltpu.VMEM((heads * e, width), BF),
            DMA((1,)),
        ]
        + scatter_scratch(size, rows, width, n)
        + (comm_sems(size, 1) + [DMA((1,))]) * len(cot)
        + sems,
        compiler_params=params(2 + layer),
        cost_estimate=cost(60e9, 20e6),
    )(qkv, qm, km, x, w, *cot, *halves)


def peak_kernel(
    size, parts, h1_ref, gain_ref, grad_ref, wu_ref, wd_ref,
    mid_ref, gain_out, gup_ref, gdown_ref, hid_out,
    a2, hid, dup, grad, wu, wd, w_sem, out_sem, *scratch
):
    rows, width = h1_ref.shape
    hidden = wu_ref.shape[1]
    depth = width // parts
    fb = min(256, hidden)
    n = chunks(rows)
    rc = rows // n
    g = Group(size)
    copies = [
        pltpu.make_async_copy(wu_ref, wu, w_sem.at[0]),
        pltpu.make_async_copy(wd_ref, wd, w_sem.at[1]),
        pltpu.make_async_copy(grad_ref, grad, w_sem.at[2]),
    ]
    for copy in copies:
        copy.start()
    g.greet()
    gather = Gather(g, a2, rc, scratch[:4])
    scatter = Scatter(g, rc, scratch[4:])

    def send(j):
        at = span(j, rc)
        a = normed(h1_ref[at, :])[0] * gain_ref[1, 1:2, :]
        a2[g.me, at, :] = a.astype(BF)
        gather.start(j)

    run(n, send)
    for copy in copies:
        copy.wait()
    gather.relay(0)

    def work(j):
        at = span(j, rc)
        gather.ready(j)
        a = flat(a2[:, at, :])
        held = flat(grad[:, at, :])
        for f in range(hidden // fb):
            cols = slice(f * fb, (f + 1) * fb)
            u = dg(a, wu[:, cols], NN)
            half = 0.5 + 0.5 * lax.erf(u * (0.5**0.5))
            slope = half + u * jnp.exp(-0.5 * u * u) * ((2 * math.pi) ** -0.5)
            hid[:, at, cols] = (u * half).astype(BF).reshape(size, rc, fb)
            d = dg(held, wd[cols, :], NT) * slope
            dup[:, at, cols] = d.astype(BF).reshape(size, rc, fb)

        @pl.when(j + 1 < n)
        def _():
            gather.relay(j + 1)

        @pl.when(j > 0)
        def _():
            scatter.second(j - 1)

        held = flat(dup[:, at, :])
        for z in range(parts):
            cols = slice(z * depth, (z + 1) * depth)
            scatter.part[:, at, cols] = dg(held, wu[cols, :], NT).reshape(size, rc, depth)
        scatter.first(j)

    run(n, work)
    scatter.second(n - 1)
    out = pltpu.make_async_copy(hid, hid_out, out_sem.at[0])
    out.start()

    def up_grad(z):
        cols = pl.ds(pl.multiple_of(z * depth, depth), depth)
        gup_ref[z] = dg(flat(a2[:, :, cols]), flat(dup[...]), TN).astype(BF)

    run(parts, up_grad)

    def down_grad(f):
        cols = pl.ds(pl.multiple_of(f * fb, fb), fb)
        r = dg(flat(hid[:, :, cols]), flat(grad[...]), TN).astype(BF)
        for z in range(parts):
            gdown_ref[z, cols, :] = r[:, z * depth : (z + 1) * depth]

    run(hidden // fb, down_grad)
    gain_out[...] = jnp.zeros_like(gain_out)

    def last(j):
        at = span(j, rc)
        dh, dgain = normed_back(h1_ref[at, :], gain_ref[1, 1:2, :], scatter.third(j))
        mid_ref[at, :] = grad[g.me, at, :].astype(F32) + dh
        gain_out[...] += dgain

    run(n, last)
    gather.drain(n)
    scatter.drain(n)
    out.wait()


def peak(size, replicas, h1, gains, grad_all, wu, wd):
    rows, width = h1.shape
    hidden = wu.shape[1]
    depth = width // replicas
    n = chunks(rows)
    return pl.pallas_call(
        functools.partial(peak_kernel, size, replicas),
        out_shape=[
            shape((rows, width), F32),
            shape((1, width), F32),
            shape((replicas, depth, hidden), BF),
            shape((replicas, hidden, depth), BF),
            shape((size, rows, hidden), BF),
        ],
        in_specs=[VM, VM, HB, HB, HB],
        out_specs=[VM, VM, VM, VM, HB],
        scratch_shapes=[
            pltpu.VMEM((size, rows, width), BF),
            pltpu.VMEM((size, rows, hidden), BF),
            pltpu.VMEM((size, rows, hidden), BF),
            pltpu.VMEM((size, rows, width), BF),
            pltpu.VMEM((width, hidden), BF),
            pltpu.VMEM((hidden, width), BF),
            DMA((3,)),
            DMA((1,)),
        ]
        + comm_sems(size, n)
        + scatter_scratch(size, rows, width, n),
        compiler_params=params(5),
        cost_estimate=cost(60e9, 30e6),
    )(h1, gains, grad_all, wu, wd)


def turn_kernel(size, columns, *refs):
    m = len(columns)
    h1_ref, gain_ref, wu_ref, wd_ref, q_stage = refs[:5]
    halves, refs = refs[5 : 5 + m], refs[5 + m :]
    y_ref, qkv_ref, a2_out, hid_out, slope_out, a1_out, wq_out = refs[:7]
    wholes, refs = refs[7 : 7 + m], refs[7 + m :]
    a2, hid, slope, wu, wd, a1, wq, w_sem, out_sem = refs[:9]
    gather_sems, next_sems, refs = refs[9:13], refs[13:17], refs[17:]
    scratch, refs = refs[:9], refs[9:]
    spread = Spread(q_stage.at[1], wq, False, refs[:5])
    riders = Riders(halves, wholes, columns, refs[5:])
    out_rider, up_rider = riders.all
    stages = len(spread.stages)
    rows, width = h1_ref.shape
    hidden = wu_ref.shape[1]
    fb = min(256, hidden)
    n = chunks(rows)
    rc = rows // n
    g = Group(size)
    copies = [
        pltpu.make_async_copy(wu_ref, wu, w_sem.at[0]),
        pltpu.make_async_copy(wd_ref, wd, w_sem.at[1]),
    ]
    for copy in copies:
        copy.start()
    g.greet(spread.replicas)
    gather = Gather(g, a2, rc, gather_sems)
    onward = Gather(g, a1, rc, next_sems)
    scatter = Scatter(g, rc, scratch)

    def send(j):
        at = span(j, rc)
        a = normed(h1_ref[at, :])[0] * gain_ref[0, 1:2, :]
        a2[g.me, at, :] = a.astype(BF)
        gather.start(j)

    run(n, send)
    spread.start()
    out_rider.start()
    for copy in copies:
        copy.wait()

    def pass_on(j):
        at = span(j, rc)
        y = (h1_ref[at, :] + scatter.third(j)).astype(BF)
        y_ref[at, :] = y
        a = normed(y.astype(F32))[0] * gain_ref[1, 0:1, :]
        a1[g.me, at, :] = a.astype(BF)
        onward.start(j)

    lag = min(2, n)
    gather.relay(0)

    def work(j):
        at = span(j, rc)
        gather.ready(j)
        a = flat(a2[:, at, :])
        for f in range(hidden // fb):
            cols = slice(f * fb, (f + 1) * fb)
            u = dg(a, wu[:, cols], NN)
            half = 0.5 + 0.5 * lax.erf(u * (0.5**0.5))
            slope[:, at, cols] = (
                (half + u * jnp.exp(-0.5 * u * u) * ((2 * math.pi) ** -0.5))
                .astype(BF)
                .reshape(size, rc, fb)
            )
            hid[:, at, cols] = (u * half).astype(BF).reshape(size, rc, fb)

        @pl.when(j + 1 < n)
        def _():
            gather.relay(j + 1)

        @pl.when(j > 0)
        def _():
            scatter.second(j - 1)

        held = flat(hid[:, at, :])
        for f in range(width // 256):
            cols = slice(f * 256, (f + 1) * 256)
            scatter.part[:, at, cols] = dg(held, wd[:, cols], NN).reshape(size, rc, 256)
        scatter.first(j)

        @pl.when(j >= lag)
        def _():
            pass_on(j - lag)

        @pl.when(j == n // 2)
        def _():
            spread.step(0)
            out_rider.step(0)
            up_rider.start()

        @pl.when(j == n - 1)
        def _():
            for i in range(1, stages):
                spread.step(i)
                out_rider.step(i)

    run(n, work)
    scatter.second(n - 1)
    outs = [
        pltpu.make_async_copy(a2, a2_out, out_sem.at[0]),
        pltpu.make_async_copy(hid, hid_out, out_sem.at[1]),
        pltpu.make_async_copy(slope, slope_out, out_sem.at[2]),
    ]
    for out in outs:
        out.start()
    for j in range(n - lag, n):
        pass_on(j)
    up_rider.step(0)
    spread.finish()
    outs.append(pltpu.make_async_copy(wq, wq_out, out_sem.at[3]))
    outs[3].start()

    onward.relay(0)

    def multiply(j):
        at = span(j, rc)

        @pl.when(j + 1 < n)
        def _():
            onward.relay(j + 1)

        onward.ready(j)
        r = dg(flat(a1[:, at, :]), wq[...], NN).astype(BF)
        qkv_ref[:, at, :] = r.reshape(size, rc, r.shape[1])

    run(n, multiply)
    outs.append(pltpu.make_async_copy(a1, a1_out, out_sem.at[4]))
    outs[4].start()
    for i in range(1, stages):
        up_rider.step(i)
    riders.finish()
    gather.drain(n)
    onward.drain(n)
    scatter.drain(n)
    for out in outs:
        out.wait()


def turn_forward(size, replicas, h1, gains, wu, wd, stage, riders):
    rows, width = h1.shape
    hidden = wu.shape[1]
    wide = stage.shape[2]
    n = chunks(rows)
    halves, columns, outs, sems = riding(riders, replicas)
    return pl.pallas_call(
        functools.partial(turn_kernel, size, columns),
        out_shape=[
            shape((rows, width), BF),
            shape((size, rows, wide), BF),
            shape((size, rows, width), BF),
            shape((size, rows, hidden), BF),
            shape((size, rows, hidden), BF),
            shape((size, rows, width), BF),
            shape((width, wide), BF),
        ]
        + outs,
        in_specs=[VM, VM] + [HB] * (3 + len(riders)),
        out_specs=[VM, VM] + [HB] * (5 + len(outs)),
        scratch_shapes=[
            pltpu.VMEM((size, rows, width), BF),
            pltpu.VMEM((size, rows, hidden), BF),
            pltpu.VMEM((size, rows, hidden), BF),
            pltpu.VMEM((width, hidden), BF),
            pltpu.VMEM((hidden, width), BF),
            pltpu.VMEM((size, rows, width), BF),
            pltpu.VMEM((width, wide), BF),
            DMA((2,)),
            DMA((5,)),
        ]
        + comm_sems(size, n) * 2
        + scatter_scratch(size, rows, width, n)
        + rider_sems(replicas)
        + sems,
        compiler_params=params(4),
        cost_estimate=cost(50e9, 30e6),
    )(h1, gains, wu, wd, stage, *halves)


def mlp_back_kernel(size, layer, parts, *refs):
    g_ref, h1_ref, gain_ref, a2_ref, hid_ref, slope_ref, wu_ref, wd_ref = refs[:8]
    refs = refs[8:]
    ys, refs = refs[:2], refs[2:]
    mid_ref, gain_out, gup_ref, gdown_ref = refs[:4]
    refs = refs[4:]
    y_out, refs = refs[0], refs[1:]
    grad, a2, hid, dup, wu, wd, w_sem = refs[:7]
    scratch, refs = refs[7:20], refs[20:]
    rows, width = h1_ref.shape
    hidden = wu_ref.shape[1]
    depth = width // parts
    fb = min(256, hidden)
    n = chunks(rows)
    rc = rows // n
    g = Group(size)
    copies = [
        pltpu.make_async_copy(wd_ref, wd, w_sem.at[0]),
        pltpu.make_async_copy(slope_ref, dup, w_sem.at[1]),
        pltpu.make_async_copy(wu_ref, wu, w_sem.at[2]),
    ]
    late = [
        pltpu.make_async_copy(hid_ref, hid, w_sem.at[3]),
        pltpu.make_async_copy(a2_ref, a2, w_sem.at[4]),
    ]
    for copy in copies:
        copy.start()
    g.greet(side=True)
    section = lax.axis_index("section")
    y_sem, y_own = refs

    def y_load(own):
        return pltpu.make_async_copy(own, y_own, y_sem.at[3])

    def y_copies(own, other, at):
        return (
            pltpu.make_async_copy(y_own, y_out.at[section], y_sem.at[0]),
            far_copy(
                other, y_out.at[at], y_sem.at[1], y_sem.at[2], {"section": 1 - section}
            ),
        )

    for i in range(2):

        @pl.when(section == i)
        def _(i=i):
            y_load(ys[i]).start()
            y_copies(ys[i], ys[1 - i], section)[1].start()

    gather = Gather(g, grad, rc, scratch[:4])
    scatter = Scatter(g, rc, scratch[4:])

    def send(j):
        at = span(j, rc)
        grad[g.me, at, :] = g_ref[at, :]
        gather.start(j)

    run(n, send)
    for copy in copies:
        copy.wait()
    for copy in late:
        copy.start()
    y_load(ys[0]).wait()
    y_copies(ys[0], ys[1], section)[0].start()

    gather.relay(0)

    def work(j):
        at = span(j, rc)
        gather.ready(j)
        held = flat(grad[:, at, :])
        for f in range(hidden // fb):
            cols = slice(f * fb, (f + 1) * fb)
            d = dg(held, wd[cols, :], NT) * flat(dup[:, at, cols]).astype(F32)
            dup[:, at, cols] = d.astype(BF).reshape(size, rc, fb)

        @pl.when(j + 1 < n)
        def _():
            gather.relay(j + 1)

        @pl.when(j > 0)
        def _():
            scatter.second(j - 1)

        held = flat(dup[:, at, :])
        for z in range(parts):
            cols = slice(z * depth, (z + 1) * depth)
            scatter.part[:, at, cols] = dg(held, wu[cols, :], NT).reshape(size, rc, depth)
        scatter.first(j)

    run(n, work)
    scatter.second(n - 1)
    for copy in late:
        copy.wait()

    def up_grad(z):
        cols = pl.ds(pl.multiple_of(z * depth, depth), depth)
        gup_ref[z] = dg(flat(a2[:, :, cols]), flat(dup[...]), TN).astype(BF)

    run(parts, up_grad)

    def down_grad(f):
        cols = pl.ds(pl.multiple_of(f * fb, fb), fb)
        r = dg(flat(hid[:, :, cols]), flat(grad[...]), TN).astype(BF)
        for z in range(parts):
            gdown_ref[z, cols, :] = r[:, z * depth : (z + 1) * depth]

    run(hidden // fb, down_grad)
    gain_out[...] = jnp.zeros_like(gain_out)

    def last(j):
        at = span(j, rc)
        dh, dgain = normed_back(h1_ref[at, :], gain_ref[layer, 1:2, :], scatter.third(j))
        mid_ref[at, :] = g_ref[at, :].astype(F32) + dh
        gain_out[...] += dgain

    run(n, last)
    local, side = y_copies(ys[0], ys[1], 1 - section)
    local.wait()
    side.wait_recv()
    y_copies(ys[0], ys[1], section)[1].wait_send()
    gather.drain(n)
    scatter.drain(n)


def mlp_backward(size, replicas, layer, grad, h1, gains, a2, hid, slope, wu, wd, extra):
    rows, width = h1.shape
    hidden = wu.shape[1]
    parts, depth = replicas, width // replicas
    n = chunks(rows)
    return pl.pallas_call(
        functools.partial(mlp_back_kernel, size, layer, parts),
        out_shape=[
            shape((rows, width), F32),
            shape((1, width), F32),
            shape((parts, depth, hidden), BF),
            shape((parts, hidden, depth), BF),
        ]
        + [shape((2, rows, width), BF)] * (len(extra) // 2),
        in_specs=[VM, VM, VM] + [HB] * (5 + len(extra)),
        out_specs=[VM, VM, VM, VM] + [HB] * (len(extra) // 2),
        scratch_shapes=[
            pltpu.VMEM((size, rows, width), BF),
            pltpu.VMEM((size, rows, width), BF),
            pltpu.VMEM((size, rows, hidden), BF),
            pltpu.VMEM((size, rows, hidden), BF),
            pltpu.VMEM((width, hidden), BF),
            pltpu.VMEM((hidden, width), BF),
            DMA((6,)),
        ]
        + comm_sems(size, n)
        + scatter_scratch(size, rows, width, n)
        + [DMA((4,)), pltpu.VMEM((rows, width), BF)] * (len(extra) // 2),
        compiler_params=params(6 + layer),
        cost_estimate=cost(60e9, 40e6),
    )(grad, h1, gains, a2, hid, slope, wu, wd, *extra)


def attend_back_kernel(size, layer, parts, *refs):
    mid_ref, qkv_ref, qm_ref, km_ref, ctx_ref, lse_ref, w_ref = refs[:7]
    refs = refs[7:]
    if layer == 0:
        gdown_ref, refs = refs[0], refs[1:]
    else:
        hid_ref, wd_ref, h1_in, refs = refs[0], refs[1], refs[2], refs[3:]
    dqkv_ref, gout_ref, refs = refs[0], refs[1], refs[2:]
    if layer == 0:
        down_out, refs = refs[0], refs[1:]
    else:
        y_ref, refs = refs[0], refs[1:]
    da, ka, va, kt, dk, dv, w, w_sem = refs[:8]
    sems, refs = refs[8:12], refs[12:]
    reduce = Reduce(layer, refs[:9])
    if layer == 0:
        down = HalfReduce(layer, refs[9 : 9 + HALF])
        down_swap = HalfSwap(gdown_ref, down.other, refs[9 + HALF])
    else:
        held_hid, wd, h1, y_sem = refs[9:13]
    _, rows, wide = qkv_ref.shape
    length = size * rows
    e = qm_ref.shape[2]
    heads = wide // (3 * e)
    scale = e**-0.5
    c = scale * math.log2(math.e)
    depth = w_ref.shape[1] // parts
    n = chunks(rows)
    rc = rows // n
    bq = size * rc
    kc = bq
    g = Group(size)
    copies = [pltpu.make_async_copy(w_ref, w, w_sem.at[0])]
    for copy in copies:
        copy.start()
    g.greet(parts)
    gather = Gather(g, da, rc, sems)
    loads = []
    if layer == 1:
        scatter = Scatter(g, rc, refs[13:])
        loads = [
            pltpu.make_async_copy(wd_ref, wd, y_sem.at[0]),
            pltpu.make_async_copy(h1_in, h1, y_sem.at[1]),
        ]
        for load in loads:
            load.start()
    if layer == 0:
        down_swap.copy().start()
        loads = down.loads(gdown_ref, None)
        for load in loads:
            load.start()

    def send(j):
        at = span(j, rc)
        da[g.me, at, :] = mid_ref[at, :].astype(BF)
        gather.start(j)

    run(n, send)
    lane = lax.broadcasted_iota(jnp.int32, (length, e), 1)
    whole = flat(qkv_ref[...])
    for h in range(heads):
        o = 3 * e * h
        ka[h, :, :e] = whole[:, o + e : o + 2 * e]
        ka[h, :, e:] = flat(km_ref[...])
        va[h, :, :e] = whole[:, o + 2 * e : o + 3 * e]
        va[h, :, e:] = jnp.where(lane < 3, 1.0, 0.0).astype(BF)
        kt[h] = whole[:, o + e : o + 2 * e].T
    dk[...] = jnp.zeros_like(dk)
    dv[...] = jnp.zeros_like(dv)
    ql = lax.broadcasted_iota(jnp.int32, (bq, e), 1)
    for copy in copies + loads:
        copy.wait()

    def out_grad(z):
        cols = pl.ds(pl.multiple_of(z * depth, depth), depth)
        return dg(flat(ctx_ref[...]), flat(da[:, :, cols]), TN)

    def work(j):
        at = span(j, rc)

        @pl.when(j == 0)
        def _():
            gather.relay(0)
            gather.ready(0)

        @pl.when(j == min(1, n - 1))
        def _():
            for i in range(1, n):
                gather.relay(i)
            for i in range(1, n):
                gather.ready(i)
            reduce.send(out_grad)

        if layer == 1:
            hid_load = pltpu.make_async_copy(hid_ref.at[:, at], held_hid, y_sem.at[2])
            hid_load.start()
        qm = flat(qm_ref[:, at, :])
        dctx = dg(flat(da[:, at, :]), w[...], NT).astype(BF)
        ctx = flat(ctx_ref[:, at, :])
        held_qkv = flat(qkv_ref[:, at, :])
        for h in range(heads):
            o = 3 * e * h
            qq = held_qkv[:, o : o + e]
            q = jnp.concatenate([qq, qm], axis=1)
            dc = dctx[:, h * e : (h + 1) * e]
            prod = dc.astype(F32) * ctx[:, h * e : (h + 1) * e].astype(F32)
            d = -jnp.sum(prod, axis=1, keepdims=True)
            d1 = d.astype(BF).astype(F32)
            d2 = (d - d1).astype(BF).astype(F32)
            d3 = d - d1 - d2
            ds_col = jnp.where(ql == 0, d1, jnp.where(ql == 1, d2, jnp.where(ql == 2, d3, 0.0)))
            dca = jnp.concatenate([dc, ds_col.astype(BF)], axis=1)
            lse = lse_ref[j, h : h + 1, :]
            dqt = None
            for k in range(length // kc):
                ks = slice(k * kc, (k + 1) * kc)
                s = dg(ka[h, ks, :], q, NT)
                p = jnp.exp2(s * c - lse)
                ds = (p * dg(va[h, ks, :], dca, NT)).astype(BF)
                dv[h, ks, :] += dg(p.astype(BF), dc, NN)
                dk[h, ks, :] += dg(ds, qq, NN)
                a = dg(kt[h, :, ks], ds, NN)
                dqt = a if dqt is None else dqt + a
            if layer == 0 and h == heads // 2:

                @pl.when(j == min(1, n - 1))
                def _():
                    down_swap.copy().wait_recv()
                    down.middle()

            if layer == 1 and h == heads // 2:

                @pl.when(j > 0)
                def _():
                    scatter.second(j - 1)

            if layer == 0 and h == heads - 1:

                @pl.when(j == n - 1)
                def _():
                    down.late()

            dqkv_ref[:, at, o : o + e] = (dqt * scale).T.astype(BF).reshape(size, rc, e)
        if layer == 1:
            hid_load.wait()
            width = wd.shape[1]
            for f in range(width // 256):
                cols = slice(f * 256, (f + 1) * 256)
                scatter.part[:, at, cols] = dg(flat(held_hid[...]), wd[:, cols], NN).reshape(
                    size, rc, 256
                )
            scatter.first(j)

    run(n, work)
    if layer == 1:
        scatter.second(n - 1)
    for h in range(heads):
        o = 3 * e * h
        dqkv_ref[:, :, o + e : o + 2 * e] = (dk[h] * scale).astype(BF).reshape(size, rows, e)
        dqkv_ref[:, :, o + 2 * e : o + 3 * e] = dv[h].astype(BF).reshape(size, rows, e)

    reduce.collect()
    if layer == 1:

        def output(j):
            at = span(j, rc)
            y_ref[at, :] = (h1[at, :] + scatter.third(j)).astype(BF)

        run(n, output)
        scatter.drain(n)
    reduce.finish(gout_ref)
    if layer == 0:
        down.finish(down_out)
        down_swap.copy().wait_send()
    gather.drain(n)


def attend_backward(size, replicas, layer, mid, qkv, qm, km, ctx, lse, w, grads, more=()):
    _, rows, wide = qkv.shape
    e = qm.shape[2]
    heads = wide // (3 * e)
    width = mid.shape[1]
    parts, depth = replicas, width // replicas
    length = size * rows
    n = chunks(rows)
    return pl.pallas_call(
        functools.partial(attend_back_kernel, size, layer, parts),
        out_shape=[shape(qkv.shape, BF), shape((heads * e, depth), F32)]
        + [shape(grad.shape[1:], F32) for grad in grads]
        + [shape((rows, width), BF)] * (len(more) // 3),
        in_specs=[VM] * 6 + [HB] * (1 + len(grads) + len(more)),
        out_specs=[VM, VM] + [VM] * (len(grads) + len(more) // 3),
        scratch_shapes=[
            pltpu.VMEM((size, rows, width), BF),
            pltpu.VMEM((heads, length, 2 * e), BF),
            pltpu.VMEM((heads, length, 2 * e), BF),
            pltpu.VMEM((heads, e, length), BF),
            pltpu.VMEM((heads, length, e), F32),
            pltpu.VMEM((heads, length, e), F32),
            pltpu.VMEM((heads * e, width), BF),
            DMA((1,)),
        ]
        + comm_sems(size, n)
        + reduce_scratch(parts, heads * e, depth)
        + sum([half_scratch(parts, *grad.shape[1:]) + [DMA((2,))] for grad in grads], [])
        + (
            [
                pltpu.VMEM((size, rows // n, more[0].shape[2]), BF),
                pltpu.VMEM(more[1].shape, BF),
                pltpu.VMEM((rows, width), F32),
                DMA((3,)),
            ]
            + scatter_scratch(size, rows, width, n)
            if more
            else []
        ),
        compiler_params=params(8 + layer),
        cost_estimate=cost(90e9, 40e6),
    )(mid, qkv, qm, km, ctx, lse, w, *grads, *more)


def qkv_back_kernel(
    size, layer, parts, dqkv_ref, gain_ref, a1_in, x_in, mid_in, w_ref,
    dx_ref, gain_out, gqkv_ref, a1_ref, x_ref, mid_ref, w, w_sem, *scratch
):
    rows, width = x_ref.shape
    late = [
        pltpu.make_async_copy(a1_in, a1_ref, w_sem.at[1]),
        pltpu.make_async_copy(x_in, x_ref, w_sem.at[2]),
        pltpu.make_async_copy(mid_in, mid_ref, w_sem.at[3]),
    ]
    depth = width // parts
    n = thin_chunks(rows)
    rc = rows // n
    g = Group(size)
    copies = [pltpu.make_async_copy(w_ref, w, w_sem.at[0])]
    for copy in copies + late:
        copy.start()
    g.greet()
    scatter = Scatter(g, rc, scratch)
    for copy in copies:
        copy.wait()

    lag = min(2, n)

    def work(j):
        at = span(j, rc)
        held = flat(dqkv_ref[:, at, :])
        for z in range(parts):
            cols = slice(z * depth, (z + 1) * depth)
            scatter.part[:, at, cols] = dg(held, w[cols, :], NT).reshape(size, rc, depth)
        scatter.first(j)

        @pl.when(j >= lag)
        def _():
            scatter.second(j - lag)


    run(n, work)
    for j in range(n - lag, n):
        scatter.second(j)
    for copy in late:
        copy.wait()

    def qkv_grad(z):
        cols = pl.ds(pl.multiple_of(z * depth, depth), depth)
        gqkv_ref[z] = dg(flat(a1_ref[:, :, cols]), flat(dqkv_ref[...]), TN).astype(BF)

    run(parts, qkv_grad)
    gain_out[...] = jnp.zeros_like(gain_out)

    def last(j):
        at = span(j, rc)
        dh, dgain = normed_back(
            x_ref[at, :].astype(F32), gain_ref[layer, 0:1, :], scatter.third(j)
        )
        dx_ref[at, :] = (mid_ref[at, :] + dh).astype(BF)
        gain_out[...] += dgain

    run(n, last)
    scatter.drain(n)


def qkv_backward(size, replicas, layer, dqkv, a1, x, mid, gains, w):
    rows, width = x.shape
    wide = w.shape[1]
    parts, depth = replicas, width // replicas
    n = thin_chunks(rows)
    return pl.pallas_call(
        functools.partial(qkv_back_kernel, size, layer, parts),
        out_shape=(
            shape((rows, width), BF),
            shape((1, width), F32),
            shape((parts, depth, wide), BF),
        ),
        in_specs=[VM, VM] + [HB] * 4,
        out_specs=(VM, VM, VM),
        scratch_shapes=[
            pltpu.VMEM((size, rows, width), BF),
            pltpu.VMEM((rows, width), BF),
            pltpu.VMEM((rows, width), F32),
            pltpu.VMEM((width, wide), BF),
            DMA((4,)),
        ]
        + scatter_scratch(size, rows, width, n),
        compiler_params=params(11),
        cost_estimate=cost(30e9, 30e6),
    )(dqkv, gains, a1, x, mid, w)


def last_kernel(
    size, parts, dqkv_ref, a1_ref, x_ref, mid_ref, gain_ref, w_ref, two_ref, above_ref, dx1_ref,
    gain_out, gqkv_out, dx_out,
    gqkv, swap_sem, w, dx, gsum, gcame, w_sem, x_sem, x_send, x_recv, g_send, g_recv, *scratch
):
    rows, width = x_ref.shape
    depth = width // parts
    n = thin_chunks(rows)
    rc = rows // n
    g = Group(size)
    section = lax.axis_index("section")
    d = lax.axis_index("dp")
    copy = pltpu.make_async_copy(w_ref, w, w_sem.at[0])
    copy.start()
    reduce = HalfReduce(0, scratch[:HALF])
    swap = HalfSwap(gqkv, reduce.other, swap_sem)
    scatter = Scatter(g, rc, scratch[HALF:])
    g.greet(parts)

    def upper():
        return far_copy(
            dx1_ref, dx_out.at[0], x_send.at[n], x_recv.at[n], {"section": 1 - section}
        )

    def keep_upper():
        return pltpu.make_async_copy(dx1_ref, dx_out.at[1], x_sem.at[0])

    def lower(j):
        at = span(j, rc)
        return far_copy(
            dx.at[at], dx_out.at[1, at], x_send.at[j], x_recv.at[j], {"section": 1 - section}
        )

    def keep_lower(j):
        at = span(j, rc)
        return pltpu.make_async_copy(dx.at[at], dx_out.at[0, at], x_sem.at[j])

    def qkv_grad(z):
        cols = pl.ds(pl.multiple_of(z * depth, depth), depth)
        gqkv[z] = dg(flat(a1_ref[:, :, cols]), flat(dqkv_ref[...]), TN).astype(BF)

    run(parts, qkv_grad)
    swap.copy().start()
    load = reduce.loads(gqkv, None)[0]
    load.start()

    @pl.when(section == 1)
    def _():
        keep_upper().start()

    copy.wait()

    lag = min(2, n)

    def work(j):
        at = span(j, rc)
        held = flat(dqkv_ref[:, at, :])
        for z in range(parts):
            cols = slice(z * depth, (z + 1) * depth)
            scatter.part[:, at, cols] = dg(held, w[cols, :], NT).reshape(size, rc, depth)
        scatter.first(j)

        @pl.when(j >= lag)
        def _():
            scatter.second(j - lag)


    run(n, work)
    for j in range(n - lag, n):
        scatter.second(j)
    gsum[0] = jnp.zeros_like(gsum[0])

    def last(j):
        at = span(j, rc)
        dh, dgain = normed_back(x_ref[at, :].astype(F32), gain_ref[0, 0:1, :], scatter.third(j))
        dx[at, :] = (mid_ref[at, :] + dh).astype(BF)

        @pl.when(section == 0)
        def _():
            keep_lower(j).start()

        @pl.when(section == 1)
        def _():
            lower(j).start()

        gsum[0, 0:1, :] += dgain

    def rest(j):
        @pl.when(j == n // 2)
        def _():
            load.wait()
            swap.copy().wait_recv()
            reduce.middle()

            @pl.when(section == 0)
            def _():
                upper().start()

        last(j)

    run(n, rest)
    gsum[0, 1:2, :] = two_ref[...]
    gsum[0, 2:4, :] = above_ref[...]

    targets = [
        [{"tensor": g.sibling}],
        [{"tensor": g.ahead(k) * 2 + g.core} for k in range(1, g.chips)],
        [{"dp": lax.rem(d + k, parts)} for k in range(1, parts)],
        [{"section": 1 - section}],
    ]
    slot = 0
    sent = []

    def exchange(stage):
        nonlocal slot
        copies = []
        for target in targets[stage]:
            copies.append(
                far_copy(gsum.at[stage], gcame.at[slot], g_send.at[slot], g_recv.at[slot], target)
            )
            copies[-1].start()
            slot += 1
        total = gsum[stage]
        for i, copy in enumerate(copies):
            copy.wait_recv()
            total = total + gcame[slot - len(copies) + i]
        gsum[stage + 1] = total
        sent.extend(copies)

    exchange(0)
    exchange(1)
    reduce.late()
    exchange(2)
    exchange(3)
    gain_out[...] = gsum[4]

    @pl.when(section == 0)
    def _():
        for j in range(n):
            lower(j).wait_recv()
            keep_lower(j).wait()
        upper().wait_send()

    @pl.when(section == 1)
    def _():
        keep_upper().wait()
        upper().wait_recv()
        for j in range(n):
            lower(j).wait_send()

    reduce.finish(gqkv_out)
    swap.copy().wait_send()
    for copy in sent:
        copy.wait_send()
    scatter.drain(n)


def last_backward(size, replicas, dqkv, a1, x, mid, gains, w, two, above, dx1):
    rows, width = x.shape
    wide = w.shape[1]
    depth = width // replicas
    n = thin_chunks(rows)
    slots = 1 + (size // 2 - 1) + (replicas - 1) + 1
    return pl.pallas_call(
        functools.partial(last_kernel, size, replicas),
        out_shape=(
            shape((8, width), F32),
            shape((depth, wide), F32),
            shape((2, rows, width), BF),
        ),
        in_specs=[VM] * 5 + [HB, VM, VM, VM],
        out_specs=(VM, VM, HB),
        scratch_shapes=[
            pltpu.VMEM((replicas, depth, wide), BF),
            DMA((2,)),
            pltpu.VMEM((width, wide), BF),
            pltpu.VMEM((rows, width), BF),
            pltpu.VMEM((5, 8, width), F32),
            pltpu.VMEM((slots, 8, width), F32),
            DMA((1,)),
            DMA((n,)),
            DMA((n + 1,)),
            DMA((n + 1,)),
            DMA((slots,)),
            DMA((slots,)),
        ]
        + half_scratch(replicas, depth, wide)
        + scatter_scratch(size, rows, width, n),
        compiler_params=params(10),
        cost_estimate=cost(40e9, 30e6),
    )(dqkv, a1, x, mid, gains, w, two, above, dx1)


def scene_masks(segments, e):
    same = (segments[..., None] == jnp.arange(e, dtype=jnp.int32)).astype(F32)
    used = jnp.arange(e) < SCENES
    return (
        jnp.where(used, same * MASKED, 0.0).astype(BF),
        jnp.where(used, 1.0 - same, 0.0).astype(BF),
    )


def swap_section(value):
    return lax.ppermute(value, "section", [(0, 1), (1, 0)])


def shards(
    block_input,
    segment_ids,
    cotangent,
    norm_one_gain,
    qkv_weight,
    out_weight,
    norm_two_gain,
    up_weight,
    down_weight,
):
    section = lax.axis_index("section")
    size = lax.axis_size("tensor")
    replicas = lax.axis_size("dp")

    mine = [
        qkv_weight[0].reshape((qkv_weight.shape[1], -1)),
        out_weight[0].reshape((-1, out_weight.shape[3])),
        up_weight[0],
        down_weight[0],
    ]
    mine = [w.astype(BF).reshape((2, -1, w.shape[1])) for w in mine]
    gains = jnp.concatenate(
        [norm_one_gain, norm_two_gain, jnp.zeros((6, norm_one_gain.shape[1]), F32)], axis=0
    )
    segments = lax.dynamic_index_in_dim(segment_ids, section, 0, keepdims=False)
    x = lax.dynamic_index_in_dim(block_input, section, 0, keepdims=False)
    head_dim = qkv_weight.shape[3] // 3
    qm, km = scene_masks(segments.reshape((size, -1)), head_dim)
    qkv, gains, a1, w_qkv_0, w_out_0, h_qkv, h_out, h_up, h_down = first_forward(
        size, replicas, x, gains, mine
    )
    h1, ctx, lse, w_up_0, w_down_0 = attend(
        size, replicas, 0, qkv, qm, km, x, w_out_0,
        [(h_up, "spread", 0, False), (h_down, "spread", 0, True)],
    )
    below = (x, a1, qkv, ctx, lse, h1)
    y0, qkv, a2, hid, slope, a1, w_qkv_1, w_out_1, w_up_1 = turn_forward(
        size, replicas, h1, gains, w_up_0, w_down_0, h_qkv,
        [(h_out, "spread", 1, True), (h_up, "spread", 1, False)],
    )
    kept = [below + (a2, hid, slope)]
    grad = lax.dynamic_index_in_dim(cotangent, section, 0, keepdims=False)
    h1, ctx, lse, grad_all, w_down_1 = attend(
        size, replicas, 1, qkv, qm, km, y0, w_out_1, [(h_down, "spread", 1, True)], [grad]
    )
    kept.append((y0, a1, qkv, ctx, lse, h1))
    weights = [
        (w_qkv_0, w_out_0, w_up_0, w_down_0),
        (w_qkv_1, w_out_1, w_up_1, w_down_1),
    ]
    def reduce_rows(value):
        return lax.psum_scatter(value, "dp", scatter_dimension=0, tiled=False)

    x, a1, qkv, ctx, lse, h1 = kept[1]
    w_qkv, w_out, w_up, w_down = weights[1]
    mid, gain_two, g_up, g_down, hid = peak(size, replicas, h1, gains, grad_all, w_up, w_down)
    d_qkv, out_1, y1 = attend_backward(
        size, replicas, 1, mid, qkv, qm, km, ctx, lse, w_out, [], [hid, w_down, h1]
    )
    up_1, down_1 = reduce_rows(g_up), reduce_rows(g_down)
    dx1, gain_one, g_qkv = qkv_backward(size, replicas, 1, d_qkv, a1, x, mid, gains, w_qkv)
    gains_above = jnp.concatenate([gain_one, gain_two], axis=0)
    dx1, up_1, down_1 = lax.optimization_barrier((dx1, up_1, down_1))
    qkv_1 = reduce_rows(g_qkv)

    x, a1, qkv, ctx, lse, h1, a2, hid, slope = kept[0]
    w_qkv, w_out, w_up, w_down = weights[0]
    mid, gain_two, g_up, g_down, layer_out = mlp_backward(
        size, replicas, 0, dx1, h1, gains, a2, hid, slope, w_up, w_down, [y0, y1]
    )
    mid, qkv_1 = lax.optimization_barrier((mid, qkv_1))
    d_qkv, out_0, down_0 = attend_backward(
        size, replicas, 0, mid, qkv, qm, km, ctx, lse, w_out, [g_down]
    )
    up_0 = reduce_rows(g_up)
    d_qkv, up_0 = lax.optimization_barrier((d_qkv, up_0))
    gains, qkv_0, input_out = last_backward(
        size, replicas, d_qkv, a1, x, mid, gains, w_qkv, gain_two, gains_above, dx1
    )

    def finish(zero, one):
        send = swap_section(jnp.where(section == 0, one, zero))
        return jnp.where(section == 0, zero, one).astype(F32) + send.astype(F32)

    other_qkv_1 = swap_section(qkv_1)
    qkv_grad = jnp.where(section == 0, qkv_0, qkv_1.astype(F32) + other_qkv_1.astype(F32))
    out_grad = jnp.where(section == 0, out_0, out_1)
    up_grad = finish(up_0, up_1)
    other_down_1 = swap_section(down_1)
    down_grad = jnp.where(section == 0, down_0, down_1.astype(F32) + other_down_1.astype(F32))
    gains = lax.dynamic_slice_in_dim(gains, 2 * section, 2, 0)
    return (
        layer_out[None],
        input_out[None],
        gains[0:1],
        qkv_grad.reshape(qkv_weight.shape),
        out_grad.reshape(out_weight.shape),
        gains[1:2],
        up_grad[None],
        down_grad[None],
    )


def solution(mesh):
    return jax.shard_map(
        shards,
        mesh=mesh,
        in_specs=(
            P(None, ("dp", "tensor"), None),
            P(None, "dp"),
            P(None, ("dp", "tensor"), None),
            P("section", None),
            P("section", "dp", "tensor", None),
            P("section", "tensor", None, "dp"),
            P("section", None),
            P("section", "dp", "tensor"),
            P("section", "tensor", "dp"),
        ),
        out_specs=(
            P("section", None, ("dp", "tensor"), None),
            P("section", None, ("dp", "tensor"), None),
            P("section", None),
            P("section", "dp", "tensor", None),
            P("section", "tensor", None, "dp"),
            P("section", None),
            P("section", "dp", "tensor"),
            P("section", "tensor", "dp"),
        ),
        check_vma=False,
    )
```

```python
import functools
import math

import jax
import jax.numpy as jnp
from jax import lax
from jax.experimental import pallas as pl
from jax.experimental.pallas import tpu as pltpu
from jax.sharding import PartitionSpec as P

F32 = jnp.float32
BF = jnp.bfloat16
NT = (((1,), (1,)), ((), ()))
NN = (((1,), (0,)), ((), ()))
TN = (((0,), (0,)), ((), ()))
MASKED = -1e30
SCENES = 3
MESH = pl.DeviceIdType.MESH
VM = pl.BlockSpec(memory_space=pltpu.VMEM)
HB = pl.BlockSpec(memory_space=pl.ANY)
DMA = pltpu.SemaphoreType.DMA
LIMIT = 58 << 20


def dg(a, b, dims):
    return lax.dot_general(a, b, dims, preferred_element_type=F32)


def chunks(rows):
    return 4 if rows % 64 == 0 else 1


def thin_chunks(rows):
    return 8 if rows % 128 == 0 else chunks(rows)


def shape(dims, dtype):
    return jax.ShapeDtypeStruct(dims, dtype)


class Group:
    def __init__(self, size):
        self.size = size
        self.chips = size // 2
        self.me = lax.axis_index("tensor")
        self.chip = lax.div(self.me, 2)
        self.core = lax.rem(self.me, 2)
        self.sibling = self.chip * 2 + 1 - self.core

    def ahead(self, k):
        return lax.rem(self.chip + k, self.chips)

    def behind(self, k):
        return lax.rem(self.chip + self.chips - k, self.chips)

    def greet(self, replicas=0, side=False):
        barrier = pltpu.get_barrier_semaphore()
        targets = [self.sibling] + [self.ahead(k) * 2 + self.core for k in range(1, self.chips)]
        targets = [{"tensor": target} for target in targets]
        if replicas:
            d = lax.axis_index("dp")
            targets += [{"dp": lax.rem(d + k, replicas)} for k in range(1, replicas)]
        if replicas or side:
            targets += [{"section": 1 - lax.axis_index("section")}]
        for target in targets:
            pl.semaphore_signal(barrier, inc=1, device_id=target, device_id_type=MESH)
        pl.semaphore_wait(barrier, len(targets))


def remote(src, dst, send, recv, target):
    return pltpu.make_async_remote_copy(
        src_ref=src,
        dst_ref=dst,
        send_sem=send,
        recv_sem=recv,
        device_id={"tensor": target},
        device_id_type=MESH,
    )


def span(j, rc):
    return pl.ds(pl.multiple_of(j * rc, rc), rc)


def comm_sems(group_size, n):
    c = group_size // 2
    far, near = DMA((max(c - 1, 1), n)), DMA((c, n))
    return [far, far, near, near]


class Gather:
    def __init__(self, g, buf, rc, sems):
        self.g, self.buf, self.rc = g, buf, rc
        self.far_send, self.far_recv, self.near_send, self.near_recv = sems

    def far(self, k, j, origin, target, src=None):
        ref = self.buf.at[origin, span(j, self.rc)]
        src = ref if src is None else src
        return remote(src, ref, self.far_send.at[k - 1, j], self.far_recv.at[k - 1, j], target)

    def near(self, k, j, origin, src=None):
        ref = self.buf.at[origin, span(j, self.rc)]
        src = ref if src is None else src
        return remote(
            src, ref, self.near_send.at[k, j], self.near_recv.at[k, j], self.g.sibling
        )

    def start(self, j, src=None):
        g = self.g
        for k in range(1, g.chips):
            self.far(k, j, g.me, g.ahead(k) * 2 + g.core, src).start()
        self.near(0, j, g.me, src).start()

    def relay(self, j):
        g = self.g
        for k in range(1, g.chips):
            origin = g.behind(k) * 2 + g.core
            self.far(k, j, origin, g.me).wait_recv()
            self.near(k, j, origin).start()

    def ready(self, j):
        g = self.g
        self.near(0, j, g.sibling).wait_recv()
        for k in range(1, g.chips):
            self.near(k, j, g.behind(k) * 2 + 1 - g.core).wait_recv()

    def drain(self, n):
        g = self.g

        def one(j, _):
            for k in range(1, g.chips):
                self.far(k, j, g.me, g.sibling).wait_send()
            for k in range(g.chips):
                self.near(k, j, g.me).wait_send()
            return 0

        lax.fori_loop(0, n, one, 0)


def scatter_scratch(group_size, rows, width, n):
    c = group_size // 2
    far = pltpu.VMEM((max(c - 1, 1), rows, width), BF)
    near = pltpu.VMEM((c, rows, width), BF)
    return [pltpu.VMEM((group_size, rows, width), F32), near, near, far, far] + comm_sems(
        group_size, n
    )


class Scatter:
    def __init__(self, g, rc, scratch):
        self.g, self.rc = g, rc
        self.part, self.near_out, self.near_in, self.far_out, self.far_in = scratch[:5]
        self.far_send, self.far_recv, self.near_send, self.near_recv = scratch[5:]

    def near(self, k, j):
        rows = span(j, self.rc)
        return remote(
            self.near_out.at[k, rows],
            self.near_in.at[k, rows],
            self.near_send.at[k, j],
            self.near_recv.at[k, j],
            self.g.sibling,
        )

    def far(self, k, j):
        rows = span(j, self.rc)
        return remote(
            self.far_out.at[k - 1, rows],
            self.far_in.at[k - 1, rows],
            self.far_send.at[k - 1, j],
            self.far_recv.at[k - 1, j],
            self.g.ahead(k) * 2 + self.g.core,
        )

    def first(self, j):
        g, rows = self.g, span(j, self.rc)
        for k in list(range(1, g.chips)) + [0]:
            owner = g.ahead(k) * 2 + 1 - g.core
            self.near_out[k, rows, :] = self.part[owner, rows, :].astype(BF)
            self.near(k, j).start()

    def second(self, j):
        g, rows = self.g, span(j, self.rc)
        for k in range(1, g.chips):
            owner = g.ahead(k) * 2 + g.core
            self.near(k, j).wait_recv()
            both = self.part[owner, rows, :] + self.near_in[k, rows, :].astype(F32)
            self.far_out[k - 1, rows, :] = both.astype(BF)
            self.far(k, j).start()

    def third(self, j):
        g, rows = self.g, span(j, self.rc)
        self.near(0, j).wait_recv()
        total = self.part[g.me, rows, :] + self.near_in[0, rows, :].astype(F32)
        for k in range(1, g.chips):
            self.far(k, j).wait_recv()
            total = total + self.far_in[k - 1, rows, :].astype(F32)
        return total

    def drain(self, n):
        g = self.g

        def one(j, _):
            for k in range(1, g.chips):
                self.far(k, j).wait_send()
            for k in range(g.chips):
                self.near(k, j).wait_send()
            return 0

        lax.fori_loop(0, n, one, 0)


def far_copy(src, dst, send, recv, target):
    return pltpu.make_async_remote_copy(
        src_ref=src,
        dst_ref=dst,
        send_sem=send,
        recv_sem=recv,
        device_id=target,
        device_id_type=MESH,
    )


class Swap:
    def __init__(self, src, stage, sems):
        self.src, self.stage, self.sems = src, stage, sems
        self.s = lax.axis_index("section")

    def copies(self, layer):
        local = pltpu.make_async_copy(self.src.at[self.s], self.stage.at[self.s], self.sems.at[0])
        side = far_copy(
            self.src.at[1 - self.s],
            self.stage.at[layer],
            self.sems.at[1],
            self.sems.at[2],
            {"section": 1 - self.s},
        )
        return local, side

    def start(self):
        for copy in self.copies(self.s):
            copy.start()

    def arrive(self):
        local, side = self.copies(1 - self.s)
        local.wait()
        side.wait_recv()

    def finish(self):
        self.copies(self.s)[1].wait_send()


def reduce_scratch(replicas, rows, cols):
    many = pltpu.VMEM((replicas - 1, rows, cols), BF)
    one = pltpu.VMEM((rows, cols), BF)
    far, side = DMA((replicas - 1, 2)), DMA((2,))
    return [pltpu.VMEM((rows, cols), F32), many, many, one, one, far, far, side, side]


class Reduce:
    def __init__(self, layer, scratch):
        self.layer = layer
        self.own, self.away, self.came, self.over, self.back = scratch[:5]
        self.z_send, self.z_recv, self.y_send, self.y_recv = scratch[5:]
        self.replicas = self.away.shape[0] + 1
        self.half = self.own.shape[0] // 2
        self.d = lax.axis_index("dp")
        self.s = lax.axis_index("section")

    def target(self, k):
        return lax.rem(self.d + k, self.replicas)

    def part(self, i):
        return pl.ds(pl.multiple_of(i * self.half, self.half), self.half)

    def z_copy(self, k, i):
        part = self.part(i)
        return far_copy(
            self.away.at[k - 1, part],
            self.came.at[k - 1, part],
            self.z_send.at[k - 1, i],
            self.z_recv.at[k - 1, i],
            {"dp": self.target(k)},
        )

    def y_copy(self, i):
        part = self.part(i)
        return far_copy(
            self.over.at[part],
            self.back.at[part],
            self.y_send.at[i],
            self.y_recv.at[i],
            {"section": 1 - self.s},
        )

    def send(self, block):
        def one(i):
            k = i + 1
            self.away[i] = block(self.target(k)).astype(BF)
            self.z_copy(k, 0).start()
            self.z_copy(k, 1).start()

        run(self.replicas - 1, one)
        self.own[...] = block(self.d)

    def collect(self):
        def one(i):
            part = self.part(i)
            total = self.own[part, :]
            for k in range(1, self.replicas):
                self.z_copy(k, i).wait_recv()
                total = total + self.came[k - 1, part, :].astype(F32)
            self.own[part, :] = total
            self.over[part, :] = total.astype(BF)

            @pl.when(self.s != self.layer)
            def _():
                self.y_copy(i).start()

        run(2, one)

    def finish(self, out):
        @pl.when(self.s == self.layer)
        def _():
            self.y_copy(0).wait_recv()
            self.y_copy(1).wait_recv()
            out[...] = self.own[...] + self.back[...].astype(F32)

        @pl.when(self.s != self.layer)
        def _():
            self.y_copy(0).wait_send()
            self.y_copy(1).wait_send()
            out[...] = self.own[...]

        for k in range(1, self.replicas):
            self.z_copy(k, 0).wait_send()
            self.z_copy(k, 1).wait_send()


class HalfSwap:
    def __init__(self, src, came, sems):
        self.src, self.came, self.sems = src, came, sems
        self.s = lax.axis_index("section")
        self.rows = came.shape[1]

    def copy(self):
        at = pl.ds(pl.multiple_of((1 - self.s) * self.rows, self.rows), self.rows)
        return far_copy(
            self.src.at[:, at],
            self.came,
            self.sems.at[0],
            self.sems.at[1],
            {"section": 1 - self.s},
        )


def half_scratch(replicas, rows, cols):
    rows = rows // 2
    all_, far = pltpu.VMEM((replicas, rows, cols), BF), pltpu.VMEM((replicas - 1, rows, cols), BF)
    one = pltpu.VMEM((rows, cols), BF)
    z = DMA((replicas - 1,))
    return [all_, all_, far, far, pltpu.VMEM((rows, cols), F32), one, one, DMA((3,)), z, z, DMA((2,))]


HALF = 11


class HalfReduce:
    def __init__(self, layer, scratch):
        self.layer = layer
        self.mine, self.other, self.away, self.came, self.own, self.over, self.back = scratch[:7]
        self.in_sem, self.z_send, self.z_recv, self.y_sem = scratch[7:]
        self.replicas, self.rows = self.mine.shape[:2]
        self.s = lax.axis_index("section")
        self.d = lax.axis_index("dp")

    def half(self, s):
        return pl.ds(pl.multiple_of(s * self.rows, self.rows), self.rows)

    def loads(self, src, other):
        loads = [pltpu.make_async_copy(src.at[:, self.half(self.s)], self.mine, self.in_sem.at[0])]
        if other is not None:
            loads.append(pltpu.make_async_copy(other, self.other, self.in_sem.at[1]))
        return loads

    def z_copy(self, k):
        return far_copy(
            self.away.at[k - 1],
            self.came.at[k - 1],
            self.z_send.at[k - 1],
            self.z_recv.at[k - 1],
            {"dp": lax.rem(self.d + k, self.replicas)},
        )

    def y_copy(self):
        return far_copy(
            self.over, self.back, self.y_sem.at[0], self.y_sem.at[1], {"section": 1 - self.s}
        )

    def middle(self):
        def both(z):
            return self.mine[z].astype(F32) + self.other[z].astype(F32)

        for k in range(1, self.replicas):
            self.away[k - 1] = both(lax.rem(self.d + k, self.replicas)).astype(BF)
            self.z_copy(k).start()
        self.own[...] = both(self.d)

    def late(self):
        total = self.own[...]
        for k in range(1, self.replicas):
            self.z_copy(k).wait_recv()
            total = total + self.came[k - 1].astype(F32)
        self.own[...] = total
        self.over[...] = total.astype(BF)

        @pl.when(self.s != self.layer)
        def _():
            self.y_copy().start()

    def finish(self, out, above=None):
        @pl.when(self.s == self.layer)
        def _():
            self.y_copy().wait_recv()
            out[self.half(self.s), :] = self.own[...]
            out[self.half(1 - self.s), :] = self.back[...].astype(F32)

        @pl.when(self.s != self.layer)
        def _():
            if above is None:
                out[...] = jnp.zeros_like(out)
            else:
                copy = pltpu.make_async_copy(above, out, self.in_sem.at[2])
                copy.start()
                copy.wait()
            self.y_copy().wait_send()

        for k in range(1, self.replicas):
            self.z_copy(k).wait_send()


class Spread:
    def __init__(self, src, dst, by_columns, sems):
        self.src, self.dst, self.by_columns = src, dst, by_columns
        self.own_sem, self.far_send, self.far_recv, self.side_send, self.side_recv = sems
        self.replicas = far = self.side_send.shape[0]
        self.s = lax.axis_index("section")
        self.d = lax.axis_index("dp")
        self.stages = [
            sorted({k, far - k}) for k in range(1, far // 2 + 1)
        ]

    def place(self, half, z):
        rows, cols = self.src.shape
        if self.by_columns:
            return self.dst.at[
                pl.ds(pl.multiple_of(half * rows, rows), rows),
                pl.ds(pl.multiple_of(z * cols, cols), cols),
            ]
        return self.dst.at[pl.ds(pl.multiple_of((2 * z + half) * rows, rows), rows)]

    def origin(self, k):
        return lax.rem(self.d + self.replicas - k, self.replicas)

    def own(self):
        return pltpu.make_async_copy(self.src, self.place(self.s, self.d), self.own_sem.at[0])

    def far(self, k, origin):
        return pltpu.make_async_remote_copy(
            src_ref=self.src,
            dst_ref=self.place(self.s, origin),
            send_sem=self.far_send.at[k - 1],
            recv_sem=self.far_recv.at[k - 1],
            device_id={"dp": lax.rem(self.d + k, self.replicas)},
            device_id_type=MESH,
        )

    def side(self, k, half):
        place = self.place(half, self.origin(k))
        return pltpu.make_async_remote_copy(
            src_ref=self.src if k == 0 else place,
            dst_ref=place,
            send_sem=self.side_send.at[k],
            recv_sem=self.side_recv.at[k],
            device_id={"section": 1 - self.s},
            device_id_type=MESH,
        )

    def start(self):
        for k in self.stages[0]:
            self.far(k, self.d).start()
        self.side(0, self.s).start()
        self.own().start()

    def step(self, i):
        for k in self.stages[i]:
            self.far(k, self.origin(k)).wait_recv()
            self.side(k, self.s).start()
        if i + 1 < len(self.stages):
            for k in self.stages[i + 1]:
                self.far(k, self.d).start()

    def finish(self):
        self.own().wait()
        for k in range(self.replicas):
            self.side(k, 1 - self.s).wait_recv()
        for k in range(1, self.replicas):
            self.far(k, self.d).wait_send()
        for k in range(self.replicas):
            self.side(k, self.s).wait_send()


class ZGather:
    def __init__(self, src, got, sems):
        self.src, self.got = src, got
        self.own_sem, self.send, self.recv = sems
        self.replicas = got.shape[0]
        self.d = lax.axis_index("dp")

    def own(self):
        return pltpu.make_async_copy(self.src, self.got.at[self.d], self.own_sem.at[0])

    def far(self, k, origin):
        return far_copy(
            self.src,
            self.got.at[origin],
            self.send.at[k - 1],
            self.recv.at[k - 1],
            {"dp": lax.rem(self.d + k, self.replicas)},
        )

    def start(self):
        for k in range(1, self.replicas):
            self.far(k, self.d).start()
        self.own().start()

    def step(self, i):
        pass

    def finish(self):
        self.own().wait()
        for k in range(1, self.replicas):
            self.far(k, lax.rem(self.d + self.replicas - k, self.replicas)).wait_recv()
        for k in range(1, self.replicas):
            self.far(k, self.d).wait_send()


class YJoin:
    def __init__(self, got, dst, by_columns, sems):
        self.src, self.dst, self.by_columns = got, dst, by_columns
        self.own_sem, self.send, self.recv, self.got, self.in_sem = sems
        self.replicas, self.rows, self.cols = got.shape
        self.s = lax.axis_index("section")

    def place(self, half, z):
        rows, cols = self.rows, self.cols
        if self.by_columns:
            return self.dst.at[
                pl.ds(pl.multiple_of(half * rows, rows), rows), pl.ds(z * cols, cols)
            ]
        return self.dst.at[pl.ds(pl.multiple_of((2 * z + half) * rows, rows), rows)]

    def own(self, z):
        return pltpu.make_async_copy(self.got.at[z], self.place(self.s, z), self.own_sem.at[z])

    def side(self, z, half):
        return far_copy(
            self.got.at[z],
            self.place(half, z),
            self.send.at[z],
            self.recv.at[z],
            {"section": 1 - self.s},
        )

    def start(self):
        load = pltpu.make_async_copy(self.src, self.got, self.in_sem.at[0])
        load.start()
        load.wait()
        for z in range(self.replicas):
            self.side(z, self.s).start()
            self.own(z).start()

    def step(self, i):
        pass

    def finish(self):
        for z in range(self.replicas):
            self.own(z).wait()
            self.side(z, 1 - self.s).wait_recv()
        for z in range(self.replicas):
            self.side(z, self.s).wait_send()


def rider_sems(replicas):
    far, side = DMA((replicas - 1,)), DMA((replicas,))
    return [DMA((1,)), far, far, side, side]


class Riders:
    def __init__(self, srcs, dsts, columns, sems):
        self.all = []
        for src, dst, (kind, layer, by) in zip(srcs, dsts, columns):
            count = 3 if kind == "z" else 5
            own, sems = sems[:count], sems[count:]
            if kind == "spread":
                self.all.append(Spread(src.at[layer], dst, by, own))
            elif kind == "z":
                self.all.append(ZGather(src.at[layer], dst, own))
            else:
                self.all.append(YJoin(src, dst, by, own))
        self.replicas = self.all[0].replicas if self.all else 0

    def start(self):
        for one in self.all[:1]:
            one.start()

    def step(self, j, n):
        if not self.all:
            return
        stages = self.replicas // 2
        turns = len(self.all) * stages
        for turn in range(turns):

            @pl.when(j == max(n * (turn + 1) // turns - 1, 0))
            def _(turn=turn):
                self.all[turn // stages].step(turn % stages)
                if (turn + 1) % stages == 0 and turn + 1 < turns:
                    self.all[turn // stages + 1].start()

    def finish(self):
        for one in self.all:
            one.finish()


def riding(riders, replicas):
    arrays = [array for array, _, _, _ in riders]
    columns = tuple(rider[1:] for rider in riders)
    outs, sems = [], []
    for array, kind, _, by in riders:
        rows, cols = array.shape[1:]
        if kind == "z":
            outs.append(shape((replicas, rows, cols), BF))
        else:
            outs.append(
                shape((2 * rows, replicas * cols) if by else (2 * replicas * rows, cols), BF)
            )
        far, side = DMA((replicas - 1,)), DMA((replicas,))
        sems += {
            "spread": rider_sems(replicas),
            "z": [DMA((1,)), far, far],
            "y": [side, side, side, pltpu.VMEM(array.shape, BF), DMA((1,))],
        }[kind]
    return arrays, columns, outs, sems


def params(key):
    return pltpu.CompilerParams(
        vmem_limit_bytes=LIMIT, collective_id=key, has_side_effects=True
    )


def cost(flops, moved, exps=0):
    return pl.CostEstimate(flops=int(flops), bytes_accessed=int(moved), transcendentals=int(exps))


def normed(source):
    center = source - jnp.mean(source, axis=-1, keepdims=True)
    r = lax.rsqrt(jnp.mean(center * center, axis=-1, keepdims=True) + 1e-05)
    return center * r, r


def normed_back(source, gain, grad):
    n, r = normed(source)
    e = grad * gain
    dh = r * (
        e - jnp.mean(e, axis=-1, keepdims=True) - n * jnp.mean(e * n, axis=-1, keepdims=True)
    )
    return dh, jnp.sum(grad * n, axis=0, keepdims=True)


def flat(value):
    return value.reshape((value.shape[0] * value.shape[1],) + value.shape[2:])


def run(n, body):
    def one(j, carry):
        body(j)
        return carry

    lax.fori_loop(0, n, one, 0)


def first_kernel(
    size, replicas, x_ref, gain_ref, wq_ref, wo_ref, wu_ref, wd_ref,
    qkv_ref, gains_out, a1_out, wq_out, wo_out, q_stage, o_stage, u_stage, d_stage,
    a1, w, gains, own_sem, q_sem, o_sem, u_sem, d_sem, gain_sem, *sems
):
    rows, width = x_ref.shape
    n = thin_chunks(rows)
    rc = rows // n
    g = Group(size)
    section = lax.axis_index("section")
    gather = Gather(g, a1, rc, sems[:4])
    swaps = [
        Swap(wq_ref, q_stage, q_sem),
        Swap(wo_ref, o_stage, o_sem),
        Swap(wu_ref, u_stage, u_sem),
        Swap(wd_ref, d_stage, d_sem),
    ]
    spreads = [
        Spread(q_stage.at[0], w, False, sems[4:9]),
        Spread(o_stage.at[0], wo_out, True, sems[9:14]),
    ]
    g.greet(replicas)

    def gain_copy(layer):
        return far_copy(
            gain_ref, gains.at[layer], gain_sem.at[0], gain_sem.at[1], {"section": 1 - section}
        )

    gain_copy(section).start()
    swaps[0].start()
    swaps[1].start()
    gains[section] = gain_ref[...]
    gain_copy(1 - section).wait_recv()
    gains_out[...] = gains[...]

    def send(j):
        at = span(j, rc)
        a = normed(x_ref[at, :].astype(F32))[0] * gains[0, 0:1, :]
        a1[g.me, at, :] = a.astype(BF)
        gather.start(j)

    run(n, send)
    swaps[0].arrive()
    swaps[1].arrive()
    for one in spreads:
        one.start()
    stages = len(spreads[0].stages)

    def relay(j):
        gather.relay(j)

        for i in range(stages):

            @pl.when(j == n * (i + 1) // stages - 1)
            def _(i=i):
                for one in spreads:
                    one.step(i)

    run(n, relay)
    swaps[2].start()
    swaps[3].start()
    for one in spreads:
        one.finish()
    outs = [
        pltpu.make_async_copy(w, wq_out, own_sem.at[0]),
        pltpu.make_async_copy(a1, a1_out, own_sem.at[1]),
    ]
    outs[0].start()

    def multiply(j):
        at = span(j, rc)
        gather.ready(j)
        r = dg(flat(a1[:, at, :]), w[...], NN).astype(BF)
        qkv_ref[:, at, :] = r.reshape(size, rc, r.shape[1])

    run(n, multiply)
    outs[1].start()
    swaps[2].arrive()
    swaps[3].arrive()
    for swap in swaps:
        swap.finish()
    gain_copy(section).wait_send()
    gather.drain(n)
    for out in outs:
        out.wait()


def first_forward(size, replicas, x, gains, ws):
    rows, width = x.shape
    wide = ws[0].shape[2]
    deep = 2 * ws[1].shape[1]
    n = thin_chunks(rows)
    return pl.pallas_call(
        functools.partial(first_kernel, size, replicas),
        out_shape=[
            shape((size, rows, wide), BF),
            shape((2,) + gains.shape, F32),
            shape((size, rows, width), BF),
            shape((width, wide), BF),
            shape((deep, width), BF),
        ]
        + [shape(w.shape, BF) for w in ws],
        in_specs=[VM] * 6,
        out_specs=[VM, VM] + [HB] * 7,
        scratch_shapes=[
            pltpu.VMEM((size, rows, width), BF),
            pltpu.VMEM((width, wide), BF),
            pltpu.VMEM((2,) + gains.shape, F32),
            DMA((2,)),
            DMA((3,)),
            DMA((3,)),
            DMA((3,)),
            DMA((3,)),
            DMA((2,)),
        ]
        + comm_sems(size, n)
        + rider_sems(replicas) * 2,
        compiler_params=params(0),
        cost_estimate=cost(30e9, 30e6),
    )(x, gains, *ws)


def attend_kernel(size, layer, columns, *refs):
    m = len(columns)
    qkv_ref, qm_ref, km_ref, x_ref, w_ref = refs[:5]
    refs = refs[5:]
    if layer == 1:
        cot_ref, refs = refs[0], refs[1:]
    halves, refs = refs[:m], refs[m:]
    h1_ref, ctx_ref, lse_ref = refs[:3]
    refs = refs[3:]
    if layer == 1:
        cot_out, refs = refs[0], refs[1:]
    wholes, refs = refs[:m], refs[m:]
    ka, vt, w, w_sem = refs[:4]
    scratch, refs = refs[4:13], refs[13:]
    if layer == 1:
        cot_sems, cot_sem, refs = refs[:4], refs[4], refs[5:]
    riders = Riders(halves, wholes, columns, refs)
    _, rows, wide = qkv_ref.shape
    length = size * rows
    e = qm_ref.shape[2]
    heads = wide // (3 * e)
    c = e**-0.5 * math.log2(math.e)
    n = chunks(rows)
    rc = rows // n
    bq = size * rc
    kc = bq
    g = Group(size)
    copy = pltpu.make_async_copy(w_ref, w, w_sem.at[0])
    copy.start()
    g.greet(riders.replicas)
    riders.start()
    if layer == 1:
        cot = Gather(g, cot_out, rows, cot_sems)
        own = pltpu.make_async_copy(cot_ref, cot_out.at[g.me], cot_sem.at[0])
        own.start()
        cot.start(0, cot_ref)
    scatter = Scatter(g, rc, scratch)
    whole = flat(qkv_ref[...])
    for h in range(heads):
        o = 3 * e * h
        ka[h, :, :e] = whole[:, o + e : o + 2 * e]
        ka[h, :, e:] = flat(km_ref[...])
        vt[h, :e, :] = whole[:, o + 2 * e : o + 3 * e].T
        vt[h, e:, :] = jnp.ones((16, length), BF)
    copy.wait()

    def work(j):
        at = span(j, rc)
        qm = flat(qm_ref[:, at, :])
        found = []
        held_qkv = flat(qkv_ref[:, at, :])
        for h in range(heads):
            o = 3 * e * h
            q = jnp.concatenate([held_qkv[:, o : o + e], qm], axis=1)
            held = []
            top = None
            for k in range(length // kc):
                s = dg(ka[h, k * kc : (k + 1) * kc, :], q, NT)
                t = jnp.max(s, axis=0, keepdims=True)
                top = t if top is None else jnp.maximum(top, t)
                held.append(s)
            top = top * c
            acc = None
            for k in range(length // kc):
                p = jnp.exp2(held[k] * c - top).astype(BF)
                a = dg(vt[h, :, k * kc : (k + 1) * kc], p, NN)
                acc = a if acc is None else acc + a
            total = acc[e : e + 1]
            found.append((acc[:e] * (1.0 / total)).astype(BF))
            lse_ref[j, h : h + 1, :] = top + jnp.log2(total)
            if h == heads // 2:

                @pl.when(j > 0)
                def _():
                    scatter.second(j - 1)

        ctx = (jnp.concatenate(found, axis=0) if heads > 1 else found[0]).T
        ctx_ref[:, at, :] = ctx.reshape(size, rc, heads * e)
        width = x_ref.shape[1]
        scatter.part[:, at, :] = dg(ctx, w[...], NN).reshape(size, rc, width)
        scatter.first(j)
        riders.step(j, n)
        if layer == 1:

            @pl.when(j == n - 1)
            def _():
                cot.relay(0)

    run(n, work)
    scatter.second(n - 1)

    def last(j):
        at = span(j, rc)
        h1_ref[at, :] = x_ref[at, :].astype(F32) + scatter.third(j)

    run(n, last)
    scatter.drain(n)
    if layer == 1:
        cot.ready(0)
        cot.drain(1)
        own.wait()
    riders.finish()


def attend(size, replicas, layer, qkv, qm, km, x, w, riders, cot=()):
    _, rows, wide = qkv.shape
    e = qm.shape[2]
    heads = wide // (3 * e)
    width = x.shape[1]
    n = chunks(rows)
    halves, columns, outs, sems = riding(riders, replicas)
    return pl.pallas_call(
        functools.partial(attend_kernel, size, layer, columns),
        out_shape=[
            shape((rows, width), F32),
            shape((size, rows, heads * e), BF),
            shape((n, heads, size * rows // n), F32),
        ]
        + [shape((size, rows, width), BF) for _ in cot]
        + outs,
        in_specs=[VM, VM, VM, VM, HB] + [VM] * len(cot) + [HB] * len(riders),
        out_specs=[VM, VM, VM] + [HB] * (len(cot) + len(outs)),
        scratch_shapes=[
            pltpu.VMEM((heads, size * rows, 2 * e), BF),
            pltpu.VMEM((heads, e + 16, size * rows), BF),
            pltpu.VMEM((heads * e, width), BF),
            DMA((1,)),
        ]
        + scatter_scratch(size, rows, width, n)
        + (comm_sems(size, 1) + [DMA((1,))]) * len(cot)
        + sems,
        compiler_params=params(2 + layer),
        cost_estimate=cost(60e9, 20e6),
    )(qkv, qm, km, x, w, *cot, *halves)


def peak_kernel(
    size, parts, h1_ref, gain_ref, grad_ref, wu_ref, wd_ref,
    mid_ref, gain_out, gup_ref, gdown_ref, hid_out,
    a2, hid, dup, grad, wu, wd, w_sem, out_sem, *scratch
):
    rows, width = h1_ref.shape
    hidden = wu_ref.shape[1]
    depth = width // parts
    fb = min(256, hidden)
    n = chunks(rows)
    rc = rows // n
    g = Group(size)
    copies = [
        pltpu.make_async_copy(wu_ref, wu, w_sem.at[0]),
        pltpu.make_async_copy(wd_ref, wd, w_sem.at[1]),
        pltpu.make_async_copy(grad_ref, grad, w_sem.at[2]),
    ]
    for copy in copies:
        copy.start()
    g.greet()
    gather = Gather(g, a2, rc, scratch[:4])
    scatter = Scatter(g, rc, scratch[4:])

    def send(j):
        at = span(j, rc)
        a = normed(h1_ref[at, :])[0] * gain_ref[1, 1:2, :]
        a2[g.me, at, :] = a.astype(BF)
        gather.start(j)

    run(n, send)
    for copy in copies:
        copy.wait()
    gather.relay(0)

    def work(j):
        at = span(j, rc)
        gather.ready(j)
        a = flat(a2[:, at, :])
        held = flat(grad[:, at, :])
        for f in range(hidden // fb):
            cols = slice(f * fb, (f + 1) * fb)
            u = dg(a, wu[:, cols], NN)
            half = 0.5 + 0.5 * lax.erf(u * (0.5**0.5))
            slope = half + u * jnp.exp(-0.5 * u * u) * ((2 * math.pi) ** -0.5)
            hid[:, at, cols] = (u * half).astype(BF).reshape(size, rc, fb)
            d = dg(held, wd[cols, :], NT) * slope
            dup[:, at, cols] = d.astype(BF).reshape(size, rc, fb)

        @pl.when(j + 1 < n)
        def _():
            gather.relay(j + 1)

        @pl.when(j > 0)
        def _():
            scatter.second(j - 1)

        held = flat(dup[:, at, :])
        for z in range(parts):
            cols = slice(z * depth, (z + 1) * depth)
            scatter.part[:, at, cols] = dg(held, wu[cols, :], NT).reshape(size, rc, depth)
        scatter.first(j)

    run(n, work)
    scatter.second(n - 1)
    out = pltpu.make_async_copy(hid, hid_out, out_sem.at[0])
    out.start()

    def up_grad(z):
        cols = pl.ds(pl.multiple_of(z * depth, depth), depth)
        gup_ref[z] = dg(flat(a2[:, :, cols]), flat(dup[...]), TN).astype(BF)

    run(parts, up_grad)

    def down_grad(f):
        cols = pl.ds(pl.multiple_of(f * fb, fb), fb)
        r = dg(flat(hid[:, :, cols]), flat(grad[...]), TN).astype(BF)
        for z in range(parts):
            gdown_ref[z, cols, :] = r[:, z * depth : (z + 1) * depth]

    run(hidden // fb, down_grad)
    gain_out[...] = jnp.zeros_like(gain_out)

    def last(j):
        at = span(j, rc)
        dh, dgain = normed_back(h1_ref[at, :], gain_ref[1, 1:2, :], scatter.third(j))
        mid_ref[at, :] = grad[g.me, at, :].astype(F32) + dh
        gain_out[...] += dgain

    run(n, last)
    gather.drain(n)
    scatter.drain(n)
    out.wait()


def peak(size, replicas, h1, gains, grad_all, wu, wd):
    rows, width = h1.shape
    hidden = wu.shape[1]
    depth = width // replicas
    n = chunks(rows)
    return pl.pallas_call(
        functools.partial(peak_kernel, size, replicas),
        out_shape=[
            shape((rows, width), F32),
            shape((1, width), F32),
            shape((replicas, depth, hidden), BF),
            shape((replicas, hidden, depth), BF),
            shape((size, rows, hidden), BF),
        ],
        in_specs=[VM, VM, HB, HB, HB],
        out_specs=[VM, VM, VM, VM, HB],
        scratch_shapes=[
            pltpu.VMEM((size, rows, width), BF),
            pltpu.VMEM((size, rows, hidden), BF),
            pltpu.VMEM((size, rows, hidden), BF),
            pltpu.VMEM((size, rows, width), BF),
            pltpu.VMEM((width, hidden), BF),
            pltpu.VMEM((hidden, width), BF),
            DMA((3,)),
            DMA((1,)),
        ]
        + comm_sems(size, n)
        + scatter_scratch(size, rows, width, n),
        compiler_params=params(5),
        cost_estimate=cost(60e9, 30e6),
    )(h1, gains, grad_all, wu, wd)


def turn_kernel(size, columns, *refs):
    m = len(columns)
    h1_ref, gain_ref, wu_ref, wd_ref, q_stage = refs[:5]
    halves, refs = refs[5 : 5 + m], refs[5 + m :]
    y_ref, qkv_ref, a2_out, hid_out, slope_out, a1_out, wq_out = refs[:7]
    wholes, refs = refs[7 : 7 + m], refs[7 + m :]
    a2, hid, slope, wu, wd, a1, wq, w_sem, out_sem = refs[:9]
    gather_sems, next_sems, refs = refs[9:13], refs[13:17], refs[17:]
    scratch, refs = refs[:9], refs[9:]
    spread = Spread(q_stage.at[1], wq, False, refs[:5])
    riders = Riders(halves, wholes, columns, refs[5:])
    out_rider, up_rider = riders.all
    stages = len(spread.stages)
    rows, width = h1_ref.shape
    hidden = wu_ref.shape[1]
    fb = min(256, hidden)
    n = chunks(rows)
    rc = rows // n
    g = Group(size)
    copies = [
        pltpu.make_async_copy(wu_ref, wu, w_sem.at[0]),
        pltpu.make_async_copy(wd_ref, wd, w_sem.at[1]),
    ]
    for copy in copies:
        copy.start()
    g.greet(spread.replicas)
    gather = Gather(g, a2, rc, gather_sems)
    onward = Gather(g, a1, rc, next_sems)
    scatter = Scatter(g, rc, scratch)

    def send(j):
        at = span(j, rc)
        a = normed(h1_ref[at, :])[0] * gain_ref[0, 1:2, :]
        a2[g.me, at, :] = a.astype(BF)
        gather.start(j)

    run(n, send)
    spread.start()
    out_rider.start()
    for copy in copies:
        copy.wait()

    def pass_on(j):
        at = span(j, rc)
        y = (h1_ref[at, :] + scatter.third(j)).astype(BF)
        y_ref[at, :] = y
        a = normed(y.astype(F32))[0] * gain_ref[1, 0:1, :]
        a1[g.me, at, :] = a.astype(BF)
        onward.start(j)

    lag = min(2, n)
    gather.relay(0)

    def work(j):
        at = span(j, rc)
        gather.ready(j)
        a = flat(a2[:, at, :])
        for f in range(hidden // fb):
            cols = slice(f * fb, (f + 1) * fb)
            u = dg(a, wu[:, cols], NN)
            half = 0.5 + 0.5 * lax.erf(u * (0.5**0.5))
            slope[:, at, cols] = (
                (half + u * jnp.exp(-0.5 * u * u) * ((2 * math.pi) ** -0.5))
                .astype(BF)
                .reshape(size, rc, fb)
            )
            hid[:, at, cols] = (u * half).astype(BF).reshape(size, rc, fb)

        @pl.when(j + 1 < n)
        def _():
            gather.relay(j + 1)

        @pl.when(j > 0)
        def _():
            scatter.second(j - 1)

        held = flat(hid[:, at, :])
        for f in range(width // 256):
            cols = slice(f * 256, (f + 1) * 256)
            scatter.part[:, at, cols] = dg(held, wd[:, cols], NN).reshape(size, rc, 256)
        scatter.first(j)

        @pl.when(j >= lag)
        def _():
            pass_on(j - lag)

        @pl.when(j == min(1, n - 1))
        def _():
            spread.step(0)
            out_rider.step(0)

        @pl.when(j == n - 1)
        def _():
            for i in range(1, stages):
                spread.step(i)
                out_rider.step(i)
            up_rider.start()

    run(n, work)
    scatter.second(n - 1)
    outs = [
        pltpu.make_async_copy(a2, a2_out, out_sem.at[0]),
        pltpu.make_async_copy(hid, hid_out, out_sem.at[1]),
        pltpu.make_async_copy(slope, slope_out, out_sem.at[2]),
    ]
    for out in outs:
        out.start()
    for j in range(n - lag, n):
        pass_on(j)
    up_rider.step(0)
    spread.finish()
    outs.append(pltpu.make_async_copy(wq, wq_out, out_sem.at[3]))
    outs[3].start()

    onward.relay(0)

    def multiply(j):
        at = span(j, rc)

        @pl.when(j + 1 < n)
        def _():
            onward.relay(j + 1)

        @pl.when(j == n // 2)
        def _():
            for i in range(1, stages):
                up_rider.step(i)

        onward.ready(j)
        r = dg(flat(a1[:, at, :]), wq[...], NN).astype(BF)
        qkv_ref[:, at, :] = r.reshape(size, rc, r.shape[1])

    run(n, multiply)
    outs.append(pltpu.make_async_copy(a1, a1_out, out_sem.at[4]))
    outs[4].start()
    riders.finish()
    gather.drain(n)
    onward.drain(n)
    scatter.drain(n)
    for out in outs:
        out.wait()


def turn_forward(size, replicas, h1, gains, wu, wd, stage, riders):
    rows, width = h1.shape
    hidden = wu.shape[1]
    wide = stage.shape[2]
    n = chunks(rows)
    halves, columns, outs, sems = riding(riders, replicas)
    return pl.pallas_call(
        functools.partial(turn_kernel, size, columns),
        out_shape=[
            shape((rows, width), BF),
            shape((size, rows, wide), BF),
            shape((size, rows, width), BF),
            shape((size, rows, hidden), BF),
            shape((size, rows, hidden), BF),
            shape((size, rows, width), BF),
            shape((width, wide), BF),
        ]
        + outs,
        in_specs=[VM, VM] + [HB] * (3 + len(riders)),
        out_specs=[VM, VM] + [HB] * (5 + len(outs)),
        scratch_shapes=[
            pltpu.VMEM((size, rows, width), BF),
            pltpu.VMEM((size, rows, hidden), BF),
            pltpu.VMEM((size, rows, hidden), BF),
            pltpu.VMEM((width, hidden), BF),
            pltpu.VMEM((hidden, width), BF),
            pltpu.VMEM((size, rows, width), BF),
            pltpu.VMEM((width, wide), BF),
            DMA((2,)),
            DMA((5,)),
        ]
        + comm_sems(size, n) * 2
        + scatter_scratch(size, rows, width, n)
        + rider_sems(replicas)
        + sems,
        compiler_params=params(4),
        cost_estimate=cost(50e9, 30e6),
    )(h1, gains, wu, wd, stage, *halves)


def mlp_back_kernel(size, layer, parts, *refs):
    g_ref, h1_ref, gain_ref, a2_ref, hid_ref, slope_ref, wu_ref, wd_ref = refs[:8]
    refs = refs[8:]
    ys, refs = refs[:2], refs[2:]
    mid_ref, gain_out, gup_ref, gdown_ref = refs[:4]
    refs = refs[4:]
    y_out, refs = refs[0], refs[1:]
    grad, a2, hid, dup, wu, wd, w_sem = refs[:7]
    scratch, refs = refs[7:20], refs[20:]
    rows, width = h1_ref.shape
    hidden = wu_ref.shape[1]
    depth = width // parts
    fb = min(256, hidden)
    n = chunks(rows)
    rc = rows // n
    g = Group(size)
    copies = [
        pltpu.make_async_copy(wd_ref, wd, w_sem.at[0]),
        pltpu.make_async_copy(slope_ref, dup, w_sem.at[1]),
        pltpu.make_async_copy(wu_ref, wu, w_sem.at[2]),
    ]
    late = [
        pltpu.make_async_copy(hid_ref, hid, w_sem.at[3]),
        pltpu.make_async_copy(a2_ref, a2, w_sem.at[4]),
    ]
    for copy in copies:
        copy.start()
    g.greet(side=True)
    section = lax.axis_index("section")
    y_sem, y_own = refs

    def y_load(own):
        return pltpu.make_async_copy(own, y_own, y_sem.at[3])

    def y_copies(own, other, at):
        return (
            pltpu.make_async_copy(y_own, y_out.at[section], y_sem.at[0]),
            far_copy(
                other, y_out.at[at], y_sem.at[1], y_sem.at[2], {"section": 1 - section}
            ),
        )

    for i in range(2):

        @pl.when(section == i)
        def _(i=i):
            y_load(ys[i]).start()
            y_copies(ys[i], ys[1 - i], section)[1].start()

    gather = Gather(g, grad, rc, scratch[:4])
    scatter = Scatter(g, rc, scratch[4:])

    def send(j):
        at = span(j, rc)
        grad[g.me, at, :] = g_ref[at, :]
        gather.start(j)

    run(n, send)
    for copy in copies:
        copy.wait()
    for copy in late:
        copy.start()
    y_load(ys[0]).wait()
    y_copies(ys[0], ys[1], section)[0].start()

    gather.relay(0)

    def work(j):
        at = span(j, rc)
        gather.ready(j)
        held = flat(grad[:, at, :])
        for f in range(hidden // fb):
            cols = slice(f * fb, (f + 1) * fb)
            d = dg(held, wd[cols, :], NT) * flat(dup[:, at, cols]).astype(F32)
            dup[:, at, cols] = d.astype(BF).reshape(size, rc, fb)

        @pl.when(j + 1 < n)
        def _():
            gather.relay(j + 1)

        @pl.when(j > 0)
        def _():
            scatter.second(j - 1)

        held = flat(dup[:, at, :])
        for z in range(parts):
            cols = slice(z * depth, (z + 1) * depth)
            scatter.part[:, at, cols] = dg(held, wu[cols, :], NT).reshape(size, rc, depth)
        scatter.first(j)

    run(n, work)
    scatter.second(n - 1)
    for copy in late:
        copy.wait()

    def up_grad(z):
        cols = pl.ds(pl.multiple_of(z * depth, depth), depth)
        gup_ref[z] = dg(flat(a2[:, :, cols]), flat(dup[...]), TN).astype(BF)

    run(parts, up_grad)

    def down_grad(f):
        cols = pl.ds(pl.multiple_of(f * fb, fb), fb)
        r = dg(flat(hid[:, :, cols]), flat(grad[...]), TN).astype(BF)
        for z in range(parts):
            gdown_ref[z, cols, :] = r[:, z * depth : (z + 1) * depth]

    run(hidden // fb, down_grad)
    gain_out[...] = jnp.zeros_like(gain_out)

    def last(j):
        at = span(j, rc)
        dh, dgain = normed_back(h1_ref[at, :], gain_ref[layer, 1:2, :], scatter.third(j))
        mid_ref[at, :] = g_ref[at, :].astype(F32) + dh
        gain_out[...] += dgain

    run(n, last)
    local, side = y_copies(ys[0], ys[1], 1 - section)
    local.wait()
    side.wait_recv()
    y_copies(ys[0], ys[1], section)[1].wait_send()
    gather.drain(n)
    scatter.drain(n)


def mlp_backward(size, replicas, layer, grad, h1, gains, a2, hid, slope, wu, wd, extra):
    rows, width = h1.shape
    hidden = wu.shape[1]
    parts, depth = replicas, width // replicas
    n = chunks(rows)
    return pl.pallas_call(
        functools.partial(mlp_back_kernel, size, layer, parts),
        out_shape=[
            shape((rows, width), F32),
            shape((1, width), F32),
            shape((parts, depth, hidden), BF),
            shape((parts, hidden, depth), BF),
        ]
        + [shape((2, rows, width), BF)] * (len(extra) // 2),
        in_specs=[VM, VM, VM] + [HB] * (5 + len(extra)),
        out_specs=[VM, VM, VM, VM] + [HB] * (len(extra) // 2),
        scratch_shapes=[
            pltpu.VMEM((size, rows, width), BF),
            pltpu.VMEM((size, rows, width), BF),
            pltpu.VMEM((size, rows, hidden), BF),
            pltpu.VMEM((size, rows, hidden), BF),
            pltpu.VMEM((width, hidden), BF),
            pltpu.VMEM((hidden, width), BF),
            DMA((6,)),
        ]
        + comm_sems(size, n)
        + scatter_scratch(size, rows, width, n)
        + [DMA((4,)), pltpu.VMEM((rows, width), BF)] * (len(extra) // 2),
        compiler_params=params(6 + layer),
        cost_estimate=cost(60e9, 40e6),
    )(grad, h1, gains, a2, hid, slope, wu, wd, *extra)


def attend_back_kernel(size, layer, parts, *refs):
    mid_ref, qkv_ref, qm_ref, km_ref, ctx_ref, lse_ref, w_ref = refs[:7]
    refs = refs[7:]
    if layer == 0:
        gdown_ref, refs = refs[0], refs[1:]
    else:
        hid_ref, wd_ref, h1_in, refs = refs[0], refs[1], refs[2], refs[3:]
    dqkv_ref, gout_ref, refs = refs[0], refs[1], refs[2:]
    if layer == 0:
        down_out, refs = refs[0], refs[1:]
    else:
        y_ref, refs = refs[0], refs[1:]
    da, ka, va, kt, dk, dv, w, w_sem = refs[:8]
    sems, refs = refs[8:12], refs[12:]
    reduce = Reduce(layer, refs[:9])
    if layer == 0:
        down = HalfReduce(layer, refs[9 : 9 + HALF])
        down_swap = HalfSwap(gdown_ref, down.other, refs[9 + HALF])
    else:
        held_hid, wd, h1, y_sem = refs[9:13]
    _, rows, wide = qkv_ref.shape
    length = size * rows
    e = qm_ref.shape[2]
    heads = wide // (3 * e)
    scale = e**-0.5
    c = scale * math.log2(math.e)
    depth = w_ref.shape[1] // parts
    n = chunks(rows)
    rc = rows // n
    bq = size * rc
    kc = bq
    g = Group(size)
    copies = [pltpu.make_async_copy(w_ref, w, w_sem.at[0])]
    for copy in copies:
        copy.start()
    g.greet(parts)
    gather = Gather(g, da, rc, sems)
    loads = []
    if layer == 1:
        scatter = Scatter(g, rc, refs[13:])
        loads = [
            pltpu.make_async_copy(wd_ref, wd, y_sem.at[0]),
            pltpu.make_async_copy(h1_in, h1, y_sem.at[1]),
        ]
        for load in loads:
            load.start()
    if layer == 0:
        down_swap.copy().start()
        loads = down.loads(gdown_ref, None)
        for load in loads:
            load.start()

    def send(j):
        at = span(j, rc)
        da[g.me, at, :] = mid_ref[at, :].astype(BF)
        gather.start(j)

    run(n, send)
    lane = lax.broadcasted_iota(jnp.int32, (length, e), 1)
    whole = flat(qkv_ref[...])
    for h in range(heads):
        o = 3 * e * h
        ka[h, :, :e] = whole[:, o + e : o + 2 * e]
        ka[h, :, e:] = flat(km_ref[...])
        va[h, :, :e] = whole[:, o + 2 * e : o + 3 * e]
        va[h, :, e:] = jnp.where(lane < 3, 1.0, 0.0).astype(BF)
        kt[h] = whole[:, o + e : o + 2 * e].T
    dk[...] = jnp.zeros_like(dk)
    dv[...] = jnp.zeros_like(dv)
    ql = lax.broadcasted_iota(jnp.int32, (bq, e), 1)
    for copy in copies + loads:
        copy.wait()

    def out_grad(z):
        cols = pl.ds(pl.multiple_of(z * depth, depth), depth)
        return dg(flat(ctx_ref[...]), flat(da[:, :, cols]), TN)

    def work(j):
        at = span(j, rc)

        @pl.when(j == 0)
        def _():
            gather.relay(0)
            gather.ready(0)

        @pl.when(j == min(1, n - 1))
        def _():
            for i in range(1, n):
                gather.relay(i)
            for i in range(1, n):
                gather.ready(i)
            reduce.send(out_grad)

        if layer == 1:
            hid_load = pltpu.make_async_copy(hid_ref.at[:, at], held_hid, y_sem.at[2])
            hid_load.start()
        qm = flat(qm_ref[:, at, :])
        dctx = dg(flat(da[:, at, :]), w[...], NT).astype(BF)
        ctx = flat(ctx_ref[:, at, :])
        held_qkv = flat(qkv_ref[:, at, :])
        for h in range(heads):
            o = 3 * e * h
            qq = held_qkv[:, o : o + e]
            q = jnp.concatenate([qq, qm], axis=1)
            dc = dctx[:, h * e : (h + 1) * e]
            prod = dc.astype(F32) * ctx[:, h * e : (h + 1) * e].astype(F32)
            d = -jnp.sum(prod, axis=1, keepdims=True)
            d1 = d.astype(BF).astype(F32)
            d2 = (d - d1).astype(BF).astype(F32)
            d3 = d - d1 - d2
            ds_col = jnp.where(ql == 0, d1, jnp.where(ql == 1, d2, jnp.where(ql == 2, d3, 0.0)))
            dca = jnp.concatenate([dc, ds_col.astype(BF)], axis=1)
            lse = lse_ref[j, h : h + 1, :]
            dqt = None
            for k in range(length // kc):
                ks = slice(k * kc, (k + 1) * kc)
                s = dg(ka[h, ks, :], q, NT)
                p = jnp.exp2(s * c - lse)
                ds = (p * dg(va[h, ks, :], dca, NT)).astype(BF)
                dv[h, ks, :] += dg(p.astype(BF), dc, NN)
                dk[h, ks, :] += dg(ds, qq, NN)
                a = dg(kt[h, :, ks], ds, NN)
                dqt = a if dqt is None else dqt + a
            if layer == 0 and h == heads // 2:

                @pl.when(j == min(1, n - 1))
                def _():
                    down_swap.copy().wait_recv()
                    down.middle()

            if layer == 1 and h == heads // 2:

                @pl.when(j > 0)
                def _():
                    scatter.second(j - 1)

            if layer == 0 and h == heads - 1:

                @pl.when(j == n - 1)
                def _():
                    down.late()

            dqkv_ref[:, at, o : o + e] = (dqt * scale).T.astype(BF).reshape(size, rc, e)
        if layer == 1:
            hid_load.wait()
            width = wd.shape[1]
            for f in range(width // 256):
                cols = slice(f * 256, (f + 1) * 256)
                scatter.part[:, at, cols] = dg(flat(held_hid[...]), wd[:, cols], NN).reshape(
                    size, rc, 256
                )
            scatter.first(j)

    run(n, work)
    if layer == 1:
        scatter.second(n - 1)
    for h in range(heads):
        o = 3 * e * h
        dqkv_ref[:, :, o + e : o + 2 * e] = (dk[h] * scale).astype(BF).reshape(size, rows, e)
        dqkv_ref[:, :, o + 2 * e : o + 3 * e] = dv[h].astype(BF).reshape(size, rows, e)

    reduce.collect()
    if layer == 1:

        def output(j):
            at = span(j, rc)
            y_ref[at, :] = (h1[at, :] + scatter.third(j)).astype(BF)

        run(n, output)
        scatter.drain(n)
    reduce.finish(gout_ref)
    if layer == 0:
        down.finish(down_out)
        down_swap.copy().wait_send()
    gather.drain(n)


def attend_backward(size, replicas, layer, mid, qkv, qm, km, ctx, lse, w, grads, more=()):
    _, rows, wide = qkv.shape
    e = qm.shape[2]
    heads = wide // (3 * e)
    width = mid.shape[1]
    parts, depth = replicas, width // replicas
    length = size * rows
    n = chunks(rows)
    return pl.pallas_call(
        functools.partial(attend_back_kernel, size, layer, parts),
        out_shape=[shape(qkv.shape, BF), shape((heads * e, depth), F32)]
        + [shape(grad.shape[1:], F32) for grad in grads]
        + [shape((rows, width), BF)] * (len(more) // 3),
        in_specs=[VM] * 6 + [HB] * (1 + len(grads) + len(more)),
        out_specs=[VM, VM] + [VM] * (len(grads) + len(more) // 3),
        scratch_shapes=[
            pltpu.VMEM((size, rows, width), BF),
            pltpu.VMEM((heads, length, 2 * e), BF),
            pltpu.VMEM((heads, length, 2 * e), BF),
            pltpu.VMEM((heads, e, length), BF),
            pltpu.VMEM((heads, length, e), F32),
            pltpu.VMEM((heads, length, e), F32),
            pltpu.VMEM((heads * e, width), BF),
            DMA((1,)),
        ]
        + comm_sems(size, n)
        + reduce_scratch(parts, heads * e, depth)
        + sum([half_scratch(parts, *grad.shape[1:]) + [DMA((2,))] for grad in grads], [])
        + (
            [
                pltpu.VMEM((size, rows // n, more[0].shape[2]), BF),
                pltpu.VMEM(more[1].shape, BF),
                pltpu.VMEM((rows, width), F32),
                DMA((3,)),
            ]
            + scatter_scratch(size, rows, width, n)
            if more
            else []
        ),
        compiler_params=params(8 + layer),
        cost_estimate=cost(90e9, 40e6),
    )(mid, qkv, qm, km, ctx, lse, w, *grads, *more)


def qkv_back_kernel(
    size, layer, parts, dqkv_ref, gain_ref, a1_in, x_in, mid_in, w_ref,
    dx_ref, gain_out, gqkv_ref, a1_ref, x_ref, mid_ref, w, w_sem, *scratch
):
    rows, width = x_ref.shape
    late = [
        pltpu.make_async_copy(a1_in, a1_ref, w_sem.at[1]),
        pltpu.make_async_copy(x_in, x_ref, w_sem.at[2]),
        pltpu.make_async_copy(mid_in, mid_ref, w_sem.at[3]),
    ]
    depth = width // parts
    n = thin_chunks(rows)
    rc = rows // n
    g = Group(size)
    copies = [pltpu.make_async_copy(w_ref, w, w_sem.at[0])]
    for copy in copies + late:
        copy.start()
    g.greet()
    scatter = Scatter(g, rc, scratch)
    for copy in copies:
        copy.wait()

    lag = min(2, n)

    def work(j):
        at = span(j, rc)
        held = flat(dqkv_ref[:, at, :])
        for z in range(parts):
            cols = slice(z * depth, (z + 1) * depth)
            scatter.part[:, at, cols] = dg(held, w[cols, :], NT).reshape(size, rc, depth)
        scatter.first(j)

        @pl.when(j >= lag)
        def _():
            scatter.second(j - lag)


    run(n, work)
    for j in range(n - lag, n):
        scatter.second(j)
    for copy in late:
        copy.wait()

    def qkv_grad(z):
        cols = pl.ds(pl.multiple_of(z * depth, depth), depth)
        gqkv_ref[z] = dg(flat(a1_ref[:, :, cols]), flat(dqkv_ref[...]), TN).astype(BF)

    run(parts, qkv_grad)
    gain_out[...] = jnp.zeros_like(gain_out)

    def last(j):
        at = span(j, rc)
        dh, dgain = normed_back(
            x_ref[at, :].astype(F32), gain_ref[layer, 0:1, :], scatter.third(j)
        )
        dx_ref[at, :] = (mid_ref[at, :] + dh).astype(BF)
        gain_out[...] += dgain

    run(n, last)
    scatter.drain(n)


def qkv_backward(size, replicas, layer, dqkv, a1, x, mid, gains, w):
    rows, width = x.shape
    wide = w.shape[1]
    parts, depth = replicas, width // replicas
    n = thin_chunks(rows)
    return pl.pallas_call(
        functools.partial(qkv_back_kernel, size, layer, parts),
        out_shape=(
            shape((rows, width), BF),
            shape((1, width), F32),
            shape((parts, depth, wide), BF),
        ),
        in_specs=[VM, VM] + [HB] * 4,
        out_specs=(VM, VM, VM),
        scratch_shapes=[
            pltpu.VMEM((size, rows, width), BF),
            pltpu.VMEM((rows, width), BF),
            pltpu.VMEM((rows, width), F32),
            pltpu.VMEM((width, wide), BF),
            DMA((4,)),
        ]
        + scatter_scratch(size, rows, width, n),
        compiler_params=params(11),
        cost_estimate=cost(30e9, 30e6),
    )(dqkv, gains, a1, x, mid, w)


def last_kernel(
    size, parts, dqkv_ref, a1_ref, x_ref, mid_ref, gain_ref, w_ref, two_ref, above_ref, dx1_ref,
    gain_out, gqkv_out, dx_out,
    gqkv, swap_sem, w, dx, gsum, gcame, w_sem, x_sem, x_send, x_recv, g_send, g_recv, *scratch
):
    rows, width = x_ref.shape
    depth = width // parts
    n = thin_chunks(rows)
    rc = rows // n
    g = Group(size)
    section = lax.axis_index("section")
    d = lax.axis_index("dp")
    copy = pltpu.make_async_copy(w_ref, w, w_sem.at[0])
    copy.start()
    reduce = HalfReduce(0, scratch[:HALF])
    swap = HalfSwap(gqkv, reduce.other, swap_sem)
    scatter = Scatter(g, rc, scratch[HALF:])
    g.greet(parts)

    def upper():
        return far_copy(
            dx1_ref, dx_out.at[0], x_send.at[n], x_recv.at[n], {"section": 1 - section}
        )

    def keep_upper():
        return pltpu.make_async_copy(dx1_ref, dx_out.at[1], x_sem.at[0])

    def lower(j):
        at = span(j, rc)
        return far_copy(
            dx.at[at], dx_out.at[1, at], x_send.at[j], x_recv.at[j], {"section": 1 - section}
        )

    def keep_lower(j):
        at = span(j, rc)
        return pltpu.make_async_copy(dx.at[at], dx_out.at[0, at], x_sem.at[j])

    def qkv_grad(z):
        cols = pl.ds(pl.multiple_of(z * depth, depth), depth)
        gqkv[z] = dg(flat(a1_ref[:, :, cols]), flat(dqkv_ref[...]), TN).astype(BF)

    run(parts, qkv_grad)
    swap.copy().start()
    load = reduce.loads(gqkv, None)[0]
    load.start()

    @pl.when(section == 1)
    def _():
        keep_upper().start()

    copy.wait()

    lag = min(2, n)

    def work(j):
        at = span(j, rc)
        held = flat(dqkv_ref[:, at, :])
        for z in range(parts):
            cols = slice(z * depth, (z + 1) * depth)
            scatter.part[:, at, cols] = dg(held, w[cols, :], NT).reshape(size, rc, depth)
        scatter.first(j)

        @pl.when(j >= lag)
        def _():
            scatter.second(j - lag)


    run(n, work)
    for j in range(n - lag, n):
        scatter.second(j)
    gsum[0] = jnp.zeros_like(gsum[0])

    def last(j):
        at = span(j, rc)
        dh, dgain = normed_back(x_ref[at, :].astype(F32), gain_ref[0, 0:1, :], scatter.third(j))
        dx[at, :] = (mid_ref[at, :] + dh).astype(BF)

        @pl.when(section == 0)
        def _():
            keep_lower(j).start()

        @pl.when(section == 1)
        def _():
            lower(j).start()

        gsum[0, 0:1, :] += dgain

    def rest(j):
        @pl.when(j == n // 2)
        def _():
            load.wait()
            swap.copy().wait_recv()
            reduce.middle()

            @pl.when(section == 0)
            def _():
                upper().start()

        last(j)

    run(n, rest)
    gsum[0, 1:2, :] = two_ref[...]
    gsum[0, 2:4, :] = above_ref[...]

    targets = [
        [{"tensor": g.sibling}],
        [{"tensor": g.ahead(k) * 2 + g.core} for k in range(1, g.chips)],
        [{"dp": lax.rem(d + k, parts)} for k in range(1, parts)],
        [{"section": 1 - section}],
    ]
    slot = 0
    sent = []

    def exchange(stage):
        nonlocal slot
        copies = []
        for target in targets[stage]:
            copies.append(
                far_copy(gsum.at[stage], gcame.at[slot], g_send.at[slot], g_recv.at[slot], target)
            )
            copies[-1].start()
            slot += 1
        total = gsum[stage]
        for i, copy in enumerate(copies):
            copy.wait_recv()
            total = total + gcame[slot - len(copies) + i]
        gsum[stage + 1] = total
        sent.extend(copies)

    exchange(0)
    exchange(1)
    reduce.late()
    exchange(2)
    exchange(3)
    gain_out[...] = gsum[4]

    @pl.when(section == 0)
    def _():
        for j in range(n):
            lower(j).wait_recv()
            keep_lower(j).wait()
        upper().wait_send()

    @pl.when(section == 1)
    def _():
        keep_upper().wait()
        upper().wait_recv()
        for j in range(n):
            lower(j).wait_send()

    reduce.finish(gqkv_out)
    swap.copy().wait_send()
    for copy in sent:
        copy.wait_send()
    scatter.drain(n)


def last_backward(size, replicas, dqkv, a1, x, mid, gains, w, two, above, dx1):
    rows, width = x.shape
    wide = w.shape[1]
    depth = width // replicas
    n = thin_chunks(rows)
    slots = 1 + (size // 2 - 1) + (replicas - 1) + 1
    return pl.pallas_call(
        functools.partial(last_kernel, size, replicas),
        out_shape=(
            shape((8, width), F32),
            shape((depth, wide), F32),
            shape((2, rows, width), BF),
        ),
        in_specs=[VM] * 5 + [HB, VM, VM, VM],
        out_specs=(VM, VM, HB),
        scratch_shapes=[
            pltpu.VMEM((replicas, depth, wide), BF),
            DMA((2,)),
            pltpu.VMEM((width, wide), BF),
            pltpu.VMEM((rows, width), BF),
            pltpu.VMEM((5, 8, width), F32),
            pltpu.VMEM((slots, 8, width), F32),
            DMA((1,)),
            DMA((n,)),
            DMA((n + 1,)),
            DMA((n + 1,)),
            DMA((slots,)),
            DMA((slots,)),
        ]
        + half_scratch(replicas, depth, wide)
        + scatter_scratch(size, rows, width, n),
        compiler_params=params(10),
        cost_estimate=cost(40e9, 30e6),
    )(dqkv, a1, x, mid, gains, w, two, above, dx1)


def scene_masks(segments, e):
    same = (segments[..., None] == jnp.arange(e, dtype=jnp.int32)).astype(F32)
    used = jnp.arange(e) < SCENES
    return (
        jnp.where(used, same * MASKED, 0.0).astype(BF),
        jnp.where(used, 1.0 - same, 0.0).astype(BF),
    )


def swap_section(value):
    return lax.ppermute(value, "section", [(0, 1), (1, 0)])


def shards(
    block_input,
    segment_ids,
    cotangent,
    norm_one_gain,
    qkv_weight,
    out_weight,
    norm_two_gain,
    up_weight,
    down_weight,
):
    section = lax.axis_index("section")
    size = lax.axis_size("tensor")
    replicas = lax.axis_size("dp")

    mine = [
        qkv_weight[0].reshape((qkv_weight.shape[1], -1)),
        out_weight[0].reshape((-1, out_weight.shape[3])),
        up_weight[0],
        down_weight[0],
    ]
    mine = [w.astype(BF).reshape((2, -1, w.shape[1])) for w in mine]
    gains = jnp.concatenate(
        [norm_one_gain, norm_two_gain, jnp.zeros((6, norm_one_gain.shape[1]), F32)], axis=0
    )
    segments = lax.dynamic_index_in_dim(segment_ids, section, 0, keepdims=False)
    x = lax.dynamic_index_in_dim(block_input, section, 0, keepdims=False)
    head_dim = qkv_weight.shape[3] // 3
    qm, km = scene_masks(segments.reshape((size, -1)), head_dim)
    qkv, gains, a1, w_qkv_0, w_out_0, h_qkv, h_out, h_up, h_down = first_forward(
        size, replicas, x, gains, mine
    )
    h1, ctx, lse, w_up_0, w_down_0 = attend(
        size, replicas, 0, qkv, qm, km, x, w_out_0,
        [(h_up, "spread", 0, False), (h_down, "spread", 0, True)],
    )
    below = (x, a1, qkv, ctx, lse, h1)
    y0, qkv, a2, hid, slope, a1, w_qkv_1, w_out_1, w_up_1 = turn_forward(
        size, replicas, h1, gains, w_up_0, w_down_0, h_qkv,
        [(h_out, "spread", 1, True), (h_up, "spread", 1, False)],
    )
    kept = [below + (a2, hid, slope)]
    grad = lax.dynamic_index_in_dim(cotangent, section, 0, keepdims=False)
    h1, ctx, lse, grad_all, w_down_1 = attend(
        size, replicas, 1, qkv, qm, km, y0, w_out_1, [(h_down, "spread", 1, True)], [grad]
    )
    kept.append((y0, a1, qkv, ctx, lse, h1))
    weights = [
        (w_qkv_0, w_out_0, w_up_0, w_down_0),
        (w_qkv_1, w_out_1, w_up_1, w_down_1),
    ]
    def reduce_rows(value):
        return lax.psum_scatter(value, "dp", scatter_dimension=0, tiled=False)

    x, a1, qkv, ctx, lse, h1 = kept[1]
    w_qkv, w_out, w_up, w_down = weights[1]
    mid, gain_two, g_up, g_down, hid = peak(size, replicas, h1, gains, grad_all, w_up, w_down)
    d_qkv, out_1, y1 = attend_backward(
        size, replicas, 1, mid, qkv, qm, km, ctx, lse, w_out, [], [hid, w_down, h1]
    )
    up_1, down_1 = reduce_rows(g_up), reduce_rows(g_down)
    dx1, gain_one, g_qkv = qkv_backward(size, replicas, 1, d_qkv, a1, x, mid, gains, w_qkv)
    gains_above = jnp.concatenate([gain_one, gain_two], axis=0)
    dx1, up_1, down_1 = lax.optimization_barrier((dx1, up_1, down_1))
    qkv_1 = reduce_rows(g_qkv)

    x, a1, qkv, ctx, lse, h1, a2, hid, slope = kept[0]
    w_qkv, w_out, w_up, w_down = weights[0]
    mid, gain_two, g_up, g_down, layer_out = mlp_backward(
        size, replicas, 0, dx1, h1, gains, a2, hid, slope, w_up, w_down, [y0, y1]
    )
    mid, qkv_1 = lax.optimization_barrier((mid, qkv_1))
    d_qkv, out_0, down_0 = attend_backward(
        size, replicas, 0, mid, qkv, qm, km, ctx, lse, w_out, [g_down]
    )
    up_0 = reduce_rows(g_up)
    d_qkv, up_0 = lax.optimization_barrier((d_qkv, up_0))
    gains, qkv_0, input_out = last_backward(
        size, replicas, d_qkv, a1, x, mid, gains, w_qkv, gain_two, gains_above, dx1
    )

    def finish(zero, one):
        send = swap_section(jnp.where(section == 0, one, zero))
        return jnp.where(section == 0, zero, one).astype(F32) + send.astype(F32)

    other_qkv_1 = swap_section(qkv_1)
    qkv_grad = jnp.where(section == 0, qkv_0, qkv_1.astype(F32) + other_qkv_1.astype(F32))
    out_grad = jnp.where(section == 0, out_0, out_1)
    up_grad = finish(up_0, up_1)
    other_down_1 = swap_section(down_1)
    down_grad = jnp.where(section == 0, down_0, down_1.astype(F32) + other_down_1.astype(F32))
    gains = lax.dynamic_slice_in_dim(gains, 2 * section, 2, 0)
    return (
        layer_out[None],
        input_out[None],
        gains[0:1],
        qkv_grad.reshape(qkv_weight.shape),
        out_grad.reshape(out_weight.shape),
        gains[1:2],
        up_grad[None],
        down_grad[None],
    )


def solution(mesh):
    return jax.shard_map(
        shards,
        mesh=mesh,
        in_specs=(
            P(None, ("dp", "tensor"), None),
            P(None, "dp"),
            P(None, ("dp", "tensor"), None),
            P("section", None),
            P("section", "dp", "tensor", None),
            P("section", "tensor", None, "dp"),
            P("section", None),
            P("section", "dp", "tensor"),
            P("section", "tensor", "dp"),
        ),
        out_specs=(
            P("section", None, ("dp", "tensor"), None),
            P("section", None, ("dp", "tensor"), None),
            P("section", None),
            P("section", "dp", "tensor", None),
            P("section", "tensor", None, "dp"),
            P("section", None),
            P("section", "dp", "tensor"),
            P("section", "tensor", "dp"),
        ),
        check_vma=False,
    )
```

```python
import functools
import math

import jax
import jax.numpy as jnp
from jax import lax
from jax.experimental import pallas as pl
from jax.experimental.pallas import tpu as pltpu
from jax.sharding import PartitionSpec as P

F32 = jnp.float32
BF = jnp.bfloat16
NT = (((1,), (1,)), ((), ()))
NN = (((1,), (0,)), ((), ()))
TN = (((0,), (0,)), ((), ()))
MASKED = -1e30
SCENES = 3
MESH = pl.DeviceIdType.MESH
VM = pl.BlockSpec(memory_space=pltpu.VMEM)
HB = pl.BlockSpec(memory_space=pl.ANY)
DMA = pltpu.SemaphoreType.DMA
LIMIT = 58 << 20


def dg(a, b, dims):
    return lax.dot_general(a, b, dims, preferred_element_type=F32)


def chunks(rows):
    return 4 if rows % 64 == 0 else 1


def thin_chunks(rows):
    return 8 if rows % 128 == 0 else chunks(rows)


def shape(dims, dtype):
    return jax.ShapeDtypeStruct(dims, dtype)


class Group:
    def __init__(self, size):
        self.size = size
        self.chips = size // 2
        self.me = lax.axis_index("tensor")
        self.chip = lax.div(self.me, 2)
        self.core = lax.rem(self.me, 2)
        self.sibling = self.chip * 2 + 1 - self.core

    def ahead(self, k):
        return lax.rem(self.chip + k, self.chips)

    def behind(self, k):
        return lax.rem(self.chip + self.chips - k, self.chips)

    def greet(self, replicas=0, side=False):
        barrier = pltpu.get_barrier_semaphore()
        targets = [self.sibling] + [self.ahead(k) * 2 + self.core for k in range(1, self.chips)]
        targets = [{"tensor": target} for target in targets]
        if replicas:
            d = lax.axis_index("dp")
            targets += [{"dp": lax.rem(d + k, replicas)} for k in range(1, replicas)]
        if replicas or side:
            targets += [{"section": 1 - lax.axis_index("section")}]
        for target in targets:
            pl.semaphore_signal(barrier, inc=1, device_id=target, device_id_type=MESH)
        pl.semaphore_wait(barrier, len(targets))


def remote(src, dst, send, recv, target):
    return pltpu.make_async_remote_copy(
        src_ref=src,
        dst_ref=dst,
        send_sem=send,
        recv_sem=recv,
        device_id={"tensor": target},
        device_id_type=MESH,
    )


def span(j, rc):
    return pl.ds(pl.multiple_of(j * rc, rc), rc)


def comm_sems(group_size, n):
    c = group_size // 2
    far, near = DMA((max(c - 1, 1), n)), DMA((c, n))
    return [far, far, near, near]


class Gather:
    def __init__(self, g, buf, rc, sems):
        self.g, self.buf, self.rc = g, buf, rc
        self.far_send, self.far_recv, self.near_send, self.near_recv = sems

    def far(self, k, j, origin, target, src=None):
        ref = self.buf.at[origin, span(j, self.rc)]
        src = ref if src is None else src
        return remote(src, ref, self.far_send.at[k - 1, j], self.far_recv.at[k - 1, j], target)

    def near(self, k, j, origin, src=None):
        ref = self.buf.at[origin, span(j, self.rc)]
        src = ref if src is None else src
        return remote(
            src, ref, self.near_send.at[k, j], self.near_recv.at[k, j], self.g.sibling
        )

    def start(self, j, src=None):
        g = self.g
        for k in range(1, g.chips):
            self.far(k, j, g.me, g.ahead(k) * 2 + g.core, src).start()
        self.near(0, j, g.me, src).start()

    def relay(self, j):
        g = self.g
        for k in range(1, g.chips):
            origin = g.behind(k) * 2 + g.core
            self.far(k, j, origin, g.me).wait_recv()
            self.near(k, j, origin).start()

    def ready(self, j):
        g = self.g
        self.near(0, j, g.sibling).wait_recv()
        for k in range(1, g.chips):
            self.near(k, j, g.behind(k) * 2 + 1 - g.core).wait_recv()

    def drain(self, n):
        g = self.g

        def one(j, _):
            for k in range(1, g.chips):
                self.far(k, j, g.me, g.sibling).wait_send()
            for k in range(g.chips):
                self.near(k, j, g.me).wait_send()
            return 0

        lax.fori_loop(0, n, one, 0)


def scatter_scratch(group_size, rows, width, n):
    c = group_size // 2
    far = pltpu.VMEM((max(c - 1, 1), rows, width), BF)
    near = pltpu.VMEM((c, rows, width), BF)
    return [pltpu.VMEM((group_size, rows, width), F32), near, near, far, far] + comm_sems(
        group_size, n
    )


class Scatter:
    def __init__(self, g, rc, scratch):
        self.g, self.rc = g, rc
        self.part, self.near_out, self.near_in, self.far_out, self.far_in = scratch[:5]
        self.far_send, self.far_recv, self.near_send, self.near_recv = scratch[5:]

    def near(self, k, j):
        rows = span(j, self.rc)
        return remote(
            self.near_out.at[k, rows],
            self.near_in.at[k, rows],
            self.near_send.at[k, j],
            self.near_recv.at[k, j],
            self.g.sibling,
        )

    def far(self, k, j):
        rows = span(j, self.rc)
        return remote(
            self.far_out.at[k - 1, rows],
            self.far_in.at[k - 1, rows],
            self.far_send.at[k - 1, j],
            self.far_recv.at[k - 1, j],
            self.g.ahead(k) * 2 + self.g.core,
        )

    def first(self, j):
        g, rows = self.g, span(j, self.rc)
        for k in list(range(1, g.chips)) + [0]:
            owner = g.ahead(k) * 2 + 1 - g.core
            self.near_out[k, rows, :] = self.part[owner, rows, :].astype(BF)
            self.near(k, j).start()

    def second(self, j):
        g, rows = self.g, span(j, self.rc)
        for k in range(1, g.chips):
            owner = g.ahead(k) * 2 + g.core
            self.near(k, j).wait_recv()
            both = self.part[owner, rows, :] + self.near_in[k, rows, :].astype(F32)
            self.far_out[k - 1, rows, :] = both.astype(BF)
            self.far(k, j).start()

    def third(self, j):
        g, rows = self.g, span(j, self.rc)
        self.near(0, j).wait_recv()
        total = self.part[g.me, rows, :] + self.near_in[0, rows, :].astype(F32)
        for k in range(1, g.chips):
            self.far(k, j).wait_recv()
            total = total + self.far_in[k - 1, rows, :].astype(F32)
        return total

    def drain(self, n):
        g = self.g

        def one(j, _):
            for k in range(1, g.chips):
                self.far(k, j).wait_send()
            for k in range(g.chips):
                self.near(k, j).wait_send()
            return 0

        lax.fori_loop(0, n, one, 0)


def far_copy(src, dst, send, recv, target):
    return pltpu.make_async_remote_copy(
        src_ref=src,
        dst_ref=dst,
        send_sem=send,
        recv_sem=recv,
        device_id=target,
        device_id_type=MESH,
    )


class Swap:
    def __init__(self, src, stage, sems):
        self.src, self.stage, self.sems = src, stage, sems
        self.s = lax.axis_index("section")

    def copies(self, layer):
        local = pltpu.make_async_copy(self.src.at[self.s], self.stage.at[self.s], self.sems.at[0])
        side = far_copy(
            self.src.at[1 - self.s],
            self.stage.at[layer],
            self.sems.at[1],
            self.sems.at[2],
            {"section": 1 - self.s},
        )
        return local, side

    def start(self):
        for copy in self.copies(self.s):
            copy.start()

    def arrive(self):
        local, side = self.copies(1 - self.s)
        local.wait()
        side.wait_recv()

    def finish(self):
        self.copies(self.s)[1].wait_send()


def reduce_scratch(replicas, rows, cols):
    many = pltpu.VMEM((replicas - 1, rows, cols), BF)
    one = pltpu.VMEM((rows, cols), BF)
    far, side = DMA((replicas - 1, 2)), DMA((2,))
    return [pltpu.VMEM((rows, cols), F32), many, many, one, one, far, far, side, side]


class Reduce:
    def __init__(self, layer, scratch):
        self.layer = layer
        self.own, self.away, self.came, self.over, self.back = scratch[:5]
        self.z_send, self.z_recv, self.y_send, self.y_recv = scratch[5:]
        self.replicas = self.away.shape[0] + 1
        self.half = self.own.shape[0] // 2
        self.d = lax.axis_index("dp")
        self.s = lax.axis_index("section")

    def target(self, k):
        return lax.rem(self.d + k, self.replicas)

    def part(self, i):
        return pl.ds(pl.multiple_of(i * self.half, self.half), self.half)

    def z_copy(self, k, i):
        part = self.part(i)
        return far_copy(
            self.away.at[k - 1, part],
            self.came.at[k - 1, part],
            self.z_send.at[k - 1, i],
            self.z_recv.at[k - 1, i],
            {"dp": self.target(k)},
        )

    def y_copy(self, i):
        part = self.part(i)
        return far_copy(
            self.over.at[part],
            self.back.at[part],
            self.y_send.at[i],
            self.y_recv.at[i],
            {"section": 1 - self.s},
        )

    def send(self, block):
        def one(i):
            k = i + 1
            self.away[i] = block(self.target(k)).astype(BF)
            self.z_copy(k, 0).start()
            self.z_copy(k, 1).start()

        run(self.replicas - 1, one)
        self.own[...] = block(self.d)

    def collect(self):
        def one(i):
            part = self.part(i)
            total = self.own[part, :]
            for k in range(1, self.replicas):
                self.z_copy(k, i).wait_recv()
                total = total + self.came[k - 1, part, :].astype(F32)
            self.own[part, :] = total
            self.over[part, :] = total.astype(BF)

            @pl.when(self.s != self.layer)
            def _():
                self.y_copy(i).start()

        run(2, one)

    def finish(self, out):
        @pl.when(self.s == self.layer)
        def _():
            self.y_copy(0).wait_recv()
            self.y_copy(1).wait_recv()
            out[...] = self.own[...] + self.back[...].astype(F32)

        @pl.when(self.s != self.layer)
        def _():
            self.y_copy(0).wait_send()
            self.y_copy(1).wait_send()
            out[...] = self.own[...]

        for k in range(1, self.replicas):
            self.z_copy(k, 0).wait_send()
            self.z_copy(k, 1).wait_send()


class HalfSwap:
    def __init__(self, src, came, sems):
        self.src, self.came, self.sems = src, came, sems
        self.s = lax.axis_index("section")
        self.rows = came.shape[1]

    def copy(self):
        at = pl.ds(pl.multiple_of((1 - self.s) * self.rows, self.rows), self.rows)
        return far_copy(
            self.src.at[:, at],
            self.came,
            self.sems.at[0],
            self.sems.at[1],
            {"section": 1 - self.s},
        )


def half_scratch(replicas, rows, cols):
    rows = rows // 2
    all_, far = pltpu.VMEM((replicas, rows, cols), BF), pltpu.VMEM((replicas - 1, rows, cols), BF)
    one = pltpu.VMEM((rows, cols), BF)
    z = DMA((replicas - 1,))
    return [all_, all_, far, far, pltpu.VMEM((rows, cols), F32), one, one, DMA((3,)), z, z, DMA((2,))]


HALF = 11


class HalfReduce:
    def __init__(self, layer, scratch):
        self.layer = layer
        self.mine, self.other, self.away, self.came, self.own, self.over, self.back = scratch[:7]
        self.in_sem, self.z_send, self.z_recv, self.y_sem = scratch[7:]
        self.replicas, self.rows = self.mine.shape[:2]
        self.s = lax.axis_index("section")
        self.d = lax.axis_index("dp")

    def half(self, s):
        return pl.ds(pl.multiple_of(s * self.rows, self.rows), self.rows)

    def loads(self, src, other):
        loads = [pltpu.make_async_copy(src.at[:, self.half(self.s)], self.mine, self.in_sem.at[0])]
        if other is not None:
            loads.append(pltpu.make_async_copy(other, self.other, self.in_sem.at[1]))
        return loads

    def z_copy(self, k):
        return far_copy(
            self.away.at[k - 1],
            self.came.at[k - 1],
            self.z_send.at[k - 1],
            self.z_recv.at[k - 1],
            {"dp": lax.rem(self.d + k, self.replicas)},
        )

    def y_copy(self):
        return far_copy(
            self.over, self.back, self.y_sem.at[0], self.y_sem.at[1], {"section": 1 - self.s}
        )

    def middle(self):
        def both(z):
            return self.mine[z].astype(F32) + self.other[z].astype(F32)

        for k in range(1, self.replicas):
            self.away[k - 1] = both(lax.rem(self.d + k, self.replicas)).astype(BF)
            self.z_copy(k).start()
        self.own[...] = both(self.d)

    def late(self):
        total = self.own[...]
        for k in range(1, self.replicas):
            self.z_copy(k).wait_recv()
            total = total + self.came[k - 1].astype(F32)
        self.own[...] = total
        self.over[...] = total.astype(BF)

        @pl.when(self.s != self.layer)
        def _():
            self.y_copy().start()

    def finish(self, out, above=None):
        @pl.when(self.s == self.layer)
        def _():
            self.y_copy().wait_recv()
            out[self.half(self.s), :] = self.own[...]
            out[self.half(1 - self.s), :] = self.back[...].astype(F32)

        @pl.when(self.s != self.layer)
        def _():
            if above is None:
                out[...] = jnp.zeros_like(out)
            else:
                copy = pltpu.make_async_copy(above, out, self.in_sem.at[2])
                copy.start()
                copy.wait()
            self.y_copy().wait_send()

        for k in range(1, self.replicas):
            self.z_copy(k).wait_send()


class Spread:
    def __init__(self, src, dst, by_columns, sems):
        self.src, self.dst, self.by_columns = src, dst, by_columns
        self.own_sem, self.far_send, self.far_recv, self.side_send, self.side_recv = sems
        self.replicas = far = self.side_send.shape[0]
        self.s = lax.axis_index("section")
        self.d = lax.axis_index("dp")
        self.stages = [
            sorted({k, far - k}) for k in range(1, far // 2 + 1)
        ]

    def place(self, half, z):
        rows, cols = self.src.shape
        if self.by_columns:
            return self.dst.at[
                pl.ds(pl.multiple_of(half * rows, rows), rows),
                pl.ds(pl.multiple_of(z * cols, cols), cols),
            ]
        return self.dst.at[pl.ds(pl.multiple_of((2 * z + half) * rows, rows), rows)]

    def origin(self, k):
        return lax.rem(self.d + self.replicas - k, self.replicas)

    def own(self):
        return pltpu.make_async_copy(self.src, self.place(self.s, self.d), self.own_sem.at[0])

    def far(self, k, origin):
        return pltpu.make_async_remote_copy(
            src_ref=self.src,
            dst_ref=self.place(self.s, origin),
            send_sem=self.far_send.at[k - 1],
            recv_sem=self.far_recv.at[k - 1],
            device_id={"dp": lax.rem(self.d + k, self.replicas)},
            device_id_type=MESH,
        )

    def side(self, k, half):
        place = self.place(half, self.origin(k))
        return pltpu.make_async_remote_copy(
            src_ref=self.src if k == 0 else place,
            dst_ref=place,
            send_sem=self.side_send.at[k],
            recv_sem=self.side_recv.at[k],
            device_id={"section": 1 - self.s},
            device_id_type=MESH,
        )

    def start(self):
        for k in self.stages[0]:
            self.far(k, self.d).start()
        self.side(0, self.s).start()
        self.own().start()

    def step(self, i):
        for k in self.stages[i]:
            self.far(k, self.origin(k)).wait_recv()
            self.side(k, self.s).start()
        if i + 1 < len(self.stages):
            for k in self.stages[i + 1]:
                self.far(k, self.d).start()

    def finish(self):
        self.own().wait()
        for k in range(self.replicas):
            self.side(k, 1 - self.s).wait_recv()
        for k in range(1, self.replicas):
            self.far(k, self.d).wait_send()
        for k in range(self.replicas):
            self.side(k, self.s).wait_send()


class ZGather:
    def __init__(self, src, got, sems):
        self.src, self.got = src, got
        self.own_sem, self.send, self.recv = sems
        self.replicas = got.shape[0]
        self.d = lax.axis_index("dp")

    def own(self):
        return pltpu.make_async_copy(self.src, self.got.at[self.d], self.own_sem.at[0])

    def far(self, k, origin):
        return far_copy(
            self.src,
            self.got.at[origin],
            self.send.at[k - 1],
            self.recv.at[k - 1],
            {"dp": lax.rem(self.d + k, self.replicas)},
        )

    def start(self):
        for k in range(1, self.replicas):
            self.far(k, self.d).start()
        self.own().start()

    def step(self, i):
        pass

    def finish(self):
        self.own().wait()
        for k in range(1, self.replicas):
            self.far(k, lax.rem(self.d + self.replicas - k, self.replicas)).wait_recv()
        for k in range(1, self.replicas):
            self.far(k, self.d).wait_send()


class YJoin:
    def __init__(self, got, dst, by_columns, sems):
        self.src, self.dst, self.by_columns = got, dst, by_columns
        self.own_sem, self.send, self.recv, self.got, self.in_sem = sems
        self.replicas, self.rows, self.cols = got.shape
        self.s = lax.axis_index("section")

    def place(self, half, z):
        rows, cols = self.rows, self.cols
        if self.by_columns:
            return self.dst.at[
                pl.ds(pl.multiple_of(half * rows, rows), rows), pl.ds(z * cols, cols)
            ]
        return self.dst.at[pl.ds(pl.multiple_of((2 * z + half) * rows, rows), rows)]

    def own(self, z):
        return pltpu.make_async_copy(self.got.at[z], self.place(self.s, z), self.own_sem.at[z])

    def side(self, z, half):
        return far_copy(
            self.got.at[z],
            self.place(half, z),
            self.send.at[z],
            self.recv.at[z],
            {"section": 1 - self.s},
        )

    def start(self):
        load = pltpu.make_async_copy(self.src, self.got, self.in_sem.at[0])
        load.start()
        load.wait()
        for z in range(self.replicas):
            self.side(z, self.s).start()
            self.own(z).start()

    def step(self, i):
        pass

    def finish(self):
        for z in range(self.replicas):
            self.own(z).wait()
            self.side(z, 1 - self.s).wait_recv()
        for z in range(self.replicas):
            self.side(z, self.s).wait_send()


def rider_sems(replicas):
    far, side = DMA((replicas - 1,)), DMA((replicas,))
    return [DMA((1,)), far, far, side, side]


class Riders:
    def __init__(self, srcs, dsts, columns, sems):
        self.all = []
        for src, dst, (kind, layer, by) in zip(srcs, dsts, columns):
            count = 3 if kind == "z" else 5
            own, sems = sems[:count], sems[count:]
            if kind == "spread":
                self.all.append(Spread(src.at[layer], dst, by, own))
            elif kind == "z":
                self.all.append(ZGather(src.at[layer], dst, own))
            else:
                self.all.append(YJoin(src, dst, by, own))
        self.replicas = self.all[0].replicas if self.all else 0

    def start(self):
        for one in self.all:
            one.start()

    def step(self, j, n):
        if not self.all:
            return
        stages = self.replicas // 2
        for i in range(stages):

            @pl.when(j == n * (i + 1) // stages - 1)
            def _(i=i):
                for one in self.all:
                    one.step(i)

    def finish(self):
        for one in self.all:
            one.finish()


def riding(riders, replicas):
    arrays = [array for array, _, _, _ in riders]
    columns = tuple(rider[1:] for rider in riders)
    outs, sems = [], []
    for array, kind, _, by in riders:
        rows, cols = array.shape[1:]
        if kind == "z":
            outs.append(shape((replicas, rows, cols), BF))
        else:
            outs.append(
                shape((2 * rows, replicas * cols) if by else (2 * replicas * rows, cols), BF)
            )
        far, side = DMA((replicas - 1,)), DMA((replicas,))
        sems += {
            "spread": rider_sems(replicas),
            "z": [DMA((1,)), far, far],
            "y": [side, side, side, pltpu.VMEM(array.shape, BF), DMA((1,))],
        }[kind]
    return arrays, columns, outs, sems


def params(key):
    return pltpu.CompilerParams(
        vmem_limit_bytes=LIMIT, collective_id=key, has_side_effects=True
    )


def cost(flops, moved, exps=0):
    return pl.CostEstimate(flops=int(flops), bytes_accessed=int(moved), transcendentals=int(exps))


def normed(source):
    center = source - jnp.mean(source, axis=-1, keepdims=True)
    r = lax.rsqrt(jnp.mean(center * center, axis=-1, keepdims=True) + 1e-05)
    return center * r, r


def normed_back(source, gain, grad):
    n, r = normed(source)
    e = grad * gain
    dh = r * (
        e - jnp.mean(e, axis=-1, keepdims=True) - n * jnp.mean(e * n, axis=-1, keepdims=True)
    )
    return dh, jnp.sum(grad * n, axis=0, keepdims=True)


def flat(value):
    return value.reshape((value.shape[0] * value.shape[1],) + value.shape[2:])


def run(n, body):
    def one(j, carry):
        body(j)
        return carry

    lax.fori_loop(0, n, one, 0)


def first_kernel(
    size, replicas, x_in, gain_ref, wq_ref, wo_ref, wu_ref, wd_ref,
    qkv_ref, gains_out, x_ref, a1_out, wq_out, wo_out, q_stage, o_stage, u_stage, d_stage,
    a1, w, gains, own_sem, q_sem, o_sem, u_sem, d_sem, gain_sem, *sems
):
    rows, width = x_ref.shape
    n = thin_chunks(rows)
    rc = rows // n
    g = Group(size)
    section = lax.axis_index("section")
    x_load = pltpu.make_async_copy(x_in.at[section], x_ref, own_sem.at[2])
    x_load.start()
    gather = Gather(g, a1, rc, sems[:4])
    swaps = [
        Swap(wq_ref, q_stage, q_sem),
        Swap(wo_ref, o_stage, o_sem),
        Swap(wu_ref, u_stage, u_sem),
        Swap(wd_ref, d_stage, d_sem),
    ]
    spreads = [
        Spread(q_stage.at[0], w, False, sems[4:9]),
        Spread(o_stage.at[0], wo_out, True, sems[9:14]),
    ]
    g.greet(replicas)

    def gain_copy(layer):
        return far_copy(
            gain_ref, gains.at[layer], gain_sem.at[0], gain_sem.at[1], {"section": 1 - section}
        )

    gain_copy(section).start()
    swaps[0].start()
    swaps[1].start()
    gains[section] = gain_ref[...]
    gain_copy(1 - section).wait_recv()
    gains_out[...] = gains[...]
    x_load.wait()

    def send(j):
        at = span(j, rc)
        a = normed(x_ref[at, :].astype(F32))[0] * gains[0, 0:1, :]
        a1[g.me, at, :] = a.astype(BF)
        gather.start(j)

    run(n, send)
    swaps[0].arrive()
    swaps[1].arrive()
    for one in spreads:
        one.start()
    stages = len(spreads[0].stages)

    def relay(j):
        gather.relay(j)

        for i in range(stages):

            @pl.when(j == n * (i + 1) // stages - 1)
            def _(i=i):
                for one in spreads:
                    one.step(i)

    run(n, relay)
    swaps[2].start()
    swaps[3].start()
    for one in spreads:
        one.finish()
    outs = [
        pltpu.make_async_copy(w, wq_out, own_sem.at[0]),
        pltpu.make_async_copy(a1, a1_out, own_sem.at[1]),
    ]
    outs[0].start()

    def multiply(j):
        at = span(j, rc)
        gather.ready(j)
        r = dg(flat(a1[:, at, :]), w[...], NN).astype(BF)
        qkv_ref[:, at, :] = r.reshape(size, rc, r.shape[1])

    run(n, multiply)
    outs[1].start()
    swaps[2].arrive()
    swaps[3].arrive()
    for swap in swaps:
        swap.finish()
    gain_copy(section).wait_send()
    gather.drain(n)
    for out in outs:
        out.wait()


def first_forward(size, replicas, x, gains, ws):
    _, rows, width = x.shape
    wide = ws[0].shape[2]
    deep = 2 * ws[1].shape[1]
    n = thin_chunks(rows)
    return pl.pallas_call(
        functools.partial(first_kernel, size, replicas),
        out_shape=[
            shape((size, rows, wide), BF),
            shape((2,) + gains.shape, F32),
            shape((rows, width), BF),
            shape((size, rows, width), BF),
            shape((width, wide), BF),
            shape((deep, width), BF),
        ]
        + [shape(w.shape, BF) for w in ws],
        in_specs=[HB] + [VM] * 5,
        out_specs=[VM, VM, VM] + [HB] * 7,
        scratch_shapes=[
            pltpu.VMEM((size, rows, width), BF),
            pltpu.VMEM((width, wide), BF),
            pltpu.VMEM((2,) + gains.shape, F32),
            DMA((3,)),
            DMA((3,)),
            DMA((3,)),
            DMA((3,)),
            DMA((3,)),
            DMA((2,)),
        ]
        + comm_sems(size, n)
        + rider_sems(replicas) * 2,
        compiler_params=params(0),
        cost_estimate=cost(30e9, 30e6),
    )(x, gains, *ws)


def attend_kernel(size, layer, columns, *refs):
    m = len(columns)
    qkv_ref, qm_ref, km_ref, x_ref, w_ref = refs[:5]
    refs = refs[5:]
    if layer == 1:
        cot_ref, refs = refs[0], refs[1:]
    halves, refs = refs[:m], refs[m:]
    h1_ref, ctx_ref, lse_ref = refs[:3]
    refs = refs[3:]
    if layer == 1:
        cot_out, refs = refs[0], refs[1:]
    wholes, refs = refs[:m], refs[m:]
    ka, vt, w, w_sem = refs[:4]
    scratch, refs = refs[4:13], refs[13:]
    if layer == 1:
        cot_sems, cot_sem, cot_mine, refs = refs[:4], refs[4], refs[5], refs[6:]
        cot_load = pltpu.make_async_copy(
            cot_ref.at[lax.axis_index("section")], cot_mine, cot_sem.at[1]
        )
        cot_load.start()
    riders = Riders(halves, wholes, columns, refs)
    _, rows, wide = qkv_ref.shape
    length = size * rows
    e = qm_ref.shape[2]
    heads = wide // (3 * e)
    c = e**-0.5 * math.log2(math.e)
    n = chunks(rows)
    rc = rows // n
    bq = size * rc
    kc = bq
    g = Group(size)
    copy = pltpu.make_async_copy(w_ref, w, w_sem.at[0])
    copy.start()
    g.greet(riders.replicas)
    riders.start()
    if layer == 1:
        cot = Gather(g, cot_out, rows, cot_sems)
        own = pltpu.make_async_copy(cot_mine, cot_out.at[g.me], cot_sem.at[0])
        cot_load.wait()
        own.start()
        cot.start(0, cot_mine)
    scatter = Scatter(g, rc, scratch)
    whole = flat(qkv_ref[...])
    for h in range(heads):
        o = 3 * e * h
        ka[h, :, :e] = whole[:, o + e : o + 2 * e]
        ka[h, :, e:] = flat(km_ref[...])
        vt[h, :e, :] = whole[:, o + 2 * e : o + 3 * e].T
        vt[h, e:, :] = jnp.ones((16, length), BF)
    copy.wait()

    def work(j):
        at = span(j, rc)
        qm = flat(qm_ref[:, at, :])
        found = []
        held_qkv = flat(qkv_ref[:, at, :])
        for h in range(heads):
            o = 3 * e * h
            q = jnp.concatenate([held_qkv[:, o : o + e], qm], axis=1)
            held = []
            top = None
            for k in range(length // kc):
                s = dg(ka[h, k * kc : (k + 1) * kc, :], q, NT)
                t = jnp.max(s, axis=0, keepdims=True)
                top = t if top is None else jnp.maximum(top, t)
                held.append(s)
            top = top * c
            acc = None
            for k in range(length // kc):
                p = jnp.exp2(held[k] * c - top).astype(BF)
                a = dg(vt[h, :, k * kc : (k + 1) * kc], p, NN)
                acc = a if acc is None else acc + a
            total = acc[e : e + 1]
            found.append((acc[:e] * (1.0 / total)).astype(BF))
            lse_ref[j, h : h + 1, :] = top + jnp.log2(total)
            if h == heads // 2:

                @pl.when(j > 0)
                def _():
                    scatter.second(j - 1)

        ctx = (jnp.concatenate(found, axis=0) if heads > 1 else found[0]).T
        ctx_ref[:, at, :] = ctx.reshape(size, rc, heads * e)
        width = x_ref.shape[1]
        scatter.part[:, at, :] = dg(ctx, w[...], NN).reshape(size, rc, width)
        scatter.first(j)
        riders.step(j, n)
        if layer == 1:

            @pl.when(j == n - 1)
            def _():
                cot.relay(0)

    run(n, work)
    scatter.second(n - 1)

    def last(j):
        at = span(j, rc)
        h1_ref[at, :] = x_ref[at, :].astype(F32) + scatter.third(j)

    run(n, last)
    scatter.drain(n)
    if layer == 1:
        cot.ready(0)
        cot.drain(1)
        own.wait()
    riders.finish()


def attend(size, replicas, layer, qkv, qm, km, x, w, riders, cot=()):
    _, rows, wide = qkv.shape
    e = qm.shape[2]
    heads = wide // (3 * e)
    width = x.shape[1]
    n = chunks(rows)
    halves, columns, outs, sems = riding(riders, replicas)
    return pl.pallas_call(
        functools.partial(attend_kernel, size, layer, columns),
        out_shape=[
            shape((rows, width), F32),
            shape((size, rows, heads * e), BF),
            shape((n, heads, size * rows // n), F32),
        ]
        + [shape((size, rows, width), BF) for _ in cot]
        + outs,
        in_specs=[VM, VM, VM, VM, HB] + [HB] * (len(cot) + len(riders)),
        out_specs=[VM, VM, VM] + [HB] * (len(cot) + len(outs)),
        scratch_shapes=[
            pltpu.VMEM((heads, size * rows, 2 * e), BF),
            pltpu.VMEM((heads, e + 16, size * rows), BF),
            pltpu.VMEM((heads * e, width), BF),
            DMA((1,)),
        ]
        + scatter_scratch(size, rows, width, n)
        + (comm_sems(size, 1) + [DMA((2,)), pltpu.VMEM((rows, width), BF)]) * len(cot)
        + sems,
        compiler_params=params(2 + layer),
        cost_estimate=cost(60e9, 20e6),
    )(qkv, qm, km, x, w, *cot, *halves)


def peak_kernel(
    size, parts, h1_ref, gain_ref, grad_ref, wu_ref, wd_ref,
    mid_ref, gain_out, gup_ref, gdown_ref, hid_out,
    a2, hid, dup, grad, wu, wd, w_sem, out_sem, *scratch
):
    rows, width = h1_ref.shape
    hidden = wu_ref.shape[1]
    depth = width // parts
    fb = min(256, hidden)
    n = chunks(rows)
    rc = rows // n
    g = Group(size)
    copies = [
        pltpu.make_async_copy(wu_ref, wu, w_sem.at[0]),
        pltpu.make_async_copy(wd_ref, wd, w_sem.at[1]),
        pltpu.make_async_copy(grad_ref, grad, w_sem.at[2]),
    ]
    for copy in copies:
        copy.start()
    g.greet()
    gather = Gather(g, a2, rc, scratch[:4])
    scatter = Scatter(g, rc, scratch[4:])

    def send(j):
        at = span(j, rc)
        a = normed(h1_ref[at, :])[0] * gain_ref[1, 1:2, :]
        a2[g.me, at, :] = a.astype(BF)
        gather.start(j)

    run(n, send)
    for copy in copies:
        copy.wait()
    gather.relay(0)

    def work(j):
        at = span(j, rc)
        gather.ready(j)
        a = flat(a2[:, at, :])
        held = flat(grad[:, at, :])
        for f in range(hidden // fb):
            cols = slice(f * fb, (f + 1) * fb)
            u = dg(a, wu[:, cols], NN)
            half = 0.5 + 0.5 * lax.erf(u * (0.5**0.5))
            slope = half + u * jnp.exp(-0.5 * u * u) * ((2 * math.pi) ** -0.5)
            hid[:, at, cols] = (u * half).astype(BF).reshape(size, rc, fb)
            d = dg(held, wd[cols, :], NT) * slope
            dup[:, at, cols] = d.astype(BF).reshape(size, rc, fb)

        @pl.when(j + 1 < n)
        def _():
            gather.relay(j + 1)

        @pl.when(j > 0)
        def _():
            scatter.second(j - 1)

        held = flat(dup[:, at, :])
        for z in range(parts):
            cols = slice(z * depth, (z + 1) * depth)
            scatter.part[:, at, cols] = dg(held, wu[cols, :], NT).reshape(size, rc, depth)
        scatter.first(j)

    run(n, work)
    scatter.second(n - 1)
    out = pltpu.make_async_copy(hid, hid_out, out_sem.at[0])
    out.start()

    def up_grad(z):
        cols = pl.ds(pl.multiple_of(z * depth, depth), depth)
        gup_ref[z] = dg(flat(a2[:, :, cols]), flat(dup[...]), TN).astype(BF)

    run(parts, up_grad)

    def down_grad(f):
        cols = pl.ds(pl.multiple_of(f * fb, fb), fb)
        r = dg(flat(hid[:, :, cols]), flat(grad[...]), TN).astype(BF)
        for z in range(parts):
            gdown_ref[z, cols, :] = r[:, z * depth : (z + 1) * depth]

    run(hidden // fb, down_grad)
    gain_out[...] = jnp.zeros_like(gain_out)

    def last(j):
        at = span(j, rc)
        dh, dgain = normed_back(h1_ref[at, :], gain_ref[1, 1:2, :], scatter.third(j))
        mid_ref[at, :] = grad[g.me, at, :].astype(F32) + dh
        gain_out[...] += dgain

    run(n, last)
    gather.drain(n)
    scatter.drain(n)
    out.wait()


def peak(size, replicas, h1, gains, grad_all, wu, wd):
    rows, width = h1.shape
    hidden = wu.shape[1]
    depth = width // replicas
    n = chunks(rows)
    return pl.pallas_call(
        functools.partial(peak_kernel, size, replicas),
        out_shape=[
            shape((rows, width), F32),
            shape((1, width), F32),
            shape((replicas, depth, hidden), BF),
            shape((replicas, hidden, depth), BF),
            shape((size, rows, hidden), BF),
        ],
        in_specs=[VM, VM, HB, HB, HB],
        out_specs=[VM, VM, VM, VM, HB],
        scratch_shapes=[
            pltpu.VMEM((size, rows, width), BF),
            pltpu.VMEM((size, rows, hidden), BF),
            pltpu.VMEM((size, rows, hidden), BF),
            pltpu.VMEM((size, rows, width), BF),
            pltpu.VMEM((width, hidden), BF),
            pltpu.VMEM((hidden, width), BF),
            DMA((3,)),
            DMA((1,)),
        ]
        + comm_sems(size, n)
        + scatter_scratch(size, rows, width, n),
        compiler_params=params(5),
        cost_estimate=cost(60e9, 30e6),
    )(h1, gains, grad_all, wu, wd)


def turn_kernel(size, columns, *refs):
    m = len(columns)
    h1_ref, gain_ref, wu_ref, wd_ref, q_stage = refs[:5]
    halves, refs = refs[5 : 5 + m], refs[5 + m :]
    y_ref, qkv_ref, a2_out, hid_out, slope_out, a1_out, wq_out = refs[:7]
    wholes, refs = refs[7 : 7 + m], refs[7 + m :]
    a2, hid, slope, wu, wd, a1, wq, w_sem, out_sem = refs[:9]
    gather_sems, next_sems, refs = refs[9:13], refs[13:17], refs[17:]
    scratch, refs = refs[:9], refs[9:]
    spread = Spread(q_stage.at[1], wq, False, refs[:5])
    riders = Riders(halves, wholes, columns, refs[5:])
    out_rider, up_rider = riders.all
    stages = len(spread.stages)
    rows, width = h1_ref.shape
    hidden = wu_ref.shape[1]
    fb = min(256, hidden)
    n = chunks(rows)
    rc = rows // n
    g = Group(size)
    copies = [
        pltpu.make_async_copy(wu_ref, wu, w_sem.at[0]),
        pltpu.make_async_copy(wd_ref, wd, w_sem.at[1]),
    ]
    for copy in copies:
        copy.start()
    g.greet(spread.replicas)
    gather = Gather(g, a2, rc, gather_sems)
    onward = Gather(g, a1, rc, next_sems)
    scatter = Scatter(g, rc, scratch)

    def send(j):
        at = span(j, rc)
        a = normed(h1_ref[at, :])[0] * gain_ref[0, 1:2, :]
        a2[g.me, at, :] = a.astype(BF)
        gather.start(j)

    run(n, send)
    spread.start()
    out_rider.start()
    for copy in copies:
        copy.wait()

    def pass_on(j):
        at = span(j, rc)
        y = (h1_ref[at, :] + scatter.third(j)).astype(BF)
        y_ref[at, :] = y
        a = normed(y.astype(F32))[0] * gain_ref[1, 0:1, :]
        a1[g.me, at, :] = a.astype(BF)
        onward.start(j)

    lag = min(2, n)
    gather.relay(0)

    def work(j):
        at = span(j, rc)
        gather.ready(j)
        a = flat(a2[:, at, :])
        for f in range(hidden // fb):
            cols = slice(f * fb, (f + 1) * fb)
            u = dg(a, wu[:, cols], NN)
            half = 0.5 + 0.5 * lax.erf(u * (0.5**0.5))
            slope[:, at, cols] = (
                (half + u * jnp.exp(-0.5 * u * u) * ((2 * math.pi) ** -0.5))
                .astype(BF)
                .reshape(size, rc, fb)
            )
            hid[:, at, cols] = (u * half).astype(BF).reshape(size, rc, fb)

        @pl.when(j + 1 < n)
        def _():
            gather.relay(j + 1)

        @pl.when(j > 0)
        def _():
            scatter.second(j - 1)

        held = flat(hid[:, at, :])
        for f in range(width // 256):
            cols = slice(f * 256, (f + 1) * 256)
            scatter.part[:, at, cols] = dg(held, wd[:, cols], NN).reshape(size, rc, 256)
        scatter.first(j)

        @pl.when(j >= lag)
        def _():
            pass_on(j - lag)

        @pl.when(j == min(1, n - 1))
        def _():
            spread.step(0)
            out_rider.step(0)

        @pl.when(j == n - 1)
        def _():
            for i in range(1, stages):
                spread.step(i)
                out_rider.step(i)
            up_rider.start()

    run(n, work)
    scatter.second(n - 1)
    outs = [
        pltpu.make_async_copy(a2, a2_out, out_sem.at[0]),
        pltpu.make_async_copy(hid, hid_out, out_sem.at[1]),
        pltpu.make_async_copy(slope, slope_out, out_sem.at[2]),
    ]
    for out in outs:
        out.start()
    for j in range(n - lag, n):
        pass_on(j)
    up_rider.step(0)
    spread.finish()
    outs.append(pltpu.make_async_copy(wq, wq_out, out_sem.at[3]))
    outs[3].start()

    onward.relay(0)

    def multiply(j):
        at = span(j, rc)

        @pl.when(j + 1 < n)
        def _():
            onward.relay(j + 1)

        @pl.when(j == n // 2)
        def _():
            for i in range(1, stages):
                up_rider.step(i)

        onward.ready(j)
        r = dg(flat(a1[:, at, :]), wq[...], NN).astype(BF)
        qkv_ref[:, at, :] = r.reshape(size, rc, r.shape[1])

    run(n, multiply)
    outs.append(pltpu.make_async_copy(a1, a1_out, out_sem.at[4]))
    outs[4].start()
    riders.finish()
    gather.drain(n)
    onward.drain(n)
    scatter.drain(n)
    for out in outs:
        out.wait()


def turn_forward(size, replicas, h1, gains, wu, wd, stage, riders):
    rows, width = h1.shape
    hidden = wu.shape[1]
    wide = stage.shape[2]
    n = chunks(rows)
    halves, columns, outs, sems = riding(riders, replicas)
    return pl.pallas_call(
        functools.partial(turn_kernel, size, columns),
        out_shape=[
            shape((rows, width), BF),
            shape((size, rows, wide), BF),
            shape((size, rows, width), BF),
            shape((size, rows, hidden), BF),
            shape((size, rows, hidden), BF),
            shape((size, rows, width), BF),
            shape((width, wide), BF),
        ]
        + outs,
        in_specs=[VM, VM] + [HB] * (3 + len(riders)),
        out_specs=[VM, VM] + [HB] * (5 + len(outs)),
        scratch_shapes=[
            pltpu.VMEM((size, rows, width), BF),
            pltpu.VMEM((size, rows, hidden), BF),
            pltpu.VMEM((size, rows, hidden), BF),
            pltpu.VMEM((width, hidden), BF),
            pltpu.VMEM((hidden, width), BF),
            pltpu.VMEM((size, rows, width), BF),
            pltpu.VMEM((width, wide), BF),
            DMA((2,)),
            DMA((5,)),
        ]
        + comm_sems(size, n) * 2
        + scatter_scratch(size, rows, width, n)
        + rider_sems(replicas)
        + sems,
        compiler_params=params(4),
        cost_estimate=cost(50e9, 30e6),
    )(h1, gains, wu, wd, stage, *halves)


def mlp_back_kernel(size, layer, parts, *refs):
    g_ref, h1_ref, gain_ref, a2_ref, hid_ref, slope_ref, wu_ref, wd_ref = refs[:8]
    refs = refs[8:]
    ys, refs = refs[:2], refs[2:]
    mid_ref, gain_out, gup_ref, gdown_ref = refs[:4]
    refs = refs[4:]
    y_out, refs = refs[0], refs[1:]
    grad, a2, hid, dup, wu, wd, w_sem = refs[:7]
    scratch, refs = refs[7:20], refs[20:]
    rows, width = h1_ref.shape
    hidden = wu_ref.shape[1]
    depth = width // parts
    fb = min(256, hidden)
    n = chunks(rows)
    rc = rows // n
    g = Group(size)
    copies = [
        pltpu.make_async_copy(wd_ref, wd, w_sem.at[0]),
        pltpu.make_async_copy(slope_ref, dup, w_sem.at[1]),
        pltpu.make_async_copy(wu_ref, wu, w_sem.at[2]),
    ]
    late = [
        pltpu.make_async_copy(hid_ref, hid, w_sem.at[3]),
        pltpu.make_async_copy(a2_ref, a2, w_sem.at[4]),
    ]
    for copy in copies:
        copy.start()
    g.greet(side=True)
    section = lax.axis_index("section")
    y_sem, y_own = refs

    def y_load(own):
        return pltpu.make_async_copy(own, y_own, y_sem.at[3])

    def y_copies(own, other, at):
        return (
            pltpu.make_async_copy(y_own, y_out.at[section], y_sem.at[0]),
            far_copy(
                other, y_out.at[at], y_sem.at[1], y_sem.at[2], {"section": 1 - section}
            ),
        )

    for i in range(2):

        @pl.when(section == i)
        def _(i=i):
            y_load(ys[i]).start()
            y_copies(ys[i], ys[1 - i], section)[1].start()

    gather = Gather(g, grad, rc, scratch[:4])
    scatter = Scatter(g, rc, scratch[4:])

    def send(j):
        at = span(j, rc)
        grad[g.me, at, :] = g_ref[at, :]
        gather.start(j)

    run(n, send)
    for copy in copies:
        copy.wait()
    for copy in late:
        copy.start()
    y_load(ys[0]).wait()
    y_copies(ys[0], ys[1], section)[0].start()

    gather.relay(0)

    def work(j):
        at = span(j, rc)
        gather.ready(j)
        held = flat(grad[:, at, :])
        for f in range(hidden // fb):
            cols = slice(f * fb, (f + 1) * fb)
            d = dg(held, wd[cols, :], NT) * flat(dup[:, at, cols]).astype(F32)
            dup[:, at, cols] = d.astype(BF).reshape(size, rc, fb)

        @pl.when(j + 1 < n)
        def _():
            gather.relay(j + 1)

        @pl.when(j > 0)
        def _():
            scatter.second(j - 1)

        held = flat(dup[:, at, :])
        for z in range(parts):
            cols = slice(z * depth, (z + 1) * depth)
            scatter.part[:, at, cols] = dg(held, wu[cols, :], NT).reshape(size, rc, depth)
        scatter.first(j)

    run(n, work)
    scatter.second(n - 1)
    for copy in late:
        copy.wait()

    def up_grad(z):
        cols = pl.ds(pl.multiple_of(z * depth, depth), depth)
        gup_ref[z] = dg(flat(a2[:, :, cols]), flat(dup[...]), TN).astype(BF)

    run(parts, up_grad)

    def down_grad(f):
        cols = pl.ds(pl.multiple_of(f * fb, fb), fb)
        r = dg(flat(hid[:, :, cols]), flat(grad[...]), TN).astype(BF)
        for z in range(parts):
            gdown_ref[z, cols, :] = r[:, z * depth : (z + 1) * depth]

    run(hidden // fb, down_grad)
    gain_out[...] = jnp.zeros_like(gain_out)

    def last(j):
        at = span(j, rc)
        dh, dgain = normed_back(h1_ref[at, :], gain_ref[layer, 1:2, :], scatter.third(j))
        mid_ref[at, :] = g_ref[at, :].astype(F32) + dh
        gain_out[...] += dgain

    run(n, last)
    local, side = y_copies(ys[0], ys[1], 1 - section)
    local.wait()
    side.wait_recv()
    y_copies(ys[0], ys[1], section)[1].wait_send()
    gather.drain(n)
    scatter.drain(n)


def mlp_backward(size, replicas, layer, grad, h1, gains, a2, hid, slope, wu, wd, extra):
    rows, width = h1.shape
    hidden = wu.shape[1]
    parts, depth = replicas, width // replicas
    n = chunks(rows)
    return pl.pallas_call(
        functools.partial(mlp_back_kernel, size, layer, parts),
        out_shape=[
            shape((rows, width), F32),
            shape((1, width), F32),
            shape((parts, depth, hidden), BF),
            shape((parts, hidden, depth), BF),
        ]
        + [shape((2, rows, width), BF)] * (len(extra) // 2),
        in_specs=[VM, VM, VM] + [HB] * (5 + len(extra)),
        out_specs=[VM, VM, VM, VM] + [HB] * (len(extra) // 2),
        scratch_shapes=[
            pltpu.VMEM((size, rows, width), BF),
            pltpu.VMEM((size, rows, width), BF),
            pltpu.VMEM((size, rows, hidden), BF),
            pltpu.VMEM((size, rows, hidden), BF),
            pltpu.VMEM((width, hidden), BF),
            pltpu.VMEM((hidden, width), BF),
            DMA((6,)),
        ]
        + comm_sems(size, n)
        + scatter_scratch(size, rows, width, n)
        + [DMA((4,)), pltpu.VMEM((rows, width), BF)] * (len(extra) // 2),
        compiler_params=params(6 + layer),
        cost_estimate=cost(60e9, 40e6),
    )(grad, h1, gains, a2, hid, slope, wu, wd, *extra)


def attend_back_kernel(size, layer, parts, *refs):
    mid_ref, qkv_ref, qm_ref, km_ref, ctx_ref, lse_ref, w_ref = refs[:7]
    refs = refs[7:]
    if layer == 0:
        gdown_ref, refs = refs[0], refs[1:]
    else:
        hid_ref, wd_ref, h1_in, refs = refs[0], refs[1], refs[2], refs[3:]
    dqkv_ref, gout_ref, refs = refs[0], refs[1], refs[2:]
    if layer == 0:
        down_out, refs = refs[0], refs[1:]
    else:
        y_ref, refs = refs[0], refs[1:]
    da, ka, va, kt, dk, dv, w, w_sem = refs[:8]
    sems, refs = refs[8:12], refs[12:]
    reduce = Reduce(layer, refs[:9])
    if layer == 0:
        down = HalfReduce(layer, refs[9 : 9 + HALF])
        down_swap = HalfSwap(gdown_ref, down.other, refs[9 + HALF])
    else:
        held_hid, wd, h1, y_sem = refs[9:13]
    _, rows, wide = qkv_ref.shape
    length = size * rows
    e = qm_ref.shape[2]
    heads = wide // (3 * e)
    scale = e**-0.5
    c = scale * math.log2(math.e)
    depth = w_ref.shape[1] // parts
    n = chunks(rows)
    rc = rows // n
    bq = size * rc
    kc = bq
    g = Group(size)
    copies = [pltpu.make_async_copy(w_ref, w, w_sem.at[0])]
    for copy in copies:
        copy.start()
    g.greet(parts)
    gather = Gather(g, da, rc, sems)
    loads = []
    if layer == 1:
        scatter = Scatter(g, rc, refs[13:])
        loads = [
            pltpu.make_async_copy(wd_ref, wd, y_sem.at[0]),
            pltpu.make_async_copy(h1_in, h1, y_sem.at[1]),
        ]
        for load in loads:
            load.start()
    if layer == 0:
        down_swap.copy().start()
        loads = down.loads(gdown_ref, None)
        for load in loads:
            load.start()

    def send(j):
        at = span(j, rc)
        da[g.me, at, :] = mid_ref[at, :].astype(BF)
        gather.start(j)

    run(n, send)
    lane = lax.broadcasted_iota(jnp.int32, (length, e), 1)
    whole = flat(qkv_ref[...])
    for h in range(heads):
        o = 3 * e * h
        ka[h, :, :e] = whole[:, o + e : o + 2 * e]
        ka[h, :, e:] = flat(km_ref[...])
        va[h, :, :e] = whole[:, o + 2 * e : o + 3 * e]
        va[h, :, e:] = jnp.where(lane < 3, 1.0, 0.0).astype(BF)
        kt[h] = whole[:, o + e : o + 2 * e].T
    dk[...] = jnp.zeros_like(dk)
    dv[...] = jnp.zeros_like(dv)
    ql = lax.broadcasted_iota(jnp.int32, (bq, e), 1)
    for copy in copies + loads:
        copy.wait()

    def out_grad(z):
        cols = pl.ds(pl.multiple_of(z * depth, depth), depth)
        return dg(flat(ctx_ref[...]), flat(da[:, :, cols]), TN)

    def work(j):
        at = span(j, rc)

        @pl.when(j == 0)
        def _():
            gather.relay(0)
            gather.ready(0)

        @pl.when(j == min(1, n - 1))
        def _():
            for i in range(1, n):
                gather.relay(i)
            for i in range(1, n):
                gather.ready(i)
            reduce.send(out_grad)

        if layer == 1:
            hid_load = pltpu.make_async_copy(hid_ref.at[:, at], held_hid, y_sem.at[2])
            hid_load.start()
        qm = flat(qm_ref[:, at, :])
        dctx = dg(flat(da[:, at, :]), w[...], NT).astype(BF)
        ctx = flat(ctx_ref[:, at, :])
        held_qkv = flat(qkv_ref[:, at, :])
        for h in range(heads):
            o = 3 * e * h
            qq = held_qkv[:, o : o + e]
            q = jnp.concatenate([qq, qm], axis=1)
            dc = dctx[:, h * e : (h + 1) * e]
            prod = dc.astype(F32) * ctx[:, h * e : (h + 1) * e].astype(F32)
            d = -jnp.sum(prod, axis=1, keepdims=True)
            d1 = d.astype(BF).astype(F32)
            d2 = (d - d1).astype(BF).astype(F32)
            d3 = d - d1 - d2
            ds_col = jnp.where(ql == 0, d1, jnp.where(ql == 1, d2, jnp.where(ql == 2, d3, 0.0)))
            dca = jnp.concatenate([dc, ds_col.astype(BF)], axis=1)
            lse = lse_ref[j, h : h + 1, :]
            dqt = None
            for k in range(length // kc):
                ks = slice(k * kc, (k + 1) * kc)
                s = dg(ka[h, ks, :], q, NT)
                p = jnp.exp2(s * c - lse)
                ds = (p * dg(va[h, ks, :], dca, NT)).astype(BF)
                dv[h, ks, :] += dg(p.astype(BF), dc, NN)
                dk[h, ks, :] += dg(ds, qq, NN)
                a = dg(kt[h, :, ks], ds, NN)
                dqt = a if dqt is None else dqt + a
            if layer == 0 and h == heads // 2:

                @pl.when(j == min(1, n - 1))
                def _():
                    down_swap.copy().wait_recv()
                    down.middle()

            if layer == 1 and h == heads // 2:

                @pl.when(j > 0)
                def _():
                    scatter.second(j - 1)

            if layer == 0 and h == heads - 1:

                @pl.when(j == n - 1)
                def _():
                    down.late()

            dqkv_ref[:, at, o : o + e] = (dqt * scale).T.astype(BF).reshape(size, rc, e)
        if layer == 1:
            hid_load.wait()
            width = wd.shape[1]
            for f in range(width // 256):
                cols = slice(f * 256, (f + 1) * 256)
                scatter.part[:, at, cols] = dg(flat(held_hid[...]), wd[:, cols], NN).reshape(
                    size, rc, 256
                )
            scatter.first(j)

    run(n, work)
    if layer == 1:
        scatter.second(n - 1)
    for h in range(heads):
        o = 3 * e * h
        dqkv_ref[:, :, o + e : o + 2 * e] = (dk[h] * scale).astype(BF).reshape(size, rows, e)
        dqkv_ref[:, :, o + 2 * e : o + 3 * e] = dv[h].astype(BF).reshape(size, rows, e)

    reduce.collect()
    if layer == 1:

        def output(j):
            at = span(j, rc)
            y_ref[at, :] = (h1[at, :] + scatter.third(j)).astype(BF)

        run(n, output)
        scatter.drain(n)
    reduce.finish(gout_ref)
    if layer == 0:
        down.finish(down_out)
        down_swap.copy().wait_send()
    gather.drain(n)


def attend_backward(size, replicas, layer, mid, qkv, qm, km, ctx, lse, w, grads, more=()):
    _, rows, wide = qkv.shape
    e = qm.shape[2]
    heads = wide // (3 * e)
    width = mid.shape[1]
    parts, depth = replicas, width // replicas
    length = size * rows
    n = chunks(rows)
    return pl.pallas_call(
        functools.partial(attend_back_kernel, size, layer, parts),
        out_shape=[shape(qkv.shape, BF), shape((heads * e, depth), F32)]
        + [shape(grad.shape[1:], F32) for grad in grads]
        + [shape((rows, width), BF)] * (len(more) // 3),
        in_specs=[VM] * 6 + [HB] * (1 + len(grads) + len(more)),
        out_specs=[VM, VM] + [VM] * (len(grads) + len(more) // 3),
        scratch_shapes=[
            pltpu.VMEM((size, rows, width), BF),
            pltpu.VMEM((heads, length, 2 * e), BF),
            pltpu.VMEM((heads, length, 2 * e), BF),
            pltpu.VMEM((heads, e, length), BF),
            pltpu.VMEM((heads, length, e), F32),
            pltpu.VMEM((heads, length, e), F32),
            pltpu.VMEM((heads * e, width), BF),
            DMA((1,)),
        ]
        + comm_sems(size, n)
        + reduce_scratch(parts, heads * e, depth)
        + sum([half_scratch(parts, *grad.shape[1:]) + [DMA((2,))] for grad in grads], [])
        + (
            [
                pltpu.VMEM((size, rows // n, more[0].shape[2]), BF),
                pltpu.VMEM(more[1].shape, BF),
                pltpu.VMEM((rows, width), F32),
                DMA((3,)),
            ]
            + scatter_scratch(size, rows, width, n)
            if more
            else []
        ),
        compiler_params=params(8 + layer),
        cost_estimate=cost(90e9, 40e6),
    )(mid, qkv, qm, km, ctx, lse, w, *grads, *more)


def qkv_back_kernel(
    size, layer, parts, dqkv_ref, gain_ref, a1_in, x_in, mid_in, w_ref,
    dx_ref, gain_out, gqkv_ref, a1_ref, x_ref, mid_ref, w, w_sem, *scratch
):
    rows, width = x_ref.shape
    late = [
        pltpu.make_async_copy(a1_in, a1_ref, w_sem.at[1]),
        pltpu.make_async_copy(x_in, x_ref, w_sem.at[2]),
        pltpu.make_async_copy(mid_in, mid_ref, w_sem.at[3]),
    ]
    depth = width // parts
    n = thin_chunks(rows)
    rc = rows // n
    g = Group(size)
    copies = [pltpu.make_async_copy(w_ref, w, w_sem.at[0])]
    for copy in copies + late:
        copy.start()
    g.greet()
    scatter = Scatter(g, rc, scratch)
    for copy in copies:
        copy.wait()

    lag = min(2, n)

    def work(j):
        at = span(j, rc)
        held = flat(dqkv_ref[:, at, :])
        for z in range(parts):
            cols = slice(z * depth, (z + 1) * depth)
            scatter.part[:, at, cols] = dg(held, w[cols, :], NT).reshape(size, rc, depth)
        scatter.first(j)

        @pl.when(j >= lag)
        def _():
            scatter.second(j - lag)


    run(n, work)
    for j in range(n - lag, n):
        scatter.second(j)
    for copy in late:
        copy.wait()

    def qkv_grad(z):
        cols = pl.ds(pl.multiple_of(z * depth, depth), depth)
        gqkv_ref[z] = dg(flat(a1_ref[:, :, cols]), flat(dqkv_ref[...]), TN).astype(BF)

    run(parts, qkv_grad)
    gain_out[...] = jnp.zeros_like(gain_out)

    def last(j):
        at = span(j, rc)
        dh, dgain = normed_back(
            x_ref[at, :].astype(F32), gain_ref[layer, 0:1, :], scatter.third(j)
        )
        dx_ref[at, :] = (mid_ref[at, :] + dh).astype(BF)
        gain_out[...] += dgain

    run(n, last)
    scatter.drain(n)


def qkv_backward(size, replicas, layer, dqkv, a1, x, mid, gains, w):
    rows, width = x.shape
    wide = w.shape[1]
    parts, depth = replicas, width // replicas
    n = thin_chunks(rows)
    return pl.pallas_call(
        functools.partial(qkv_back_kernel, size, layer, parts),
        out_shape=(
            shape((rows, width), BF),
            shape((1, width), F32),
            shape((parts, depth, wide), BF),
        ),
        in_specs=[VM, VM] + [HB] * 4,
        out_specs=(VM, VM, VM),
        scratch_shapes=[
            pltpu.VMEM((size, rows, width), BF),
            pltpu.VMEM((rows, width), BF),
            pltpu.VMEM((rows, width), F32),
            pltpu.VMEM((width, wide), BF),
            DMA((4,)),
        ]
        + scatter_scratch(size, rows, width, n),
        compiler_params=params(11),
        cost_estimate=cost(30e9, 30e6),
    )(dqkv, gains, a1, x, mid, w)


def last_kernel(
    size, parts, dqkv_ref, a1_ref, x_ref, mid_ref, gain_ref, w_ref, two_ref, above_ref, dx1_ref,
    gain_out, gqkv_out, dx_out,
    gqkv, swap_sem, w, dx, gsum, gcame, w_sem, x_sem, x_send, x_recv, g_send, g_recv, *scratch
):
    rows, width = x_ref.shape
    depth = width // parts
    n = thin_chunks(rows)
    rc = rows // n
    g = Group(size)
    section = lax.axis_index("section")
    d = lax.axis_index("dp")
    copy = pltpu.make_async_copy(w_ref, w, w_sem.at[0])
    copy.start()
    reduce = HalfReduce(0, scratch[:HALF])
    swap = HalfSwap(gqkv, reduce.other, swap_sem)
    scatter = Scatter(g, rc, scratch[HALF:])
    g.greet(parts)

    def upper():
        return far_copy(
            dx1_ref, dx_out.at[0], x_send.at[n], x_recv.at[n], {"section": 1 - section}
        )

    def keep_upper():
        return pltpu.make_async_copy(dx1_ref, dx_out.at[1], x_sem.at[0])

    def lower(j):
        at = span(j, rc)
        return far_copy(
            dx.at[at], dx_out.at[1, at], x_send.at[j], x_recv.at[j], {"section": 1 - section}
        )

    def keep_lower(j):
        at = span(j, rc)
        return pltpu.make_async_copy(dx.at[at], dx_out.at[0, at], x_sem.at[j])

    def qkv_grad(z):
        cols = pl.ds(pl.multiple_of(z * depth, depth), depth)
        gqkv[z] = dg(flat(a1_ref[:, :, cols]), flat(dqkv_ref[...]), TN).astype(BF)

    run(parts, qkv_grad)
    swap.copy().start()
    load = reduce.loads(gqkv, None)[0]
    load.start()

    @pl.when(section == 1)
    def _():
        keep_upper().start()

    copy.wait()

    lag = min(2, n)

    def work(j):
        at = span(j, rc)
        held = flat(dqkv_ref[:, at, :])
        for z in range(parts):
            cols = slice(z * depth, (z + 1) * depth)
            scatter.part[:, at, cols] = dg(held, w[cols, :], NT).reshape(size, rc, depth)
        scatter.first(j)

        @pl.when(j >= lag)
        def _():
            scatter.second(j - lag)


    run(n, work)
    for j in range(n - lag, n):
        scatter.second(j)
    gsum[0] = jnp.zeros_like(gsum[0])

    def last(j):
        at = span(j, rc)
        dh, dgain = normed_back(x_ref[at, :].astype(F32), gain_ref[0, 0:1, :], scatter.third(j))
        dx[at, :] = (mid_ref[at, :] + dh).astype(BF)

        @pl.when(section == 0)
        def _():
            keep_lower(j).start()

        @pl.when(section == 1)
        def _():
            lower(j).start()

        gsum[0, 0:1, :] += dgain

    def rest(j):
        @pl.when(j == n // 2)
        def _():
            load.wait()
            swap.copy().wait_recv()
            reduce.middle()

            @pl.when(section == 0)
            def _():
                upper().start()

        last(j)

    run(n, rest)
    gsum[0, 1:2, :] = two_ref[...]
    gsum[0, 2:4, :] = above_ref[...]

    targets = [
        [{"tensor": g.sibling}],
        [{"tensor": g.ahead(k) * 2 + g.core} for k in range(1, g.chips)],
        [{"dp": lax.rem(d + k, parts)} for k in range(1, parts)],
        [{"section": 1 - section}],
    ]
    slot = 0
    sent = []

    def exchange(stage):
        nonlocal slot
        copies = []
        for target in targets[stage]:
            copies.append(
                far_copy(gsum.at[stage], gcame.at[slot], g_send.at[slot], g_recv.at[slot], target)
            )
            copies[-1].start()
            slot += 1
        total = gsum[stage]
        for i, copy in enumerate(copies):
            copy.wait_recv()
            total = total + gcame[slot - len(copies) + i]
        gsum[stage + 1] = total
        sent.extend(copies)

    exchange(0)
    exchange(1)
    reduce.late()
    exchange(2)
    exchange(3)
    gain_out[...] = gsum[4]

    @pl.when(section == 0)
    def _():
        for j in range(n):
            lower(j).wait_recv()
            keep_lower(j).wait()
        upper().wait_send()

    @pl.when(section == 1)
    def _():
        keep_upper().wait()
        upper().wait_recv()
        for j in range(n):
            lower(j).wait_send()

    reduce.finish(gqkv_out)
    swap.copy().wait_send()
    for copy in sent:
        copy.wait_send()
    scatter.drain(n)


def last_backward(size, replicas, dqkv, a1, x, mid, gains, w, two, above, dx1):
    rows, width = x.shape
    wide = w.shape[1]
    depth = width // replicas
    n = thin_chunks(rows)
    slots = 1 + (size // 2 - 1) + (replicas - 1) + 1
    return pl.pallas_call(
        functools.partial(last_kernel, size, replicas),
        out_shape=(
            shape((8, width), F32),
            shape((depth, wide), F32),
            shape((2, rows, width), BF),
        ),
        in_specs=[VM] * 5 + [HB, VM, VM, VM],
        out_specs=(VM, VM, HB),
        scratch_shapes=[
            pltpu.VMEM((replicas, depth, wide), BF),
            DMA((2,)),
            pltpu.VMEM((width, wide), BF),
            pltpu.VMEM((rows, width), BF),
            pltpu.VMEM((5, 8, width), F32),
            pltpu.VMEM((slots, 8, width), F32),
            DMA((1,)),
            DMA((n,)),
            DMA((n + 1,)),
            DMA((n + 1,)),
            DMA((slots,)),
            DMA((slots,)),
        ]
        + half_scratch(replicas, depth, wide)
        + scatter_scratch(size, rows, width, n),
        compiler_params=params(10),
        cost_estimate=cost(40e9, 30e6),
    )(dqkv, a1, x, mid, gains, w, two, above, dx1)


def scene_masks(segments, e):
    same = (segments[..., None] == jnp.arange(e, dtype=jnp.int32)).astype(F32)
    used = jnp.arange(e) < SCENES
    return (
        jnp.where(used, same * MASKED, 0.0).astype(BF),
        jnp.where(used, 1.0 - same, 0.0).astype(BF),
    )


def swap_section(value):
    return lax.ppermute(value, "section", [(0, 1), (1, 0)])


def shards(
    block_input,
    segment_ids,
    cotangent,
    norm_one_gain,
    qkv_weight,
    out_weight,
    norm_two_gain,
    up_weight,
    down_weight,
):
    section = lax.axis_index("section")
    size = lax.axis_size("tensor")
    replicas = lax.axis_size("dp")

    mine = [
        qkv_weight[0].reshape((qkv_weight.shape[1], -1)),
        out_weight[0].reshape((-1, out_weight.shape[3])),
        up_weight[0],
        down_weight[0],
    ]
    mine = [w.astype(BF).reshape((2, -1, w.shape[1])) for w in mine]
    gains = jnp.concatenate(
        [norm_one_gain, norm_two_gain, jnp.zeros((6, norm_one_gain.shape[1]), F32)], axis=0
    )
    segments = lax.dynamic_index_in_dim(segment_ids, section, 0, keepdims=False)
    head_dim = qkv_weight.shape[3] // 3
    qm, km = scene_masks(segments.reshape((size, -1)), head_dim)
    qkv, gains, x, a1, w_qkv_0, w_out_0, h_qkv, h_out, h_up, h_down = first_forward(
        size, replicas, block_input, gains, mine
    )
    h1, ctx, lse, w_up_0, w_down_0 = attend(
        size, replicas, 0, qkv, qm, km, x, w_out_0,
        [(h_up, "spread", 0, False), (h_down, "spread", 0, True)],
    )
    below = (x, a1, qkv, ctx, lse, h1)
    y0, qkv, a2, hid, slope, a1, w_qkv_1, w_out_1, w_up_1 = turn_forward(
        size, replicas, h1, gains, w_up_0, w_down_0, h_qkv,
        [(h_out, "spread", 1, True), (h_up, "spread", 1, False)],
    )
    kept = [below + (a2, hid, slope)]
    h1, ctx, lse, grad_all, w_down_1 = attend(
        size, replicas, 1, qkv, qm, km, y0, w_out_1, [(h_down, "spread", 1, True)], [cotangent]
    )
    kept.append((y0, a1, qkv, ctx, lse, h1))
    weights = [
        (w_qkv_0, w_out_0, w_up_0, w_down_0),
        (w_qkv_1, w_out_1, w_up_1, w_down_1),
    ]
    def reduce_rows(value):
        return lax.psum_scatter(value, "dp", scatter_dimension=0, tiled=False)

    x, a1, qkv, ctx, lse, h1 = kept[1]
    w_qkv, w_out, w_up, w_down = weights[1]
    mid, gain_two, g_up, g_down, hid = peak(size, replicas, h1, gains, grad_all, w_up, w_down)
    d_qkv, out_1, y1 = attend_backward(
        size, replicas, 1, mid, qkv, qm, km, ctx, lse, w_out, [], [hid, w_down, h1]
    )
    up_1, down_1 = reduce_rows(g_up), reduce_rows(g_down)
    dx1, gain_one, g_qkv = qkv_backward(size, replicas, 1, d_qkv, a1, x, mid, gains, w_qkv)
    gains_above = jnp.concatenate([gain_one, gain_two], axis=0)
    dx1, up_1, down_1 = lax.optimization_barrier((dx1, up_1, down_1))
    qkv_1 = reduce_rows(g_qkv)

    x, a1, qkv, ctx, lse, h1, a2, hid, slope = kept[0]
    w_qkv, w_out, w_up, w_down = weights[0]
    mid, gain_two, g_up, g_down, layer_out = mlp_backward(
        size, replicas, 0, dx1, h1, gains, a2, hid, slope, w_up, w_down, [y0, y1]
    )
    mid, qkv_1 = lax.optimization_barrier((mid, qkv_1))
    d_qkv, out_0, down_0 = attend_backward(
        size, replicas, 0, mid, qkv, qm, km, ctx, lse, w_out, [g_down]
    )
    up_0 = reduce_rows(g_up)
    d_qkv, up_0 = lax.optimization_barrier((d_qkv, up_0))
    gains, qkv_0, input_out = last_backward(
        size, replicas, d_qkv, a1, x, mid, gains, w_qkv, gain_two, gains_above, dx1
    )

    def finish(zero, one):
        send = swap_section(jnp.where(section == 0, one, zero))
        return jnp.where(section == 0, zero, one).astype(F32) + send.astype(F32)

    other_qkv_1 = swap_section(qkv_1)
    qkv_grad = jnp.where(section == 0, qkv_0, qkv_1.astype(F32) + other_qkv_1.astype(F32))
    out_grad = jnp.where(section == 0, out_0, out_1)
    up_grad = finish(up_0, up_1)
    other_down_1 = swap_section(down_1)
    down_grad = jnp.where(section == 0, down_0, down_1.astype(F32) + other_down_1.astype(F32))
    gains = lax.dynamic_slice_in_dim(gains, 2 * section, 2, 0)
    return (
        layer_out[None],
        input_out[None],
        gains[0:1],
        qkv_grad.reshape(qkv_weight.shape),
        out_grad.reshape(out_weight.shape),
        gains[1:2],
        up_grad[None],
        down_grad[None],
    )


def solution(mesh):
    return jax.shard_map(
        shards,
        mesh=mesh,
        in_specs=(
            P(None, ("dp", "tensor"), None),
            P(None, "dp"),
            P(None, ("dp", "tensor"), None),
            P("section", None),
            P("section", "dp", "tensor", None),
            P("section", "tensor", None, "dp"),
            P("section", None),
            P("section", "dp", "tensor"),
            P("section", "tensor", "dp"),
        ),
        out_specs=(
            P("section", None, ("dp", "tensor"), None),
            P("section", None, ("dp", "tensor"), None),
            P("section", None),
            P("section", "dp", "tensor", None),
            P("section", "tensor", None, "dp"),
            P("section", None),
            P("section", "dp", "tensor"),
            P("section", "tensor", "dp"),
        ),
        check_vma=False,
    )
```

```python
import functools
import math

import jax
import jax.numpy as jnp
from jax import lax
from jax.experimental import pallas as pl
from jax.experimental.pallas import tpu as pltpu
from jax.sharding import PartitionSpec as P

F32 = jnp.float32
BF = jnp.bfloat16
NT = (((1,), (1,)), ((), ()))
NN = (((1,), (0,)), ((), ()))
TN = (((0,), (0,)), ((), ()))
MASKED = -1e30
SCENES = 3
MESH = pl.DeviceIdType.MESH
VM = pl.BlockSpec(memory_space=pltpu.VMEM)
HB = pl.BlockSpec(memory_space=pl.ANY)
DMA = pltpu.SemaphoreType.DMA
LIMIT = 58 << 20


def dg(a, b, dims):
    return lax.dot_general(a, b, dims, preferred_element_type=F32)


def chunks(rows):
    return 4 if rows % 64 == 0 else 1


def thin_chunks(rows):
    return 8 if rows % 128 == 0 else chunks(rows)


def shape(dims, dtype):
    return jax.ShapeDtypeStruct(dims, dtype)


class Group:
    def __init__(self, size):
        self.size = size
        self.chips = size // 2
        self.me = lax.axis_index("tensor")
        self.chip = lax.div(self.me, 2)
        self.core = lax.rem(self.me, 2)
        self.sibling = self.chip * 2 + 1 - self.core

    def ahead(self, k):
        return lax.rem(self.chip + k, self.chips)

    def behind(self, k):
        return lax.rem(self.chip + self.chips - k, self.chips)

    def greet(self, replicas=0, side=False):
        barrier = pltpu.get_barrier_semaphore()
        targets = [self.sibling] + [self.ahead(k) * 2 + self.core for k in range(1, self.chips)]
        targets = [{"tensor": target} for target in targets]
        if replicas:
            d = lax.axis_index("dp")
            targets += [{"dp": lax.rem(d + k, replicas)} for k in range(1, replicas)]
        if replicas or side:
            targets += [{"section": 1 - lax.axis_index("section")}]
        for target in targets:
            pl.semaphore_signal(barrier, inc=1, device_id=target, device_id_type=MESH)
        pl.semaphore_wait(barrier, len(targets))


def remote(src, dst, send, recv, target):
    return pltpu.make_async_remote_copy(
        src_ref=src,
        dst_ref=dst,
        send_sem=send,
        recv_sem=recv,
        device_id={"tensor": target},
        device_id_type=MESH,
    )


def span(j, rc):
    return pl.ds(pl.multiple_of(j * rc, rc), rc)


def comm_sems(group_size, n):
    c = group_size // 2
    far, near = DMA((max(c - 1, 1), n)), DMA((c, n))
    return [far, far, near, near]


class Gather:
    def __init__(self, g, buf, rc, sems):
        self.g, self.buf, self.rc = g, buf, rc
        self.far_send, self.far_recv, self.near_send, self.near_recv = sems

    def far(self, k, j, origin, target, src=None):
        ref = self.buf.at[origin, span(j, self.rc)]
        src = ref if src is None else src
        return remote(src, ref, self.far_send.at[k - 1, j], self.far_recv.at[k - 1, j], target)

    def near(self, k, j, origin, src=None):
        ref = self.buf.at[origin, span(j, self.rc)]
        src = ref if src is None else src
        return remote(
            src, ref, self.near_send.at[k, j], self.near_recv.at[k, j], self.g.sibling
        )

    def start(self, j, src=None):
        g = self.g
        for k in range(1, g.chips):
            self.far(k, j, g.me, g.ahead(k) * 2 + g.core, src).start()
        self.near(0, j, g.me, src).start()

    def relay(self, j):
        g = self.g
        for k in range(1, g.chips):
            origin = g.behind(k) * 2 + g.core
            self.far(k, j, origin, g.me).wait_recv()
            self.near(k, j, origin).start()

    def ready(self, j):
        g = self.g
        self.near(0, j, g.sibling).wait_recv()
        for k in range(1, g.chips):
            self.near(k, j, g.behind(k) * 2 + 1 - g.core).wait_recv()

    def drain(self, n):
        g = self.g

        def one(j, _):
            for k in range(1, g.chips):
                self.far(k, j, g.me, g.sibling).wait_send()
            for k in range(g.chips):
                self.near(k, j, g.me).wait_send()
            return 0

        lax.fori_loop(0, n, one, 0)


def scatter_scratch(group_size, rows, width, n):
    c = group_size // 2
    far = pltpu.VMEM((max(c - 1, 1), rows, width), BF)
    near = pltpu.VMEM((c, rows, width), BF)
    return [pltpu.VMEM((group_size, rows, width), F32), near, near, far, far] + comm_sems(
        group_size, n
    )


class Scatter:
    def __init__(self, g, rc, scratch):
        self.g, self.rc = g, rc
        self.part, self.near_out, self.near_in, self.far_out, self.far_in = scratch[:5]
        self.far_send, self.far_recv, self.near_send, self.near_recv = scratch[5:]

    def near(self, k, j):
        rows = span(j, self.rc)
        return remote(
            self.near_out.at[k, rows],
            self.near_in.at[k, rows],
            self.near_send.at[k, j],
            self.near_recv.at[k, j],
            self.g.sibling,
        )

    def far(self, k, j):
        rows = span(j, self.rc)
        return remote(
            self.far_out.at[k - 1, rows],
            self.far_in.at[k - 1, rows],
            self.far_send.at[k - 1, j],
            self.far_recv.at[k - 1, j],
            self.g.ahead(k) * 2 + self.g.core,
        )

    def first(self, j):
        g, rows = self.g, span(j, self.rc)
        for k in list(range(1, g.chips)) + [0]:
            owner = g.ahead(k) * 2 + 1 - g.core
            self.near_out[k, rows, :] = self.part[owner, rows, :].astype(BF)
            self.near(k, j).start()

    def second(self, j):
        g, rows = self.g, span(j, self.rc)
        for k in range(1, g.chips):
            owner = g.ahead(k) * 2 + g.core
            self.near(k, j).wait_recv()
            both = self.part[owner, rows, :] + self.near_in[k, rows, :].astype(F32)
            self.far_out[k - 1, rows, :] = both.astype(BF)
            self.far(k, j).start()

    def third(self, j):
        g, rows = self.g, span(j, self.rc)
        self.near(0, j).wait_recv()
        total = self.part[g.me, rows, :] + self.near_in[0, rows, :].astype(F32)
        for k in range(1, g.chips):
            self.far(k, j).wait_recv()
            total = total + self.far_in[k - 1, rows, :].astype(F32)
        return total

    def drain(self, n):
        g = self.g

        def one(j, _):
            for k in range(1, g.chips):
                self.far(k, j).wait_send()
            for k in range(g.chips):
                self.near(k, j).wait_send()
            return 0

        lax.fori_loop(0, n, one, 0)


def far_copy(src, dst, send, recv, target):
    return pltpu.make_async_remote_copy(
        src_ref=src,
        dst_ref=dst,
        send_sem=send,
        recv_sem=recv,
        device_id=target,
        device_id_type=MESH,
    )


class Swap:
    def __init__(self, src, stage, sems):
        self.src, self.stage, self.sems = src, stage, sems
        self.s = lax.axis_index("section")

    def copies(self, layer):
        local = pltpu.make_async_copy(self.src.at[self.s], self.stage.at[self.s], self.sems.at[0])
        side = far_copy(
            self.src.at[1 - self.s],
            self.stage.at[layer],
            self.sems.at[1],
            self.sems.at[2],
            {"section": 1 - self.s},
        )
        return local, side

    def start(self):
        for copy in self.copies(self.s):
            copy.start()

    def arrive(self):
        local, side = self.copies(1 - self.s)
        local.wait()
        side.wait_recv()

    def finish(self):
        self.copies(self.s)[1].wait_send()


def reduce_scratch(replicas, rows, cols):
    many = pltpu.VMEM((replicas - 1, rows, cols), BF)
    one = pltpu.VMEM((rows, cols), BF)
    far, side = DMA((replicas - 1, 2)), DMA((2,))
    return [pltpu.VMEM((rows, cols), F32), many, many, one, one, far, far, side, side]


class Reduce:
    def __init__(self, layer, scratch):
        self.layer = layer
        self.own, self.away, self.came, self.over, self.back = scratch[:5]
        self.z_send, self.z_recv, self.y_send, self.y_recv = scratch[5:]
        self.replicas = self.away.shape[0] + 1
        self.half = self.own.shape[0] // 2
        self.d = lax.axis_index("dp")
        self.s = lax.axis_index("section")

    def target(self, k):
        return lax.rem(self.d + k, self.replicas)

    def part(self, i):
        return pl.ds(pl.multiple_of(i * self.half, self.half), self.half)

    def z_copy(self, k, i):
        part = self.part(i)
        return far_copy(
            self.away.at[k - 1, part],
            self.came.at[k - 1, part],
            self.z_send.at[k - 1, i],
            self.z_recv.at[k - 1, i],
            {"dp": self.target(k)},
        )

    def y_copy(self, i):
        part = self.part(i)
        return far_copy(
            self.over.at[part],
            self.back.at[part],
            self.y_send.at[i],
            self.y_recv.at[i],
            {"section": 1 - self.s},
        )

    def send(self, block):
        def one(i):
            k = i + 1
            self.away[i] = block(self.target(k)).astype(BF)
            self.z_copy(k, 0).start()
            self.z_copy(k, 1).start()

        run(self.replicas - 1, one)
        self.own[...] = block(self.d)

    def collect(self):
        def one(i):
            part = self.part(i)
            total = self.own[part, :]
            for k in range(1, self.replicas):
                self.z_copy(k, i).wait_recv()
                total = total + self.came[k - 1, part, :].astype(F32)
            self.own[part, :] = total
            self.over[part, :] = total.astype(BF)

            @pl.when(self.s != self.layer)
            def _():
                self.y_copy(i).start()

        run(2, one)

    def finish(self, out):
        @pl.when(self.s == self.layer)
        def _():
            self.y_copy(0).wait_recv()
            self.y_copy(1).wait_recv()
            out[...] = self.own[...] + self.back[...].astype(F32)

        @pl.when(self.s != self.layer)
        def _():
            self.y_copy(0).wait_send()
            self.y_copy(1).wait_send()
            out[...] = self.own[...]

        for k in range(1, self.replicas):
            self.z_copy(k, 0).wait_send()
            self.z_copy(k, 1).wait_send()


class HalfSwap:
    def __init__(self, src, came, sems):
        self.src, self.came, self.sems = src, came, sems
        self.s = lax.axis_index("section")
        self.rows = came.shape[1]

    def copy(self):
        at = pl.ds(pl.multiple_of((1 - self.s) * self.rows, self.rows), self.rows)
        return far_copy(
            self.src.at[:, at],
            self.came,
            self.sems.at[0],
            self.sems.at[1],
            {"section": 1 - self.s},
        )


def half_scratch(replicas, rows, cols):
    rows = rows // 2
    all_, far = pltpu.VMEM((replicas, rows, cols), BF), pltpu.VMEM((replicas - 1, rows, cols), BF)
    one = pltpu.VMEM((rows, cols), BF)
    z = DMA((replicas - 1,))
    return [all_, all_, far, far, pltpu.VMEM((rows, cols), F32), one, one, DMA((3,)), z, z, DMA((2,))]


HALF = 11


class HalfReduce:
    def __init__(self, layer, scratch):
        self.layer = layer
        self.mine, self.other, self.away, self.came, self.own, self.over, self.back = scratch[:7]
        self.in_sem, self.z_send, self.z_recv, self.y_sem = scratch[7:]
        self.replicas, self.rows = self.mine.shape[:2]
        self.s = lax.axis_index("section")
        self.d = lax.axis_index("dp")

    def half(self, s):
        return pl.ds(pl.multiple_of(s * self.rows, self.rows), self.rows)

    def loads(self, src, other):
        loads = [pltpu.make_async_copy(src.at[:, self.half(self.s)], self.mine, self.in_sem.at[0])]
        if other is not None:
            loads.append(pltpu.make_async_copy(other, self.other, self.in_sem.at[1]))
        return loads

    def z_copy(self, k):
        return far_copy(
            self.away.at[k - 1],
            self.came.at[k - 1],
            self.z_send.at[k - 1],
            self.z_recv.at[k - 1],
            {"dp": lax.rem(self.d + k, self.replicas)},
        )

    def y_copy(self):
        return far_copy(
            self.over, self.back, self.y_sem.at[0], self.y_sem.at[1], {"section": 1 - self.s}
        )

    def middle(self):
        def both(z):
            return self.mine[z].astype(F32) + self.other[z].astype(F32)

        for k in range(1, self.replicas):
            self.away[k - 1] = both(lax.rem(self.d + k, self.replicas)).astype(BF)
            self.z_copy(k).start()
        self.own[...] = both(self.d)

    def late(self):
        total = self.own[...]
        for k in range(1, self.replicas):
            self.z_copy(k).wait_recv()
            total = total + self.came[k - 1].astype(F32)
        self.own[...] = total
        self.over[...] = total.astype(BF)

        @pl.when(self.s != self.layer)
        def _():
            self.y_copy().start()

    def finish(self, out, above=None):
        @pl.when(self.s == self.layer)
        def _():
            self.y_copy().wait_recv()
            out[self.half(self.s), :] = self.own[...]
            out[self.half(1 - self.s), :] = self.back[...].astype(F32)

        @pl.when(self.s != self.layer)
        def _():
            if above is None:
                out[...] = jnp.zeros_like(out)
            else:
                copy = pltpu.make_async_copy(above, out, self.in_sem.at[2])
                copy.start()
                copy.wait()
            self.y_copy().wait_send()

        for k in range(1, self.replicas):
            self.z_copy(k).wait_send()


class Spread:
    def __init__(self, src, dst, by_columns, sems):
        self.src, self.dst, self.by_columns = src, dst, by_columns
        self.own_sem, self.far_send, self.far_recv, self.side_send, self.side_recv = sems
        self.replicas = far = self.side_send.shape[0]
        self.s = lax.axis_index("section")
        self.d = lax.axis_index("dp")
        self.stages = [
            sorted({k, far - k}) for k in range(1, far // 2 + 1)
        ]

    def place(self, half, z):
        rows, cols = self.src.shape
        if self.by_columns:
            return self.dst.at[
                pl.ds(pl.multiple_of(half * rows, rows), rows),
                pl.ds(pl.multiple_of(z * cols, cols), cols),
            ]
        return self.dst.at[pl.ds(pl.multiple_of((2 * z + half) * rows, rows), rows)]

    def origin(self, k):
        return lax.rem(self.d + self.replicas - k, self.replicas)

    def own(self):
        return pltpu.make_async_copy(self.src, self.place(self.s, self.d), self.own_sem.at[0])

    def far(self, k, origin):
        return pltpu.make_async_remote_copy(
            src_ref=self.src,
            dst_ref=self.place(self.s, origin),
            send_sem=self.far_send.at[k - 1],
            recv_sem=self.far_recv.at[k - 1],
            device_id={"dp": lax.rem(self.d + k, self.replicas)},
            device_id_type=MESH,
        )

    def side(self, k, half):
        place = self.place(half, self.origin(k))
        return pltpu.make_async_remote_copy(
            src_ref=self.src if k == 0 else place,
            dst_ref=place,
            send_sem=self.side_send.at[k],
            recv_sem=self.side_recv.at[k],
            device_id={"section": 1 - self.s},
            device_id_type=MESH,
        )

    def start(self):
        for k in self.stages[0]:
            self.far(k, self.d).start()
        self.side(0, self.s).start()
        self.own().start()

    def step(self, i):
        for k in self.stages[i]:
            self.far(k, self.origin(k)).wait_recv()
            self.side(k, self.s).start()
        if i + 1 < len(self.stages):
            for k in self.stages[i + 1]:
                self.far(k, self.d).start()

    def finish(self):
        self.own().wait()
        for k in range(self.replicas):
            self.side(k, 1 - self.s).wait_recv()
        for k in range(1, self.replicas):
            self.far(k, self.d).wait_send()
        for k in range(self.replicas):
            self.side(k, self.s).wait_send()


class ZGather:
    def __init__(self, src, got, sems):
        self.src, self.got = src, got
        self.own_sem, self.send, self.recv = sems
        self.replicas = got.shape[0]
        self.d = lax.axis_index("dp")

    def own(self):
        return pltpu.make_async_copy(self.src, self.got.at[self.d], self.own_sem.at[0])

    def far(self, k, origin):
        return far_copy(
            self.src,
            self.got.at[origin],
            self.send.at[k - 1],
            self.recv.at[k - 1],
            {"dp": lax.rem(self.d + k, self.replicas)},
        )

    def start(self):
        for k in range(1, self.replicas):
            self.far(k, self.d).start()
        self.own().start()

    def step(self, i):
        pass

    def finish(self):
        self.own().wait()
        for k in range(1, self.replicas):
            self.far(k, lax.rem(self.d + self.replicas - k, self.replicas)).wait_recv()
        for k in range(1, self.replicas):
            self.far(k, self.d).wait_send()


class YJoin:
    def __init__(self, got, dst, by_columns, sems):
        self.src, self.dst, self.by_columns = got, dst, by_columns
        self.own_sem, self.send, self.recv, self.got, self.in_sem = sems
        self.replicas, self.rows, self.cols = got.shape
        self.s = lax.axis_index("section")

    def place(self, half, z):
        rows, cols = self.rows, self.cols
        if self.by_columns:
            return self.dst.at[
                pl.ds(pl.multiple_of(half * rows, rows), rows), pl.ds(z * cols, cols)
            ]
        return self.dst.at[pl.ds(pl.multiple_of((2 * z + half) * rows, rows), rows)]

    def own(self, z):
        return pltpu.make_async_copy(self.got.at[z], self.place(self.s, z), self.own_sem.at[z])

    def side(self, z, half):
        return far_copy(
            self.got.at[z],
            self.place(half, z),
            self.send.at[z],
            self.recv.at[z],
            {"section": 1 - self.s},
        )

    def start(self):
        load = pltpu.make_async_copy(self.src, self.got, self.in_sem.at[0])
        load.start()
        load.wait()
        for z in range(self.replicas):
            self.side(z, self.s).start()
            self.own(z).start()

    def step(self, i):
        pass

    def finish(self):
        for z in range(self.replicas):
            self.own(z).wait()
            self.side(z, 1 - self.s).wait_recv()
        for z in range(self.replicas):
            self.side(z, self.s).wait_send()


def rider_sems(replicas):
    far, side = DMA((replicas - 1,)), DMA((replicas,))
    return [DMA((1,)), far, far, side, side]


class Riders:
    def __init__(self, srcs, dsts, columns, sems):
        self.all = []
        for src, dst, (kind, layer, by) in zip(srcs, dsts, columns):
            count = 3 if kind == "z" else 5
            own, sems = sems[:count], sems[count:]
            if kind == "spread":
                self.all.append(Spread(src.at[layer], dst, by, own))
            elif kind == "z":
                self.all.append(ZGather(src.at[layer], dst, own))
            else:
                self.all.append(YJoin(src, dst, by, own))
        self.replicas = self.all[0].replicas if self.all else 0

    def start(self):
        for one in self.all:
            one.start()

    def step(self, j, n):
        if not self.all:
            return
        stages = self.replicas // 2
        for i in range(stages):

            @pl.when(j == n * (i + 1) // stages - 1)
            def _(i=i):
                for one in self.all:
                    one.step(i)

    def finish(self):
        for one in self.all:
            one.finish()


def riding(riders, replicas):
    arrays = [array for array, _, _, _ in riders]
    columns = tuple(rider[1:] for rider in riders)
    outs, sems = [], []
    for array, kind, _, by in riders:
        rows, cols = array.shape[1:]
        if kind == "z":
            outs.append(shape((replicas, rows, cols), BF))
        else:
            outs.append(
                shape((2 * rows, replicas * cols) if by else (2 * replicas * rows, cols), BF)
            )
        far, side = DMA((replicas - 1,)), DMA((replicas,))
        sems += {
            "spread": rider_sems(replicas),
            "z": [DMA((1,)), far, far],
            "y": [side, side, side, pltpu.VMEM(array.shape, BF), DMA((1,))],
        }[kind]
    return arrays, columns, outs, sems


def params(key):
    return pltpu.CompilerParams(
        vmem_limit_bytes=LIMIT, collective_id=key, has_side_effects=True
    )


def cost(flops, moved, exps=0):
    return pl.CostEstimate(flops=int(flops), bytes_accessed=int(moved), transcendentals=int(exps))


def normed(source):
    center = source - jnp.mean(source, axis=-1, keepdims=True)
    r = lax.rsqrt(jnp.mean(center * center, axis=-1, keepdims=True) + 1e-05)
    return center * r, r


def normed_back(source, gain, grad):
    n, r = normed(source)
    e = grad * gain
    dh = r * (
        e - jnp.mean(e, axis=-1, keepdims=True) - n * jnp.mean(e * n, axis=-1, keepdims=True)
    )
    return dh, jnp.sum(grad * n, axis=0, keepdims=True)


def flat(value):
    return value.reshape((value.shape[0] * value.shape[1],) + value.shape[2:])


def run(n, body):
    def one(j, carry):
        body(j)
        return carry

    lax.fori_loop(0, n, one, 0)


def first_kernel(
    size, replicas, x_in, gain_ref, wq_ref, wo_ref, wu_ref, wd_ref,
    qkv_ref, gains_out, x_ref, a1_out, wq_out, wo_out, q_stage, o_stage, u_stage, d_stage,
    a1, w, gains, own_sem, q_sem, o_sem, u_sem, d_sem, gain_sem, *sems
):
    rows, width = x_ref.shape
    n = thin_chunks(rows)
    rc = rows // n
    g = Group(size)
    section = lax.axis_index("section")
    x_load = pltpu.make_async_copy(x_in.at[section], x_ref, own_sem.at[2])
    x_load.start()
    gather = Gather(g, a1, rc, sems[:4])
    swaps = [
        Swap(wq_ref, q_stage, q_sem),
        Swap(wo_ref, o_stage, o_sem),
        Swap(wu_ref, u_stage, u_sem),
        Swap(wd_ref, d_stage, d_sem),
    ]
    spreads = [
        Spread(q_stage.at[0], w, False, sems[4:9]),
        Spread(o_stage.at[0], wo_out, True, sems[9:14]),
    ]
    g.greet(replicas)

    def gain_copy(layer):
        return far_copy(
            gain_ref, gains.at[layer], gain_sem.at[0], gain_sem.at[1], {"section": 1 - section}
        )

    gain_copy(section).start()
    swaps[0].start()
    swaps[1].start()
    gains[section] = gain_ref[...]
    gain_copy(1 - section).wait_recv()
    gains_out[...] = gains[...]
    x_load.wait()

    def send(j):
        at = span(j, rc)
        a = normed(x_ref[at, :].astype(F32))[0] * gains[0, 0:1, :]
        a1[g.me, at, :] = a.astype(BF)
        gather.start(j)

    run(n, send)
    swaps[0].arrive()
    swaps[1].arrive()
    for one in spreads:
        one.start()
    stages = len(spreads[0].stages)

    def relay(j):
        gather.relay(j)

        for i in range(stages):

            @pl.when(j == n * (i + 1) // stages - 1)
            def _(i=i):
                for one in spreads:
                    one.step(i)

    run(n, relay)
    swaps[2].start()
    swaps[3].start()
    for one in spreads:
        one.finish()
    outs = [
        pltpu.make_async_copy(w, wq_out, own_sem.at[0]),
        pltpu.make_async_copy(a1, a1_out, own_sem.at[1]),
    ]
    outs[0].start()

    def multiply(j):
        at = span(j, rc)
        gather.ready(j)
        r = dg(flat(a1[:, at, :]), w[...], NN).astype(BF)
        qkv_ref[:, at, :] = r.reshape(size, rc, r.shape[1])

    run(n, multiply)
    outs[1].start()
    swaps[2].arrive()
    swaps[3].arrive()
    for swap in swaps:
        swap.finish()
    gain_copy(section).wait_send()
    gather.drain(n)
    for out in outs:
        out.wait()


def first_forward(size, replicas, x, gains, ws):
    _, rows, width = x.shape
    wide = ws[0].shape[2]
    deep = 2 * ws[1].shape[1]
    n = thin_chunks(rows)
    return pl.pallas_call(
        functools.partial(first_kernel, size, replicas),
        out_shape=[
            shape((size, rows, wide), BF),
            shape((2,) + gains.shape, F32),
            shape((rows, width), BF),
            shape((size, rows, width), BF),
            shape((width, wide), BF),
            shape((deep, width), BF),
        ]
        + [shape(w.shape, BF) for w in ws],
        in_specs=[HB] + [VM] * 5,
        out_specs=[VM, VM, VM] + [HB] * 7,
        scratch_shapes=[
            pltpu.VMEM((size, rows, width), BF),
            pltpu.VMEM((width, wide), BF),
            pltpu.VMEM((2,) + gains.shape, F32),
            DMA((3,)),
            DMA((3,)),
            DMA((3,)),
            DMA((3,)),
            DMA((3,)),
            DMA((2,)),
        ]
        + comm_sems(size, n)
        + rider_sems(replicas) * 2,
        compiler_params=params(0),
        cost_estimate=cost(30e9, 30e6),
    )(x, gains, *ws)


def attend_kernel(size, layer, columns, *refs):
    m = len(columns)
    qkv_ref, qm_ref, km_ref, x_ref, w_ref = refs[:5]
    refs = refs[5:]
    if layer == 1:
        cot_ref, refs = refs[0], refs[1:]
    halves, refs = refs[:m], refs[m:]
    h1_ref, ctx_ref, lse_ref = refs[:3]
    refs = refs[3:]
    if layer == 1:
        cot_out, refs = refs[0], refs[1:]
    wholes, refs = refs[:m], refs[m:]
    ka, vt, w, w_sem = refs[:4]
    scratch, refs = refs[4:13], refs[13:]
    if layer == 1:
        cot_sems, cot_sem, cot_mine, refs = refs[:4], refs[4], refs[5], refs[6:]
        cot_load = pltpu.make_async_copy(
            cot_ref.at[lax.axis_index("section")], cot_mine, cot_sem.at[1]
        )
        cot_load.start()
    riders = Riders(halves, wholes, columns, refs)
    _, rows, wide = qkv_ref.shape
    length = size * rows
    e = qm_ref.shape[2]
    heads = wide // (3 * e)
    c = e**-0.5 * math.log2(math.e)
    n = chunks(rows)
    rc = rows // n
    bq = size * rc
    kc = bq
    g = Group(size)
    copy = pltpu.make_async_copy(w_ref, w, w_sem.at[0])
    copy.start()
    g.greet(riders.replicas)
    riders.start()
    if layer == 1:
        cot = Gather(g, cot_out, rows, cot_sems)
        own = pltpu.make_async_copy(cot_mine, cot_out.at[g.me], cot_sem.at[0])
        cot_load.wait()
        own.start()
        cot.start(0, cot_mine)
    scatter = Scatter(g, rc, scratch)
    whole = flat(qkv_ref[...])
    for h in range(heads):
        o = 3 * e * h
        ka[h, :, :e] = whole[:, o + e : o + 2 * e]
        ka[h, :, e:] = flat(km_ref[...])
        vt[h, :e, :] = whole[:, o + 2 * e : o + 3 * e].T
        vt[h, e:, :] = jnp.ones((16, length), BF)
    copy.wait()

    def work(j):
        at = span(j, rc)
        qm = flat(qm_ref[:, at, :])
        found = []
        held_qkv = flat(qkv_ref[:, at, :])
        for h in range(heads):
            o = 3 * e * h
            q = jnp.concatenate([held_qkv[:, o : o + e], qm], axis=1)
            held = []
            top = None
            for k in range(length // kc):
                s = dg(ka[h, k * kc : (k + 1) * kc, :], q, NT)
                t = jnp.max(s, axis=0, keepdims=True)
                top = t if top is None else jnp.maximum(top, t)
                held.append(s)
            top = top * c
            acc = None
            for k in range(length // kc):
                p = jnp.exp2(held[k] * c - top).astype(BF)
                a = dg(vt[h, :, k * kc : (k + 1) * kc], p, NN)
                acc = a if acc is None else acc + a
            total = acc[e : e + 1]
            found.append((acc[:e] * (1.0 / total)).astype(BF))
            lse_ref[j, h : h + 1, :] = top + jnp.log2(total)
            if h == heads // 2:

                @pl.when(j > 0)
                def _():
                    scatter.second(j - 1)

        ctx = (jnp.concatenate(found, axis=0) if heads > 1 else found[0]).T
        ctx_ref[:, at, :] = ctx.reshape(size, rc, heads * e)
        width = x_ref.shape[1]
        scatter.part[:, at, :] = dg(ctx, w[...], NN).reshape(size, rc, width)
        scatter.first(j)
        riders.step(j, n)
        if layer == 1:

            @pl.when(j == n - 1)
            def _():
                cot.relay(0)

    run(n, work)
    scatter.second(n - 1)

    def last(j):
        at = span(j, rc)
        h1_ref[at, :] = x_ref[at, :].astype(F32) + scatter.third(j)

    run(n, last)
    scatter.drain(n)
    if layer == 1:
        cot.ready(0)
        cot.drain(1)
        own.wait()
    riders.finish()


def attend(size, replicas, layer, qkv, qm, km, x, w, riders, cot=()):
    _, rows, wide = qkv.shape
    e = qm.shape[2]
    heads = wide // (3 * e)
    width = x.shape[1]
    n = chunks(rows)
    halves, columns, outs, sems = riding(riders, replicas)
    return pl.pallas_call(
        functools.partial(attend_kernel, size, layer, columns),
        out_shape=[
            shape((rows, width), F32),
            shape((size, rows, heads * e), BF),
            shape((n, heads, size * rows // n), F32),
        ]
        + [shape((size, rows, width), BF) for _ in cot]
        + outs,
        in_specs=[VM, VM, VM, VM, HB] + [HB] * (len(cot) + len(riders)),
        out_specs=[VM, VM, VM] + [HB] * (len(cot) + len(outs)),
        scratch_shapes=[
            pltpu.VMEM((heads, size * rows, 2 * e), BF),
            pltpu.VMEM((heads, e + 16, size * rows), BF),
            pltpu.VMEM((heads * e, width), BF),
            DMA((1,)),
        ]
        + scatter_scratch(size, rows, width, n)
        + (comm_sems(size, 1) + [DMA((2,)), pltpu.VMEM((rows, width), BF)]) * len(cot)
        + sems,
        compiler_params=params(2 + layer),
        cost_estimate=cost(60e9, 20e6),
    )(qkv, qm, km, x, w, *cot, *halves)


def peak_kernel(
    size, parts, h1_ref, gain_ref, grad_ref, wu_ref, wd_ref,
    mid_ref, gain_out, gup_ref, gdown_ref, hid_out,
    a2, hid, dup, grad, wu, wd, w_sem, out_sem, *scratch
):
    rows, width = h1_ref.shape
    hidden = wu_ref.shape[1]
    depth = width // parts
    fb = min(256, hidden)
    n = chunks(rows)
    rc = rows // n
    g = Group(size)
    copies = [
        pltpu.make_async_copy(wu_ref, wu, w_sem.at[0]),
        pltpu.make_async_copy(wd_ref, wd, w_sem.at[1]),
        pltpu.make_async_copy(grad_ref, grad, w_sem.at[2]),
    ]
    for copy in copies:
        copy.start()
    g.greet()
    gather = Gather(g, a2, rc, scratch[:4])
    scatter = Scatter(g, rc, scratch[4:])

    def send(j):
        at = span(j, rc)
        a = normed(h1_ref[at, :])[0] * gain_ref[1, 1:2, :]
        a2[g.me, at, :] = a.astype(BF)
        gather.start(j)

    run(n, send)
    for copy in copies:
        copy.wait()
    gather.relay(0)

    def work(j):
        at = span(j, rc)
        gather.ready(j)
        a = flat(a2[:, at, :])
        held = flat(grad[:, at, :])
        for f in range(hidden // fb):
            cols = slice(f * fb, (f + 1) * fb)
            u = dg(a, wu[:, cols], NN)
            half = 0.5 + 0.5 * lax.erf(u * (0.5**0.5))
            slope = half + u * jnp.exp(-0.5 * u * u) * ((2 * math.pi) ** -0.5)
            hid[:, at, cols] = (u * half).astype(BF).reshape(size, rc, fb)
            d = dg(held, wd[cols, :], NT) * slope
            dup[:, at, cols] = d.astype(BF).reshape(size, rc, fb)

        @pl.when(j + 1 < n)
        def _():
            gather.relay(j + 1)

        @pl.when(j > 0)
        def _():
            scatter.second(j - 1)

        held = flat(dup[:, at, :])
        for z in range(parts):
            cols = slice(z * depth, (z + 1) * depth)
            scatter.part[:, at, cols] = dg(held, wu[cols, :], NT).reshape(size, rc, depth)
        scatter.first(j)

    run(n, work)
    scatter.second(n - 1)
    out = pltpu.make_async_copy(hid, hid_out, out_sem.at[0])
    out.start()

    def up_grad(z):
        cols = pl.ds(pl.multiple_of(z * depth, depth), depth)
        gup_ref[z] = dg(flat(a2[:, :, cols]), flat(dup[...]), TN).astype(BF)

    run(parts, up_grad)

    def down_grad(f):
        cols = pl.ds(pl.multiple_of(f * fb, fb), fb)
        r = dg(flat(hid[:, :, cols]), flat(grad[...]), TN).astype(BF)
        for z in range(parts):
            gdown_ref[z, cols, :] = r[:, z * depth : (z + 1) * depth]

    run(hidden // fb, down_grad)
    gain_out[...] = jnp.zeros_like(gain_out)

    def last(j):
        at = span(j, rc)
        dh, dgain = normed_back(h1_ref[at, :], gain_ref[1, 1:2, :], scatter.third(j))
        mid_ref[at, :] = grad[g.me, at, :].astype(F32) + dh
        gain_out[...] += dgain

    run(n, last)
    gather.drain(n)
    scatter.drain(n)
    out.wait()


def peak(size, replicas, h1, gains, grad_all, wu, wd):
    rows, width = h1.shape
    hidden = wu.shape[1]
    depth = width // replicas
    n = chunks(rows)
    return pl.pallas_call(
        functools.partial(peak_kernel, size, replicas),
        out_shape=[
            shape((rows, width), F32),
            shape((1, width), F32),
            shape((replicas, depth, hidden), BF),
            shape((replicas, hidden, depth), BF),
            shape((size, rows, hidden), BF),
        ],
        in_specs=[VM, VM, HB, HB, HB],
        out_specs=[VM, VM, VM, VM, HB],
        scratch_shapes=[
            pltpu.VMEM((size, rows, width), BF),
            pltpu.VMEM((size, rows, hidden), BF),
            pltpu.VMEM((size, rows, hidden), BF),
            pltpu.VMEM((size, rows, width), BF),
            pltpu.VMEM((width, hidden), BF),
            pltpu.VMEM((hidden, width), BF),
            DMA((3,)),
            DMA((1,)),
        ]
        + comm_sems(size, n)
        + scatter_scratch(size, rows, width, n),
        compiler_params=params(5),
        cost_estimate=cost(60e9, 30e6),
    )(h1, gains, grad_all, wu, wd)


def turn_kernel(size, columns, *refs):
    m = len(columns)
    h1_ref, gain_ref, wu_ref, wd_ref, q_stage = refs[:5]
    halves, refs = refs[5 : 5 + m], refs[5 + m :]
    y_ref, qkv_ref, a2_out, hid_out, slope_out, a1_out, wq_out = refs[:7]
    wholes, refs = refs[7 : 7 + m], refs[7 + m :]
    a2, hid, slope, wu, wd, a1, wq, w_sem, out_sem = refs[:9]
    gather_sems, next_sems, refs = refs[9:13], refs[13:17], refs[17:]
    scratch, refs = refs[:9], refs[9:]
    spread = Spread(q_stage.at[1], wq, False, refs[:5])
    riders = Riders(halves, wholes, columns, refs[5:])
    out_rider, up_rider = riders.all
    stages = len(spread.stages)
    rows, width = h1_ref.shape
    hidden = wu_ref.shape[1]
    fb = min(256, hidden)
    n = chunks(rows)
    rc = rows // n
    g = Group(size)
    copies = [
        pltpu.make_async_copy(wu_ref, wu, w_sem.at[0]),
        pltpu.make_async_copy(wd_ref, wd, w_sem.at[1]),
    ]
    for copy in copies:
        copy.start()
    g.greet(spread.replicas)
    gather = Gather(g, a2, rc, gather_sems)
    onward = Gather(g, a1, rc, next_sems)
    scatter = Scatter(g, rc, scratch)

    def send(j):
        at = span(j, rc)
        a = normed(h1_ref[at, :])[0] * gain_ref[0, 1:2, :]
        a2[g.me, at, :] = a.astype(BF)
        gather.start(j)

    run(n, send)
    spread.start()
    out_rider.start()
    for copy in copies:
        copy.wait()

    def pass_on(j):
        at = span(j, rc)
        y = (h1_ref[at, :] + scatter.third(j)).astype(BF)
        y_ref[at, :] = y
        a = normed(y.astype(F32))[0] * gain_ref[1, 0:1, :]
        a1[g.me, at, :] = a.astype(BF)
        onward.start(j)

    lag = min(2, n)
    gather.relay(0)

    def work(j):
        at = span(j, rc)
        gather.ready(j)
        a = flat(a2[:, at, :])
        for f in range(hidden // fb):
            cols = slice(f * fb, (f + 1) * fb)
            u = dg(a, wu[:, cols], NN)
            half = 0.5 + 0.5 * lax.erf(u * (0.5**0.5))
            slope[:, at, cols] = (
                (half + u * jnp.exp(-0.5 * u * u) * ((2 * math.pi) ** -0.5))
                .astype(BF)
                .reshape(size, rc, fb)
            )
            hid[:, at, cols] = (u * half).astype(BF).reshape(size, rc, fb)

        @pl.when(j + 1 < n)
        def _():
            gather.relay(j + 1)

        @pl.when(j > 0)
        def _():
            scatter.second(j - 1)

        held = flat(hid[:, at, :])
        for f in range(width // 256):
            cols = slice(f * 256, (f + 1) * 256)
            scatter.part[:, at, cols] = dg(held, wd[:, cols], NN).reshape(size, rc, 256)
        scatter.first(j)

        @pl.when(j >= lag)
        def _():
            pass_on(j - lag)

        @pl.when(j == min(1, n - 1))
        def _():
            spread.step(0)
            out_rider.step(0)

        @pl.when(j == n - 1)
        def _():
            for i in range(1, stages):
                spread.step(i)
                out_rider.step(i)
            up_rider.start()

    run(n, work)
    scatter.second(n - 1)
    outs = [
        pltpu.make_async_copy(a2, a2_out, out_sem.at[0]),
        pltpu.make_async_copy(hid, hid_out, out_sem.at[1]),
        pltpu.make_async_copy(slope, slope_out, out_sem.at[2]),
    ]
    for out in outs:
        out.start()
    for j in range(n - lag, n):
        pass_on(j)
    up_rider.step(0)
    spread.finish()
    outs.append(pltpu.make_async_copy(wq, wq_out, out_sem.at[3]))
    outs[3].start()

    onward.relay(0)

    def multiply(j):
        at = span(j, rc)

        @pl.when(j + 1 < n)
        def _():
            onward.relay(j + 1)

        @pl.when(j == n // 2)
        def _():
            for i in range(1, stages):
                up_rider.step(i)

        onward.ready(j)
        r = dg(flat(a1[:, at, :]), wq[...], NN).astype(BF)
        qkv_ref[:, at, :] = r.reshape(size, rc, r.shape[1])

    run(n, multiply)
    outs.append(pltpu.make_async_copy(a1, a1_out, out_sem.at[4]))
    outs[4].start()
    riders.finish()
    gather.drain(n)
    onward.drain(n)
    scatter.drain(n)
    for out in outs:
        out.wait()


def turn_forward(size, replicas, h1, gains, wu, wd, stage, riders):
    rows, width = h1.shape
    hidden = wu.shape[1]
    wide = stage.shape[2]
    n = chunks(rows)
    halves, columns, outs, sems = riding(riders, replicas)
    return pl.pallas_call(
        functools.partial(turn_kernel, size, columns),
        out_shape=[
            shape((rows, width), BF),
            shape((size, rows, wide), BF),
            shape((size, rows, width), BF),
            shape((size, rows, hidden), BF),
            shape((size, rows, hidden), BF),
            shape((size, rows, width), BF),
            shape((width, wide), BF),
        ]
        + outs,
        in_specs=[VM, VM] + [HB] * (3 + len(riders)),
        out_specs=[VM, VM] + [HB] * (5 + len(outs)),
        scratch_shapes=[
            pltpu.VMEM((size, rows, width), BF),
            pltpu.VMEM((size, rows, hidden), BF),
            pltpu.VMEM((size, rows, hidden), BF),
            pltpu.VMEM((width, hidden), BF),
            pltpu.VMEM((hidden, width), BF),
            pltpu.VMEM((size, rows, width), BF),
            pltpu.VMEM((width, wide), BF),
            DMA((2,)),
            DMA((5,)),
        ]
        + comm_sems(size, n) * 2
        + scatter_scratch(size, rows, width, n)
        + rider_sems(replicas)
        + sems,
        compiler_params=params(4),
        cost_estimate=cost(50e9, 30e6),
    )(h1, gains, wu, wd, stage, *halves)


def mlp_back_kernel(size, layer, parts, *refs):
    g_ref, h1_ref, gain_ref, a2_ref, hid_ref, slope_ref, wu_ref, wd_ref = refs[:8]
    refs = refs[8:]
    ys, refs = refs[:2], refs[2:]
    mid_ref, gain_out, gup_ref, gdown_ref = refs[:4]
    refs = refs[4:]
    y_out, refs = refs[0], refs[1:]
    grad, a2, hid, dup, wu, wd, w_sem = refs[:7]
    scratch, refs = refs[7:20], refs[20:]
    rows, width = h1_ref.shape
    hidden = wu_ref.shape[1]
    depth = width // parts
    fb = min(256, hidden)
    n = chunks(rows)
    rc = rows // n
    g = Group(size)
    copies = [
        pltpu.make_async_copy(wd_ref, wd, w_sem.at[0]),
        pltpu.make_async_copy(slope_ref, dup, w_sem.at[1]),
        pltpu.make_async_copy(wu_ref, wu, w_sem.at[2]),
    ]
    late = [
        pltpu.make_async_copy(hid_ref, hid, w_sem.at[3]),
        pltpu.make_async_copy(a2_ref, a2, w_sem.at[4]),
    ]
    for copy in copies:
        copy.start()
    g.greet(side=True)
    section = lax.axis_index("section")
    y_sem, y_own = refs

    def y_load(own):
        return pltpu.make_async_copy(own, y_own, y_sem.at[3])

    def y_copies(own, other, at):
        return (
            pltpu.make_async_copy(y_own, y_out.at[section], y_sem.at[0]),
            far_copy(
                other, y_out.at[at], y_sem.at[1], y_sem.at[2], {"section": 1 - section}
            ),
        )

    for i in range(2):

        @pl.when(section == i)
        def _(i=i):
            y_load(ys[i]).start()
            y_copies(ys[i], ys[1 - i], section)[1].start()

    gather = Gather(g, grad, rc, scratch[:4])
    scatter = Scatter(g, rc, scratch[4:])

    def send(j):
        at = span(j, rc)
        grad[g.me, at, :] = g_ref[at, :]
        gather.start(j)

    run(n, send)
    for copy in copies:
        copy.wait()
    for copy in late:
        copy.start()
    y_load(ys[0]).wait()
    y_copies(ys[0], ys[1], section)[0].start()

    gather.relay(0)

    def work(j):
        at = span(j, rc)
        gather.ready(j)
        held = flat(grad[:, at, :])
        for f in range(hidden // fb):
            cols = slice(f * fb, (f + 1) * fb)
            d = dg(held, wd[cols, :], NT) * flat(dup[:, at, cols]).astype(F32)
            dup[:, at, cols] = d.astype(BF).reshape(size, rc, fb)

        @pl.when(j + 1 < n)
        def _():
            gather.relay(j + 1)

        @pl.when(j > 0)
        def _():
            scatter.second(j - 1)

        held = flat(dup[:, at, :])
        for z in range(parts):
            cols = slice(z * depth, (z + 1) * depth)
            scatter.part[:, at, cols] = dg(held, wu[cols, :], NT).reshape(size, rc, depth)
        scatter.first(j)

    run(n, work)
    scatter.second(n - 1)
    for copy in late:
        copy.wait()

    def up_grad(z):
        cols = pl.ds(pl.multiple_of(z * depth, depth), depth)
        gup_ref[z] = dg(flat(a2[:, :, cols]), flat(dup[...]), TN).astype(BF)

    run(parts, up_grad)

    def down_grad(f):
        cols = pl.ds(pl.multiple_of(f * fb, fb), fb)
        r = dg(flat(hid[:, :, cols]), flat(grad[...]), TN).astype(BF)
        for z in range(parts):
            gdown_ref[z, cols, :] = r[:, z * depth : (z + 1) * depth]

    run(hidden // fb, down_grad)
    gain_out[...] = jnp.zeros_like(gain_out)

    def last(j):
        at = span(j, rc)
        dh, dgain = normed_back(h1_ref[at, :], gain_ref[layer, 1:2, :], scatter.third(j))
        mid_ref[at, :] = g_ref[at, :].astype(F32) + dh
        gain_out[...] += dgain

    run(n, last)
    local, side = y_copies(ys[0], ys[1], 1 - section)
    local.wait()
    side.wait_recv()
    y_copies(ys[0], ys[1], section)[1].wait_send()
    gather.drain(n)
    scatter.drain(n)


def mlp_backward(size, replicas, layer, grad, h1, gains, a2, hid, slope, wu, wd, extra):
    rows, width = h1.shape
    hidden = wu.shape[1]
    parts, depth = replicas, width // replicas
    n = chunks(rows)
    return pl.pallas_call(
        functools.partial(mlp_back_kernel, size, layer, parts),
        out_shape=[
            shape((rows, width), F32),
            shape((1, width), F32),
            shape((parts, depth, hidden), BF),
            shape((parts, hidden, depth), BF),
        ]
        + [shape((2, rows, width), BF)] * (len(extra) // 2),
        in_specs=[VM, VM, VM] + [HB] * (5 + len(extra)),
        out_specs=[VM, VM, VM, VM] + [HB] * (len(extra) // 2),
        scratch_shapes=[
            pltpu.VMEM((size, rows, width), BF),
            pltpu.VMEM((size, rows, width), BF),
            pltpu.VMEM((size, rows, hidden), BF),
            pltpu.VMEM((size, rows, hidden), BF),
            pltpu.VMEM((width, hidden), BF),
            pltpu.VMEM((hidden, width), BF),
            DMA((6,)),
        ]
        + comm_sems(size, n)
        + scatter_scratch(size, rows, width, n)
        + [DMA((4,)), pltpu.VMEM((rows, width), BF)] * (len(extra) // 2),
        compiler_params=params(6 + layer),
        cost_estimate=cost(60e9, 40e6),
    )(grad, h1, gains, a2, hid, slope, wu, wd, *extra)


def attend_back_kernel(size, layer, parts, *refs):
    mid_ref, qkv_ref, qm_ref, km_ref, ctx_ref, lse_ref, w_ref = refs[:7]
    refs = refs[7:]
    if layer == 0:
        gdown_ref, refs = refs[0], refs[1:]
    else:
        hid_ref, wd_ref, h1_in, refs = refs[0], refs[1], refs[2], refs[3:]
    dqkv_ref, gout_ref, refs = refs[0], refs[1], refs[2:]
    if layer == 0:
        down_out, refs = refs[0], refs[1:]
    else:
        y_ref, refs = refs[0], refs[1:]
    da, ka, va, kt, dk, dv, w, w_sem = refs[:8]
    sems, refs = refs[8:12], refs[12:]
    reduce = Reduce(layer, refs[:9])
    if layer == 0:
        down = HalfReduce(layer, refs[9 : 9 + HALF])
        down_swap = HalfSwap(gdown_ref, down.other, refs[9 + HALF])
    else:
        held_hid, wd, h1, y_sem = refs[9:13]
    _, rows, wide = qkv_ref.shape
    length = size * rows
    e = qm_ref.shape[2]
    heads = wide // (3 * e)
    scale = e**-0.5
    c = scale * math.log2(math.e)
    depth = w_ref.shape[1] // parts
    n = chunks(rows)
    rc = rows // n
    bq = size * rc
    kc = bq
    g = Group(size)
    copies = [pltpu.make_async_copy(w_ref, w, w_sem.at[0])]
    for copy in copies:
        copy.start()
    g.greet(parts)
    gather = Gather(g, da, rc, sems)
    loads = []
    if layer == 1:
        scatter = Scatter(g, rc, refs[13:])
        loads = [
            pltpu.make_async_copy(wd_ref, wd, y_sem.at[0]),
            pltpu.make_async_copy(h1_in, h1, y_sem.at[1]),
        ]
        for load in loads:
            load.start()
    if layer == 0:
        down_swap.copy().start()
        loads = down.loads(gdown_ref, None)
        for load in loads:
            load.start()

    def send(j):
        at = span(j, rc)
        da[g.me, at, :] = mid_ref[at, :].astype(BF)
        gather.start(j)

    run(n, send)
    lane = lax.broadcasted_iota(jnp.int32, (length, e), 1)
    whole = flat(qkv_ref[...])
    for h in range(heads):
        o = 3 * e * h
        ka[h, :, :e] = whole[:, o + e : o + 2 * e]
        ka[h, :, e:] = flat(km_ref[...])
        va[h, :, :e] = whole[:, o + 2 * e : o + 3 * e]
        va[h, :, e:] = jnp.where(lane < 3, 1.0, 0.0).astype(BF)
        kt[h] = whole[:, o + e : o + 2 * e].T
    dk[...] = jnp.zeros_like(dk)
    dv[...] = jnp.zeros_like(dv)
    ql = lax.broadcasted_iota(jnp.int32, (bq, e), 1)
    for copy in copies + loads:
        copy.wait()

    def out_grad(z):
        cols = pl.ds(pl.multiple_of(z * depth, depth), depth)
        return dg(flat(ctx_ref[...]), flat(da[:, :, cols]), TN)

    def work(j):
        at = span(j, rc)

        @pl.when(j == 0)
        def _():
            gather.relay(0)
            gather.ready(0)

        @pl.when(j == min(1, n - 1))
        def _():
            for i in range(1, n):
                gather.relay(i)
            for i in range(1, n):
                gather.ready(i)
            reduce.send(out_grad)

        if layer == 1:
            hid_load = pltpu.make_async_copy(hid_ref.at[:, at], held_hid, y_sem.at[2])
            hid_load.start()
        qm = flat(qm_ref[:, at, :])
        dctx = dg(flat(da[:, at, :]), w[...], NT).astype(BF)
        ctx = flat(ctx_ref[:, at, :])
        held_qkv = flat(qkv_ref[:, at, :])
        for h in range(heads):
            o = 3 * e * h
            qq = held_qkv[:, o : o + e]
            q = jnp.concatenate([qq, qm], axis=1)
            dc = dctx[:, h * e : (h + 1) * e]
            prod = dc.astype(F32) * ctx[:, h * e : (h + 1) * e].astype(F32)
            d = -jnp.sum(prod, axis=1, keepdims=True)
            d1 = d.astype(BF).astype(F32)
            d2 = (d - d1).astype(BF).astype(F32)
            d3 = d - d1 - d2
            ds_col = jnp.where(ql == 0, d1, jnp.where(ql == 1, d2, jnp.where(ql == 2, d3, 0.0)))
            dca = jnp.concatenate([dc, ds_col.astype(BF)], axis=1)
            lse = lse_ref[j, h : h + 1, :]
            dqt = None
            for k in range(length // kc):
                ks = slice(k * kc, (k + 1) * kc)
                s = dg(ka[h, ks, :], q, NT)
                p = jnp.exp2(s * c - lse)
                ds = (p * dg(va[h, ks, :], dca, NT)).astype(BF)
                dv[h, ks, :] += dg(p.astype(BF), dc, NN)
                dk[h, ks, :] += dg(ds, qq, NN)
                a = dg(kt[h, :, ks], ds, NN)
                dqt = a if dqt is None else dqt + a
            if layer == 0 and h == heads // 2:

                @pl.when(j == min(1, n - 1))
                def _():
                    down_swap.copy().wait_recv()
                    down.middle()

            if layer == 1 and h == heads // 2:

                @pl.when(j > 0)
                def _():
                    scatter.second(j - 1)

            if layer == 0 and h == heads - 1:

                @pl.when(j == n - 1)
                def _():
                    down.late()

            dqkv_ref[:, at, o : o + e] = (dqt * scale).T.astype(BF).reshape(size, rc, e)
        if layer == 1:
            hid_load.wait()
            width = wd.shape[1]
            for f in range(width // 256):
                cols = slice(f * 256, (f + 1) * 256)
                scatter.part[:, at, cols] = dg(flat(held_hid[...]), wd[:, cols], NN).reshape(
                    size, rc, 256
                )
            scatter.first(j)

    run(n, work)
    if layer == 1:
        scatter.second(n - 1)
    for h in range(heads):
        o = 3 * e * h
        dqkv_ref[:, :, o + e : o + 2 * e] = (dk[h] * scale).astype(BF).reshape(size, rows, e)
        dqkv_ref[:, :, o + 2 * e : o + 3 * e] = dv[h].astype(BF).reshape(size, rows, e)

    reduce.collect()
    if layer == 1:

        def output(j):
            at = span(j, rc)
            y_ref[at, :] = (h1[at, :] + scatter.third(j)).astype(BF)

        run(n, output)
        scatter.drain(n)
    reduce.finish(gout_ref)
    if layer == 0:
        down.finish(down_out)
        down_swap.copy().wait_send()
    gather.drain(n)


def attend_backward(size, replicas, layer, mid, qkv, qm, km, ctx, lse, w, grads, more=()):
    _, rows, wide = qkv.shape
    e = qm.shape[2]
    heads = wide // (3 * e)
    width = mid.shape[1]
    parts, depth = replicas, width // replicas
    length = size * rows
    n = chunks(rows)
    return pl.pallas_call(
        functools.partial(attend_back_kernel, size, layer, parts),
        out_shape=[shape(qkv.shape, BF), shape((heads * e, depth), F32)]
        + [shape(grad.shape[1:], F32) for grad in grads]
        + [shape((rows, width), BF)] * (len(more) // 3),
        in_specs=[VM] * 6 + [HB] * (1 + len(grads) + len(more)),
        out_specs=[VM, VM] + [VM] * (len(grads) + len(more) // 3),
        scratch_shapes=[
            pltpu.VMEM((size, rows, width), BF),
            pltpu.VMEM((heads, length, 2 * e), BF),
            pltpu.VMEM((heads, length, 2 * e), BF),
            pltpu.VMEM((heads, e, length), BF),
            pltpu.VMEM((heads, length, e), F32),
            pltpu.VMEM((heads, length, e), F32),
            pltpu.VMEM((heads * e, width), BF),
            DMA((1,)),
        ]
        + comm_sems(size, n)
        + reduce_scratch(parts, heads * e, depth)
        + sum([half_scratch(parts, *grad.shape[1:]) + [DMA((2,))] for grad in grads], [])
        + (
            [
                pltpu.VMEM((size, rows // n, more[0].shape[2]), BF),
                pltpu.VMEM(more[1].shape, BF),
                pltpu.VMEM((rows, width), F32),
                DMA((3,)),
            ]
            + scatter_scratch(size, rows, width, n)
            if more
            else []
        ),
        compiler_params=params(8 + layer),
        cost_estimate=cost(90e9, 40e6),
    )(mid, qkv, qm, km, ctx, lse, w, *grads, *more)


def qkv_back_kernel(
    size, layer, parts, dqkv_ref, gain_ref, a1_in, x_in, mid_in, w_ref,
    dx_ref, gain_out, gqkv_ref, a1_ref, x_ref, mid_ref, w, w_sem, *scratch
):
    rows, width = x_ref.shape
    late = [
        pltpu.make_async_copy(a1_in, a1_ref, w_sem.at[1]),
        pltpu.make_async_copy(x_in, x_ref, w_sem.at[2]),
        pltpu.make_async_copy(mid_in, mid_ref, w_sem.at[3]),
    ]
    depth = width // parts
    n = thin_chunks(rows)
    rc = rows // n
    g = Group(size)
    copies = [pltpu.make_async_copy(w_ref, w, w_sem.at[0])]
    for copy in copies + late:
        copy.start()
    g.greet()
    scatter = Scatter(g, rc, scratch)
    for copy in copies:
        copy.wait()

    lag = min(2, n)

    def work(j):
        at = span(j, rc)
        held = flat(dqkv_ref[:, at, :])
        for z in range(parts):
            cols = slice(z * depth, (z + 1) * depth)
            scatter.part[:, at, cols] = dg(held, w[cols, :], NT).reshape(size, rc, depth)
        scatter.first(j)

        @pl.when(j >= lag)
        def _():
            scatter.second(j - lag)


    run(n, work)
    for j in range(n - lag, n):
        scatter.second(j)
    for copy in late:
        copy.wait()

    def qkv_grad(z):
        cols = pl.ds(pl.multiple_of(z * depth, depth), depth)
        gqkv_ref[z] = dg(flat(a1_ref[:, :, cols]), flat(dqkv_ref[...]), TN).astype(BF)

    run(parts, qkv_grad)
    gain_out[...] = jnp.zeros_like(gain_out)

    def last(j):
        at = span(j, rc)
        dh, dgain = normed_back(
            x_ref[at, :].astype(F32), gain_ref[layer, 0:1, :], scatter.third(j)
        )
        dx_ref[at, :] = (mid_ref[at, :] + dh).astype(BF)
        gain_out[...] += dgain

    run(n, last)
    scatter.drain(n)


def qkv_backward(size, replicas, layer, dqkv, a1, x, mid, gains, w):
    rows, width = x.shape
    wide = w.shape[1]
    parts, depth = replicas, width // replicas
    n = thin_chunks(rows)
    return pl.pallas_call(
        functools.partial(qkv_back_kernel, size, layer, parts),
        out_shape=(
            shape((rows, width), BF),
            shape((1, width), F32),
            shape((parts, depth, wide), BF),
        ),
        in_specs=[VM, VM] + [HB] * 4,
        out_specs=(VM, VM, VM),
        scratch_shapes=[
            pltpu.VMEM((size, rows, width), BF),
            pltpu.VMEM((rows, width), BF),
            pltpu.VMEM((rows, width), F32),
            pltpu.VMEM((width, wide), BF),
            DMA((4,)),
        ]
        + scatter_scratch(size, rows, width, n),
        compiler_params=params(11),
        cost_estimate=cost(30e9, 30e6),
    )(dqkv, gains, a1, x, mid, w)


def last_kernel(
    size, parts, dqkv_ref, a1_ref, x_ref, mid_ref, gain_ref, w_ref, two_ref, up_one_ref, up_two_ref, dx1_ref,
    one_out, two_out, gqkv_out, dx_out,
    gqkv, swap_sem, w, dx, gsum, gcame, w_sem, x_sem, x_send, x_recv, g_send, g_recv, *scratch
):
    rows, width = x_ref.shape
    depth = width // parts
    n = thin_chunks(rows)
    rc = rows // n
    g = Group(size)
    section = lax.axis_index("section")
    d = lax.axis_index("dp")
    copy = pltpu.make_async_copy(w_ref, w, w_sem.at[0])
    copy.start()
    reduce = HalfReduce(0, scratch[:HALF])
    swap = HalfSwap(gqkv, reduce.other, swap_sem)
    scatter = Scatter(g, rc, scratch[HALF:])
    g.greet(parts)

    def upper():
        return far_copy(
            dx1_ref, dx_out.at[0], x_send.at[n], x_recv.at[n], {"section": 1 - section}
        )

    def keep_upper():
        return pltpu.make_async_copy(dx1_ref, dx_out.at[1], x_sem.at[0])

    def lower(j):
        at = span(j, rc)
        return far_copy(
            dx.at[at], dx_out.at[1, at], x_send.at[j], x_recv.at[j], {"section": 1 - section}
        )

    def keep_lower(j):
        at = span(j, rc)
        return pltpu.make_async_copy(dx.at[at], dx_out.at[0, at], x_sem.at[j])

    def qkv_grad(z):
        cols = pl.ds(pl.multiple_of(z * depth, depth), depth)
        gqkv[z] = dg(flat(a1_ref[:, :, cols]), flat(dqkv_ref[...]), TN).astype(BF)

    run(parts, qkv_grad)
    swap.copy().start()
    load = reduce.loads(gqkv, None)[0]
    load.start()

    @pl.when(section == 1)
    def _():
        keep_upper().start()

    copy.wait()

    lag = min(2, n)

    def work(j):
        at = span(j, rc)
        held = flat(dqkv_ref[:, at, :])
        for z in range(parts):
            cols = slice(z * depth, (z + 1) * depth)
            scatter.part[:, at, cols] = dg(held, w[cols, :], NT).reshape(size, rc, depth)
        scatter.first(j)

        @pl.when(j >= lag)
        def _():
            scatter.second(j - lag)


    run(n, work)
    for j in range(n - lag, n):
        scatter.second(j)
    gsum[0] = jnp.zeros_like(gsum[0])

    def last(j):
        at = span(j, rc)
        dh, dgain = normed_back(x_ref[at, :].astype(F32), gain_ref[0, 0:1, :], scatter.third(j))
        dx[at, :] = (mid_ref[at, :] + dh).astype(BF)

        @pl.when(section == 0)
        def _():
            keep_lower(j).start()

        @pl.when(section == 1)
        def _():
            lower(j).start()

        gsum[0, 0:1, :] += dgain

    def rest(j):
        @pl.when(j == n // 2)
        def _():
            load.wait()
            swap.copy().wait_recv()
            reduce.middle()

            @pl.when(section == 0)
            def _():
                upper().start()

        last(j)

    run(n, rest)
    gsum[0, 1:2, :] = two_ref[...]
    gsum[0, 2:3, :] = up_one_ref[...]
    gsum[0, 3:4, :] = up_two_ref[...]

    targets = [
        [{"tensor": g.sibling}],
        [{"tensor": g.ahead(k) * 2 + g.core} for k in range(1, g.chips)],
        [{"dp": lax.rem(d + k, parts)} for k in range(1, parts)],
        [{"section": 1 - section}],
    ]
    slot = 0
    sent = []

    def exchange(stage):
        nonlocal slot
        copies = []
        for target in targets[stage]:
            copies.append(
                far_copy(gsum.at[stage], gcame.at[slot], g_send.at[slot], g_recv.at[slot], target)
            )
            copies[-1].start()
            slot += 1
        total = gsum[stage]
        for i, copy in enumerate(copies):
            copy.wait_recv()
            total = total + gcame[slot - len(copies) + i]
        gsum[stage + 1] = total
        sent.extend(copies)

    exchange(0)
    exchange(1)
    reduce.late()
    exchange(2)
    exchange(3)
    lower_layer = section == 0
    one_out[...] = jnp.where(lower_layer, gsum[4, 0:1, :], gsum[4, 2:3, :])
    two_out[...] = jnp.where(lower_layer, gsum[4, 1:2, :], gsum[4, 3:4, :])

    @pl.when(section == 0)
    def _():
        for j in range(n):
            lower(j).wait_recv()
            keep_lower(j).wait()
        upper().wait_send()

    @pl.when(section == 1)
    def _():
        keep_upper().wait()
        upper().wait_recv()
        for j in range(n):
            lower(j).wait_send()

    reduce.finish(gqkv_out)
    swap.copy().wait_send()
    for copy in sent:
        copy.wait_send()
    scatter.drain(n)


def last_backward(size, replicas, dqkv, a1, x, mid, gains, w, two, up_one, up_two, dx1):
    rows, width = x.shape
    wide = w.shape[1]
    depth = width // replicas
    n = thin_chunks(rows)
    slots = 1 + (size // 2 - 1) + (replicas - 1) + 1
    return pl.pallas_call(
        functools.partial(last_kernel, size, replicas),
        out_shape=(
            shape((1, width), F32),
            shape((1, width), F32),
            shape((depth, wide), F32),
            shape((2, rows, width), BF),
        ),
        in_specs=[VM] * 5 + [HB, VM, VM, VM, VM],
        out_specs=(VM, VM, VM, HB),
        scratch_shapes=[
            pltpu.VMEM((replicas, depth, wide), BF),
            DMA((2,)),
            pltpu.VMEM((width, wide), BF),
            pltpu.VMEM((rows, width), BF),
            pltpu.VMEM((5, 8, width), F32),
            pltpu.VMEM((slots, 8, width), F32),
            DMA((1,)),
            DMA((n,)),
            DMA((n + 1,)),
            DMA((n + 1,)),
            DMA((slots,)),
            DMA((slots,)),
        ]
        + half_scratch(replicas, depth, wide)
        + scatter_scratch(size, rows, width, n),
        compiler_params=params(10),
        cost_estimate=cost(40e9, 30e6),
    )(dqkv, a1, x, mid, gains, w, two, up_one, up_two, dx1)


def scene_masks(segments, e):
    same = (segments[..., None] == jnp.arange(e, dtype=jnp.int32)).astype(F32)
    used = jnp.arange(e) < SCENES
    return (
        jnp.where(used, same * MASKED, 0.0).astype(BF),
        jnp.where(used, 1.0 - same, 0.0).astype(BF),
    )


def swap_section(value):
    return lax.ppermute(value, "section", [(0, 1), (1, 0)])


def shards(
    block_input,
    segment_ids,
    cotangent,
    norm_one_gain,
    qkv_weight,
    out_weight,
    norm_two_gain,
    up_weight,
    down_weight,
):
    section = lax.axis_index("section")
    size = lax.axis_size("tensor")
    replicas = lax.axis_size("dp")

    mine = [
        qkv_weight[0].reshape((qkv_weight.shape[1], -1)),
        out_weight[0].reshape((-1, out_weight.shape[3])),
        up_weight[0],
        down_weight[0],
    ]
    mine = [w.astype(BF).reshape((2, -1, w.shape[1])) for w in mine]
    gains = jnp.concatenate(
        [norm_one_gain, norm_two_gain, jnp.zeros((6, norm_one_gain.shape[1]), F32)], axis=0
    )
    segments = lax.dynamic_index_in_dim(segment_ids, section, 0, keepdims=False)
    head_dim = qkv_weight.shape[3] // 3
    qm, km = scene_masks(segments.reshape((size, -1)), head_dim)
    qkv, gains, x, a1, w_qkv_0, w_out_0, h_qkv, h_out, h_up, h_down = first_forward(
        size, replicas, block_input, gains, mine
    )
    h1, ctx, lse, w_up_0, w_down_0 = attend(
        size, replicas, 0, qkv, qm, km, x, w_out_0,
        [(h_up, "spread", 0, False), (h_down, "spread", 0, True)],
    )
    below = (x, a1, qkv, ctx, lse, h1)
    y0, qkv, a2, hid, slope, a1, w_qkv_1, w_out_1, w_up_1 = turn_forward(
        size, replicas, h1, gains, w_up_0, w_down_0, h_qkv,
        [(h_out, "spread", 1, True), (h_up, "spread", 1, False)],
    )
    kept = [below + (a2, hid, slope)]
    h1, ctx, lse, grad_all, w_down_1 = attend(
        size, replicas, 1, qkv, qm, km, y0, w_out_1, [(h_down, "spread", 1, True)], [cotangent]
    )
    kept.append((y0, a1, qkv, ctx, lse, h1))
    weights = [
        (w_qkv_0, w_out_0, w_up_0, w_down_0),
        (w_qkv_1, w_out_1, w_up_1, w_down_1),
    ]
    def reduce_rows(value):
        return lax.psum_scatter(value, "dp", scatter_dimension=0, tiled=False)

    x, a1, qkv, ctx, lse, h1 = kept[1]
    w_qkv, w_out, w_up, w_down = weights[1]
    mid, gain_two, g_up, g_down, hid = peak(size, replicas, h1, gains, grad_all, w_up, w_down)
    d_qkv, out_1, y1 = attend_backward(
        size, replicas, 1, mid, qkv, qm, km, ctx, lse, w_out, [], [hid, w_down, h1]
    )
    up_1, down_1 = reduce_rows(g_up), reduce_rows(g_down)
    dx1, gain_one, g_qkv = qkv_backward(size, replicas, 1, d_qkv, a1, x, mid, gains, w_qkv)
    up_one, up_two = gain_one, gain_two
    dx1, up_1, down_1 = lax.optimization_barrier((dx1, up_1, down_1))
    qkv_1 = reduce_rows(g_qkv)

    x, a1, qkv, ctx, lse, h1, a2, hid, slope = kept[0]
    w_qkv, w_out, w_up, w_down = weights[0]
    mid, gain_two, g_up, g_down, layer_out = mlp_backward(
        size, replicas, 0, dx1, h1, gains, a2, hid, slope, w_up, w_down, [y0, y1]
    )
    mid, qkv_1 = lax.optimization_barrier((mid, qkv_1))
    d_qkv, out_0, down_0 = attend_backward(
        size, replicas, 0, mid, qkv, qm, km, ctx, lse, w_out, [g_down]
    )
    up_0 = reduce_rows(g_up)
    d_qkv, up_0 = lax.optimization_barrier((d_qkv, up_0))
    one_grad, two_grad, qkv_0, input_out = last_backward(
        size, replicas, d_qkv, a1, x, mid, gains, w_qkv, gain_two, up_one, up_two, dx1
    )

    def finish(zero, one):
        send = swap_section(jnp.where(section == 0, one, zero))
        return jnp.where(section == 0, zero, one).astype(F32) + send.astype(F32)

    other_qkv_1 = swap_section(qkv_1)
    qkv_grad = jnp.where(section == 0, qkv_0, qkv_1.astype(F32) + other_qkv_1.astype(F32))
    out_grad = jnp.where(section == 0, out_0, out_1)
    up_grad = finish(up_0, up_1)
    other_down_1 = swap_section(down_1)
    down_grad = jnp.where(section == 0, down_0, down_1.astype(F32) + other_down_1.astype(F32))
    return (
        layer_out[None],
        input_out[None],
        one_grad,
        qkv_grad.reshape(qkv_weight.shape),
        out_grad.reshape(out_weight.shape),
        two_grad,
        up_grad[None],
        down_grad[None],
    )


def solution(mesh):
    return jax.shard_map(
        shards,
        mesh=mesh,
        in_specs=(
            P(None, ("dp", "tensor"), None),
            P(None, "dp"),
            P(None, ("dp", "tensor"), None),
            P("section", None),
            P("section", "dp", "tensor", None),
            P("section", "tensor", None, "dp"),
            P("section", None),
            P("section", "dp", "tensor"),
            P("section", "tensor", "dp"),
        ),
        out_specs=(
            P("section", None, ("dp", "tensor"), None),
            P("section", None, ("dp", "tensor"), None),
            P("section", None),
            P("section", "dp", "tensor", None),
            P("section", "tensor", None, "dp"),
            P("section", None),
            P("section", "dp", "tensor"),
            P("section", "tensor", "dp"),
        ),
        check_vma=False,
    )
```

```python
import functools
import math

import jax
import jax.numpy as jnp
from jax import lax
from jax.experimental import pallas as pl
from jax.experimental.pallas import tpu as pltpu
from jax.sharding import PartitionSpec as P

F32 = jnp.float32
BF = jnp.bfloat16
NT = (((1,), (1,)), ((), ()))
NN = (((1,), (0,)), ((), ()))
TN = (((0,), (0,)), ((), ()))
MASKED = -1e30
SCENES = 3
MESH = pl.DeviceIdType.MESH
VM = pl.BlockSpec(memory_space=pltpu.VMEM)
HB = pl.BlockSpec(memory_space=pl.ANY)
DMA = pltpu.SemaphoreType.DMA
LIMIT = 58 << 20


def dg(a, b, dims):
    return lax.dot_general(a, b, dims, preferred_element_type=F32)


def chunks(rows):
    return 4 if rows % 64 == 0 else 1


def thin_chunks(rows):
    return 8 if rows % 128 == 0 else chunks(rows)


def shape(dims, dtype):
    return jax.ShapeDtypeStruct(dims, dtype)


class Group:
    def __init__(self, size):
        self.size = size
        self.chips = size // 2
        self.me = lax.axis_index("tensor")
        self.chip = lax.div(self.me, 2)
        self.core = lax.rem(self.me, 2)
        self.sibling = self.chip * 2 + 1 - self.core

    def ahead(self, k):
        return lax.rem(self.chip + k, self.chips)

    def behind(self, k):
        return lax.rem(self.chip + self.chips - k, self.chips)

    def greet(self, replicas=0, side=False):
        barrier = pltpu.get_barrier_semaphore()
        targets = [self.sibling] + [self.ahead(k) * 2 + self.core for k in range(1, self.chips)]
        targets = [{"tensor": target} for target in targets]
        if replicas:
            d = lax.axis_index("dp")
            targets += [{"dp": lax.rem(d + k, replicas)} for k in range(1, replicas)]
        if replicas or side:
            targets += [{"section": 1 - lax.axis_index("section")}]
        for target in targets:
            pl.semaphore_signal(barrier, inc=1, device_id=target, device_id_type=MESH)
        pl.semaphore_wait(barrier, len(targets))


def remote(src, dst, send, recv, target):
    return pltpu.make_async_remote_copy(
        src_ref=src,
        dst_ref=dst,
        send_sem=send,
        recv_sem=recv,
        device_id={"tensor": target},
        device_id_type=MESH,
    )


def span(j, rc):
    return pl.ds(pl.multiple_of(j * rc, rc), rc)


def comm_sems(group_size, n):
    c = group_size // 2
    far, near = DMA((max(c - 1, 1), n)), DMA((c, n))
    return [far, far, near, near]


class Gather:
    def __init__(self, g, buf, rc, sems):
        self.g, self.buf, self.rc = g, buf, rc
        self.far_send, self.far_recv, self.near_send, self.near_recv = sems

    def far(self, k, j, origin, target, src=None):
        ref = self.buf.at[origin, span(j, self.rc)]
        src = ref if src is None else src
        return remote(src, ref, self.far_send.at[k - 1, j], self.far_recv.at[k - 1, j], target)

    def near(self, k, j, origin, src=None):
        ref = self.buf.at[origin, span(j, self.rc)]
        src = ref if src is None else src
        return remote(
            src, ref, self.near_send.at[k, j], self.near_recv.at[k, j], self.g.sibling
        )

    def start(self, j, src=None):
        g = self.g
        for k in range(1, g.chips):
            self.far(k, j, g.me, g.ahead(k) * 2 + g.core, src).start()
        self.near(0, j, g.me, src).start()

    def relay(self, j):
        g = self.g
        for k in range(1, g.chips):
            origin = g.behind(k) * 2 + g.core
            self.far(k, j, origin, g.me).wait_recv()
            self.near(k, j, origin).start()

    def ready(self, j):
        g = self.g
        self.near(0, j, g.sibling).wait_recv()
        for k in range(1, g.chips):
            self.near(k, j, g.behind(k) * 2 + 1 - g.core).wait_recv()

    def drain(self, n):
        g = self.g

        def one(j, _):
            for k in range(1, g.chips):
                self.far(k, j, g.me, g.sibling).wait_send()
            for k in range(g.chips):
                self.near(k, j, g.me).wait_send()
            return 0

        lax.fori_loop(0, n, one, 0)


def scatter_scratch(group_size, rows, width, n):
    c = group_size // 2
    far = pltpu.VMEM((max(c - 1, 1), rows, width), BF)
    near = pltpu.VMEM((c, rows, width), BF)
    return [pltpu.VMEM((group_size, rows, width), F32), near, near, far, far] + comm_sems(
        group_size, n
    )


class Scatter:
    def __init__(self, g, rc, scratch):
        self.g, self.rc = g, rc
        self.part, self.near_out, self.near_in, self.far_out, self.far_in = scratch[:5]
        self.far_send, self.far_recv, self.near_send, self.near_recv = scratch[5:]

    def near(self, k, j):
        rows = span(j, self.rc)
        return remote(
            self.near_out.at[k, rows],
            self.near_in.at[k, rows],
            self.near_send.at[k, j],
            self.near_recv.at[k, j],
            self.g.sibling,
        )

    def far(self, k, j):
        rows = span(j, self.rc)
        return remote(
            self.far_out.at[k - 1, rows],
            self.far_in.at[k - 1, rows],
            self.far_send.at[k - 1, j],
            self.far_recv.at[k - 1, j],
            self.g.ahead(k) * 2 + self.g.core,
        )

    def first(self, j):
        g, rows = self.g, span(j, self.rc)
        for k in list(range(1, g.chips)) + [0]:
            owner = g.ahead(k) * 2 + 1 - g.core
            self.near_out[k, rows, :] = self.part[owner, rows, :].astype(BF)
            self.near(k, j).start()

    def second(self, j):
        g, rows = self.g, span(j, self.rc)
        for k in range(1, g.chips):
            owner = g.ahead(k) * 2 + g.core
            self.near(k, j).wait_recv()
            both = self.part[owner, rows, :] + self.near_in[k, rows, :].astype(F32)
            self.far_out[k - 1, rows, :] = both.astype(BF)
            self.far(k, j).start()

    def third(self, j):
        g, rows = self.g, span(j, self.rc)
        self.near(0, j).wait_recv()
        total = self.part[g.me, rows, :] + self.near_in[0, rows, :].astype(F32)
        for k in range(1, g.chips):
            self.far(k, j).wait_recv()
            total = total + self.far_in[k - 1, rows, :].astype(F32)
        return total

    def drain(self, n):
        g = self.g

        def one(j, _):
            for k in range(1, g.chips):
                self.far(k, j).wait_send()
            for k in range(g.chips):
                self.near(k, j).wait_send()
            return 0

        lax.fori_loop(0, n, one, 0)


def far_copy(src, dst, send, recv, target):
    return pltpu.make_async_remote_copy(
        src_ref=src,
        dst_ref=dst,
        send_sem=send,
        recv_sem=recv,
        device_id=target,
        device_id_type=MESH,
    )


class Swap:
    def __init__(self, src, stage, sems):
        self.src, self.stage, self.sems = src, stage, sems
        self.s = lax.axis_index("section")

    def copies(self, layer):
        local = pltpu.make_async_copy(self.src.at[self.s], self.stage.at[self.s], self.sems.at[0])
        side = far_copy(
            self.src.at[1 - self.s],
            self.stage.at[layer],
            self.sems.at[1],
            self.sems.at[2],
            {"section": 1 - self.s},
        )
        return local, side

    def start(self):
        for copy in self.copies(self.s):
            copy.start()

    def arrive(self):
        local, side = self.copies(1 - self.s)
        local.wait()
        side.wait_recv()

    def finish(self):
        self.copies(self.s)[1].wait_send()


def reduce_scratch(replicas, rows, cols):
    many = pltpu.VMEM((replicas - 1, rows, cols), BF)
    one = pltpu.VMEM((rows, cols), BF)
    far, side = DMA((replicas - 1, 2)), DMA((2,))
    return [pltpu.VMEM((rows, cols), F32), many, many, one, one, far, far, side, side]


class Reduce:
    def __init__(self, layer, scratch):
        self.layer = layer
        self.own, self.away, self.came, self.over, self.back = scratch[:5]
        self.z_send, self.z_recv, self.y_send, self.y_recv = scratch[5:]
        self.replicas = self.away.shape[0] + 1
        self.half = self.own.shape[0] // 2
        self.d = lax.axis_index("dp")
        self.s = lax.axis_index("section")

    def target(self, k):
        return lax.rem(self.d + k, self.replicas)

    def part(self, i):
        return pl.ds(pl.multiple_of(i * self.half, self.half), self.half)

    def z_copy(self, k, i):
        part = self.part(i)
        return far_copy(
            self.away.at[k - 1, part],
            self.came.at[k - 1, part],
            self.z_send.at[k - 1, i],
            self.z_recv.at[k - 1, i],
            {"dp": self.target(k)},
        )

    def y_copy(self, i):
        part = self.part(i)
        return far_copy(
            self.over.at[part],
            self.back.at[part],
            self.y_send.at[i],
            self.y_recv.at[i],
            {"section": 1 - self.s},
        )

    def send(self, block):
        def one(i):
            k = i + 1
            self.away[i] = block(self.target(k)).astype(BF)
            self.z_copy(k, 0).start()
            self.z_copy(k, 1).start()

        run(self.replicas - 1, one)
        self.own[...] = block(self.d)

    def collect(self):
        def one(i):
            part = self.part(i)
            total = self.own[part, :]
            for k in range(1, self.replicas):
                self.z_copy(k, i).wait_recv()
                total = total + self.came[k - 1, part, :].astype(F32)
            self.own[part, :] = total
            self.over[part, :] = total.astype(BF)

            @pl.when(self.s != self.layer)
            def _():
                self.y_copy(i).start()

        run(2, one)

    def finish(self, out, above=None):
        @pl.when(self.s == self.layer)
        def _():
            self.y_copy(0).wait_recv()
            self.y_copy(1).wait_recv()
            out[...] = self.own[...] + self.back[...].astype(F32)

        @pl.when(self.s != self.layer)
        def _():
            self.y_copy(0).wait_send()
            self.y_copy(1).wait_send()
            out[...] = self.own[...] if above is None else above[...]

        for k in range(1, self.replicas):
            self.z_copy(k, 0).wait_send()
            self.z_copy(k, 1).wait_send()


class HalfSwap:
    def __init__(self, src, came, sems):
        self.src, self.came, self.sems = src, came, sems
        self.s = lax.axis_index("section")
        self.rows = came.shape[1]

    def copy(self):
        at = pl.ds(pl.multiple_of((1 - self.s) * self.rows, self.rows), self.rows)
        return far_copy(
            self.src.at[:, at],
            self.came,
            self.sems.at[0],
            self.sems.at[1],
            {"section": 1 - self.s},
        )


def half_scratch(replicas, rows, cols):
    rows = rows // 2
    all_, far = pltpu.VMEM((replicas, rows, cols), BF), pltpu.VMEM((replicas - 1, rows, cols), BF)
    one = pltpu.VMEM((rows, cols), BF)
    z = DMA((replicas - 1,))
    return [all_, all_, far, far, pltpu.VMEM((rows, cols), F32), one, one, DMA((3,)), z, z, DMA((2,))]


HALF = 11


class HalfReduce:
    def __init__(self, layer, scratch):
        self.layer = layer
        self.mine, self.other, self.away, self.came, self.own, self.over, self.back = scratch[:7]
        self.in_sem, self.z_send, self.z_recv, self.y_sem = scratch[7:]
        self.replicas, self.rows = self.mine.shape[:2]
        self.s = lax.axis_index("section")
        self.d = lax.axis_index("dp")

    def half(self, s):
        return pl.ds(pl.multiple_of(s * self.rows, self.rows), self.rows)

    def loads(self, src, other):
        loads = [pltpu.make_async_copy(src.at[:, self.half(self.s)], self.mine, self.in_sem.at[0])]
        if other is not None:
            loads.append(pltpu.make_async_copy(other, self.other, self.in_sem.at[1]))
        return loads

    def z_copy(self, k):
        return far_copy(
            self.away.at[k - 1],
            self.came.at[k - 1],
            self.z_send.at[k - 1],
            self.z_recv.at[k - 1],
            {"dp": lax.rem(self.d + k, self.replicas)},
        )

    def y_copy(self):
        return far_copy(
            self.over, self.back, self.y_sem.at[0], self.y_sem.at[1], {"section": 1 - self.s}
        )

    def middle(self):
        def both(z):
            return self.mine[z].astype(F32) + self.other[z].astype(F32)

        for k in range(1, self.replicas):
            self.away[k - 1] = both(lax.rem(self.d + k, self.replicas)).astype(BF)
            self.z_copy(k).start()
        self.own[...] = both(self.d)

    def late(self):
        total = self.own[...]
        for k in range(1, self.replicas):
            self.z_copy(k).wait_recv()
            total = total + self.came[k - 1].astype(F32)
        self.own[...] = total
        self.over[...] = total.astype(BF)

        @pl.when(self.s != self.layer)
        def _():
            self.y_copy().start()

    def finish(self, out, above=None):
        @pl.when(self.s == self.layer)
        def _():
            self.y_copy().wait_recv()
            out[self.half(self.s), :] = self.own[...]
            out[self.half(1 - self.s), :] = self.back[...].astype(F32)

        @pl.when(self.s != self.layer)
        def _():
            if above is None:
                out[...] = jnp.zeros_like(out)
            else:
                copy = pltpu.make_async_copy(above, out, self.in_sem.at[2])
                copy.start()
                copy.wait()
            self.y_copy().wait_send()

        for k in range(1, self.replicas):
            self.z_copy(k).wait_send()


class Spread:
    def __init__(self, src, dst, by_columns, sems):
        self.src, self.dst, self.by_columns = src, dst, by_columns
        self.own_sem, self.far_send, self.far_recv, self.side_send, self.side_recv = sems
        self.replicas = far = self.side_send.shape[0]
        self.s = lax.axis_index("section")
        self.d = lax.axis_index("dp")
        self.stages = [
            sorted({k, far - k}) for k in range(1, far // 2 + 1)
        ]

    def place(self, half, z):
        rows, cols = self.src.shape
        if self.by_columns:
            return self.dst.at[
                pl.ds(pl.multiple_of(half * rows, rows), rows),
                pl.ds(pl.multiple_of(z * cols, cols), cols),
            ]
        return self.dst.at[pl.ds(pl.multiple_of((2 * z + half) * rows, rows), rows)]

    def origin(self, k):
        return lax.rem(self.d + self.replicas - k, self.replicas)

    def own(self):
        return pltpu.make_async_copy(self.src, self.place(self.s, self.d), self.own_sem.at[0])

    def far(self, k, origin):
        return pltpu.make_async_remote_copy(
            src_ref=self.src,
            dst_ref=self.place(self.s, origin),
            send_sem=self.far_send.at[k - 1],
            recv_sem=self.far_recv.at[k - 1],
            device_id={"dp": lax.rem(self.d + k, self.replicas)},
            device_id_type=MESH,
        )

    def side(self, k, half):
        place = self.place(half, self.origin(k))
        return pltpu.make_async_remote_copy(
            src_ref=self.src if k == 0 else place,
            dst_ref=place,
            send_sem=self.side_send.at[k],
            recv_sem=self.side_recv.at[k],
            device_id={"section": 1 - self.s},
            device_id_type=MESH,
        )

    def start(self):
        for k in self.stages[0]:
            self.far(k, self.d).start()
        self.side(0, self.s).start()
        self.own().start()

    def step(self, i):
        for k in self.stages[i]:
            self.far(k, self.origin(k)).wait_recv()
            self.side(k, self.s).start()
        if i + 1 < len(self.stages):
            for k in self.stages[i + 1]:
                self.far(k, self.d).start()

    def finish(self):
        self.own().wait()
        for k in range(self.replicas):
            self.side(k, 1 - self.s).wait_recv()
        for k in range(1, self.replicas):
            self.far(k, self.d).wait_send()
        for k in range(self.replicas):
            self.side(k, self.s).wait_send()


class ZGather:
    def __init__(self, src, got, sems):
        self.src, self.got = src, got
        self.own_sem, self.send, self.recv = sems
        self.replicas = got.shape[0]
        self.d = lax.axis_index("dp")

    def own(self):
        return pltpu.make_async_copy(self.src, self.got.at[self.d], self.own_sem.at[0])

    def far(self, k, origin):
        return far_copy(
            self.src,
            self.got.at[origin],
            self.send.at[k - 1],
            self.recv.at[k - 1],
            {"dp": lax.rem(self.d + k, self.replicas)},
        )

    def start(self):
        for k in range(1, self.replicas):
            self.far(k, self.d).start()
        self.own().start()

    def step(self, i):
        pass

    def finish(self):
        self.own().wait()
        for k in range(1, self.replicas):
            self.far(k, lax.rem(self.d + self.replicas - k, self.replicas)).wait_recv()
        for k in range(1, self.replicas):
            self.far(k, self.d).wait_send()


class YJoin:
    def __init__(self, got, dst, by_columns, sems):
        self.src, self.dst, self.by_columns = got, dst, by_columns
        self.own_sem, self.send, self.recv, self.got, self.in_sem = sems
        self.replicas, self.rows, self.cols = got.shape
        self.s = lax.axis_index("section")

    def place(self, half, z):
        rows, cols = self.rows, self.cols
        if self.by_columns:
            return self.dst.at[
                pl.ds(pl.multiple_of(half * rows, rows), rows), pl.ds(z * cols, cols)
            ]
        return self.dst.at[pl.ds(pl.multiple_of((2 * z + half) * rows, rows), rows)]

    def own(self, z):
        return pltpu.make_async_copy(self.got.at[z], self.place(self.s, z), self.own_sem.at[z])

    def side(self, z, half):
        return far_copy(
            self.got.at[z],
            self.place(half, z),
            self.send.at[z],
            self.recv.at[z],
            {"section": 1 - self.s},
        )

    def start(self):
        load = pltpu.make_async_copy(self.src, self.got, self.in_sem.at[0])
        load.start()
        load.wait()
        for z in range(self.replicas):
            self.side(z, self.s).start()
            self.own(z).start()

    def step(self, i):
        pass

    def finish(self):
        for z in range(self.replicas):
            self.own(z).wait()
            self.side(z, 1 - self.s).wait_recv()
        for z in range(self.replicas):
            self.side(z, self.s).wait_send()


def rider_sems(replicas):
    far, side = DMA((replicas - 1,)), DMA((replicas,))
    return [DMA((1,)), far, far, side, side]


class Riders:
    def __init__(self, srcs, dsts, columns, sems):
        self.all = []
        for src, dst, (kind, layer, by) in zip(srcs, dsts, columns):
            count = 3 if kind == "z" else 5
            own, sems = sems[:count], sems[count:]
            if kind == "spread":
                self.all.append(Spread(src.at[layer], dst, by, own))
            elif kind == "z":
                self.all.append(ZGather(src.at[layer], dst, own))
            else:
                self.all.append(YJoin(src, dst, by, own))
        self.replicas = self.all[0].replicas if self.all else 0

    def start(self):
        for one in self.all:
            one.start()

    def step(self, j, n):
        if not self.all:
            return
        stages = self.replicas // 2
        for i in range(stages):

            @pl.when(j == n * (i + 1) // stages - 1)
            def _(i=i):
                for one in self.all:
                    one.step(i)

    def finish(self):
        for one in self.all:
            one.finish()


def riding(riders, replicas):
    arrays = [array for array, _, _, _ in riders]
    columns = tuple(rider[1:] for rider in riders)
    outs, sems = [], []
    for array, kind, _, by in riders:
        rows, cols = array.shape[1:]
        if kind == "z":
            outs.append(shape((replicas, rows, cols), BF))
        else:
            outs.append(
                shape((2 * rows, replicas * cols) if by else (2 * replicas * rows, cols), BF)
            )
        far, side = DMA((replicas - 1,)), DMA((replicas,))
        sems += {
            "spread": rider_sems(replicas),
            "z": [DMA((1,)), far, far],
            "y": [side, side, side, pltpu.VMEM(array.shape, BF), DMA((1,))],
        }[kind]
    return arrays, columns, outs, sems


def params(key):
    return pltpu.CompilerParams(
        vmem_limit_bytes=LIMIT, collective_id=key, has_side_effects=True
    )


def cost(flops, moved, exps=0):
    return pl.CostEstimate(flops=int(flops), bytes_accessed=int(moved), transcendentals=int(exps))


def normed(source):
    center = source - jnp.mean(source, axis=-1, keepdims=True)
    r = lax.rsqrt(jnp.mean(center * center, axis=-1, keepdims=True) + 1e-05)
    return center * r, r


def normed_back(source, gain, grad):
    n, r = normed(source)
    e = grad * gain
    dh = r * (
        e - jnp.mean(e, axis=-1, keepdims=True) - n * jnp.mean(e * n, axis=-1, keepdims=True)
    )
    return dh, jnp.sum(grad * n, axis=0, keepdims=True)


def flat(value):
    return value.reshape((value.shape[0] * value.shape[1],) + value.shape[2:])


def run(n, body):
    def one(j, carry):
        body(j)
        return carry

    lax.fori_loop(0, n, one, 0)


def first_kernel(
    size, replicas, x_in, gain_ref, wq_ref, wo_ref, wu_ref, wd_ref,
    qkv_ref, gains_out, x_ref, a1_out, wq_out, wo_out, q_stage, o_stage, u_stage, d_stage,
    a1, w, gains, own_sem, q_sem, o_sem, u_sem, d_sem, gain_sem, *sems
):
    rows, width = x_ref.shape
    n = thin_chunks(rows)
    rc = rows // n
    g = Group(size)
    section = lax.axis_index("section")
    x_load = pltpu.make_async_copy(x_in.at[section], x_ref, own_sem.at[2])
    x_load.start()
    gather = Gather(g, a1, rc, sems[:4])
    swaps = [
        Swap(wq_ref, q_stage, q_sem),
        Swap(wo_ref, o_stage, o_sem),
        Swap(wu_ref, u_stage, u_sem),
        Swap(wd_ref, d_stage, d_sem),
    ]
    spreads = [
        Spread(q_stage.at[0], w, False, sems[4:9]),
        Spread(o_stage.at[0], wo_out, True, sems[9:14]),
    ]
    g.greet(replicas)

    def gain_copy(layer):
        return far_copy(
            gain_ref, gains.at[layer], gain_sem.at[0], gain_sem.at[1], {"section": 1 - section}
        )

    gain_copy(section).start()
    swaps[0].start()
    swaps[1].start()
    gains[section] = gain_ref[...]
    gain_copy(1 - section).wait_recv()
    gains_out[...] = gains[...]
    x_load.wait()

    def send(j):
        at = span(j, rc)
        a = normed(x_ref[at, :].astype(F32))[0] * gains[0, 0:1, :]
        a1[g.me, at, :] = a.astype(BF)
        gather.start(j)

    run(n, send)
    swaps[0].arrive()
    swaps[1].arrive()
    for one in spreads:
        one.start()
    stages = len(spreads[0].stages)

    def relay(j):
        gather.relay(j)

        for i in range(stages):

            @pl.when(j == n * (i + 1) // stages - 1)
            def _(i=i):
                for one in spreads:
                    one.step(i)

    run(n, relay)
    swaps[2].start()
    swaps[3].start()
    for one in spreads:
        one.finish()
    outs = [
        pltpu.make_async_copy(w, wq_out, own_sem.at[0]),
        pltpu.make_async_copy(a1, a1_out, own_sem.at[1]),
    ]
    outs[0].start()

    def multiply(j):
        at = span(j, rc)
        gather.ready(j)
        r = dg(flat(a1[:, at, :]), w[...], NN).astype(BF)
        qkv_ref[:, at, :] = r.reshape(size, rc, r.shape[1])

    run(n, multiply)
    outs[1].start()
    swaps[2].arrive()
    swaps[3].arrive()
    for swap in swaps:
        swap.finish()
    gain_copy(section).wait_send()
    gather.drain(n)
    for out in outs:
        out.wait()


def first_forward(size, replicas, x, gains, ws):
    _, rows, width = x.shape
    wide = ws[0].shape[2]
    deep = 2 * ws[1].shape[1]
    n = thin_chunks(rows)
    return pl.pallas_call(
        functools.partial(first_kernel, size, replicas),
        out_shape=[
            shape((size, rows, wide), BF),
            shape((2,) + gains.shape, F32),
            shape((rows, width), BF),
            shape((size, rows, width), BF),
            shape((width, wide), BF),
            shape((deep, width), BF),
        ]
        + [shape(w.shape, BF) for w in ws],
        in_specs=[HB] + [VM] * 5,
        out_specs=[VM, VM, VM] + [HB] * 7,
        scratch_shapes=[
            pltpu.VMEM((size, rows, width), BF),
            pltpu.VMEM((width, wide), BF),
            pltpu.VMEM((2,) + gains.shape, F32),
            DMA((3,)),
            DMA((3,)),
            DMA((3,)),
            DMA((3,)),
            DMA((3,)),
            DMA((2,)),
        ]
        + comm_sems(size, n)
        + rider_sems(replicas) * 2,
        compiler_params=params(0),
        cost_estimate=cost(30e9, 30e6),
    )(x, gains, *ws)


def attend_kernel(size, layer, columns, *refs):
    m = len(columns)
    qkv_ref, qm_ref, km_ref, x_ref, w_ref = refs[:5]
    refs = refs[5:]
    if layer == 1:
        cot_ref, refs = refs[0], refs[1:]
    halves, refs = refs[:m], refs[m:]
    h1_ref, ctx_ref, lse_ref = refs[:3]
    refs = refs[3:]
    if layer == 1:
        cot_out, refs = refs[0], refs[1:]
    wholes, refs = refs[:m], refs[m:]
    ka, vt, w, w_sem = refs[:4]
    scratch, refs = refs[4:13], refs[13:]
    if layer == 1:
        cot_sems, cot_sem, cot_mine, refs = refs[:4], refs[4], refs[5], refs[6:]
        cot_load = pltpu.make_async_copy(
            cot_ref.at[lax.axis_index("section")], cot_mine, cot_sem.at[1]
        )
        cot_load.start()
    riders = Riders(halves, wholes, columns, refs)
    _, rows, wide = qkv_ref.shape
    length = size * rows
    e = qm_ref.shape[2]
    heads = wide // (3 * e)
    c = e**-0.5 * math.log2(math.e)
    n = chunks(rows)
    rc = rows // n
    bq = size * rc
    kc = bq
    g = Group(size)
    copy = pltpu.make_async_copy(w_ref, w, w_sem.at[0])
    copy.start()
    g.greet(riders.replicas)
    riders.start()
    if layer == 1:
        cot = Gather(g, cot_out, rows, cot_sems)
        own = pltpu.make_async_copy(cot_mine, cot_out.at[g.me], cot_sem.at[0])
        cot_load.wait()
        own.start()
        cot.start(0, cot_mine)
    scatter = Scatter(g, rc, scratch)
    whole = flat(qkv_ref[...])
    for h in range(heads):
        o = 3 * e * h
        ka[h, :, :e] = whole[:, o + e : o + 2 * e]
        ka[h, :, e:] = flat(km_ref[...])
        vt[h, :e, :] = whole[:, o + 2 * e : o + 3 * e].T
        vt[h, e:, :] = jnp.ones((16, length), BF)
    copy.wait()

    def work(j):
        at = span(j, rc)
        qm = flat(qm_ref[:, at, :])
        found = []
        held_qkv = flat(qkv_ref[:, at, :])
        for h in range(heads):
            o = 3 * e * h
            q = jnp.concatenate([held_qkv[:, o : o + e], qm], axis=1)
            held = []
            top = None
            for k in range(length // kc):
                s = dg(ka[h, k * kc : (k + 1) * kc, :], q, NT)
                t = jnp.max(s, axis=0, keepdims=True)
                top = t if top is None else jnp.maximum(top, t)
                held.append(s)
            top = top * c
            acc = None
            for k in range(length // kc):
                p = jnp.exp2(held[k] * c - top).astype(BF)
                a = dg(vt[h, :, k * kc : (k + 1) * kc], p, NN)
                acc = a if acc is None else acc + a
            total = acc[e : e + 1]
            found.append((acc[:e] * (1.0 / total)).astype(BF))
            lse_ref[j, h : h + 1, :] = top + jnp.log2(total)
            if h == heads // 2:

                @pl.when(j > 0)
                def _():
                    scatter.second(j - 1)

        ctx = (jnp.concatenate(found, axis=0) if heads > 1 else found[0]).T
        ctx_ref[:, at, :] = ctx.reshape(size, rc, heads * e)
        width = x_ref.shape[1]
        scatter.part[:, at, :] = dg(ctx, w[...], NN).reshape(size, rc, width)
        scatter.first(j)
        riders.step(j, n)
        if layer == 1:

            @pl.when(j == n - 1)
            def _():
                cot.relay(0)

    run(n, work)
    scatter.second(n - 1)

    def last(j):
        at = span(j, rc)
        h1_ref[at, :] = x_ref[at, :].astype(F32) + scatter.third(j)

    run(n, last)
    scatter.drain(n)
    if layer == 1:
        cot.ready(0)
        cot.drain(1)
        own.wait()
    riders.finish()


def attend(size, replicas, layer, qkv, qm, km, x, w, riders, cot=()):
    _, rows, wide = qkv.shape
    e = qm.shape[2]
    heads = wide // (3 * e)
    width = x.shape[1]
    n = chunks(rows)
    halves, columns, outs, sems = riding(riders, replicas)
    return pl.pallas_call(
        functools.partial(attend_kernel, size, layer, columns),
        out_shape=[
            shape((rows, width), F32),
            shape((size, rows, heads * e), BF),
            shape((n, heads, size * rows // n), F32),
        ]
        + [shape((size, rows, width), BF) for _ in cot]
        + outs,
        in_specs=[VM, VM, VM, VM, HB] + [HB] * (len(cot) + len(riders)),
        out_specs=[VM, VM, VM] + [HB] * (len(cot) + len(outs)),
        scratch_shapes=[
            pltpu.VMEM((heads, size * rows, 2 * e), BF),
            pltpu.VMEM((heads, e + 16, size * rows), BF),
            pltpu.VMEM((heads * e, width), BF),
            DMA((1,)),
        ]
        + scatter_scratch(size, rows, width, n)
        + (comm_sems(size, 1) + [DMA((2,)), pltpu.VMEM((rows, width), BF)]) * len(cot)
        + sems,
        compiler_params=params(2 + layer),
        cost_estimate=cost(60e9, 20e6),
    )(qkv, qm, km, x, w, *cot, *halves)


def peak_kernel(
    size, parts, h1_ref, gain_ref, grad_ref, wu_ref, wd_ref,
    mid_ref, gain_out, gup_ref, gdown_ref, hid_out,
    a2, hid, dup, grad, wu, wd, w_sem, out_sem, *scratch
):
    rows, width = h1_ref.shape
    hidden = wu_ref.shape[1]
    depth = width // parts
    fb = min(256, hidden)
    n = chunks(rows)
    rc = rows // n
    g = Group(size)
    copies = [
        pltpu.make_async_copy(wu_ref, wu, w_sem.at[0]),
        pltpu.make_async_copy(wd_ref, wd, w_sem.at[1]),
        pltpu.make_async_copy(grad_ref, grad, w_sem.at[2]),
    ]
    for copy in copies:
        copy.start()
    g.greet()
    gather = Gather(g, a2, rc, scratch[:4])
    scatter = Scatter(g, rc, scratch[4:])

    def send(j):
        at = span(j, rc)
        a = normed(h1_ref[at, :])[0] * gain_ref[1, 1:2, :]
        a2[g.me, at, :] = a.astype(BF)
        gather.start(j)

    run(n, send)
    for copy in copies:
        copy.wait()
    gather.relay(0)

    def work(j):
        at = span(j, rc)
        gather.ready(j)
        a = flat(a2[:, at, :])
        held = flat(grad[:, at, :])
        for f in range(hidden // fb):
            cols = slice(f * fb, (f + 1) * fb)
            u = dg(a, wu[:, cols], NN)
            half = 0.5 + 0.5 * lax.erf(u * (0.5**0.5))
            slope = half + u * jnp.exp(-0.5 * u * u) * ((2 * math.pi) ** -0.5)
            hid[:, at, cols] = (u * half).astype(BF).reshape(size, rc, fb)
            d = dg(held, wd[cols, :], NT) * slope
            dup[:, at, cols] = d.astype(BF).reshape(size, rc, fb)

        @pl.when(j + 1 < n)
        def _():
            gather.relay(j + 1)

        @pl.when(j > 0)
        def _():
            scatter.second(j - 1)

        held = flat(dup[:, at, :])
        for z in range(parts):
            cols = slice(z * depth, (z + 1) * depth)
            scatter.part[:, at, cols] = dg(held, wu[cols, :], NT).reshape(size, rc, depth)
        scatter.first(j)

    run(n, work)
    scatter.second(n - 1)
    out = pltpu.make_async_copy(hid, hid_out, out_sem.at[0])
    out.start()

    def up_grad(z):
        cols = pl.ds(pl.multiple_of(z * depth, depth), depth)
        gup_ref[z] = dg(flat(a2[:, :, cols]), flat(dup[...]), TN).astype(BF)

    run(parts, up_grad)

    def down_grad(f):
        cols = pl.ds(pl.multiple_of(f * fb, fb), fb)
        r = dg(flat(hid[:, :, cols]), flat(grad[...]), TN).astype(BF)
        for z in range(parts):
            gdown_ref[z, cols, :] = r[:, z * depth : (z + 1) * depth]

    run(hidden // fb, down_grad)
    gain_out[...] = jnp.zeros_like(gain_out)

    def last(j):
        at = span(j, rc)
        dh, dgain = normed_back(h1_ref[at, :], gain_ref[1, 1:2, :], scatter.third(j))
        mid_ref[at, :] = grad[g.me, at, :].astype(F32) + dh
        gain_out[...] += dgain

    run(n, last)
    gather.drain(n)
    scatter.drain(n)
    out.wait()


def peak(size, replicas, h1, gains, grad_all, wu, wd):
    rows, width = h1.shape
    hidden = wu.shape[1]
    depth = width // replicas
    n = chunks(rows)
    return pl.pallas_call(
        functools.partial(peak_kernel, size, replicas),
        out_shape=[
            shape((rows, width), F32),
            shape((1, width), F32),
            shape((replicas, depth, hidden), BF),
            shape((replicas, hidden, depth), BF),
            shape((size, rows, hidden), BF),
        ],
        in_specs=[VM, VM, HB, HB, HB],
        out_specs=[VM, VM, VM, VM, HB],
        scratch_shapes=[
            pltpu.VMEM((size, rows, width), BF),
            pltpu.VMEM((size, rows, hidden), BF),
            pltpu.VMEM((size, rows, hidden), BF),
            pltpu.VMEM((size, rows, width), BF),
            pltpu.VMEM((width, hidden), BF),
            pltpu.VMEM((hidden, width), BF),
            DMA((3,)),
            DMA((1,)),
        ]
        + comm_sems(size, n)
        + scatter_scratch(size, rows, width, n),
        compiler_params=params(5),
        cost_estimate=cost(60e9, 30e6),
    )(h1, gains, grad_all, wu, wd)


def turn_kernel(size, columns, *refs):
    m = len(columns)
    h1_ref, gain_ref, wu_ref, wd_ref, q_stage = refs[:5]
    halves, refs = refs[5 : 5 + m], refs[5 + m :]
    y_ref, qkv_ref, a2_out, hid_out, slope_out, a1_out, wq_out = refs[:7]
    wholes, refs = refs[7 : 7 + m], refs[7 + m :]
    a2, hid, slope, wu, wd, a1, wq, w_sem, out_sem = refs[:9]
    gather_sems, next_sems, refs = refs[9:13], refs[13:17], refs[17:]
    scratch, refs = refs[:9], refs[9:]
    spread = Spread(q_stage.at[1], wq, False, refs[:5])
    riders = Riders(halves, wholes, columns, refs[5:])
    out_rider, up_rider = riders.all
    stages = len(spread.stages)
    rows, width = h1_ref.shape
    hidden = wu_ref.shape[1]
    fb = min(256, hidden)
    n = chunks(rows)
    rc = rows // n
    g = Group(size)
    copies = [
        pltpu.make_async_copy(wu_ref, wu, w_sem.at[0]),
        pltpu.make_async_copy(wd_ref, wd, w_sem.at[1]),
    ]
    for copy in copies:
        copy.start()
    g.greet(spread.replicas)
    gather = Gather(g, a2, rc, gather_sems)
    onward = Gather(g, a1, rc, next_sems)
    scatter = Scatter(g, rc, scratch)

    def send(j):
        at = span(j, rc)
        a = normed(h1_ref[at, :])[0] * gain_ref[0, 1:2, :]
        a2[g.me, at, :] = a.astype(BF)
        gather.start(j)

    run(n, send)
    spread.start()
    out_rider.start()
    for copy in copies:
        copy.wait()

    def pass_on(j):
        at = span(j, rc)
        y = (h1_ref[at, :] + scatter.third(j)).astype(BF)
        y_ref[at, :] = y
        a = normed(y.astype(F32))[0] * gain_ref[1, 0:1, :]
        a1[g.me, at, :] = a.astype(BF)
        onward.start(j)

    lag = min(2, n)
    gather.relay(0)

    def work(j):
        at = span(j, rc)
        gather.ready(j)
        a = flat(a2[:, at, :])
        for f in range(hidden // fb):
            cols = slice(f * fb, (f + 1) * fb)
            u = dg(a, wu[:, cols], NN)
            half = 0.5 + 0.5 * lax.erf(u * (0.5**0.5))
            slope[:, at, cols] = (
                (half + u * jnp.exp(-0.5 * u * u) * ((2 * math.pi) ** -0.5))
                .astype(BF)
                .reshape(size, rc, fb)
            )
            hid[:, at, cols] = (u * half).astype(BF).reshape(size, rc, fb)

        @pl.when(j + 1 < n)
        def _():
            gather.relay(j + 1)

        @pl.when(j > 0)
        def _():
            scatter.second(j - 1)

        held = flat(hid[:, at, :])
        for f in range(width // 256):
            cols = slice(f * 256, (f + 1) * 256)
            scatter.part[:, at, cols] = dg(held, wd[:, cols], NN).reshape(size, rc, 256)
        scatter.first(j)

        @pl.when(j >= lag)
        def _():
            pass_on(j - lag)

        @pl.when(j == min(1, n - 1))
        def _():
            spread.step(0)
            out_rider.step(0)

        @pl.when(j == n - 1)
        def _():
            for i in range(1, stages):
                spread.step(i)
                out_rider.step(i)
            up_rider.start()

    run(n, work)
    scatter.second(n - 1)
    outs = [
        pltpu.make_async_copy(a2, a2_out, out_sem.at[0]),
        pltpu.make_async_copy(hid, hid_out, out_sem.at[1]),
        pltpu.make_async_copy(slope, slope_out, out_sem.at[2]),
    ]
    for out in outs:
        out.start()
    for j in range(n - lag, n):
        pass_on(j)
    up_rider.step(0)
    spread.finish()
    outs.append(pltpu.make_async_copy(wq, wq_out, out_sem.at[3]))
    outs[3].start()

    onward.relay(0)

    def multiply(j):
        at = span(j, rc)

        @pl.when(j + 1 < n)
        def _():
            onward.relay(j + 1)

        @pl.when(j == n // 2)
        def _():
            for i in range(1, stages):
                up_rider.step(i)

        onward.ready(j)
        r = dg(flat(a1[:, at, :]), wq[...], NN).astype(BF)
        qkv_ref[:, at, :] = r.reshape(size, rc, r.shape[1])

    run(n, multiply)
    outs.append(pltpu.make_async_copy(a1, a1_out, out_sem.at[4]))
    outs[4].start()
    riders.finish()
    gather.drain(n)
    onward.drain(n)
    scatter.drain(n)
    for out in outs:
        out.wait()


def turn_forward(size, replicas, h1, gains, wu, wd, stage, riders):
    rows, width = h1.shape
    hidden = wu.shape[1]
    wide = stage.shape[2]
    n = chunks(rows)
    halves, columns, outs, sems = riding(riders, replicas)
    return pl.pallas_call(
        functools.partial(turn_kernel, size, columns),
        out_shape=[
            shape((rows, width), BF),
            shape((size, rows, wide), BF),
            shape((size, rows, width), BF),
            shape((size, rows, hidden), BF),
            shape((size, rows, hidden), BF),
            shape((size, rows, width), BF),
            shape((width, wide), BF),
        ]
        + outs,
        in_specs=[VM, VM] + [HB] * (3 + len(riders)),
        out_specs=[VM, VM] + [HB] * (5 + len(outs)),
        scratch_shapes=[
            pltpu.VMEM((size, rows, width), BF),
            pltpu.VMEM((size, rows, hidden), BF),
            pltpu.VMEM((size, rows, hidden), BF),
            pltpu.VMEM((width, hidden), BF),
            pltpu.VMEM((hidden, width), BF),
            pltpu.VMEM((size, rows, width), BF),
            pltpu.VMEM((width, wide), BF),
            DMA((2,)),
            DMA((5,)),
        ]
        + comm_sems(size, n) * 2
        + scatter_scratch(size, rows, width, n)
        + rider_sems(replicas)
        + sems,
        compiler_params=params(4),
        cost_estimate=cost(50e9, 30e6),
    )(h1, gains, wu, wd, stage, *halves)


def mlp_back_kernel(size, layer, parts, *refs):
    g_ref, h1_ref, gain_ref, a2_ref, hid_ref, slope_ref, wu_ref, wd_ref = refs[:8]
    refs = refs[8:]
    ys, refs = refs[:2], refs[2:]
    mid_ref, gain_out, gup_ref, gdown_ref = refs[:4]
    refs = refs[4:]
    y_out, refs = refs[0], refs[1:]
    grad, a2, hid, dup, wu, wd, w_sem = refs[:7]
    scratch, refs = refs[7:20], refs[20:]
    rows, width = h1_ref.shape
    hidden = wu_ref.shape[1]
    depth = width // parts
    fb = min(256, hidden)
    n = chunks(rows)
    rc = rows // n
    g = Group(size)
    copies = [
        pltpu.make_async_copy(wd_ref, wd, w_sem.at[0]),
        pltpu.make_async_copy(slope_ref, dup, w_sem.at[1]),
        pltpu.make_async_copy(wu_ref, wu, w_sem.at[2]),
    ]
    late = [
        pltpu.make_async_copy(hid_ref, hid, w_sem.at[3]),
        pltpu.make_async_copy(a2_ref, a2, w_sem.at[4]),
    ]
    for copy in copies:
        copy.start()
    g.greet(side=True)
    section = lax.axis_index("section")
    y_sem, y_own = refs

    def y_load(own):
        return pltpu.make_async_copy(own, y_own, y_sem.at[3])

    def y_copies(own, other, at):
        return (
            pltpu.make_async_copy(y_own, y_out.at[section], y_sem.at[0]),
            far_copy(
                other, y_out.at[at], y_sem.at[1], y_sem.at[2], {"section": 1 - section}
            ),
        )

    for i in range(2):

        @pl.when(section == i)
        def _(i=i):
            y_load(ys[i]).start()
            y_copies(ys[i], ys[1 - i], section)[1].start()

    gather = Gather(g, grad, rc, scratch[:4])
    scatter = Scatter(g, rc, scratch[4:])

    def send(j):
        at = span(j, rc)
        grad[g.me, at, :] = g_ref[at, :]
        gather.start(j)

    run(n, send)
    for copy in copies:
        copy.wait()
    for copy in late:
        copy.start()
    y_load(ys[0]).wait()
    y_copies(ys[0], ys[1], section)[0].start()

    gather.relay(0)

    def work(j):
        at = span(j, rc)
        gather.ready(j)
        held = flat(grad[:, at, :])
        for f in range(hidden // fb):
            cols = slice(f * fb, (f + 1) * fb)
            d = dg(held, wd[cols, :], NT) * flat(dup[:, at, cols]).astype(F32)
            dup[:, at, cols] = d.astype(BF).reshape(size, rc, fb)

        @pl.when(j + 1 < n)
        def _():
            gather.relay(j + 1)

        @pl.when(j > 0)
        def _():
            scatter.second(j - 1)

        held = flat(dup[:, at, :])
        for z in range(parts):
            cols = slice(z * depth, (z + 1) * depth)
            scatter.part[:, at, cols] = dg(held, wu[cols, :], NT).reshape(size, rc, depth)
        scatter.first(j)

    run(n, work)
    scatter.second(n - 1)
    for copy in late:
        copy.wait()

    def up_grad(z):
        cols = pl.ds(pl.multiple_of(z * depth, depth), depth)
        gup_ref[z] = dg(flat(a2[:, :, cols]), flat(dup[...]), TN).astype(BF)

    run(parts, up_grad)

    def down_grad(f):
        cols = pl.ds(pl.multiple_of(f * fb, fb), fb)
        r = dg(flat(hid[:, :, cols]), flat(grad[...]), TN).astype(BF)
        for z in range(parts):
            gdown_ref[z, cols, :] = r[:, z * depth : (z + 1) * depth]

    run(hidden // fb, down_grad)
    gain_out[...] = jnp.zeros_like(gain_out)

    def last(j):
        at = span(j, rc)
        dh, dgain = normed_back(h1_ref[at, :], gain_ref[layer, 1:2, :], scatter.third(j))
        mid_ref[at, :] = g_ref[at, :].astype(F32) + dh
        gain_out[...] += dgain

    run(n, last)
    local, side = y_copies(ys[0], ys[1], 1 - section)
    local.wait()
    side.wait_recv()
    y_copies(ys[0], ys[1], section)[1].wait_send()
    gather.drain(n)
    scatter.drain(n)


def mlp_backward(size, replicas, layer, grad, h1, gains, a2, hid, slope, wu, wd, extra):
    rows, width = h1.shape
    hidden = wu.shape[1]
    parts, depth = replicas, width // replicas
    n = chunks(rows)
    return pl.pallas_call(
        functools.partial(mlp_back_kernel, size, layer, parts),
        out_shape=[
            shape((rows, width), F32),
            shape((1, width), F32),
            shape((parts, depth, hidden), BF),
            shape((parts, hidden, depth), BF),
        ]
        + [shape((2, rows, width), BF)] * (len(extra) // 2),
        in_specs=[VM, VM, VM] + [HB] * (5 + len(extra)),
        out_specs=[VM, VM, VM, VM] + [HB] * (len(extra) // 2),
        scratch_shapes=[
            pltpu.VMEM((size, rows, width), BF),
            pltpu.VMEM((size, rows, width), BF),
            pltpu.VMEM((size, rows, hidden), BF),
            pltpu.VMEM((size, rows, hidden), BF),
            pltpu.VMEM((width, hidden), BF),
            pltpu.VMEM((hidden, width), BF),
            DMA((6,)),
        ]
        + comm_sems(size, n)
        + scatter_scratch(size, rows, width, n)
        + [DMA((4,)), pltpu.VMEM((rows, width), BF)] * (len(extra) // 2),
        compiler_params=params(6 + layer),
        cost_estimate=cost(60e9, 40e6),
    )(grad, h1, gains, a2, hid, slope, wu, wd, *extra)


def attend_back_kernel(size, layer, parts, *refs):
    mid_ref, qkv_ref, qm_ref, km_ref, ctx_ref, lse_ref, w_ref = refs[:7]
    refs = refs[7:]
    if layer == 0:
        gdown_ref, above_ref, refs = refs[0], refs[1], refs[2:]
    else:
        above_ref = None
        hid_ref, wd_ref, h1_in, refs = refs[0], refs[1], refs[2], refs[3:]
    dqkv_ref, gout_ref, refs = refs[0], refs[1], refs[2:]
    if layer == 0:
        down_out, refs = refs[0], refs[1:]
    else:
        y_ref, refs = refs[0], refs[1:]
    da, ka, va, kt, dk, dv, w, w_sem = refs[:8]
    sems, refs = refs[8:12], refs[12:]
    reduce = Reduce(layer, refs[:9])
    if layer == 0:
        down = HalfReduce(layer, refs[9 : 9 + HALF])
        down_swap = HalfSwap(gdown_ref, down.other, refs[9 + HALF])
    else:
        held_hid, wd, h1, y_sem = refs[9:13]
    _, rows, wide = qkv_ref.shape
    length = size * rows
    e = qm_ref.shape[2]
    heads = wide // (3 * e)
    scale = e**-0.5
    c = scale * math.log2(math.e)
    depth = w_ref.shape[1] // parts
    n = chunks(rows)
    rc = rows // n
    bq = size * rc
    kc = bq
    g = Group(size)
    copies = [pltpu.make_async_copy(w_ref, w, w_sem.at[0])]
    for copy in copies:
        copy.start()
    g.greet(parts)
    gather = Gather(g, da, rc, sems)
    loads = []
    if layer == 1:
        scatter = Scatter(g, rc, refs[13:])
        loads = [
            pltpu.make_async_copy(wd_ref, wd, y_sem.at[0]),
            pltpu.make_async_copy(h1_in, h1, y_sem.at[1]),
        ]
        for load in loads:
            load.start()
    if layer == 0:
        down_swap.copy().start()
        loads = down.loads(gdown_ref, None)
        for load in loads:
            load.start()

    def send(j):
        at = span(j, rc)
        da[g.me, at, :] = mid_ref[at, :].astype(BF)
        gather.start(j)

    run(n, send)
    lane = lax.broadcasted_iota(jnp.int32, (length, e), 1)
    whole = flat(qkv_ref[...])
    for h in range(heads):
        o = 3 * e * h
        ka[h, :, :e] = whole[:, o + e : o + 2 * e]
        ka[h, :, e:] = flat(km_ref[...])
        va[h, :, :e] = whole[:, o + 2 * e : o + 3 * e]
        va[h, :, e:] = jnp.where(lane < 3, 1.0, 0.0).astype(BF)
        kt[h] = whole[:, o + e : o + 2 * e].T
    dk[...] = jnp.zeros_like(dk)
    dv[...] = jnp.zeros_like(dv)
    ql = lax.broadcasted_iota(jnp.int32, (bq, e), 1)
    for copy in copies + loads:
        copy.wait()

    def out_grad(z):
        cols = pl.ds(pl.multiple_of(z * depth, depth), depth)
        return dg(flat(ctx_ref[...]), flat(da[:, :, cols]), TN)

    def work(j):
        at = span(j, rc)

        @pl.when(j == 0)
        def _():
            gather.relay(0)
            gather.ready(0)

        @pl.when(j == min(1, n - 1))
        def _():
            for i in range(1, n):
                gather.relay(i)
            for i in range(1, n):
                gather.ready(i)
            reduce.send(out_grad)

        if layer == 1:
            hid_load = pltpu.make_async_copy(hid_ref.at[:, at], held_hid, y_sem.at[2])
            hid_load.start()
        qm = flat(qm_ref[:, at, :])
        dctx = dg(flat(da[:, at, :]), w[...], NT).astype(BF)
        ctx = flat(ctx_ref[:, at, :])
        held_qkv = flat(qkv_ref[:, at, :])
        for h in range(heads):
            o = 3 * e * h
            qq = held_qkv[:, o : o + e]
            q = jnp.concatenate([qq, qm], axis=1)
            dc = dctx[:, h * e : (h + 1) * e]
            prod = dc.astype(F32) * ctx[:, h * e : (h + 1) * e].astype(F32)
            d = -jnp.sum(prod, axis=1, keepdims=True)
            d1 = d.astype(BF).astype(F32)
            d2 = (d - d1).astype(BF).astype(F32)
            d3 = d - d1 - d2
            ds_col = jnp.where(ql == 0, d1, jnp.where(ql == 1, d2, jnp.where(ql == 2, d3, 0.0)))
            dca = jnp.concatenate([dc, ds_col.astype(BF)], axis=1)
            lse = lse_ref[j, h : h + 1, :]
            dqt = None
            for k in range(length // kc):
                ks = slice(k * kc, (k + 1) * kc)
                s = dg(ka[h, ks, :], q, NT)
                p = jnp.exp2(s * c - lse)
                ds = (p * dg(va[h, ks, :], dca, NT)).astype(BF)
                dv[h, ks, :] += dg(p.astype(BF), dc, NN)
                dk[h, ks, :] += dg(ds, qq, NN)
                a = dg(kt[h, :, ks], ds, NN)
                dqt = a if dqt is None else dqt + a
            if layer == 0 and h == heads // 2:

                @pl.when(j == min(1, n - 1))
                def _():
                    down_swap.copy().wait_recv()
                    down.middle()

            if layer == 1 and h == heads // 2:

                @pl.when(j > 0)
                def _():
                    scatter.second(j - 1)

            if layer == 0 and h == heads - 1:

                @pl.when(j == n - 1)
                def _():
                    down.late()

            dqkv_ref[:, at, o : o + e] = (dqt * scale).T.astype(BF).reshape(size, rc, e)
        if layer == 1:
            hid_load.wait()
            width = wd.shape[1]
            for f in range(width // 256):
                cols = slice(f * 256, (f + 1) * 256)
                scatter.part[:, at, cols] = dg(flat(held_hid[...]), wd[:, cols], NN).reshape(
                    size, rc, 256
                )
            scatter.first(j)

    run(n, work)
    if layer == 1:
        scatter.second(n - 1)
    for h in range(heads):
        o = 3 * e * h
        dqkv_ref[:, :, o + e : o + 2 * e] = (dk[h] * scale).astype(BF).reshape(size, rows, e)
        dqkv_ref[:, :, o + 2 * e : o + 3 * e] = dv[h].astype(BF).reshape(size, rows, e)

    reduce.collect()
    if layer == 1:

        def output(j):
            at = span(j, rc)
            y_ref[at, :] = (h1[at, :] + scatter.third(j)).astype(BF)

        run(n, output)
        scatter.drain(n)
    reduce.finish(gout_ref, above_ref)
    if layer == 0:
        down.finish(down_out)
        down_swap.copy().wait_send()
    gather.drain(n)


def attend_backward(size, replicas, layer, mid, qkv, qm, km, ctx, lse, w, grads, more=(), above=()):
    _, rows, wide = qkv.shape
    e = qm.shape[2]
    heads = wide // (3 * e)
    width = mid.shape[1]
    parts, depth = replicas, width // replicas
    length = size * rows
    n = chunks(rows)
    return pl.pallas_call(
        functools.partial(attend_back_kernel, size, layer, parts),
        out_shape=[shape(qkv.shape, BF), shape((heads * e, depth), F32)]
        + [shape(grad.shape[1:], F32) for grad in grads]
        + [shape((rows, width), BF)] * (len(more) // 3),
        in_specs=[VM] * 6 + [HB] * (1 + len(grads) + len(more)) + [VM] * len(above),
        out_specs=[VM, VM] + [VM] * (len(grads) + len(more) // 3),
        scratch_shapes=[
            pltpu.VMEM((size, rows, width), BF),
            pltpu.VMEM((heads, length, 2 * e), BF),
            pltpu.VMEM((heads, length, 2 * e), BF),
            pltpu.VMEM((heads, e, length), BF),
            pltpu.VMEM((heads, length, e), F32),
            pltpu.VMEM((heads, length, e), F32),
            pltpu.VMEM((heads * e, width), BF),
            DMA((1,)),
        ]
        + comm_sems(size, n)
        + reduce_scratch(parts, heads * e, depth)
        + sum([half_scratch(parts, *grad.shape[1:]) + [DMA((2,))] for grad in grads], [])
        + (
            [
                pltpu.VMEM((size, rows // n, more[0].shape[2]), BF),
                pltpu.VMEM(more[1].shape, BF),
                pltpu.VMEM((rows, width), F32),
                DMA((3,)),
            ]
            + scatter_scratch(size, rows, width, n)
            if more
            else []
        ),
        compiler_params=params(8 + layer),
        cost_estimate=cost(90e9, 40e6),
    )(mid, qkv, qm, km, ctx, lse, w, *grads, *more, *above)


def qkv_back_kernel(
    size, layer, parts, dqkv_ref, gain_ref, a1_in, x_in, mid_in, w_ref,
    dx_ref, gain_out, gqkv_ref, a1_ref, x_ref, mid_ref, w, w_sem, *scratch
):
    rows, width = x_ref.shape
    late = [
        pltpu.make_async_copy(a1_in, a1_ref, w_sem.at[1]),
        pltpu.make_async_copy(x_in, x_ref, w_sem.at[2]),
        pltpu.make_async_copy(mid_in, mid_ref, w_sem.at[3]),
    ]
    depth = width // parts
    n = thin_chunks(rows)
    rc = rows // n
    g = Group(size)
    copies = [pltpu.make_async_copy(w_ref, w, w_sem.at[0])]
    for copy in copies + late:
        copy.start()
    g.greet()
    scatter = Scatter(g, rc, scratch)
    for copy in copies:
        copy.wait()

    lag = min(2, n)

    def work(j):
        at = span(j, rc)
        held = flat(dqkv_ref[:, at, :])
        for z in range(parts):
            cols = slice(z * depth, (z + 1) * depth)
            scatter.part[:, at, cols] = dg(held, w[cols, :], NT).reshape(size, rc, depth)
        scatter.first(j)

        @pl.when(j >= lag)
        def _():
            scatter.second(j - lag)


    run(n, work)
    for j in range(n - lag, n):
        scatter.second(j)
    for copy in late:
        copy.wait()

    def qkv_grad(z):
        cols = pl.ds(pl.multiple_of(z * depth, depth), depth)
        gqkv_ref[z] = dg(flat(a1_ref[:, :, cols]), flat(dqkv_ref[...]), TN).astype(BF)

    run(parts, qkv_grad)
    gain_out[...] = jnp.zeros_like(gain_out)

    def last(j):
        at = span(j, rc)
        dh, dgain = normed_back(
            x_ref[at, :].astype(F32), gain_ref[layer, 0:1, :], scatter.third(j)
        )
        dx_ref[at, :] = (mid_ref[at, :] + dh).astype(BF)
        gain_out[...] += dgain

    run(n, last)
    scatter.drain(n)


def qkv_backward(size, replicas, layer, dqkv, a1, x, mid, gains, w):
    rows, width = x.shape
    wide = w.shape[1]
    parts, depth = replicas, width // replicas
    n = thin_chunks(rows)
    return pl.pallas_call(
        functools.partial(qkv_back_kernel, size, layer, parts),
        out_shape=(
            shape((rows, width), BF),
            shape((1, width), F32),
            shape((parts, depth, wide), BF),
        ),
        in_specs=[VM, VM] + [HB] * 4,
        out_specs=(VM, VM, VM),
        scratch_shapes=[
            pltpu.VMEM((size, rows, width), BF),
            pltpu.VMEM((rows, width), BF),
            pltpu.VMEM((rows, width), F32),
            pltpu.VMEM((width, wide), BF),
            DMA((4,)),
        ]
        + scatter_scratch(size, rows, width, n),
        compiler_params=params(11),
        cost_estimate=cost(30e9, 30e6),
    )(dqkv, gains, a1, x, mid, w)


def last_kernel(
    size, parts, dqkv_ref, a1_ref, x_ref, mid_ref, gain_ref, w_ref, two_ref, up_one_ref, up_two_ref, dx1_ref,
    one_out, two_out, gqkv_out, dx_out,
    gqkv, swap_sem, w, dx, gsum, gcame, w_sem, x_sem, x_send, x_recv, g_send, g_recv, *scratch
):
    rows, width = x_ref.shape
    depth = width // parts
    n = thin_chunks(rows)
    rc = rows // n
    g = Group(size)
    section = lax.axis_index("section")
    d = lax.axis_index("dp")
    copy = pltpu.make_async_copy(w_ref, w, w_sem.at[0])
    copy.start()
    reduce = HalfReduce(0, scratch[:HALF])
    swap = HalfSwap(gqkv, reduce.other, swap_sem)
    scatter = Scatter(g, rc, scratch[HALF:])
    g.greet(parts)

    def upper():
        return far_copy(
            dx1_ref, dx_out.at[0], x_send.at[n], x_recv.at[n], {"section": 1 - section}
        )

    def keep_upper():
        return pltpu.make_async_copy(dx1_ref, dx_out.at[1], x_sem.at[0])

    def lower(j):
        at = span(j, rc)
        return far_copy(
            dx.at[at], dx_out.at[1, at], x_send.at[j], x_recv.at[j], {"section": 1 - section}
        )

    def keep_lower(j):
        at = span(j, rc)
        return pltpu.make_async_copy(dx.at[at], dx_out.at[0, at], x_sem.at[j])

    def qkv_grad(z):
        cols = pl.ds(pl.multiple_of(z * depth, depth), depth)
        gqkv[z] = dg(flat(a1_ref[:, :, cols]), flat(dqkv_ref[...]), TN).astype(BF)

    run(parts, qkv_grad)
    swap.copy().start()
    load = reduce.loads(gqkv, None)[0]
    load.start()

    @pl.when(section == 1)
    def _():
        keep_upper().start()

    copy.wait()

    lag = min(2, n)

    def work(j):
        at = span(j, rc)
        held = flat(dqkv_ref[:, at, :])
        for z in range(parts):
            cols = slice(z * depth, (z + 1) * depth)
            scatter.part[:, at, cols] = dg(held, w[cols, :], NT).reshape(size, rc, depth)
        scatter.first(j)

        @pl.when(j >= lag)
        def _():
            scatter.second(j - lag)


    run(n, work)
    for j in range(n - lag, n):
        scatter.second(j)
    gsum[0] = jnp.zeros_like(gsum[0])

    def last(j):
        at = span(j, rc)
        dh, dgain = normed_back(x_ref[at, :].astype(F32), gain_ref[0, 0:1, :], scatter.third(j))
        dx[at, :] = (mid_ref[at, :] + dh).astype(BF)

        @pl.when(section == 0)
        def _():
            keep_lower(j).start()

        @pl.when(section == 1)
        def _():
            lower(j).start()

        gsum[0, 0:1, :] += dgain

    def rest(j):
        @pl.when(j == n // 2)
        def _():
            load.wait()
            swap.copy().wait_recv()
            reduce.middle()

            @pl.when(section == 0)
            def _():
                upper().start()

        last(j)

    run(n, rest)
    gsum[0, 1:2, :] = two_ref[...]
    gsum[0, 2:3, :] = up_one_ref[...]
    gsum[0, 3:4, :] = up_two_ref[...]

    targets = [
        [{"tensor": g.sibling}],
        [{"tensor": g.ahead(k) * 2 + g.core} for k in range(1, g.chips)],
        [{"dp": lax.rem(d + k, parts)} for k in range(1, parts)],
        [{"section": 1 - section}],
    ]
    slot = 0
    sent = []

    def exchange(stage):
        nonlocal slot
        copies = []
        for target in targets[stage]:
            copies.append(
                far_copy(gsum.at[stage], gcame.at[slot], g_send.at[slot], g_recv.at[slot], target)
            )
            copies[-1].start()
            slot += 1
        total = gsum[stage]
        for i, copy in enumerate(copies):
            copy.wait_recv()
            total = total + gcame[slot - len(copies) + i]
        gsum[stage + 1] = total
        sent.extend(copies)

    exchange(0)
    exchange(1)
    reduce.late()
    exchange(2)
    exchange(3)
    lower_layer = section == 0
    one_out[...] = jnp.where(lower_layer, gsum[4, 0:1, :], gsum[4, 2:3, :])
    two_out[...] = jnp.where(lower_layer, gsum[4, 1:2, :], gsum[4, 3:4, :])

    @pl.when(section == 0)
    def _():
        for j in range(n):
            lower(j).wait_recv()
            keep_lower(j).wait()
        upper().wait_send()

    @pl.when(section == 1)
    def _():
        keep_upper().wait()
        upper().wait_recv()
        for j in range(n):
            lower(j).wait_send()

    reduce.finish(gqkv_out)
    swap.copy().wait_send()
    for copy in sent:
        copy.wait_send()
    scatter.drain(n)


def last_backward(size, replicas, dqkv, a1, x, mid, gains, w, two, up_one, up_two, dx1):
    rows, width = x.shape
    wide = w.shape[1]
    depth = width // replicas
    n = thin_chunks(rows)
    slots = 1 + (size // 2 - 1) + (replicas - 1) + 1
    return pl.pallas_call(
        functools.partial(last_kernel, size, replicas),
        out_shape=(
            shape((1, width), F32),
            shape((1, width), F32),
            shape((depth, wide), F32),
            shape((2, rows, width), BF),
        ),
        in_specs=[VM] * 5 + [HB, VM, VM, VM, VM],
        out_specs=(VM, VM, VM, HB),
        scratch_shapes=[
            pltpu.VMEM((replicas, depth, wide), BF),
            DMA((2,)),
            pltpu.VMEM((width, wide), BF),
            pltpu.VMEM((rows, width), BF),
            pltpu.VMEM((5, 8, width), F32),
            pltpu.VMEM((slots, 8, width), F32),
            DMA((1,)),
            DMA((n,)),
            DMA((n + 1,)),
            DMA((n + 1,)),
            DMA((slots,)),
            DMA((slots,)),
        ]
        + half_scratch(replicas, depth, wide)
        + scatter_scratch(size, rows, width, n),
        compiler_params=params(10),
        cost_estimate=cost(40e9, 30e6),
    )(dqkv, a1, x, mid, gains, w, two, up_one, up_two, dx1)


def scene_masks(segments, e):
    same = (segments[..., None] == jnp.arange(e, dtype=jnp.int32)).astype(F32)
    used = jnp.arange(e) < SCENES
    return (
        jnp.where(used, same * MASKED, 0.0).astype(BF),
        jnp.where(used, 1.0 - same, 0.0).astype(BF),
    )


def swap_section(value):
    return lax.ppermute(value, "section", [(0, 1), (1, 0)])


def shards(
    block_input,
    segment_ids,
    cotangent,
    norm_one_gain,
    qkv_weight,
    out_weight,
    norm_two_gain,
    up_weight,
    down_weight,
):
    section = lax.axis_index("section")
    size = lax.axis_size("tensor")
    replicas = lax.axis_size("dp")

    mine = [
        qkv_weight[0].reshape((qkv_weight.shape[1], -1)),
        out_weight[0].reshape((-1, out_weight.shape[3])),
        up_weight[0],
        down_weight[0],
    ]
    mine = [w.astype(BF).reshape((2, -1, w.shape[1])) for w in mine]
    gains = jnp.concatenate(
        [norm_one_gain, norm_two_gain, jnp.zeros((6, norm_one_gain.shape[1]), F32)], axis=0
    )
    segments = lax.dynamic_index_in_dim(segment_ids, section, 0, keepdims=False)
    head_dim = qkv_weight.shape[3] // 3
    qm, km = scene_masks(segments.reshape((size, -1)), head_dim)
    qkv, gains, x, a1, w_qkv_0, w_out_0, h_qkv, h_out, h_up, h_down = first_forward(
        size, replicas, block_input, gains, mine
    )
    h1, ctx, lse, w_up_0, w_down_0 = attend(
        size, replicas, 0, qkv, qm, km, x, w_out_0,
        [(h_up, "spread", 0, False), (h_down, "spread", 0, True)],
    )
    below = (x, a1, qkv, ctx, lse, h1)
    y0, qkv, a2, hid, slope, a1, w_qkv_1, w_out_1, w_up_1 = turn_forward(
        size, replicas, h1, gains, w_up_0, w_down_0, h_qkv,
        [(h_out, "spread", 1, True), (h_up, "spread", 1, False)],
    )
    kept = [below + (a2, hid, slope)]
    h1, ctx, lse, grad_all, w_down_1 = attend(
        size, replicas, 1, qkv, qm, km, y0, w_out_1, [(h_down, "spread", 1, True)], [cotangent]
    )
    kept.append((y0, a1, qkv, ctx, lse, h1))
    weights = [
        (w_qkv_0, w_out_0, w_up_0, w_down_0),
        (w_qkv_1, w_out_1, w_up_1, w_down_1),
    ]
    def reduce_rows(value):
        return lax.psum_scatter(value, "dp", scatter_dimension=0, tiled=False)

    x, a1, qkv, ctx, lse, h1 = kept[1]
    w_qkv, w_out, w_up, w_down = weights[1]
    mid, gain_two, g_up, g_down, hid = peak(size, replicas, h1, gains, grad_all, w_up, w_down)
    d_qkv, out_1, y1 = attend_backward(
        size, replicas, 1, mid, qkv, qm, km, ctx, lse, w_out, [], [hid, w_down, h1]
    )
    up_1, down_1 = reduce_rows(g_up), reduce_rows(g_down)
    dx1, gain_one, g_qkv = qkv_backward(size, replicas, 1, d_qkv, a1, x, mid, gains, w_qkv)
    up_one, up_two = gain_one, gain_two
    dx1, up_1, down_1 = lax.optimization_barrier((dx1, up_1, down_1))
    qkv_1 = reduce_rows(g_qkv)

    x, a1, qkv, ctx, lse, h1, a2, hid, slope = kept[0]
    w_qkv, w_out, w_up, w_down = weights[0]
    mid, gain_two, g_up, g_down, layer_out = mlp_backward(
        size, replicas, 0, dx1, h1, gains, a2, hid, slope, w_up, w_down, [y0, y1]
    )
    mid, qkv_1 = lax.optimization_barrier((mid, qkv_1))
    d_qkv, out_0, down_0 = attend_backward(
        size, replicas, 0, mid, qkv, qm, km, ctx, lse, w_out, [g_down], (), [out_1]
    )
    up_0 = reduce_rows(g_up)
    d_qkv, up_0 = lax.optimization_barrier((d_qkv, up_0))
    one_grad, two_grad, qkv_0, input_out = last_backward(
        size, replicas, d_qkv, a1, x, mid, gains, w_qkv, gain_two, up_one, up_two, dx1
    )

    def finish(zero, one):
        send = swap_section(jnp.where(section == 0, one, zero))
        return jnp.where(section == 0, zero, one).astype(F32) + send.astype(F32)

    other_qkv_1 = swap_section(qkv_1)
    qkv_grad = jnp.where(section == 0, qkv_0, qkv_1.astype(F32) + other_qkv_1.astype(F32))
    out_grad = out_0
    up_grad = finish(up_0, up_1)
    other_down_1 = swap_section(down_1)
    down_grad = jnp.where(section == 0, down_0, down_1.astype(F32) + other_down_1.astype(F32))
    return (
        layer_out[None],
        input_out[None],
        one_grad,
        qkv_grad.reshape(qkv_weight.shape),
        out_grad.reshape(out_weight.shape),
        two_grad,
        up_grad[None],
        down_grad[None],
    )


def solution(mesh):
    return jax.shard_map(
        shards,
        mesh=mesh,
        in_specs=(
            P(None, ("dp", "tensor"), None),
            P(None, "dp"),
            P(None, ("dp", "tensor"), None),
            P("section", None),
            P("section", "dp", "tensor", None),
            P("section", "tensor", None, "dp"),
            P("section", None),
            P("section", "dp", "tensor"),
            P("section", "tensor", "dp"),
        ),
        out_specs=(
            P("section", None, ("dp", "tensor"), None),
            P("section", None, ("dp", "tensor"), None),
            P("section", None),
            P("section", "dp", "tensor", None),
            P("section", "tensor", None, "dp"),
            P("section", None),
            P("section", "dp", "tensor"),
            P("section", "tensor", "dp"),
        ),
        check_vma=False,
    )
```
